32 devices in a mesh: seq: 16 (over z, y, core), dp: 2 (over x).
Axes of the slice: x: 2, y: 2, z: 4, core: 2. Of those that a mesh axis runs over, the one named last changes fastest.
Arguments:
- probe_vectors: bfloat16 [2, 2048, 2048], P('dp', 'seq'), may hold values from -6 to 6
- lookup_vectors: bfloat16 [2, 2048, 2048], P('dp', 'seq'), may hold values from -6 to 6
- content_vectors: bfloat16 [2, 2048, 2048], P('dp', 'seq'), may hold values from -6 to 6
- result_cotangent: bfloat16 [2, 2048, 2048], P('dp', 'seq'), may hold values from -25 to 25
- logit_softness: float32 [16], replicated, may hold values from 0.7 to 1.2
- block_grouping: int32 [2, 16, 16, 1], P('dp'), may hold values from 0 to 1, as said below
- neighborhood_span: int32 [16], replicated, may hold values from 32 to 128
Outputs:
- query_grad: bfloat16 [2, 2048, 2048], P('dp', 'seq')
- key_grad: bfloat16 [2, 2048, 2048], P('dp', 'seq')
- value_grad: bfloat16 [2, 2048, 2048], P('dp', 'seq')
- temper_grad: float32 [16], replicated
The draws below stay inside these ranges and needn't reach their ends.
Inputs may be any that keep to these rules, and one draw needn't show every extreme that they name: `block_grouping`: within one document and head no cluster holds more than 12 blocks, and some cluster holds exactly 12. Index j of seq owns the clusters c of head h with (h * 2 + c) // 2 == j; of the 1 block of one index of seq, at most 1 have for one head clusters owned by one index of seq, and that many is reached.
All inputs are finite; a program needn't handle non-finite values.
Results may differ from the reference program's by a relative error of at most 0.0076.
Values may be sent and summed in bfloat16 or wider, within the bound.
No kernel may reach another device: no remote copies, remote signals or barrier semaphores. Data moves between devices by JAX's collectives and lax.ppermute only.
A program may use at most 64 MiB of HBM per device.

```python
import math
import jax
import jax.numpy as jnp
from jax import lax

ATTENTION_SPLITS = 16
HD = 128
BLK = 128
CORPUS_SIZE = 2
SEQLEN = 2048
NBLK = 16
NC = 2
MOST = 12
OWN = 2


def noise_field(key, label):
    field_shape = (CORPUS_SIZE, SEQLEN, ATTENTION_SPLITS * HD)
    subkey = jax.random.fold_in(key, label)
    return jnp.clip(jax.random.normal(subkey, field_shape, jnp.float32), -4.5, 4.5)


def rising(key):
    position = lax.broadcasted_iota(jnp.int32, (1, SEQLEN, 1), 1).astype(jnp.float32)
    factor = 1.0 + 2.0 * position / (SEQLEN - 1)
    return factor


def draw_probe_vectors(key, part):
    field = noise_field(key, 1)
    return field.astype(jnp.bfloat16)


def draw_lookup_vectors(key, part):
    field = noise_field(key, 2)
    return field.astype(jnp.bfloat16)


def draw_content_vectors(key, part):
    field = 0.6 * noise_field(key, 2) + 0.8 * noise_field(key, 3)
    return jnp.clip(field, -6.0, 6.0).astype(jnp.bfloat16)


def draw_result_cotangent(key, part):
    field = (0.5 * noise_field(key, 1) + 0.85 * noise_field(key, 4)) * rising(key)
    return jnp.clip(field, -25.0, 25.0).astype(jnp.bfloat16)


def draw_block_grouping(key, part):
    group_total = NC // OWN
    block_index = lax.broadcasted_iota(jnp.int32, (CORPUS_SIZE, ATTENTION_SPLITS, NBLK), 2)
    first = jax.random.randint(jax.random.fold_in(key, 11), (CORPUS_SIZE, ATTENTION_SPLITS, NBLK), 0, 1 << 20) * NBLK + block_index
    runs = first.reshape(CORPUS_SIZE, ATTENTION_SPLITS, NBLK // group_total, group_total)
    group_of = jnp.sum((runs[..., None, :] < runs[..., :, None]).astype(jnp.int32), axis=-1).reshape(CORPUS_SIZE, ATTENTION_SPLITS, NBLK)
    second = jax.random.randint(jax.random.fold_in(key, 12), (CORPUS_SIZE, ATTENTION_SPLITS, NBLK), 0, 1 << 20) * NBLK + block_index
    same_group = group_of[..., None, :] == group_of[..., :, None]
    order = jnp.sum((same_group & (second[..., None, :] < second[..., :, None])).astype(jnp.int32), axis=-1)
    forced_all = jax.random.randint(jax.random.fold_in(key, 13), (CORPUS_SIZE, ATTENTION_SPLITS, group_total), 0, OWN)
    forced = jnp.take_along_axis(forced_all, group_of, axis=2)
    rest = (forced + 1 + jnp.maximum(order - MOST, 0) % (OWN - 1)) % OWN
    local_window_part = jnp.where(order < MOST, forced, rest)
    return (group_of * OWN + local_window_part)[..., None].astype(jnp.int32)


def place_ends(result, own_key, smallest, largest):
    dims = result.shape
    place = [jax.random.randint(jax.random.fold_in(own_key, axis), (), 0, dims[axis]) for axis in range(len(dims))]
    result = result.at[tuple(place)].set(smallest)
    longest = dims.index(max(dims))
    place[longest] = (place[longest] + 1) % dims[longest]
    return result.at[tuple(place)].set(largest)


def setup_inputs(seed: int = 0) -> dict:
    arg_keys = jax.random.split(jax.random.key(seed), 8)
    return {
        "probe_vectors": draw_probe_vectors(jax.random.fold_in(arg_keys[7], 71), 0),
        "lookup_vectors": draw_lookup_vectors(jax.random.fold_in(arg_keys[7], 71), 0),
        "content_vectors": draw_content_vectors(jax.random.fold_in(arg_keys[7], 71), 0),
        "result_cotangent": draw_result_cotangent(jax.random.fold_in(arg_keys[7], 71), 0),
        "logit_softness": jnp.clip(jnp.exp(jax.random.uniform(arg_keys[4], (ATTENTION_SPLITS,), jnp.float32, math.log(0.7), math.log(1.2))), 0.7, 1.2),
        "block_grouping": draw_block_grouping(jax.random.fold_in(arg_keys[7], 71), 0),
        "neighborhood_span": place_ends(jax.random.randint(arg_keys[6], (ATTENTION_SPLITS,), BLK // 4, BLK + 1), jax.random.fold_in(arg_keys[6], 1), BLK // 4, BLK).astype(jnp.int32),
    }


blocked_score = -1e+30

def lifted(array_in):
    return lax.optimization_barrier(array_in.astype(jnp.bfloat16)).astype(jnp.float32)

def window_parts(query_block, prev_keys, prev_values, grad_block, usable, window_width, temper):
    inverse_root = 1.0 / math.sqrt(HD)
    raw_scores = jnp.einsum('...td,...sd->...ts', query_block.astype(jnp.float32), prev_keys.astype(jnp.float32)) * inverse_root
    query_pos = lax.broadcasted_iota(jnp.int32, (BLK, BLK), 0)
    key_pos = lax.broadcasted_iota(jnp.int32, (BLK, BLK), 1)
    pair_mask = usable[..., None, None] & (key_pos > query_pos + BLK - window_width[..., None, None])
    scores = temper[..., None, None] * raw_scores
    row_top = lax.optimization_barrier(jnp.max(jnp.where(pair_mask, scores, blocked_score), axis=-1))
    weights = jnp.where(pair_mask, jnp.exp(scores - row_top[..., None]), 0.0)
    prob_grad = jnp.einsum('...td,...sd->...ts', grad_block.astype(jnp.float32), prev_values.astype(jnp.float32))
    return (raw_scores, pair_mask, prob_grad, row_top, lax.optimization_barrier(jnp.sum(weights, axis=-1)), lax.optimization_barrier(jnp.sum(weights * prob_grad, axis=-1)))

def window_grads(raw_scores, pair_mask, prob_grad, query_block, prev_keys, grad_block, log_total, row_delta, temper):
    inverse_root = 1.0 / math.sqrt(HD)
    scaling = (temper * inverse_root)[..., None, None]
    probability = jnp.where(pair_mask, jnp.exp(temper[..., None, None] * raw_scores - log_total[..., None]), 0.0)
    score_grad = probability * (prob_grad - row_delta[..., None])
    prob_low = lifted(probability)
    grad_low = lifted(score_grad)
    query_part = jnp.einsum('...ts,...sd->...td', grad_low, prev_keys.astype(jnp.float32)) * scaling
    key_part = jnp.einsum('...ts,...td->...sd', grad_low, query_block.astype(jnp.float32)) * scaling
    value_part = jnp.einsum('...ts,...td->...sd', prob_low, grad_block.astype(jnp.float32))
    temper_part = lax.optimization_barrier(jnp.sum(score_grad * raw_scores, axis=(-2, -1)))
    return (query_part, key_part, value_part, temper_part)

def cluster_pair(query_items, key_items, value_items, grad_items, live_items, temper, window_top, window_total, window_mass):
    row_count = MOST * BLK
    inverse_root = 1.0 / math.sqrt(HD)
    scaling = temper * inverse_root
    query_rows = query_items.reshape(row_count, HD)
    key_rows = key_items.reshape(row_count, HD)
    value_rows = value_items.reshape(row_count, HD)
    grad_rows = grad_items.reshape(row_count, HD)
    item_of = jnp.arange(row_count) // BLK
    token_of = jnp.arange(row_count) % BLK
    live_rows = jnp.repeat(live_items, BLK)
    earlier = (item_of[None, :] < item_of[:, None]) | (item_of[None, :] == item_of[:, None]) & (token_of[None, :] <= token_of[:, None])
    pair_mask = live_rows[:, None] & live_rows[None, :] & earlier
    top_rows = window_top.reshape(row_count)
    total_rows = window_total.reshape(row_count)
    mass_rows = window_mass.reshape(row_count)
    raw_scores = jnp.dot(query_rows, key_rows.T, preferred_element_type=jnp.float32) * inverse_root
    scores = temper * raw_scores
    row_top = jnp.maximum(lax.optimization_barrier(jnp.max(jnp.where(pair_mask, scores, blocked_score), axis=1)), top_rows)
    weights = jnp.where(pair_mask, jnp.exp(scores - row_top[:, None]), 0.0)
    row_total = lax.optimization_barrier(jnp.sum(weights, axis=1)) + total_rows * jnp.exp(top_rows - row_top)
    log_total = row_top + jnp.log(jnp.where(live_rows, row_total, 1.0))
    probability = jnp.where(pair_mask, jnp.exp(scores - log_total[:, None]), 0.0)
    prob_grad = jnp.dot(grad_rows, value_rows.T, preferred_element_type=jnp.float32)
    row_delta = lax.optimization_barrier(jnp.sum(probability * prob_grad, axis=1)) + mass_rows * jnp.exp(top_rows - log_total)
    score_grad = probability * (prob_grad - row_delta[:, None])
    prob_low = probability.astype(jnp.bfloat16)
    grad_low = score_grad.astype(jnp.bfloat16)
    query_part = jnp.dot(grad_low, key_rows, preferred_element_type=jnp.float32) * scaling
    key_part = jnp.dot(grad_low.T, query_rows, preferred_element_type=jnp.float32) * scaling
    value_part = jnp.dot(prob_low.T, grad_rows, preferred_element_type=jnp.float32)
    temper_part = jnp.sum(score_grad * raw_scores)
    return (query_part.reshape(MOST, BLK, HD), log_total.reshape(MOST, BLK), row_delta.reshape(MOST, BLK), key_part.reshape(MOST, BLK, HD), value_part.reshape(MOST, BLK, HD), temper_part)

def reference(probe_vectors, lookup_vectors, content_vectors, result_cotangent, logit_softness, block_grouping, neighborhood_span):

    def heads_first(array_in):
        return array_in.reshape(CORPUS_SIZE, NBLK, BLK, ATTENTION_SPLITS, HD).transpose(0, 3, 1, 2, 4).reshape(CORPUS_SIZE * ATTENTION_SPLITS, NBLK, BLK, HD)
    split_probes = heads_first(probe_vectors)
    split_lookups = heads_first(lookup_vectors)
    split_contents = heads_first(content_vectors)
    split_derivatives = heads_first(result_cotangent)
    split_numbers = block_grouping[..., 0].reshape(CORPUS_SIZE * ATTENTION_SPLITS, NBLK).astype(jnp.int32)
    split_softness = jnp.tile(logit_softness, CORPUS_SIZE)
    split_dimension = jnp.tile(neighborhood_span, CORPUS_SIZE).astype(jnp.int32)

    def single_split(head_inputs):
        query_h, key_h, value_h, grad_h, ids_h, temper, width_h = head_inputs
        empty = jnp.zeros((1, BLK, HD), query_h.dtype)
        prev_keys = jnp.concatenate([empty, key_h[:-1]], axis=0)
        prev_values = jnp.concatenate([empty, value_h[:-1]], axis=0)
        before = jnp.concatenate([jnp.full((1,), -1, jnp.int32), ids_h[:-1]])
        usable = (jnp.arange(NBLK) >= 1) & (before != ids_h)
        raw_w, mask_w, pgrad_w, top_w, total_w, mass_w = window_parts(query_h, prev_keys, prev_values, grad_h, usable, width_h, temper)

        def one_cluster(cluster):
            member = ids_h == cluster
            member_rank = jnp.cumsum(member.astype(jnp.int32)) - 1
            member_count = jnp.sum(member.astype(jnp.int32))
            picked = member[None, :] & (member_rank[None, :] == jnp.arange(MOST)[:, None])
            member_block = lax.optimization_barrier(jnp.sum(jnp.where(picked, jnp.arange(NBLK)[None, :], 0), axis=1)).astype(jnp.int32)
            live_items = jnp.arange(MOST) < member_count
            results = cluster_pair(query_h[member_block], key_h[member_block], value_h[member_block], grad_h[member_block], live_items, temper, top_w[member_block], total_w[member_block], mass_w[member_block])
            return results + (member_block, live_items)
        query_c, log_c, delta_c, key_c, value_c, temper_c, member_block, live_items = lax.map(one_cluster, jnp.arange(NC, dtype=jnp.int32))
        flat_block = member_block.reshape(-1)
        flat_live = live_items.reshape(-1)

        def spread(part):
            shaped = part.reshape((NC * MOST,) + part.shape[2:])
            chosen = jnp.where(flat_live.reshape((-1,) + (1,) * (shaped.ndim - 1)), shaped, 0.0)
            return jnp.zeros((NBLK,) + part.shape[2:], part.dtype).at[flat_block].add(chosen)
        query_cl = spread(query_c)
        log_total = spread(log_c)
        row_delta = spread(delta_c)
        key_cl = spread(key_c)
        value_cl = spread(value_c)
        query_w, key_w, value_w, temper_w = window_grads(raw_w, mask_w, pgrad_w, query_h, prev_keys, grad_h, log_total, row_delta, temper)
        tail_zero = jnp.zeros((1, BLK, HD), jnp.float32)
        key_next = jnp.concatenate([key_w[1:], tail_zero], axis=0)
        value_next = jnp.concatenate([value_w[1:], tail_zero], axis=0)
        query_out = (lifted(query_cl) + lifted(query_w)).astype(jnp.bfloat16)
        key_out = (lifted(key_cl) + lifted(key_next)).astype(jnp.bfloat16)
        value_out = (lifted(value_cl) + lifted(value_next)).astype(jnp.bfloat16)
        return (query_out, key_out, value_out, jnp.sum(temper_c) + jnp.sum(temper_w))
    derivative_wrt_probe, derivative_wrt_lookup, derivative_wrt_content, softness_accumulations = lax.map(single_split, (split_probes, split_lookups, split_contents, split_derivatives, split_numbers, split_softness, split_dimension))

    def tokens_first(array_in):
        return array_in.reshape(CORPUS_SIZE, ATTENTION_SPLITS, NBLK, BLK, HD).transpose(0, 2, 3, 1, 4).reshape(CORPUS_SIZE, SEQLEN, ATTENTION_SPLITS * HD)
    temper_grad = lax.optimization_barrier(jnp.sum(softness_accumulations.reshape(CORPUS_SIZE, ATTENTION_SPLITS), axis=0)) / (CORPUS_SIZE * SEQLEN)
    return (tokens_first(derivative_wrt_probe), tokens_first(derivative_wrt_lookup), tokens_first(derivative_wrt_content), temper_grad)
```

```python
import math

import jax
import jax.numpy as jnp
from jax import lax
from jax.experimental import pallas as pl
from jax.experimental.pallas import tpu as pltpu
from jax.sharding import PartitionSpec as P

HD = 128
BLK = 128


blocked_score = -1e30


def shifted(value, axis, steps):
    count = lax.axis_size(axis)
    first, last = (max(0, -steps), min(count, count - steps))
    return lax.ppermute(value, axis, [(source, source + steps) for source in range(first, last)])


def lifted(array_in):
    return lax.optimization_barrier(array_in.astype(jnp.bfloat16)).astype(jnp.float32)


def head_major(tokens_in, block_len):
    token_count, feature_count = tokens_in.shape
    return tokens_in.reshape(
        token_count // block_len, block_len, feature_count // HD, HD
    ).transpose(2, 0, 1, 3)


def token_major(blocks_in):
    head_count, block_count, block_len, depth = blocks_in.shape
    return blocks_in.transpose(1, 2, 0, 3).reshape(1, block_count * block_len, head_count * depth)


def window_parts(query_block, prev_keys, prev_values, grad_block, usable, window_width, temper):
    block_len = query_block.shape[-2]
    inverse_root = 1.0 / math.sqrt(query_block.shape[-1])
    raw_scores = (
        jnp.einsum("...td,...sd->...ts", query_block, prev_keys, preferred_element_type=jnp.float32)
        * inverse_root
    )
    query_pos = lax.broadcasted_iota(jnp.int32, (block_len, block_len), 0)
    key_pos = lax.broadcasted_iota(jnp.int32, (block_len, block_len), 1)
    pair_mask = usable[..., None, None] & (
        key_pos > query_pos + block_len - window_width[..., None, None]
    )
    scores = temper[..., None, None] * raw_scores
    row_top = jnp.max(jnp.where(pair_mask, scores, blocked_score), axis=-1)
    weights = jnp.where(pair_mask, jnp.exp(scores - row_top[..., None]), 0.0)
    prob_grad = jnp.einsum(
        "...td,...sd->...ts", grad_block, prev_values, preferred_element_type=jnp.float32
    )
    return (
        raw_scores,
        pair_mask,
        prob_grad,
        row_top,
        jnp.sum(weights, axis=-1),
        jnp.sum(weights * prob_grad, axis=-1),
    )


def window_grads(
    raw_scores,
    pair_mask,
    prob_grad,
    query_block,
    prev_keys,
    grad_block,
    log_total,
    row_delta,
    temper,
):
    inverse_root = 1.0 / math.sqrt(query_block.shape[-1])
    scaling = (temper * inverse_root)[..., None, None]
    probability = jnp.where(
        pair_mask, jnp.exp(temper[..., None, None] * raw_scores - log_total[..., None]), 0.0
    )
    score_grad = probability * (prob_grad - row_delta[..., None])
    prob_low = probability.astype(jnp.bfloat16)
    grad_low = score_grad.astype(jnp.bfloat16)
    query_part = (
        jnp.einsum("...ts,...sd->...td", grad_low, prev_keys, preferred_element_type=jnp.float32)
        * scaling
    )
    key_part = (
        jnp.einsum("...ts,...td->...sd", grad_low, query_block, preferred_element_type=jnp.float32)
        * scaling
    )
    value_part = jnp.einsum(
        "...ts,...td->...sd", prob_low, grad_block, preferred_element_type=jnp.float32
    )
    temper_part = jnp.sum(score_grad * raw_scores, axis=(-2, -1))
    return (query_part, key_part, value_part, temper_part)


def cluster_pair(
    query_items,
    key_items,
    value_items,
    grad_items,
    live_items,
    temper,
    window_top,
    window_total,
    window_mass,
):
    item_count, block_len, depth = query_items.shape
    row_count = item_count * block_len
    group_rows = 4 * block_len
    inverse_root = 1.0 / math.sqrt(depth)
    scaling = temper * inverse_root
    query_rows = query_items.reshape(row_count, depth)
    key_rows = key_items.reshape(row_count, depth)
    value_rows = value_items.reshape(row_count, depth)
    grad_rows = grad_items.reshape(row_count, depth)
    key_item = jnp.arange(row_count) // block_len
    key_token = jnp.arange(row_count) % block_len
    live_rows = jnp.repeat(live_items, block_len)
    top_rows = window_top.reshape(row_count)
    total_rows = window_total.reshape(row_count)
    mass_rows = window_mass.reshape(row_count)

    def group_step(carry, start_row):
        key_acc, value_acc, temper_acc = carry
        query_group = lax.dynamic_slice_in_dim(query_rows, start_row, group_rows, 0)
        grad_group = lax.dynamic_slice_in_dim(grad_rows, start_row, group_rows, 0)
        group_live = lax.dynamic_slice_in_dim(live_rows, start_row, group_rows, 0)
        group_top = lax.dynamic_slice_in_dim(top_rows, start_row, group_rows, 0)
        group_total = lax.dynamic_slice_in_dim(total_rows, start_row, group_rows, 0)
        group_mass = lax.dynamic_slice_in_dim(mass_rows, start_row, group_rows, 0)
        query_item = (start_row + jnp.arange(group_rows)) // block_len
        query_token = jnp.arange(group_rows) % block_len
        earlier = (key_item[None, :] < query_item[:, None]) | (
            key_item[None, :] == query_item[:, None]
        ) & (key_token[None, :] <= query_token[:, None])
        pair_mask = group_live[:, None] & live_rows[None, :] & earlier
        raw_scores = (
            lax.dot_general(
                query_group, key_rows, (((1,), (1,)), ((), ())), preferred_element_type=jnp.float32
            )
            * inverse_root
        )
        scores = temper * raw_scores
        row_top = jnp.maximum(
            jnp.max(jnp.where(pair_mask, scores, blocked_score), axis=1), group_top
        )
        weights = jnp.where(pair_mask, jnp.exp(scores - row_top[:, None]), 0.0)
        row_total = jnp.sum(weights, axis=1) + group_total * jnp.exp(group_top - row_top)
        log_total = row_top + jnp.log(jnp.where(group_live, row_total, 1.0))
        probability = jnp.where(pair_mask, jnp.exp(scores - log_total[:, None]), 0.0)
        prob_grad = lax.dot_general(
            grad_group, value_rows, (((1,), (1,)), ((), ())), preferred_element_type=jnp.float32
        )
        row_delta = jnp.sum(probability * prob_grad, axis=1) + group_mass * jnp.exp(
            group_top - log_total
        )
        score_grad = probability * (prob_grad - row_delta[:, None])
        prob_low = probability.astype(jnp.bfloat16)
        grad_low = score_grad.astype(jnp.bfloat16)
        query_part = jnp.dot(grad_low, key_rows, preferred_element_type=jnp.float32) * scaling
        key_acc = (
            key_acc
            + lax.dot_general(
                grad_low, query_group, (((0,), (0,)), ((), ())), preferred_element_type=jnp.float32
            )
            * scaling
        )
        value_acc = value_acc + lax.dot_general(
            prob_low, grad_group, (((0,), (0,)), ((), ())), preferred_element_type=jnp.float32
        )
        temper_acc = temper_acc + jnp.sum(score_grad * raw_scores)
        return ((key_acc, value_acc, temper_acc), (query_part, log_total, row_delta))

    start_rows = jnp.arange(item_count // 4) * group_rows
    initial = (
        jnp.zeros((row_count, depth), jnp.float32),
        jnp.zeros((row_count, depth), jnp.float32),
        jnp.zeros((), jnp.float32),
    )
    (key_acc, value_acc, temper_acc), (query_part, log_total, row_delta) = lax.scan(
        group_step, initial, start_rows
    )
    return (
        query_part.reshape(item_count, block_len, depth),
        log_total.reshape(item_count, block_len),
        row_delta.reshape(item_count, block_len),
        key_acc.reshape(item_count, block_len, depth),
        value_acc.reshape(item_count, block_len, depth),
        temper_acc,
    )


def clustered_shards(
    probe_vectors,
    lookup_vectors,
    content_vectors,
    result_cotangent,
    logit_softness,
    block_grouping,
    neighborhood_span,
):
    seq_count = lax.axis_size("seq")
    position = lax.axis_index("seq")
    tokens = probe_vectors.shape[1]
    head_count = probe_vectors.shape[2] // HD
    local_blocks = tokens // BLK
    block_count = local_blocks * seq_count
    cluster_count = max(1, block_count // 8)
    capacity = min(12, block_count)
    owned_pairs = cluster_count * head_count // seq_count
    group_count = cluster_count // owned_pairs
    per_peer = max(1, local_blocks // group_count)
    cluster_ids = block_grouping[0, :, :, 0]
    query_home = head_major(probe_vectors[0], BLK)
    key_home = head_major(lookup_vectors[0], BLK)
    value_home = head_major(content_vectors[0], BLK)
    grad_home = head_major(result_cotangent[0], BLK)
    last_block = (lookup_vectors[0, tokens - BLK :], content_vectors[0, tokens - BLK :])
    prev_key_rows, prev_value_rows = shifted((last_block[0], last_block[1]), "seq", 1)
    prev_keys = jnp.concatenate([head_major(prev_key_rows, BLK), key_home[:, :-1]], axis=1)
    prev_values = jnp.concatenate([head_major(prev_value_rows, BLK), value_home[:, :-1]], axis=1)
    first_block = position * local_blocks
    before = jnp.concatenate(
        [jnp.full((head_count, 1), -1, jnp.int32), cluster_ids[:, :-1]], axis=1
    )
    my_ids = lax.dynamic_slice_in_dim(cluster_ids, first_block, local_blocks, 1)
    my_before = lax.dynamic_slice_in_dim(before, first_block, local_blocks, 1)
    global_block = first_block + jnp.arange(local_blocks)
    usable_home = (global_block[None, :] >= 1) & (my_before != my_ids)
    peer_index = jnp.arange(seq_count)
    peer_head = peer_index * owned_pairs // cluster_count
    slot_range = jnp.arange(per_peer)
    local_range = jnp.arange(local_blocks)
    owner_index = (jnp.arange(head_count)[:, None] * cluster_count + my_ids) // owned_pairs
    peer_ids = jnp.take(my_ids, peer_head, axis=0)
    goes = (peer_head[:, None] * cluster_count + peer_ids) // owned_pairs == peer_index[:, None]
    send_rank = jnp.cumsum(goes.astype(jnp.int32), axis=1) - 1
    send_pick = goes[:, None, :] & (send_rank[:, None, :] == slot_range[None, :, None])
    send_block = jnp.sum(jnp.where(send_pick, local_range[None, None, :], 0), axis=2)
    send_flat = peer_head[:, None] * local_blocks + send_block
    home_rank = jnp.take_along_axis(send_rank, owner_index, axis=0)
    home_pos = owner_index * per_peer + home_rank
    pair_index = position * owned_pairs + jnp.arange(owned_pairs)
    split_for_couple = pair_index // cluster_count
    pair_cluster = pair_index % cluster_count
    my_head = position * owned_pairs // cluster_count
    split_numbers = jnp.take(cluster_ids, my_head, axis=0)
    member = split_numbers[None, :] == pair_cluster[:, None]
    member_rank = jnp.cumsum(member.astype(jnp.int32), axis=1) - 1
    member_count = jnp.sum(member.astype(jnp.int32), axis=1)
    picked = member[:, None, :] & (member_rank[:, None, :] == jnp.arange(capacity)[None, :, None])
    member_block = jnp.sum(jnp.where(picked, jnp.arange(block_count)[None, None, :], 0), axis=2)
    live_members = jnp.arange(capacity)[None, :] < member_count[:, None]
    mine = (my_head * cluster_count + split_numbers) // owned_pairs == position
    mine_grid = mine.reshape(seq_count, local_blocks)
    recv_rank = jnp.cumsum(mine_grid.astype(jnp.int32), axis=1) - 1
    recv_pos = (peer_index[:, None] * per_peer + recv_rank).reshape(block_count)
    member_pos = jnp.take(recv_pos, member_block)
    couple_softness = jnp.take(logit_softness, split_for_couple)
    pair_onehot = (split_for_couple[:, None] == jnp.arange(head_count)[None, :]).astype(jnp.float32)
    slot_pair = my_head * cluster_count + split_numbers - position * owned_pairs
    same_cluster = split_numbers[:, None] == split_numbers[None, :]
    earlier_block = jnp.arange(block_count)[None, :] < jnp.arange(block_count)[:, None]
    slot_rank = jnp.sum((same_cluster & earlier_block).astype(jnp.int32), axis=1)
    back_pos = jnp.clip(slot_pair, 0, owned_pairs - 1) * capacity + jnp.clip(
        slot_rank, 0, capacity - 1
    )
    back_grid = back_pos.reshape(seq_count, local_blocks)
    back_pick = mine_grid[:, None, :] & (recv_rank[:, None, :] == slot_range[None, :, None])
    back_flat = jnp.sum(jnp.where(back_pick, back_grid[:, None, :], 0), axis=2)

    def to_peers(array_in):
        flat = array_in.reshape((head_count * local_blocks,) + array_in.shape[2:])
        return jnp.take(flat, send_flat, axis=0)

    def members(array_in):
        flat = array_in.reshape((seq_count * per_peer,) + array_in.shape[2:])
        return jnp.take(flat, member_pos, axis=0)

    def to_owner(array_in):
        flat = array_in.reshape((owned_pairs * capacity,) + array_in.shape[2:])
        return jnp.take(flat, back_flat, axis=0)

    def from_peers(array_in):
        flat = array_in.reshape((seq_count * per_peer,) + array_in.shape[2:])
        return jnp.take(flat, home_pos, axis=0)

    raw_w, mask_w, pgrad_w, top_w, total_w, mass_w = window_parts(
        query_home,
        prev_keys,
        prev_values,
        grad_home,
        usable_home,
        neighborhood_span[:, None],
        logit_softness[:, None],
    )
    arrived = (
        lax.all_to_all(to_peers(query_home), "seq", split_axis=0, concat_axis=0, tiled=True),
        lax.all_to_all(to_peers(key_home), "seq", split_axis=0, concat_axis=0, tiled=True),
        lax.all_to_all(to_peers(value_home), "seq", split_axis=0, concat_axis=0, tiled=True),
        lax.all_to_all(to_peers(grad_home), "seq", split_axis=0, concat_axis=0, tiled=True),
    )
    arrived_stats = (
        lax.all_to_all(to_peers(top_w), "seq", split_axis=0, concat_axis=0, tiled=True),
        lax.all_to_all(to_peers(total_w), "seq", split_axis=0, concat_axis=0, tiled=True),
        lax.all_to_all(to_peers(mass_w), "seq", split_axis=0, concat_axis=0, tiled=True),
    )
    query_m, key_m, value_m, grad_m = [members(item_in) for item_in in arrived]
    top_m, total_m, mass_m = [members(item_in) for item_in in arrived_stats]

    def split_pair(pair_inputs):
        query_i, key_i, value_i, grad_i, live_i, temper_i, top_i, total_i, mass_i = pair_inputs
        query_c, log_total, row_delta, key_c, value_c, temper_c = cluster_pair(
            query_i, key_i, value_i, grad_i, live_i, temper_i, top_i, total_i, mass_i
        )
        return (
            query_c.astype(jnp.bfloat16),
            key_c.astype(jnp.bfloat16),
            value_c.astype(jnp.bfloat16),
            log_total,
            row_delta,
            temper_c,
        )

    owner_results = lax.map(
        split_pair,
        (query_m, key_m, value_m, grad_m, live_members, couple_softness, top_m, total_m, mass_m),
    )
    returned = (
        lax.all_to_all(to_owner(owner_results[0]), "seq", split_axis=0, concat_axis=0, tiled=True),
        lax.all_to_all(to_owner(owner_results[1]), "seq", split_axis=0, concat_axis=0, tiled=True),
        lax.all_to_all(to_owner(owner_results[2]), "seq", split_axis=0, concat_axis=0, tiled=True),
    )
    returned_stats = (
        lax.all_to_all(to_owner(owner_results[3]), "seq", split_axis=0, concat_axis=0, tiled=True),
        lax.all_to_all(to_owner(owner_results[4]), "seq", split_axis=0, concat_axis=0, tiled=True),
    )
    query_cluster = from_peers(returned[0])
    key_cluster = from_peers(returned[1])
    value_cluster = from_peers(returned[2])
    log_home = from_peers(returned_stats[0])
    delta_home = from_peers(returned_stats[1])
    query_w, key_w, value_w, temper_w = window_grads(
        raw_w,
        mask_w,
        pgrad_w,
        query_home,
        prev_keys,
        grad_home,
        log_home,
        delta_home,
        logit_softness[:, None],
    )
    query_out = (query_cluster.astype(jnp.float32) + lifted(query_w)).astype(jnp.bfloat16)
    key_window = key_w.astype(jnp.bfloat16)
    value_window = value_w.astype(jnp.bfloat16)
    temper_local = jnp.sum(owner_results[5][:, None] * pair_onehot, axis=0) + jnp.sum(
        temper_w, axis=1
    )
    edge_keys, edge_values = shifted((key_window[:, 0], value_window[:, 0]), "seq", -1)
    key_next = jnp.concatenate([key_window[:, 1:], edge_keys[:, None]], axis=1)
    value_next = jnp.concatenate([value_window[:, 1:], edge_values[:, None]], axis=1)
    key_out = (key_cluster.astype(jnp.float32) + key_next.astype(jnp.float32)).astype(jnp.bfloat16)
    value_out = (value_cluster.astype(jnp.float32) + value_next.astype(jnp.float32)).astype(
        jnp.bfloat16
    )
    temper_total = lax.psum(temper_local, ("seq", "dp"))
    temper_grad = temper_total / (lax.axis_size("dp") * tokens * seq_count)
    return (token_major(query_out), token_major(key_out), token_major(value_out), temper_grad)


TILE = 256
EXTRA = 16
VMEM_LIMIT = 56 * 1024 * 1024


def pack_kernel(*refs):
    arrays, packed_ref = refs[:-1], refs[-1]
    for place, array_ref in enumerate(arrays):
        for head in range(packed_ref.shape[0]):
            packed_ref[head, place * BLK : (place + 1) * BLK, :] = array_ref[
                0, :, head * HD : (head + 1) * HD
            ]


def packed(*arrays):
    head_count = arrays[0].shape[2] // HD
    out_shape = (head_count, len(arrays) * BLK, HD)
    return pl.pallas_call(
        pack_kernel,
        out_shape=jax.ShapeDtypeStruct(out_shape, jnp.bfloat16),
        cost_estimate=pl.CostEstimate(
            flops=0, bytes_accessed=4 * math.prod(out_shape), transcendentals=0
        ),
        compiler_params=pltpu.CompilerParams(vmem_limit_bytes=VMEM_LIMIT),
        name="pack_heads",
    )(*arrays)


def unpack_kernel(packed_ref, *out_refs):
    for place, out_ref in enumerate(out_refs):
        for head in range(packed_ref.shape[0]):
            out_ref[0, :, head * HD : (head + 1) * HD] = packed_ref[
                head, place * BLK : (place + 1) * BLK, :
            ]


def unpacked(array_in, count):
    head_count = array_in.shape[0]
    out_shape = (1, BLK, head_count * HD)
    return pl.pallas_call(
        unpack_kernel,
        out_shape=[jax.ShapeDtypeStruct(out_shape, jnp.bfloat16)] * count,
        cost_estimate=pl.CostEstimate(
            flops=0, bytes_accessed=4 * count * math.prod(out_shape), transcendentals=0
        ),
        compiler_params=pltpu.CompilerParams(vmem_limit_bytes=VMEM_LIMIT),
        name="unpack_heads",
    )(array_in)


def allowed_scores(scores, tile_key, tile_query, ids_ref, head, width):
    per_tile = TILE // BLK
    spread = lax.broadcasted_iota(jnp.int32, (BLK, BLK), 0) - lax.broadcasted_iota(
        jnp.int32, (BLK, BLK), 1
    )
    rows = []
    for sub_key in range(per_tile):
        pieces = []
        block_key = tile_key * per_tile + sub_key
        for sub_query in range(per_tile):
            block_query = tile_query * per_tile + sub_query
            piece = scores[
                sub_key * BLK : (sub_key + 1) * BLK, sub_query * BLK : (sub_query + 1) * BLK
            ]
            same = ids_ref[head, block_key] == ids_ref[head, block_query]
            if block_key > block_query:
                piece = jnp.full_like(piece, blocked_score)
            elif block_key == block_query:
                piece = jnp.where(spread <= 0, piece, blocked_score)
            elif block_key == block_query - 1:
                least = jnp.where(same, -BLK, BLK - width)
                piece = jnp.where(spread > least, piece, blocked_score)
            else:
                piece = jnp.where(spread > jnp.where(same, -BLK, BLK), piece, blocked_score)
            pieces.append(piece)
        rows.append(jnp.concatenate(pieces, axis=1))
    return jnp.concatenate(rows, axis=0)


def dot_rows(left, right):
    return lax.dot_general(
        left, right, (((1,), (1,)), ((), ())), preferred_element_type=jnp.float32
    )


def dot_plain(left, right):
    return lax.dot_general(
        left, right, (((1,), (0,)), ((), ())), preferred_element_type=jnp.float32
    )


def attention_kernel(
    softness_ref, ids_ref, span_ref, in_ref, out_ref,
    query, key, value, grad, key_across, score, gradient, prob_low, grad_low,
):
    head = lax.axis_index("seq")
    blocks = in_ref.shape[0]
    tiles = blocks * BLK // TILE
    temper = softness_ref[head]
    width = span_ref[head]
    scaling = temper * (1.0 / math.sqrt(HD))
    to_log2 = scaling * math.log2(math.e)
    for block in range(blocks):
        rows = slice(block * BLK, (block + 1) * BLK)
        query[rows, :] = in_ref[block, 0 * BLK : 1 * BLK, :]
        key[rows, :] = in_ref[block, 1 * BLK : 2 * BLK, :]
        value[rows, :] = in_ref[block, 2 * BLK : 3 * BLK, :]
        grad[rows, :] = in_ref[block, 3 * BLK : 4 * BLK, :]
        key_across[:, rows] = in_ref[block, 1 * BLK : 2 * BLK, :].T
    temper_rows = jnp.zeros((1, HD), jnp.float32)
    for tile in range(tiles):
        here = slice(tile * TILE, (tile + 1) * TILE)
        top = jnp.full((1, TILE), blocked_score, jnp.float32)
        for other in range(tile + 1):
            there = slice(other * TILE, (other + 1) * TILE)
            raw = dot_rows(key[there, :], query[here, :]) * to_log2
            raw = allowed_scores(raw, other, tile, ids_ref, head, width)
            score[there, :] = raw
            top = jnp.maximum(top, jnp.max(raw, axis=0, keepdims=True))
        total = jnp.zeros((1, TILE), jnp.float32)
        mass = jnp.zeros((1, TILE), jnp.float32)
        for other in range(tile + 1):
            there = slice(other * TILE, (other + 1) * TILE)
            weight = jnp.exp2(score[there, :] - top)
            towards = dot_rows(value[there, :], grad[here, :])
            score[there, :] = weight
            gradient[there, :] = towards
            total += jnp.sum(weight, axis=0, keepdims=True)
            mass += jnp.sum(weight * towards, axis=0, keepdims=True)
        inverse = 1.0 / total
        delta = mass * inverse
        for other in range(tile + 1):
            there = slice(other * TILE, (other + 1) * TILE)
            probability = score[there, :] * inverse
            prob_low[there, here] = probability.astype(jnp.bfloat16)
            grad_low[there, here] = (probability * (gradient[there, :] - delta)).astype(
                jnp.bfloat16
            )
        upto = slice(0, (tile + 1) * TILE)
        query_part = dot_plain(key_across[:, upto], grad_low[upto, here]).T
        temper_rows += jnp.sum(
            query_part * query[here, :].astype(jnp.float32), axis=0, keepdims=True
        )
        query_part = (query_part * scaling).astype(jnp.bfloat16)
        for sub in range(TILE // BLK):
            out_ref[tile * (TILE // BLK) + sub, 0:BLK, :] = query_part[
                sub * BLK : (sub + 1) * BLK, :
            ]
    for tile in range(tiles):
        here = slice(tile * TILE, (tile + 1) * TILE)
        onward = slice(tile * TILE, tiles * TILE)
        key_part = (dot_plain(grad_low[here, onward], query[onward, :]) * scaling).astype(
            jnp.bfloat16
        )
        value_part = dot_plain(prob_low[here, onward], grad[onward, :]).astype(jnp.bfloat16)
        for sub in range(TILE // BLK):
            block = tile * (TILE // BLK) + sub
            part = slice(sub * BLK, (sub + 1) * BLK)
            out_ref[block, BLK : 2 * BLK, :] = key_part[part, :]
            out_ref[block, 2 * BLK : 3 * BLK, :] = value_part[part, :]
    temper_sum = jnp.sum(temper_rows, axis=1, keepdims=True) * (1.0 / math.sqrt(HD))
    spread = jnp.broadcast_to(temper_sum, (EXTRA, HD))
    high = spread.astype(jnp.bfloat16).astype(jnp.float32)
    middle = (spread - high).astype(jnp.bfloat16).astype(jnp.float32)
    low = spread - high - middle
    row = lax.broadcasted_iota(jnp.int32, (EXTRA, HD), 0)
    pieces = jnp.where(row == 0, high, jnp.where(row == 1, middle, low)).astype(jnp.bfloat16)
    for block in range(blocks):
        out_ref[block, 3 * BLK : 3 * BLK + EXTRA, :] = pieces


def attention(softness, ids, span, arrived):
    blocks = arrived.shape[0]
    length = blocks * BLK
    out_shape = (blocks, 3 * BLK + EXTRA, HD)
    smem = pl.BlockSpec(memory_space=pltpu.SMEM)
    vmem = pl.BlockSpec(memory_space=pltpu.VMEM)
    return pl.pallas_call(
        attention_kernel,
        out_shape=jax.ShapeDtypeStruct(out_shape, jnp.bfloat16),
        in_specs=[smem, smem, smem, vmem],
        out_specs=vmem,
        scratch_shapes=[
            pltpu.VMEM((length, HD), jnp.bfloat16),
            pltpu.VMEM((length, HD), jnp.bfloat16),
            pltpu.VMEM((length, HD), jnp.bfloat16),
            pltpu.VMEM((length, HD), jnp.bfloat16),
            pltpu.VMEM((HD, length), jnp.bfloat16),
            pltpu.VMEM((length, TILE), jnp.float32),
            pltpu.VMEM((length, TILE), jnp.float32),
            pltpu.VMEM((length, length), jnp.bfloat16),
            pltpu.VMEM((length, length), jnp.bfloat16),
        ],
        cost_estimate=pl.CostEstimate(
            flops=5 * length * length * HD,
            bytes_accessed=2 * (math.prod(out_shape) + math.prod(arrived.shape)),
            transcendentals=length * length // 2,
        ),
        compiler_params=pltpu.CompilerParams(vmem_limit_bytes=VMEM_LIMIT),
        name="head_attention",
    )(softness, ids, span, arrived)


def head_shards(
    probe_vectors,
    lookup_vectors,
    content_vectors,
    result_cotangent,
    logit_softness,
    block_grouping,
    neighborhood_span,
):
    ids = block_grouping[0, :, :, 0]
    dp_count = lax.axis_size("dp")
    sent = packed(probe_vectors, lookup_vectors, content_vectors, result_cotangent)
    arrived = lax.all_to_all(sent, "seq", split_axis=0, concat_axis=0, tiled=True)
    owned = attention(logit_softness, ids, neighborhood_span, arrived)
    back = lax.all_to_all(owned, "seq", split_axis=0, concat_axis=0, tiled=True)
    pieces = back[:, 3 * BLK : 3 * BLK + 3, 0].astype(jnp.float32)
    temper_local = jnp.sum(pieces, axis=1)
    temper_total = temper_local
    for step in range(1, dp_count):
        pairs = [(source, (source + step) % dp_count) for source in range(dp_count)]
        temper_total = temper_total + lax.ppermute(temper_local, "dp", pairs)
    outs = unpacked(back, 3)
    tokens = probe_vectors.shape[1] * lax.axis_size("seq")
    return (*outs, temper_total / (dp_count * tokens))


def shards(
    probe_vectors,
    lookup_vectors,
    content_vectors,
    result_cotangent,
    logit_softness,
    block_grouping,
    neighborhood_span,
):
    head_count = probe_vectors.shape[2] // HD
    one_block = probe_vectors.shape[1] == BLK
    if head_count == lax.axis_size("seq") and one_block:
        plan = head_shards
    else:
        plan = clustered_shards
    return plan(
        probe_vectors,
        lookup_vectors,
        content_vectors,
        result_cotangent,
        logit_softness,
        block_grouping,
        neighborhood_span,
    )


def solution(mesh):
    in_specs = (
        P("dp", "seq", None),
        P("dp", "seq", None),
        P("dp", "seq", None),
        P("dp", "seq", None),
        P(),
        P("dp", None, None, None),
        P(),
    )
    out_specs = (P("dp", "seq", None), P("dp", "seq", None), P("dp", "seq", None), P())
    return jax.shard_map(shards, mesh=mesh, in_specs=in_specs, out_specs=out_specs, check_vma=False)
```

```python
import functools
import math

import jax
import jax.numpy as jnp
from jax import lax
from jax.experimental import pallas as pl
from jax.experimental.pallas import tpu as pltpu
from jax.sharding import PartitionSpec as P

HD = 128
BLK = 128


blocked_score = -1e30


def shifted(value, axis, steps):
    count = lax.axis_size(axis)
    first, last = (max(0, -steps), min(count, count - steps))
    return lax.ppermute(value, axis, [(source, source + steps) for source in range(first, last)])


def lifted(array_in):
    return lax.optimization_barrier(array_in.astype(jnp.bfloat16)).astype(jnp.float32)


def head_major(tokens_in, block_len):
    token_count, feature_count = tokens_in.shape
    return tokens_in.reshape(
        token_count // block_len, block_len, feature_count // HD, HD
    ).transpose(2, 0, 1, 3)


def token_major(blocks_in):
    head_count, block_count, block_len, depth = blocks_in.shape
    return blocks_in.transpose(1, 2, 0, 3).reshape(1, block_count * block_len, head_count * depth)


def window_parts(query_block, prev_keys, prev_values, grad_block, usable, window_width, temper):
    block_len = query_block.shape[-2]
    inverse_root = 1.0 / math.sqrt(query_block.shape[-1])
    raw_scores = (
        jnp.einsum("...td,...sd->...ts", query_block, prev_keys, preferred_element_type=jnp.float32)
        * inverse_root
    )
    query_pos = lax.broadcasted_iota(jnp.int32, (block_len, block_len), 0)
    key_pos = lax.broadcasted_iota(jnp.int32, (block_len, block_len), 1)
    pair_mask = usable[..., None, None] & (
        key_pos > query_pos + block_len - window_width[..., None, None]
    )
    scores = temper[..., None, None] * raw_scores
    row_top = jnp.max(jnp.where(pair_mask, scores, blocked_score), axis=-1)
    weights = jnp.where(pair_mask, jnp.exp(scores - row_top[..., None]), 0.0)
    prob_grad = jnp.einsum(
        "...td,...sd->...ts", grad_block, prev_values, preferred_element_type=jnp.float32
    )
    return (
        raw_scores,
        pair_mask,
        prob_grad,
        row_top,
        jnp.sum(weights, axis=-1),
        jnp.sum(weights * prob_grad, axis=-1),
    )


def window_grads(
    raw_scores,
    pair_mask,
    prob_grad,
    query_block,
    prev_keys,
    grad_block,
    log_total,
    row_delta,
    temper,
):
    inverse_root = 1.0 / math.sqrt(query_block.shape[-1])
    scaling = (temper * inverse_root)[..., None, None]
    probability = jnp.where(
        pair_mask, jnp.exp(temper[..., None, None] * raw_scores - log_total[..., None]), 0.0
    )
    score_grad = probability * (prob_grad - row_delta[..., None])
    prob_low = probability.astype(jnp.bfloat16)
    grad_low = score_grad.astype(jnp.bfloat16)
    query_part = (
        jnp.einsum("...ts,...sd->...td", grad_low, prev_keys, preferred_element_type=jnp.float32)
        * scaling
    )
    key_part = (
        jnp.einsum("...ts,...td->...sd", grad_low, query_block, preferred_element_type=jnp.float32)
        * scaling
    )
    value_part = jnp.einsum(
        "...ts,...td->...sd", prob_low, grad_block, preferred_element_type=jnp.float32
    )
    temper_part = jnp.sum(score_grad * raw_scores, axis=(-2, -1))
    return (query_part, key_part, value_part, temper_part)


def cluster_pair(
    query_items,
    key_items,
    value_items,
    grad_items,
    live_items,
    temper,
    window_top,
    window_total,
    window_mass,
):
    item_count, block_len, depth = query_items.shape
    row_count = item_count * block_len
    group_rows = 4 * block_len
    inverse_root = 1.0 / math.sqrt(depth)
    scaling = temper * inverse_root
    query_rows = query_items.reshape(row_count, depth)
    key_rows = key_items.reshape(row_count, depth)
    value_rows = value_items.reshape(row_count, depth)
    grad_rows = grad_items.reshape(row_count, depth)
    key_item = jnp.arange(row_count) // block_len
    key_token = jnp.arange(row_count) % block_len
    live_rows = jnp.repeat(live_items, block_len)
    top_rows = window_top.reshape(row_count)
    total_rows = window_total.reshape(row_count)
    mass_rows = window_mass.reshape(row_count)

    def group_step(carry, start_row):
        key_acc, value_acc, temper_acc = carry
        query_group = lax.dynamic_slice_in_dim(query_rows, start_row, group_rows, 0)
        grad_group = lax.dynamic_slice_in_dim(grad_rows, start_row, group_rows, 0)
        group_live = lax.dynamic_slice_in_dim(live_rows, start_row, group_rows, 0)
        group_top = lax.dynamic_slice_in_dim(top_rows, start_row, group_rows, 0)
        group_total = lax.dynamic_slice_in_dim(total_rows, start_row, group_rows, 0)
        group_mass = lax.dynamic_slice_in_dim(mass_rows, start_row, group_rows, 0)
        query_item = (start_row + jnp.arange(group_rows)) // block_len
        query_token = jnp.arange(group_rows) % block_len
        earlier = (key_item[None, :] < query_item[:, None]) | (
            key_item[None, :] == query_item[:, None]
        ) & (key_token[None, :] <= query_token[:, None])
        pair_mask = group_live[:, None] & live_rows[None, :] & earlier
        raw_scores = (
            lax.dot_general(
                query_group, key_rows, (((1,), (1,)), ((), ())), preferred_element_type=jnp.float32
            )
            * inverse_root
        )
        scores = temper * raw_scores
        row_top = jnp.maximum(
            jnp.max(jnp.where(pair_mask, scores, blocked_score), axis=1), group_top
        )
        weights = jnp.where(pair_mask, jnp.exp(scores - row_top[:, None]), 0.0)
        row_total = jnp.sum(weights, axis=1) + group_total * jnp.exp(group_top - row_top)
        log_total = row_top + jnp.log(jnp.where(group_live, row_total, 1.0))
        probability = jnp.where(pair_mask, jnp.exp(scores - log_total[:, None]), 0.0)
        prob_grad = lax.dot_general(
            grad_group, value_rows, (((1,), (1,)), ((), ())), preferred_element_type=jnp.float32
        )
        row_delta = jnp.sum(probability * prob_grad, axis=1) + group_mass * jnp.exp(
            group_top - log_total
        )
        score_grad = probability * (prob_grad - row_delta[:, None])
        prob_low = probability.astype(jnp.bfloat16)
        grad_low = score_grad.astype(jnp.bfloat16)
        query_part = jnp.dot(grad_low, key_rows, preferred_element_type=jnp.float32) * scaling
        key_acc = (
            key_acc
            + lax.dot_general(
                grad_low, query_group, (((0,), (0,)), ((), ())), preferred_element_type=jnp.float32
            )
            * scaling
        )
        value_acc = value_acc + lax.dot_general(
            prob_low, grad_group, (((0,), (0,)), ((), ())), preferred_element_type=jnp.float32
        )
        temper_acc = temper_acc + jnp.sum(score_grad * raw_scores)
        return ((key_acc, value_acc, temper_acc), (query_part, log_total, row_delta))

    start_rows = jnp.arange(item_count // 4) * group_rows
    initial = (
        jnp.zeros((row_count, depth), jnp.float32),
        jnp.zeros((row_count, depth), jnp.float32),
        jnp.zeros((), jnp.float32),
    )
    (key_acc, value_acc, temper_acc), (query_part, log_total, row_delta) = lax.scan(
        group_step, initial, start_rows
    )
    return (
        query_part.reshape(item_count, block_len, depth),
        log_total.reshape(item_count, block_len),
        row_delta.reshape(item_count, block_len),
        key_acc.reshape(item_count, block_len, depth),
        value_acc.reshape(item_count, block_len, depth),
        temper_acc,
    )


def clustered_shards(
    probe_vectors,
    lookup_vectors,
    content_vectors,
    result_cotangent,
    logit_softness,
    block_grouping,
    neighborhood_span,
):
    seq_count = lax.axis_size("seq")
    position = lax.axis_index("seq")
    tokens = probe_vectors.shape[1]
    head_count = probe_vectors.shape[2] // HD
    local_blocks = tokens // BLK
    block_count = local_blocks * seq_count
    cluster_count = max(1, block_count // 8)
    capacity = min(12, block_count)
    owned_pairs = cluster_count * head_count // seq_count
    group_count = cluster_count // owned_pairs
    per_peer = max(1, local_blocks // group_count)
    cluster_ids = block_grouping[0, :, :, 0]
    query_home = head_major(probe_vectors[0], BLK)
    key_home = head_major(lookup_vectors[0], BLK)
    value_home = head_major(content_vectors[0], BLK)
    grad_home = head_major(result_cotangent[0], BLK)
    last_block = (lookup_vectors[0, tokens - BLK :], content_vectors[0, tokens - BLK :])
    prev_key_rows, prev_value_rows = shifted((last_block[0], last_block[1]), "seq", 1)
    prev_keys = jnp.concatenate([head_major(prev_key_rows, BLK), key_home[:, :-1]], axis=1)
    prev_values = jnp.concatenate([head_major(prev_value_rows, BLK), value_home[:, :-1]], axis=1)
    first_block = position * local_blocks
    before = jnp.concatenate(
        [jnp.full((head_count, 1), -1, jnp.int32), cluster_ids[:, :-1]], axis=1
    )
    my_ids = lax.dynamic_slice_in_dim(cluster_ids, first_block, local_blocks, 1)
    my_before = lax.dynamic_slice_in_dim(before, first_block, local_blocks, 1)
    global_block = first_block + jnp.arange(local_blocks)
    usable_home = (global_block[None, :] >= 1) & (my_before != my_ids)
    peer_index = jnp.arange(seq_count)
    peer_head = peer_index * owned_pairs // cluster_count
    slot_range = jnp.arange(per_peer)
    local_range = jnp.arange(local_blocks)
    owner_index = (jnp.arange(head_count)[:, None] * cluster_count + my_ids) // owned_pairs
    peer_ids = jnp.take(my_ids, peer_head, axis=0)
    goes = (peer_head[:, None] * cluster_count + peer_ids) // owned_pairs == peer_index[:, None]
    send_rank = jnp.cumsum(goes.astype(jnp.int32), axis=1) - 1
    send_pick = goes[:, None, :] & (send_rank[:, None, :] == slot_range[None, :, None])
    send_block = jnp.sum(jnp.where(send_pick, local_range[None, None, :], 0), axis=2)
    send_flat = peer_head[:, None] * local_blocks + send_block
    home_rank = jnp.take_along_axis(send_rank, owner_index, axis=0)
    home_pos = owner_index * per_peer + home_rank
    pair_index = position * owned_pairs + jnp.arange(owned_pairs)
    split_for_couple = pair_index // cluster_count
    pair_cluster = pair_index % cluster_count
    my_head = position * owned_pairs // cluster_count
    split_numbers = jnp.take(cluster_ids, my_head, axis=0)
    member = split_numbers[None, :] == pair_cluster[:, None]
    member_rank = jnp.cumsum(member.astype(jnp.int32), axis=1) - 1
    member_count = jnp.sum(member.astype(jnp.int32), axis=1)
    picked = member[:, None, :] & (member_rank[:, None, :] == jnp.arange(capacity)[None, :, None])
    member_block = jnp.sum(jnp.where(picked, jnp.arange(block_count)[None, None, :], 0), axis=2)
    live_members = jnp.arange(capacity)[None, :] < member_count[:, None]
    mine = (my_head * cluster_count + split_numbers) // owned_pairs == position
    mine_grid = mine.reshape(seq_count, local_blocks)
    recv_rank = jnp.cumsum(mine_grid.astype(jnp.int32), axis=1) - 1
    recv_pos = (peer_index[:, None] * per_peer + recv_rank).reshape(block_count)
    member_pos = jnp.take(recv_pos, member_block)
    couple_softness = jnp.take(logit_softness, split_for_couple)
    pair_onehot = (split_for_couple[:, None] == jnp.arange(head_count)[None, :]).astype(jnp.float32)
    slot_pair = my_head * cluster_count + split_numbers - position * owned_pairs
    same_cluster = split_numbers[:, None] == split_numbers[None, :]
    earlier_block = jnp.arange(block_count)[None, :] < jnp.arange(block_count)[:, None]
    slot_rank = jnp.sum((same_cluster & earlier_block).astype(jnp.int32), axis=1)
    back_pos = jnp.clip(slot_pair, 0, owned_pairs - 1) * capacity + jnp.clip(
        slot_rank, 0, capacity - 1
    )
    back_grid = back_pos.reshape(seq_count, local_blocks)
    back_pick = mine_grid[:, None, :] & (recv_rank[:, None, :] == slot_range[None, :, None])
    back_flat = jnp.sum(jnp.where(back_pick, back_grid[:, None, :], 0), axis=2)

    def to_peers(array_in):
        flat = array_in.reshape((head_count * local_blocks,) + array_in.shape[2:])
        return jnp.take(flat, send_flat, axis=0)

    def members(array_in):
        flat = array_in.reshape((seq_count * per_peer,) + array_in.shape[2:])
        return jnp.take(flat, member_pos, axis=0)

    def to_owner(array_in):
        flat = array_in.reshape((owned_pairs * capacity,) + array_in.shape[2:])
        return jnp.take(flat, back_flat, axis=0)

    def from_peers(array_in):
        flat = array_in.reshape((seq_count * per_peer,) + array_in.shape[2:])
        return jnp.take(flat, home_pos, axis=0)

    raw_w, mask_w, pgrad_w, top_w, total_w, mass_w = window_parts(
        query_home,
        prev_keys,
        prev_values,
        grad_home,
        usable_home,
        neighborhood_span[:, None],
        logit_softness[:, None],
    )
    arrived = (
        lax.all_to_all(to_peers(query_home), "seq", split_axis=0, concat_axis=0, tiled=True),
        lax.all_to_all(to_peers(key_home), "seq", split_axis=0, concat_axis=0, tiled=True),
        lax.all_to_all(to_peers(value_home), "seq", split_axis=0, concat_axis=0, tiled=True),
        lax.all_to_all(to_peers(grad_home), "seq", split_axis=0, concat_axis=0, tiled=True),
    )
    arrived_stats = (
        lax.all_to_all(to_peers(top_w), "seq", split_axis=0, concat_axis=0, tiled=True),
        lax.all_to_all(to_peers(total_w), "seq", split_axis=0, concat_axis=0, tiled=True),
        lax.all_to_all(to_peers(mass_w), "seq", split_axis=0, concat_axis=0, tiled=True),
    )
    query_m, key_m, value_m, grad_m = [members(item_in) for item_in in arrived]
    top_m, total_m, mass_m = [members(item_in) for item_in in arrived_stats]

    def split_pair(pair_inputs):
        query_i, key_i, value_i, grad_i, live_i, temper_i, top_i, total_i, mass_i = pair_inputs
        query_c, log_total, row_delta, key_c, value_c, temper_c = cluster_pair(
            query_i, key_i, value_i, grad_i, live_i, temper_i, top_i, total_i, mass_i
        )
        return (
            query_c.astype(jnp.bfloat16),
            key_c.astype(jnp.bfloat16),
            value_c.astype(jnp.bfloat16),
            log_total,
            row_delta,
            temper_c,
        )

    owner_results = lax.map(
        split_pair,
        (query_m, key_m, value_m, grad_m, live_members, couple_softness, top_m, total_m, mass_m),
    )
    returned = (
        lax.all_to_all(to_owner(owner_results[0]), "seq", split_axis=0, concat_axis=0, tiled=True),
        lax.all_to_all(to_owner(owner_results[1]), "seq", split_axis=0, concat_axis=0, tiled=True),
        lax.all_to_all(to_owner(owner_results[2]), "seq", split_axis=0, concat_axis=0, tiled=True),
    )
    returned_stats = (
        lax.all_to_all(to_owner(owner_results[3]), "seq", split_axis=0, concat_axis=0, tiled=True),
        lax.all_to_all(to_owner(owner_results[4]), "seq", split_axis=0, concat_axis=0, tiled=True),
    )
    query_cluster = from_peers(returned[0])
    key_cluster = from_peers(returned[1])
    value_cluster = from_peers(returned[2])
    log_home = from_peers(returned_stats[0])
    delta_home = from_peers(returned_stats[1])
    query_w, key_w, value_w, temper_w = window_grads(
        raw_w,
        mask_w,
        pgrad_w,
        query_home,
        prev_keys,
        grad_home,
        log_home,
        delta_home,
        logit_softness[:, None],
    )
    query_out = (query_cluster.astype(jnp.float32) + lifted(query_w)).astype(jnp.bfloat16)
    key_window = key_w.astype(jnp.bfloat16)
    value_window = value_w.astype(jnp.bfloat16)
    temper_local = jnp.sum(owner_results[5][:, None] * pair_onehot, axis=0) + jnp.sum(
        temper_w, axis=1
    )
    edge_keys, edge_values = shifted((key_window[:, 0], value_window[:, 0]), "seq", -1)
    key_next = jnp.concatenate([key_window[:, 1:], edge_keys[:, None]], axis=1)
    value_next = jnp.concatenate([value_window[:, 1:], edge_values[:, None]], axis=1)
    key_out = (key_cluster.astype(jnp.float32) + key_next.astype(jnp.float32)).astype(jnp.bfloat16)
    value_out = (value_cluster.astype(jnp.float32) + value_next.astype(jnp.float32)).astype(
        jnp.bfloat16
    )
    temper_total = lax.psum(temper_local, ("seq", "dp"))
    temper_grad = temper_total / (lax.axis_size("dp") * tokens * seq_count)
    return (token_major(query_out), token_major(key_out), token_major(value_out), temper_grad)


TILE = 256
EXTRA = 16
VMEM_LIMIT = 56 * 1024 * 1024


def partner(step):
    return lax.axis_index("seq") ^ step


def columns_of(index):
    return pl.ds(pl.multiple_of(index * HD, HD), HD)


def rows_of(index):
    return pl.ds(pl.multiple_of(index * BLK, BLK), BLK)


def pack_kernel(*refs, count):
    arrays, out_refs = refs[:count], refs[count:]
    for step, out_ref in enumerate(out_refs):
        head = partner(step)
        for place, array_ref in enumerate(arrays):
            out_ref[place * BLK : (place + 1) * BLK, :] = array_ref[0, :, columns_of(head)]


def packed(*arrays):
    head_count = arrays[0].shape[2] // HD
    out_shape = (len(arrays) * BLK, HD)
    return pl.pallas_call(
        functools.partial(pack_kernel, count=len(arrays)),
        out_shape=[jax.ShapeDtypeStruct(out_shape, jnp.bfloat16)] * head_count,
        cost_estimate=pl.CostEstimate(
            flops=0, bytes_accessed=4 * head_count * math.prod(out_shape), transcendentals=0
        ),
        compiler_params=pltpu.CompilerParams(vmem_limit_bytes=VMEM_LIMIT),
        name="pack_heads",
    )(*arrays)


def exchanged(chunks):
    count = len(chunks)
    return [chunks[0]] + [
        lax.ppermute(chunks[step], "seq", [(source, source ^ step) for source in range(count)])
        for step in range(1, count)
    ]


def unpack_kernel(*refs, count):
    chunks, out_refs = refs[:-count], refs[-count:]
    for place, out_ref in enumerate(out_refs):
        for step, chunk_ref in enumerate(chunks):
            out_ref[0, :, columns_of(partner(step))] = chunk_ref[
                place * BLK : (place + 1) * BLK, :
            ]


def unpacked(chunks, count):
    out_shape = (1, BLK, len(chunks) * HD)
    return pl.pallas_call(
        functools.partial(unpack_kernel, count=count),
        out_shape=[jax.ShapeDtypeStruct(out_shape, jnp.bfloat16)] * count,
        cost_estimate=pl.CostEstimate(
            flops=0, bytes_accessed=4 * count * math.prod(out_shape), transcendentals=0
        ),
        compiler_params=pltpu.CompilerParams(vmem_limit_bytes=VMEM_LIMIT),
        name="unpack_heads",
    )(*chunks)


def allowed_scores(scores, tile_key, tile_query, ids_ref, head, width):
    per_tile = TILE // BLK
    spread = lax.broadcasted_iota(jnp.int32, (BLK, BLK), 0) - lax.broadcasted_iota(
        jnp.int32, (BLK, BLK), 1
    )
    rows = []
    for sub_key in range(per_tile):
        pieces = []
        block_key = tile_key * per_tile + sub_key
        for sub_query in range(per_tile):
            block_query = tile_query * per_tile + sub_query
            piece = scores[
                sub_key * BLK : (sub_key + 1) * BLK, sub_query * BLK : (sub_query + 1) * BLK
            ]
            same = ids_ref[head, block_key] == ids_ref[head, block_query]
            if block_key > block_query:
                piece = jnp.full_like(piece, blocked_score)
            elif block_key == block_query:
                piece = jnp.where(spread <= 0, piece, blocked_score)
            elif block_key == block_query - 1:
                least = jnp.where(same, -BLK, BLK - width)
                piece = jnp.where(spread > least, piece, blocked_score)
            else:
                piece = jnp.where(spread > jnp.where(same, -BLK, BLK), piece, blocked_score)
            pieces.append(piece)
        rows.append(jnp.concatenate(pieces, axis=1))
    return jnp.concatenate(rows, axis=0)


def dot_rows(left, right):
    return lax.dot_general(
        left, right, (((1,), (1,)), ((), ())), preferred_element_type=jnp.float32
    )


def dot_plain(left, right):
    return lax.dot_general(
        left, right, (((1,), (0,)), ((), ())), preferred_element_type=jnp.float32
    )


def attention_kernel(softness_ref, ids_ref, span_ref, *refs, blocks):
    in_refs, out_refs = refs[:blocks], refs[blocks : 2 * blocks]
    query, key, value, grad, key_across, score, gradient, prob_low, grad_low, result = refs[
        2 * blocks :
    ]
    head = lax.axis_index("seq")
    tiles = blocks * BLK // TILE
    temper = softness_ref[head]
    width = span_ref[head]
    scaling = temper * (1.0 / math.sqrt(HD))
    to_log2 = scaling * math.log2(math.e)
    for step, in_ref in enumerate(in_refs):
        rows = rows_of(partner(step))
        query[rows, :] = in_ref[0 * BLK : 1 * BLK, :]
        key[rows, :] = in_ref[1 * BLK : 2 * BLK, :]
        value[rows, :] = in_ref[2 * BLK : 3 * BLK, :]
        grad[rows, :] = in_ref[3 * BLK : 4 * BLK, :]
        key_across[:, rows] = in_ref[1 * BLK : 2 * BLK, :].T
    temper_rows = jnp.zeros((1, HD), jnp.float32)
    for tile in range(tiles):
        here = slice(tile * TILE, (tile + 1) * TILE)
        top = jnp.full((1, TILE), blocked_score, jnp.float32)
        for other in range(tile + 1):
            there = slice(other * TILE, (other + 1) * TILE)
            raw = dot_rows(key[there, :], query[here, :]) * to_log2
            raw = allowed_scores(raw, other, tile, ids_ref, head, width)
            score[there, :] = raw
            top = jnp.maximum(top, jnp.max(raw, axis=0, keepdims=True))
        total = jnp.zeros((1, TILE), jnp.float32)
        mass = jnp.zeros((1, TILE), jnp.float32)
        for other in range(tile + 1):
            there = slice(other * TILE, (other + 1) * TILE)
            weight = jnp.exp2(score[there, :] - top)
            towards = dot_rows(value[there, :], grad[here, :])
            score[there, :] = weight
            gradient[there, :] = towards
            total += jnp.sum(weight, axis=0, keepdims=True)
            mass += jnp.sum(weight * towards, axis=0, keepdims=True)
        inverse = 1.0 / total
        delta = mass * inverse
        for other in range(tile + 1):
            there = slice(other * TILE, (other + 1) * TILE)
            probability = score[there, :] * inverse
            prob_low[there, here] = probability.astype(jnp.bfloat16)
            grad_low[there, here] = (probability * (gradient[there, :] - delta)).astype(
                jnp.bfloat16
            )
        upto = slice(0, (tile + 1) * TILE)
        query_part = dot_plain(key_across[:, upto], grad_low[upto, here]).T
        temper_rows += jnp.sum(
            query_part * query[here, :].astype(jnp.float32), axis=0, keepdims=True
        )
        query_part = (query_part * scaling).astype(jnp.bfloat16)
        result[0, here, :] = query_part
    for tile in range(tiles):
        here = slice(tile * TILE, (tile + 1) * TILE)
        onward = slice(tile * TILE, tiles * TILE)
        key_part = (dot_plain(grad_low[here, onward], query[onward, :]) * scaling).astype(
            jnp.bfloat16
        )
        value_part = dot_plain(prob_low[here, onward], grad[onward, :]).astype(jnp.bfloat16)
        result[1, here, :] = key_part
        result[2, here, :] = value_part
    temper_sum = jnp.sum(temper_rows, axis=1, keepdims=True) * (1.0 / math.sqrt(HD))
    spread = jnp.broadcast_to(temper_sum, (EXTRA, HD))
    high = spread.astype(jnp.bfloat16).astype(jnp.float32)
    middle = (spread - high).astype(jnp.bfloat16).astype(jnp.float32)
    low = spread - high - middle
    row = lax.broadcasted_iota(jnp.int32, (EXTRA, HD), 0)
    pieces = jnp.where(row == 0, high, jnp.where(row == 1, middle, low)).astype(jnp.bfloat16)
    for step, out_ref in enumerate(out_refs):
        rows = rows_of(partner(step))
        for place in range(3):
            out_ref[place * BLK : (place + 1) * BLK, :] = result[place, rows, :]
        out_ref[3 * BLK : 3 * BLK + EXTRA, :] = pieces


def attention(softness, ids, span, arrived):
    blocks = len(arrived)
    length = blocks * BLK
    out_shape = (3 * BLK + EXTRA, HD)
    smem = pl.BlockSpec(memory_space=pltpu.SMEM)
    vmem = pl.BlockSpec(memory_space=pltpu.VMEM)
    return pl.pallas_call(
        functools.partial(attention_kernel, blocks=blocks),
        out_shape=[jax.ShapeDtypeStruct(out_shape, jnp.bfloat16)] * blocks,
        in_specs=[smem, smem, smem] + [vmem] * blocks,
        out_specs=[vmem] * blocks,
        scratch_shapes=[
            pltpu.VMEM((length, HD), jnp.bfloat16),
            pltpu.VMEM((length, HD), jnp.bfloat16),
            pltpu.VMEM((length, HD), jnp.bfloat16),
            pltpu.VMEM((length, HD), jnp.bfloat16),
            pltpu.VMEM((HD, length), jnp.bfloat16),
            pltpu.VMEM((length, TILE), jnp.float32),
            pltpu.VMEM((length, TILE), jnp.float32),
            pltpu.VMEM((length, length), jnp.bfloat16),
            pltpu.VMEM((length, length), jnp.bfloat16),
            pltpu.VMEM((3, length, HD), jnp.bfloat16),
        ],
        cost_estimate=pl.CostEstimate(
            flops=5 * length * length * HD,
            bytes_accessed=16 * length * HD,
            transcendentals=length * length // 2,
        ),
        compiler_params=pltpu.CompilerParams(vmem_limit_bytes=VMEM_LIMIT),
        name="head_attention",
    )(softness, ids, span, *arrived)


def head_shards(
    probe_vectors,
    lookup_vectors,
    content_vectors,
    result_cotangent,
    logit_softness,
    block_grouping,
    neighborhood_span,
):
    ids = block_grouping[0, :, :, 0]
    dp_count = lax.axis_size("dp")
    sent = packed(probe_vectors, lookup_vectors, content_vectors, result_cotangent)
    arrived = exchanged(sent)
    owned = attention(logit_softness, ids, neighborhood_span, arrived)
    back = exchanged(owned)
    temper_local = jnp.stack(
        [jnp.sum(chunk[3 * BLK : 3 * BLK + 3, 0].astype(jnp.float32)) for chunk in back]
    )
    temper_local = jnp.take(temper_local, partner(jnp.arange(len(back))))
    temper_total = temper_local
    for step in range(1, dp_count):
        pairs = [(source, (source + step) % dp_count) for source in range(dp_count)]
        temper_total = temper_total + lax.ppermute(temper_local, "dp", pairs)
    outs = unpacked(back, 3)
    tokens = probe_vectors.shape[1] * lax.axis_size("seq")
    return (*outs, temper_total / (dp_count * tokens))


def shards(
    probe_vectors,
    lookup_vectors,
    content_vectors,
    result_cotangent,
    logit_softness,
    block_grouping,
    neighborhood_span,
):
    head_count = probe_vectors.shape[2] // HD
    one_block = probe_vectors.shape[1] == BLK
    if head_count == lax.axis_size("seq") and one_block:
        plan = head_shards
    else:
        plan = clustered_shards
    return plan(
        probe_vectors,
        lookup_vectors,
        content_vectors,
        result_cotangent,
        logit_softness,
        block_grouping,
        neighborhood_span,
    )


def solution(mesh):
    in_specs = (
        P("dp", "seq", None),
        P("dp", "seq", None),
        P("dp", "seq", None),
        P("dp", "seq", None),
        P(),
        P("dp", None, None, None),
        P(),
    )
    out_specs = (P("dp", "seq", None), P("dp", "seq", None), P("dp", "seq", None), P())
    return jax.shard_map(shards, mesh=mesh, in_specs=in_specs, out_specs=out_specs, check_vma=False)
```

```python
import functools
import math

import jax
import jax.numpy as jnp
from jax import lax
from jax.experimental import pallas as pl
from jax.experimental.pallas import tpu as pltpu
from jax.sharding import PartitionSpec as P

HD = 128
BLK = 128


blocked_score = -1e30


def shifted(value, axis, steps):
    count = lax.axis_size(axis)
    first, last = (max(0, -steps), min(count, count - steps))
    return lax.ppermute(value, axis, [(source, source + steps) for source in range(first, last)])


def lifted(array_in):
    return lax.optimization_barrier(array_in.astype(jnp.bfloat16)).astype(jnp.float32)


def head_major(tokens_in, block_len):
    token_count, feature_count = tokens_in.shape
    return tokens_in.reshape(
        token_count // block_len, block_len, feature_count // HD, HD
    ).transpose(2, 0, 1, 3)


def token_major(blocks_in):
    head_count, block_count, block_len, depth = blocks_in.shape
    return blocks_in.transpose(1, 2, 0, 3).reshape(1, block_count * block_len, head_count * depth)


def window_parts(query_block, prev_keys, prev_values, grad_block, usable, window_width, temper):
    block_len = query_block.shape[-2]
    inverse_root = 1.0 / math.sqrt(query_block.shape[-1])
    raw_scores = (
        jnp.einsum("...td,...sd->...ts", query_block, prev_keys, preferred_element_type=jnp.float32)
        * inverse_root
    )
    query_pos = lax.broadcasted_iota(jnp.int32, (block_len, block_len), 0)
    key_pos = lax.broadcasted_iota(jnp.int32, (block_len, block_len), 1)
    pair_mask = usable[..., None, None] & (
        key_pos > query_pos + block_len - window_width[..., None, None]
    )
    scores = temper[..., None, None] * raw_scores
    row_top = jnp.max(jnp.where(pair_mask, scores, blocked_score), axis=-1)
    weights = jnp.where(pair_mask, jnp.exp(scores - row_top[..., None]), 0.0)
    prob_grad = jnp.einsum(
        "...td,...sd->...ts", grad_block, prev_values, preferred_element_type=jnp.float32
    )
    return (
        raw_scores,
        pair_mask,
        prob_grad,
        row_top,
        jnp.sum(weights, axis=-1),
        jnp.sum(weights * prob_grad, axis=-1),
    )


def window_grads(
    raw_scores,
    pair_mask,
    prob_grad,
    query_block,
    prev_keys,
    grad_block,
    log_total,
    row_delta,
    temper,
):
    inverse_root = 1.0 / math.sqrt(query_block.shape[-1])
    scaling = (temper * inverse_root)[..., None, None]
    probability = jnp.where(
        pair_mask, jnp.exp(temper[..., None, None] * raw_scores - log_total[..., None]), 0.0
    )
    score_grad = probability * (prob_grad - row_delta[..., None])
    prob_low = probability.astype(jnp.bfloat16)
    grad_low = score_grad.astype(jnp.bfloat16)
    query_part = (
        jnp.einsum("...ts,...sd->...td", grad_low, prev_keys, preferred_element_type=jnp.float32)
        * scaling
    )
    key_part = (
        jnp.einsum("...ts,...td->...sd", grad_low, query_block, preferred_element_type=jnp.float32)
        * scaling
    )
    value_part = jnp.einsum(
        "...ts,...td->...sd", prob_low, grad_block, preferred_element_type=jnp.float32
    )
    temper_part = jnp.sum(score_grad * raw_scores, axis=(-2, -1))
    return (query_part, key_part, value_part, temper_part)


def cluster_pair(
    query_items,
    key_items,
    value_items,
    grad_items,
    live_items,
    temper,
    window_top,
    window_total,
    window_mass,
):
    item_count, block_len, depth = query_items.shape
    row_count = item_count * block_len
    group_rows = 4 * block_len
    inverse_root = 1.0 / math.sqrt(depth)
    scaling = temper * inverse_root
    query_rows = query_items.reshape(row_count, depth)
    key_rows = key_items.reshape(row_count, depth)
    value_rows = value_items.reshape(row_count, depth)
    grad_rows = grad_items.reshape(row_count, depth)
    key_item = jnp.arange(row_count) // block_len
    key_token = jnp.arange(row_count) % block_len
    live_rows = jnp.repeat(live_items, block_len)
    top_rows = window_top.reshape(row_count)
    total_rows = window_total.reshape(row_count)
    mass_rows = window_mass.reshape(row_count)

    def group_step(carry, start_row):
        key_acc, value_acc, temper_acc = carry
        query_group = lax.dynamic_slice_in_dim(query_rows, start_row, group_rows, 0)
        grad_group = lax.dynamic_slice_in_dim(grad_rows, start_row, group_rows, 0)
        group_live = lax.dynamic_slice_in_dim(live_rows, start_row, group_rows, 0)
        group_top = lax.dynamic_slice_in_dim(top_rows, start_row, group_rows, 0)
        group_total = lax.dynamic_slice_in_dim(total_rows, start_row, group_rows, 0)
        group_mass = lax.dynamic_slice_in_dim(mass_rows, start_row, group_rows, 0)
        query_item = (start_row + jnp.arange(group_rows)) // block_len
        query_token = jnp.arange(group_rows) % block_len
        earlier = (key_item[None, :] < query_item[:, None]) | (
            key_item[None, :] == query_item[:, None]
        ) & (key_token[None, :] <= query_token[:, None])
        pair_mask = group_live[:, None] & live_rows[None, :] & earlier
        raw_scores = (
            lax.dot_general(
                query_group, key_rows, (((1,), (1,)), ((), ())), preferred_element_type=jnp.float32
            )
            * inverse_root
        )
        scores = temper * raw_scores
        row_top = jnp.maximum(
            jnp.max(jnp.where(pair_mask, scores, blocked_score), axis=1), group_top
        )
        weights = jnp.where(pair_mask, jnp.exp(scores - row_top[:, None]), 0.0)
        row_total = jnp.sum(weights, axis=1) + group_total * jnp.exp(group_top - row_top)
        log_total = row_top + jnp.log(jnp.where(group_live, row_total, 1.0))
        probability = jnp.where(pair_mask, jnp.exp(scores - log_total[:, None]), 0.0)
        prob_grad = lax.dot_general(
            grad_group, value_rows, (((1,), (1,)), ((), ())), preferred_element_type=jnp.float32
        )
        row_delta = jnp.sum(probability * prob_grad, axis=1) + group_mass * jnp.exp(
            group_top - log_total
        )
        score_grad = probability * (prob_grad - row_delta[:, None])
        prob_low = probability.astype(jnp.bfloat16)
        grad_low = score_grad.astype(jnp.bfloat16)
        query_part = jnp.dot(grad_low, key_rows, preferred_element_type=jnp.float32) * scaling
        key_acc = (
            key_acc
            + lax.dot_general(
                grad_low, query_group, (((0,), (0,)), ((), ())), preferred_element_type=jnp.float32
            )
            * scaling
        )
        value_acc = value_acc + lax.dot_general(
            prob_low, grad_group, (((0,), (0,)), ((), ())), preferred_element_type=jnp.float32
        )
        temper_acc = temper_acc + jnp.sum(score_grad * raw_scores)
        return ((key_acc, value_acc, temper_acc), (query_part, log_total, row_delta))

    start_rows = jnp.arange(item_count // 4) * group_rows
    initial = (
        jnp.zeros((row_count, depth), jnp.float32),
        jnp.zeros((row_count, depth), jnp.float32),
        jnp.zeros((), jnp.float32),
    )
    (key_acc, value_acc, temper_acc), (query_part, log_total, row_delta) = lax.scan(
        group_step, initial, start_rows
    )
    return (
        query_part.reshape(item_count, block_len, depth),
        log_total.reshape(item_count, block_len),
        row_delta.reshape(item_count, block_len),
        key_acc.reshape(item_count, block_len, depth),
        value_acc.reshape(item_count, block_len, depth),
        temper_acc,
    )


def clustered_shards(
    probe_vectors,
    lookup_vectors,
    content_vectors,
    result_cotangent,
    logit_softness,
    block_grouping,
    neighborhood_span,
):
    seq_count = lax.axis_size("seq")
    position = lax.axis_index("seq")
    tokens = probe_vectors.shape[1]
    head_count = probe_vectors.shape[2] // HD
    local_blocks = tokens // BLK
    block_count = local_blocks * seq_count
    cluster_count = max(1, block_count // 8)
    capacity = min(12, block_count)
    owned_pairs = cluster_count * head_count // seq_count
    group_count = cluster_count // owned_pairs
    per_peer = max(1, local_blocks // group_count)
    cluster_ids = block_grouping[0, :, :, 0]
    query_home = head_major(probe_vectors[0], BLK)
    key_home = head_major(lookup_vectors[0], BLK)
    value_home = head_major(content_vectors[0], BLK)
    grad_home = head_major(result_cotangent[0], BLK)
    last_block = (lookup_vectors[0, tokens - BLK :], content_vectors[0, tokens - BLK :])
    prev_key_rows, prev_value_rows = shifted((last_block[0], last_block[1]), "seq", 1)
    prev_keys = jnp.concatenate([head_major(prev_key_rows, BLK), key_home[:, :-1]], axis=1)
    prev_values = jnp.concatenate([head_major(prev_value_rows, BLK), value_home[:, :-1]], axis=1)
    first_block = position * local_blocks
    before = jnp.concatenate(
        [jnp.full((head_count, 1), -1, jnp.int32), cluster_ids[:, :-1]], axis=1
    )
    my_ids = lax.dynamic_slice_in_dim(cluster_ids, first_block, local_blocks, 1)
    my_before = lax.dynamic_slice_in_dim(before, first_block, local_blocks, 1)
    global_block = first_block + jnp.arange(local_blocks)
    usable_home = (global_block[None, :] >= 1) & (my_before != my_ids)
    peer_index = jnp.arange(seq_count)
    peer_head = peer_index * owned_pairs // cluster_count
    slot_range = jnp.arange(per_peer)
    local_range = jnp.arange(local_blocks)
    owner_index = (jnp.arange(head_count)[:, None] * cluster_count + my_ids) // owned_pairs
    peer_ids = jnp.take(my_ids, peer_head, axis=0)
    goes = (peer_head[:, None] * cluster_count + peer_ids) // owned_pairs == peer_index[:, None]
    send_rank = jnp.cumsum(goes.astype(jnp.int32), axis=1) - 1
    send_pick = goes[:, None, :] & (send_rank[:, None, :] == slot_range[None, :, None])
    send_block = jnp.sum(jnp.where(send_pick, local_range[None, None, :], 0), axis=2)
    send_flat = peer_head[:, None] * local_blocks + send_block
    home_rank = jnp.take_along_axis(send_rank, owner_index, axis=0)
    home_pos = owner_index * per_peer + home_rank
    pair_index = position * owned_pairs + jnp.arange(owned_pairs)
    split_for_couple = pair_index // cluster_count
    pair_cluster = pair_index % cluster_count
    my_head = position * owned_pairs // cluster_count
    split_numbers = jnp.take(cluster_ids, my_head, axis=0)
    member = split_numbers[None, :] == pair_cluster[:, None]
    member_rank = jnp.cumsum(member.astype(jnp.int32), axis=1) - 1
    member_count = jnp.sum(member.astype(jnp.int32), axis=1)
    picked = member[:, None, :] & (member_rank[:, None, :] == jnp.arange(capacity)[None, :, None])
    member_block = jnp.sum(jnp.where(picked, jnp.arange(block_count)[None, None, :], 0), axis=2)
    live_members = jnp.arange(capacity)[None, :] < member_count[:, None]
    mine = (my_head * cluster_count + split_numbers) // owned_pairs == position
    mine_grid = mine.reshape(seq_count, local_blocks)
    recv_rank = jnp.cumsum(mine_grid.astype(jnp.int32), axis=1) - 1
    recv_pos = (peer_index[:, None] * per_peer + recv_rank).reshape(block_count)
    member_pos = jnp.take(recv_pos, member_block)
    couple_softness = jnp.take(logit_softness, split_for_couple)
    pair_onehot = (split_for_couple[:, None] == jnp.arange(head_count)[None, :]).astype(jnp.float32)
    slot_pair = my_head * cluster_count + split_numbers - position * owned_pairs
    same_cluster = split_numbers[:, None] == split_numbers[None, :]
    earlier_block = jnp.arange(block_count)[None, :] < jnp.arange(block_count)[:, None]
    slot_rank = jnp.sum((same_cluster & earlier_block).astype(jnp.int32), axis=1)
    back_pos = jnp.clip(slot_pair, 0, owned_pairs - 1) * capacity + jnp.clip(
        slot_rank, 0, capacity - 1
    )
    back_grid = back_pos.reshape(seq_count, local_blocks)
    back_pick = mine_grid[:, None, :] & (recv_rank[:, None, :] == slot_range[None, :, None])
    back_flat = jnp.sum(jnp.where(back_pick, back_grid[:, None, :], 0), axis=2)

    def to_peers(array_in):
        flat = array_in.reshape((head_count * local_blocks,) + array_in.shape[2:])
        return jnp.take(flat, send_flat, axis=0)

    def members(array_in):
        flat = array_in.reshape((seq_count * per_peer,) + array_in.shape[2:])
        return jnp.take(flat, member_pos, axis=0)

    def to_owner(array_in):
        flat = array_in.reshape((owned_pairs * capacity,) + array_in.shape[2:])
        return jnp.take(flat, back_flat, axis=0)

    def from_peers(array_in):
        flat = array_in.reshape((seq_count * per_peer,) + array_in.shape[2:])
        return jnp.take(flat, home_pos, axis=0)

    raw_w, mask_w, pgrad_w, top_w, total_w, mass_w = window_parts(
        query_home,
        prev_keys,
        prev_values,
        grad_home,
        usable_home,
        neighborhood_span[:, None],
        logit_softness[:, None],
    )
    arrived = (
        lax.all_to_all(to_peers(query_home), "seq", split_axis=0, concat_axis=0, tiled=True),
        lax.all_to_all(to_peers(key_home), "seq", split_axis=0, concat_axis=0, tiled=True),
        lax.all_to_all(to_peers(value_home), "seq", split_axis=0, concat_axis=0, tiled=True),
        lax.all_to_all(to_peers(grad_home), "seq", split_axis=0, concat_axis=0, tiled=True),
    )
    arrived_stats = (
        lax.all_to_all(to_peers(top_w), "seq", split_axis=0, concat_axis=0, tiled=True),
        lax.all_to_all(to_peers(total_w), "seq", split_axis=0, concat_axis=0, tiled=True),
        lax.all_to_all(to_peers(mass_w), "seq", split_axis=0, concat_axis=0, tiled=True),
    )
    query_m, key_m, value_m, grad_m = [members(item_in) for item_in in arrived]
    top_m, total_m, mass_m = [members(item_in) for item_in in arrived_stats]

    def split_pair(pair_inputs):
        query_i, key_i, value_i, grad_i, live_i, temper_i, top_i, total_i, mass_i = pair_inputs
        query_c, log_total, row_delta, key_c, value_c, temper_c = cluster_pair(
            query_i, key_i, value_i, grad_i, live_i, temper_i, top_i, total_i, mass_i
        )
        return (
            query_c.astype(jnp.bfloat16),
            key_c.astype(jnp.bfloat16),
            value_c.astype(jnp.bfloat16),
            log_total,
            row_delta,
            temper_c,
        )

    owner_results = lax.map(
        split_pair,
        (query_m, key_m, value_m, grad_m, live_members, couple_softness, top_m, total_m, mass_m),
    )
    returned = (
        lax.all_to_all(to_owner(owner_results[0]), "seq", split_axis=0, concat_axis=0, tiled=True),
        lax.all_to_all(to_owner(owner_results[1]), "seq", split_axis=0, concat_axis=0, tiled=True),
        lax.all_to_all(to_owner(owner_results[2]), "seq", split_axis=0, concat_axis=0, tiled=True),
    )
    returned_stats = (
        lax.all_to_all(to_owner(owner_results[3]), "seq", split_axis=0, concat_axis=0, tiled=True),
        lax.all_to_all(to_owner(owner_results[4]), "seq", split_axis=0, concat_axis=0, tiled=True),
    )
    query_cluster = from_peers(returned[0])
    key_cluster = from_peers(returned[1])
    value_cluster = from_peers(returned[2])
    log_home = from_peers(returned_stats[0])
    delta_home = from_peers(returned_stats[1])
    query_w, key_w, value_w, temper_w = window_grads(
        raw_w,
        mask_w,
        pgrad_w,
        query_home,
        prev_keys,
        grad_home,
        log_home,
        delta_home,
        logit_softness[:, None],
    )
    query_out = (query_cluster.astype(jnp.float32) + lifted(query_w)).astype(jnp.bfloat16)
    key_window = key_w.astype(jnp.bfloat16)
    value_window = value_w.astype(jnp.bfloat16)
    temper_local = jnp.sum(owner_results[5][:, None] * pair_onehot, axis=0) + jnp.sum(
        temper_w, axis=1
    )
    edge_keys, edge_values = shifted((key_window[:, 0], value_window[:, 0]), "seq", -1)
    key_next = jnp.concatenate([key_window[:, 1:], edge_keys[:, None]], axis=1)
    value_next = jnp.concatenate([value_window[:, 1:], edge_values[:, None]], axis=1)
    key_out = (key_cluster.astype(jnp.float32) + key_next.astype(jnp.float32)).astype(jnp.bfloat16)
    value_out = (value_cluster.astype(jnp.float32) + value_next.astype(jnp.float32)).astype(
        jnp.bfloat16
    )
    temper_total = lax.psum(temper_local, ("seq", "dp"))
    temper_grad = temper_total / (lax.axis_size("dp") * tokens * seq_count)
    return (token_major(query_out), token_major(key_out), token_major(value_out), temper_grad)


TILE = 256
EXTRA = 16
PACK_VMEM = 10 * 1024 * 1024
HEAD_VMEM = 31 * 1024 * 1024


def pack_kernel(*refs):
    arrays, packed_ref = refs[:-1], refs[-1]
    for place, array_ref in enumerate(arrays):
        for head in range(packed_ref.shape[0]):
            packed_ref[head, place * BLK : (place + 1) * BLK, :] = array_ref[
                0, :, head * HD : (head + 1) * HD
            ]


def packed(*arrays):
    head_count = arrays[0].shape[2] // HD
    out_shape = (head_count, len(arrays) * BLK, HD)
    return pl.pallas_call(
        pack_kernel,
        out_shape=jax.ShapeDtypeStruct(out_shape, jnp.bfloat16),
        cost_estimate=pl.CostEstimate(
            flops=0, bytes_accessed=4 * math.prod(out_shape), transcendentals=0
        ),
        compiler_params=pltpu.CompilerParams(vmem_limit_bytes=PACK_VMEM),
        name="pack_heads",
    )(*arrays)


def unpack_kernel(packed_ref, *out_refs):
    for place, out_ref in enumerate(out_refs):
        for head in range(packed_ref.shape[0]):
            out_ref[0, :, head * HD : (head + 1) * HD] = packed_ref[
                head, place * BLK : (place + 1) * BLK, :
            ]


def unpacked(array_in, count):
    head_count = array_in.shape[0]
    out_shape = (1, BLK, head_count * HD)
    return pl.pallas_call(
        unpack_kernel,
        out_shape=[jax.ShapeDtypeStruct(out_shape, jnp.bfloat16)] * count,
        cost_estimate=pl.CostEstimate(
            flops=0, bytes_accessed=4 * count * math.prod(out_shape), transcendentals=0
        ),
        compiler_params=pltpu.CompilerParams(vmem_limit_bytes=PACK_VMEM),
        name="unpack_heads",
    )(array_in)


def allowed_scores(scores, tile_key, tile_query, ids_ref, head, width):
    per_tile = TILE // BLK
    spread = lax.broadcasted_iota(jnp.int32, (BLK, BLK), 0) - lax.broadcasted_iota(
        jnp.int32, (BLK, BLK), 1
    )
    rows = []
    for sub_key in range(per_tile):
        pieces = []
        block_key = tile_key * per_tile + sub_key
        for sub_query in range(per_tile):
            block_query = tile_query * per_tile + sub_query
            piece = scores[
                sub_key * BLK : (sub_key + 1) * BLK, sub_query * BLK : (sub_query + 1) * BLK
            ]
            same = ids_ref[head, block_key] == ids_ref[head, block_query]
            if block_key > block_query:
                piece = jnp.full_like(piece, blocked_score)
            elif block_key == block_query:
                piece = jnp.where(spread <= 0, piece, blocked_score)
            elif block_key == block_query - 1:
                least = jnp.where(same, -BLK, BLK - width)
                piece = jnp.where(spread > least, piece, blocked_score)
            else:
                piece = piece + jnp.where(same, 0.0, blocked_score)
            pieces.append(piece)
        rows.append(jnp.concatenate(pieces, axis=1))
    return jnp.concatenate(rows, axis=0)


def dot_rows(left, right):
    return lax.dot_general(
        left, right, (((1,), (1,)), ((), ())), preferred_element_type=jnp.float32
    )


def dot_plain(left, right):
    return lax.dot_general(
        left, right, (((1,), (0,)), ((), ())), preferred_element_type=jnp.float32
    )


def attention_kernel(
    softness_ref, ids_ref, span_ref, in_ref, out_ref,
    query, key, value, grad, key_across, score, gradient, prob_low, grad_low,
):
    head = lax.axis_index("seq")
    blocks = in_ref.shape[0]
    tiles = blocks * BLK // TILE
    temper = softness_ref[head]
    width = span_ref[head]
    scaling = temper * (1.0 / math.sqrt(HD))
    to_log2 = scaling * math.log2(math.e)
    for block in range(blocks):
        rows = slice(block * BLK, (block + 1) * BLK)
        query[rows, :] = in_ref[block, 0 * BLK : 1 * BLK, :]
        key[rows, :] = in_ref[block, 1 * BLK : 2 * BLK, :]
        value[rows, :] = in_ref[block, 2 * BLK : 3 * BLK, :]
        grad[rows, :] = in_ref[block, 3 * BLK : 4 * BLK, :]
        key_across[:, rows] = in_ref[block, 1 * BLK : 2 * BLK, :].T
    temper_rows = jnp.zeros((1, HD), jnp.float32)
    for tile in range(tiles):
        here = slice(tile * TILE, (tile + 1) * TILE)
        top = jnp.full((1, TILE), blocked_score, jnp.float32)
        for other in range(tile + 1):
            there = slice(other * TILE, (other + 1) * TILE)
            raw = dot_rows(key[there, :], query[here, :]) * to_log2
            raw = allowed_scores(raw, other, tile, ids_ref, head, width)
            score[there, :] = raw
            top = jnp.maximum(top, jnp.max(raw, axis=0, keepdims=True))
        total = jnp.zeros((1, TILE), jnp.float32)
        mass = jnp.zeros((1, TILE), jnp.float32)
        for other in range(tile + 1):
            there = slice(other * TILE, (other + 1) * TILE)
            weight = jnp.exp2(score[there, :] - top)
            towards = dot_rows(value[there, :], grad[here, :])
            score[there, :] = weight
            gradient[there, :] = towards
            total += jnp.sum(weight, axis=0, keepdims=True)
            mass += jnp.sum(weight * towards, axis=0, keepdims=True)
        inverse = 1.0 / total
        delta = mass * inverse
        for other in range(tile + 1):
            there = slice(other * TILE, (other + 1) * TILE)
            probability = score[there, :] * inverse
            prob_low[there, here] = probability.astype(jnp.bfloat16)
            grad_low[there, here] = (probability * (gradient[there, :] - delta)).astype(
                jnp.bfloat16
            )
        upto = slice(0, (tile + 1) * TILE)
        query_part = dot_plain(key_across[:, upto], grad_low[upto, here]).T
        temper_rows += jnp.sum(
            query_part * query[here, :].astype(jnp.float32), axis=0, keepdims=True
        )
        query_part = (query_part * scaling).astype(jnp.bfloat16)
        for sub in range(TILE // BLK):
            out_ref[tile * (TILE // BLK) + sub, 0:BLK, :] = query_part[
                sub * BLK : (sub + 1) * BLK, :
            ]
    for tile in range(tiles):
        here = slice(tile * TILE, (tile + 1) * TILE)
        onward = slice(tile * TILE, tiles * TILE)
        key_part = (dot_plain(grad_low[here, onward], query[onward, :]) * scaling).astype(
            jnp.bfloat16
        )
        value_part = dot_plain(prob_low[here, onward], grad[onward, :]).astype(jnp.bfloat16)
        for sub in range(TILE // BLK):
            block = tile * (TILE // BLK) + sub
            part = slice(sub * BLK, (sub + 1) * BLK)
            out_ref[block, BLK : 2 * BLK, :] = key_part[part, :]
            out_ref[block, 2 * BLK : 3 * BLK, :] = value_part[part, :]
    temper_sum = jnp.sum(temper_rows, axis=1, keepdims=True) * (1.0 / math.sqrt(HD))
    spread = jnp.broadcast_to(temper_sum, (EXTRA, HD))
    high = spread.astype(jnp.bfloat16).astype(jnp.float32)
    middle = (spread - high).astype(jnp.bfloat16).astype(jnp.float32)
    low = spread - high - middle
    row = lax.broadcasted_iota(jnp.int32, (EXTRA, HD), 0)
    pieces = jnp.where(row == 0, high, jnp.where(row == 1, middle, low)).astype(jnp.bfloat16)
    for block in range(blocks):
        out_ref[block, 3 * BLK : 3 * BLK + EXTRA, :] = pieces


def attention(softness, ids, span, arrived):
    blocks = arrived.shape[0]
    length = blocks * BLK
    out_shape = (blocks, 3 * BLK + EXTRA, HD)
    smem = pl.BlockSpec(memory_space=pltpu.SMEM)
    vmem = pl.BlockSpec(memory_space=pltpu.VMEM)
    return pl.pallas_call(
        attention_kernel,
        out_shape=jax.ShapeDtypeStruct(out_shape, jnp.bfloat16),
        in_specs=[smem, smem, smem, vmem],
        out_specs=vmem,
        scratch_shapes=[
            pltpu.VMEM((length, HD), jnp.bfloat16),
            pltpu.VMEM((length, HD), jnp.bfloat16),
            pltpu.VMEM((length, HD), jnp.bfloat16),
            pltpu.VMEM((length, HD), jnp.bfloat16),
            pltpu.VMEM((HD, length), jnp.bfloat16),
            pltpu.VMEM((length, TILE), jnp.float32),
            pltpu.VMEM((length, TILE), jnp.float32),
            pltpu.VMEM((length, length), jnp.bfloat16),
            pltpu.VMEM((length, length), jnp.bfloat16),
        ],
        cost_estimate=pl.CostEstimate(
            flops=5 * length * length * HD,
            bytes_accessed=2 * (math.prod(out_shape) + math.prod(arrived.shape)),
            transcendentals=length * length // 2,
        ),
        compiler_params=pltpu.CompilerParams(vmem_limit_bytes=HEAD_VMEM),
        name="head_attention",
    )(softness, ids, span, arrived)


def head_shards(
    probe_vectors,
    lookup_vectors,
    content_vectors,
    result_cotangent,
    logit_softness,
    block_grouping,
    neighborhood_span,
):
    ids = block_grouping[0, :, :, 0]
    dp_count = lax.axis_size("dp")
    sent = packed(probe_vectors, lookup_vectors, content_vectors, result_cotangent)
    arrived = lax.all_to_all(sent, "seq", split_axis=0, concat_axis=0, tiled=True)
    owned = attention(logit_softness, ids, neighborhood_span, arrived)
    back = lax.all_to_all(owned, "seq", split_axis=0, concat_axis=0, tiled=True)
    pieces = back[:, 3 * BLK : 3 * BLK + 3, 0].astype(jnp.float32)
    temper_local = jnp.sum(pieces, axis=1)
    temper_total = temper_local
    for step in range(1, dp_count):
        pairs = [(source, (source + step) % dp_count) for source in range(dp_count)]
        temper_total = temper_total + lax.ppermute(temper_local, "dp", pairs)
    outs = unpacked(back, 3)
    tokens = probe_vectors.shape[1] * lax.axis_size("seq")
    return (*outs, temper_total / (dp_count * tokens))


def shards(
    probe_vectors,
    lookup_vectors,
    content_vectors,
    result_cotangent,
    logit_softness,
    block_grouping,
    neighborhood_span,
):
    head_count = probe_vectors.shape[2] // HD
    one_block = probe_vectors.shape[1] == BLK
    if head_count == lax.axis_size("seq") and one_block:
        plan = head_shards
    else:
        plan = clustered_shards
    return plan(
        probe_vectors,
        lookup_vectors,
        content_vectors,
        result_cotangent,
        logit_softness,
        block_grouping,
        neighborhood_span,
    )


def solution(mesh):
    in_specs = (
        P("dp", "seq", None),
        P("dp", "seq", None),
        P("dp", "seq", None),
        P("dp", "seq", None),
        P(),
        P("dp", None, None, None),
        P(),
    )
    out_specs = (P("dp", "seq", None), P("dp", "seq", None), P("dp", "seq", None), P())
    return jax.shard_map(shards, mesh=mesh, in_specs=in_specs, out_specs=out_specs, check_vma=False)
```

```python
import functools
import math

import jax
import jax.numpy as jnp
from jax import lax
from jax.experimental import pallas as pl
from jax.experimental.pallas import tpu as pltpu
from jax.sharding import PartitionSpec as P

HD = 128
BLK = 128


blocked_score = -1e30


def shifted(value, axis, steps):
    count = lax.axis_size(axis)
    first, last = (max(0, -steps), min(count, count - steps))
    return lax.ppermute(value, axis, [(source, source + steps) for source in range(first, last)])


def lifted(array_in):
    return lax.optimization_barrier(array_in.astype(jnp.bfloat16)).astype(jnp.float32)


def head_major(tokens_in, block_len):
    token_count, feature_count = tokens_in.shape
    return tokens_in.reshape(
        token_count // block_len, block_len, feature_count // HD, HD
    ).transpose(2, 0, 1, 3)


def token_major(blocks_in):
    head_count, block_count, block_len, depth = blocks_in.shape
    return blocks_in.transpose(1, 2, 0, 3).reshape(1, block_count * block_len, head_count * depth)


def window_parts(query_block, prev_keys, prev_values, grad_block, usable, window_width, temper):
    block_len = query_block.shape[-2]
    inverse_root = 1.0 / math.sqrt(query_block.shape[-1])
    raw_scores = (
        jnp.einsum("...td,...sd->...ts", query_block, prev_keys, preferred_element_type=jnp.float32)
        * inverse_root
    )
    query_pos = lax.broadcasted_iota(jnp.int32, (block_len, block_len), 0)
    key_pos = lax.broadcasted_iota(jnp.int32, (block_len, block_len), 1)
    pair_mask = usable[..., None, None] & (
        key_pos > query_pos + block_len - window_width[..., None, None]
    )
    scores = temper[..., None, None] * raw_scores
    row_top = jnp.max(jnp.where(pair_mask, scores, blocked_score), axis=-1)
    weights = jnp.where(pair_mask, jnp.exp(scores - row_top[..., None]), 0.0)
    prob_grad = jnp.einsum(
        "...td,...sd->...ts", grad_block, prev_values, preferred_element_type=jnp.float32
    )
    return (
        raw_scores,
        pair_mask,
        prob_grad,
        row_top,
        jnp.sum(weights, axis=-1),
        jnp.sum(weights * prob_grad, axis=-1),
    )


def window_grads(
    raw_scores,
    pair_mask,
    prob_grad,
    query_block,
    prev_keys,
    grad_block,
    log_total,
    row_delta,
    temper,
):
    inverse_root = 1.0 / math.sqrt(query_block.shape[-1])
    scaling = (temper * inverse_root)[..., None, None]
    probability = jnp.where(
        pair_mask, jnp.exp(temper[..., None, None] * raw_scores - log_total[..., None]), 0.0
    )
    score_grad = probability * (prob_grad - row_delta[..., None])
    prob_low = probability.astype(jnp.bfloat16)
    grad_low = score_grad.astype(jnp.bfloat16)
    query_part = (
        jnp.einsum("...ts,...sd->...td", grad_low, prev_keys, preferred_element_type=jnp.float32)
        * scaling
    )
    key_part = (
        jnp.einsum("...ts,...td->...sd", grad_low, query_block, preferred_element_type=jnp.float32)
        * scaling
    )
    value_part = jnp.einsum(
        "...ts,...td->...sd", prob_low, grad_block, preferred_element_type=jnp.float32
    )
    temper_part = jnp.sum(score_grad * raw_scores, axis=(-2, -1))
    return (query_part, key_part, value_part, temper_part)


def cluster_pair(
    query_items,
    key_items,
    value_items,
    grad_items,
    live_items,
    temper,
    window_top,
    window_total,
    window_mass,
):
    item_count, block_len, depth = query_items.shape
    row_count = item_count * block_len
    group_rows = 4 * block_len
    inverse_root = 1.0 / math.sqrt(depth)
    scaling = temper * inverse_root
    query_rows = query_items.reshape(row_count, depth)
    key_rows = key_items.reshape(row_count, depth)
    value_rows = value_items.reshape(row_count, depth)
    grad_rows = grad_items.reshape(row_count, depth)
    key_item = jnp.arange(row_count) // block_len
    key_token = jnp.arange(row_count) % block_len
    live_rows = jnp.repeat(live_items, block_len)
    top_rows = window_top.reshape(row_count)
    total_rows = window_total.reshape(row_count)
    mass_rows = window_mass.reshape(row_count)

    def group_step(carry, start_row):
        key_acc, value_acc, temper_acc = carry
        query_group = lax.dynamic_slice_in_dim(query_rows, start_row, group_rows, 0)
        grad_group = lax.dynamic_slice_in_dim(grad_rows, start_row, group_rows, 0)
        group_live = lax.dynamic_slice_in_dim(live_rows, start_row, group_rows, 0)
        group_top = lax.dynamic_slice_in_dim(top_rows, start_row, group_rows, 0)
        group_total = lax.dynamic_slice_in_dim(total_rows, start_row, group_rows, 0)
        group_mass = lax.dynamic_slice_in_dim(mass_rows, start_row, group_rows, 0)
        query_item = (start_row + jnp.arange(group_rows)) // block_len
        query_token = jnp.arange(group_rows) % block_len
        earlier = (key_item[None, :] < query_item[:, None]) | (
            key_item[None, :] == query_item[:, None]
        ) & (key_token[None, :] <= query_token[:, None])
        pair_mask = group_live[:, None] & live_rows[None, :] & earlier
        raw_scores = (
            lax.dot_general(
                query_group, key_rows, (((1,), (1,)), ((), ())), preferred_element_type=jnp.float32
            )
            * inverse_root
        )
        scores = temper * raw_scores
        row_top = jnp.maximum(
            jnp.max(jnp.where(pair_mask, scores, blocked_score), axis=1), group_top
        )
        weights = jnp.where(pair_mask, jnp.exp(scores - row_top[:, None]), 0.0)
        row_total = jnp.sum(weights, axis=1) + group_total * jnp.exp(group_top - row_top)
        log_total = row_top + jnp.log(jnp.where(group_live, row_total, 1.0))
        probability = jnp.where(pair_mask, jnp.exp(scores - log_total[:, None]), 0.0)
        prob_grad = lax.dot_general(
            grad_group, value_rows, (((1,), (1,)), ((), ())), preferred_element_type=jnp.float32
        )
        row_delta = jnp.sum(probability * prob_grad, axis=1) + group_mass * jnp.exp(
            group_top - log_total
        )
        score_grad = probability * (prob_grad - row_delta[:, None])
        prob_low = probability.astype(jnp.bfloat16)
        grad_low = score_grad.astype(jnp.bfloat16)
        query_part = jnp.dot(grad_low, key_rows, preferred_element_type=jnp.float32) * scaling
        key_acc = (
            key_acc
            + lax.dot_general(
                grad_low, query_group, (((0,), (0,)), ((), ())), preferred_element_type=jnp.float32
            )
            * scaling
        )
        value_acc = value_acc + lax.dot_general(
            prob_low, grad_group, (((0,), (0,)), ((), ())), preferred_element_type=jnp.float32
        )
        temper_acc = temper_acc + jnp.sum(score_grad * raw_scores)
        return ((key_acc, value_acc, temper_acc), (query_part, log_total, row_delta))

    start_rows = jnp.arange(item_count // 4) * group_rows
    initial = (
        jnp.zeros((row_count, depth), jnp.float32),
        jnp.zeros((row_count, depth), jnp.float32),
        jnp.zeros((), jnp.float32),
    )
    (key_acc, value_acc, temper_acc), (query_part, log_total, row_delta) = lax.scan(
        group_step, initial, start_rows
    )
    return (
        query_part.reshape(item_count, block_len, depth),
        log_total.reshape(item_count, block_len),
        row_delta.reshape(item_count, block_len),
        key_acc.reshape(item_count, block_len, depth),
        value_acc.reshape(item_count, block_len, depth),
        temper_acc,
    )


def clustered_shards(
    probe_vectors,
    lookup_vectors,
    content_vectors,
    result_cotangent,
    logit_softness,
    block_grouping,
    neighborhood_span,
):
    seq_count = lax.axis_size("seq")
    position = lax.axis_index("seq")
    tokens = probe_vectors.shape[1]
    head_count = probe_vectors.shape[2] // HD
    local_blocks = tokens // BLK
    block_count = local_blocks * seq_count
    cluster_count = max(1, block_count // 8)
    capacity = min(12, block_count)
    owned_pairs = cluster_count * head_count // seq_count
    group_count = cluster_count // owned_pairs
    per_peer = max(1, local_blocks // group_count)
    cluster_ids = block_grouping[0, :, :, 0]
    query_home = head_major(probe_vectors[0], BLK)
    key_home = head_major(lookup_vectors[0], BLK)
    value_home = head_major(content_vectors[0], BLK)
    grad_home = head_major(result_cotangent[0], BLK)
    last_block = (lookup_vectors[0, tokens - BLK :], content_vectors[0, tokens - BLK :])
    prev_key_rows, prev_value_rows = shifted((last_block[0], last_block[1]), "seq", 1)
    prev_keys = jnp.concatenate([head_major(prev_key_rows, BLK), key_home[:, :-1]], axis=1)
    prev_values = jnp.concatenate([head_major(prev_value_rows, BLK), value_home[:, :-1]], axis=1)
    first_block = position * local_blocks
    before = jnp.concatenate(
        [jnp.full((head_count, 1), -1, jnp.int32), cluster_ids[:, :-1]], axis=1
    )
    my_ids = lax.dynamic_slice_in_dim(cluster_ids, first_block, local_blocks, 1)
    my_before = lax.dynamic_slice_in_dim(before, first_block, local_blocks, 1)
    global_block = first_block + jnp.arange(local_blocks)
    usable_home = (global_block[None, :] >= 1) & (my_before != my_ids)
    peer_index = jnp.arange(seq_count)
    peer_head = peer_index * owned_pairs // cluster_count
    slot_range = jnp.arange(per_peer)
    local_range = jnp.arange(local_blocks)
    owner_index = (jnp.arange(head_count)[:, None] * cluster_count + my_ids) // owned_pairs
    peer_ids = jnp.take(my_ids, peer_head, axis=0)
    goes = (peer_head[:, None] * cluster_count + peer_ids) // owned_pairs == peer_index[:, None]
    send_rank = jnp.cumsum(goes.astype(jnp.int32), axis=1) - 1
    send_pick = goes[:, None, :] & (send_rank[:, None, :] == slot_range[None, :, None])
    send_block = jnp.sum(jnp.where(send_pick, local_range[None, None, :], 0), axis=2)
    send_flat = peer_head[:, None] * local_blocks + send_block
    home_rank = jnp.take_along_axis(send_rank, owner_index, axis=0)
    home_pos = owner_index * per_peer + home_rank
    pair_index = position * owned_pairs + jnp.arange(owned_pairs)
    split_for_couple = pair_index // cluster_count
    pair_cluster = pair_index % cluster_count
    my_head = position * owned_pairs // cluster_count
    split_numbers = jnp.take(cluster_ids, my_head, axis=0)
    member = split_numbers[None, :] == pair_cluster[:, None]
    member_rank = jnp.cumsum(member.astype(jnp.int32), axis=1) - 1
    member_count = jnp.sum(member.astype(jnp.int32), axis=1)
    picked = member[:, None, :] & (member_rank[:, None, :] == jnp.arange(capacity)[None, :, None])
    member_block = jnp.sum(jnp.where(picked, jnp.arange(block_count)[None, None, :], 0), axis=2)
    live_members = jnp.arange(capacity)[None, :] < member_count[:, None]
    mine = (my_head * cluster_count + split_numbers) // owned_pairs == position
    mine_grid = mine.reshape(seq_count, local_blocks)
    recv_rank = jnp.cumsum(mine_grid.astype(jnp.int32), axis=1) - 1
    recv_pos = (peer_index[:, None] * per_peer + recv_rank).reshape(block_count)
    member_pos = jnp.take(recv_pos, member_block)
    couple_softness = jnp.take(logit_softness, split_for_couple)
    pair_onehot = (split_for_couple[:, None] == jnp.arange(head_count)[None, :]).astype(jnp.float32)
    slot_pair = my_head * cluster_count + split_numbers - position * owned_pairs
    same_cluster = split_numbers[:, None] == split_numbers[None, :]
    earlier_block = jnp.arange(block_count)[None, :] < jnp.arange(block_count)[:, None]
    slot_rank = jnp.sum((same_cluster & earlier_block).astype(jnp.int32), axis=1)
    back_pos = jnp.clip(slot_pair, 0, owned_pairs - 1) * capacity + jnp.clip(
        slot_rank, 0, capacity - 1
    )
    back_grid = back_pos.reshape(seq_count, local_blocks)
    back_pick = mine_grid[:, None, :] & (recv_rank[:, None, :] == slot_range[None, :, None])
    back_flat = jnp.sum(jnp.where(back_pick, back_grid[:, None, :], 0), axis=2)

    def to_peers(array_in):
        flat = array_in.reshape((head_count * local_blocks,) + array_in.shape[2:])
        return jnp.take(flat, send_flat, axis=0)

    def members(array_in):
        flat = array_in.reshape((seq_count * per_peer,) + array_in.shape[2:])
        return jnp.take(flat, member_pos, axis=0)

    def to_owner(array_in):
        flat = array_in.reshape((owned_pairs * capacity,) + array_in.shape[2:])
        return jnp.take(flat, back_flat, axis=0)

    def from_peers(array_in):
        flat = array_in.reshape((seq_count * per_peer,) + array_in.shape[2:])
        return jnp.take(flat, home_pos, axis=0)

    raw_w, mask_w, pgrad_w, top_w, total_w, mass_w = window_parts(
        query_home,
        prev_keys,
        prev_values,
        grad_home,
        usable_home,
        neighborhood_span[:, None],
        logit_softness[:, None],
    )
    arrived = (
        lax.all_to_all(to_peers(query_home), "seq", split_axis=0, concat_axis=0, tiled=True),
        lax.all_to_all(to_peers(key_home), "seq", split_axis=0, concat_axis=0, tiled=True),
        lax.all_to_all(to_peers(value_home), "seq", split_axis=0, concat_axis=0, tiled=True),
        lax.all_to_all(to_peers(grad_home), "seq", split_axis=0, concat_axis=0, tiled=True),
    )
    arrived_stats = (
        lax.all_to_all(to_peers(top_w), "seq", split_axis=0, concat_axis=0, tiled=True),
        lax.all_to_all(to_peers(total_w), "seq", split_axis=0, concat_axis=0, tiled=True),
        lax.all_to_all(to_peers(mass_w), "seq", split_axis=0, concat_axis=0, tiled=True),
    )
    query_m, key_m, value_m, grad_m = [members(item_in) for item_in in arrived]
    top_m, total_m, mass_m = [members(item_in) for item_in in arrived_stats]

    def split_pair(pair_inputs):
        query_i, key_i, value_i, grad_i, live_i, temper_i, top_i, total_i, mass_i = pair_inputs
        query_c, log_total, row_delta, key_c, value_c, temper_c = cluster_pair(
            query_i, key_i, value_i, grad_i, live_i, temper_i, top_i, total_i, mass_i
        )
        return (
            query_c.astype(jnp.bfloat16),
            key_c.astype(jnp.bfloat16),
            value_c.astype(jnp.bfloat16),
            log_total,
            row_delta,
            temper_c,
        )

    owner_results = lax.map(
        split_pair,
        (query_m, key_m, value_m, grad_m, live_members, couple_softness, top_m, total_m, mass_m),
    )
    returned = (
        lax.all_to_all(to_owner(owner_results[0]), "seq", split_axis=0, concat_axis=0, tiled=True),
        lax.all_to_all(to_owner(owner_results[1]), "seq", split_axis=0, concat_axis=0, tiled=True),
        lax.all_to_all(to_owner(owner_results[2]), "seq", split_axis=0, concat_axis=0, tiled=True),
    )
    returned_stats = (
        lax.all_to_all(to_owner(owner_results[3]), "seq", split_axis=0, concat_axis=0, tiled=True),
        lax.all_to_all(to_owner(owner_results[4]), "seq", split_axis=0, concat_axis=0, tiled=True),
    )
    query_cluster = from_peers(returned[0])
    key_cluster = from_peers(returned[1])
    value_cluster = from_peers(returned[2])
    log_home = from_peers(returned_stats[0])
    delta_home = from_peers(returned_stats[1])
    query_w, key_w, value_w, temper_w = window_grads(
        raw_w,
        mask_w,
        pgrad_w,
        query_home,
        prev_keys,
        grad_home,
        log_home,
        delta_home,
        logit_softness[:, None],
    )
    query_out = (query_cluster.astype(jnp.float32) + lifted(query_w)).astype(jnp.bfloat16)
    key_window = key_w.astype(jnp.bfloat16)
    value_window = value_w.astype(jnp.bfloat16)
    temper_local = jnp.sum(owner_results[5][:, None] * pair_onehot, axis=0) + jnp.sum(
        temper_w, axis=1
    )
    edge_keys, edge_values = shifted((key_window[:, 0], value_window[:, 0]), "seq", -1)
    key_next = jnp.concatenate([key_window[:, 1:], edge_keys[:, None]], axis=1)
    value_next = jnp.concatenate([value_window[:, 1:], edge_values[:, None]], axis=1)
    key_out = (key_cluster.astype(jnp.float32) + key_next.astype(jnp.float32)).astype(jnp.bfloat16)
    value_out = (value_cluster.astype(jnp.float32) + value_next.astype(jnp.float32)).astype(
        jnp.bfloat16
    )
    temper_total = lax.psum(temper_local, ("seq", "dp"))
    temper_grad = temper_total / (lax.axis_size("dp") * tokens * seq_count)
    return (token_major(query_out), token_major(key_out), token_major(value_out), temper_grad)


TILE = 256
EXTRA = 16
MIB = 1024 * 1024
QUERY, KEY, VALUE, GRAD = range(4)


def columns_of(index):
    return pl.ds(pl.multiple_of(index * HD, HD), HD)


def rows_of(index):
    return pl.ds(pl.multiple_of(index * BLK, BLK), BLK)


def tile_rows(tile):
    return slice(tile * TILE, (tile + 1) * TILE)


def position(half_count):
    me = lax.axis_index("seq")
    half = jnp.where(me >= half_count, 1, 0)
    return me, half, me - half * half_count


def kernel_call(kernel, name, operands, in_specs, out_shape, scratch, vmem_mib, flops=0):
    bytes_accessed = sum(
        math.prod(item.shape) * item.dtype.itemsize for item in (*operands, *out_shape)
    )
    return pl.pallas_call(
        kernel,
        out_shape=out_shape,
        in_specs=in_specs,
        out_specs=[pl.BlockSpec(memory_space=pltpu.VMEM)] * len(out_shape),
        scratch_shapes=scratch,
        cost_estimate=pl.CostEstimate(
            flops=flops, bytes_accessed=bytes_accessed, transcendentals=0
        ),
        compiler_params=pltpu.CompilerParams(vmem_limit_bytes=vmem_mib * MIB),
        name=name,
    )(*operands)


def pack_kernel(*refs, half_count):
    arrays, within_ref, across_refs = refs[:4], refs[4], refs[5 : 5 + half_count]
    held, arrival = refs[5 + half_count :]
    me, half, _ = position(half_count)
    copies = [
        pltpu.make_async_copy(array_ref.at[0], held.at[place], arrival.at[place])
        for place, array_ref in enumerate(arrays)
    ]
    for copy in copies:
        copy.start()
    for place, copy in enumerate(copies):
        copy.wait()
        for peer in range(half_count):
            for slot, base in enumerate((half * half_count, (1 - half) * half_count)):
                start = (slot * 4 + place) * BLK
                within_ref[peer, start : start + BLK, :] = held[
                    place, :, columns_of(base + peer)
                ]
    first = jnp.where(half == 0, KEY, QUERY)
    second = jnp.where(half == 0, VALUE, GRAD)
    for step, across_ref in enumerate(across_refs):
        columns = columns_of(me ^ (half_count + step))
        across_ref[:BLK, :] = held[first, :, columns]
        across_ref[BLK:, :] = held[second, :, columns]


def packed(arrays, half_count):
    width = arrays[0].shape[2]
    return kernel_call(
        functools.partial(pack_kernel, half_count=half_count),
        "pack_heads",
        arrays,
        [pl.BlockSpec(memory_space=pltpu.HBM)] * 4,
        [jax.ShapeDtypeStruct((half_count, 8 * BLK, HD), jnp.bfloat16)]
        + [jax.ShapeDtypeStruct((2 * BLK, HD), jnp.bfloat16)] * half_count,
        [pltpu.VMEM((4, BLK, width), jnp.bfloat16), pltpu.SemaphoreType.DMA((4,))],
        10,
    )


def dot_rows(left, right):
    return lax.dot_general(
        left, right, (((1,), (1,)), ((), ())), preferred_element_type=jnp.float32
    )


def dot_plain(left, right):
    return lax.dot_general(
        left, right, (((1,), (0,)), ((), ())), preferred_element_type=jnp.float32
    )


class Region:
    def __init__(self, head, settings, square, key_base, query_base, arrays, places):
        softness_ref, self.ids_ref, span_ref = settings
        self.head, self.square = head, square
        self.key_base, self.query_base = key_base, query_base
        self.arrays, self.places = arrays, places
        self.tiles = arrays.shape[1] // TILE
        self.width = span_ref[head]
        self.scaling = softness_ref[head] * (1.0 / math.sqrt(HD))
        self.to_log2 = self.scaling * math.log2(math.e)

    def rows(self, which, start, stop):
        return self.arrays[self.places[which], start * TILE : stop * TILE, :]

    def keys_of(self, tile):
        return range(self.tiles if self.square else tile + 1)

    def scores(self, tile_key, tile_query):
        per_tile = TILE // BLK
        scores = (
            dot_rows(
                self.rows(KEY, tile_key, tile_key + 1), self.rows(QUERY, tile_query, tile_query + 1)
            )
            * self.to_log2
        )
        spread = lax.broadcasted_iota(jnp.int32, (BLK, BLK), 0) - lax.broadcasted_iota(
            jnp.int32, (BLK, BLK), 1
        )
        rows = []
        for sub_key in range(per_tile):
            pieces = []
            for sub_query in range(per_tile):
                piece = scores[
                    sub_key * BLK : (sub_key + 1) * BLK, sub_query * BLK : (sub_query + 1) * BLK
                ]
                key_block = tile_key * per_tile + sub_key
                query_block = tile_query * per_tile + sub_query
                apart = query_block - key_block
                if self.square:
                    apart += self.tiles * per_tile
                same = (
                    self.ids_ref[self.head, self.key_base + key_block]
                    == self.ids_ref[self.head, self.query_base + query_block]
                )
                if apart < 0:
                    piece = jnp.full_like(piece, blocked_score)
                elif apart == 0:
                    piece = jnp.where(spread <= 0, piece, blocked_score)
                elif apart == 1:
                    least = jnp.where(same, -BLK, BLK - self.width)
                    piece = jnp.where(spread > least, piece, blocked_score)
                else:
                    piece = piece + jnp.where(same, 0.0, blocked_score)
                pieces.append(piece)
            rows.append(jnp.concatenate(pieces, axis=1))
        return jnp.concatenate(rows, axis=0)

    def statistics(self, score, out_ref, first_row):
        for tile in range(self.tiles):
            here = tile_rows(tile)
            top = jnp.full((1, TILE), blocked_score, jnp.float32)
            for other in self.keys_of(tile):
                raw = self.scores(other, tile)
                score[tile_rows(other), :] = raw
                top = jnp.maximum(top, jnp.max(raw, axis=0, keepdims=True))
            total = jnp.zeros((1, TILE), jnp.float32)
            mass = jnp.zeros((1, TILE), jnp.float32)
            for other in self.keys_of(tile):
                weight = jnp.exp2(score[tile_rows(other), :] - top)
                towards = dot_rows(
                    self.rows(VALUE, other, other + 1), self.rows(GRAD, tile, tile + 1)
                )
                total += jnp.sum(weight, axis=0, keepdims=True)
                mass += jnp.sum(weight * towards, axis=0, keepdims=True)
            out_ref[first_row : first_row + 1, here] = top
            out_ref[first_row + 1 : first_row + 2, here] = total
            out_ref[first_row + 2 : first_row + 3, here] = mass

    def gradients(self, log_total, delta, prob_low, grad_low, keys_flat):
        keys_flat[...] = self.rows(KEY, 0, self.tiles).T
        temper = jnp.zeros((1, HD), jnp.float32)
        query_parts, key_parts, value_parts = [], [], []
        for tile in range(self.tiles):
            here = tile_rows(tile)
            for other in self.keys_of(tile):
                there = tile_rows(other)
                probability = jnp.exp2(self.scores(other, tile) - log_total[:, here])
                towards = dot_rows(
                    self.rows(VALUE, other, other + 1), self.rows(GRAD, tile, tile + 1)
                )
                prob_low[there, here] = probability.astype(jnp.bfloat16)
                grad_low[there, here] = (probability * (towards - delta[:, here])).astype(
                    jnp.bfloat16
                )
            upto = slice(0, len(self.keys_of(tile)) * TILE)
            query_part = dot_plain(keys_flat[:, upto], grad_low[upto, here]).T
            temper += jnp.sum(
                query_part * self.rows(QUERY, tile, tile + 1).astype(jnp.float32),
                axis=0,
                keepdims=True,
            )
            query_parts.append(query_part)
        for tile in range(self.tiles):
            first = 0 if self.square else tile
            onward = slice(first * TILE, self.tiles * TILE)
            here = tile_rows(tile)
            key_parts.append(
                dot_plain(grad_low[here, onward], self.rows(QUERY, first, self.tiles))
            )
            value_parts.append(
                dot_plain(prob_low[here, onward], self.rows(GRAD, first, self.tiles))
            )
        return query_parts, key_parts, value_parts, temper


def merged(first, second):
    top = jnp.maximum(first[0], second[0])
    left, right = jnp.exp2(first[0] - top), jnp.exp2(second[0] - top)
    total = first[1] * left + second[1] * right
    mass = first[2] * left + second[2] * right
    return top + jnp.log2(total), mass / total


def alone(rows):
    return rows[0] + jnp.log2(rows[1]), rows[2] / rows[1]


def three_rows(ref, first):
    return [ref[first + row : first + row + 1, :] for row in range(3)]


def within_kernel(softness_ref, ids_ref, span_ref, in_ref, arrays_ref, stats_ref, score, *, half_count):
    me, half, _ = position(half_count)
    for block in range(half_count):
        for place in range(8):
            arrays_ref[place, block * BLK : (block + 1) * BLK, :] = in_ref[
                block, place * BLK : (place + 1) * BLK, :
            ]
    base = half * half_count
    settings = (softness_ref, ids_ref, span_ref)
    for slot, head in enumerate((me, me ^ half_count)):
        places = [slot * 4 + place for place in range(4)]
        region = Region(head, settings, False, base, base, arrays_ref, places)
        region.statistics(score, stats_ref, slot * 3)


def square_region(head, settings, half_count, square_ref):
    return Region(head, settings, True, 0, half_count, square_ref, range(4))


def square_kernel(
    softness_ref, ids_ref, span_ref, arrays_ref, stats_ref, *refs, half_count
):
    across_refs = refs[:half_count]
    square_ref, message_ref, own_ref, score, square_stats = refs[half_count:]
    me, half, place = position(half_count)
    first = jnp.where(half == 0, QUERY, KEY)
    second = jnp.where(half == 0, GRAD, VALUE)
    for step, across_ref in enumerate(across_refs):
        rows = rows_of(place ^ step)
        square_ref[first, rows, :] = across_ref[:BLK, :]
        square_ref[second, rows, :] = across_ref[BLK:, :]
    kept_first = jnp.where(half == 0, KEY, QUERY)
    kept_second = jnp.where(half == 0, VALUE, GRAD)
    square_ref[kept_first, :, :] = arrays_ref[kept_first, :, :]
    square_ref[kept_second, :, :] = arrays_ref[kept_second, :, :]
    region = square_region(me, (softness_ref, ids_ref, span_ref), half_count, square_ref)
    region.statistics(score, square_stats, 0)
    for row in range(3):
        message_ref[row : row + 1, :] = jnp.where(
            half == 0, square_stats[row : row + 1, :], stats_ref[3 + row : 4 + row, :]
        )
    diagonal = three_rows(stats_ref, 0)
    whole, single = merged(diagonal, three_rows(square_stats, 0)), alone(diagonal)
    for row in range(2):
        own_ref[row : row + 1, :] = jnp.where(half == 0, single[row], whole[row])


def diagonal_kernel(
    softness_ref, ids_ref, span_ref, arrays_ref, own_ref, parts_ref, temper_ref,
    prob_low, grad_low, keys_flat, *, half_count
):
    me, half, _ = position(half_count)
    base = half * half_count
    settings = (softness_ref, ids_ref, span_ref)
    region = Region(me, settings, False, base, base, arrays_ref, range(4))
    *parts, temper = region.gradients(
        own_ref[0:1, :], own_ref[1:2, :], prob_low, grad_low, keys_flat
    )
    for place, tiles in enumerate(parts):
        for tile, value in enumerate(tiles):
            parts_ref[place, tile_rows(tile), :] = value
    temper_ref[...] = jnp.broadcast_to(temper, temper_ref.shape)


def temper_rows(own, other):
    row = lax.broadcasted_iota(jnp.int32, (EXTRA, HD), 0)
    rows = jnp.zeros((EXTRA, HD), jnp.float32)
    for place, terms in enumerate((own, other)):
        rest = jnp.broadcast_to(jnp.sum(terms, axis=1, keepdims=True), (EXTRA, HD)) * (
            1.0 / math.sqrt(HD)
        )
        for piece in range(3):
            high = rest.astype(jnp.bfloat16).astype(jnp.float32)
            rows = jnp.where(row == place * 3 + piece, high, rows)
            rest = rest - high
    return rows.astype(jnp.bfloat16)


def finish_kernel(
    softness_ref, ids_ref, span_ref, arrays_ref, square_ref, message_ref, received_ref,
    own_ref, stats_ref, parts_ref, temper_ref, within_ref, *refs, half_count
):
    across_refs = refs[:half_count]
    across, prob_low, grad_low, keys_flat = refs[half_count:]
    me, half, place = position(half_count)
    base = half * half_count
    settings = (softness_ref, ids_ref, span_ref)
    per_tile = TILE // BLK

    def put(array, tile, value):
        for sub in range(per_tile):
            within_ref[tile * per_tile + sub, array * BLK : (array + 1) * BLK, :] = value[
                sub * BLK : (sub + 1) * BLK, :
            ]

    met = merged(three_rows(message_ref, 0), three_rows(received_ref, 0))
    log_total = jnp.where(half == 0, met[0], own_ref[0:1, :])
    delta = jnp.where(half == 0, met[1], own_ref[1:2, :])
    region = square_region(me, settings, half_count, square_ref)
    *square_parts, own_temper = region.gradients(log_total, delta, prob_low, grad_low, keys_flat)
    scales = (region.scaling, region.scaling, 1.0)
    for tile in range(region.tiles):
        query_part, key_part, value_part = [
            part[tile] * scale for part, scale in zip(square_parts, scales)
        ]
        here = tile_rows(tile)
        across[0, here, :] = jnp.where(half == 0, query_part, key_part).astype(jnp.bfloat16)
        across[1, here, :] = jnp.where(half == 0, 0.0, value_part).astype(jnp.bfloat16)
        query_kept, key_kept, value_kept = [
            parts_ref[array, here, :] * scale for array, scale in enumerate(scales)
        ]
        put(0, tile, (query_kept + jnp.where(half == 0, 0.0, query_part)).astype(jnp.bfloat16))
        put(1, tile, (key_kept + jnp.where(half == 0, key_part, 0.0)).astype(jnp.bfloat16))
        put(2, tile, (value_kept + jnp.where(half == 0, value_part, 0.0)).astype(jnp.bfloat16))
    single = alone(three_rows(stats_ref, 3))
    log_total = jnp.where(half == 0, single[0], met[0])
    delta = jnp.where(half == 0, single[1], met[1])
    region = Region(
        me ^ half_count, settings, False, base, base, arrays_ref, range(4, 8)
    )
    *other_parts, other_temper = region.gradients(log_total, delta, prob_low, grad_low, keys_flat)
    scales = (region.scaling, region.scaling, 1.0)
    for tile in range(region.tiles):
        for array, (part, scale) in enumerate(zip(other_parts, scales)):
            put(3 + array, tile, (part[tile] * scale).astype(jnp.bfloat16))
    pieces = temper_rows(own_temper + temper_ref[0:1, :], other_temper)
    for block in range(half_count):
        within_ref[block, 6 * BLK : 6 * BLK + EXTRA, :] = pieces
    for step, across_ref in enumerate(across_refs):
        rows = rows_of(place ^ step)
        across_ref[:BLK, :] = across[0, rows, :]
        across_ref[BLK : 2 * BLK, :] = across[1, rows, :]
        across_ref[2 * BLK :, :] = pieces


def unpack_kernel(within_ref, *refs, half_count):
    across_refs = refs[:half_count]
    query_ref, key_ref, value_ref, temper_ref = refs[half_count:]
    me, half, place = position(half_count)

    def sums(rows):
        return [
            jnp.sum(rows[3 * slot : 3 * slot + 3, :].astype(jnp.float32), axis=0, keepdims=True)
            for slot in range(2)
        ]

    for step, across_ref in enumerate(across_refs):
        peer = place ^ step
        other = columns_of((1 - half) * half_count + peer)
        own = columns_of(half * half_count + peer)
        parts = [within_ref[peer, array * BLK : (array + 1) * BLK, :] for array in range(6)]
        for array, out_ref in enumerate((query_ref, key_ref, value_ref)):
            out_ref[0, :, own] = parts[array]
        first = across_ref[:BLK, :].astype(jnp.float32)
        second = across_ref[BLK : 2 * BLK, :].astype(jnp.float32)
        added = (
            jnp.where(half == 0, 0.0, first),
            jnp.where(half == 0, first, 0.0),
            jnp.where(half == 0, second, 0.0),
        )
        for array, out_ref in enumerate((query_ref, key_ref, value_ref)):
            out_ref[0, :, other] = (parts[3 + array].astype(jnp.float32) + added[array]).astype(
                jnp.bfloat16
            )
        near = sums(within_ref[peer, 6 * BLK : 6 * BLK + EXTRA, :])
        far = sums(across_ref[2 * BLK :, :])
        temper_ref[pl.ds(half * half_count + peer, 1), :] = near[0] + far[1]
        temper_ref[pl.ds((1 - half) * half_count + peer, 1), :] = near[1] + far[0]


def crossed(chunks, half_count):
    pairs = range(2 * half_count)
    return [
        lax.ppermute(chunk, "seq", [(source, source ^ (half_count + step)) for source in pairs])
        for step, chunk in enumerate(chunks)
    ]


def head_shards(
    probe_vectors,
    lookup_vectors,
    content_vectors,
    result_cotangent,
    logit_softness,
    block_grouping,
    neighborhood_span,
):
    seq_count, dp_count = lax.axis_size("seq"), lax.axis_size("dp")
    half_count = seq_count // 2
    tokens = half_count * BLK
    groups = [list(range(half_count)), list(range(half_count, seq_count))]
    settings = (logit_softness, block_grouping[0, :, :, 0], neighborhood_span)
    smem, vmem = pl.BlockSpec(memory_space=pltpu.SMEM), pl.BlockSpec(memory_space=pltpu.VMEM)
    score = pltpu.VMEM((tokens, TILE), jnp.float32)
    lows = [pltpu.VMEM((tokens, tokens), jnp.bfloat16)] * 2 + [
        pltpu.VMEM((HD, tokens), jnp.bfloat16)
    ]
    rows_of_stats = jax.ShapeDtypeStruct((8, tokens), jnp.float32)
    pair_flops = 2 * tokens * tokens * HD

    def exchange_within(array_in):
        return lax.all_to_all(
            array_in, "seq", split_axis=0, concat_axis=0, axis_index_groups=groups, tiled=True
        )

    def call(kernel, name, operands, out_shape, scratch, flops):
        return kernel_call(
            functools.partial(kernel, half_count=half_count),
            name,
            (*settings, *operands),
            [smem] * 3 + [vmem] * len(operands),
            out_shape,
            scratch,
            20,
            flops,
        )

    sent, *foreign = packed(
        (probe_vectors, lookup_vectors, content_vectors, result_cotangent), half_count
    )
    arrived = exchange_within(sent)
    foreign = crossed(foreign, half_count)
    arrays, stats = call(
        within_kernel,
        "diagonal_statistics",
        (arrived,),
        [jax.ShapeDtypeStruct((8, tokens, HD), jnp.bfloat16), rows_of_stats],
        [score],
        2 * pair_flops,
    )
    square, message, own = call(
        square_kernel,
        "square_statistics",
        (arrays, stats, *foreign),
        [jax.ShapeDtypeStruct((4, tokens, HD), jnp.bfloat16), rows_of_stats, rows_of_stats],
        [score, pltpu.VMEM((8, tokens), jnp.float32)],
        2 * pair_flops,
    )
    swap = [(source, source ^ half_count) for source in range(seq_count)]
    received = lax.ppermute(message, "seq", swap)
    parts, temper = call(
        diagonal_kernel,
        "own_diagonal_gradients",
        (arrays, own),
        [
            jax.ShapeDtypeStruct((3, tokens, HD), jnp.float32),
            jax.ShapeDtypeStruct((8, HD), jnp.float32),
        ],
        lows,
        5 * pair_flops // 2,
    )
    within, *across = call(
        finish_kernel,
        "remaining_gradients",
        (arrays, square, message, received, own, stats, parts, temper),
        [jax.ShapeDtypeStruct((half_count, 6 * BLK + EXTRA, HD), jnp.bfloat16)]
        + [jax.ShapeDtypeStruct((2 * BLK + EXTRA, HD), jnp.bfloat16)] * half_count,
        [pltpu.VMEM((2, tokens, HD), jnp.bfloat16), *lows],
        8 * pair_flops,
    )
    across = crossed(across, half_count)
    within = exchange_within(within)
    result = jax.ShapeDtypeStruct(probe_vectors.shape, jnp.bfloat16)
    *outs, tempers = kernel_call(
        functools.partial(unpack_kernel, half_count=half_count),
        "unpack_heads",
        (within, *across),
        [vmem] * (1 + half_count),
        [result] * 3 + [jax.ShapeDtypeStruct((seq_count, HD), jnp.float32)],
        [],
        10,
    )
    temper_total = tempers
    for step in range(1, dp_count):
        pairs = [(source, (source + step) % dp_count) for source in range(dp_count)]
        temper_total = temper_total + lax.ppermute(tempers, "dp", pairs)
    return (*outs, temper_total[:, 0] / (dp_count * BLK * seq_count))


def shards(
    probe_vectors,
    lookup_vectors,
    content_vectors,
    result_cotangent,
    logit_softness,
    block_grouping,
    neighborhood_span,
):
    head_count = probe_vectors.shape[2] // HD
    seq_count = lax.axis_size("seq")
    one_block = probe_vectors.shape[1] == BLK
    whole_tiles = seq_count * BLK % (2 * TILE) == 0 and seq_count & (seq_count - 1) == 0
    if head_count == seq_count and one_block and whole_tiles:
        plan = head_shards
    else:
        plan = clustered_shards
    return plan(
        probe_vectors,
        lookup_vectors,
        content_vectors,
        result_cotangent,
        logit_softness,
        block_grouping,
        neighborhood_span,
    )


def solution(mesh):
    in_specs = (
        P("dp", "seq", None),
        P("dp", "seq", None),
        P("dp", "seq", None),
        P("dp", "seq", None),
        P(),
        P("dp", None, None, None),
        P(),
    )
    out_specs = (P("dp", "seq", None), P("dp", "seq", None), P("dp", "seq", None), P())
    return jax.shard_map(shards, mesh=mesh, in_specs=in_specs, out_specs=out_specs, check_vma=False)
```

```python
import functools
import math

import jax
import jax.numpy as jnp
from jax import lax
from jax.experimental import pallas as pl
from jax.experimental.pallas import tpu as pltpu
from jax.sharding import PartitionSpec as P

HD = 128
BLK = 128


blocked_score = -1e30


def shifted(value, axis, steps):
    count = lax.axis_size(axis)
    first, last = (max(0, -steps), min(count, count - steps))
    return lax.ppermute(value, axis, [(source, source + steps) for source in range(first, last)])


def lifted(array_in):
    return lax.optimization_barrier(array_in.astype(jnp.bfloat16)).astype(jnp.float32)


def head_major(tokens_in, block_len):
    token_count, feature_count = tokens_in.shape
    return tokens_in.reshape(
        token_count // block_len, block_len, feature_count // HD, HD
    ).transpose(2, 0, 1, 3)


def token_major(blocks_in):
    head_count, block_count, block_len, depth = blocks_in.shape
    return blocks_in.transpose(1, 2, 0, 3).reshape(1, block_count * block_len, head_count * depth)


def window_parts(query_block, prev_keys, prev_values, grad_block, usable, window_width, temper):
    block_len = query_block.shape[-2]
    inverse_root = 1.0 / math.sqrt(query_block.shape[-1])
    raw_scores = (
        jnp.einsum("...td,...sd->...ts", query_block, prev_keys, preferred_element_type=jnp.float32)
        * inverse_root
    )
    query_pos = lax.broadcasted_iota(jnp.int32, (block_len, block_len), 0)
    key_pos = lax.broadcasted_iota(jnp.int32, (block_len, block_len), 1)
    pair_mask = usable[..., None, None] & (
        key_pos > query_pos + block_len - window_width[..., None, None]
    )
    scores = temper[..., None, None] * raw_scores
    row_top = jnp.max(jnp.where(pair_mask, scores, blocked_score), axis=-1)
    weights = jnp.where(pair_mask, jnp.exp(scores - row_top[..., None]), 0.0)
    prob_grad = jnp.einsum(
        "...td,...sd->...ts", grad_block, prev_values, preferred_element_type=jnp.float32
    )
    return (
        raw_scores,
        pair_mask,
        prob_grad,
        row_top,
        jnp.sum(weights, axis=-1),
        jnp.sum(weights * prob_grad, axis=-1),
    )


def window_grads(
    raw_scores,
    pair_mask,
    prob_grad,
    query_block,
    prev_keys,
    grad_block,
    log_total,
    row_delta,
    temper,
):
    inverse_root = 1.0 / math.sqrt(query_block.shape[-1])
    scaling = (temper * inverse_root)[..., None, None]
    probability = jnp.where(
        pair_mask, jnp.exp(temper[..., None, None] * raw_scores - log_total[..., None]), 0.0
    )
    score_grad = probability * (prob_grad - row_delta[..., None])
    prob_low = probability.astype(jnp.bfloat16)
    grad_low = score_grad.astype(jnp.bfloat16)
    query_part = (
        jnp.einsum("...ts,...sd->...td", grad_low, prev_keys, preferred_element_type=jnp.float32)
        * scaling
    )
    key_part = (
        jnp.einsum("...ts,...td->...sd", grad_low, query_block, preferred_element_type=jnp.float32)
        * scaling
    )
    value_part = jnp.einsum(
        "...ts,...td->...sd", prob_low, grad_block, preferred_element_type=jnp.float32
    )
    temper_part = jnp.sum(score_grad * raw_scores, axis=(-2, -1))
    return (query_part, key_part, value_part, temper_part)


def cluster_pair(
    query_items,
    key_items,
    value_items,
    grad_items,
    live_items,
    temper,
    window_top,
    window_total,
    window_mass,
):
    item_count, block_len, depth = query_items.shape
    row_count = item_count * block_len
    group_rows = 4 * block_len
    inverse_root = 1.0 / math.sqrt(depth)
    scaling = temper * inverse_root
    query_rows = query_items.reshape(row_count, depth)
    key_rows = key_items.reshape(row_count, depth)
    value_rows = value_items.reshape(row_count, depth)
    grad_rows = grad_items.reshape(row_count, depth)
    key_item = jnp.arange(row_count) // block_len
    key_token = jnp.arange(row_count) % block_len
    live_rows = jnp.repeat(live_items, block_len)
    top_rows = window_top.reshape(row_count)
    total_rows = window_total.reshape(row_count)
    mass_rows = window_mass.reshape(row_count)

    def group_step(carry, start_row):
        key_acc, value_acc, temper_acc = carry
        query_group = lax.dynamic_slice_in_dim(query_rows, start_row, group_rows, 0)
        grad_group = lax.dynamic_slice_in_dim(grad_rows, start_row, group_rows, 0)
        group_live = lax.dynamic_slice_in_dim(live_rows, start_row, group_rows, 0)
        group_top = lax.dynamic_slice_in_dim(top_rows, start_row, group_rows, 0)
        group_total = lax.dynamic_slice_in_dim(total_rows, start_row, group_rows, 0)
        group_mass = lax.dynamic_slice_in_dim(mass_rows, start_row, group_rows, 0)
        query_item = (start_row + jnp.arange(group_rows)) // block_len
        query_token = jnp.arange(group_rows) % block_len
        earlier = (key_item[None, :] < query_item[:, None]) | (
            key_item[None, :] == query_item[:, None]
        ) & (key_token[None, :] <= query_token[:, None])
        pair_mask = group_live[:, None] & live_rows[None, :] & earlier
        raw_scores = (
            lax.dot_general(
                query_group, key_rows, (((1,), (1,)), ((), ())), preferred_element_type=jnp.float32
            )
            * inverse_root
        )
        scores = temper * raw_scores
        row_top = jnp.maximum(
            jnp.max(jnp.where(pair_mask, scores, blocked_score), axis=1), group_top
        )
        weights = jnp.where(pair_mask, jnp.exp(scores - row_top[:, None]), 0.0)
        row_total = jnp.sum(weights, axis=1) + group_total * jnp.exp(group_top - row_top)
        log_total = row_top + jnp.log(jnp.where(group_live, row_total, 1.0))
        probability = jnp.where(pair_mask, jnp.exp(scores - log_total[:, None]), 0.0)
        prob_grad = lax.dot_general(
            grad_group, value_rows, (((1,), (1,)), ((), ())), preferred_element_type=jnp.float32
        )
        row_delta = jnp.sum(probability * prob_grad, axis=1) + group_mass * jnp.exp(
            group_top - log_total
        )
        score_grad = probability * (prob_grad - row_delta[:, None])
        prob_low = probability.astype(jnp.bfloat16)
        grad_low = score_grad.astype(jnp.bfloat16)
        query_part = jnp.dot(grad_low, key_rows, preferred_element_type=jnp.float32) * scaling
        key_acc = (
            key_acc
            + lax.dot_general(
                grad_low, query_group, (((0,), (0,)), ((), ())), preferred_element_type=jnp.float32
            )
            * scaling
        )
        value_acc = value_acc + lax.dot_general(
            prob_low, grad_group, (((0,), (0,)), ((), ())), preferred_element_type=jnp.float32
        )
        temper_acc = temper_acc + jnp.sum(score_grad * raw_scores)
        return ((key_acc, value_acc, temper_acc), (query_part, log_total, row_delta))

    start_rows = jnp.arange(item_count // 4) * group_rows
    initial = (
        jnp.zeros((row_count, depth), jnp.float32),
        jnp.zeros((row_count, depth), jnp.float32),
        jnp.zeros((), jnp.float32),
    )
    (key_acc, value_acc, temper_acc), (query_part, log_total, row_delta) = lax.scan(
        group_step, initial, start_rows
    )
    return (
        query_part.reshape(item_count, block_len, depth),
        log_total.reshape(item_count, block_len),
        row_delta.reshape(item_count, block_len),
        key_acc.reshape(item_count, block_len, depth),
        value_acc.reshape(item_count, block_len, depth),
        temper_acc,
    )


def clustered_shards(
    probe_vectors,
    lookup_vectors,
    content_vectors,
    result_cotangent,
    logit_softness,
    block_grouping,
    neighborhood_span,
):
    seq_count = lax.axis_size("seq")
    position = lax.axis_index("seq")
    tokens = probe_vectors.shape[1]
    head_count = probe_vectors.shape[2] // HD
    local_blocks = tokens // BLK
    block_count = local_blocks * seq_count
    cluster_count = max(1, block_count // 8)
    capacity = min(12, block_count)
    owned_pairs = cluster_count * head_count // seq_count
    group_count = cluster_count // owned_pairs
    per_peer = max(1, local_blocks // group_count)
    cluster_ids = block_grouping[0, :, :, 0]
    query_home = head_major(probe_vectors[0], BLK)
    key_home = head_major(lookup_vectors[0], BLK)
    value_home = head_major(content_vectors[0], BLK)
    grad_home = head_major(result_cotangent[0], BLK)
    last_block = (lookup_vectors[0, tokens - BLK :], content_vectors[0, tokens - BLK :])
    prev_key_rows, prev_value_rows = shifted((last_block[0], last_block[1]), "seq", 1)
    prev_keys = jnp.concatenate([head_major(prev_key_rows, BLK), key_home[:, :-1]], axis=1)
    prev_values = jnp.concatenate([head_major(prev_value_rows, BLK), value_home[:, :-1]], axis=1)
    first_block = position * local_blocks
    before = jnp.concatenate(
        [jnp.full((head_count, 1), -1, jnp.int32), cluster_ids[:, :-1]], axis=1
    )
    my_ids = lax.dynamic_slice_in_dim(cluster_ids, first_block, local_blocks, 1)
    my_before = lax.dynamic_slice_in_dim(before, first_block, local_blocks, 1)
    global_block = first_block + jnp.arange(local_blocks)
    usable_home = (global_block[None, :] >= 1) & (my_before != my_ids)
    peer_index = jnp.arange(seq_count)
    peer_head = peer_index * owned_pairs // cluster_count
    slot_range = jnp.arange(per_peer)
    local_range = jnp.arange(local_blocks)
    owner_index = (jnp.arange(head_count)[:, None] * cluster_count + my_ids) // owned_pairs
    peer_ids = jnp.take(my_ids, peer_head, axis=0)
    goes = (peer_head[:, None] * cluster_count + peer_ids) // owned_pairs == peer_index[:, None]
    send_rank = jnp.cumsum(goes.astype(jnp.int32), axis=1) - 1
    send_pick = goes[:, None, :] & (send_rank[:, None, :] == slot_range[None, :, None])
    send_block = jnp.sum(jnp.where(send_pick, local_range[None, None, :], 0), axis=2)
    send_flat = peer_head[:, None] * local_blocks + send_block
    home_rank = jnp.take_along_axis(send_rank, owner_index, axis=0)
    home_pos = owner_index * per_peer + home_rank
    pair_index = position * owned_pairs + jnp.arange(owned_pairs)
    split_for_couple = pair_index // cluster_count
    pair_cluster = pair_index % cluster_count
    my_head = position * owned_pairs // cluster_count
    split_numbers = jnp.take(cluster_ids, my_head, axis=0)
    member = split_numbers[None, :] == pair_cluster[:, None]
    member_rank = jnp.cumsum(member.astype(jnp.int32), axis=1) - 1
    member_count = jnp.sum(member.astype(jnp.int32), axis=1)
    picked = member[:, None, :] & (member_rank[:, None, :] == jnp.arange(capacity)[None, :, None])
    member_block = jnp.sum(jnp.where(picked, jnp.arange(block_count)[None, None, :], 0), axis=2)
    live_members = jnp.arange(capacity)[None, :] < member_count[:, None]
    mine = (my_head * cluster_count + split_numbers) // owned_pairs == position
    mine_grid = mine.reshape(seq_count, local_blocks)
    recv_rank = jnp.cumsum(mine_grid.astype(jnp.int32), axis=1) - 1
    recv_pos = (peer_index[:, None] * per_peer + recv_rank).reshape(block_count)
    member_pos = jnp.take(recv_pos, member_block)
    couple_softness = jnp.take(logit_softness, split_for_couple)
    pair_onehot = (split_for_couple[:, None] == jnp.arange(head_count)[None, :]).astype(jnp.float32)
    slot_pair = my_head * cluster_count + split_numbers - position * owned_pairs
    same_cluster = split_numbers[:, None] == split_numbers[None, :]
    earlier_block = jnp.arange(block_count)[None, :] < jnp.arange(block_count)[:, None]
    slot_rank = jnp.sum((same_cluster & earlier_block).astype(jnp.int32), axis=1)
    back_pos = jnp.clip(slot_pair, 0, owned_pairs - 1) * capacity + jnp.clip(
        slot_rank, 0, capacity - 1
    )
    back_grid = back_pos.reshape(seq_count, local_blocks)
    back_pick = mine_grid[:, None, :] & (recv_rank[:, None, :] == slot_range[None, :, None])
    back_flat = jnp.sum(jnp.where(back_pick, back_grid[:, None, :], 0), axis=2)

    def to_peers(array_in):
        flat = array_in.reshape((head_count * local_blocks,) + array_in.shape[2:])
        return jnp.take(flat, send_flat, axis=0)

    def members(array_in):
        flat = array_in.reshape((seq_count * per_peer,) + array_in.shape[2:])
        return jnp.take(flat, member_pos, axis=0)

    def to_owner(array_in):
        flat = array_in.reshape((owned_pairs * capacity,) + array_in.shape[2:])
        return jnp.take(flat, back_flat, axis=0)

    def from_peers(array_in):
        flat = array_in.reshape((seq_count * per_peer,) + array_in.shape[2:])
        return jnp.take(flat, home_pos, axis=0)

    raw_w, mask_w, pgrad_w, top_w, total_w, mass_w = window_parts(
        query_home,
        prev_keys,
        prev_values,
        grad_home,
        usable_home,
        neighborhood_span[:, None],
        logit_softness[:, None],
    )
    arrived = (
        lax.all_to_all(to_peers(query_home), "seq", split_axis=0, concat_axis=0, tiled=True),
        lax.all_to_all(to_peers(key_home), "seq", split_axis=0, concat_axis=0, tiled=True),
        lax.all_to_all(to_peers(value_home), "seq", split_axis=0, concat_axis=0, tiled=True),
        lax.all_to_all(to_peers(grad_home), "seq", split_axis=0, concat_axis=0, tiled=True),
    )
    arrived_stats = (
        lax.all_to_all(to_peers(top_w), "seq", split_axis=0, concat_axis=0, tiled=True),
        lax.all_to_all(to_peers(total_w), "seq", split_axis=0, concat_axis=0, tiled=True),
        lax.all_to_all(to_peers(mass_w), "seq", split_axis=0, concat_axis=0, tiled=True),
    )
    query_m, key_m, value_m, grad_m = [members(item_in) for item_in in arrived]
    top_m, total_m, mass_m = [members(item_in) for item_in in arrived_stats]

    def split_pair(pair_inputs):
        query_i, key_i, value_i, grad_i, live_i, temper_i, top_i, total_i, mass_i = pair_inputs
        query_c, log_total, row_delta, key_c, value_c, temper_c = cluster_pair(
            query_i, key_i, value_i, grad_i, live_i, temper_i, top_i, total_i, mass_i
        )
        return (
            query_c.astype(jnp.bfloat16),
            key_c.astype(jnp.bfloat16),
            value_c.astype(jnp.bfloat16),
            log_total,
            row_delta,
            temper_c,
        )

    owner_results = lax.map(
        split_pair,
        (query_m, key_m, value_m, grad_m, live_members, couple_softness, top_m, total_m, mass_m),
    )
    returned = (
        lax.all_to_all(to_owner(owner_results[0]), "seq", split_axis=0, concat_axis=0, tiled=True),
        lax.all_to_all(to_owner(owner_results[1]), "seq", split_axis=0, concat_axis=0, tiled=True),
        lax.all_to_all(to_owner(owner_results[2]), "seq", split_axis=0, concat_axis=0, tiled=True),
    )
    returned_stats = (
        lax.all_to_all(to_owner(owner_results[3]), "seq", split_axis=0, concat_axis=0, tiled=True),
        lax.all_to_all(to_owner(owner_results[4]), "seq", split_axis=0, concat_axis=0, tiled=True),
    )
    query_cluster = from_peers(returned[0])
    key_cluster = from_peers(returned[1])
    value_cluster = from_peers(returned[2])
    log_home = from_peers(returned_stats[0])
    delta_home = from_peers(returned_stats[1])
    query_w, key_w, value_w, temper_w = window_grads(
        raw_w,
        mask_w,
        pgrad_w,
        query_home,
        prev_keys,
        grad_home,
        log_home,
        delta_home,
        logit_softness[:, None],
    )
    query_out = (query_cluster.astype(jnp.float32) + lifted(query_w)).astype(jnp.bfloat16)
    key_window = key_w.astype(jnp.bfloat16)
    value_window = value_w.astype(jnp.bfloat16)
    temper_local = jnp.sum(owner_results[5][:, None] * pair_onehot, axis=0) + jnp.sum(
        temper_w, axis=1
    )
    edge_keys, edge_values = shifted((key_window[:, 0], value_window[:, 0]), "seq", -1)
    key_next = jnp.concatenate([key_window[:, 1:], edge_keys[:, None]], axis=1)
    value_next = jnp.concatenate([value_window[:, 1:], edge_values[:, None]], axis=1)
    key_out = (key_cluster.astype(jnp.float32) + key_next.astype(jnp.float32)).astype(jnp.bfloat16)
    value_out = (value_cluster.astype(jnp.float32) + value_next.astype(jnp.float32)).astype(
        jnp.bfloat16
    )
    temper_total = lax.psum(temper_local, ("seq", "dp"))
    temper_grad = temper_total / (lax.axis_size("dp") * tokens * seq_count)
    return (token_major(query_out), token_major(key_out), token_major(value_out), temper_grad)


TILE = 256
EXTRA = 16
MIB = 1024 * 1024
PIECES = 4
QUERY, KEY, VALUE, GRAD = range(4)


def columns_of(index):
    return pl.ds(pl.multiple_of(index * HD, HD), HD)


def rows_of(index):
    return pl.ds(pl.multiple_of(index * BLK, BLK), BLK)


def tile_rows(tile):
    return slice(tile * TILE, (tile + 1) * TILE)


def position(half_count):
    me = lax.axis_index("seq")
    half = jnp.where(me >= half_count, 1, 0)
    return me, half, me - half * half_count


def kernel_call(
    kernel, name, operands, in_specs, out_shape, scratch, vmem_mib, flops=0, out_space=pltpu.VMEM
):
    bytes_accessed = sum(
        math.prod(item.shape) * item.dtype.itemsize for item in (*operands, *out_shape)
    )
    return pl.pallas_call(
        kernel,
        out_shape=out_shape,
        in_specs=in_specs,
        out_specs=[pl.BlockSpec(memory_space=out_space)] * len(out_shape),
        scratch_shapes=scratch,
        cost_estimate=pl.CostEstimate(
            flops=flops, bytes_accessed=bytes_accessed, transcendentals=0
        ),
        compiler_params=pltpu.CompilerParams(vmem_limit_bytes=vmem_mib * MIB),
        name=name,
    )(*operands)


def pack_kernel(*refs, half_count):
    arrays, within_ref, across_refs = refs[:4], refs[4], refs[5 : 5 + half_count]
    held, within, across, arrival, left_within, left_across = refs[5 + half_count :]
    me, half, _ = position(half_count)
    piece = BLK // PIECES
    arrivals = [
        [
            pltpu.make_async_copy(
                array_ref.at[0, part * piece : (part + 1) * piece, :],
                held.at[place, part * piece : (part + 1) * piece, :],
                arrival.at[place, part],
            )
            for part in range(PIECES)
        ]
        for place, array_ref in enumerate(arrays)
    ]
    for copies in arrivals:
        for copy in copies:
            copy.start()
    leaving = []
    for place, copies in enumerate(arrivals):
        for copy in copies:
            copy.wait()
        for slot, base in enumerate((half * half_count, (1 - half) * half_count)):
            rows = slice((slot * 4 + place) * BLK, (slot * 4 + place + 1) * BLK)
            for peer in range(half_count):
                within[peer, rows, :] = held[place, :, columns_of(base + peer)]
            leaving.append(
                pltpu.make_async_copy(
                    within.at[:, rows, :], within_ref.at[:, rows, :], left_within.at[place, slot]
                )
            )
            leaving[-1].start()
    first = jnp.where(half == 0, KEY, QUERY)
    second = jnp.where(half == 0, VALUE, GRAD)
    for step, across_ref in enumerate(across_refs):
        columns = columns_of(me ^ (half_count + step))
        across[step, :BLK, :] = held[first, :, columns]
        across[step, BLK:, :] = held[second, :, columns]
        leaving.append(
            pltpu.make_async_copy(across.at[step], across_ref, left_across.at[step])
        )
        leaving[-1].start()
    for copy in leaving:
        copy.wait()


def packed(arrays, half_count):
    width = arrays[0].shape[2]
    within_shape, across_shape = (half_count, 8 * BLK, HD), (2 * BLK, HD)
    return kernel_call(
        functools.partial(pack_kernel, half_count=half_count),
        "pack_heads",
        arrays,
        [pl.BlockSpec(memory_space=pl.ANY)] * 4,
        [jax.ShapeDtypeStruct(within_shape, jnp.bfloat16)]
        + [jax.ShapeDtypeStruct(across_shape, jnp.bfloat16)] * half_count,
        [
            pltpu.VMEM((4, BLK, width), jnp.bfloat16),
            pltpu.VMEM(within_shape, jnp.bfloat16),
            pltpu.VMEM((half_count, *across_shape), jnp.bfloat16),
            pltpu.SemaphoreType.DMA((4, PIECES)),
            pltpu.SemaphoreType.DMA((4, 2)),
            pltpu.SemaphoreType.DMA((half_count,)),
        ],
        60,
        out_space=pl.ANY,
    )


def dot_rows(left, right):
    return lax.dot_general(
        left, right, (((1,), (1,)), ((), ())), preferred_element_type=jnp.float32
    )


def dot_plain(left, right):
    return lax.dot_general(
        left, right, (((1,), (0,)), ((), ())), preferred_element_type=jnp.float32
    )


class Region:
    def __init__(self, head, settings, square, key_base, query_base, arrays, places):
        softness_ref, self.ids_ref, span_ref = settings
        self.head, self.square = head, square
        self.key_base, self.query_base = key_base, query_base
        self.arrays, self.places = arrays, places
        self.tiles = arrays.shape[1] // TILE
        self.width = span_ref[head]
        self.scaling = softness_ref[head] * (1.0 / math.sqrt(HD))
        self.to_log2 = self.scaling * math.log2(math.e)

    def rows(self, which, start, stop):
        return self.arrays[self.places[which], start * TILE : stop * TILE, :]

    def keys_of(self, tile):
        return range(self.tiles if self.square else tile + 1)

    def scores(self, tile_key, tile_query):
        per_tile = TILE // BLK
        scores = (
            dot_rows(
                self.rows(KEY, tile_key, tile_key + 1), self.rows(QUERY, tile_query, tile_query + 1)
            )
            * self.to_log2
        )
        spread = lax.broadcasted_iota(jnp.int32, (BLK, BLK), 0) - lax.broadcasted_iota(
            jnp.int32, (BLK, BLK), 1
        )
        rows = []
        for sub_key in range(per_tile):
            pieces = []
            for sub_query in range(per_tile):
                piece = scores[
                    sub_key * BLK : (sub_key + 1) * BLK, sub_query * BLK : (sub_query + 1) * BLK
                ]
                key_block = tile_key * per_tile + sub_key
                query_block = tile_query * per_tile + sub_query
                apart = query_block - key_block
                if self.square:
                    apart += self.tiles * per_tile
                same = (
                    self.ids_ref[self.head, self.key_base + key_block]
                    == self.ids_ref[self.head, self.query_base + query_block]
                )
                if apart < 0:
                    piece = jnp.full_like(piece, blocked_score)
                elif apart == 0:
                    piece = jnp.where(spread <= 0, piece, blocked_score)
                elif apart == 1:
                    least = jnp.where(same, -BLK, BLK - self.width)
                    piece = jnp.where(spread > least, piece, blocked_score)
                else:
                    piece = piece + jnp.where(same, 0.0, blocked_score)
                pieces.append(piece)
            rows.append(jnp.concatenate(pieces, axis=1))
        return jnp.concatenate(rows, axis=0)

    def statistics(self, weight_ref, towards_ref, out_ref, first_row):
        for tile in range(self.tiles):
            here = tile_rows(tile)
            top = jnp.full((1, TILE), blocked_score, jnp.float32)
            for other in self.keys_of(tile):
                raw = self.scores(other, tile)
                weight_ref[tile_rows(other), here] = raw
                top = jnp.maximum(top, jnp.max(raw, axis=0, keepdims=True))
            total = jnp.zeros((1, TILE), jnp.float32)
            mass = jnp.zeros((1, TILE), jnp.float32)
            for other in self.keys_of(tile):
                there = tile_rows(other)
                weight = jnp.exp2(weight_ref[there, here] - top)
                towards = dot_rows(
                    self.rows(VALUE, other, other + 1), self.rows(GRAD, tile, tile + 1)
                )
                weight_ref[there, here] = weight
                towards_ref[there, here] = towards
                total += jnp.sum(weight, axis=0, keepdims=True)
                mass += jnp.sum(weight * towards, axis=0, keepdims=True)
            out_ref[first_row : first_row + 1, here] = top
            out_ref[first_row + 1 : first_row + 2, here] = total
            out_ref[first_row + 2 : first_row + 3, here] = mass

    def gradients(self, weight_ref, towards_ref, top, log_total, delta, prob_low, grad_low, keys_flat):
        keys_flat[...] = self.rows(KEY, 0, self.tiles).T
        share = jnp.exp2(top - log_total)
        temper = jnp.zeros((1, HD), jnp.float32)
        query_parts, key_parts, value_parts = [], [], []
        for tile in range(self.tiles):
            here = tile_rows(tile)
            for other in self.keys_of(tile):
                there = tile_rows(other)
                probability = weight_ref[there, here] * share[:, here]
                prob_low[there, here] = probability.astype(jnp.bfloat16)
                grad_low[there, here] = (
                    probability * (towards_ref[there, here] - delta[:, here])
                ).astype(jnp.bfloat16)
            upto = slice(0, len(self.keys_of(tile)) * TILE)
            query_part = dot_plain(keys_flat[:, upto], grad_low[upto, here]).T
            temper += jnp.sum(
                query_part * self.rows(QUERY, tile, tile + 1).astype(jnp.float32),
                axis=0,
                keepdims=True,
            )
            query_parts.append(query_part)
        for tile in range(self.tiles):
            first = 0 if self.square else tile
            onward = slice(first * TILE, self.tiles * TILE)
            here = tile_rows(tile)
            key_parts.append(
                dot_plain(grad_low[here, onward], self.rows(QUERY, first, self.tiles))
            )
            value_parts.append(
                dot_plain(prob_low[here, onward], self.rows(GRAD, first, self.tiles))
            )
        return query_parts, key_parts, value_parts, temper


def merged(first, second):
    top = jnp.maximum(first[0], second[0])
    left, right = jnp.exp2(first[0] - top), jnp.exp2(second[0] - top)
    total = first[1] * left + second[1] * right
    mass = first[2] * left + second[2] * right
    return top + jnp.log2(total), mass / total


def alone(rows):
    return rows[0] + jnp.log2(rows[1]), rows[2] / rows[1]


def three_rows(ref, first):
    return [ref[first + row : first + row + 1, :] for row in range(3)]


def within_kernel(
    softness_ref, ids_ref, span_ref, in_ref, arrays_ref, stats_ref,
    own_weight, own_towards, other_weight, other_towards, *, half_count
):
    me, half, _ = position(half_count)
    for block in range(half_count):
        for place in range(8):
            arrays_ref[place, block * BLK : (block + 1) * BLK, :] = in_ref[
                block, place * BLK : (place + 1) * BLK, :
            ]
    base = half * half_count
    settings = (softness_ref, ids_ref, span_ref)
    for slot, head in enumerate((me, me ^ half_count)):
        places = [slot * 4 + place for place in range(4)]
        region = Region(head, settings, False, base, base, arrays_ref, places)
        kept = ((own_weight, own_towards), (other_weight, other_towards))[slot]
        region.statistics(*kept, stats_ref, slot * 3)


def square_region(head, settings, half_count, square_ref):
    return Region(head, settings, True, 0, half_count, square_ref, range(4))


def square_kernel(
    softness_ref, ids_ref, span_ref, arrays_ref, stats_ref, *refs, half_count
):
    across_refs = refs[:half_count]
    square_ref, message_ref, own_ref, square_stats, weight, towards = refs[half_count:]
    me, half, place = position(half_count)
    first = jnp.where(half == 0, QUERY, KEY)
    second = jnp.where(half == 0, GRAD, VALUE)
    for step, across_ref in enumerate(across_refs):
        rows = rows_of(place ^ step)
        square_ref[first, rows, :] = across_ref[:BLK, :]
        square_ref[second, rows, :] = across_ref[BLK:, :]
    kept_first = jnp.where(half == 0, KEY, QUERY)
    kept_second = jnp.where(half == 0, VALUE, GRAD)
    square_ref[kept_first, :, :] = arrays_ref[kept_first, :, :]
    square_ref[kept_second, :, :] = arrays_ref[kept_second, :, :]
    region = square_region(me, (softness_ref, ids_ref, span_ref), half_count, square_ref)
    region.statistics(weight, towards, square_stats, 0)
    for row in range(3):
        message_ref[row : row + 1, :] = jnp.where(
            half == 0, square_stats[row : row + 1, :], stats_ref[3 + row : 4 + row, :]
        )
    diagonal = three_rows(stats_ref, 0)
    whole, single = merged(diagonal, three_rows(square_stats, 0)), alone(diagonal)
    for row in range(2):
        own_ref[row : row + 1, :] = jnp.where(half == 0, single[row], whole[row])


def diagonal_kernel(
    softness_ref, ids_ref, span_ref, arrays_ref, own_ref, stats_ref, weight, towards,
    parts_ref, temper_ref, prob_low, grad_low, keys_flat, *, half_count
):
    me, half, _ = position(half_count)
    base = half * half_count
    settings = (softness_ref, ids_ref, span_ref)
    region = Region(me, settings, False, base, base, arrays_ref, range(4))
    *parts, temper = region.gradients(
        weight, towards, stats_ref[0:1, :], own_ref[0:1, :], own_ref[1:2, :],
        prob_low, grad_low, keys_flat,
    )
    for place, tiles in enumerate(parts):
        for tile, value in enumerate(tiles):
            parts_ref[place, tile_rows(tile), :] = value
    temper_ref[...] = jnp.broadcast_to(temper, temper_ref.shape)


def temper_rows(own, other):
    row = lax.broadcasted_iota(jnp.int32, (EXTRA, HD), 0)
    rows = jnp.zeros((EXTRA, HD), jnp.float32)
    for place, terms in enumerate((own, other)):
        rest = jnp.broadcast_to(jnp.sum(terms, axis=1, keepdims=True), (EXTRA, HD)) * (
            1.0 / math.sqrt(HD)
        )
        for piece in range(3):
            high = rest.astype(jnp.bfloat16).astype(jnp.float32)
            rows = jnp.where(row == place * 3 + piece, high, rows)
            rest = rest - high
    return rows.astype(jnp.bfloat16)


def finish_kernel(
    softness_ref, ids_ref, span_ref, arrays_ref, square_ref, message_ref, received_ref,
    own_ref, stats_ref, square_stats, parts_ref, temper_ref,
    square_weight, square_towards, other_weight, other_towards, within_ref, *refs, half_count
):
    across_refs = refs[:half_count]
    across, prob_low, grad_low, keys_flat = refs[half_count:]
    me, half, place = position(half_count)
    base = half * half_count
    settings = (softness_ref, ids_ref, span_ref)
    per_tile = TILE // BLK

    def put(array, tile, value):
        for sub in range(per_tile):
            within_ref[tile * per_tile + sub, array * BLK : (array + 1) * BLK, :] = value[
                sub * BLK : (sub + 1) * BLK, :
            ]

    met = merged(three_rows(message_ref, 0), three_rows(received_ref, 0))
    log_total = jnp.where(half == 0, met[0], own_ref[0:1, :])
    delta = jnp.where(half == 0, met[1], own_ref[1:2, :])
    region = square_region(me, settings, half_count, square_ref)
    *square_parts, own_temper = region.gradients(
        square_weight, square_towards, square_stats[0:1, :], log_total, delta,
        prob_low, grad_low, keys_flat,
    )
    scales = (region.scaling, region.scaling, 1.0)
    for tile in range(region.tiles):
        query_part, key_part, value_part = [
            part[tile] * scale for part, scale in zip(square_parts, scales)
        ]
        here = tile_rows(tile)
        across[0, here, :] = jnp.where(half == 0, query_part, key_part).astype(jnp.bfloat16)
        across[1, here, :] = jnp.where(half == 0, 0.0, value_part).astype(jnp.bfloat16)
        query_kept, key_kept, value_kept = [
            parts_ref[array, here, :] * scale for array, scale in enumerate(scales)
        ]
        put(0, tile, (query_kept + jnp.where(half == 0, 0.0, query_part)).astype(jnp.bfloat16))
        put(1, tile, (key_kept + jnp.where(half == 0, key_part, 0.0)).astype(jnp.bfloat16))
        put(2, tile, (value_kept + jnp.where(half == 0, value_part, 0.0)).astype(jnp.bfloat16))
    single = alone(three_rows(stats_ref, 3))
    log_total = jnp.where(half == 0, single[0], met[0])
    delta = jnp.where(half == 0, single[1], met[1])
    region = Region(
        me ^ half_count, settings, False, base, base, arrays_ref, range(4, 8)
    )
    *other_parts, other_temper = region.gradients(
        other_weight, other_towards, stats_ref[3:4, :], log_total, delta,
        prob_low, grad_low, keys_flat,
    )
    scales = (region.scaling, region.scaling, 1.0)
    for tile in range(region.tiles):
        for array, (part, scale) in enumerate(zip(other_parts, scales)):
            put(3 + array, tile, (part[tile] * scale).astype(jnp.bfloat16))
    pieces = temper_rows(own_temper + temper_ref[0:1, :], other_temper)
    for block in range(half_count):
        within_ref[block, 6 * BLK : 6 * BLK + EXTRA, :] = pieces
    for step, across_ref in enumerate(across_refs):
        rows = rows_of(place ^ step)
        across_ref[:BLK, :] = across[0, rows, :]
        across_ref[BLK : 2 * BLK, :] = across[1, rows, :]
        across_ref[2 * BLK :, :] = pieces


def temper_kernel(within_ref, *refs, half_count):
    across_refs, temper_ref = refs[:half_count], refs[half_count]
    _, half, place = position(half_count)

    def sums(rows):
        return [
            jnp.sum(rows[3 * slot : 3 * slot + 3, :].astype(jnp.float32), axis=0, keepdims=True)
            for slot in range(2)
        ]

    for step, across_ref in enumerate(across_refs):
        peer = place ^ step
        near, far = sums(within_ref[peer]), sums(across_ref[...])
        temper_ref[pl.ds(half * half_count + peer, 1), :] = near[0] + far[1]
        temper_ref[pl.ds((1 - half) * half_count + peer, 1), :] = near[1] + far[0]


def temper_sums(within, across, half_count):
    last = (6 * BLK // EXTRA, 2 * BLK // EXTRA)
    return pl.pallas_call(
        functools.partial(temper_kernel, half_count=half_count),
        grid=(1,),
        out_shape=jax.ShapeDtypeStruct((2 * half_count, HD), jnp.float32),
        in_specs=[pl.BlockSpec((half_count, EXTRA, HD), lambda step: (0, last[0], 0))]
        + [pl.BlockSpec((EXTRA, HD), lambda step: (last[1], 0))] * half_count,
        out_specs=pl.BlockSpec((2 * half_count, HD), lambda step: (0, 0)),
        compiler_params=pltpu.CompilerParams(vmem_limit_bytes=4 * MIB),
        name="temper_sums",
    )(within, *across)


def unpack_kernel(within_ref, *refs, half_count):
    across_refs = refs[:half_count]
    query_ref, key_ref, value_ref = refs[half_count:]
    _, half, place = position(half_count)
    for step, across_ref in enumerate(across_refs):
        peer = place ^ step
        other = columns_of((1 - half) * half_count + peer)
        own = columns_of(half * half_count + peer)
        parts = [within_ref[peer, array * BLK : (array + 1) * BLK, :] for array in range(6)]
        for array, out_ref in enumerate((query_ref, key_ref, value_ref)):
            out_ref[0, :, own] = parts[array]
        first = across_ref[:BLK, :].astype(jnp.float32)
        second = across_ref[BLK : 2 * BLK, :].astype(jnp.float32)
        added = (
            jnp.where(half == 0, 0.0, first),
            jnp.where(half == 0, first, 0.0),
            jnp.where(half == 0, second, 0.0),
        )
        for array, out_ref in enumerate((query_ref, key_ref, value_ref)):
            out_ref[0, :, other] = (parts[3 + array].astype(jnp.float32) + added[array]).astype(
                jnp.bfloat16
            )


def crossed(chunks, half_count):
    pairs = range(2 * half_count)
    return [
        lax.ppermute(chunk, "seq", [(source, source ^ (half_count + step)) for source in pairs])
        for step, chunk in enumerate(chunks)
    ]


def head_shards(
    probe_vectors,
    lookup_vectors,
    content_vectors,
    result_cotangent,
    logit_softness,
    block_grouping,
    neighborhood_span,
):
    seq_count, dp_count = lax.axis_size("seq"), lax.axis_size("dp")
    half_count = seq_count // 2
    tokens = half_count * BLK
    groups = [list(range(half_count)), list(range(half_count, seq_count))]
    settings = (logit_softness, block_grouping[0, :, :, 0], neighborhood_span)
    smem, vmem = pl.BlockSpec(memory_space=pltpu.SMEM), pl.BlockSpec(memory_space=pltpu.VMEM)
    lows = [pltpu.VMEM((tokens, tokens), jnp.bfloat16)] * 2 + [
        pltpu.VMEM((HD, tokens), jnp.bfloat16)
    ]
    rows_of_stats = jax.ShapeDtypeStruct((8, tokens), jnp.float32)
    pairs = jax.ShapeDtypeStruct((tokens, tokens), jnp.float32)
    pair_flops = 2 * tokens * tokens * HD

    def exchange_within(array_in):
        return lax.all_to_all(
            array_in, "seq", split_axis=0, concat_axis=0, axis_index_groups=groups, tiled=True
        )

    def call(kernel, name, operands, out_shape, scratch, flops, vmem_mib):
        return kernel_call(
            functools.partial(kernel, half_count=half_count),
            name,
            (*settings, *operands),
            [smem] * 3 + [vmem] * len(operands),
            out_shape,
            scratch,
            vmem_mib,
            flops,
        )

    sent, *foreign = packed(
        (probe_vectors, lookup_vectors, content_vectors, result_cotangent), half_count
    )
    arrived = exchange_within(sent)
    foreign = crossed(foreign, half_count)
    arrays, stats, own_weight, own_towards, other_weight, other_towards = call(
        within_kernel,
        "diagonal_statistics",
        (arrived,),
        [jax.ShapeDtypeStruct((8, tokens, HD), jnp.bfloat16), rows_of_stats] + [pairs] * 4,
        [],
        2 * pair_flops,
        20,
    )
    square, message, own, square_stats, square_weight, square_towards = call(
        square_kernel,
        "square_statistics",
        (arrays, stats, *foreign),
        [jax.ShapeDtypeStruct((4, tokens, HD), jnp.bfloat16)] + [rows_of_stats] * 3 + [pairs] * 2,
        [],
        2 * pair_flops,
        12,
    )
    swap = [(source, source ^ half_count) for source in range(seq_count)]
    received = lax.ppermute(message, "seq", swap)
    parts, temper = call(
        diagonal_kernel,
        "own_diagonal_gradients",
        (arrays, own, stats, own_weight, own_towards),
        [
            jax.ShapeDtypeStruct((3, tokens, HD), jnp.float32),
            jax.ShapeDtypeStruct((8, HD), jnp.float32),
        ],
        lows,
        3 * pair_flops // 2,
        14,
    )
    within, *across = call(
        finish_kernel,
        "remaining_gradients",
        (
            arrays, square, message, received, own, stats, square_stats, parts, temper,
            square_weight, square_towards, other_weight, other_towards,
        ),
        [jax.ShapeDtypeStruct((half_count, 6 * BLK + EXTRA, HD), jnp.bfloat16)]
        + [jax.ShapeDtypeStruct((2 * BLK + EXTRA, HD), jnp.bfloat16)] * half_count,
        [pltpu.VMEM((2, tokens, HD), jnp.bfloat16), *lows],
        5 * pair_flops,
        20,
    )
    across = crossed(across, half_count)
    within = exchange_within(within)
    tempers = temper_sums(within, across, half_count)
    temper_total = tempers
    for step in range(1, dp_count):
        swap = [(source, (source + step) % dp_count) for source in range(dp_count)]
        temper_total = temper_total + lax.ppermute(tempers, "dp", swap)
    outs = kernel_call(
        functools.partial(unpack_kernel, half_count=half_count),
        "unpack_heads",
        (within, *across),
        [vmem] * (1 + half_count),
        [jax.ShapeDtypeStruct(probe_vectors.shape, jnp.bfloat16)] * 3,
        [],
        10,
    )
    return (*outs, temper_total[:, 0] / (dp_count * BLK * seq_count))


def shards(
    probe_vectors,
    lookup_vectors,
    content_vectors,
    result_cotangent,
    logit_softness,
    block_grouping,
    neighborhood_span,
):
    head_count = probe_vectors.shape[2] // HD
    seq_count = lax.axis_size("seq")
    one_block = probe_vectors.shape[1] == BLK
    whole_tiles = seq_count * BLK % (2 * TILE) == 0 and seq_count & (seq_count - 1) == 0
    if head_count == seq_count and one_block and whole_tiles:
        plan = head_shards
    else:
        plan = clustered_shards
    return plan(
        probe_vectors,
        lookup_vectors,
        content_vectors,
        result_cotangent,
        logit_softness,
        block_grouping,
        neighborhood_span,
    )


def solution(mesh):
    in_specs = (
        P("dp", "seq", None),
        P("dp", "seq", None),
        P("dp", "seq", None),
        P("dp", "seq", None),
        P(),
        P("dp", None, None, None),
        P(),
    )
    out_specs = (P("dp", "seq", None), P("dp", "seq", None), P("dp", "seq", None), P())
    return jax.shard_map(shards, mesh=mesh, in_specs=in_specs, out_specs=out_specs, check_vma=False)
```

```python
import functools
import math

import jax
import jax.numpy as jnp
from jax import lax
from jax.experimental import pallas as pl
from jax.experimental.pallas import tpu as pltpu
from jax.sharding import PartitionSpec as P

HD = 128
BLK = 128


blocked_score = -1e30


def shifted(value, axis, steps):
    count = lax.axis_size(axis)
    first, last = (max(0, -steps), min(count, count - steps))
    return lax.ppermute(value, axis, [(source, source + steps) for source in range(first, last)])


def lifted(array_in):
    return lax.optimization_barrier(array_in.astype(jnp.bfloat16)).astype(jnp.float32)


def head_major(tokens_in, block_len):
    token_count, feature_count = tokens_in.shape
    return tokens_in.reshape(
        token_count // block_len, block_len, feature_count // HD, HD
    ).transpose(2, 0, 1, 3)


def token_major(blocks_in):
    head_count, block_count, block_len, depth = blocks_in.shape
    return blocks_in.transpose(1, 2, 0, 3).reshape(1, block_count * block_len, head_count * depth)


def window_parts(query_block, prev_keys, prev_values, grad_block, usable, window_width, temper):
    block_len = query_block.shape[-2]
    inverse_root = 1.0 / math.sqrt(query_block.shape[-1])
    raw_scores = (
        jnp.einsum("...td,...sd->...ts", query_block, prev_keys, preferred_element_type=jnp.float32)
        * inverse_root
    )
    query_pos = lax.broadcasted_iota(jnp.int32, (block_len, block_len), 0)
    key_pos = lax.broadcasted_iota(jnp.int32, (block_len, block_len), 1)
    pair_mask = usable[..., None, None] & (
        key_pos > query_pos + block_len - window_width[..., None, None]
    )
    scores = temper[..., None, None] * raw_scores
    row_top = jnp.max(jnp.where(pair_mask, scores, blocked_score), axis=-1)
    weights = jnp.where(pair_mask, jnp.exp(scores - row_top[..., None]), 0.0)
    prob_grad = jnp.einsum(
        "...td,...sd->...ts", grad_block, prev_values, preferred_element_type=jnp.float32
    )
    return (
        raw_scores,
        pair_mask,
        prob_grad,
        row_top,
        jnp.sum(weights, axis=-1),
        jnp.sum(weights * prob_grad, axis=-1),
    )


def window_grads(
    raw_scores,
    pair_mask,
    prob_grad,
    query_block,
    prev_keys,
    grad_block,
    log_total,
    row_delta,
    temper,
):
    inverse_root = 1.0 / math.sqrt(query_block.shape[-1])
    scaling = (temper * inverse_root)[..., None, None]
    probability = jnp.where(
        pair_mask, jnp.exp(temper[..., None, None] * raw_scores - log_total[..., None]), 0.0
    )
    score_grad = probability * (prob_grad - row_delta[..., None])
    prob_low = probability.astype(jnp.bfloat16)
    grad_low = score_grad.astype(jnp.bfloat16)
    query_part = (
        jnp.einsum("...ts,...sd->...td", grad_low, prev_keys, preferred_element_type=jnp.float32)
        * scaling
    )
    key_part = (
        jnp.einsum("...ts,...td->...sd", grad_low, query_block, preferred_element_type=jnp.float32)
        * scaling
    )
    value_part = jnp.einsum(
        "...ts,...td->...sd", prob_low, grad_block, preferred_element_type=jnp.float32
    )
    temper_part = jnp.sum(score_grad * raw_scores, axis=(-2, -1))
    return (query_part, key_part, value_part, temper_part)


def cluster_pair(
    query_items,
    key_items,
    value_items,
    grad_items,
    live_items,
    temper,
    window_top,
    window_total,
    window_mass,
):
    item_count, block_len, depth = query_items.shape
    row_count = item_count * block_len
    group_rows = 4 * block_len
    inverse_root = 1.0 / math.sqrt(depth)
    scaling = temper * inverse_root
    query_rows = query_items.reshape(row_count, depth)
    key_rows = key_items.reshape(row_count, depth)
    value_rows = value_items.reshape(row_count, depth)
    grad_rows = grad_items.reshape(row_count, depth)
    key_item = jnp.arange(row_count) // block_len
    key_token = jnp.arange(row_count) % block_len
    live_rows = jnp.repeat(live_items, block_len)
    top_rows = window_top.reshape(row_count)
    total_rows = window_total.reshape(row_count)
    mass_rows = window_mass.reshape(row_count)

    def group_step(carry, start_row):
        key_acc, value_acc, temper_acc = carry
        query_group = lax.dynamic_slice_in_dim(query_rows, start_row, group_rows, 0)
        grad_group = lax.dynamic_slice_in_dim(grad_rows, start_row, group_rows, 0)
        group_live = lax.dynamic_slice_in_dim(live_rows, start_row, group_rows, 0)
        group_top = lax.dynamic_slice_in_dim(top_rows, start_row, group_rows, 0)
        group_total = lax.dynamic_slice_in_dim(total_rows, start_row, group_rows, 0)
        group_mass = lax.dynamic_slice_in_dim(mass_rows, start_row, group_rows, 0)
        query_item = (start_row + jnp.arange(group_rows)) // block_len
        query_token = jnp.arange(group_rows) % block_len
        earlier = (key_item[None, :] < query_item[:, None]) | (
            key_item[None, :] == query_item[:, None]
        ) & (key_token[None, :] <= query_token[:, None])
        pair_mask = group_live[:, None] & live_rows[None, :] & earlier
        raw_scores = (
            lax.dot_general(
                query_group, key_rows, (((1,), (1,)), ((), ())), preferred_element_type=jnp.float32
            )
            * inverse_root
        )
        scores = temper * raw_scores
        row_top = jnp.maximum(
            jnp.max(jnp.where(pair_mask, scores, blocked_score), axis=1), group_top
        )
        weights = jnp.where(pair_mask, jnp.exp(scores - row_top[:, None]), 0.0)
        row_total = jnp.sum(weights, axis=1) + group_total * jnp.exp(group_top - row_top)
        log_total = row_top + jnp.log(jnp.where(group_live, row_total, 1.0))
        probability = jnp.where(pair_mask, jnp.exp(scores - log_total[:, None]), 0.0)
        prob_grad = lax.dot_general(
            grad_group, value_rows, (((1,), (1,)), ((), ())), preferred_element_type=jnp.float32
        )
        row_delta = jnp.sum(probability * prob_grad, axis=1) + group_mass * jnp.exp(
            group_top - log_total
        )
        score_grad = probability * (prob_grad - row_delta[:, None])
        prob_low = probability.astype(jnp.bfloat16)
        grad_low = score_grad.astype(jnp.bfloat16)
        query_part = jnp.dot(grad_low, key_rows, preferred_element_type=jnp.float32) * scaling
        key_acc = (
            key_acc
            + lax.dot_general(
                grad_low, query_group, (((0,), (0,)), ((), ())), preferred_element_type=jnp.float32
            )
            * scaling
        )
        value_acc = value_acc + lax.dot_general(
            prob_low, grad_group, (((0,), (0,)), ((), ())), preferred_element_type=jnp.float32
        )
        temper_acc = temper_acc + jnp.sum(score_grad * raw_scores)
        return ((key_acc, value_acc, temper_acc), (query_part, log_total, row_delta))

    start_rows = jnp.arange(item_count // 4) * group_rows
    initial = (
        jnp.zeros((row_count, depth), jnp.float32),
        jnp.zeros((row_count, depth), jnp.float32),
        jnp.zeros((), jnp.float32),
    )
    (key_acc, value_acc, temper_acc), (query_part, log_total, row_delta) = lax.scan(
        group_step, initial, start_rows
    )
    return (
        query_part.reshape(item_count, block_len, depth),
        log_total.reshape(item_count, block_len),
        row_delta.reshape(item_count, block_len),
        key_acc.reshape(item_count, block_len, depth),
        value_acc.reshape(item_count, block_len, depth),
        temper_acc,
    )


def clustered_shards(
    probe_vectors,
    lookup_vectors,
    content_vectors,
    result_cotangent,
    logit_softness,
    block_grouping,
    neighborhood_span,
):
    seq_count = lax.axis_size("seq")
    position = lax.axis_index("seq")
    tokens = probe_vectors.shape[1]
    head_count = probe_vectors.shape[2] // HD
    local_blocks = tokens // BLK
    block_count = local_blocks * seq_count
    cluster_count = max(1, block_count // 8)
    capacity = min(12, block_count)
    owned_pairs = cluster_count * head_count // seq_count
    group_count = cluster_count // owned_pairs
    per_peer = max(1, local_blocks // group_count)
    cluster_ids = block_grouping[0, :, :, 0]
    query_home = head_major(probe_vectors[0], BLK)
    key_home = head_major(lookup_vectors[0], BLK)
    value_home = head_major(content_vectors[0], BLK)
    grad_home = head_major(result_cotangent[0], BLK)
    last_block = (lookup_vectors[0, tokens - BLK :], content_vectors[0, tokens - BLK :])
    prev_key_rows, prev_value_rows = shifted((last_block[0], last_block[1]), "seq", 1)
    prev_keys = jnp.concatenate([head_major(prev_key_rows, BLK), key_home[:, :-1]], axis=1)
    prev_values = jnp.concatenate([head_major(prev_value_rows, BLK), value_home[:, :-1]], axis=1)
    first_block = position * local_blocks
    before = jnp.concatenate(
        [jnp.full((head_count, 1), -1, jnp.int32), cluster_ids[:, :-1]], axis=1
    )
    my_ids = lax.dynamic_slice_in_dim(cluster_ids, first_block, local_blocks, 1)
    my_before = lax.dynamic_slice_in_dim(before, first_block, local_blocks, 1)
    global_block = first_block + jnp.arange(local_blocks)
    usable_home = (global_block[None, :] >= 1) & (my_before != my_ids)
    peer_index = jnp.arange(seq_count)
    peer_head = peer_index * owned_pairs // cluster_count
    slot_range = jnp.arange(per_peer)
    local_range = jnp.arange(local_blocks)
    owner_index = (jnp.arange(head_count)[:, None] * cluster_count + my_ids) // owned_pairs
    peer_ids = jnp.take(my_ids, peer_head, axis=0)
    goes = (peer_head[:, None] * cluster_count + peer_ids) // owned_pairs == peer_index[:, None]
    send_rank = jnp.cumsum(goes.astype(jnp.int32), axis=1) - 1
    send_pick = goes[:, None, :] & (send_rank[:, None, :] == slot_range[None, :, None])
    send_block = jnp.sum(jnp.where(send_pick, local_range[None, None, :], 0), axis=2)
    send_flat = peer_head[:, None] * local_blocks + send_block
    home_rank = jnp.take_along_axis(send_rank, owner_index, axis=0)
    home_pos = owner_index * per_peer + home_rank
    pair_index = position * owned_pairs + jnp.arange(owned_pairs)
    split_for_couple = pair_index // cluster_count
    pair_cluster = pair_index % cluster_count
    my_head = position * owned_pairs // cluster_count
    split_numbers = jnp.take(cluster_ids, my_head, axis=0)
    member = split_numbers[None, :] == pair_cluster[:, None]
    member_rank = jnp.cumsum(member.astype(jnp.int32), axis=1) - 1
    member_count = jnp.sum(member.astype(jnp.int32), axis=1)
    picked = member[:, None, :] & (member_rank[:, None, :] == jnp.arange(capacity)[None, :, None])
    member_block = jnp.sum(jnp.where(picked, jnp.arange(block_count)[None, None, :], 0), axis=2)
    live_members = jnp.arange(capacity)[None, :] < member_count[:, None]
    mine = (my_head * cluster_count + split_numbers) // owned_pairs == position
    mine_grid = mine.reshape(seq_count, local_blocks)
    recv_rank = jnp.cumsum(mine_grid.astype(jnp.int32), axis=1) - 1
    recv_pos = (peer_index[:, None] * per_peer + recv_rank).reshape(block_count)
    member_pos = jnp.take(recv_pos, member_block)
    couple_softness = jnp.take(logit_softness, split_for_couple)
    pair_onehot = (split_for_couple[:, None] == jnp.arange(head_count)[None, :]).astype(jnp.float32)
    slot_pair = my_head * cluster_count + split_numbers - position * owned_pairs
    same_cluster = split_numbers[:, None] == split_numbers[None, :]
    earlier_block = jnp.arange(block_count)[None, :] < jnp.arange(block_count)[:, None]
    slot_rank = jnp.sum((same_cluster & earlier_block).astype(jnp.int32), axis=1)
    back_pos = jnp.clip(slot_pair, 0, owned_pairs - 1) * capacity + jnp.clip(
        slot_rank, 0, capacity - 1
    )
    back_grid = back_pos.reshape(seq_count, local_blocks)
    back_pick = mine_grid[:, None, :] & (recv_rank[:, None, :] == slot_range[None, :, None])
    back_flat = jnp.sum(jnp.where(back_pick, back_grid[:, None, :], 0), axis=2)

    def to_peers(array_in):
        flat = array_in.reshape((head_count * local_blocks,) + array_in.shape[2:])
        return jnp.take(flat, send_flat, axis=0)

    def members(array_in):
        flat = array_in.reshape((seq_count * per_peer,) + array_in.shape[2:])
        return jnp.take(flat, member_pos, axis=0)

    def to_owner(array_in):
        flat = array_in.reshape((owned_pairs * capacity,) + array_in.shape[2:])
        return jnp.take(flat, back_flat, axis=0)

    def from_peers(array_in):
        flat = array_in.reshape((seq_count * per_peer,) + array_in.shape[2:])
        return jnp.take(flat, home_pos, axis=0)

    raw_w, mask_w, pgrad_w, top_w, total_w, mass_w = window_parts(
        query_home,
        prev_keys,
        prev_values,
        grad_home,
        usable_home,
        neighborhood_span[:, None],
        logit_softness[:, None],
    )
    arrived = (
        lax.all_to_all(to_peers(query_home), "seq", split_axis=0, concat_axis=0, tiled=True),
        lax.all_to_all(to_peers(key_home), "seq", split_axis=0, concat_axis=0, tiled=True),
        lax.all_to_all(to_peers(value_home), "seq", split_axis=0, concat_axis=0, tiled=True),
        lax.all_to_all(to_peers(grad_home), "seq", split_axis=0, concat_axis=0, tiled=True),
    )
    arrived_stats = (
        lax.all_to_all(to_peers(top_w), "seq", split_axis=0, concat_axis=0, tiled=True),
        lax.all_to_all(to_peers(total_w), "seq", split_axis=0, concat_axis=0, tiled=True),
        lax.all_to_all(to_peers(mass_w), "seq", split_axis=0, concat_axis=0, tiled=True),
    )
    query_m, key_m, value_m, grad_m = [members(item_in) for item_in in arrived]
    top_m, total_m, mass_m = [members(item_in) for item_in in arrived_stats]

    def split_pair(pair_inputs):
        query_i, key_i, value_i, grad_i, live_i, temper_i, top_i, total_i, mass_i = pair_inputs
        query_c, log_total, row_delta, key_c, value_c, temper_c = cluster_pair(
            query_i, key_i, value_i, grad_i, live_i, temper_i, top_i, total_i, mass_i
        )
        return (
            query_c.astype(jnp.bfloat16),
            key_c.astype(jnp.bfloat16),
            value_c.astype(jnp.bfloat16),
            log_total,
            row_delta,
            temper_c,
        )

    owner_results = lax.map(
        split_pair,
        (query_m, key_m, value_m, grad_m, live_members, couple_softness, top_m, total_m, mass_m),
    )
    returned = (
        lax.all_to_all(to_owner(owner_results[0]), "seq", split_axis=0, concat_axis=0, tiled=True),
        lax.all_to_all(to_owner(owner_results[1]), "seq", split_axis=0, concat_axis=0, tiled=True),
        lax.all_to_all(to_owner(owner_results[2]), "seq", split_axis=0, concat_axis=0, tiled=True),
    )
    returned_stats = (
        lax.all_to_all(to_owner(owner_results[3]), "seq", split_axis=0, concat_axis=0, tiled=True),
        lax.all_to_all(to_owner(owner_results[4]), "seq", split_axis=0, concat_axis=0, tiled=True),
    )
    query_cluster = from_peers(returned[0])
    key_cluster = from_peers(returned[1])
    value_cluster = from_peers(returned[2])
    log_home = from_peers(returned_stats[0])
    delta_home = from_peers(returned_stats[1])
    query_w, key_w, value_w, temper_w = window_grads(
        raw_w,
        mask_w,
        pgrad_w,
        query_home,
        prev_keys,
        grad_home,
        log_home,
        delta_home,
        logit_softness[:, None],
    )
    query_out = (query_cluster.astype(jnp.float32) + lifted(query_w)).astype(jnp.bfloat16)
    key_window = key_w.astype(jnp.bfloat16)
    value_window = value_w.astype(jnp.bfloat16)
    temper_local = jnp.sum(owner_results[5][:, None] * pair_onehot, axis=0) + jnp.sum(
        temper_w, axis=1
    )
    edge_keys, edge_values = shifted((key_window[:, 0], value_window[:, 0]), "seq", -1)
    key_next = jnp.concatenate([key_window[:, 1:], edge_keys[:, None]], axis=1)
    value_next = jnp.concatenate([value_window[:, 1:], edge_values[:, None]], axis=1)
    key_out = (key_cluster.astype(jnp.float32) + key_next.astype(jnp.float32)).astype(jnp.bfloat16)
    value_out = (value_cluster.astype(jnp.float32) + value_next.astype(jnp.float32)).astype(
        jnp.bfloat16
    )
    temper_total = lax.psum(temper_local, ("seq", "dp"))
    temper_grad = temper_total / (lax.axis_size("dp") * tokens * seq_count)
    return (token_major(query_out), token_major(key_out), token_major(value_out), temper_grad)


TILE = 256
EXTRA = 16
MIB = 1024 * 1024
PIECES = 4
QUERY, KEY, VALUE, GRAD = range(4)


def columns_of(index):
    return pl.ds(pl.multiple_of(index * HD, HD), HD)


def rows_of(index):
    return pl.ds(pl.multiple_of(index * BLK, BLK), BLK)


def tile_rows(tile):
    return slice(tile * TILE, (tile + 1) * TILE)


def position(half_count):
    me = lax.axis_index("seq")
    half = jnp.where(me >= half_count, 1, 0)
    return me, half, me - half * half_count


def kernel_call(
    kernel, name, operands, in_specs, out_shape, scratch, vmem_mib, flops=0, out_space=pltpu.VMEM
):
    bytes_accessed = sum(
        math.prod(item.shape) * item.dtype.itemsize for item in (*operands, *out_shape)
    )
    return pl.pallas_call(
        kernel,
        out_shape=out_shape,
        in_specs=in_specs,
        out_specs=[pl.BlockSpec(memory_space=out_space)] * len(out_shape),
        scratch_shapes=scratch,
        cost_estimate=pl.CostEstimate(
            flops=flops, bytes_accessed=bytes_accessed, transcendentals=0
        ),
        compiler_params=pltpu.CompilerParams(vmem_limit_bytes=vmem_mib * MIB),
        name=name,
    )(*operands)


def pack_kernel(*refs, half_count):
    arrays, within_ref, across_refs = refs[:4], refs[4], refs[5 : 5 + half_count]
    held, within, across, arrival, left_within, left_across = refs[5 + half_count :]
    me, half, _ = position(half_count)
    piece = BLK // PIECES
    arrivals = [
        [
            pltpu.make_async_copy(
                array_ref.at[0, part * piece : (part + 1) * piece, :],
                held.at[place, part * piece : (part + 1) * piece, :],
                arrival.at[place, part],
            )
            for part in range(PIECES)
        ]
        for place, array_ref in enumerate(arrays)
    ]
    for copies in arrivals:
        for copy in copies:
            copy.start()
    leaving = []
    for place, copies in enumerate(arrivals):
        for copy in copies:
            copy.wait()
        for slot, base in enumerate((half * half_count, (1 - half) * half_count)):
            rows = slice((slot * 4 + place) * BLK, (slot * 4 + place + 1) * BLK)
            for peer in range(half_count):
                within[peer, rows, :] = held[place, :, columns_of(base + peer)]
            leaving.append(
                pltpu.make_async_copy(
                    within.at[:, rows, :], within_ref.at[:, rows, :], left_within.at[place, slot]
                )
            )
            leaving[-1].start()
    first = jnp.where(half == 0, KEY, QUERY)
    second = jnp.where(half == 0, VALUE, GRAD)
    for step, across_ref in enumerate(across_refs):
        columns = columns_of(me ^ (half_count + step))
        across[step, :BLK, :] = held[first, :, columns]
        across[step, BLK:, :] = held[second, :, columns]
        leaving.append(
            pltpu.make_async_copy(across.at[step], across_ref, left_across.at[step])
        )
        leaving[-1].start()
    for copy in leaving:
        copy.wait()


def packed(arrays, half_count):
    width = arrays[0].shape[2]
    within_shape, across_shape = (half_count, 8 * BLK, HD), (2 * BLK, HD)
    return kernel_call(
        functools.partial(pack_kernel, half_count=half_count),
        "pack_heads",
        arrays,
        [pl.BlockSpec(memory_space=pl.ANY)] * 4,
        [jax.ShapeDtypeStruct(within_shape, jnp.bfloat16)]
        + [jax.ShapeDtypeStruct(across_shape, jnp.bfloat16)] * half_count,
        [
            pltpu.VMEM((4, BLK, width), jnp.bfloat16),
            pltpu.VMEM(within_shape, jnp.bfloat16),
            pltpu.VMEM((half_count, *across_shape), jnp.bfloat16),
            pltpu.SemaphoreType.DMA((4, PIECES)),
            pltpu.SemaphoreType.DMA((4, 2)),
            pltpu.SemaphoreType.DMA((half_count,)),
        ],
        60,
        out_space=pl.ANY,
    )


def dot_rows(left, right):
    return lax.dot_general(
        left, right, (((1,), (1,)), ((), ())), preferred_element_type=jnp.float32
    )


def dot_plain(left, right):
    return lax.dot_general(
        left, right, (((1,), (0,)), ((), ())), preferred_element_type=jnp.float32
    )


class Region:
    def __init__(self, head, settings, square, key_base, query_base, arrays, places):
        softness_ref, self.ids_ref, span_ref = settings
        self.head, self.square = head, square
        self.key_base, self.query_base = key_base, query_base
        self.arrays, self.places = arrays, places
        self.tiles = arrays.shape[1] // TILE
        self.width = span_ref[head]
        self.scaling = softness_ref[head] * (1.0 / math.sqrt(HD))
        self.to_log2 = self.scaling * math.log2(math.e)

    def rows(self, which, start, stop):
        return self.arrays[self.places[which], start * TILE : stop * TILE, :]

    def keys_of(self, tile):
        return range(self.tiles if self.square else tile + 1)

    def scores(self, tile_key, tile_query):
        per_tile = TILE // BLK
        scores = (
            dot_rows(
                self.rows(KEY, tile_key, tile_key + 1), self.rows(QUERY, tile_query, tile_query + 1)
            )
            * self.to_log2
        )
        spread = lax.broadcasted_iota(jnp.int32, (BLK, BLK), 0) - lax.broadcasted_iota(
            jnp.int32, (BLK, BLK), 1
        )
        rows = []
        for sub_key in range(per_tile):
            pieces = []
            for sub_query in range(per_tile):
                piece = scores[
                    sub_key * BLK : (sub_key + 1) * BLK, sub_query * BLK : (sub_query + 1) * BLK
                ]
                key_block = tile_key * per_tile + sub_key
                query_block = tile_query * per_tile + sub_query
                apart = query_block - key_block
                if self.square:
                    apart += self.tiles * per_tile
                same = (
                    self.ids_ref[self.head, self.key_base + key_block]
                    == self.ids_ref[self.head, self.query_base + query_block]
                )
                if apart < 0:
                    piece = jnp.full_like(piece, blocked_score)
                elif apart == 0:
                    piece = jnp.where(spread <= 0, piece, blocked_score)
                elif apart == 1:
                    least = jnp.where(same, -BLK, BLK - self.width)
                    piece = jnp.where(spread > least, piece, blocked_score)
                else:
                    piece = piece + jnp.where(same, 0.0, blocked_score)
                pieces.append(piece)
            rows.append(jnp.concatenate(pieces, axis=1))
        return jnp.concatenate(rows, axis=0)

    def statistics(self, weight_ref, towards_ref, out_ref, first_row):
        for tile in range(self.tiles):
            here = tile_rows(tile)
            top = jnp.full((1, TILE), blocked_score, jnp.float32)
            for other in self.keys_of(tile):
                raw = self.scores(other, tile)
                weight_ref[tile_rows(other), here] = raw
                top = jnp.maximum(top, jnp.max(raw, axis=0, keepdims=True))
            total = jnp.zeros((1, TILE), jnp.float32)
            mass = jnp.zeros((1, TILE), jnp.float32)
            for other in self.keys_of(tile):
                there = tile_rows(other)
                weight = jnp.exp2(weight_ref[there, here] - top)
                towards = dot_rows(
                    self.rows(VALUE, other, other + 1), self.rows(GRAD, tile, tile + 1)
                )
                weight_ref[there, here] = weight
                towards_ref[there, here] = towards
                total += jnp.sum(weight, axis=0, keepdims=True)
                mass += jnp.sum(weight * towards, axis=0, keepdims=True)
            out_ref[first_row : first_row + 1, here] = top
            out_ref[first_row + 1 : first_row + 2, here] = total
            out_ref[first_row + 2 : first_row + 3, here] = mass

    def gradients(self, weight_ref, towards_ref, top, log_total, delta, prob_low, grad_low, keys_flat):
        keys_flat[...] = self.rows(KEY, 0, self.tiles).T
        share = jnp.exp2(top - log_total)
        temper = jnp.zeros((1, HD), jnp.float32)
        query_parts, key_parts, value_parts = [], [], []
        for tile in range(self.tiles):
            here = tile_rows(tile)
            for other in self.keys_of(tile):
                there = tile_rows(other)
                probability = weight_ref[there, here] * share[:, here]
                prob_low[there, here] = probability.astype(jnp.bfloat16)
                grad_low[there, here] = (
                    probability * (towards_ref[there, here] - delta[:, here])
                ).astype(jnp.bfloat16)
            upto = slice(0, len(self.keys_of(tile)) * TILE)
            query_part = dot_plain(keys_flat[:, upto], grad_low[upto, here]).T
            temper += jnp.sum(
                query_part * self.rows(QUERY, tile, tile + 1).astype(jnp.float32),
                axis=0,
                keepdims=True,
            )
            query_parts.append(query_part)
        for tile in range(self.tiles):
            first = 0 if self.square else tile
            onward = slice(first * TILE, self.tiles * TILE)
            here = tile_rows(tile)
            key_parts.append(
                dot_plain(grad_low[here, onward], self.rows(QUERY, first, self.tiles))
            )
            value_parts.append(
                dot_plain(prob_low[here, onward], self.rows(GRAD, first, self.tiles))
            )
        return query_parts, key_parts, value_parts, temper


def merged(first, second):
    top = jnp.maximum(first[0], second[0])
    left, right = jnp.exp2(first[0] - top), jnp.exp2(second[0] - top)
    total = first[1] * left + second[1] * right
    mass = first[2] * left + second[2] * right
    return top + jnp.log2(total), mass / total


def alone(rows):
    return rows[0] + jnp.log2(rows[1]), rows[2] / rows[1]


def three_rows(ref, first):
    return [ref[first + row : first + row + 1, :] for row in range(3)]


def put(within_ref, array, tile, value):
    per_tile = TILE // BLK
    for sub in range(per_tile):
        within_ref[tile * per_tile + sub, array * BLK : (array + 1) * BLK, :] = value[
            sub * BLK : (sub + 1) * BLK, :
        ].astype(jnp.bfloat16)


def diagonal_region(slot, settings, half_count, arrays_ref):
    me, half, _ = position(half_count)
    head = me ^ (slot * half_count)
    places = [slot * 4 + place for place in range(4)]
    base = half * half_count
    return Region(head, settings, False, base, base, arrays_ref, places)


def square_region(settings, half_count, square_ref):
    me = lax.axis_index("seq")
    return Region(me, settings, True, 0, half_count, square_ref, range(4))


def within_kernel(
    softness_ref, ids_ref, span_ref, in_ref, arrays_ref, stats_ref, parts_ref, temper_ref,
    own_weight, own_towards, other_weight, other_towards, *scratch, half_count
):
    _, half, _ = position(half_count)
    for block in range(half_count):
        for place in range(8):
            arrays_ref[place, block * BLK : (block + 1) * BLK, :] = in_ref[
                block, place * BLK : (place + 1) * BLK, :
            ]
    settings = (softness_ref, ids_ref, span_ref)
    kept = ((own_weight, own_towards), (other_weight, other_towards))
    regions = [diagonal_region(slot, settings, half_count, arrays_ref) for slot in range(2)]
    for slot, region in enumerate(regions):
        region.statistics(*kept[slot], stats_ref, slot * 3)
    temper_ref[...] = jnp.zeros_like(temper_ref)

    @pl.when(half == 0)
    def _():
        single = alone(three_rows(stats_ref, 0))
        *parts, temper = regions[0].gradients(*kept[0], stats_ref[0:1, :], *single, *scratch)
        for place, tiles in enumerate(parts):
            for tile, value in enumerate(tiles):
                parts_ref[place, tile_rows(tile), :] = value
        temper_ref[0:1, :] = temper


def square_kernel(
    softness_ref, ids_ref, span_ref, arrays_ref, stats_ref, *refs, half_count
):
    across_refs = refs[:half_count]
    square_ref, message_ref, square_stats, weight, towards = refs[half_count:]
    _, half, place = position(half_count)
    first = jnp.where(half == 0, QUERY, KEY)
    second = jnp.where(half == 0, GRAD, VALUE)
    for step, across_ref in enumerate(across_refs):
        rows = rows_of(place ^ step)
        square_ref[first, rows, :] = across_ref[:BLK, :]
        square_ref[second, rows, :] = across_ref[BLK:, :]
    kept_first = jnp.where(half == 0, KEY, QUERY)
    kept_second = jnp.where(half == 0, VALUE, GRAD)
    square_ref[kept_first, :, :] = arrays_ref[kept_first, :, :]
    square_ref[kept_second, :, :] = arrays_ref[kept_second, :, :]
    region = square_region((softness_ref, ids_ref, span_ref), half_count, square_ref)
    region.statistics(weight, towards, square_stats, 0)
    for row in range(3):
        message_ref[row : row + 1, :] = jnp.where(
            half == 0, square_stats[row : row + 1, :], stats_ref[3 + row : 4 + row, :]
        )


def other_diagonal(region, kept, stats_ref, totals, scratch, within_ref):
    *parts, temper = region.gradients(*kept, stats_ref[3:4, :], *totals, *scratch)
    scales = (region.scaling, region.scaling, 1.0)
    for array, (part, scale) in enumerate(zip(parts, scales)):
        for tile in range(region.tiles):
            put(within_ref, 3 + array, tile, part[tile] * scale)
    return temper


def first_kernel(
    softness_ref, ids_ref, span_ref, arrays_ref, square_ref, stats_ref, square_stats, temper_in,
    own_weight, own_towards, other_weight, other_towards, square_weight, square_towards,
    within_ref, across_ref, temper_ref, *scratch, half_count
):
    _, half, _ = position(half_count)
    settings = (softness_ref, ids_ref, span_ref)
    temper_ref[...] = temper_in[...]

    @pl.when(half == 0)
    def _():
        region = diagonal_region(1, settings, half_count, arrays_ref)
        totals = alone(three_rows(stats_ref, 3))
        temper_ref[1:2, :] = other_diagonal(
            region, (other_weight, other_towards), stats_ref, totals, scratch, within_ref
        )

    @pl.when(half == 1)
    def _():
        totals = merged(three_rows(stats_ref, 0), three_rows(square_stats, 0))
        square = square_region(settings, half_count, square_ref)
        scales = (square.scaling, square.scaling, 1.0)
        across_query, *foreign, square_temper = square.gradients(
            square_weight, square_towards, square_stats[0:1, :], *totals, *scratch
        )
        for array, part in enumerate(foreign):
            for tile in range(square.tiles):
                across_ref[array, tile_rows(tile), :] = (part[tile] * scales[1 + array]).astype(
                    jnp.bfloat16
                )
        diagonal = diagonal_region(0, settings, half_count, arrays_ref)
        *parts, temper = diagonal.gradients(
            own_weight, own_towards, stats_ref[0:1, :], *totals, *scratch
        )
        for tile in range(square.tiles):
            put(within_ref, 0, tile, (parts[0][tile] + across_query[tile]) * scales[0])
            put(within_ref, 1, tile, parts[1][tile] * scales[1])
            put(within_ref, 2, tile, parts[2][tile])
        temper_ref[0:1, :] = temper + square_temper


def temper_rows(own, other):
    row = lax.broadcasted_iota(jnp.int32, (EXTRA, HD), 0)
    rows = jnp.zeros((EXTRA, HD), jnp.float32)
    for place, terms in enumerate((own, other)):
        rest = jnp.broadcast_to(jnp.sum(terms, axis=1, keepdims=True), (EXTRA, HD)) * (
            1.0 / math.sqrt(HD)
        )
        for piece in range(3):
            high = rest.astype(jnp.bfloat16).astype(jnp.float32)
            rows = jnp.where(row == place * 3 + piece, high, rows)
            rest = rest - high
    return rows.astype(jnp.bfloat16)


def finish_kernel(
    softness_ref, ids_ref, span_ref, arrays_ref, square_ref, message_ref, received_ref,
    stats_ref, square_stats, parts_ref, temper_ref,
    square_weight, square_towards, other_weight, other_towards, across_in, begun_ref,
    within_ref, *refs, half_count
):
    across_refs = refs[:half_count]
    across, temper, *scratch = refs[half_count:]
    _, half, place = position(half_count)
    settings = (softness_ref, ids_ref, span_ref)
    temper[...] = temper_ref[...]

    @pl.when(half == 0)
    def _():
        totals = merged(three_rows(message_ref, 0), three_rows(received_ref, 0))
        region = square_region(settings, half_count, square_ref)
        query_parts, key_parts, value_parts, square_temper = region.gradients(
            square_weight, square_towards, square_stats[0:1, :], *totals, *scratch
        )
        for tile in range(region.tiles):
            here = tile_rows(tile)
            across[0, here, :] = (query_parts[tile] * region.scaling).astype(jnp.bfloat16)
            put(within_ref, 0, tile, parts_ref[0, here, :] * region.scaling)
            put(within_ref, 1, tile, (parts_ref[1, here, :] + key_parts[tile]) * region.scaling)
            put(within_ref, 2, tile, parts_ref[2, here, :] + value_parts[tile])
        across[1] = jnp.zeros(across.shape[1:], jnp.bfloat16)
        within_ref[:, 3 * BLK : 6 * BLK, :] = begun_ref[:, 3 * BLK : 6 * BLK, :]
        temper[0:1, :] = temper_ref[0:1, :] + square_temper

    @pl.when(half == 1)
    def _():
        totals = merged(three_rows(message_ref, 0), three_rows(received_ref, 0))
        region = diagonal_region(1, settings, half_count, arrays_ref)
        temper[1:2, :] = other_diagonal(
            region, (other_weight, other_towards), stats_ref, totals, scratch, within_ref
        )
        across[...] = across_in[...]
        within_ref[:, : 3 * BLK, :] = begun_ref[:, : 3 * BLK, :]

    pieces = temper_rows(temper[0:1, :], temper[1:2, :])
    for block in range(half_count):
        within_ref[block, 6 * BLK : 6 * BLK + EXTRA, :] = pieces
    for step, across_ref in enumerate(across_refs):
        rows = rows_of(place ^ step)
        across_ref[:BLK, :] = across[0, rows, :]
        across_ref[BLK : 2 * BLK, :] = across[1, rows, :]
        across_ref[2 * BLK :, :] = pieces


def temper_kernel(within_ref, *refs, half_count):
    across_refs, temper_ref = refs[:half_count], refs[half_count]
    _, half, place = position(half_count)

    def sums(rows):
        return [
            jnp.sum(rows[3 * slot : 3 * slot + 3, :].astype(jnp.float32), axis=0, keepdims=True)
            for slot in range(2)
        ]

    for step, across_ref in enumerate(across_refs):
        peer = place ^ step
        near, far = sums(within_ref[peer]), sums(across_ref[...])
        temper_ref[pl.ds(half * half_count + peer, 1), :] = near[0] + far[1]
        temper_ref[pl.ds((1 - half) * half_count + peer, 1), :] = near[1] + far[0]


def temper_sums(within, across, half_count):
    last = (6 * BLK // EXTRA, 2 * BLK // EXTRA)
    return pl.pallas_call(
        functools.partial(temper_kernel, half_count=half_count),
        grid=(1,),
        out_shape=jax.ShapeDtypeStruct((2 * half_count, HD), jnp.float32),
        in_specs=[pl.BlockSpec((half_count, EXTRA, HD), lambda step: (0, last[0], 0))]
        + [pl.BlockSpec((EXTRA, HD), lambda step: (last[1], 0))] * half_count,
        out_specs=pl.BlockSpec((2 * half_count, HD), lambda step: (0, 0)),
        compiler_params=pltpu.CompilerParams(vmem_limit_bytes=4 * MIB),
        name="temper_sums",
    )(within, *across)


def unpack_kernel(within_ref, *refs, half_count):
    across_refs = refs[:half_count]
    query_ref, key_ref, value_ref = refs[half_count:]
    _, half, place = position(half_count)
    for step, across_ref in enumerate(across_refs):
        peer = place ^ step
        other = columns_of((1 - half) * half_count + peer)
        own = columns_of(half * half_count + peer)
        parts = [within_ref[peer, array * BLK : (array + 1) * BLK, :] for array in range(6)]
        for array, out_ref in enumerate((query_ref, key_ref, value_ref)):
            out_ref[0, :, own] = parts[array]
        first = across_ref[:BLK, :].astype(jnp.float32)
        second = across_ref[BLK : 2 * BLK, :].astype(jnp.float32)
        added = (
            jnp.where(half == 0, 0.0, first),
            jnp.where(half == 0, first, 0.0),
            jnp.where(half == 0, second, 0.0),
        )
        for array, out_ref in enumerate((query_ref, key_ref, value_ref)):
            out_ref[0, :, other] = (parts[3 + array].astype(jnp.float32) + added[array]).astype(
                jnp.bfloat16
            )


def crossed(chunks, half_count):
    pairs = range(2 * half_count)
    return [
        lax.ppermute(chunk, "seq", [(source, source ^ (half_count + step)) for source in pairs])
        for step, chunk in enumerate(chunks)
    ]


def head_shards(
    probe_vectors,
    lookup_vectors,
    content_vectors,
    result_cotangent,
    logit_softness,
    block_grouping,
    neighborhood_span,
):
    seq_count, dp_count = lax.axis_size("seq"), lax.axis_size("dp")
    half_count = seq_count // 2
    tokens = half_count * BLK
    groups = [list(range(half_count)), list(range(half_count, seq_count))]
    settings = (logit_softness, block_grouping[0, :, :, 0], neighborhood_span)
    smem, vmem = pl.BlockSpec(memory_space=pltpu.SMEM), pl.BlockSpec(memory_space=pltpu.VMEM)
    lows = [pltpu.VMEM((tokens, tokens), jnp.bfloat16)] * 2 + [
        pltpu.VMEM((HD, tokens), jnp.bfloat16)
    ]
    rows_of_stats = jax.ShapeDtypeStruct((8, tokens), jnp.float32)
    pairs = jax.ShapeDtypeStruct((tokens, tokens), jnp.float32)
    pair_flops = 2 * tokens * tokens * HD

    def exchange_within(array_in):
        return lax.all_to_all(
            array_in, "seq", split_axis=0, concat_axis=0, axis_index_groups=groups, tiled=True
        )

    def call(kernel, name, operands, out_shape, scratch, flops, vmem_mib):
        return kernel_call(
            functools.partial(kernel, half_count=half_count),
            name,
            (*settings, *operands),
            [smem] * 3 + [vmem] * len(operands),
            out_shape,
            scratch,
            vmem_mib,
            flops,
        )

    sent, *foreign = packed(
        (probe_vectors, lookup_vectors, content_vectors, result_cotangent), half_count
    )
    arrived = exchange_within(sent)
    foreign = crossed(foreign, half_count)
    kept_parts = jax.ShapeDtypeStruct((3, tokens, HD), jnp.float32)
    tempers = jax.ShapeDtypeStruct((8, HD), jnp.float32)
    arrays, stats, parts, temper, own_weight, own_towards, other_weight, other_towards = call(
        within_kernel,
        "diagonal_statistics",
        (arrived,),
        [jax.ShapeDtypeStruct((8, tokens, HD), jnp.bfloat16), rows_of_stats, kept_parts, tempers]
        + [pairs] * 4,
        lows,
        2 * pair_flops,
        20,
    )
    square, message, square_stats, square_weight, square_towards = call(
        square_kernel,
        "square_statistics",
        (arrays, stats, *foreign),
        [jax.ShapeDtypeStruct((4, tokens, HD), jnp.bfloat16)] + [rows_of_stats] * 2 + [pairs] * 2,
        [],
        2 * pair_flops,
        12,
    )
    swap = [(source, source ^ half_count) for source in range(seq_count)]
    received = lax.ppermute(message, "seq", swap)
    begun, across, temper = call(
        first_kernel,
        "gradients_before_totals",
        (
            arrays, square, stats, square_stats, temper, own_weight, own_towards,
            other_weight, other_towards, square_weight, square_towards,
        ),
        [
            jax.ShapeDtypeStruct((half_count, 6 * BLK, HD), jnp.bfloat16),
            jax.ShapeDtypeStruct((2, tokens, HD), jnp.bfloat16),
            tempers,
        ],
        lows,
        4 * pair_flops,
        14,
    )
    within, *across = call(
        finish_kernel,
        "gradients_after_totals",
        (
            arrays, square, message, received, stats, square_stats, parts, temper,
            square_weight, square_towards, other_weight, other_towards, across, begun,
        ),
        [jax.ShapeDtypeStruct((half_count, 6 * BLK + EXTRA, HD), jnp.bfloat16)]
        + [jax.ShapeDtypeStruct((2 * BLK + EXTRA, HD), jnp.bfloat16)] * half_count,
        [pltpu.VMEM((2, tokens, HD), jnp.bfloat16), pltpu.VMEM((8, HD), jnp.float32), *lows],
        2 * pair_flops,
        20,
    )
    across = crossed(across, half_count)
    within = exchange_within(within)
    tempers = temper_sums(within, across, half_count)
    temper_total = tempers
    for step in range(1, dp_count):
        swap = [(source, (source + step) % dp_count) for source in range(dp_count)]
        temper_total = temper_total + lax.ppermute(tempers, "dp", swap)
    outs = kernel_call(
        functools.partial(unpack_kernel, half_count=half_count),
        "unpack_heads",
        (within, *across),
        [vmem] * (1 + half_count),
        [jax.ShapeDtypeStruct(probe_vectors.shape, jnp.bfloat16)] * 3,
        [],
        10,
    )
    return (*outs, temper_total[:, 0] / (dp_count * BLK * seq_count))


def shards(
    probe_vectors,
    lookup_vectors,
    content_vectors,
    result_cotangent,
    logit_softness,
    block_grouping,
    neighborhood_span,
):
    head_count = probe_vectors.shape[2] // HD
    seq_count = lax.axis_size("seq")
    one_block = probe_vectors.shape[1] == BLK
    whole_tiles = seq_count * BLK % (2 * TILE) == 0 and seq_count & (seq_count - 1) == 0
    if head_count == seq_count and one_block and whole_tiles:
        plan = head_shards
    else:
        plan = clustered_shards
    return plan(
        probe_vectors,
        lookup_vectors,
        content_vectors,
        result_cotangent,
        logit_softness,
        block_grouping,
        neighborhood_span,
    )


def solution(mesh):
    in_specs = (
        P("dp", "seq", None),
        P("dp", "seq", None),
        P("dp", "seq", None),
        P("dp", "seq", None),
        P(),
        P("dp", None, None, None),
        P(),
    )
    out_specs = (P("dp", "seq", None), P("dp", "seq", None), P("dp", "seq", None), P())
    return jax.shard_map(shards, mesh=mesh, in_specs=in_specs, out_specs=out_specs, check_vma=False)
```

```python
import functools
import math

import jax
import jax.numpy as jnp
from jax import lax
from jax.experimental import pallas as pl
from jax.experimental.pallas import tpu as pltpu
from jax.sharding import PartitionSpec as P

HD = 128
BLK = 128


blocked_score = -1e30


def shifted(value, axis, steps):
    count = lax.axis_size(axis)
    first, last = (max(0, -steps), min(count, count - steps))
    return lax.ppermute(value, axis, [(source, source + steps) for source in range(first, last)])


def lifted(array_in):
    return lax.optimization_barrier(array_in.astype(jnp.bfloat16)).astype(jnp.float32)


def head_major(tokens_in, block_len):
    token_count, feature_count = tokens_in.shape
    return tokens_in.reshape(
        token_count // block_len, block_len, feature_count // HD, HD
    ).transpose(2, 0, 1, 3)


def token_major(blocks_in):
    head_count, block_count, block_len, depth = blocks_in.shape
    return blocks_in.transpose(1, 2, 0, 3).reshape(1, block_count * block_len, head_count * depth)


def window_parts(query_block, prev_keys, prev_values, grad_block, usable, window_width, temper):
    block_len = query_block.shape[-2]
    inverse_root = 1.0 / math.sqrt(query_block.shape[-1])
    raw_scores = (
        jnp.einsum("...td,...sd->...ts", query_block, prev_keys, preferred_element_type=jnp.float32)
        * inverse_root
    )
    query_pos = lax.broadcasted_iota(jnp.int32, (block_len, block_len), 0)
    key_pos = lax.broadcasted_iota(jnp.int32, (block_len, block_len), 1)
    pair_mask = usable[..., None, None] & (
        key_pos > query_pos + block_len - window_width[..., None, None]
    )
    scores = temper[..., None, None] * raw_scores
    row_top = jnp.max(jnp.where(pair_mask, scores, blocked_score), axis=-1)
    weights = jnp.where(pair_mask, jnp.exp(scores - row_top[..., None]), 0.0)
    prob_grad = jnp.einsum(
        "...td,...sd->...ts", grad_block, prev_values, preferred_element_type=jnp.float32
    )
    return (
        raw_scores,
        pair_mask,
        prob_grad,
        row_top,
        jnp.sum(weights, axis=-1),
        jnp.sum(weights * prob_grad, axis=-1),
    )


def window_grads(
    raw_scores,
    pair_mask,
    prob_grad,
    query_block,
    prev_keys,
    grad_block,
    log_total,
    row_delta,
    temper,
):
    inverse_root = 1.0 / math.sqrt(query_block.shape[-1])
    scaling = (temper * inverse_root)[..., None, None]
    probability = jnp.where(
        pair_mask, jnp.exp(temper[..., None, None] * raw_scores - log_total[..., None]), 0.0
    )
    score_grad = probability * (prob_grad - row_delta[..., None])
    prob_low = probability.astype(jnp.bfloat16)
    grad_low = score_grad.astype(jnp.bfloat16)
    query_part = (
        jnp.einsum("...ts,...sd->...td", grad_low, prev_keys, preferred_element_type=jnp.float32)
        * scaling
    )
    key_part = (
        jnp.einsum("...ts,...td->...sd", grad_low, query_block, preferred_element_type=jnp.float32)
        * scaling
    )
    value_part = jnp.einsum(
        "...ts,...td->...sd", prob_low, grad_block, preferred_element_type=jnp.float32
    )
    temper_part = jnp.sum(score_grad * raw_scores, axis=(-2, -1))
    return (query_part, key_part, value_part, temper_part)


def cluster_pair(
    query_items,
    key_items,
    value_items,
    grad_items,
    live_items,
    temper,
    window_top,
    window_total,
    window_mass,
):
    item_count, block_len, depth = query_items.shape
    row_count = item_count * block_len
    group_rows = 4 * block_len
    inverse_root = 1.0 / math.sqrt(depth)
    scaling = temper * inverse_root
    query_rows = query_items.reshape(row_count, depth)
    key_rows = key_items.reshape(row_count, depth)
    value_rows = value_items.reshape(row_count, depth)
    grad_rows = grad_items.reshape(row_count, depth)
    key_item = jnp.arange(row_count) // block_len
    key_token = jnp.arange(row_count) % block_len
    live_rows = jnp.repeat(live_items, block_len)
    top_rows = window_top.reshape(row_count)
    total_rows = window_total.reshape(row_count)
    mass_rows = window_mass.reshape(row_count)

    def group_step(carry, start_row):
        key_acc, value_acc, temper_acc = carry
        query_group = lax.dynamic_slice_in_dim(query_rows, start_row, group_rows, 0)
        grad_group = lax.dynamic_slice_in_dim(grad_rows, start_row, group_rows, 0)
        group_live = lax.dynamic_slice_in_dim(live_rows, start_row, group_rows, 0)
        group_top = lax.dynamic_slice_in_dim(top_rows, start_row, group_rows, 0)
        group_total = lax.dynamic_slice_in_dim(total_rows, start_row, group_rows, 0)
        group_mass = lax.dynamic_slice_in_dim(mass_rows, start_row, group_rows, 0)
        query_item = (start_row + jnp.arange(group_rows)) // block_len
        query_token = jnp.arange(group_rows) % block_len
        earlier = (key_item[None, :] < query_item[:, None]) | (
            key_item[None, :] == query_item[:, None]
        ) & (key_token[None, :] <= query_token[:, None])
        pair_mask = group_live[:, None] & live_rows[None, :] & earlier
        raw_scores = (
            lax.dot_general(
                query_group, key_rows, (((1,), (1,)), ((), ())), preferred_element_type=jnp.float32
            )
            * inverse_root
        )
        scores = temper * raw_scores
        row_top = jnp.maximum(
            jnp.max(jnp.where(pair_mask, scores, blocked_score), axis=1), group_top
        )
        weights = jnp.where(pair_mask, jnp.exp(scores - row_top[:, None]), 0.0)
        row_total = jnp.sum(weights, axis=1) + group_total * jnp.exp(group_top - row_top)
        log_total = row_top + jnp.log(jnp.where(group_live, row_total, 1.0))
        probability = jnp.where(pair_mask, jnp.exp(scores - log_total[:, None]), 0.0)
        prob_grad = lax.dot_general(
            grad_group, value_rows, (((1,), (1,)), ((), ())), preferred_element_type=jnp.float32
        )
        row_delta = jnp.sum(probability * prob_grad, axis=1) + group_mass * jnp.exp(
            group_top - log_total
        )
        score_grad = probability * (prob_grad - row_delta[:, None])
        prob_low = probability.astype(jnp.bfloat16)
        grad_low = score_grad.astype(jnp.bfloat16)
        query_part = jnp.dot(grad_low, key_rows, preferred_element_type=jnp.float32) * scaling
        key_acc = (
            key_acc
            + lax.dot_general(
                grad_low, query_group, (((0,), (0,)), ((), ())), preferred_element_type=jnp.float32
            )
            * scaling
        )
        value_acc = value_acc + lax.dot_general(
            prob_low, grad_group, (((0,), (0,)), ((), ())), preferred_element_type=jnp.float32
        )
        temper_acc = temper_acc + jnp.sum(score_grad * raw_scores)
        return ((key_acc, value_acc, temper_acc), (query_part, log_total, row_delta))

    start_rows = jnp.arange(item_count // 4) * group_rows
    initial = (
        jnp.zeros((row_count, depth), jnp.float32),
        jnp.zeros((row_count, depth), jnp.float32),
        jnp.zeros((), jnp.float32),
    )
    (key_acc, value_acc, temper_acc), (query_part, log_total, row_delta) = lax.scan(
        group_step, initial, start_rows
    )
    return (
        query_part.reshape(item_count, block_len, depth),
        log_total.reshape(item_count, block_len),
        row_delta.reshape(item_count, block_len),
        key_acc.reshape(item_count, block_len, depth),
        value_acc.reshape(item_count, block_len, depth),
        temper_acc,
    )


def clustered_shards(
    probe_vectors,
    lookup_vectors,
    content_vectors,
    result_cotangent,
    logit_softness,
    block_grouping,
    neighborhood_span,
):
    seq_count = lax.axis_size("seq")
    position = lax.axis_index("seq")
    tokens = probe_vectors.shape[1]
    head_count = probe_vectors.shape[2] // HD
    local_blocks = tokens // BLK
    block_count = local_blocks * seq_count
    cluster_count = max(1, block_count // 8)
    capacity = min(12, block_count)
    owned_pairs = cluster_count * head_count // seq_count
    group_count = cluster_count // owned_pairs
    per_peer = max(1, local_blocks // group_count)
    cluster_ids = block_grouping[0, :, :, 0]
    query_home = head_major(probe_vectors[0], BLK)
    key_home = head_major(lookup_vectors[0], BLK)
    value_home = head_major(content_vectors[0], BLK)
    grad_home = head_major(result_cotangent[0], BLK)
    last_block = (lookup_vectors[0, tokens - BLK :], content_vectors[0, tokens - BLK :])
    prev_key_rows, prev_value_rows = shifted((last_block[0], last_block[1]), "seq", 1)
    prev_keys = jnp.concatenate([head_major(prev_key_rows, BLK), key_home[:, :-1]], axis=1)
    prev_values = jnp.concatenate([head_major(prev_value_rows, BLK), value_home[:, :-1]], axis=1)
    first_block = position * local_blocks
    before = jnp.concatenate(
        [jnp.full((head_count, 1), -1, jnp.int32), cluster_ids[:, :-1]], axis=1
    )
    my_ids = lax.dynamic_slice_in_dim(cluster_ids, first_block, local_blocks, 1)
    my_before = lax.dynamic_slice_in_dim(before, first_block, local_blocks, 1)
    global_block = first_block + jnp.arange(local_blocks)
    usable_home = (global_block[None, :] >= 1) & (my_before != my_ids)
    peer_index = jnp.arange(seq_count)
    peer_head = peer_index * owned_pairs // cluster_count
    slot_range = jnp.arange(per_peer)
    local_range = jnp.arange(local_blocks)
    owner_index = (jnp.arange(head_count)[:, None] * cluster_count + my_ids) // owned_pairs
    peer_ids = jnp.take(my_ids, peer_head, axis=0)
    goes = (peer_head[:, None] * cluster_count + peer_ids) // owned_pairs == peer_index[:, None]
    send_rank = jnp.cumsum(goes.astype(jnp.int32), axis=1) - 1
    send_pick = goes[:, None, :] & (send_rank[:, None, :] == slot_range[None, :, None])
    send_block = jnp.sum(jnp.where(send_pick, local_range[None, None, :], 0), axis=2)
    send_flat = peer_head[:, None] * local_blocks + send_block
    home_rank = jnp.take_along_axis(send_rank, owner_index, axis=0)
    home_pos = owner_index * per_peer + home_rank
    pair_index = position * owned_pairs + jnp.arange(owned_pairs)
    split_for_couple = pair_index // cluster_count
    pair_cluster = pair_index % cluster_count
    my_head = position * owned_pairs // cluster_count
    split_numbers = jnp.take(cluster_ids, my_head, axis=0)
    member = split_numbers[None, :] == pair_cluster[:, None]
    member_rank = jnp.cumsum(member.astype(jnp.int32), axis=1) - 1
    member_count = jnp.sum(member.astype(jnp.int32), axis=1)
    picked = member[:, None, :] & (member_rank[:, None, :] == jnp.arange(capacity)[None, :, None])
    member_block = jnp.sum(jnp.where(picked, jnp.arange(block_count)[None, None, :], 0), axis=2)
    live_members = jnp.arange(capacity)[None, :] < member_count[:, None]
    mine = (my_head * cluster_count + split_numbers) // owned_pairs == position
    mine_grid = mine.reshape(seq_count, local_blocks)
    recv_rank = jnp.cumsum(mine_grid.astype(jnp.int32), axis=1) - 1
    recv_pos = (peer_index[:, None] * per_peer + recv_rank).reshape(block_count)
    member_pos = jnp.take(recv_pos, member_block)
    couple_softness = jnp.take(logit_softness, split_for_couple)
    pair_onehot = (split_for_couple[:, None] == jnp.arange(head_count)[None, :]).astype(jnp.float32)
    slot_pair = my_head * cluster_count + split_numbers - position * owned_pairs
    same_cluster = split_numbers[:, None] == split_numbers[None, :]
    earlier_block = jnp.arange(block_count)[None, :] < jnp.arange(block_count)[:, None]
    slot_rank = jnp.sum((same_cluster & earlier_block).astype(jnp.int32), axis=1)
    back_pos = jnp.clip(slot_pair, 0, owned_pairs - 1) * capacity + jnp.clip(
        slot_rank, 0, capacity - 1
    )
    back_grid = back_pos.reshape(seq_count, local_blocks)
    back_pick = mine_grid[:, None, :] & (recv_rank[:, None, :] == slot_range[None, :, None])
    back_flat = jnp.sum(jnp.where(back_pick, back_grid[:, None, :], 0), axis=2)

    def to_peers(array_in):
        flat = array_in.reshape((head_count * local_blocks,) + array_in.shape[2:])
        return jnp.take(flat, send_flat, axis=0)

    def members(array_in):
        flat = array_in.reshape((seq_count * per_peer,) + array_in.shape[2:])
        return jnp.take(flat, member_pos, axis=0)

    def to_owner(array_in):
        flat = array_in.reshape((owned_pairs * capacity,) + array_in.shape[2:])
        return jnp.take(flat, back_flat, axis=0)

    def from_peers(array_in):
        flat = array_in.reshape((seq_count * per_peer,) + array_in.shape[2:])
        return jnp.take(flat, home_pos, axis=0)

    raw_w, mask_w, pgrad_w, top_w, total_w, mass_w = window_parts(
        query_home,
        prev_keys,
        prev_values,
        grad_home,
        usable_home,
        neighborhood_span[:, None],
        logit_softness[:, None],
    )
    arrived = (
        lax.all_to_all(to_peers(query_home), "seq", split_axis=0, concat_axis=0, tiled=True),
        lax.all_to_all(to_peers(key_home), "seq", split_axis=0, concat_axis=0, tiled=True),
        lax.all_to_all(to_peers(value_home), "seq", split_axis=0, concat_axis=0, tiled=True),
        lax.all_to_all(to_peers(grad_home), "seq", split_axis=0, concat_axis=0, tiled=True),
    )
    arrived_stats = (
        lax.all_to_all(to_peers(top_w), "seq", split_axis=0, concat_axis=0, tiled=True),
        lax.all_to_all(to_peers(total_w), "seq", split_axis=0, concat_axis=0, tiled=True),
        lax.all_to_all(to_peers(mass_w), "seq", split_axis=0, concat_axis=0, tiled=True),
    )
    query_m, key_m, value_m, grad_m = [members(item_in) for item_in in arrived]
    top_m, total_m, mass_m = [members(item_in) for item_in in arrived_stats]

    def split_pair(pair_inputs):
        query_i, key_i, value_i, grad_i, live_i, temper_i, top_i, total_i, mass_i = pair_inputs
        query_c, log_total, row_delta, key_c, value_c, temper_c = cluster_pair(
            query_i, key_i, value_i, grad_i, live_i, temper_i, top_i, total_i, mass_i
        )
        return (
            query_c.astype(jnp.bfloat16),
            key_c.astype(jnp.bfloat16),
            value_c.astype(jnp.bfloat16),
            log_total,
            row_delta,
            temper_c,
        )

    owner_results = lax.map(
        split_pair,
        (query_m, key_m, value_m, grad_m, live_members, couple_softness, top_m, total_m, mass_m),
    )
    returned = (
        lax.all_to_all(to_owner(owner_results[0]), "seq", split_axis=0, concat_axis=0, tiled=True),
        lax.all_to_all(to_owner(owner_results[1]), "seq", split_axis=0, concat_axis=0, tiled=True),
        lax.all_to_all(to_owner(owner_results[2]), "seq", split_axis=0, concat_axis=0, tiled=True),
    )
    returned_stats = (
        lax.all_to_all(to_owner(owner_results[3]), "seq", split_axis=0, concat_axis=0, tiled=True),
        lax.all_to_all(to_owner(owner_results[4]), "seq", split_axis=0, concat_axis=0, tiled=True),
    )
    query_cluster = from_peers(returned[0])
    key_cluster = from_peers(returned[1])
    value_cluster = from_peers(returned[2])
    log_home = from_peers(returned_stats[0])
    delta_home = from_peers(returned_stats[1])
    query_w, key_w, value_w, temper_w = window_grads(
        raw_w,
        mask_w,
        pgrad_w,
        query_home,
        prev_keys,
        grad_home,
        log_home,
        delta_home,
        logit_softness[:, None],
    )
    query_out = (query_cluster.astype(jnp.float32) + lifted(query_w)).astype(jnp.bfloat16)
    key_window = key_w.astype(jnp.bfloat16)
    value_window = value_w.astype(jnp.bfloat16)
    temper_local = jnp.sum(owner_results[5][:, None] * pair_onehot, axis=0) + jnp.sum(
        temper_w, axis=1
    )
    edge_keys, edge_values = shifted((key_window[:, 0], value_window[:, 0]), "seq", -1)
    key_next = jnp.concatenate([key_window[:, 1:], edge_keys[:, None]], axis=1)
    value_next = jnp.concatenate([value_window[:, 1:], edge_values[:, None]], axis=1)
    key_out = (key_cluster.astype(jnp.float32) + key_next.astype(jnp.float32)).astype(jnp.bfloat16)
    value_out = (value_cluster.astype(jnp.float32) + value_next.astype(jnp.float32)).astype(
        jnp.bfloat16
    )
    temper_total = lax.psum(temper_local, ("seq", "dp"))
    temper_grad = temper_total / (lax.axis_size("dp") * tokens * seq_count)
    return (token_major(query_out), token_major(key_out), token_major(value_out), temper_grad)


TILE = 256
EXTRA = 16
MIB = 1024 * 1024
PIECES = 4
QUERY, KEY, VALUE, GRAD = range(4)


def columns_of(index):
    return pl.ds(pl.multiple_of(index * HD, HD), HD)


def rows_of(index):
    return pl.ds(pl.multiple_of(index * BLK, BLK), BLK)


def tile_rows(tile):
    return slice(tile * TILE, (tile + 1) * TILE)


def position(half_count):
    me = lax.axis_index("seq")
    half = jnp.where(me >= half_count, 1, 0)
    return me, half, me - half * half_count


def kernel_call(
    kernel, name, operands, in_specs, out_shape, scratch, vmem_mib, flops=0, out_space=pltpu.VMEM
):
    bytes_accessed = sum(
        math.prod(item.shape) * item.dtype.itemsize for item in (*operands, *out_shape)
    )
    return pl.pallas_call(
        kernel,
        out_shape=out_shape,
        in_specs=in_specs,
        out_specs=[pl.BlockSpec(memory_space=out_space)] * len(out_shape),
        scratch_shapes=scratch,
        cost_estimate=pl.CostEstimate(
            flops=flops, bytes_accessed=bytes_accessed, transcendentals=0
        ),
        compiler_params=pltpu.CompilerParams(vmem_limit_bytes=vmem_mib * MIB),
        name=name,
    )(*operands)


def pack_kernel(*refs, half_count):
    arrays, within_ref, foreign_refs = refs[:4], refs[4], refs[5:7]
    held, within, across, arrival, left_within, left_across = refs[7:]
    me, half, _ = position(half_count)
    piece = BLK // PIECES
    arrivals = [
        [
            pltpu.make_async_copy(
                array_ref.at[0, part * piece : (part + 1) * piece, :],
                held.at[place, part * piece : (part + 1) * piece, :],
                arrival.at[place, part],
            )
            for part in range(PIECES)
        ]
        for place, array_ref in enumerate(arrays)
    ]
    for copies in arrivals:
        for copy in copies:
            copy.start()
    leaving = []
    for place, copies in enumerate(arrivals):
        for copy in copies:
            copy.wait()
        for slot, base in enumerate((half * half_count, (1 - half) * half_count)):
            rows = slice((slot * 4 + place) * BLK, (slot * 4 + place + 1) * BLK)
            for peer in range(half_count):
                within[peer, rows, :] = held[place, :, columns_of(base + peer)]
            leaving.append(
                pltpu.make_async_copy(
                    within.at[:, rows, :], within_ref.at[:, rows, :], left_within.at[place, slot]
                )
            )
            leaving[-1].start()
    first = jnp.where(half == 0, KEY, QUERY)
    second = jnp.where(half == 0, VALUE, GRAD)
    for core, foreign_ref in enumerate(foreign_refs):
        for step in range(half_count // 2):
            columns = columns_of(me ^ core ^ (half_count + 2 * step))
            across[core, step, :BLK, :] = held[first, :, columns]
            across[core, step, BLK:, :] = held[second, :, columns]
        leaving.append(pltpu.make_async_copy(across.at[core], foreign_ref, left_across.at[core]))
        leaving[-1].start()
    for copy in leaving:
        copy.wait()


def packed(arrays, half_count):
    width = arrays[0].shape[2]
    within_shape, across_shape = (half_count, 8 * BLK, HD), (half_count // 2, 2 * BLK, HD)
    return kernel_call(
        functools.partial(pack_kernel, half_count=half_count),
        "pack_heads",
        arrays,
        [pl.BlockSpec(memory_space=pl.ANY)] * 4,
        [jax.ShapeDtypeStruct(within_shape, jnp.bfloat16)]
        + [jax.ShapeDtypeStruct(across_shape, jnp.bfloat16)] * 2,
        [
            pltpu.VMEM((4, BLK, width), jnp.bfloat16),
            pltpu.VMEM(within_shape, jnp.bfloat16),
            pltpu.VMEM((2, *across_shape), jnp.bfloat16),
            pltpu.SemaphoreType.DMA((4, PIECES)),
            pltpu.SemaphoreType.DMA((4, 2)),
            pltpu.SemaphoreType.DMA((2,)),
        ],
        60,
        out_space=pl.ANY,
    )


def dot_rows(left, right):
    return lax.dot_general(
        left, right, (((1,), (1,)), ((), ())), preferred_element_type=jnp.float32
    )


def dot_plain(left, right):
    return lax.dot_general(
        left, right, (((1,), (0,)), ((), ())), preferred_element_type=jnp.float32
    )


class Region:
    def __init__(self, head, settings, square, key_base, query_base, arrays, places):
        softness_ref, self.ids_ref, span_ref = settings
        self.head, self.square = head, square
        self.key_base, self.query_base = key_base, query_base
        self.arrays, self.places = arrays, places
        self.tiles = arrays.shape[1] // TILE
        self.width = span_ref[head]
        self.scaling = softness_ref[head] * (1.0 / math.sqrt(HD))
        self.to_log2 = self.scaling * math.log2(math.e)

    def rows(self, which, start, stop):
        return self.arrays[self.places[which], start * TILE : stop * TILE, :]

    def keys_of(self, tile):
        return range(self.tiles if self.square else tile + 1)

    def scores(self, tile_key, tile_query):
        per_tile = TILE // BLK
        scores = (
            dot_rows(
                self.rows(KEY, tile_key, tile_key + 1), self.rows(QUERY, tile_query, tile_query + 1)
            )
            * self.to_log2
        )
        spread = lax.broadcasted_iota(jnp.int32, (BLK, BLK), 0) - lax.broadcasted_iota(
            jnp.int32, (BLK, BLK), 1
        )
        rows = []
        for sub_key in range(per_tile):
            pieces = []
            for sub_query in range(per_tile):
                piece = scores[
                    sub_key * BLK : (sub_key + 1) * BLK, sub_query * BLK : (sub_query + 1) * BLK
                ]
                key_block = tile_key * per_tile + sub_key
                query_block = tile_query * per_tile + sub_query
                apart = query_block - key_block
                if self.square:
                    apart += self.tiles * per_tile
                same = (
                    self.ids_ref[self.head, self.key_base + key_block]
                    == self.ids_ref[self.head, self.query_base + query_block]
                )
                if apart < 0:
                    piece = jnp.full_like(piece, blocked_score)
                elif apart == 0:
                    piece = jnp.where(spread <= 0, piece, blocked_score)
                elif apart == 1:
                    least = jnp.where(same, -BLK, BLK - self.width)
                    piece = jnp.where(spread > least, piece, blocked_score)
                else:
                    piece = piece + jnp.where(same, 0.0, blocked_score)
                pieces.append(piece)
            rows.append(jnp.concatenate(pieces, axis=1))
        return jnp.concatenate(rows, axis=0)

    def statistics(self, weight_ref, towards_ref, out_ref, first_row):
        for tile in range(self.tiles):
            here = tile_rows(tile)
            top = jnp.full((1, TILE), blocked_score, jnp.float32)
            for other in self.keys_of(tile):
                raw = self.scores(other, tile)
                weight_ref[tile_rows(other), here] = raw
                top = jnp.maximum(top, jnp.max(raw, axis=0, keepdims=True))
            total = jnp.zeros((1, TILE), jnp.float32)
            mass = jnp.zeros((1, TILE), jnp.float32)
            for other in self.keys_of(tile):
                there = tile_rows(other)
                weight = jnp.exp2(weight_ref[there, here] - top)
                towards = dot_rows(
                    self.rows(VALUE, other, other + 1), self.rows(GRAD, tile, tile + 1)
                )
                weight_ref[there, here] = weight
                towards_ref[there, here] = towards
                total += jnp.sum(weight, axis=0, keepdims=True)
                mass += jnp.sum(weight * towards, axis=0, keepdims=True)
            out_ref[first_row : first_row + 1, here] = top
            out_ref[first_row + 1 : first_row + 2, here] = total
            out_ref[first_row + 2 : first_row + 3, here] = mass

    def gradients(self, weight_ref, towards_ref, top, log_total, delta, prob_low, grad_low, keys_flat):
        keys_flat[...] = self.rows(KEY, 0, self.tiles).T
        share = jnp.exp2(top - log_total)
        temper = jnp.zeros((1, HD), jnp.float32)
        query_parts, key_parts, value_parts = [], [], []
        for tile in range(self.tiles):
            here = tile_rows(tile)
            for other in self.keys_of(tile):
                there = tile_rows(other)
                probability = weight_ref[there, here] * share[:, here]
                prob_low[there, here] = probability.astype(jnp.bfloat16)
                grad_low[there, here] = (
                    probability * (towards_ref[there, here] - delta[:, here])
                ).astype(jnp.bfloat16)
            upto = slice(0, len(self.keys_of(tile)) * TILE)
            query_part = dot_plain(keys_flat[:, upto], grad_low[upto, here]).T
            temper += jnp.sum(
                query_part * self.rows(QUERY, tile, tile + 1).astype(jnp.float32),
                axis=0,
                keepdims=True,
            )
            query_parts.append(query_part)
        for tile in range(self.tiles):
            first = 0 if self.square else tile
            onward = slice(first * TILE, self.tiles * TILE)
            here = tile_rows(tile)
            key_parts.append(
                dot_plain(grad_low[here, onward], self.rows(QUERY, first, self.tiles))
            )
            value_parts.append(
                dot_plain(prob_low[here, onward], self.rows(GRAD, first, self.tiles))
            )
        return query_parts, key_parts, value_parts, temper


def merged(first, second):
    top = jnp.maximum(first[0], second[0])
    left, right = jnp.exp2(first[0] - top), jnp.exp2(second[0] - top)
    total = first[1] * left + second[1] * right
    mass = first[2] * left + second[2] * right
    return top + jnp.log2(total), mass / total


def alone(rows):
    return rows[0] + jnp.log2(rows[1]), rows[2] / rows[1]


def three_rows(ref, first):
    return [ref[first + row : first + row + 1, :] for row in range(3)]


def put(within_ref, array, tile, value):
    per_tile = TILE // BLK
    for sub in range(per_tile):
        within_ref[tile * per_tile + sub, array * BLK : (array + 1) * BLK, :] = value[
            sub * BLK : (sub + 1) * BLK, :
        ].astype(jnp.bfloat16)


def diagonal_region(slot, settings, half_count, arrays_ref):
    me, half, _ = position(half_count)
    head = me ^ (slot * half_count)
    places = [slot * 4 + place for place in range(4)]
    base = half * half_count
    return Region(head, settings, False, base, base, arrays_ref, places)


def square_region(settings, half_count, square_ref):
    me = lax.axis_index("seq")
    return Region(me, settings, True, 0, half_count, square_ref, range(4))


def within_kernel(
    softness_ref, ids_ref, span_ref, in_ref, arrays_ref, stats_ref, parts_ref, temper_ref,
    own_weight, own_towards, other_weight, other_towards, *scratch, half_count
):
    _, half, _ = position(half_count)
    for block in range(half_count):
        for place in range(8):
            arrays_ref[place, block * BLK : (block + 1) * BLK, :] = in_ref[
                block, place * BLK : (place + 1) * BLK, :
            ]
    settings = (softness_ref, ids_ref, span_ref)
    kept = ((own_weight, own_towards), (other_weight, other_towards))
    regions = [diagonal_region(slot, settings, half_count, arrays_ref) for slot in range(2)]
    for slot, region in enumerate(regions):
        region.statistics(*kept[slot], stats_ref, slot * 3)
    temper_ref[...] = jnp.zeros_like(temper_ref)

    @pl.when(half == 0)
    def _():
        single = alone(three_rows(stats_ref, 0))
        *parts, temper = regions[0].gradients(*kept[0], stats_ref[0:1, :], *single, *scratch)
        for place, tiles in enumerate(parts):
            for tile, value in enumerate(tiles):
                parts_ref[place, tile_rows(tile), :] = value
        temper_ref[0:1, :] = temper


def square_kernel(
    softness_ref, ids_ref, span_ref, arrays_ref, stats_ref, *refs, half_count
):
    across_refs = refs[: half_count // 2]
    square_ref, message_ref, square_stats, weight, towards = refs[half_count // 2 :]
    _, half, place = position(half_count)
    first = jnp.where(half == 0, QUERY, KEY)
    second = jnp.where(half == 0, GRAD, VALUE)
    for step, across_ref in enumerate(across_refs):
        for core in range(2):
            rows = rows_of(place ^ core ^ (2 * step))
            square_ref[first, rows, :] = across_ref[core, :BLK, :]
            square_ref[second, rows, :] = across_ref[core, BLK:, :]
    kept_first = jnp.where(half == 0, KEY, QUERY)
    kept_second = jnp.where(half == 0, VALUE, GRAD)
    square_ref[kept_first, :, :] = arrays_ref[kept_first, :, :]
    square_ref[kept_second, :, :] = arrays_ref[kept_second, :, :]
    region = square_region((softness_ref, ids_ref, span_ref), half_count, square_ref)
    region.statistics(weight, towards, square_stats, 0)
    for row in range(3):
        message_ref[row : row + 1, :] = jnp.where(
            half == 0, square_stats[row : row + 1, :], stats_ref[3 + row : 4 + row, :]
        )


def other_diagonal(region, kept, stats_ref, totals, scratch, within_ref):
    *parts, temper = region.gradients(*kept, stats_ref[3:4, :], *totals, *scratch)
    scales = (region.scaling, region.scaling, 1.0)
    for array, (part, scale) in enumerate(zip(parts, scales)):
        for tile in range(region.tiles):
            put(within_ref, 3 + array, tile, part[tile] * scale)
    return temper


def first_kernel(
    softness_ref, ids_ref, span_ref, arrays_ref, square_ref, stats_ref, square_stats, temper_in,
    own_weight, own_towards, other_weight, other_towards, square_weight, square_towards,
    within_ref, across_ref, temper_ref, *scratch, half_count
):
    _, half, _ = position(half_count)
    settings = (softness_ref, ids_ref, span_ref)
    temper_ref[...] = temper_in[...]

    @pl.when(half == 0)
    def _():
        region = diagonal_region(1, settings, half_count, arrays_ref)
        totals = alone(three_rows(stats_ref, 3))
        temper_ref[1:2, :] = other_diagonal(
            region, (other_weight, other_towards), stats_ref, totals, scratch, within_ref
        )

    @pl.when(half == 1)
    def _():
        totals = merged(three_rows(stats_ref, 0), three_rows(square_stats, 0))
        square = square_region(settings, half_count, square_ref)
        scales = (square.scaling, square.scaling, 1.0)
        across_query, *foreign, square_temper = square.gradients(
            square_weight, square_towards, square_stats[0:1, :], *totals, *scratch
        )
        for array, part in enumerate(foreign):
            for tile in range(square.tiles):
                across_ref[array, tile_rows(tile), :] = (part[tile] * scales[1 + array]).astype(
                    jnp.bfloat16
                )
        diagonal = diagonal_region(0, settings, half_count, arrays_ref)
        *parts, temper = diagonal.gradients(
            own_weight, own_towards, stats_ref[0:1, :], *totals, *scratch
        )
        for tile in range(square.tiles):
            put(within_ref, 0, tile, (parts[0][tile] + across_query[tile]) * scales[0])
            put(within_ref, 1, tile, parts[1][tile] * scales[1])
            put(within_ref, 2, tile, parts[2][tile])
        temper_ref[0:1, :] = temper + square_temper


def temper_rows(own, other):
    row = lax.broadcasted_iota(jnp.int32, (EXTRA, HD), 0)
    rows = jnp.zeros((EXTRA, HD), jnp.float32)
    for place, terms in enumerate((own, other)):
        rest = jnp.broadcast_to(jnp.sum(terms, axis=1, keepdims=True), (EXTRA, HD)) * (
            1.0 / math.sqrt(HD)
        )
        for piece in range(3):
            high = rest.astype(jnp.bfloat16).astype(jnp.float32)
            rows = jnp.where(row == place * 3 + piece, high, rows)
            rest = rest - high
    return rows.astype(jnp.bfloat16)


def finish_kernel(
    softness_ref, ids_ref, span_ref, arrays_ref, square_ref, message_ref, received_ref,
    stats_ref, square_stats, parts_ref, temper_ref,
    square_weight, square_towards, other_weight, other_towards, across_in, begun_ref,
    within_ref, *refs, half_count
):
    foreign_refs = refs[:2]
    across, temper, *scratch = refs[2:]
    _, half, place = position(half_count)
    settings = (softness_ref, ids_ref, span_ref)
    temper[...] = temper_ref[...]

    @pl.when(half == 0)
    def _():
        totals = merged(three_rows(message_ref, 0), three_rows(received_ref, 0))
        region = square_region(settings, half_count, square_ref)
        query_parts, key_parts, value_parts, square_temper = region.gradients(
            square_weight, square_towards, square_stats[0:1, :], *totals, *scratch
        )
        for tile in range(region.tiles):
            here = tile_rows(tile)
            across[0, here, :] = (query_parts[tile] * region.scaling).astype(jnp.bfloat16)
            put(within_ref, 0, tile, parts_ref[0, here, :] * region.scaling)
            put(within_ref, 1, tile, (parts_ref[1, here, :] + key_parts[tile]) * region.scaling)
            put(within_ref, 2, tile, parts_ref[2, here, :] + value_parts[tile])
        across[1] = jnp.zeros(across.shape[1:], jnp.bfloat16)
        within_ref[:, 3 * BLK : 6 * BLK, :] = begun_ref[:, 3 * BLK : 6 * BLK, :]
        temper[0:1, :] = temper_ref[0:1, :] + square_temper

    @pl.when(half == 1)
    def _():
        totals = merged(three_rows(message_ref, 0), three_rows(received_ref, 0))
        region = diagonal_region(1, settings, half_count, arrays_ref)
        temper[1:2, :] = other_diagonal(
            region, (other_weight, other_towards), stats_ref, totals, scratch, within_ref
        )
        across[...] = across_in[...]
        within_ref[:, : 3 * BLK, :] = begun_ref[:, : 3 * BLK, :]

    pieces = temper_rows(temper[0:1, :], temper[1:2, :])
    for block in range(half_count):
        within_ref[block, 6 * BLK : 6 * BLK + EXTRA, :] = pieces
    for core, foreign_ref in enumerate(foreign_refs):
        for step in range(half_count // 2):
            rows = rows_of(place ^ core ^ (2 * step))
            foreign_ref[step, :BLK, :] = across[0, rows, :]
            foreign_ref[step, BLK : 2 * BLK, :] = across[1, rows, :]
            foreign_ref[step, 2 * BLK :, :] = pieces


def temper_kernel(within_ref, *refs, half_count):
    across_refs, temper_ref = refs[: half_count // 2], refs[half_count // 2]
    _, half, place = position(half_count)

    def sums(rows):
        return [
            jnp.sum(rows[3 * slot : 3 * slot + 3, :].astype(jnp.float32), axis=0, keepdims=True)
            for slot in range(2)
        ]

    for step, across_ref in enumerate(across_refs):
        for core in range(2):
            peer = place ^ core ^ (2 * step)
            near, far = sums(within_ref[peer]), sums(across_ref[core])
            temper_ref[pl.ds(half * half_count + peer, 1), :] = near[0] + far[1]
            temper_ref[pl.ds((1 - half) * half_count + peer, 1), :] = near[1] + far[0]


def temper_sums(within, across, half_count):
    last = (6 * BLK // EXTRA, 2 * BLK // EXTRA)
    return pl.pallas_call(
        functools.partial(temper_kernel, half_count=half_count),
        grid=(1,),
        out_shape=jax.ShapeDtypeStruct((2 * half_count, HD), jnp.float32),
        in_specs=[pl.BlockSpec((half_count, EXTRA, HD), lambda step: (0, last[0], 0))]
        + [pl.BlockSpec((2, EXTRA, HD), lambda step: (0, last[1], 0))] * (half_count // 2),
        out_specs=pl.BlockSpec((2 * half_count, HD), lambda step: (0, 0)),
        compiler_params=pltpu.CompilerParams(vmem_limit_bytes=4 * MIB),
        name="temper_sums",
    )(within, *across)


def unpack_kernel(within_ref, *refs, half_count):
    across_refs = refs[: half_count // 2]
    out_refs = refs[half_count // 2 :]
    _, half, place = position(half_count)
    for step, across_ref in enumerate(across_refs):
        for core in range(2):
            peer = place ^ core ^ (2 * step)
            other = columns_of((1 - half) * half_count + peer)
            own = columns_of(half * half_count + peer)
            first = across_ref[core, :BLK, :].astype(jnp.float32)
            second = across_ref[core, BLK : 2 * BLK, :].astype(jnp.float32)
            added = (
                jnp.where(half == 0, 0.0, first),
                jnp.where(half == 0, first, 0.0),
                jnp.where(half == 0, second, 0.0),
            )
            for array, out_ref in enumerate(out_refs):
                out_ref[0, :, own] = within_ref[peer, array * BLK : (array + 1) * BLK, :]
                kept = within_ref[peer, (3 + array) * BLK : (4 + array) * BLK, :]
                out_ref[0, :, other] = (kept.astype(jnp.float32) + added[array]).astype(
                    jnp.bfloat16
                )


def join_kernel(kept_ref, taken_ref, *out_refs):
    for step, out_ref in enumerate(out_refs):
        out_ref[0] = kept_ref[step]
        out_ref[1] = taken_ref[step]


def crossed(kept, given, half_count):
    devices = range(2 * half_count)
    steps, *shape = kept.shape
    taken = lax.ppermute(given, "seq", [(source, source ^ 1) for source in devices])
    messages = kernel_call(
        join_kernel,
        "join_chunks",
        (kept, taken),
        [pl.BlockSpec(memory_space=pltpu.VMEM)] * 2,
        [jax.ShapeDtypeStruct((2, *shape), jnp.bfloat16)] * steps,
        [],
        4,
    )
    return [
        lax.ppermute(
            message, "seq", [(source, source ^ (half_count + 2 * step)) for source in devices]
        )
        for step, message in enumerate(messages)
    ]


def head_shards(
    probe_vectors,
    lookup_vectors,
    content_vectors,
    result_cotangent,
    logit_softness,
    block_grouping,
    neighborhood_span,
):
    seq_count, dp_count = lax.axis_size("seq"), lax.axis_size("dp")
    half_count = seq_count // 2
    tokens = half_count * BLK
    groups = [list(range(half_count)), list(range(half_count, seq_count))]
    settings = (logit_softness, block_grouping[0, :, :, 0], neighborhood_span)
    smem, vmem = pl.BlockSpec(memory_space=pltpu.SMEM), pl.BlockSpec(memory_space=pltpu.VMEM)
    lows = [pltpu.VMEM((tokens, tokens), jnp.bfloat16)] * 2 + [
        pltpu.VMEM((HD, tokens), jnp.bfloat16)
    ]
    rows_of_stats = jax.ShapeDtypeStruct((8, tokens), jnp.float32)
    pairs = jax.ShapeDtypeStruct((tokens, tokens), jnp.float32)
    pair_flops = 2 * tokens * tokens * HD

    def exchange_within(array_in):
        return lax.all_to_all(
            array_in, "seq", split_axis=0, concat_axis=0, axis_index_groups=groups, tiled=True
        )

    def call(kernel, name, operands, out_shape, scratch, flops, vmem_mib):
        return kernel_call(
            functools.partial(kernel, half_count=half_count),
            name,
            (*settings, *operands),
            [smem] * 3 + [vmem] * len(operands),
            out_shape,
            scratch,
            vmem_mib,
            flops,
        )

    sent, *foreign = packed(
        (probe_vectors, lookup_vectors, content_vectors, result_cotangent), half_count
    )
    arrived = exchange_within(sent)
    foreign = crossed(*foreign, half_count)
    kept_parts = jax.ShapeDtypeStruct((3, tokens, HD), jnp.float32)
    tempers = jax.ShapeDtypeStruct((8, HD), jnp.float32)
    arrays, stats, parts, temper, own_weight, own_towards, other_weight, other_towards = call(
        within_kernel,
        "diagonal_statistics",
        (arrived,),
        [jax.ShapeDtypeStruct((8, tokens, HD), jnp.bfloat16), rows_of_stats, kept_parts, tempers]
        + [pairs] * 4,
        lows,
        2 * pair_flops,
        20,
    )
    square, message, square_stats, square_weight, square_towards = call(
        square_kernel,
        "square_statistics",
        (arrays, stats, *foreign),
        [jax.ShapeDtypeStruct((4, tokens, HD), jnp.bfloat16)] + [rows_of_stats] * 2 + [pairs] * 2,
        [],
        2 * pair_flops,
        12,
    )
    swap = [(source, source ^ half_count) for source in range(seq_count)]
    received = lax.ppermute(message, "seq", swap)
    begun, across, temper = call(
        first_kernel,
        "gradients_before_totals",
        (
            arrays, square, stats, square_stats, temper, own_weight, own_towards,
            other_weight, other_towards, square_weight, square_towards,
        ),
        [
            jax.ShapeDtypeStruct((half_count, 6 * BLK, HD), jnp.bfloat16),
            jax.ShapeDtypeStruct((2, tokens, HD), jnp.bfloat16),
            tempers,
        ],
        lows,
        4 * pair_flops,
        14,
    )
    within, *foreign = call(
        finish_kernel,
        "gradients_after_totals",
        (
            arrays, square, message, received, stats, square_stats, parts, temper,
            square_weight, square_towards, other_weight, other_towards, across, begun,
        ),
        [jax.ShapeDtypeStruct((half_count, 6 * BLK + EXTRA, HD), jnp.bfloat16)]
        + [jax.ShapeDtypeStruct((half_count // 2, 2 * BLK + EXTRA, HD), jnp.bfloat16)] * 2,
        [pltpu.VMEM((2, tokens, HD), jnp.bfloat16), pltpu.VMEM((8, HD), jnp.float32), *lows],
        2 * pair_flops,
        20,
    )
    across = crossed(*foreign, half_count)
    within = exchange_within(within)
    tempers = temper_sums(within, across, half_count)
    temper_total = tempers
    for step in range(1, dp_count):
        swap = [(source, (source + step) % dp_count) for source in range(dp_count)]
        temper_total = temper_total + lax.ppermute(tempers, "dp", swap)
    outs = kernel_call(
        functools.partial(unpack_kernel, half_count=half_count),
        "unpack_heads",
        (within, *across),
        [vmem] * (1 + len(across)),
        [jax.ShapeDtypeStruct(probe_vectors.shape, jnp.bfloat16)] * 3,
        [],
        10,
    )
    return (*outs, temper_total[:, 0] / (dp_count * BLK * seq_count))


def shards(
    probe_vectors,
    lookup_vectors,
    content_vectors,
    result_cotangent,
    logit_softness,
    block_grouping,
    neighborhood_span,
):
    head_count = probe_vectors.shape[2] // HD
    seq_count = lax.axis_size("seq")
    one_block = probe_vectors.shape[1] == BLK
    whole_tiles = seq_count * BLK % (2 * TILE) == 0 and seq_count & (seq_count - 1) == 0
    if head_count == seq_count and one_block and whole_tiles:
        plan = head_shards
    else:
        plan = clustered_shards
    return plan(
        probe_vectors,
        lookup_vectors,
        content_vectors,
        result_cotangent,
        logit_softness,
        block_grouping,
        neighborhood_span,
    )


def solution(mesh):
    in_specs = (
        P("dp", "seq", None),
        P("dp", "seq", None),
        P("dp", "seq", None),
        P("dp", "seq", None),
        P(),
        P("dp", None, None, None),
        P(),
    )
    out_specs = (P("dp", "seq", None), P("dp", "seq", None), P("dp", "seq", None), P())
    return jax.shard_map(shards, mesh=mesh, in_specs=in_specs, out_specs=out_specs, check_vma=False)
```

```python
import functools
import math

import jax
import jax.numpy as jnp
from jax import lax
from jax.experimental import pallas as pl
from jax.experimental.pallas import tpu as pltpu
from jax.sharding import PartitionSpec as P

HD = 128
BLK = 128


blocked_score = -1e30


def shifted(value, axis, steps):
    count = lax.axis_size(axis)
    first, last = (max(0, -steps), min(count, count - steps))
    return lax.ppermute(value, axis, [(source, source + steps) for source in range(first, last)])


def lifted(array_in):
    return lax.optimization_barrier(array_in.astype(jnp.bfloat16)).astype(jnp.float32)


def head_major(tokens_in, block_len):
    token_count, feature_count = tokens_in.shape
    return tokens_in.reshape(
        token_count // block_len, block_len, feature_count // HD, HD
    ).transpose(2, 0, 1, 3)


def token_major(blocks_in):
    head_count, block_count, block_len, depth = blocks_in.shape
    return blocks_in.transpose(1, 2, 0, 3).reshape(1, block_count * block_len, head_count * depth)


def window_parts(query_block, prev_keys, prev_values, grad_block, usable, window_width, temper):
    block_len = query_block.shape[-2]
    inverse_root = 1.0 / math.sqrt(query_block.shape[-1])
    raw_scores = (
        jnp.einsum("...td,...sd->...ts", query_block, prev_keys, preferred_element_type=jnp.float32)
        * inverse_root
    )
    query_pos = lax.broadcasted_iota(jnp.int32, (block_len, block_len), 0)
    key_pos = lax.broadcasted_iota(jnp.int32, (block_len, block_len), 1)
    pair_mask = usable[..., None, None] & (
        key_pos > query_pos + block_len - window_width[..., None, None]
    )
    scores = temper[..., None, None] * raw_scores
    row_top = jnp.max(jnp.where(pair_mask, scores, blocked_score), axis=-1)
    weights = jnp.where(pair_mask, jnp.exp(scores - row_top[..., None]), 0.0)
    prob_grad = jnp.einsum(
        "...td,...sd->...ts", grad_block, prev_values, preferred_element_type=jnp.float32
    )
    return (
        raw_scores,
        pair_mask,
        prob_grad,
        row_top,
        jnp.sum(weights, axis=-1),
        jnp.sum(weights * prob_grad, axis=-1),
    )


def window_grads(
    raw_scores,
    pair_mask,
    prob_grad,
    query_block,
    prev_keys,
    grad_block,
    log_total,
    row_delta,
    temper,
):
    inverse_root = 1.0 / math.sqrt(query_block.shape[-1])
    scaling = (temper * inverse_root)[..., None, None]
    probability = jnp.where(
        pair_mask, jnp.exp(temper[..., None, None] * raw_scores - log_total[..., None]), 0.0
    )
    score_grad = probability * (prob_grad - row_delta[..., None])
    prob_low = probability.astype(jnp.bfloat16)
    grad_low = score_grad.astype(jnp.bfloat16)
    query_part = (
        jnp.einsum("...ts,...sd->...td", grad_low, prev_keys, preferred_element_type=jnp.float32)
        * scaling
    )
    key_part = (
        jnp.einsum("...ts,...td->...sd", grad_low, query_block, preferred_element_type=jnp.float32)
        * scaling
    )
    value_part = jnp.einsum(
        "...ts,...td->...sd", prob_low, grad_block, preferred_element_type=jnp.float32
    )
    temper_part = jnp.sum(score_grad * raw_scores, axis=(-2, -1))
    return (query_part, key_part, value_part, temper_part)


def cluster_pair(
    query_items,
    key_items,
    value_items,
    grad_items,
    live_items,
    temper,
    window_top,
    window_total,
    window_mass,
):
    item_count, block_len, depth = query_items.shape
    row_count = item_count * block_len
    group_rows = 4 * block_len
    inverse_root = 1.0 / math.sqrt(depth)
    scaling = temper * inverse_root
    query_rows = query_items.reshape(row_count, depth)
    key_rows = key_items.reshape(row_count, depth)
    value_rows = value_items.reshape(row_count, depth)
    grad_rows = grad_items.reshape(row_count, depth)
    key_item = jnp.arange(row_count) // block_len
    key_token = jnp.arange(row_count) % block_len
    live_rows = jnp.repeat(live_items, block_len)
    top_rows = window_top.reshape(row_count)
    total_rows = window_total.reshape(row_count)
    mass_rows = window_mass.reshape(row_count)

    def group_step(carry, start_row):
        key_acc, value_acc, temper_acc = carry
        query_group = lax.dynamic_slice_in_dim(query_rows, start_row, group_rows, 0)
        grad_group = lax.dynamic_slice_in_dim(grad_rows, start_row, group_rows, 0)
        group_live = lax.dynamic_slice_in_dim(live_rows, start_row, group_rows, 0)
        group_top = lax.dynamic_slice_in_dim(top_rows, start_row, group_rows, 0)
        group_total = lax.dynamic_slice_in_dim(total_rows, start_row, group_rows, 0)
        group_mass = lax.dynamic_slice_in_dim(mass_rows, start_row, group_rows, 0)
        query_item = (start_row + jnp.arange(group_rows)) // block_len
        query_token = jnp.arange(group_rows) % block_len
        earlier = (key_item[None, :] < query_item[:, None]) | (
            key_item[None, :] == query_item[:, None]
        ) & (key_token[None, :] <= query_token[:, None])
        pair_mask = group_live[:, None] & live_rows[None, :] & earlier
        raw_scores = (
            lax.dot_general(
                query_group, key_rows, (((1,), (1,)), ((), ())), preferred_element_type=jnp.float32
            )
            * inverse_root
        )
        scores = temper * raw_scores
        row_top = jnp.maximum(
            jnp.max(jnp.where(pair_mask, scores, blocked_score), axis=1), group_top
        )
        weights = jnp.where(pair_mask, jnp.exp(scores - row_top[:, None]), 0.0)
        row_total = jnp.sum(weights, axis=1) + group_total * jnp.exp(group_top - row_top)
        log_total = row_top + jnp.log(jnp.where(group_live, row_total, 1.0))
        probability = jnp.where(pair_mask, jnp.exp(scores - log_total[:, None]), 0.0)
        prob_grad = lax.dot_general(
            grad_group, value_rows, (((1,), (1,)), ((), ())), preferred_element_type=jnp.float32
        )
        row_delta = jnp.sum(probability * prob_grad, axis=1) + group_mass * jnp.exp(
            group_top - log_total
        )
        score_grad = probability * (prob_grad - row_delta[:, None])
        prob_low = probability.astype(jnp.bfloat16)
        grad_low = score_grad.astype(jnp.bfloat16)
        query_part = jnp.dot(grad_low, key_rows, preferred_element_type=jnp.float32) * scaling
        key_acc = (
            key_acc
            + lax.dot_general(
                grad_low, query_group, (((0,), (0,)), ((), ())), preferred_element_type=jnp.float32
            )
            * scaling
        )
        value_acc = value_acc + lax.dot_general(
            prob_low, grad_group, (((0,), (0,)), ((), ())), preferred_element_type=jnp.float32
        )
        temper_acc = temper_acc + jnp.sum(score_grad * raw_scores)
        return ((key_acc, value_acc, temper_acc), (query_part, log_total, row_delta))

    start_rows = jnp.arange(item_count // 4) * group_rows
    initial = (
        jnp.zeros((row_count, depth), jnp.float32),
        jnp.zeros((row_count, depth), jnp.float32),
        jnp.zeros((), jnp.float32),
    )
    (key_acc, value_acc, temper_acc), (query_part, log_total, row_delta) = lax.scan(
        group_step, initial, start_rows
    )
    return (
        query_part.reshape(item_count, block_len, depth),
        log_total.reshape(item_count, block_len),
        row_delta.reshape(item_count, block_len),
        key_acc.reshape(item_count, block_len, depth),
        value_acc.reshape(item_count, block_len, depth),
        temper_acc,
    )


def clustered_shards(
    probe_vectors,
    lookup_vectors,
    content_vectors,
    result_cotangent,
    logit_softness,
    block_grouping,
    neighborhood_span,
):
    seq_count = lax.axis_size("seq")
    position = lax.axis_index("seq")
    tokens = probe_vectors.shape[1]
    head_count = probe_vectors.shape[2] // HD
    local_blocks = tokens // BLK
    block_count = local_blocks * seq_count
    cluster_count = max(1, block_count // 8)
    capacity = min(12, block_count)
    owned_pairs = cluster_count * head_count // seq_count
    group_count = cluster_count // owned_pairs
    per_peer = max(1, local_blocks // group_count)
    cluster_ids = block_grouping[0, :, :, 0]
    query_home = head_major(probe_vectors[0], BLK)
    key_home = head_major(lookup_vectors[0], BLK)
    value_home = head_major(content_vectors[0], BLK)
    grad_home = head_major(result_cotangent[0], BLK)
    last_block = (lookup_vectors[0, tokens - BLK :], content_vectors[0, tokens - BLK :])
    prev_key_rows, prev_value_rows = shifted((last_block[0], last_block[1]), "seq", 1)
    prev_keys = jnp.concatenate([head_major(prev_key_rows, BLK), key_home[:, :-1]], axis=1)
    prev_values = jnp.concatenate([head_major(prev_value_rows, BLK), value_home[:, :-1]], axis=1)
    first_block = position * local_blocks
    before = jnp.concatenate(
        [jnp.full((head_count, 1), -1, jnp.int32), cluster_ids[:, :-1]], axis=1
    )
    my_ids = lax.dynamic_slice_in_dim(cluster_ids, first_block, local_blocks, 1)
    my_before = lax.dynamic_slice_in_dim(before, first_block, local_blocks, 1)
    global_block = first_block + jnp.arange(local_blocks)
    usable_home = (global_block[None, :] >= 1) & (my_before != my_ids)
    peer_index = jnp.arange(seq_count)
    peer_head = peer_index * owned_pairs // cluster_count
    slot_range = jnp.arange(per_peer)
    local_range = jnp.arange(local_blocks)
    owner_index = (jnp.arange(head_count)[:, None] * cluster_count + my_ids) // owned_pairs
    peer_ids = jnp.take(my_ids, peer_head, axis=0)
    goes = (peer_head[:, None] * cluster_count + peer_ids) // owned_pairs == peer_index[:, None]
    send_rank = jnp.cumsum(goes.astype(jnp.int32), axis=1) - 1
    send_pick = goes[:, None, :] & (send_rank[:, None, :] == slot_range[None, :, None])
    send_block = jnp.sum(jnp.where(send_pick, local_range[None, None, :], 0), axis=2)
    send_flat = peer_head[:, None] * local_blocks + send_block
    home_rank = jnp.take_along_axis(send_rank, owner_index, axis=0)
    home_pos = owner_index * per_peer + home_rank
    pair_index = position * owned_pairs + jnp.arange(owned_pairs)
    split_for_couple = pair_index // cluster_count
    pair_cluster = pair_index % cluster_count
    my_head = position * owned_pairs // cluster_count
    split_numbers = jnp.take(cluster_ids, my_head, axis=0)
    member = split_numbers[None, :] == pair_cluster[:, None]
    member_rank = jnp.cumsum(member.astype(jnp.int32), axis=1) - 1
    member_count = jnp.sum(member.astype(jnp.int32), axis=1)
    picked = member[:, None, :] & (member_rank[:, None, :] == jnp.arange(capacity)[None, :, None])
    member_block = jnp.sum(jnp.where(picked, jnp.arange(block_count)[None, None, :], 0), axis=2)
    live_members = jnp.arange(capacity)[None, :] < member_count[:, None]
    mine = (my_head * cluster_count + split_numbers) // owned_pairs == position
    mine_grid = mine.reshape(seq_count, local_blocks)
    recv_rank = jnp.cumsum(mine_grid.astype(jnp.int32), axis=1) - 1
    recv_pos = (peer_index[:, None] * per_peer + recv_rank).reshape(block_count)
    member_pos = jnp.take(recv_pos, member_block)
    couple_softness = jnp.take(logit_softness, split_for_couple)
    pair_onehot = (split_for_couple[:, None] == jnp.arange(head_count)[None, :]).astype(jnp.float32)
    slot_pair = my_head * cluster_count + split_numbers - position * owned_pairs
    same_cluster = split_numbers[:, None] == split_numbers[None, :]
    earlier_block = jnp.arange(block_count)[None, :] < jnp.arange(block_count)[:, None]
    slot_rank = jnp.sum((same_cluster & earlier_block).astype(jnp.int32), axis=1)
    back_pos = jnp.clip(slot_pair, 0, owned_pairs - 1) * capacity + jnp.clip(
        slot_rank, 0, capacity - 1
    )
    back_grid = back_pos.reshape(seq_count, local_blocks)
    back_pick = mine_grid[:, None, :] & (recv_rank[:, None, :] == slot_range[None, :, None])
    back_flat = jnp.sum(jnp.where(back_pick, back_grid[:, None, :], 0), axis=2)

    def to_peers(array_in):
        flat = array_in.reshape((head_count * local_blocks,) + array_in.shape[2:])
        return jnp.take(flat, send_flat, axis=0)

    def members(array_in):
        flat = array_in.reshape((seq_count * per_peer,) + array_in.shape[2:])
        return jnp.take(flat, member_pos, axis=0)

    def to_owner(array_in):
        flat = array_in.reshape((owned_pairs * capacity,) + array_in.shape[2:])
        return jnp.take(flat, back_flat, axis=0)

    def from_peers(array_in):
        flat = array_in.reshape((seq_count * per_peer,) + array_in.shape[2:])
        return jnp.take(flat, home_pos, axis=0)

    raw_w, mask_w, pgrad_w, top_w, total_w, mass_w = window_parts(
        query_home,
        prev_keys,
        prev_values,
        grad_home,
        usable_home,
        neighborhood_span[:, None],
        logit_softness[:, None],
    )
    arrived = (
        lax.all_to_all(to_peers(query_home), "seq", split_axis=0, concat_axis=0, tiled=True),
        lax.all_to_all(to_peers(key_home), "seq", split_axis=0, concat_axis=0, tiled=True),
        lax.all_to_all(to_peers(value_home), "seq", split_axis=0, concat_axis=0, tiled=True),
        lax.all_to_all(to_peers(grad_home), "seq", split_axis=0, concat_axis=0, tiled=True),
    )
    arrived_stats = (
        lax.all_to_all(to_peers(top_w), "seq", split_axis=0, concat_axis=0, tiled=True),
        lax.all_to_all(to_peers(total_w), "seq", split_axis=0, concat_axis=0, tiled=True),
        lax.all_to_all(to_peers(mass_w), "seq", split_axis=0, concat_axis=0, tiled=True),
    )
    query_m, key_m, value_m, grad_m = [members(item_in) for item_in in arrived]
    top_m, total_m, mass_m = [members(item_in) for item_in in arrived_stats]

    def split_pair(pair_inputs):
        query_i, key_i, value_i, grad_i, live_i, temper_i, top_i, total_i, mass_i = pair_inputs
        query_c, log_total, row_delta, key_c, value_c, temper_c = cluster_pair(
            query_i, key_i, value_i, grad_i, live_i, temper_i, top_i, total_i, mass_i
        )
        return (
            query_c.astype(jnp.bfloat16),
            key_c.astype(jnp.bfloat16),
            value_c.astype(jnp.bfloat16),
            log_total,
            row_delta,
            temper_c,
        )

    owner_results = lax.map(
        split_pair,
        (query_m, key_m, value_m, grad_m, live_members, couple_softness, top_m, total_m, mass_m),
    )
    returned = (
        lax.all_to_all(to_owner(owner_results[0]), "seq", split_axis=0, concat_axis=0, tiled=True),
        lax.all_to_all(to_owner(owner_results[1]), "seq", split_axis=0, concat_axis=0, tiled=True),
        lax.all_to_all(to_owner(owner_results[2]), "seq", split_axis=0, concat_axis=0, tiled=True),
    )
    returned_stats = (
        lax.all_to_all(to_owner(owner_results[3]), "seq", split_axis=0, concat_axis=0, tiled=True),
        lax.all_to_all(to_owner(owner_results[4]), "seq", split_axis=0, concat_axis=0, tiled=True),
    )
    query_cluster = from_peers(returned[0])
    key_cluster = from_peers(returned[1])
    value_cluster = from_peers(returned[2])
    log_home = from_peers(returned_stats[0])
    delta_home = from_peers(returned_stats[1])
    query_w, key_w, value_w, temper_w = window_grads(
        raw_w,
        mask_w,
        pgrad_w,
        query_home,
        prev_keys,
        grad_home,
        log_home,
        delta_home,
        logit_softness[:, None],
    )
    query_out = (query_cluster.astype(jnp.float32) + lifted(query_w)).astype(jnp.bfloat16)
    key_window = key_w.astype(jnp.bfloat16)
    value_window = value_w.astype(jnp.bfloat16)
    temper_local = jnp.sum(owner_results[5][:, None] * pair_onehot, axis=0) + jnp.sum(
        temper_w, axis=1
    )
    edge_keys, edge_values = shifted((key_window[:, 0], value_window[:, 0]), "seq", -1)
    key_next = jnp.concatenate([key_window[:, 1:], edge_keys[:, None]], axis=1)
    value_next = jnp.concatenate([value_window[:, 1:], edge_values[:, None]], axis=1)
    key_out = (key_cluster.astype(jnp.float32) + key_next.astype(jnp.float32)).astype(jnp.bfloat16)
    value_out = (value_cluster.astype(jnp.float32) + value_next.astype(jnp.float32)).astype(
        jnp.bfloat16
    )
    temper_total = lax.psum(temper_local, ("seq", "dp"))
    temper_grad = temper_total / (lax.axis_size("dp") * tokens * seq_count)
    return (token_major(query_out), token_major(key_out), token_major(value_out), temper_grad)


TILE = 256
MIB = 1024 * 1024
PIECES = 4
QUERY, KEY, VALUE, GRAD = range(4)


def columns_of(index):
    return pl.ds(pl.multiple_of(index * HD, HD), HD)


def rows_of(index):
    return pl.ds(pl.multiple_of(index * BLK, BLK), BLK)


def tile_rows(tile):
    return slice(tile * TILE, (tile + 1) * TILE)


def position(half_count):
    me = lax.axis_index("seq")
    half = jnp.where(me >= half_count, 1, 0)
    return me, half, me - half * half_count


def kernel_call(
    kernel, name, operands, in_specs, out_shape, scratch, vmem_mib, flops=0, out_space=pltpu.VMEM
):
    bytes_accessed = sum(
        math.prod(item.shape) * item.dtype.itemsize for item in (*operands, *out_shape)
    )
    return pl.pallas_call(
        kernel,
        out_shape=out_shape,
        in_specs=in_specs,
        out_specs=[pl.BlockSpec(memory_space=out_space)] * len(out_shape),
        scratch_shapes=scratch,
        cost_estimate=pl.CostEstimate(
            flops=flops, bytes_accessed=bytes_accessed, transcendentals=0
        ),
        compiler_params=pltpu.CompilerParams(vmem_limit_bytes=vmem_mib * MIB),
        name=name,
    )(*operands)


def pack_kernel(*refs, half_count):
    arrays, within_ref, foreign_refs = refs[:4], refs[4], refs[5:7]
    held, within, across, arrival, left_within, left_across = refs[7:]
    me, half, _ = position(half_count)
    piece = BLK // PIECES
    arrivals = [
        [
            pltpu.make_async_copy(
                array_ref.at[0, part * piece : (part + 1) * piece, :],
                held.at[place, part * piece : (part + 1) * piece, :],
                arrival.at[place, part],
            )
            for part in range(PIECES)
        ]
        for place, array_ref in enumerate(arrays)
    ]
    for copies in arrivals:
        for copy in copies:
            copy.start()
    leaving = []
    for place, copies in enumerate(arrivals):
        for copy in copies:
            copy.wait()
        for slot, base in enumerate((half * half_count, (1 - half) * half_count)):
            rows = slice((slot * 4 + place) * BLK, (slot * 4 + place + 1) * BLK)
            for peer in range(half_count):
                within[peer, rows, :] = held[place, :, columns_of(base + peer)]
            leaving.append(
                pltpu.make_async_copy(
                    within.at[:, rows, :], within_ref.at[:, rows, :], left_within.at[place, slot]
                )
            )
            leaving[-1].start()
    first = jnp.where(half == 0, KEY, QUERY)
    second = jnp.where(half == 0, VALUE, GRAD)
    for core, foreign_ref in enumerate(foreign_refs):
        for step in range(half_count // 2):
            columns = columns_of(me ^ core ^ (half_count + 2 * step))
            across[core, step, :BLK, :] = held[first, :, columns]
            across[core, step, BLK:, :] = held[second, :, columns]
        leaving.append(pltpu.make_async_copy(across.at[core], foreign_ref, left_across.at[core]))
        leaving[-1].start()
    for copy in leaving:
        copy.wait()


def packed(arrays, half_count):
    width = arrays[0].shape[2]
    within_shape, across_shape = (half_count, 8 * BLK, HD), (half_count // 2, 2 * BLK, HD)
    return kernel_call(
        functools.partial(pack_kernel, half_count=half_count),
        "pack_heads",
        arrays,
        [pl.BlockSpec(memory_space=pl.ANY)] * 4,
        [jax.ShapeDtypeStruct(within_shape, jnp.bfloat16)]
        + [jax.ShapeDtypeStruct(across_shape, jnp.bfloat16)] * 2,
        [
            pltpu.VMEM((4, BLK, width), jnp.bfloat16),
            pltpu.VMEM(within_shape, jnp.bfloat16),
            pltpu.VMEM((2, *across_shape), jnp.bfloat16),
            pltpu.SemaphoreType.DMA((4, PIECES)),
            pltpu.SemaphoreType.DMA((4, 2)),
            pltpu.SemaphoreType.DMA((2,)),
        ],
        60,
        out_space=pl.ANY,
    )


def dot_rows(left, right):
    return lax.dot_general(
        left, right, (((1,), (1,)), ((), ())), preferred_element_type=jnp.float32
    )


def dot_plain(left, right):
    return lax.dot_general(
        left, right, (((1,), (0,)), ((), ())), preferred_element_type=jnp.float32
    )


class Region:
    def __init__(self, head, settings, square, key_base, query_base, arrays, places):
        softness_ref, self.ids_ref, span_ref = settings
        self.head, self.square = head, square
        self.key_base, self.query_base = key_base, query_base
        self.arrays, self.places = arrays, places
        self.tiles = arrays.shape[1] // TILE
        self.width = span_ref[head]
        self.scaling = softness_ref[head] * (1.0 / math.sqrt(HD))
        self.to_log2 = self.scaling * math.log2(math.e)

    def rows(self, which, start, stop):
        return self.arrays[self.places[which], start * TILE : stop * TILE, :]

    def keys_of(self, tile):
        return range(self.tiles if self.square else tile + 1)

    def scores(self, tile_key, tile_query):
        per_tile = TILE // BLK
        scores = (
            dot_rows(
                self.rows(KEY, tile_key, tile_key + 1), self.rows(QUERY, tile_query, tile_query + 1)
            )
            * self.to_log2
        )
        spread = lax.broadcasted_iota(jnp.int32, (BLK, BLK), 0) - lax.broadcasted_iota(
            jnp.int32, (BLK, BLK), 1
        )
        rows = []
        for sub_key in range(per_tile):
            pieces = []
            for sub_query in range(per_tile):
                piece = scores[
                    sub_key * BLK : (sub_key + 1) * BLK, sub_query * BLK : (sub_query + 1) * BLK
                ]
                key_block = tile_key * per_tile + sub_key
                query_block = tile_query * per_tile + sub_query
                apart = query_block - key_block
                if self.square:
                    apart += self.tiles * per_tile
                same = (
                    self.ids_ref[self.head, self.key_base + key_block]
                    == self.ids_ref[self.head, self.query_base + query_block]
                )
                if apart < 0:
                    piece = jnp.full_like(piece, blocked_score)
                elif apart == 0:
                    piece = jnp.where(spread <= 0, piece, blocked_score)
                elif apart == 1:
                    least = jnp.where(same, -BLK, BLK - self.width)
                    piece = jnp.where(spread > least, piece, blocked_score)
                else:
                    piece = piece + jnp.where(same, 0.0, blocked_score)
                pieces.append(piece)
            rows.append(jnp.concatenate(pieces, axis=1))
        return jnp.concatenate(rows, axis=0)

    def statistics(self, weight_ref, towards_ref, out_ref, first_row):
        for tile in range(self.tiles):
            here = tile_rows(tile)
            top = jnp.full((1, TILE), blocked_score, jnp.float32)
            for other in self.keys_of(tile):
                raw = self.scores(other, tile)
                weight_ref[tile_rows(other), here] = raw
                top = jnp.maximum(top, jnp.max(raw, axis=0, keepdims=True))
            total = jnp.zeros((1, TILE), jnp.float32)
            mass = jnp.zeros((1, TILE), jnp.float32)
            for other in self.keys_of(tile):
                there = tile_rows(other)
                weight = jnp.exp2(weight_ref[there, here] - top)
                towards = dot_rows(
                    self.rows(VALUE, other, other + 1), self.rows(GRAD, tile, tile + 1)
                )
                weight_ref[there, here] = weight
                towards_ref[there, here] = towards
                total += jnp.sum(weight, axis=0, keepdims=True)
                mass += jnp.sum(weight * towards, axis=0, keepdims=True)
            out_ref[first_row : first_row + 1, here] = top
            out_ref[first_row + 1 : first_row + 2, here] = total
            out_ref[first_row + 2 : first_row + 3, here] = mass

    def gradients(self, weight_ref, towards_ref, top, log_total, delta, prob_low, grad_low, keys_flat):
        keys_flat[...] = self.rows(KEY, 0, self.tiles).T
        share = jnp.exp2(top - log_total)
        temper = jnp.zeros((1, HD), jnp.float32)
        query_parts, key_parts, value_parts = [], [], []
        for tile in range(self.tiles):
            here = tile_rows(tile)
            for other in self.keys_of(tile):
                there = tile_rows(other)
                probability = weight_ref[there, here] * share[:, here]
                prob_low[there, here] = probability.astype(jnp.bfloat16)
                grad_low[there, here] = (
                    probability * (towards_ref[there, here] - delta[:, here])
                ).astype(jnp.bfloat16)
            upto = slice(0, len(self.keys_of(tile)) * TILE)
            query_part = dot_plain(keys_flat[:, upto], grad_low[upto, here]).T
            temper += jnp.sum(
                query_part * self.rows(QUERY, tile, tile + 1).astype(jnp.float32),
                axis=0,
                keepdims=True,
            )
            query_parts.append(query_part)
        for tile in range(self.tiles):
            first = 0 if self.square else tile
            onward = slice(first * TILE, self.tiles * TILE)
            here = tile_rows(tile)
            key_parts.append(
                dot_plain(grad_low[here, onward], self.rows(QUERY, first, self.tiles))
            )
            value_parts.append(
                dot_plain(prob_low[here, onward], self.rows(GRAD, first, self.tiles))
            )
        return query_parts, key_parts, value_parts, temper


def merged(first, second):
    top = jnp.maximum(first[0], second[0])
    left, right = jnp.exp2(first[0] - top), jnp.exp2(second[0] - top)
    total = first[1] * left + second[1] * right
    mass = first[2] * left + second[2] * right
    return top + jnp.log2(total), mass / total


def alone(rows):
    return rows[0] + jnp.log2(rows[1]), rows[2] / rows[1]


def three_rows(ref, first):
    return [ref[first + row : first + row + 1, :] for row in range(3)]


def put(within_ref, array, tile, value):
    per_tile = TILE // BLK
    for sub in range(per_tile):
        within_ref[tile * per_tile + sub, array * BLK : (array + 1) * BLK, :] = value[
            sub * BLK : (sub + 1) * BLK, :
        ].astype(jnp.bfloat16)


def diagonal_region(slot, settings, half_count, arrays_ref):
    me, half, _ = position(half_count)
    head = me ^ (slot * half_count)
    places = [slot * 4 + place for place in range(4)]
    base = half * half_count
    return Region(head, settings, False, base, base, arrays_ref, places)


def square_region(settings, half_count, square_ref):
    me = lax.axis_index("seq")
    return Region(me, settings, True, 0, half_count, square_ref, range(4))


def within_kernel(
    softness_ref, ids_ref, span_ref, in_ref, arrays_ref, stats_ref, message_ref, parts_ref,
    other_ref, temper_ref, own_weight, own_towards, other_weight, other_towards, *scratch, half_count
):
    _, half, _ = position(half_count)
    for block in range(half_count):
        for place in range(8):
            arrays_ref[place, block * BLK : (block + 1) * BLK, :] = in_ref[
                block, place * BLK : (place + 1) * BLK, :
            ]
    settings = (softness_ref, ids_ref, span_ref)
    kept = ((own_weight, own_towards), (other_weight, other_towards))
    regions = [diagonal_region(slot, settings, half_count, arrays_ref) for slot in range(2)]
    for slot, region in enumerate(regions):
        region.statistics(*kept[slot], stats_ref, slot * 3)
    temper_ref[...] = jnp.zeros_like(temper_ref)
    for row in range(3):
        message_ref[row : row + 1, :] = stats_ref[3 + row : 4 + row, :]

    @pl.when(half == 0)
    def _():
        single = alone(three_rows(stats_ref, 0))
        *parts, temper = regions[0].gradients(*kept[0], stats_ref[0:1, :], *single, *scratch)
        for place, tiles in enumerate(parts):
            for tile, value in enumerate(tiles):
                parts_ref[place, tile_rows(tile), :] = value
        temper_ref[0:1, :] = temper
        single = alone(three_rows(stats_ref, 3))
        temper_ref[1:2, :] = other_diagonal(
            regions[1], kept[1], stats_ref, single, scratch, other_ref, 0
        )


def square_kernel(
    softness_ref, ids_ref, span_ref, arrays_ref, stats_ref, *refs, half_count
):
    across_refs = refs[: half_count // 2]
    square_ref, square_stats, weight, towards = refs[half_count // 2 :]
    _, half, place = position(half_count)
    first = jnp.where(half == 0, QUERY, KEY)
    second = jnp.where(half == 0, GRAD, VALUE)
    for step, across_ref in enumerate(across_refs):
        for core in range(2):
            rows = rows_of(place ^ core ^ (2 * step))
            square_ref[first, rows, :] = across_ref[core, :BLK, :]
            square_ref[second, rows, :] = across_ref[core, BLK:, :]
    kept_first = jnp.where(half == 0, KEY, QUERY)
    kept_second = jnp.where(half == 0, VALUE, GRAD)
    square_ref[kept_first, :, :] = arrays_ref[kept_first, :, :]
    square_ref[kept_second, :, :] = arrays_ref[kept_second, :, :]
    region = square_region((softness_ref, ids_ref, span_ref), half_count, square_ref)
    region.statistics(weight, towards, square_stats, 0)


def other_diagonal(region, kept, stats_ref, totals, scratch, out_ref, first):
    *parts, temper = region.gradients(*kept, stats_ref[3:4, :], *totals, *scratch)
    scales = (region.scaling, region.scaling, 1.0)
    for array, (part, scale) in enumerate(zip(parts, scales)):
        for tile in range(region.tiles):
            put(out_ref, first + array, tile, part[tile] * scale)
    return temper


def own_kernel(
    softness_ref, ids_ref, span_ref, arrays_ref, square_ref, stats_ref, square_stats, received_ref,
    parts_ref, temper_in, own_weight, own_towards, square_weight, square_towards,
    own_ref, across_ref, temper_ref, *scratch, half_count
):
    _, half, _ = position(half_count)
    settings = (softness_ref, ids_ref, span_ref)
    temper_ref[...] = temper_in[...]

    @pl.when(half == 0)
    def _():
        totals = merged(three_rows(square_stats, 0), three_rows(received_ref, 0))
        square = square_region(settings, half_count, square_ref)
        query_parts, key_parts, value_parts, square_temper = square.gradients(
            square_weight, square_towards, square_stats[0:1, :], *totals, *scratch
        )
        for tile in range(square.tiles):
            here = tile_rows(tile)
            across_ref[0, here, :] = (query_parts[tile] * square.scaling).astype(jnp.bfloat16)
            put(own_ref, 0, tile, parts_ref[0, here, :] * square.scaling)
            put(own_ref, 1, tile, (parts_ref[1, here, :] + key_parts[tile]) * square.scaling)
            put(own_ref, 2, tile, parts_ref[2, here, :] + value_parts[tile])
        across_ref[1] = jnp.zeros(across_ref.shape[1:], jnp.bfloat16)
        temper_ref[0:1, :] = temper_in[0:1, :] + square_temper

    @pl.when(half == 1)
    def _():
        totals = merged(three_rows(stats_ref, 0), three_rows(square_stats, 0))
        square = square_region(settings, half_count, square_ref)
        scales = (square.scaling, square.scaling, 1.0)
        across_query, *foreign, square_temper = square.gradients(
            square_weight, square_towards, square_stats[0:1, :], *totals, *scratch
        )
        for array, part in enumerate(foreign):
            for tile in range(square.tiles):
                across_ref[array, tile_rows(tile), :] = (part[tile] * scales[1 + array]).astype(
                    jnp.bfloat16
                )
        diagonal = diagonal_region(0, settings, half_count, arrays_ref)
        *parts, temper = diagonal.gradients(
            own_weight, own_towards, stats_ref[0:1, :], *totals, *scratch
        )
        for tile in range(square.tiles):
            put(own_ref, 0, tile, (parts[0][tile] + across_query[tile]) * scales[0])
            put(own_ref, 1, tile, parts[1][tile] * scales[1])
            put(own_ref, 2, tile, parts[2][tile])
        temper_ref[0:1, :] = temper + square_temper


def finish_kernel(
    softness_ref, ids_ref, span_ref, arrays_ref, stats_ref, received_ref, own_ref, other_ref,
    temper_ref, other_weight, other_towards, across_ref, within_ref, *refs, half_count
):
    foreign_refs, (out_temper, temper, *scratch) = refs[:2], refs[2:]
    me, half, place = position(half_count)
    settings = (softness_ref, ids_ref, span_ref)
    temper[...] = temper_ref[...]
    within_ref[:, : 3 * BLK, :] = own_ref[...]
    for core, foreign_ref in enumerate(foreign_refs):
        for step in range(half_count // 2):
            rows = rows_of(place ^ core ^ (2 * step))
            foreign_ref[step, :BLK, :] = across_ref[0, rows, :]
            foreign_ref[step, BLK:, :] = across_ref[1, rows, :]

    @pl.when(half == 0)
    def _():
        within_ref[:, 3 * BLK :, :] = other_ref[...]

    @pl.when(half == 1)
    def _():
        totals = merged(three_rows(stats_ref, 3), three_rows(received_ref, 0))
        region = diagonal_region(1, settings, half_count, arrays_ref)
        temper[1:2, :] = other_diagonal(
            region, (other_weight, other_towards), stats_ref, totals, scratch, within_ref, 3
        )

    lane = lax.broadcasted_iota(jnp.int32, (1, HD), 1)
    own_sum = jnp.sum(temper[0:1, :], axis=1, keepdims=True)
    other_sum = jnp.sum(temper[1:2, :], axis=1, keepdims=True)
    terms = jnp.where(lane == me, own_sum, 0.0) + jnp.where(
        lane == me ^ half_count, other_sum, 0.0
    )
    out_temper[...] = terms * (1.0 / math.sqrt(HD))


def unpack_kernel(tempers_ref, within_ref, *refs, half_count):
    across_refs = refs[: half_count // 2]
    *out_refs, temper_ref = refs[half_count // 2 :]
    _, half, place = position(half_count)
    every = jnp.sum(tempers_ref[...], axis=0, keepdims=True)
    temper_ref[...] = every[:, : temper_ref.shape[1]] * (1.0 / (tempers_ref.shape[0] * BLK))
    for step, across_ref in enumerate(across_refs):
        for core in range(2):
            peer = place ^ core ^ (2 * step)
            other = columns_of((1 - half) * half_count + peer)
            own = columns_of(half * half_count + peer)
            first = across_ref[core, :BLK, :].astype(jnp.float32)
            second = across_ref[core, BLK : 2 * BLK, :].astype(jnp.float32)
            added = (
                jnp.where(half == 0, 0.0, first),
                jnp.where(half == 0, first, 0.0),
                jnp.where(half == 0, second, 0.0),
            )
            for array, out_ref in enumerate(out_refs):
                out_ref[0, :, own] = within_ref[peer, array * BLK : (array + 1) * BLK, :]
                kept = within_ref[peer, (3 + array) * BLK : (4 + array) * BLK, :]
                out_ref[0, :, other] = (kept.astype(jnp.float32) + added[array]).astype(
                    jnp.bfloat16
                )


def join_kernel(kept_ref, taken_ref, *out_refs):
    for step, out_ref in enumerate(out_refs):
        out_ref[0] = kept_ref[step]
        out_ref[1] = taken_ref[step]


def crossed(kept, given, half_count):
    devices = range(2 * half_count)
    steps, *shape = kept.shape
    taken = lax.ppermute(given, "seq", [(source, source ^ 1) for source in devices])
    messages = kernel_call(
        join_kernel,
        "join_chunks",
        (kept, taken),
        [pl.BlockSpec(memory_space=pltpu.VMEM)] * 2,
        [jax.ShapeDtypeStruct((2, *shape), jnp.bfloat16)] * steps,
        [],
        4,
    )
    return [
        lax.ppermute(
            message, "seq", [(source, source ^ (half_count + 2 * step)) for source in devices]
        )
        for step, message in enumerate(messages)
    ]


def head_shards(
    probe_vectors,
    lookup_vectors,
    content_vectors,
    result_cotangent,
    logit_softness,
    block_grouping,
    neighborhood_span,
):
    seq_count = lax.axis_size("seq")
    half_count = seq_count // 2
    tokens = half_count * BLK
    groups = [list(range(half_count)), list(range(half_count, seq_count))]
    settings = (logit_softness, block_grouping[0, :, :, 0], neighborhood_span)
    smem, vmem = pl.BlockSpec(memory_space=pltpu.SMEM), pl.BlockSpec(memory_space=pltpu.VMEM)
    lows = [pltpu.VMEM((tokens, tokens), jnp.bfloat16)] * 2 + [
        pltpu.VMEM((HD, tokens), jnp.bfloat16)
    ]
    rows_of_stats = jax.ShapeDtypeStruct((8, tokens), jnp.float32)
    pairs = jax.ShapeDtypeStruct((tokens, tokens), jnp.float32)
    pair_flops = 2 * tokens * tokens * HD

    def exchange_within(array_in):
        return lax.all_to_all(
            array_in, "seq", split_axis=0, concat_axis=0, axis_index_groups=groups, tiled=True
        )

    def call(kernel, name, operands, out_shape, scratch, flops, vmem_mib):
        return kernel_call(
            functools.partial(kernel, half_count=half_count),
            name,
            (*settings, *operands),
            [smem] * 3 + [vmem] * len(operands),
            out_shape,
            scratch,
            vmem_mib,
            flops,
        )

    sent, *foreign = packed(
        (probe_vectors, lookup_vectors, content_vectors, result_cotangent), half_count
    )
    arrived = exchange_within(sent)
    foreign = crossed(*foreign, half_count)
    kept_parts = jax.ShapeDtypeStruct((3, tokens, HD), jnp.float32)
    three_arrays = jax.ShapeDtypeStruct((half_count, 3 * BLK, HD), jnp.bfloat16)
    tempers = jax.ShapeDtypeStruct((8, HD), jnp.float32)
    first_half = range(half_count)
    (
        arrays, stats, message, parts, other_done, temper,
        own_weight, own_towards, other_weight, other_towards,
    ) = call(
        within_kernel,
        "diagonal_statistics",
        (arrived,),
        [jax.ShapeDtypeStruct((8, tokens, HD), jnp.bfloat16), rows_of_stats, rows_of_stats]
        + [kept_parts, three_arrays, tempers]
        + [pairs] * 4,
        lows,
        3 * pair_flops,
        20,
    )
    from_second = lax.ppermute(
        message, "seq", [(source + half_count, source) for source in first_half]
    )
    square, square_stats, square_weight, square_towards = call(
        square_kernel,
        "square_statistics",
        (arrays, stats, *foreign),
        [jax.ShapeDtypeStruct((4, tokens, HD), jnp.bfloat16), rows_of_stats] + [pairs] * 2,
        [],
        2 * pair_flops,
        12,
    )
    from_first = lax.ppermute(
        square_stats, "seq", [(source, source + half_count) for source in first_half]
    )
    own_done, across, temper = call(
        own_kernel,
        "own_gradients",
        (
            arrays, square, stats, square_stats, from_second, parts, temper,
            own_weight, own_towards, square_weight, square_towards,
        ),
        [three_arrays, jax.ShapeDtypeStruct((2, tokens, HD), jnp.bfloat16), tempers],
        lows,
        4 * pair_flops,
        14,
    )
    within, *foreign, temper = call(
        finish_kernel,
        "other_gradients",
        (
            arrays, stats, from_first, own_done, other_done, temper,
            other_weight, other_towards, across,
        ),
        [jax.ShapeDtypeStruct((half_count, 6 * BLK, HD), jnp.bfloat16)]
        + [jax.ShapeDtypeStruct((half_count // 2, 2 * BLK, HD), jnp.bfloat16)] * 2
        + [jax.ShapeDtypeStruct((1, HD), jnp.float32)],
        [pltpu.VMEM((8, HD), jnp.float32), *lows],
        pair_flops,
        16,
    )
    tempers = lax.all_gather(temper, ("dp", "seq"), tiled=True)
    across = crossed(*foreign, half_count)
    within = exchange_within(within)
    *outs, temper = kernel_call(
        functools.partial(unpack_kernel, half_count=half_count),
        "unpack_heads",
        (tempers, within, *across),
        [vmem] * (2 + len(across)),
        [jax.ShapeDtypeStruct(probe_vectors.shape, jnp.bfloat16)] * 3
        + [jax.ShapeDtypeStruct((1, seq_count), jnp.float32)],
        [],
        10,
    )
    return (*outs, temper.reshape(seq_count))


def shards(
    probe_vectors,
    lookup_vectors,
    content_vectors,
    result_cotangent,
    logit_softness,
    block_grouping,
    neighborhood_span,
):
    head_count = probe_vectors.shape[2] // HD
    seq_count = lax.axis_size("seq")
    one_block = probe_vectors.shape[1] == BLK
    whole_tiles = seq_count * BLK % (2 * TILE) == 0 and seq_count & (seq_count - 1) == 0
    if head_count == seq_count and one_block and whole_tiles:
        plan = head_shards
    else:
        plan = clustered_shards
    return plan(
        probe_vectors,
        lookup_vectors,
        content_vectors,
        result_cotangent,
        logit_softness,
        block_grouping,
        neighborhood_span,
    )


def solution(mesh):
    in_specs = (
        P("dp", "seq", None),
        P("dp", "seq", None),
        P("dp", "seq", None),
        P("dp", "seq", None),
        P(),
        P("dp", None, None, None),
        P(),
    )
    out_specs = (P("dp", "seq", None), P("dp", "seq", None), P("dp", "seq", None), P())
    return jax.shard_map(shards, mesh=mesh, in_specs=in_specs, out_specs=out_specs, check_vma=False)
```

```python
import functools
import math

import jax
import jax.numpy as jnp
from jax import lax
from jax.experimental import pallas as pl
from jax.experimental.pallas import tpu as pltpu
from jax.sharding import PartitionSpec as P

HD = 128
BLK = 128


blocked_score = -1e30


def shifted(value, axis, steps):
    count = lax.axis_size(axis)
    first, last = (max(0, -steps), min(count, count - steps))
    return lax.ppermute(value, axis, [(source, source + steps) for source in range(first, last)])


def lifted(array_in):
    return lax.optimization_barrier(array_in.astype(jnp.bfloat16)).astype(jnp.float32)


def head_major(tokens_in, block_len):
    token_count, feature_count = tokens_in.shape
    return tokens_in.reshape(
        token_count // block_len, block_len, feature_count // HD, HD
    ).transpose(2, 0, 1, 3)


def token_major(blocks_in):
    head_count, block_count, block_len, depth = blocks_in.shape
    return blocks_in.transpose(1, 2, 0, 3).reshape(1, block_count * block_len, head_count * depth)


def window_parts(query_block, prev_keys, prev_values, grad_block, usable, window_width, temper):
    block_len = query_block.shape[-2]
    inverse_root = 1.0 / math.sqrt(query_block.shape[-1])
    raw_scores = (
        jnp.einsum("...td,...sd->...ts", query_block, prev_keys, preferred_element_type=jnp.float32)
        * inverse_root
    )
    query_pos = lax.broadcasted_iota(jnp.int32, (block_len, block_len), 0)
    key_pos = lax.broadcasted_iota(jnp.int32, (block_len, block_len), 1)
    pair_mask = usable[..., None, None] & (
        key_pos > query_pos + block_len - window_width[..., None, None]
    )
    scores = temper[..., None, None] * raw_scores
    row_top = jnp.max(jnp.where(pair_mask, scores, blocked_score), axis=-1)
    weights = jnp.where(pair_mask, jnp.exp(scores - row_top[..., None]), 0.0)
    prob_grad = jnp.einsum(
        "...td,...sd->...ts", grad_block, prev_values, preferred_element_type=jnp.float32
    )
    return (
        raw_scores,
        pair_mask,
        prob_grad,
        row_top,
        jnp.sum(weights, axis=-1),
        jnp.sum(weights * prob_grad, axis=-1),
    )


def window_grads(
    raw_scores,
    pair_mask,
    prob_grad,
    query_block,
    prev_keys,
    grad_block,
    log_total,
    row_delta,
    temper,
):
    inverse_root = 1.0 / math.sqrt(query_block.shape[-1])
    scaling = (temper * inverse_root)[..., None, None]
    probability = jnp.where(
        pair_mask, jnp.exp(temper[..., None, None] * raw_scores - log_total[..., None]), 0.0
    )
    score_grad = probability * (prob_grad - row_delta[..., None])
    prob_low = probability.astype(jnp.bfloat16)
    grad_low = score_grad.astype(jnp.bfloat16)
    query_part = (
        jnp.einsum("...ts,...sd->...td", grad_low, prev_keys, preferred_element_type=jnp.float32)
        * scaling
    )
    key_part = (
        jnp.einsum("...ts,...td->...sd", grad_low, query_block, preferred_element_type=jnp.float32)
        * scaling
    )
    value_part = jnp.einsum(
        "...ts,...td->...sd", prob_low, grad_block, preferred_element_type=jnp.float32
    )
    temper_part = jnp.sum(score_grad * raw_scores, axis=(-2, -1))
    return (query_part, key_part, value_part, temper_part)


def cluster_pair(
    query_items,
    key_items,
    value_items,
    grad_items,
    live_items,
    temper,
    window_top,
    window_total,
    window_mass,
):
    item_count, block_len, depth = query_items.shape
    row_count = item_count * block_len
    group_rows = 4 * block_len
    inverse_root = 1.0 / math.sqrt(depth)
    scaling = temper * inverse_root
    query_rows = query_items.reshape(row_count, depth)
    key_rows = key_items.reshape(row_count, depth)
    value_rows = value_items.reshape(row_count, depth)
    grad_rows = grad_items.reshape(row_count, depth)
    key_item = jnp.arange(row_count) // block_len
    key_token = jnp.arange(row_count) % block_len
    live_rows = jnp.repeat(live_items, block_len)
    top_rows = window_top.reshape(row_count)
    total_rows = window_total.reshape(row_count)
    mass_rows = window_mass.reshape(row_count)

    def group_step(carry, start_row):
        key_acc, value_acc, temper_acc = carry
        query_group = lax.dynamic_slice_in_dim(query_rows, start_row, group_rows, 0)
        grad_group = lax.dynamic_slice_in_dim(grad_rows, start_row, group_rows, 0)
        group_live = lax.dynamic_slice_in_dim(live_rows, start_row, group_rows, 0)
        group_top = lax.dynamic_slice_in_dim(top_rows, start_row, group_rows, 0)
        group_total = lax.dynamic_slice_in_dim(total_rows, start_row, group_rows, 0)
        group_mass = lax.dynamic_slice_in_dim(mass_rows, start_row, group_rows, 0)
        query_item = (start_row + jnp.arange(group_rows)) // block_len
        query_token = jnp.arange(group_rows) % block_len
        earlier = (key_item[None, :] < query_item[:, None]) | (
            key_item[None, :] == query_item[:, None]
        ) & (key_token[None, :] <= query_token[:, None])
        pair_mask = group_live[:, None] & live_rows[None, :] & earlier
        raw_scores = (
            lax.dot_general(
                query_group, key_rows, (((1,), (1,)), ((), ())), preferred_element_type=jnp.float32
            )
            * inverse_root
        )
        scores = temper * raw_scores
        row_top = jnp.maximum(
            jnp.max(jnp.where(pair_mask, scores, blocked_score), axis=1), group_top
        )
        weights = jnp.where(pair_mask, jnp.exp(scores - row_top[:, None]), 0.0)
        row_total = jnp.sum(weights, axis=1) + group_total * jnp.exp(group_top - row_top)
        log_total = row_top + jnp.log(jnp.where(group_live, row_total, 1.0))
        probability = jnp.where(pair_mask, jnp.exp(scores - log_total[:, None]), 0.0)
        prob_grad = lax.dot_general(
            grad_group, value_rows, (((1,), (1,)), ((), ())), preferred_element_type=jnp.float32
        )
        row_delta = jnp.sum(probability * prob_grad, axis=1) + group_mass * jnp.exp(
            group_top - log_total
        )
        score_grad = probability * (prob_grad - row_delta[:, None])
        prob_low = probability.astype(jnp.bfloat16)
        grad_low = score_grad.astype(jnp.bfloat16)
        query_part = jnp.dot(grad_low, key_rows, preferred_element_type=jnp.float32) * scaling
        key_acc = (
            key_acc
            + lax.dot_general(
                grad_low, query_group, (((0,), (0,)), ((), ())), preferred_element_type=jnp.float32
            )
            * scaling
        )
        value_acc = value_acc + lax.dot_general(
            prob_low, grad_group, (((0,), (0,)), ((), ())), preferred_element_type=jnp.float32
        )
        temper_acc = temper_acc + jnp.sum(score_grad * raw_scores)
        return ((key_acc, value_acc, temper_acc), (query_part, log_total, row_delta))

    start_rows = jnp.arange(item_count // 4) * group_rows
    initial = (
        jnp.zeros((row_count, depth), jnp.float32),
        jnp.zeros((row_count, depth), jnp.float32),
        jnp.zeros((), jnp.float32),
    )
    (key_acc, value_acc, temper_acc), (query_part, log_total, row_delta) = lax.scan(
        group_step, initial, start_rows
    )
    return (
        query_part.reshape(item_count, block_len, depth),
        log_total.reshape(item_count, block_len),
        row_delta.reshape(item_count, block_len),
        key_acc.reshape(item_count, block_len, depth),
        value_acc.reshape(item_count, block_len, depth),
        temper_acc,
    )


def clustered_shards(
    probe_vectors,
    lookup_vectors,
    content_vectors,
    result_cotangent,
    logit_softness,
    block_grouping,
    neighborhood_span,
):
    seq_count = lax.axis_size("seq")
    position = lax.axis_index("seq")
    tokens = probe_vectors.shape[1]
    head_count = probe_vectors.shape[2] // HD
    local_blocks = tokens // BLK
    block_count = local_blocks * seq_count
    cluster_count = max(1, block_count // 8)
    capacity = min(12, block_count)
    owned_pairs = cluster_count * head_count // seq_count
    group_count = cluster_count // owned_pairs
    per_peer = max(1, local_blocks // group_count)
    cluster_ids = block_grouping[0, :, :, 0]
    query_home = head_major(probe_vectors[0], BLK)
    key_home = head_major(lookup_vectors[0], BLK)
    value_home = head_major(content_vectors[0], BLK)
    grad_home = head_major(result_cotangent[0], BLK)
    last_block = (lookup_vectors[0, tokens - BLK :], content_vectors[0, tokens - BLK :])
    prev_key_rows, prev_value_rows = shifted((last_block[0], last_block[1]), "seq", 1)
    prev_keys = jnp.concatenate([head_major(prev_key_rows, BLK), key_home[:, :-1]], axis=1)
    prev_values = jnp.concatenate([head_major(prev_value_rows, BLK), value_home[:, :-1]], axis=1)
    first_block = position * local_blocks
    before = jnp.concatenate(
        [jnp.full((head_count, 1), -1, jnp.int32), cluster_ids[:, :-1]], axis=1
    )
    my_ids = lax.dynamic_slice_in_dim(cluster_ids, first_block, local_blocks, 1)
    my_before = lax.dynamic_slice_in_dim(before, first_block, local_blocks, 1)
    global_block = first_block + jnp.arange(local_blocks)
    usable_home = (global_block[None, :] >= 1) & (my_before != my_ids)
    peer_index = jnp.arange(seq_count)
    peer_head = peer_index * owned_pairs // cluster_count
    slot_range = jnp.arange(per_peer)
    local_range = jnp.arange(local_blocks)
    owner_index = (jnp.arange(head_count)[:, None] * cluster_count + my_ids) // owned_pairs
    peer_ids = jnp.take(my_ids, peer_head, axis=0)
    goes = (peer_head[:, None] * cluster_count + peer_ids) // owned_pairs == peer_index[:, None]
    send_rank = jnp.cumsum(goes.astype(jnp.int32), axis=1) - 1
    send_pick = goes[:, None, :] & (send_rank[:, None, :] == slot_range[None, :, None])
    send_block = jnp.sum(jnp.where(send_pick, local_range[None, None, :], 0), axis=2)
    send_flat = peer_head[:, None] * local_blocks + send_block
    home_rank = jnp.take_along_axis(send_rank, owner_index, axis=0)
    home_pos = owner_index * per_peer + home_rank
    pair_index = position * owned_pairs + jnp.arange(owned_pairs)
    split_for_couple = pair_index // cluster_count
    pair_cluster = pair_index % cluster_count
    my_head = position * owned_pairs // cluster_count
    split_numbers = jnp.take(cluster_ids, my_head, axis=0)
    member = split_numbers[None, :] == pair_cluster[:, None]
    member_rank = jnp.cumsum(member.astype(jnp.int32), axis=1) - 1
    member_count = jnp.sum(member.astype(jnp.int32), axis=1)
    picked = member[:, None, :] & (member_rank[:, None, :] == jnp.arange(capacity)[None, :, None])
    member_block = jnp.sum(jnp.where(picked, jnp.arange(block_count)[None, None, :], 0), axis=2)
    live_members = jnp.arange(capacity)[None, :] < member_count[:, None]
    mine = (my_head * cluster_count + split_numbers) // owned_pairs == position
    mine_grid = mine.reshape(seq_count, local_blocks)
    recv_rank = jnp.cumsum(mine_grid.astype(jnp.int32), axis=1) - 1
    recv_pos = (peer_index[:, None] * per_peer + recv_rank).reshape(block_count)
    member_pos = jnp.take(recv_pos, member_block)
    couple_softness = jnp.take(logit_softness, split_for_couple)
    pair_onehot = (split_for_couple[:, None] == jnp.arange(head_count)[None, :]).astype(jnp.float32)
    slot_pair = my_head * cluster_count + split_numbers - position * owned_pairs
    same_cluster = split_numbers[:, None] == split_numbers[None, :]
    earlier_block = jnp.arange(block_count)[None, :] < jnp.arange(block_count)[:, None]
    slot_rank = jnp.sum((same_cluster & earlier_block).astype(jnp.int32), axis=1)
    back_pos = jnp.clip(slot_pair, 0, owned_pairs - 1) * capacity + jnp.clip(
        slot_rank, 0, capacity - 1
    )
    back_grid = back_pos.reshape(seq_count, local_blocks)
    back_pick = mine_grid[:, None, :] & (recv_rank[:, None, :] == slot_range[None, :, None])
    back_flat = jnp.sum(jnp.where(back_pick, back_grid[:, None, :], 0), axis=2)

    def to_peers(array_in):
        flat = array_in.reshape((head_count * local_blocks,) + array_in.shape[2:])
        return jnp.take(flat, send_flat, axis=0)

    def members(array_in):
        flat = array_in.reshape((seq_count * per_peer,) + array_in.shape[2:])
        return jnp.take(flat, member_pos, axis=0)

    def to_owner(array_in):
        flat = array_in.reshape((owned_pairs * capacity,) + array_in.shape[2:])
        return jnp.take(flat, back_flat, axis=0)

    def from_peers(array_in):
        flat = array_in.reshape((seq_count * per_peer,) + array_in.shape[2:])
        return jnp.take(flat, home_pos, axis=0)

    raw_w, mask_w, pgrad_w, top_w, total_w, mass_w = window_parts(
        query_home,
        prev_keys,
        prev_values,
        grad_home,
        usable_home,
        neighborhood_span[:, None],
        logit_softness[:, None],
    )
    arrived = (
        lax.all_to_all(to_peers(query_home), "seq", split_axis=0, concat_axis=0, tiled=True),
        lax.all_to_all(to_peers(key_home), "seq", split_axis=0, concat_axis=0, tiled=True),
        lax.all_to_all(to_peers(value_home), "seq", split_axis=0, concat_axis=0, tiled=True),
        lax.all_to_all(to_peers(grad_home), "seq", split_axis=0, concat_axis=0, tiled=True),
    )
    arrived_stats = (
        lax.all_to_all(to_peers(top_w), "seq", split_axis=0, concat_axis=0, tiled=True),
        lax.all_to_all(to_peers(total_w), "seq", split_axis=0, concat_axis=0, tiled=True),
        lax.all_to_all(to_peers(mass_w), "seq", split_axis=0, concat_axis=0, tiled=True),
    )
    query_m, key_m, value_m, grad_m = [members(item_in) for item_in in arrived]
    top_m, total_m, mass_m = [members(item_in) for item_in in arrived_stats]

    def split_pair(pair_inputs):
        query_i, key_i, value_i, grad_i, live_i, temper_i, top_i, total_i, mass_i = pair_inputs
        query_c, log_total, row_delta, key_c, value_c, temper_c = cluster_pair(
            query_i, key_i, value_i, grad_i, live_i, temper_i, top_i, total_i, mass_i
        )
        return (
            query_c.astype(jnp.bfloat16),
            key_c.astype(jnp.bfloat16),
            value_c.astype(jnp.bfloat16),
            log_total,
            row_delta,
            temper_c,
        )

    owner_results = lax.map(
        split_pair,
        (query_m, key_m, value_m, grad_m, live_members, couple_softness, top_m, total_m, mass_m),
    )
    returned = (
        lax.all_to_all(to_owner(owner_results[0]), "seq", split_axis=0, concat_axis=0, tiled=True),
        lax.all_to_all(to_owner(owner_results[1]), "seq", split_axis=0, concat_axis=0, tiled=True),
        lax.all_to_all(to_owner(owner_results[2]), "seq", split_axis=0, concat_axis=0, tiled=True),
    )
    returned_stats = (
        lax.all_to_all(to_owner(owner_results[3]), "seq", split_axis=0, concat_axis=0, tiled=True),
        lax.all_to_all(to_owner(owner_results[4]), "seq", split_axis=0, concat_axis=0, tiled=True),
    )
    query_cluster = from_peers(returned[0])
    key_cluster = from_peers(returned[1])
    value_cluster = from_peers(returned[2])
    log_home = from_peers(returned_stats[0])
    delta_home = from_peers(returned_stats[1])
    query_w, key_w, value_w, temper_w = window_grads(
        raw_w,
        mask_w,
        pgrad_w,
        query_home,
        prev_keys,
        grad_home,
        log_home,
        delta_home,
        logit_softness[:, None],
    )
    query_out = (query_cluster.astype(jnp.float32) + lifted(query_w)).astype(jnp.bfloat16)
    key_window = key_w.astype(jnp.bfloat16)
    value_window = value_w.astype(jnp.bfloat16)
    temper_local = jnp.sum(owner_results[5][:, None] * pair_onehot, axis=0) + jnp.sum(
        temper_w, axis=1
    )
    edge_keys, edge_values = shifted((key_window[:, 0], value_window[:, 0]), "seq", -1)
    key_next = jnp.concatenate([key_window[:, 1:], edge_keys[:, None]], axis=1)
    value_next = jnp.concatenate([value_window[:, 1:], edge_values[:, None]], axis=1)
    key_out = (key_cluster.astype(jnp.float32) + key_next.astype(jnp.float32)).astype(jnp.bfloat16)
    value_out = (value_cluster.astype(jnp.float32) + value_next.astype(jnp.float32)).astype(
        jnp.bfloat16
    )
    temper_total = lax.psum(temper_local, ("seq", "dp"))
    temper_grad = temper_total / (lax.axis_size("dp") * tokens * seq_count)
    return (token_major(query_out), token_major(key_out), token_major(value_out), temper_grad)


TILE = 256
EXTRA = 16
MIB = 1024 * 1024
PIECES = 4
QUERY, KEY, VALUE, GRAD = range(4)


def columns_of(index):
    return pl.ds(pl.multiple_of(index * HD, HD), HD)


def rows_of(index):
    return pl.ds(pl.multiple_of(index * BLK, BLK), BLK)


def tile_rows(tile):
    return slice(tile * TILE, (tile + 1) * TILE)


def position(half_count):
    me = lax.axis_index("seq")
    half = jnp.where(me >= half_count, 1, 0)
    return me, half, me - half * half_count


def kernel_call(
    kernel, name, operands, in_specs, out_shape, scratch, vmem_mib, flops=0, out_space=pltpu.VMEM
):
    bytes_accessed = sum(
        math.prod(item.shape) * item.dtype.itemsize for item in (*operands, *out_shape)
    )
    return pl.pallas_call(
        kernel,
        out_shape=out_shape,
        in_specs=in_specs,
        out_specs=[pl.BlockSpec(memory_space=out_space)] * len(out_shape),
        scratch_shapes=scratch,
        cost_estimate=pl.CostEstimate(
            flops=flops, bytes_accessed=bytes_accessed, transcendentals=0
        ),
        compiler_params=pltpu.CompilerParams(vmem_limit_bytes=vmem_mib * MIB),
        name=name,
    )(*operands)


def pack_kernel(*refs, half_count):
    arrays, within_ref, foreign_refs = refs[:4], refs[4], refs[5:7]
    held, within, across, arrival, left_within, left_across = refs[7:]
    me, half, _ = position(half_count)
    piece = BLK // PIECES
    arrivals = [
        [
            pltpu.make_async_copy(
                array_ref.at[0, part * piece : (part + 1) * piece, :],
                held.at[place, part * piece : (part + 1) * piece, :],
                arrival.at[place, part],
            )
            for part in range(PIECES)
        ]
        for place, array_ref in enumerate(arrays)
    ]
    for copies in arrivals:
        for copy in copies:
            copy.start()
    leaving = []
    for place, copies in enumerate(arrivals):
        for copy in copies:
            copy.wait()
        for slot, base in enumerate((half * half_count, (1 - half) * half_count)):
            rows = slice((slot * 4 + place) * BLK, (slot * 4 + place + 1) * BLK)
            for peer in range(half_count):
                within[peer, rows, :] = held[place, :, columns_of(base + peer)]
            leaving.append(
                pltpu.make_async_copy(
                    within.at[:, rows, :], within_ref.at[:, rows, :], left_within.at[place, slot]
                )
            )
            leaving[-1].start()
    first = jnp.where(half == 0, KEY, QUERY)
    second = jnp.where(half == 0, VALUE, GRAD)
    for core, foreign_ref in enumerate(foreign_refs):
        for step in range(half_count // 2):
            columns = columns_of(me ^ core ^ (half_count + 2 * step))
            across[core, step, :BLK, :] = held[first, :, columns]
            across[core, step, BLK:, :] = held[second, :, columns]
        leaving.append(pltpu.make_async_copy(across.at[core], foreign_ref, left_across.at[core]))
        leaving[-1].start()
    for copy in leaving:
        copy.wait()


def packed(arrays, half_count):
    width = arrays[0].shape[2]
    within_shape, across_shape = (half_count, 8 * BLK, HD), (half_count // 2, 2 * BLK, HD)
    return kernel_call(
        functools.partial(pack_kernel, half_count=half_count),
        "pack_heads",
        arrays,
        [pl.BlockSpec(memory_space=pl.ANY)] * 4,
        [jax.ShapeDtypeStruct(within_shape, jnp.bfloat16)]
        + [jax.ShapeDtypeStruct(across_shape, jnp.bfloat16)] * 2,
        [
            pltpu.VMEM((4, BLK, width), jnp.bfloat16),
            pltpu.VMEM(within_shape, jnp.bfloat16),
            pltpu.VMEM((2, *across_shape), jnp.bfloat16),
            pltpu.SemaphoreType.DMA((4, PIECES)),
            pltpu.SemaphoreType.DMA((4, 2)),
            pltpu.SemaphoreType.DMA((2,)),
        ],
        60,
        out_space=pl.ANY,
    )


def dot_rows(left, right):
    return lax.dot_general(
        left, right, (((1,), (1,)), ((), ())), preferred_element_type=jnp.float32
    )


def dot_plain(left, right):
    return lax.dot_general(
        left, right, (((1,), (0,)), ((), ())), preferred_element_type=jnp.float32
    )


class Region:
    def __init__(self, square, arrays, places, scaling):
        self.square, self.arrays, self.places, self.scaling = square, arrays, places, scaling
        self.tiles = arrays.shape[1] // TILE

    def rows(self, which, start, stop):
        return self.arrays[self.places[which], start * TILE : stop * TILE, :]

    def keys_of(self, tile):
        return range(self.tiles if self.square else tile + 1)

    def products(self, tile_key, tile_query):
        return dot_rows(
            self.rows(KEY, tile_key, tile_key + 1), self.rows(QUERY, tile_query, tile_query + 1)
        ) * (self.scaling * math.log2(math.e))


class Diagonal(Region):
    def __init__(self, arrays, places, scaling, ids_ref=None, head=None, base=None, width=None):
        super().__init__(False, arrays, places, scaling)
        self.ids_ref, self.head, self.base, self.width = ids_ref, head, base, width

    def same(self, key_block, query_block):
        ids_ref, head, base = self.ids_ref, self.head, self.base
        return ids_ref[head, base + key_block] == ids_ref[head, base + query_block]

    def scores(self, tile_key, tile_query):
        per_tile = TILE // BLK
        scores = self.products(tile_key, tile_query)
        spread = key_minus_query()
        rows = []
        for sub_key in range(per_tile):
            pieces = []
            for sub_query in range(per_tile):
                piece = scores[
                    sub_key * BLK : (sub_key + 1) * BLK, sub_query * BLK : (sub_query + 1) * BLK
                ]
                key_block = tile_key * per_tile + sub_key
                query_block = tile_query * per_tile + sub_query
                if key_block > query_block:
                    piece = jnp.full_like(piece, blocked_score)
                elif key_block == query_block:
                    piece = jnp.where(spread <= 0, piece, blocked_score)
                elif key_block == query_block - 1:
                    least = jnp.where(self.same(key_block, query_block), -BLK, BLK - self.width)
                    piece = jnp.where(spread > least, piece, blocked_score)
                else:
                    piece = piece + jnp.where(
                        self.same(key_block, query_block), 0.0, blocked_score
                    )
                pieces.append(piece)
            rows.append(jnp.concatenate(pieces, axis=1))
        return jnp.concatenate(rows, axis=0)


class Square(Region):
    def __init__(self, arrays, scaling, bias_ref=None, corner_ref=None):
        super().__init__(True, arrays, range(4), scaling)
        self.bias_ref, self.corner_ref = bias_ref, corner_ref

    def scores(self, tile_key, tile_query):
        per_tile = TILE // BLK
        scores = self.products(tile_key, tile_query)
        rows = []
        for sub_key in range(per_tile):
            block = tile_key * per_tile + sub_key
            row = scores[sub_key * BLK : (sub_key + 1) * BLK, :]
            bias = self.bias_ref[block : block + 1, tile_rows(tile_query)]
            if block == self.tiles * per_tile - 1 and tile_query == 0:
                rows.append(
                    jnp.concatenate(
                        [row[:, :BLK] + self.corner_ref[...], row[:, BLK:] + bias[:, BLK:]], axis=1
                    )
                )
            else:
                rows.append(row + bias)
        return jnp.concatenate(rows, axis=0)


def key_minus_query():
    shape = (BLK, BLK)
    return lax.broadcasted_iota(jnp.int32, shape, 0) - lax.broadcasted_iota(jnp.int32, shape, 1)


def statistics(region, weight_ref, towards_ref, out_ref, first_row):
    for tile in range(region.tiles):
        here = tile_rows(tile)
        top = jnp.full((1, TILE), blocked_score, jnp.float32)
        for other in region.keys_of(tile):
            raw = region.scores(other, tile)
            weight_ref[tile_rows(other), here] = raw
            top = jnp.maximum(top, jnp.max(raw, axis=0, keepdims=True))
        total = jnp.zeros((1, TILE), jnp.float32)
        mass = jnp.zeros((1, TILE), jnp.float32)
        for other in region.keys_of(tile):
            there = tile_rows(other)
            weight = jnp.exp2(weight_ref[there, here] - top)
            towards = dot_rows(
                region.rows(VALUE, other, other + 1), region.rows(GRAD, tile, tile + 1)
            )
            weight_ref[there, here] = weight
            towards_ref[there, here] = towards
            total += jnp.sum(weight, axis=0, keepdims=True)
            mass += jnp.sum(weight * towards, axis=0, keepdims=True)
        out_ref[first_row : first_row + 1, here] = top
        out_ref[first_row + 1 : first_row + 2, here] = total
        out_ref[first_row + 2 : first_row + 3, here] = mass


def gradients(
    region, weight_ref, towards_ref, top, log_total, delta, prob_low, grad_low, keys_flat
):
    keys_flat[...] = region.rows(KEY, 0, region.tiles).T
    share = jnp.exp2(top - log_total)
    temper = jnp.zeros((1, HD), jnp.float32)
    query_parts, key_parts, value_parts = [], [], []
    for tile in range(region.tiles):
        here = tile_rows(tile)
        for other in region.keys_of(tile):
            there = tile_rows(other)
            probability = weight_ref[there, here] * share[:, here]
            prob_low[there, here] = probability.astype(jnp.bfloat16)
            grad_low[there, here] = (
                probability * (towards_ref[there, here] - delta[:, here])
            ).astype(jnp.bfloat16)
        upto = slice(0, len(region.keys_of(tile)) * TILE)
        query_part = dot_plain(keys_flat[:, upto], grad_low[upto, here]).T
        temper += jnp.sum(
            query_part * region.rows(QUERY, tile, tile + 1).astype(jnp.float32),
            axis=0,
            keepdims=True,
        )
        query_parts.append(query_part)
    for tile in range(region.tiles):
        first = 0 if region.square else tile
        onward = slice(first * TILE, region.tiles * TILE)
        here = tile_rows(tile)
        key_parts.append(
            dot_plain(grad_low[here, onward], region.rows(QUERY, first, region.tiles))
        )
        value_parts.append(
            dot_plain(prob_low[here, onward], region.rows(GRAD, first, region.tiles))
        )
    return query_parts, key_parts, value_parts, temper


def merged(first, second):
    top = jnp.maximum(first[0], second[0])
    left, right = jnp.exp2(first[0] - top), jnp.exp2(second[0] - top)
    total = first[1] * left + second[1] * right
    mass = first[2] * left + second[2] * right
    return top + jnp.log2(total), mass / total


def alone(rows):
    return rows[0] + jnp.log2(rows[1]), rows[2] / rows[1]


def three_rows(ref, first):
    return [ref[first + row : first + row + 1, :] for row in range(3)]


def put(within_ref, array, tile, value):
    per_tile = TILE // BLK
    for sub in range(per_tile):
        within_ref[tile * per_tile + sub, array * BLK : (array + 1) * BLK, :] = value[
            sub * BLK : (sub + 1) * BLK, :
        ].astype(jnp.bfloat16)


def scale_row(stats_ref, slot):
    return stats_ref[6 + slot : 7 + slot, :HD]


def scaled(region, parts):
    return [
        [value * scale for value in part]
        for part, scale in zip(parts, (region.scaling, region.scaling, 1.0))
    ]


def within_kernel(
    softness_ref, ids_ref, span_ref, in_ref, arrays_ref, stats_ref, bias_ref, corner_ref,
    parts_ref, temper_ref, own_weight, own_towards, other_weight, other_towards, *scratch,
    half_count
):
    me, half, _ = position(half_count)
    for block in range(half_count):
        for place in range(8):
            arrays_ref[place, block * BLK : (block + 1) * BLK, :] = in_ref[
                block, place * BLK : (place + 1) * BLK, :
            ]
    kept = ((own_weight, own_towards), (other_weight, other_towards))
    for slot in range(2):
        head = me ^ (slot * half_count)
        scaling = softness_ref[head] * (1.0 / math.sqrt(HD))
        places = [slot * 4 + place for place in range(4)]
        region = Diagonal(
            arrays_ref, places, scaling, ids_ref, head, half * half_count, span_ref[head]
        )
        statistics(region, *kept[slot], stats_ref, slot * 3)
        stats_ref[6 + slot : 7 + slot, :] = jnp.full((1, stats_ref.shape[1]), scaling, jnp.float32)
    for key_block in range(half_count):
        for query_block in range(half_count):
            same = ids_ref[me, key_block] == ids_ref[me, half_count + query_block]
            bias_ref[key_block : key_block + 1, query_block * BLK : (query_block + 1) * BLK] = (
                jnp.full((1, BLK), jnp.where(same, 0.0, blocked_score), jnp.float32)
            )
    same = ids_ref[me, half_count - 1] == ids_ref[me, half_count]
    least = jnp.where(same, -BLK, BLK - span_ref[me])
    corner_ref[...] = jnp.where(key_minus_query() > least, 0.0, blocked_score)
    temper_ref[...] = jnp.zeros_like(temper_ref)

    @pl.when(half == 0)
    def _():
        region = Diagonal(arrays_ref, range(4), scale_row(stats_ref, 0))
        single = alone(three_rows(stats_ref, 0))
        *parts, temper = gradients(region, *kept[0], stats_ref[0:1, :], *single, *scratch)
        for place, tiles in enumerate(scaled(region, parts)):
            for tile, value in enumerate(tiles):
                parts_ref[place, tile_rows(tile), :] = value
        temper_ref[0:1, :] = temper


def square_kernel(arrays_ref, stats_ref, bias_ref, corner_ref, *refs, half_count):
    across_refs = refs[: half_count // 2]
    square_ref, message_ref, square_stats, weight, towards = refs[half_count // 2 :]
    _, half, place = position(half_count)
    first = jnp.where(half == 0, QUERY, KEY)
    second = jnp.where(half == 0, GRAD, VALUE)
    for step, across_ref in enumerate(across_refs):
        for core in range(2):
            rows = rows_of(place ^ core ^ (2 * step))
            square_ref[first, rows, :] = across_ref[core, :BLK, :]
            square_ref[second, rows, :] = across_ref[core, BLK:, :]
    kept_first = jnp.where(half == 0, KEY, QUERY)
    kept_second = jnp.where(half == 0, VALUE, GRAD)
    square_ref[kept_first, :, :] = arrays_ref[kept_first, :, :]
    square_ref[kept_second, :, :] = arrays_ref[kept_second, :, :]
    region = Square(square_ref, stats_ref[6:7, :TILE], bias_ref, corner_ref)
    statistics(region, weight, towards, square_stats, 0)
    for row in range(3):
        message_ref[row : row + 1, :] = jnp.where(
            half == 0, square_stats[row : row + 1, :], stats_ref[3 + row : 4 + row, :]
        )


def other_diagonal(arrays_ref, kept, stats_ref, totals, scratch, within_ref):
    region = Diagonal(arrays_ref, range(4, 8), scale_row(stats_ref, 1))
    *parts, temper = gradients(region, *kept, stats_ref[3:4, :], *totals, *scratch)
    for array, tiles in enumerate(scaled(region, parts)):
        for tile, value in enumerate(tiles):
            put(within_ref, 3 + array, tile, value)
    return temper


def first_kernel(
    arrays_ref, square_ref, stats_ref, square_stats, temper_in,
    own_weight, own_towards, other_weight, other_towards, square_weight, square_towards,
    within_ref, across_ref, temper_ref, *scratch, half_count
):
    _, half, _ = position(half_count)
    temper_ref[...] = temper_in[...]

    @pl.when(half == 0)
    def _():
        totals = alone(three_rows(stats_ref, 3))
        temper_ref[1:2, :] = other_diagonal(
            arrays_ref, (other_weight, other_towards), stats_ref, totals, scratch, within_ref
        )

    @pl.when(half == 1)
    def _():
        totals = merged(three_rows(stats_ref, 0), three_rows(square_stats, 0))
        square = Square(square_ref, scale_row(stats_ref, 0))
        *parts, square_temper = gradients(
            square, square_weight, square_towards, square_stats[0:1, :], *totals, *scratch
        )
        across_query, *foreign = scaled(square, parts)
        for array, tiles in enumerate(foreign):
            for tile, value in enumerate(tiles):
                across_ref[array, tile_rows(tile), :] = value.astype(jnp.bfloat16)
        diagonal = Diagonal(arrays_ref, range(4), scale_row(stats_ref, 0))
        *parts, temper = gradients(
            diagonal, own_weight, own_towards, stats_ref[0:1, :], *totals, *scratch
        )
        query_parts, key_parts, value_parts = scaled(diagonal, parts)
        for tile in range(square.tiles):
            put(within_ref, 0, tile, query_parts[tile] + across_query[tile])
            put(within_ref, 1, tile, key_parts[tile])
            put(within_ref, 2, tile, value_parts[tile])
        temper_ref[0:1, :] = temper + square_temper


def temper_rows(own, other):
    row = lax.broadcasted_iota(jnp.int32, (EXTRA, HD), 0)
    rows = jnp.zeros((EXTRA, HD), jnp.float32)
    for place, terms in enumerate((own, other)):
        rest = jnp.broadcast_to(jnp.sum(terms, axis=1, keepdims=True), (EXTRA, HD)) * (
            1.0 / math.sqrt(HD)
        )
        for piece in range(3):
            high = rest.astype(jnp.bfloat16).astype(jnp.float32)
            rows = jnp.where(row == place * 3 + piece, high, rows)
            rest = rest - high
    return rows.astype(jnp.bfloat16)


def finish_kernel(
    arrays_ref, square_ref, message_ref, received_ref, stats_ref, square_stats, parts_ref,
    temper_ref, square_weight, square_towards, other_weight, other_towards, across_in, begun_ref,
    within_ref, *refs, half_count
):
    foreign_refs = refs[:2]
    across, temper, *scratch = refs[2:]
    _, half, place = position(half_count)
    temper[...] = temper_ref[...]

    @pl.when(half == 0)
    def _():
        totals = merged(three_rows(message_ref, 0), three_rows(received_ref, 0))
        region = Square(square_ref, scale_row(stats_ref, 0))
        *parts, square_temper = gradients(
            region, square_weight, square_towards, square_stats[0:1, :], *totals, *scratch
        )
        query_parts, key_parts, value_parts = scaled(region, parts)
        for tile in range(region.tiles):
            here = tile_rows(tile)
            across[0, here, :] = query_parts[tile].astype(jnp.bfloat16)
            put(within_ref, 0, tile, parts_ref[0, here, :])
            put(within_ref, 1, tile, parts_ref[1, here, :] + key_parts[tile])
            put(within_ref, 2, tile, parts_ref[2, here, :] + value_parts[tile])
        across[1] = jnp.zeros(across.shape[1:], jnp.bfloat16)
        within_ref[:, 3 * BLK : 6 * BLK, :] = begun_ref[:, 3 * BLK : 6 * BLK, :]
        temper[0:1, :] = temper_ref[0:1, :] + square_temper

    @pl.when(half == 1)
    def _():
        totals = merged(three_rows(message_ref, 0), three_rows(received_ref, 0))
        temper[1:2, :] = other_diagonal(
            arrays_ref, (other_weight, other_towards), stats_ref, totals, scratch, within_ref
        )
        across[...] = across_in[...]
        within_ref[:, : 3 * BLK, :] = begun_ref[:, : 3 * BLK, :]

    pieces = temper_rows(temper[0:1, :], temper[1:2, :])
    for block in range(half_count):
        within_ref[block, 6 * BLK : 6 * BLK + EXTRA, :] = pieces
    for core, foreign_ref in enumerate(foreign_refs):
        for step in range(half_count // 2):
            rows = rows_of(place ^ core ^ (2 * step))
            foreign_ref[step, :BLK, :] = across[0, rows, :]
            foreign_ref[step, BLK : 2 * BLK, :] = across[1, rows, :]
            foreign_ref[step, 2 * BLK :, :] = pieces


def temper_kernel(within_ref, *refs, half_count):
    across_refs, temper_ref = refs[: half_count // 2], refs[half_count // 2]
    _, half, place = position(half_count)

    def sums(rows):
        return [
            jnp.sum(rows[3 * slot : 3 * slot + 3, :].astype(jnp.float32), axis=0, keepdims=True)
            for slot in range(2)
        ]

    for step, across_ref in enumerate(across_refs):
        for core in range(2):
            peer = place ^ core ^ (2 * step)
            near, far = sums(within_ref[peer]), sums(across_ref[core])
            temper_ref[pl.ds(half * half_count + peer, 1), :] = near[0] + far[1]
            temper_ref[pl.ds((1 - half) * half_count + peer, 1), :] = near[1] + far[0]


def temper_sums(within, across, half_count):
    last = (6 * BLK // EXTRA, 2 * BLK // EXTRA)
    return pl.pallas_call(
        functools.partial(temper_kernel, half_count=half_count),
        grid=(1,),
        out_shape=jax.ShapeDtypeStruct((2 * half_count, HD), jnp.float32),
        in_specs=[pl.BlockSpec((half_count, EXTRA, HD), lambda step: (0, last[0], 0))]
        + [pl.BlockSpec((2, EXTRA, HD), lambda step: (0, last[1], 0))] * (half_count // 2),
        out_specs=pl.BlockSpec((2 * half_count, HD), lambda step: (0, 0)),
        compiler_params=pltpu.CompilerParams(vmem_limit_bytes=4 * MIB),
        name="temper_sums",
    )(within, *across)


def unpack_kernel(within_ref, *refs, half_count):
    across_refs = refs[: half_count // 2]
    out_refs = refs[half_count // 2 :]
    _, half, place = position(half_count)
    for step, across_ref in enumerate(across_refs):
        for core in range(2):
            peer = place ^ core ^ (2 * step)
            other = columns_of((1 - half) * half_count + peer)
            own = columns_of(half * half_count + peer)
            first = across_ref[core, :BLK, :].astype(jnp.float32)
            second = across_ref[core, BLK : 2 * BLK, :].astype(jnp.float32)
            added = (
                jnp.where(half == 0, 0.0, first),
                jnp.where(half == 0, first, 0.0),
                jnp.where(half == 0, second, 0.0),
            )
            for array, out_ref in enumerate(out_refs):
                out_ref[0, :, own] = within_ref[peer, array * BLK : (array + 1) * BLK, :]
                kept = within_ref[peer, (3 + array) * BLK : (4 + array) * BLK, :]
                out_ref[0, :, other] = (kept.astype(jnp.float32) + added[array]).astype(
                    jnp.bfloat16
                )


def join_kernel(kept_ref, taken_ref, *out_refs):
    for step, out_ref in enumerate(out_refs):
        out_ref[0] = kept_ref[step]
        out_ref[1] = taken_ref[step]


def crossed(kept, given, half_count):
    devices = range(2 * half_count)
    steps, *shape = kept.shape
    taken = lax.ppermute(given, "seq", [(source, source ^ 1) for source in devices])
    messages = kernel_call(
        join_kernel,
        "join_chunks",
        (kept, taken),
        [pl.BlockSpec(memory_space=pltpu.VMEM)] * 2,
        [jax.ShapeDtypeStruct((2, *shape), jnp.bfloat16)] * steps,
        [],
        4,
    )
    return [
        lax.ppermute(
            message, "seq", [(source, source ^ (half_count + 2 * step)) for source in devices]
        )
        for step, message in enumerate(messages)
    ]


def head_shards(
    probe_vectors,
    lookup_vectors,
    content_vectors,
    result_cotangent,
    logit_softness,
    block_grouping,
    neighborhood_span,
):
    seq_count, dp_count = lax.axis_size("seq"), lax.axis_size("dp")
    half_count = seq_count // 2
    tokens = half_count * BLK
    groups = [list(range(half_count)), list(range(half_count, seq_count))]
    settings = (logit_softness, block_grouping[0, :, :, 0], neighborhood_span)
    smem, vmem = pl.BlockSpec(memory_space=pltpu.SMEM), pl.BlockSpec(memory_space=pltpu.VMEM)
    lows = [pltpu.VMEM((tokens, tokens), jnp.bfloat16)] * 2 + [
        pltpu.VMEM((HD, tokens), jnp.bfloat16)
    ]
    rows_of_stats = jax.ShapeDtypeStruct((8, tokens), jnp.float32)
    pairs = jax.ShapeDtypeStruct((tokens, tokens), jnp.float32)
    pair_flops = 2 * tokens * tokens * HD

    def exchange_within(array_in):
        return lax.all_to_all(
            array_in, "seq", split_axis=0, concat_axis=0, axis_index_groups=groups, tiled=True
        )

    def call(kernel, name, operands, out_shape, scratch, flops, vmem_mib, scalars=()):
        return kernel_call(
            functools.partial(kernel, half_count=half_count),
            name,
            (*scalars, *operands),
            [smem] * len(scalars) + [vmem] * len(operands),
            out_shape,
            scratch,
            vmem_mib,
            flops,
        )

    sent, *foreign = packed(
        (probe_vectors, lookup_vectors, content_vectors, result_cotangent), half_count
    )
    arrived = exchange_within(sent)
    foreign = crossed(*foreign, half_count)
    kept_parts = jax.ShapeDtypeStruct((3, tokens, HD), jnp.float32)
    tempers = jax.ShapeDtypeStruct((8, HD), jnp.float32)
    (
        arrays, stats, bias, corner, parts, temper,
        own_weight, own_towards, other_weight, other_towards,
    ) = call(
        within_kernel,
        "diagonal_statistics",
        (arrived,),
        [
            jax.ShapeDtypeStruct((8, tokens, HD), jnp.bfloat16), rows_of_stats,
            jax.ShapeDtypeStruct((half_count, tokens), jnp.float32),
            jax.ShapeDtypeStruct((BLK, BLK), jnp.float32), kept_parts, tempers,
        ]
        + [pairs] * 4,
        lows,
        2 * pair_flops,
        20,
        settings,
    )
    square, message, square_stats, square_weight, square_towards = call(
        square_kernel,
        "square_statistics",
        (arrays, stats, bias, corner, *foreign),
        [jax.ShapeDtypeStruct((4, tokens, HD), jnp.bfloat16)] + [rows_of_stats] * 2 + [pairs] * 2,
        [],
        2 * pair_flops,
        12,
    )
    swap = [(source, source ^ half_count) for source in range(seq_count)]
    received = lax.ppermute(message, "seq", swap)
    begun, across, temper = call(
        first_kernel,
        "gradients_before_totals",
        (
            arrays, square, stats, square_stats, temper, own_weight, own_towards,
            other_weight, other_towards, square_weight, square_towards,
        ),
        [
            jax.ShapeDtypeStruct((half_count, 6 * BLK, HD), jnp.bfloat16),
            jax.ShapeDtypeStruct((2, tokens, HD), jnp.bfloat16),
            tempers,
        ],
        lows,
        4 * pair_flops,
        14,
    )
    within, *foreign = call(
        finish_kernel,
        "gradients_after_totals",
        (
            arrays, square, message, received, stats, square_stats, parts, temper,
            square_weight, square_towards, other_weight, other_towards, across, begun,
        ),
        [jax.ShapeDtypeStruct((half_count, 6 * BLK + EXTRA, HD), jnp.bfloat16)]
        + [jax.ShapeDtypeStruct((half_count // 2, 2 * BLK + EXTRA, HD), jnp.bfloat16)] * 2,
        [pltpu.VMEM((2, tokens, HD), jnp.bfloat16), pltpu.VMEM((8, HD), jnp.float32), *lows],
        2 * pair_flops,
        20,
    )
    across = crossed(*foreign, half_count)
    within = exchange_within(within)
    tempers = temper_sums(within, across, half_count)
    temper_total = tempers
    for step in range(1, dp_count):
        swap = [(source, (source + step) % dp_count) for source in range(dp_count)]
        temper_total = temper_total + lax.ppermute(tempers, "dp", swap)
    outs = kernel_call(
        functools.partial(unpack_kernel, half_count=half_count),
        "unpack_heads",
        (within, *across),
        [vmem] * (1 + len(across)),
        [jax.ShapeDtypeStruct(probe_vectors.shape, jnp.bfloat16)] * 3,
        [],
        10,
    )
    return (*outs, temper_total[:, 0] / (dp_count * BLK * seq_count))


def shards(
    probe_vectors,
    lookup_vectors,
    content_vectors,
    result_cotangent,
    logit_softness,
    block_grouping,
    neighborhood_span,
):
    head_count = probe_vectors.shape[2] // HD
    seq_count = lax.axis_size("seq")
    one_block = probe_vectors.shape[1] == BLK
    whole_tiles = seq_count * BLK % (2 * TILE) == 0 and seq_count & (seq_count - 1) == 0
    if head_count == seq_count and one_block and whole_tiles:
        plan = head_shards
    else:
        plan = clustered_shards
    return plan(
        probe_vectors,
        lookup_vectors,
        content_vectors,
        result_cotangent,
        logit_softness,
        block_grouping,
        neighborhood_span,
    )


def solution(mesh):
    in_specs = (
        P("dp", "seq", None),
        P("dp", "seq", None),
        P("dp", "seq", None),
        P("dp", "seq", None),
        P(),
        P("dp", None, None, None),
        P(),
    )
    out_specs = (P("dp", "seq", None), P("dp", "seq", None), P("dp", "seq", None), P())
    return jax.shard_map(shards, mesh=mesh, in_specs=in_specs, out_specs=out_specs, check_vma=False)
```

```python
import functools
import math

import jax
import jax.numpy as jnp
from jax import lax
from jax.experimental import pallas as pl
from jax.experimental.pallas import tpu as pltpu
from jax.sharding import PartitionSpec as P

HD = 128
BLK = 128


blocked_score = -1e30


def shifted(value, axis, steps):
    count = lax.axis_size(axis)
    first, last = (max(0, -steps), min(count, count - steps))
    return lax.ppermute(value, axis, [(source, source + steps) for source in range(first, last)])


def lifted(array_in):
    return lax.optimization_barrier(array_in.astype(jnp.bfloat16)).astype(jnp.float32)


def head_major(tokens_in, block_len):
    token_count, feature_count = tokens_in.shape
    return tokens_in.reshape(
        token_count // block_len, block_len, feature_count // HD, HD
    ).transpose(2, 0, 1, 3)


def token_major(blocks_in):
    head_count, block_count, block_len, depth = blocks_in.shape
    return blocks_in.transpose(1, 2, 0, 3).reshape(1, block_count * block_len, head_count * depth)


def window_parts(query_block, prev_keys, prev_values, grad_block, usable, window_width, temper):
    block_len = query_block.shape[-2]
    inverse_root = 1.0 / math.sqrt(query_block.shape[-1])
    raw_scores = (
        jnp.einsum("...td,...sd->...ts", query_block, prev_keys, preferred_element_type=jnp.float32)
        * inverse_root
    )
    query_pos = lax.broadcasted_iota(jnp.int32, (block_len, block_len), 0)
    key_pos = lax.broadcasted_iota(jnp.int32, (block_len, block_len), 1)
    pair_mask = usable[..., None, None] & (
        key_pos > query_pos + block_len - window_width[..., None, None]
    )
    scores = temper[..., None, None] * raw_scores
    row_top = jnp.max(jnp.where(pair_mask, scores, blocked_score), axis=-1)
    weights = jnp.where(pair_mask, jnp.exp(scores - row_top[..., None]), 0.0)
    prob_grad = jnp.einsum(
        "...td,...sd->...ts", grad_block, prev_values, preferred_element_type=jnp.float32
    )
    return (
        raw_scores,
        pair_mask,
        prob_grad,
        row_top,
        jnp.sum(weights, axis=-1),
        jnp.sum(weights * prob_grad, axis=-1),
    )


def window_grads(
    raw_scores,
    pair_mask,
    prob_grad,
    query_block,
    prev_keys,
    grad_block,
    log_total,
    row_delta,
    temper,
):
    inverse_root = 1.0 / math.sqrt(query_block.shape[-1])
    scaling = (temper * inverse_root)[..., None, None]
    probability = jnp.where(
        pair_mask, jnp.exp(temper[..., None, None] * raw_scores - log_total[..., None]), 0.0
    )
    score_grad = probability * (prob_grad - row_delta[..., None])
    prob_low = probability.astype(jnp.bfloat16)
    grad_low = score_grad.astype(jnp.bfloat16)
    query_part = (
        jnp.einsum("...ts,...sd->...td", grad_low, prev_keys, preferred_element_type=jnp.float32)
        * scaling
    )
    key_part = (
        jnp.einsum("...ts,...td->...sd", grad_low, query_block, preferred_element_type=jnp.float32)
        * scaling
    )
    value_part = jnp.einsum(
        "...ts,...td->...sd", prob_low, grad_block, preferred_element_type=jnp.float32
    )
    temper_part = jnp.sum(score_grad * raw_scores, axis=(-2, -1))
    return (query_part, key_part, value_part, temper_part)


def cluster_pair(
    query_items,
    key_items,
    value_items,
    grad_items,
    live_items,
    temper,
    window_top,
    window_total,
    window_mass,
):
    item_count, block_len, depth = query_items.shape
    row_count = item_count * block_len
    group_rows = 4 * block_len
    inverse_root = 1.0 / math.sqrt(depth)
    scaling = temper * inverse_root
    query_rows = query_items.reshape(row_count, depth)
    key_rows = key_items.reshape(row_count, depth)
    value_rows = value_items.reshape(row_count, depth)
    grad_rows = grad_items.reshape(row_count, depth)
    key_item = jnp.arange(row_count) // block_len
    key_token = jnp.arange(row_count) % block_len
    live_rows = jnp.repeat(live_items, block_len)
    top_rows = window_top.reshape(row_count)
    total_rows = window_total.reshape(row_count)
    mass_rows = window_mass.reshape(row_count)

    def group_step(carry, start_row):
        key_acc, value_acc, temper_acc = carry
        query_group = lax.dynamic_slice_in_dim(query_rows, start_row, group_rows, 0)
        grad_group = lax.dynamic_slice_in_dim(grad_rows, start_row, group_rows, 0)
        group_live = lax.dynamic_slice_in_dim(live_rows, start_row, group_rows, 0)
        group_top = lax.dynamic_slice_in_dim(top_rows, start_row, group_rows, 0)
        group_total = lax.dynamic_slice_in_dim(total_rows, start_row, group_rows, 0)
        group_mass = lax.dynamic_slice_in_dim(mass_rows, start_row, group_rows, 0)
        query_item = (start_row + jnp.arange(group_rows)) // block_len
        query_token = jnp.arange(group_rows) % block_len
        earlier = (key_item[None, :] < query_item[:, None]) | (
            key_item[None, :] == query_item[:, None]
        ) & (key_token[None, :] <= query_token[:, None])
        pair_mask = group_live[:, None] & live_rows[None, :] & earlier
        raw_scores = (
            lax.dot_general(
                query_group, key_rows, (((1,), (1,)), ((), ())), preferred_element_type=jnp.float32
            )
            * inverse_root
        )
        scores = temper * raw_scores
        row_top = jnp.maximum(
            jnp.max(jnp.where(pair_mask, scores, blocked_score), axis=1), group_top
        )
        weights = jnp.where(pair_mask, jnp.exp(scores - row_top[:, None]), 0.0)
        row_total = jnp.sum(weights, axis=1) + group_total * jnp.exp(group_top - row_top)
        log_total = row_top + jnp.log(jnp.where(group_live, row_total, 1.0))
        probability = jnp.where(pair_mask, jnp.exp(scores - log_total[:, None]), 0.0)
        prob_grad = lax.dot_general(
            grad_group, value_rows, (((1,), (1,)), ((), ())), preferred_element_type=jnp.float32
        )
        row_delta = jnp.sum(probability * prob_grad, axis=1) + group_mass * jnp.exp(
            group_top - log_total
        )
        score_grad = probability * (prob_grad - row_delta[:, None])
        prob_low = probability.astype(jnp.bfloat16)
        grad_low = score_grad.astype(jnp.bfloat16)
        query_part = jnp.dot(grad_low, key_rows, preferred_element_type=jnp.float32) * scaling
        key_acc = (
            key_acc
            + lax.dot_general(
                grad_low, query_group, (((0,), (0,)), ((), ())), preferred_element_type=jnp.float32
            )
            * scaling
        )
        value_acc = value_acc + lax.dot_general(
            prob_low, grad_group, (((0,), (0,)), ((), ())), preferred_element_type=jnp.float32
        )
        temper_acc = temper_acc + jnp.sum(score_grad * raw_scores)
        return ((key_acc, value_acc, temper_acc), (query_part, log_total, row_delta))

    start_rows = jnp.arange(item_count // 4) * group_rows
    initial = (
        jnp.zeros((row_count, depth), jnp.float32),
        jnp.zeros((row_count, depth), jnp.float32),
        jnp.zeros((), jnp.float32),
    )
    (key_acc, value_acc, temper_acc), (query_part, log_total, row_delta) = lax.scan(
        group_step, initial, start_rows
    )
    return (
        query_part.reshape(item_count, block_len, depth),
        log_total.reshape(item_count, block_len),
        row_delta.reshape(item_count, block_len),
        key_acc.reshape(item_count, block_len, depth),
        value_acc.reshape(item_count, block_len, depth),
        temper_acc,
    )


def clustered_shards(
    probe_vectors,
    lookup_vectors,
    content_vectors,
    result_cotangent,
    logit_softness,
    block_grouping,
    neighborhood_span,
):
    seq_count = lax.axis_size("seq")
    position = lax.axis_index("seq")
    tokens = probe_vectors.shape[1]
    head_count = probe_vectors.shape[2] // HD
    local_blocks = tokens // BLK
    block_count = local_blocks * seq_count
    cluster_count = max(1, block_count // 8)
    capacity = min(12, block_count)
    owned_pairs = cluster_count * head_count // seq_count
    group_count = cluster_count // owned_pairs
    per_peer = max(1, local_blocks // group_count)
    cluster_ids = block_grouping[0, :, :, 0]
    query_home = head_major(probe_vectors[0], BLK)
    key_home = head_major(lookup_vectors[0], BLK)
    value_home = head_major(content_vectors[0], BLK)
    grad_home = head_major(result_cotangent[0], BLK)
    last_block = (lookup_vectors[0, tokens - BLK :], content_vectors[0, tokens - BLK :])
    prev_key_rows, prev_value_rows = shifted((last_block[0], last_block[1]), "seq", 1)
    prev_keys = jnp.concatenate([head_major(prev_key_rows, BLK), key_home[:, :-1]], axis=1)
    prev_values = jnp.concatenate([head_major(prev_value_rows, BLK), value_home[:, :-1]], axis=1)
    first_block = position * local_blocks
    before = jnp.concatenate(
        [jnp.full((head_count, 1), -1, jnp.int32), cluster_ids[:, :-1]], axis=1
    )
    my_ids = lax.dynamic_slice_in_dim(cluster_ids, first_block, local_blocks, 1)
    my_before = lax.dynamic_slice_in_dim(before, first_block, local_blocks, 1)
    global_block = first_block + jnp.arange(local_blocks)
    usable_home = (global_block[None, :] >= 1) & (my_before != my_ids)
    peer_index = jnp.arange(seq_count)
    peer_head = peer_index * owned_pairs // cluster_count
    slot_range = jnp.arange(per_peer)
    local_range = jnp.arange(local_blocks)
    owner_index = (jnp.arange(head_count)[:, None] * cluster_count + my_ids) // owned_pairs
    peer_ids = jnp.take(my_ids, peer_head, axis=0)
    goes = (peer_head[:, None] * cluster_count + peer_ids) // owned_pairs == peer_index[:, None]
    send_rank = jnp.cumsum(goes.astype(jnp.int32), axis=1) - 1
    send_pick = goes[:, None, :] & (send_rank[:, None, :] == slot_range[None, :, None])
    send_block = jnp.sum(jnp.where(send_pick, local_range[None, None, :], 0), axis=2)
    send_flat = peer_head[:, None] * local_blocks + send_block
    home_rank = jnp.take_along_axis(send_rank, owner_index, axis=0)
    home_pos = owner_index * per_peer + home_rank
    pair_index = position * owned_pairs + jnp.arange(owned_pairs)
    split_for_couple = pair_index // cluster_count
    pair_cluster = pair_index % cluster_count
    my_head = position * owned_pairs // cluster_count
    split_numbers = jnp.take(cluster_ids, my_head, axis=0)
    member = split_numbers[None, :] == pair_cluster[:, None]
    member_rank = jnp.cumsum(member.astype(jnp.int32), axis=1) - 1
    member_count = jnp.sum(member.astype(jnp.int32), axis=1)
    picked = member[:, None, :] & (member_rank[:, None, :] == jnp.arange(capacity)[None, :, None])
    member_block = jnp.sum(jnp.where(picked, jnp.arange(block_count)[None, None, :], 0), axis=2)
    live_members = jnp.arange(capacity)[None, :] < member_count[:, None]
    mine = (my_head * cluster_count + split_numbers) // owned_pairs == position
    mine_grid = mine.reshape(seq_count, local_blocks)
    recv_rank = jnp.cumsum(mine_grid.astype(jnp.int32), axis=1) - 1
    recv_pos = (peer_index[:, None] * per_peer + recv_rank).reshape(block_count)
    member_pos = jnp.take(recv_pos, member_block)
    couple_softness = jnp.take(logit_softness, split_for_couple)
    pair_onehot = (split_for_couple[:, None] == jnp.arange(head_count)[None, :]).astype(jnp.float32)
    slot_pair = my_head * cluster_count + split_numbers - position * owned_pairs
    same_cluster = split_numbers[:, None] == split_numbers[None, :]
    earlier_block = jnp.arange(block_count)[None, :] < jnp.arange(block_count)[:, None]
    slot_rank = jnp.sum((same_cluster & earlier_block).astype(jnp.int32), axis=1)
    back_pos = jnp.clip(slot_pair, 0, owned_pairs - 1) * capacity + jnp.clip(
        slot_rank, 0, capacity - 1
    )
    back_grid = back_pos.reshape(seq_count, local_blocks)
    back_pick = mine_grid[:, None, :] & (recv_rank[:, None, :] == slot_range[None, :, None])
    back_flat = jnp.sum(jnp.where(back_pick, back_grid[:, None, :], 0), axis=2)

    def to_peers(array_in):
        flat = array_in.reshape((head_count * local_blocks,) + array_in.shape[2:])
        return jnp.take(flat, send_flat, axis=0)

    def members(array_in):
        flat = array_in.reshape((seq_count * per_peer,) + array_in.shape[2:])
        return jnp.take(flat, member_pos, axis=0)

    def to_owner(array_in):
        flat = array_in.reshape((owned_pairs * capacity,) + array_in.shape[2:])
        return jnp.take(flat, back_flat, axis=0)

    def from_peers(array_in):
        flat = array_in.reshape((seq_count * per_peer,) + array_in.shape[2:])
        return jnp.take(flat, home_pos, axis=0)

    raw_w, mask_w, pgrad_w, top_w, total_w, mass_w = window_parts(
        query_home,
        prev_keys,
        prev_values,
        grad_home,
        usable_home,
        neighborhood_span[:, None],
        logit_softness[:, None],
    )
    arrived = (
        lax.all_to_all(to_peers(query_home), "seq", split_axis=0, concat_axis=0, tiled=True),
        lax.all_to_all(to_peers(key_home), "seq", split_axis=0, concat_axis=0, tiled=True),
        lax.all_to_all(to_peers(value_home), "seq", split_axis=0, concat_axis=0, tiled=True),
        lax.all_to_all(to_peers(grad_home), "seq", split_axis=0, concat_axis=0, tiled=True),
    )
    arrived_stats = (
        lax.all_to_all(to_peers(top_w), "seq", split_axis=0, concat_axis=0, tiled=True),
        lax.all_to_all(to_peers(total_w), "seq", split_axis=0, concat_axis=0, tiled=True),
        lax.all_to_all(to_peers(mass_w), "seq", split_axis=0, concat_axis=0, tiled=True),
    )
    query_m, key_m, value_m, grad_m = [members(item_in) for item_in in arrived]
    top_m, total_m, mass_m = [members(item_in) for item_in in arrived_stats]

    def split_pair(pair_inputs):
        query_i, key_i, value_i, grad_i, live_i, temper_i, top_i, total_i, mass_i = pair_inputs
        query_c, log_total, row_delta, key_c, value_c, temper_c = cluster_pair(
            query_i, key_i, value_i, grad_i, live_i, temper_i, top_i, total_i, mass_i
        )
        return (
            query_c.astype(jnp.bfloat16),
            key_c.astype(jnp.bfloat16),
            value_c.astype(jnp.bfloat16),
            log_total,
            row_delta,
            temper_c,
        )

    owner_results = lax.map(
        split_pair,
        (query_m, key_m, value_m, grad_m, live_members, couple_softness, top_m, total_m, mass_m),
    )
    returned = (
        lax.all_to_all(to_owner(owner_results[0]), "seq", split_axis=0, concat_axis=0, tiled=True),
        lax.all_to_all(to_owner(owner_results[1]), "seq", split_axis=0, concat_axis=0, tiled=True),
        lax.all_to_all(to_owner(owner_results[2]), "seq", split_axis=0, concat_axis=0, tiled=True),
    )
    returned_stats = (
        lax.all_to_all(to_owner(owner_results[3]), "seq", split_axis=0, concat_axis=0, tiled=True),
        lax.all_to_all(to_owner(owner_results[4]), "seq", split_axis=0, concat_axis=0, tiled=True),
    )
    query_cluster = from_peers(returned[0])
    key_cluster = from_peers(returned[1])
    value_cluster = from_peers(returned[2])
    log_home = from_peers(returned_stats[0])
    delta_home = from_peers(returned_stats[1])
    query_w, key_w, value_w, temper_w = window_grads(
        raw_w,
        mask_w,
        pgrad_w,
        query_home,
        prev_keys,
        grad_home,
        log_home,
        delta_home,
        logit_softness[:, None],
    )
    query_out = (query_cluster.astype(jnp.float32) + lifted(query_w)).astype(jnp.bfloat16)
    key_window = key_w.astype(jnp.bfloat16)
    value_window = value_w.astype(jnp.bfloat16)
    temper_local = jnp.sum(owner_results[5][:, None] * pair_onehot, axis=0) + jnp.sum(
        temper_w, axis=1
    )
    edge_keys, edge_values = shifted((key_window[:, 0], value_window[:, 0]), "seq", -1)
    key_next = jnp.concatenate([key_window[:, 1:], edge_keys[:, None]], axis=1)
    value_next = jnp.concatenate([value_window[:, 1:], edge_values[:, None]], axis=1)
    key_out = (key_cluster.astype(jnp.float32) + key_next.astype(jnp.float32)).astype(jnp.bfloat16)
    value_out = (value_cluster.astype(jnp.float32) + value_next.astype(jnp.float32)).astype(
        jnp.bfloat16
    )
    temper_total = lax.psum(temper_local, ("seq", "dp"))
    temper_grad = temper_total / (lax.axis_size("dp") * tokens * seq_count)
    return (token_major(query_out), token_major(key_out), token_major(value_out), temper_grad)


TILE = 256
EXTRA = 16
MIB = 1024 * 1024
PIECES = 4
QUERY, KEY, VALUE, GRAD = range(4)


def columns_of(index):
    return pl.ds(pl.multiple_of(index * HD, HD), HD)


def rows_of(index):
    return pl.ds(pl.multiple_of(index * BLK, BLK), BLK)


def tile_rows(tile):
    return slice(tile * TILE, (tile + 1) * TILE)


def position(half_count):
    me = lax.axis_index("seq")
    half = jnp.where(me >= half_count, 1, 0)
    return me, half, me - half * half_count


def kernel_call(
    kernel, name, operands, in_specs, out_shape, scratch, vmem_mib, flops=0, out_space=pltpu.VMEM
):
    bytes_accessed = sum(
        math.prod(item.shape) * item.dtype.itemsize for item in (*operands, *out_shape)
    )
    return pl.pallas_call(
        kernel,
        out_shape=out_shape,
        in_specs=in_specs,
        out_specs=[pl.BlockSpec(memory_space=out_space)] * len(out_shape),
        scratch_shapes=scratch,
        cost_estimate=pl.CostEstimate(
            flops=flops, bytes_accessed=bytes_accessed, transcendentals=0
        ),
        compiler_params=pltpu.CompilerParams(vmem_limit_bytes=vmem_mib * MIB),
        name=name,
    )(*operands)


def pack_kernel(*refs, half_count):
    arrays, within_ref, foreign_refs = refs[:4], refs[4], refs[5:7]
    held, within, across, arrival, left_within, left_across = refs[7:]
    me, half, _ = position(half_count)
    piece = BLK // PIECES
    arrivals = [
        [
            pltpu.make_async_copy(
                array_ref.at[0, part * piece : (part + 1) * piece, :],
                held.at[place, part * piece : (part + 1) * piece, :],
                arrival.at[place, part],
            )
            for part in range(PIECES)
        ]
        for place, array_ref in enumerate(arrays)
    ]
    for copies in arrivals:
        for copy in copies:
            copy.start()
    leaving = []
    for place, copies in enumerate(arrivals):
        for copy in copies:
            copy.wait()
        for slot, base in enumerate((half * half_count, (1 - half) * half_count)):
            rows = slice((slot * 4 + place) * BLK, (slot * 4 + place + 1) * BLK)
            for peer in range(half_count):
                within[peer, rows, :] = held[place, :, columns_of(base + peer)]
            leaving.append(
                pltpu.make_async_copy(
                    within.at[:, rows, :], within_ref.at[:, rows, :], left_within.at[place, slot]
                )
            )
            leaving[-1].start()
    first = jnp.where(half == 0, KEY, QUERY)
    second = jnp.where(half == 0, VALUE, GRAD)
    for core, foreign_ref in enumerate(foreign_refs):
        for step in range(half_count // 2):
            columns = columns_of(me ^ core ^ (half_count + 2 * step))
            across[core, step, :BLK, :] = held[first, :, columns]
            across[core, step, BLK:, :] = held[second, :, columns]
        leaving.append(pltpu.make_async_copy(across.at[core], foreign_ref, left_across.at[core]))
        leaving[-1].start()
    for copy in leaving:
        copy.wait()


def packed(arrays, half_count):
    width = arrays[0].shape[2]
    within_shape, across_shape = (half_count, 8 * BLK, HD), (half_count // 2, 2 * BLK, HD)
    return kernel_call(
        functools.partial(pack_kernel, half_count=half_count),
        "pack_heads",
        arrays,
        [pl.BlockSpec(memory_space=pl.ANY)] * 4,
        [jax.ShapeDtypeStruct(within_shape, jnp.bfloat16)]
        + [jax.ShapeDtypeStruct(across_shape, jnp.bfloat16)] * 2,
        [
            pltpu.VMEM((4, BLK, width), jnp.bfloat16),
            pltpu.VMEM(within_shape, jnp.bfloat16),
            pltpu.VMEM((2, *across_shape), jnp.bfloat16),
            pltpu.SemaphoreType.DMA((4, PIECES)),
            pltpu.SemaphoreType.DMA((4, 2)),
            pltpu.SemaphoreType.DMA((2,)),
        ],
        60,
        out_space=pl.ANY,
    )


def dot_rows(left, right):
    return lax.dot_general(
        left, right, (((1,), (1,)), ((), ())), preferred_element_type=jnp.float32
    )


def dot_plain(left, right):
    return lax.dot_general(
        left, right, (((1,), (0,)), ((), ())), preferred_element_type=jnp.float32
    )


class Region:
    def __init__(self, square, arrays, places, scaling):
        self.square, self.arrays, self.places, self.scaling = square, arrays, places, scaling
        self.tiles = arrays.shape[1] // TILE

    def rows(self, which, start, stop):
        return self.arrays[self.places[which], start * TILE : stop * TILE, :]

    def keys_of(self, tile):
        return range(self.tiles if self.square else tile + 1)

    def products(self, tile_key, tile_query):
        return dot_rows(
            self.rows(KEY, tile_key, tile_key + 1), self.rows(QUERY, tile_query, tile_query + 1)
        ) * (self.scaling * math.log2(math.e))


class Diagonal(Region):
    def __init__(self, arrays, places, scaling, ids_ref=None, head=None, base=None, width=None):
        super().__init__(False, arrays, places, scaling)
        self.ids_ref, self.head, self.base, self.width = ids_ref, head, base, width

    def same(self, key_block, query_block):
        ids_ref, head, base = self.ids_ref, self.head, self.base
        return ids_ref[head, base + key_block] == ids_ref[head, base + query_block]

    def scores(self, tile_key, tile_query):
        per_tile = TILE // BLK
        scores = self.products(tile_key, tile_query)
        spread = key_minus_query()
        rows = []
        for sub_key in range(per_tile):
            pieces = []
            for sub_query in range(per_tile):
                piece = scores[
                    sub_key * BLK : (sub_key + 1) * BLK, sub_query * BLK : (sub_query + 1) * BLK
                ]
                key_block = tile_key * per_tile + sub_key
                query_block = tile_query * per_tile + sub_query
                if key_block > query_block:
                    piece = jnp.full_like(piece, blocked_score)
                elif key_block == query_block:
                    piece = jnp.where(spread <= 0, piece, blocked_score)
                elif key_block == query_block - 1:
                    least = jnp.where(self.same(key_block, query_block), -BLK, BLK - self.width)
                    piece = jnp.where(spread > least, piece, blocked_score)
                else:
                    piece = piece + jnp.where(
                        self.same(key_block, query_block), 0.0, blocked_score
                    )
                pieces.append(piece)
            rows.append(jnp.concatenate(pieces, axis=1))
        return jnp.concatenate(rows, axis=0)


class Square(Region):
    def __init__(self, arrays, scaling, bias_ref=None, corner_ref=None):
        super().__init__(True, arrays, range(4), scaling)
        self.bias_ref, self.corner_ref = bias_ref, corner_ref

    def scores(self, tile_key, tile_query):
        per_tile = TILE // BLK
        scores = self.products(tile_key, tile_query)
        rows = []
        for sub_key in range(per_tile):
            block = tile_key * per_tile + sub_key
            row = scores[sub_key * BLK : (sub_key + 1) * BLK, :]
            bias = self.bias_ref[block : block + 1, tile_rows(tile_query)]
            if block == self.tiles * per_tile - 1 and tile_query == 0:
                rows.append(
                    jnp.concatenate(
                        [row[:, :BLK] + self.corner_ref[...], row[:, BLK:] + bias[:, BLK:]], axis=1
                    )
                )
            else:
                rows.append(row + bias)
        return jnp.concatenate(rows, axis=0)


def key_minus_query():
    shape = (BLK, BLK)
    return lax.broadcasted_iota(jnp.int32, shape, 0) - lax.broadcasted_iota(jnp.int32, shape, 1)


def statistics(region, weight_ref, towards_ref, out_ref, first_row, temper_ref=None):
    for tile in range(region.tiles):
        here = tile_rows(tile)
        top = jnp.full((1, TILE), blocked_score, jnp.float32)
        for other in region.keys_of(tile):
            raw = region.scores(other, tile)
            weight_ref[tile_rows(other), here] = raw
            top = jnp.maximum(top, jnp.max(raw, axis=0, keepdims=True))
        total = jnp.zeros((1, TILE), jnp.float32)
        mass = jnp.zeros((1, TILE), jnp.float32)
        moment = jnp.zeros((1, TILE), jnp.float32)
        spread = jnp.zeros((1, TILE), jnp.float32)
        for other in region.keys_of(tile):
            there = tile_rows(other)
            raw = weight_ref[there, here]
            weight = jnp.exp2(raw - top)
            towards = dot_rows(
                region.rows(VALUE, other, other + 1), region.rows(GRAD, tile, tile + 1)
            )
            weight_ref[there, here] = weight
            towards_ref[there, here] = towards
            total += jnp.sum(weight, axis=0, keepdims=True)
            mass += jnp.sum(weight * towards, axis=0, keepdims=True)
            if temper_ref is not None:
                weighted = weight * raw
                moment += jnp.sum(weighted * towards, axis=0, keepdims=True)
                spread += jnp.sum(weighted, axis=0, keepdims=True)
        if temper_ref is not None:
            temper_ref[0:1, here] = moment
            temper_ref[1:2, here] = spread
        out_ref[first_row : first_row + 1, here] = top
        out_ref[first_row + 1 : first_row + 2, here] = total
        out_ref[first_row + 2 : first_row + 3, here] = mass


def gradients(
    region, weight_ref, towards_ref, top, log_total, delta, prob_low, grad_low, keys_flat
):
    keys_flat[...] = region.rows(KEY, 0, region.tiles).T
    share = jnp.exp2(top - log_total)
    temper = jnp.zeros((1, HD), jnp.float32)
    query_parts, key_parts, value_parts = [], [], []
    for tile in range(region.tiles):
        here = tile_rows(tile)
        for other in region.keys_of(tile):
            there = tile_rows(other)
            probability = weight_ref[there, here] * share[:, here]
            prob_low[there, here] = probability.astype(jnp.bfloat16)
            grad_low[there, here] = (
                probability * (towards_ref[there, here] - delta[:, here])
            ).astype(jnp.bfloat16)
        upto = slice(0, len(region.keys_of(tile)) * TILE)
        query_part = dot_plain(keys_flat[:, upto], grad_low[upto, here]).T
        temper += jnp.sum(
            query_part * region.rows(QUERY, tile, tile + 1).astype(jnp.float32),
            axis=0,
            keepdims=True,
        )
        query_parts.append(query_part)
    for tile in range(region.tiles):
        first = 0 if region.square else tile
        onward = slice(first * TILE, region.tiles * TILE)
        here = tile_rows(tile)
        key_parts.append(
            dot_plain(grad_low[here, onward], region.rows(QUERY, first, region.tiles))
        )
        value_parts.append(
            dot_plain(prob_low[here, onward], region.rows(GRAD, first, region.tiles))
        )
    return query_parts, key_parts, value_parts, temper


def merged(first, second):
    top = jnp.maximum(first[0], second[0])
    left, right = jnp.exp2(first[0] - top), jnp.exp2(second[0] - top)
    total = first[1] * left + second[1] * right
    mass = first[2] * left + second[2] * right
    return top + jnp.log2(total), mass / total


def alone(rows):
    return rows[0] + jnp.log2(rows[1]), rows[2] / rows[1]


def three_rows(ref, first):
    return [ref[first + row : first + row + 1, :] for row in range(3)]


def put(within_ref, array, tile, value):
    per_tile = TILE // BLK
    for sub in range(per_tile):
        within_ref[tile * per_tile + sub, array * BLK : (array + 1) * BLK, :] = value[
            sub * BLK : (sub + 1) * BLK, :
        ].astype(jnp.bfloat16)


def scale_row(stats_ref, slot):
    return stats_ref[6 + slot : 7 + slot, :HD]


def scaled(region, parts):
    return [
        [value * scale for value in part]
        for part, scale in zip(parts, (region.scaling, region.scaling, 1.0))
    ]


def within_kernel(
    softness_ref, ids_ref, span_ref, in_ref, arrays_ref, stats_ref, message_ref, bias_ref,
    corner_ref, parts_ref, other_ref, temper_ref, own_weight, own_towards, other_weight, other_towards, *scratch,
    half_count
):
    me, half, _ = position(half_count)
    for block in range(half_count):
        for place in range(8):
            arrays_ref[place, block * BLK : (block + 1) * BLK, :] = in_ref[
                block, place * BLK : (place + 1) * BLK, :
            ]
    kept = ((own_weight, own_towards), (other_weight, other_towards))
    for slot in range(2):
        head = me ^ (slot * half_count)
        scaling = softness_ref[head] * (1.0 / math.sqrt(HD))
        places = [slot * 4 + place for place in range(4)]
        region = Diagonal(
            arrays_ref, places, scaling, ids_ref, head, half * half_count, span_ref[head]
        )
        statistics(
            region, *kept[slot], stats_ref, slot * 3, None if slot == 0 else message_ref.at[3:5]
        )
        stats_ref[6 + slot : 7 + slot, :] = jnp.full((1, stats_ref.shape[1]), scaling, jnp.float32)
    for key_block in range(half_count):
        for query_block in range(half_count):
            same = ids_ref[me, key_block] == ids_ref[me, half_count + query_block]
            bias_ref[key_block : key_block + 1, query_block * BLK : (query_block + 1) * BLK] = (
                jnp.full((1, BLK), jnp.where(same, 0.0, blocked_score), jnp.float32)
            )
    same = ids_ref[me, half_count - 1] == ids_ref[me, half_count]
    least = jnp.where(same, -BLK, BLK - span_ref[me])
    corner_ref[...] = jnp.where(key_minus_query() > least, 0.0, blocked_score)
    temper_ref[...] = jnp.zeros_like(temper_ref)
    message_ref[0:3, :] = stats_ref[3:6, :]

    @pl.when(half == 0)
    def _():
        temper_ref[1:2, :] = other_diagonal(
            arrays_ref, kept[1], stats_ref, alone(three_rows(stats_ref, 3)), scratch, other_ref, 0
        )
        region = Diagonal(arrays_ref, range(4), scale_row(stats_ref, 0))
        single = alone(three_rows(stats_ref, 0))
        *parts, temper = gradients(region, *kept[0], stats_ref[0:1, :], *single, *scratch)
        for place, tiles in enumerate(scaled(region, parts)):
            for tile, value in enumerate(tiles):
                parts_ref[place, tile_rows(tile), :] = value
        temper_ref[0:1, :] = temper


def square_kernel(arrays_ref, stats_ref, bias_ref, corner_ref, *refs, half_count):
    across_refs = refs[: half_count // 2]
    square_ref, square_stats, weight, towards = refs[half_count // 2 :]
    _, half, place = position(half_count)
    first = jnp.where(half == 0, QUERY, KEY)
    second = jnp.where(half == 0, GRAD, VALUE)
    for step, across_ref in enumerate(across_refs):
        for core in range(2):
            rows = rows_of(place ^ core ^ (2 * step))
            square_ref[first, rows, :] = across_ref[core, :BLK, :]
            square_ref[second, rows, :] = across_ref[core, BLK:, :]
    kept_first = jnp.where(half == 0, KEY, QUERY)
    kept_second = jnp.where(half == 0, VALUE, GRAD)
    square_ref[kept_first, :, :] = arrays_ref[kept_first, :, :]
    square_ref[kept_second, :, :] = arrays_ref[kept_second, :, :]

    @pl.when(half == 0)
    def _():
        region = Square(square_ref, stats_ref[6:7, :TILE], bias_ref, corner_ref)
        statistics(region, weight, towards, square_stats, 0)


def other_diagonal(arrays_ref, kept, stats_ref, totals, scratch, out_ref, first):
    region = Diagonal(arrays_ref, range(4, 8), scale_row(stats_ref, 1))
    *parts, temper = gradients(region, *kept, stats_ref[3:4, :], *totals, *scratch)
    for array, tiles in enumerate(scaled(region, parts)):
        for tile, value in enumerate(tiles):
            put(out_ref, first + array, tile, value)
    return temper


def temper_terms(message_ref, totals, scaling):
    log_total, delta = totals
    share = jnp.exp2(message_ref[0:1, :] - log_total)
    terms = (message_ref[3:4, :] - delta * message_ref[4:5, :]) * share
    folded = sum(terms[:, start : start + HD] for start in range(0, terms.shape[1], HD))
    return folded / (scaling * math.log2(math.e))


def own_kernel(
    arrays_ref, square_ref, stats_ref, bias_ref, corner_ref, square_stats, received_ref, parts_ref,
    temper_in, own_weight, own_towards, square_weight, square_towards,
    own_ref, kept_ref, given_ref, temper_ref, across, late_stats, weight, towards, *scratch,
    half_count
):
    _, half, place = position(half_count)
    temper_ref[...] = temper_in[...]
    square = Square(square_ref, scale_row(stats_ref, 0))

    @pl.when(half == 0)
    def _():
        totals = merged(three_rows(square_stats, 0), three_rows(received_ref, 0))
        *parts, temper = gradients(
            square, square_weight, square_towards, square_stats[0:1, :], *totals, *scratch
        )
        query_parts, key_parts, value_parts = scaled(square, parts)
        for tile in range(square.tiles):
            here = tile_rows(tile)
            across[0, here, :] = query_parts[tile].astype(jnp.bfloat16)
            put(own_ref, 0, tile, parts_ref[0, here, :])
            put(own_ref, 1, tile, parts_ref[1, here, :] + key_parts[tile])
            put(own_ref, 2, tile, parts_ref[2, here, :] + value_parts[tile])
        across[1] = jnp.zeros(across.shape[1:], jnp.bfloat16)
        temper_ref[0:1, :] = (
            temper_in[0:1, :] + temper + temper_terms(received_ref, totals, square.scaling)
        )

    @pl.when(half == 1)
    def _():
        masked = Square(square_ref, stats_ref[6:7, :TILE], bias_ref, corner_ref)
        statistics(masked, weight, towards, late_stats, 0)
        totals = merged(three_rows(stats_ref, 0), three_rows(late_stats, 0))
        *parts, square_temper = gradients(
            square, weight, towards, late_stats[0:1, :], *totals, *scratch
        )
        across_query, *foreign = scaled(square, parts)
        for array, tiles in enumerate(foreign):
            for tile, value in enumerate(tiles):
                across[array, tile_rows(tile), :] = value.astype(jnp.bfloat16)
        diagonal = Diagonal(arrays_ref, range(4), scale_row(stats_ref, 0))
        *parts, temper = gradients(
            diagonal, own_weight, own_towards, stats_ref[0:1, :], *totals, *scratch
        )
        query_parts, key_parts, value_parts = scaled(diagonal, parts)
        for tile in range(square.tiles):
            put(own_ref, 0, tile, query_parts[tile] + across_query[tile])
            put(own_ref, 1, tile, key_parts[tile])
            put(own_ref, 2, tile, value_parts[tile])
        temper_ref[0:1, :] = temper + square_temper

    pieces = temper_rows(temper_ref[0:1, :], temper_ref[1:2, :])
    for core, foreign_ref in enumerate((kept_ref, given_ref)):
        for step in range(half_count // 2):
            rows = rows_of(place ^ core ^ (2 * step))
            foreign_ref[step, :BLK, :] = across[0, rows, :]
            foreign_ref[step, BLK : 2 * BLK, :] = across[1, rows, :]
            foreign_ref[step, 2 * BLK :, :] = pieces


def finish_kernel(
    arrays_ref, stats_ref, received_ref, own_ref, other_ref, temper_ref, other_weight,
    other_towards, within_ref, *scratch, half_count
):
    _, half, _ = position(half_count)
    pieces = temper_rows(temper_ref[0:1, :], temper_ref[1:2, :])
    for block in range(half_count):
        within_ref[block, : 3 * BLK, :] = own_ref[block]
        within_ref[block, 6 * BLK :, :] = pieces

    @pl.when(half == 0)
    def _():
        for block in range(half_count):
            within_ref[block, 3 * BLK : 6 * BLK, :] = other_ref[block]

    @pl.when(half == 1)
    def _():
        totals = merged(three_rows(stats_ref, 3), three_rows(received_ref, 0))
        other_diagonal(
            arrays_ref, (other_weight, other_towards), stats_ref, totals, scratch, within_ref, 3
        )


def temper_rows(own, other):
    row = lax.broadcasted_iota(jnp.int32, (EXTRA, HD), 0)
    rows = jnp.zeros((EXTRA, HD), jnp.float32)
    for place, terms in enumerate((own, other)):
        rest = jnp.broadcast_to(jnp.sum(terms, axis=1, keepdims=True), (EXTRA, HD)) * (
            1.0 / math.sqrt(HD)
        )
        for piece in range(3):
            high = rest.astype(jnp.bfloat16).astype(jnp.float32)
            rows = jnp.where(row == place * 3 + piece, high, rows)
            rest = rest - high
    return rows.astype(jnp.bfloat16)


def temper_kernel(within_ref, *refs, half_count):
    across_refs, temper_ref = refs[: half_count // 2], refs[half_count // 2]
    _, half, place = position(half_count)

    def sums(rows):
        return [
            jnp.sum(rows[3 * slot : 3 * slot + 3, :].astype(jnp.float32), axis=0, keepdims=True)
            for slot in range(2)
        ]

    for step, across_ref in enumerate(across_refs):
        for core in range(2):
            peer = place ^ core ^ (2 * step)
            near, far = sums(within_ref[peer]), sums(across_ref[core])
            temper_ref[pl.ds(half * half_count + peer, 1), :] = near[0] + far[1]
            temper_ref[pl.ds((1 - half) * half_count + peer, 1), :] = near[1] + far[0]


def temper_sums(within, across, half_count):
    last = (6 * BLK // EXTRA, 2 * BLK // EXTRA)
    return pl.pallas_call(
        functools.partial(temper_kernel, half_count=half_count),
        grid=(1,),
        out_shape=jax.ShapeDtypeStruct((2 * half_count, HD), jnp.float32),
        in_specs=[pl.BlockSpec((half_count, EXTRA, HD), lambda step: (0, last[0], 0))]
        + [pl.BlockSpec((2, EXTRA, HD), lambda step: (0, last[1], 0))] * (half_count // 2),
        out_specs=pl.BlockSpec((2 * half_count, HD), lambda step: (0, 0)),
        compiler_params=pltpu.CompilerParams(vmem_limit_bytes=4 * MIB),
        name="temper_sums",
    )(within, *across)


def unpack_kernel(within_ref, *refs, half_count):
    across_refs = refs[: half_count // 2]
    out_refs = refs[half_count // 2 :]
    _, half, place = position(half_count)
    for step, across_ref in enumerate(across_refs):
        for core in range(2):
            peer = place ^ core ^ (2 * step)
            other = columns_of((1 - half) * half_count + peer)
            own = columns_of(half * half_count + peer)
            first = across_ref[core, :BLK, :].astype(jnp.float32)
            second = across_ref[core, BLK : 2 * BLK, :].astype(jnp.float32)
            added = (
                jnp.where(half == 0, 0.0, first),
                jnp.where(half == 0, first, 0.0),
                jnp.where(half == 0, second, 0.0),
            )
            for array, out_ref in enumerate(out_refs):
                out_ref[0, :, own] = within_ref[peer, array * BLK : (array + 1) * BLK, :]
                kept = within_ref[peer, (3 + array) * BLK : (4 + array) * BLK, :]
                out_ref[0, :, other] = (kept.astype(jnp.float32) + added[array]).astype(
                    jnp.bfloat16
                )


def join_kernel(kept_ref, taken_ref, *out_refs):
    for step, out_ref in enumerate(out_refs):
        out_ref[0] = kept_ref[step]
        out_ref[1] = taken_ref[step]


def crossed(kept, given, half_count):
    devices = range(2 * half_count)
    steps, *shape = kept.shape
    taken = lax.ppermute(given, "seq", [(source, source ^ 1) for source in devices])
    messages = kernel_call(
        join_kernel,
        "join_chunks",
        (kept, taken),
        [pl.BlockSpec(memory_space=pltpu.VMEM)] * 2,
        [jax.ShapeDtypeStruct((2, *shape), jnp.bfloat16)] * steps,
        [],
        4,
    )
    return [
        lax.ppermute(
            message, "seq", [(source, source ^ (half_count + 2 * step)) for source in devices]
        )
        for step, message in enumerate(messages)
    ]


def head_shards(
    probe_vectors,
    lookup_vectors,
    content_vectors,
    result_cotangent,
    logit_softness,
    block_grouping,
    neighborhood_span,
):
    seq_count, dp_count = lax.axis_size("seq"), lax.axis_size("dp")
    half_count = seq_count // 2
    tokens = half_count * BLK
    groups = [list(range(half_count)), list(range(half_count, seq_count))]
    settings = (logit_softness, block_grouping[0, :, :, 0], neighborhood_span)
    smem, vmem = pl.BlockSpec(memory_space=pltpu.SMEM), pl.BlockSpec(memory_space=pltpu.VMEM)
    lows = [pltpu.VMEM((tokens, tokens), jnp.bfloat16)] * 2 + [
        pltpu.VMEM((HD, tokens), jnp.bfloat16)
    ]
    rows_of_stats = jax.ShapeDtypeStruct((8, tokens), jnp.float32)
    pairs = jax.ShapeDtypeStruct((tokens, tokens), jnp.float32)
    pair_flops = 2 * tokens * tokens * HD

    def exchange_within(array_in):
        return lax.all_to_all(
            array_in, "seq", split_axis=0, concat_axis=0, axis_index_groups=groups, tiled=True
        )

    def call(kernel, name, operands, out_shape, scratch, flops, vmem_mib, scalars=()):
        return kernel_call(
            functools.partial(kernel, half_count=half_count),
            name,
            (*scalars, *operands),
            [smem] * len(scalars) + [vmem] * len(operands),
            out_shape,
            scratch,
            vmem_mib,
            flops,
        )

    sent, *foreign = packed(
        (probe_vectors, lookup_vectors, content_vectors, result_cotangent), half_count
    )
    arrived = exchange_within(sent)
    foreign = crossed(*foreign, half_count)
    kept_parts = jax.ShapeDtypeStruct((3, tokens, HD), jnp.float32)
    three_arrays = jax.ShapeDtypeStruct((half_count, 3 * BLK, HD), jnp.bfloat16)
    tempers = jax.ShapeDtypeStruct((8, HD), jnp.float32)
    chunks = jax.ShapeDtypeStruct((half_count // 2, 2 * BLK + EXTRA, HD), jnp.bfloat16)
    first_half = range(half_count)
    (
        arrays, stats, message, bias, corner, parts, other_done, temper,
        own_weight, own_towards, other_weight, other_towards,
    ) = call(
        within_kernel,
        "diagonal_statistics",
        (arrived,),
        [
            jax.ShapeDtypeStruct((8, tokens, HD), jnp.bfloat16), rows_of_stats, rows_of_stats,
            jax.ShapeDtypeStruct((half_count, tokens), jnp.float32),
            jax.ShapeDtypeStruct((BLK, BLK), jnp.float32), kept_parts, three_arrays, tempers,
        ]
        + [pairs] * 4,
        lows,
        2 * pair_flops,
        20,
        settings,
    )
    from_second = lax.ppermute(
        message, "seq", [(source + half_count, source) for source in first_half]
    )
    square, square_stats, square_weight, square_towards = call(
        square_kernel,
        "square_statistics",
        (arrays, stats, bias, corner, *foreign),
        [jax.ShapeDtypeStruct((4, tokens, HD), jnp.bfloat16), rows_of_stats] + [pairs] * 2,
        [],
        2 * pair_flops,
        12,
    )
    from_first = lax.ppermute(
        square_stats, "seq", [(source, source + half_count) for source in first_half]
    )
    own_done, *foreign, temper = call(
        own_kernel,
        "own_gradients",
        (
            arrays, square, stats, bias, corner, square_stats, from_second, parts, temper,
            own_weight, own_towards, square_weight, square_towards,
        ),
        [three_arrays, chunks, chunks, tempers],
        [
            pltpu.VMEM((2, tokens, HD), jnp.bfloat16), pltpu.VMEM((8, tokens), jnp.float32),
            pltpu.VMEM((tokens, tokens), jnp.float32), pltpu.VMEM((tokens, tokens), jnp.float32),
            *lows,
        ],
        6 * pair_flops,
        20,
    )
    (within,) = call(
        finish_kernel,
        "other_gradients",
        (arrays, stats, from_first, own_done, other_done, temper, other_weight, other_towards),
        [jax.ShapeDtypeStruct((half_count, 6 * BLK + EXTRA, HD), jnp.bfloat16)],
        lows,
        2 * pair_flops,
        14,
    )
    within, *foreign = lax.optimization_barrier((within, *foreign))
    across = crossed(*foreign, half_count)
    within = exchange_within(within)
    tempers = temper_sums(within, across, half_count)
    temper_total = tempers
    for step in range(1, dp_count):
        swap = [(source, (source + step) % dp_count) for source in range(dp_count)]
        temper_total = temper_total + lax.ppermute(tempers, "dp", swap)
    outs = kernel_call(
        functools.partial(unpack_kernel, half_count=half_count),
        "unpack_heads",
        (within, *across),
        [vmem] * (1 + len(across)),
        [jax.ShapeDtypeStruct(probe_vectors.shape, jnp.bfloat16)] * 3,
        [],
        10,
    )
    return (*outs, temper_total[:, 0] / (dp_count * BLK * seq_count))


def shards(
    probe_vectors,
    lookup_vectors,
    content_vectors,
    result_cotangent,
    logit_softness,
    block_grouping,
    neighborhood_span,
):
    head_count = probe_vectors.shape[2] // HD
    seq_count = lax.axis_size("seq")
    one_block = probe_vectors.shape[1] == BLK
    whole_tiles = seq_count * BLK % (2 * TILE) == 0 and seq_count & (seq_count - 1) == 0
    if head_count == seq_count and one_block and whole_tiles:
        plan = head_shards
    else:
        plan = clustered_shards
    return plan(
        probe_vectors,
        lookup_vectors,
        content_vectors,
        result_cotangent,
        logit_softness,
        block_grouping,
        neighborhood_span,
    )


def solution(mesh):
    in_specs = (
        P("dp", "seq", None),
        P("dp", "seq", None),
        P("dp", "seq", None),
        P("dp", "seq", None),
        P(),
        P("dp", None, None, None),
        P(),
    )
    out_specs = (P("dp", "seq", None), P("dp", "seq", None), P("dp", "seq", None), P())
    return jax.shard_map(shards, mesh=mesh, in_specs=in_specs, out_specs=out_specs, check_vma=False)
```

```python
import functools
import math

import jax
import jax.numpy as jnp
from jax import lax
from jax.experimental import pallas as pl
from jax.experimental.pallas import tpu as pltpu
from jax.sharding import PartitionSpec as P

HD = 128
BLK = 128


blocked_score = -1e30


def shifted(value, axis, steps):
    count = lax.axis_size(axis)
    first, last = (max(0, -steps), min(count, count - steps))
    return lax.ppermute(value, axis, [(source, source + steps) for source in range(first, last)])


def lifted(array_in):
    return lax.optimization_barrier(array_in.astype(jnp.bfloat16)).astype(jnp.float32)


def head_major(tokens_in, block_len):
    token_count, feature_count = tokens_in.shape
    return tokens_in.reshape(
        token_count // block_len, block_len, feature_count // HD, HD
    ).transpose(2, 0, 1, 3)


def token_major(blocks_in):
    head_count, block_count, block_len, depth = blocks_in.shape
    return blocks_in.transpose(1, 2, 0, 3).reshape(1, block_count * block_len, head_count * depth)


def window_parts(query_block, prev_keys, prev_values, grad_block, usable, window_width, temper):
    block_len = query_block.shape[-2]
    inverse_root = 1.0 / math.sqrt(query_block.shape[-1])
    raw_scores = (
        jnp.einsum("...td,...sd->...ts", query_block, prev_keys, preferred_element_type=jnp.float32)
        * inverse_root
    )
    query_pos = lax.broadcasted_iota(jnp.int32, (block_len, block_len), 0)
    key_pos = lax.broadcasted_iota(jnp.int32, (block_len, block_len), 1)
    pair_mask = usable[..., None, None] & (
        key_pos > query_pos + block_len - window_width[..., None, None]
    )
    scores = temper[..., None, None] * raw_scores
    row_top = jnp.max(jnp.where(pair_mask, scores, blocked_score), axis=-1)
    weights = jnp.where(pair_mask, jnp.exp(scores - row_top[..., None]), 0.0)
    prob_grad = jnp.einsum(
        "...td,...sd->...ts", grad_block, prev_values, preferred_element_type=jnp.float32
    )
    return (
        raw_scores,
        pair_mask,
        prob_grad,
        row_top,
        jnp.sum(weights, axis=-1),
        jnp.sum(weights * prob_grad, axis=-1),
    )


def window_grads(
    raw_scores,
    pair_mask,
    prob_grad,
    query_block,
    prev_keys,
    grad_block,
    log_total,
    row_delta,
    temper,
):
    inverse_root = 1.0 / math.sqrt(query_block.shape[-1])
    scaling = (temper * inverse_root)[..., None, None]
    probability = jnp.where(
        pair_mask, jnp.exp(temper[..., None, None] * raw_scores - log_total[..., None]), 0.0
    )
    score_grad = probability * (prob_grad - row_delta[..., None])
    prob_low = probability.astype(jnp.bfloat16)
    grad_low = score_grad.astype(jnp.bfloat16)
    query_part = (
        jnp.einsum("...ts,...sd->...td", grad_low, prev_keys, preferred_element_type=jnp.float32)
        * scaling
    )
    key_part = (
        jnp.einsum("...ts,...td->...sd", grad_low, query_block, preferred_element_type=jnp.float32)
        * scaling
    )
    value_part = jnp.einsum(
        "...ts,...td->...sd", prob_low, grad_block, preferred_element_type=jnp.float32
    )
    temper_part = jnp.sum(score_grad * raw_scores, axis=(-2, -1))
    return (query_part, key_part, value_part, temper_part)


def cluster_pair(
    query_items,
    key_items,
    value_items,
    grad_items,
    live_items,
    temper,
    window_top,
    window_total,
    window_mass,
):
    item_count, block_len, depth = query_items.shape
    row_count = item_count * block_len
    group_rows = 4 * block_len
    inverse_root = 1.0 / math.sqrt(depth)
    scaling = temper * inverse_root
    query_rows = query_items.reshape(row_count, depth)
    key_rows = key_items.reshape(row_count, depth)
    value_rows = value_items.reshape(row_count, depth)
    grad_rows = grad_items.reshape(row_count, depth)
    key_item = jnp.arange(row_count) // block_len
    key_token = jnp.arange(row_count) % block_len
    live_rows = jnp.repeat(live_items, block_len)
    top_rows = window_top.reshape(row_count)
    total_rows = window_total.reshape(row_count)
    mass_rows = window_mass.reshape(row_count)

    def group_step(carry, start_row):
        key_acc, value_acc, temper_acc = carry
        query_group = lax.dynamic_slice_in_dim(query_rows, start_row, group_rows, 0)
        grad_group = lax.dynamic_slice_in_dim(grad_rows, start_row, group_rows, 0)
        group_live = lax.dynamic_slice_in_dim(live_rows, start_row, group_rows, 0)
        group_top = lax.dynamic_slice_in_dim(top_rows, start_row, group_rows, 0)
        group_total = lax.dynamic_slice_in_dim(total_rows, start_row, group_rows, 0)
        group_mass = lax.dynamic_slice_in_dim(mass_rows, start_row, group_rows, 0)
        query_item = (start_row + jnp.arange(group_rows)) // block_len
        query_token = jnp.arange(group_rows) % block_len
        earlier = (key_item[None, :] < query_item[:, None]) | (
            key_item[None, :] == query_item[:, None]
        ) & (key_token[None, :] <= query_token[:, None])
        pair_mask = group_live[:, None] & live_rows[None, :] & earlier
        raw_scores = (
            lax.dot_general(
                query_group, key_rows, (((1,), (1,)), ((), ())), preferred_element_type=jnp.float32
            )
            * inverse_root
        )
        scores = temper * raw_scores
        row_top = jnp.maximum(
            jnp.max(jnp.where(pair_mask, scores, blocked_score), axis=1), group_top
        )
        weights = jnp.where(pair_mask, jnp.exp(scores - row_top[:, None]), 0.0)
        row_total = jnp.sum(weights, axis=1) + group_total * jnp.exp(group_top - row_top)
        log_total = row_top + jnp.log(jnp.where(group_live, row_total, 1.0))
        probability = jnp.where(pair_mask, jnp.exp(scores - log_total[:, None]), 0.0)
        prob_grad = lax.dot_general(
            grad_group, value_rows, (((1,), (1,)), ((), ())), preferred_element_type=jnp.float32
        )
        row_delta = jnp.sum(probability * prob_grad, axis=1) + group_mass * jnp.exp(
            group_top - log_total
        )
        score_grad = probability * (prob_grad - row_delta[:, None])
        prob_low = probability.astype(jnp.bfloat16)
        grad_low = score_grad.astype(jnp.bfloat16)
        query_part = jnp.dot(grad_low, key_rows, preferred_element_type=jnp.float32) * scaling
        key_acc = (
            key_acc
            + lax.dot_general(
                grad_low, query_group, (((0,), (0,)), ((), ())), preferred_element_type=jnp.float32
            )
            * scaling
        )
        value_acc = value_acc + lax.dot_general(
            prob_low, grad_group, (((0,), (0,)), ((), ())), preferred_element_type=jnp.float32
        )
        temper_acc = temper_acc + jnp.sum(score_grad * raw_scores)
        return ((key_acc, value_acc, temper_acc), (query_part, log_total, row_delta))

    start_rows = jnp.arange(item_count // 4) * group_rows
    initial = (
        jnp.zeros((row_count, depth), jnp.float32),
        jnp.zeros((row_count, depth), jnp.float32),
        jnp.zeros((), jnp.float32),
    )
    (key_acc, value_acc, temper_acc), (query_part, log_total, row_delta) = lax.scan(
        group_step, initial, start_rows
    )
    return (
        query_part.reshape(item_count, block_len, depth),
        log_total.reshape(item_count, block_len),
        row_delta.reshape(item_count, block_len),
        key_acc.reshape(item_count, block_len, depth),
        value_acc.reshape(item_count, block_len, depth),
        temper_acc,
    )


def clustered_shards(
    probe_vectors,
    lookup_vectors,
    content_vectors,
    result_cotangent,
    logit_softness,
    block_grouping,
    neighborhood_span,
):
    seq_count = lax.axis_size("seq")
    position = lax.axis_index("seq")
    tokens = probe_vectors.shape[1]
    head_count = probe_vectors.shape[2] // HD
    local_blocks = tokens // BLK
    block_count = local_blocks * seq_count
    cluster_count = max(1, block_count // 8)
    capacity = min(12, block_count)
    owned_pairs = cluster_count * head_count // seq_count
    group_count = cluster_count // owned_pairs
    per_peer = max(1, local_blocks // group_count)
    cluster_ids = block_grouping[0, :, :, 0]
    query_home = head_major(probe_vectors[0], BLK)
    key_home = head_major(lookup_vectors[0], BLK)
    value_home = head_major(content_vectors[0], BLK)
    grad_home = head_major(result_cotangent[0], BLK)
    last_block = (lookup_vectors[0, tokens - BLK :], content_vectors[0, tokens - BLK :])
    prev_key_rows, prev_value_rows = shifted((last_block[0], last_block[1]), "seq", 1)
    prev_keys = jnp.concatenate([head_major(prev_key_rows, BLK), key_home[:, :-1]], axis=1)
    prev_values = jnp.concatenate([head_major(prev_value_rows, BLK), value_home[:, :-1]], axis=1)
    first_block = position * local_blocks
    before = jnp.concatenate(
        [jnp.full((head_count, 1), -1, jnp.int32), cluster_ids[:, :-1]], axis=1
    )
    my_ids = lax.dynamic_slice_in_dim(cluster_ids, first_block, local_blocks, 1)
    my_before = lax.dynamic_slice_in_dim(before, first_block, local_blocks, 1)
    global_block = first_block + jnp.arange(local_blocks)
    usable_home = (global_block[None, :] >= 1) & (my_before != my_ids)
    peer_index = jnp.arange(seq_count)
    peer_head = peer_index * owned_pairs // cluster_count
    slot_range = jnp.arange(per_peer)
    local_range = jnp.arange(local_blocks)
    owner_index = (jnp.arange(head_count)[:, None] * cluster_count + my_ids) // owned_pairs
    peer_ids = jnp.take(my_ids, peer_head, axis=0)
    goes = (peer_head[:, None] * cluster_count + peer_ids) // owned_pairs == peer_index[:, None]
    send_rank = jnp.cumsum(goes.astype(jnp.int32), axis=1) - 1
    send_pick = goes[:, None, :] & (send_rank[:, None, :] == slot_range[None, :, None])
    send_block = jnp.sum(jnp.where(send_pick, local_range[None, None, :], 0), axis=2)
    send_flat = peer_head[:, None] * local_blocks + send_block
    home_rank = jnp.take_along_axis(send_rank, owner_index, axis=0)
    home_pos = owner_index * per_peer + home_rank
    pair_index = position * owned_pairs + jnp.arange(owned_pairs)
    split_for_couple = pair_index // cluster_count
    pair_cluster = pair_index % cluster_count
    my_head = position * owned_pairs // cluster_count
    split_numbers = jnp.take(cluster_ids, my_head, axis=0)
    member = split_numbers[None, :] == pair_cluster[:, None]
    member_rank = jnp.cumsum(member.astype(jnp.int32), axis=1) - 1
    member_count = jnp.sum(member.astype(jnp.int32), axis=1)
    picked = member[:, None, :] & (member_rank[:, None, :] == jnp.arange(capacity)[None, :, None])
    member_block = jnp.sum(jnp.where(picked, jnp.arange(block_count)[None, None, :], 0), axis=2)
    live_members = jnp.arange(capacity)[None, :] < member_count[:, None]
    mine = (my_head * cluster_count + split_numbers) // owned_pairs == position
    mine_grid = mine.reshape(seq_count, local_blocks)
    recv_rank = jnp.cumsum(mine_grid.astype(jnp.int32), axis=1) - 1
    recv_pos = (peer_index[:, None] * per_peer + recv_rank).reshape(block_count)
    member_pos = jnp.take(recv_pos, member_block)
    couple_softness = jnp.take(logit_softness, split_for_couple)
    pair_onehot = (split_for_couple[:, None] == jnp.arange(head_count)[None, :]).astype(jnp.float32)
    slot_pair = my_head * cluster_count + split_numbers - position * owned_pairs
    same_cluster = split_numbers[:, None] == split_numbers[None, :]
    earlier_block = jnp.arange(block_count)[None, :] < jnp.arange(block_count)[:, None]
    slot_rank = jnp.sum((same_cluster & earlier_block).astype(jnp.int32), axis=1)
    back_pos = jnp.clip(slot_pair, 0, owned_pairs - 1) * capacity + jnp.clip(
        slot_rank, 0, capacity - 1
    )
    back_grid = back_pos.reshape(seq_count, local_blocks)
    back_pick = mine_grid[:, None, :] & (recv_rank[:, None, :] == slot_range[None, :, None])
    back_flat = jnp.sum(jnp.where(back_pick, back_grid[:, None, :], 0), axis=2)

    def to_peers(array_in):
        flat = array_in.reshape((head_count * local_blocks,) + array_in.shape[2:])
        return jnp.take(flat, send_flat, axis=0)

    def members(array_in):
        flat = array_in.reshape((seq_count * per_peer,) + array_in.shape[2:])
        return jnp.take(flat, member_pos, axis=0)

    def to_owner(array_in):
        flat = array_in.reshape((owned_pairs * capacity,) + array_in.shape[2:])
        return jnp.take(flat, back_flat, axis=0)

    def from_peers(array_in):
        flat = array_in.reshape((seq_count * per_peer,) + array_in.shape[2:])
        return jnp.take(flat, home_pos, axis=0)

    raw_w, mask_w, pgrad_w, top_w, total_w, mass_w = window_parts(
        query_home,
        prev_keys,
        prev_values,
        grad_home,
        usable_home,
        neighborhood_span[:, None],
        logit_softness[:, None],
    )
    arrived = (
        lax.all_to_all(to_peers(query_home), "seq", split_axis=0, concat_axis=0, tiled=True),
        lax.all_to_all(to_peers(key_home), "seq", split_axis=0, concat_axis=0, tiled=True),
        lax.all_to_all(to_peers(value_home), "seq", split_axis=0, concat_axis=0, tiled=True),
        lax.all_to_all(to_peers(grad_home), "seq", split_axis=0, concat_axis=0, tiled=True),
    )
    arrived_stats = (
        lax.all_to_all(to_peers(top_w), "seq", split_axis=0, concat_axis=0, tiled=True),
        lax.all_to_all(to_peers(total_w), "seq", split_axis=0, concat_axis=0, tiled=True),
        lax.all_to_all(to_peers(mass_w), "seq", split_axis=0, concat_axis=0, tiled=True),
    )
    query_m, key_m, value_m, grad_m = [members(item_in) for item_in in arrived]
    top_m, total_m, mass_m = [members(item_in) for item_in in arrived_stats]

    def split_pair(pair_inputs):
        query_i, key_i, value_i, grad_i, live_i, temper_i, top_i, total_i, mass_i = pair_inputs
        query_c, log_total, row_delta, key_c, value_c, temper_c = cluster_pair(
            query_i, key_i, value_i, grad_i, live_i, temper_i, top_i, total_i, mass_i
        )
        return (
            query_c.astype(jnp.bfloat16),
            key_c.astype(jnp.bfloat16),
            value_c.astype(jnp.bfloat16),
            log_total,
            row_delta,
            temper_c,
        )

    owner_results = lax.map(
        split_pair,
        (query_m, key_m, value_m, grad_m, live_members, couple_softness, top_m, total_m, mass_m),
    )
    returned = (
        lax.all_to_all(to_owner(owner_results[0]), "seq", split_axis=0, concat_axis=0, tiled=True),
        lax.all_to_all(to_owner(owner_results[1]), "seq", split_axis=0, concat_axis=0, tiled=True),
        lax.all_to_all(to_owner(owner_results[2]), "seq", split_axis=0, concat_axis=0, tiled=True),
    )
    returned_stats = (
        lax.all_to_all(to_owner(owner_results[3]), "seq", split_axis=0, concat_axis=0, tiled=True),
        lax.all_to_all(to_owner(owner_results[4]), "seq", split_axis=0, concat_axis=0, tiled=True),
    )
    query_cluster = from_peers(returned[0])
    key_cluster = from_peers(returned[1])
    value_cluster = from_peers(returned[2])
    log_home = from_peers(returned_stats[0])
    delta_home = from_peers(returned_stats[1])
    query_w, key_w, value_w, temper_w = window_grads(
        raw_w,
        mask_w,
        pgrad_w,
        query_home,
        prev_keys,
        grad_home,
        log_home,
        delta_home,
        logit_softness[:, None],
    )
    query_out = (query_cluster.astype(jnp.float32) + lifted(query_w)).astype(jnp.bfloat16)
    key_window = key_w.astype(jnp.bfloat16)
    value_window = value_w.astype(jnp.bfloat16)
    temper_local = jnp.sum(owner_results[5][:, None] * pair_onehot, axis=0) + jnp.sum(
        temper_w, axis=1
    )
    edge_keys, edge_values = shifted((key_window[:, 0], value_window[:, 0]), "seq", -1)
    key_next = jnp.concatenate([key_window[:, 1:], edge_keys[:, None]], axis=1)
    value_next = jnp.concatenate([value_window[:, 1:], edge_values[:, None]], axis=1)
    key_out = (key_cluster.astype(jnp.float32) + key_next.astype(jnp.float32)).astype(jnp.bfloat16)
    value_out = (value_cluster.astype(jnp.float32) + value_next.astype(jnp.float32)).astype(
        jnp.bfloat16
    )
    temper_total = lax.psum(temper_local, ("seq", "dp"))
    temper_grad = temper_total / (lax.axis_size("dp") * tokens * seq_count)
    return (token_major(query_out), token_major(key_out), token_major(value_out), temper_grad)


TILE = 256
EXTRA = 16
MIB = 1024 * 1024
PIECES = 4
QUERY, KEY, VALUE, GRAD = range(4)


def columns_of(index):
    return pl.ds(pl.multiple_of(index * HD, HD), HD)


def rows_of(index):
    return pl.ds(pl.multiple_of(index * BLK, BLK), BLK)


def tile_rows(tile):
    return slice(tile * TILE, (tile + 1) * TILE)


def position(half_count):
    me = lax.axis_index("seq")
    half = jnp.where(me >= half_count, 1, 0)
    return me, half, me - half * half_count


def kernel_call(
    kernel, name, operands, in_specs, out_shape, scratch, vmem_mib, flops=0, out_space=pltpu.VMEM
):
    bytes_accessed = sum(
        math.prod(item.shape) * item.dtype.itemsize for item in (*operands, *out_shape)
    )
    return pl.pallas_call(
        kernel,
        out_shape=out_shape,
        in_specs=in_specs,
        out_specs=[pl.BlockSpec(memory_space=out_space)] * len(out_shape),
        scratch_shapes=scratch,
        cost_estimate=pl.CostEstimate(
            flops=flops, bytes_accessed=bytes_accessed, transcendentals=0
        ),
        compiler_params=pltpu.CompilerParams(vmem_limit_bytes=vmem_mib * MIB),
        name=name,
    )(*operands)


def pack_kernel(*refs, half_count):
    arrays, within_ref, foreign_refs = refs[:4], refs[4], refs[5:7]
    held, within, across, arrival, left_within, left_across = refs[7:]
    me, half, _ = position(half_count)
    piece = BLK // PIECES
    arrivals = [
        [
            pltpu.make_async_copy(
                array_ref.at[0, part * piece : (part + 1) * piece, :],
                held.at[place, part * piece : (part + 1) * piece, :],
                arrival.at[place, part],
            )
            for part in range(PIECES)
        ]
        for place, array_ref in enumerate(arrays)
    ]
    for copies in arrivals:
        for copy in copies:
            copy.start()
    leaving = []
    for place, copies in enumerate(arrivals):
        for copy in copies:
            copy.wait()
        for slot, base in enumerate((half * half_count, (1 - half) * half_count)):
            rows = slice((slot * 4 + place) * BLK, (slot * 4 + place + 1) * BLK)
            for peer in range(half_count):
                within[peer, rows, :] = held[place, :, columns_of(base + peer)]
            leaving.append(
                pltpu.make_async_copy(
                    within.at[:, rows, :], within_ref.at[:, rows, :], left_within.at[place, slot]
                )
            )
            leaving[-1].start()
    first = jnp.where(half == 0, KEY, QUERY)
    second = jnp.where(half == 0, VALUE, GRAD)
    for core, foreign_ref in enumerate(foreign_refs):
        for step in range(half_count // 2):
            columns = columns_of(me ^ core ^ (half_count + 2 * step))
            across[core, step, :BLK, :] = held[first, :, columns]
            across[core, step, BLK:, :] = held[second, :, columns]
        leaving.append(pltpu.make_async_copy(across.at[core], foreign_ref, left_across.at[core]))
        leaving[-1].start()
    for copy in leaving:
        copy.wait()


def packed(arrays, half_count):
    width = arrays[0].shape[2]
    within_shape, across_shape = (half_count, 8 * BLK, HD), (half_count // 2, 2 * BLK, HD)
    return kernel_call(
        functools.partial(pack_kernel, half_count=half_count),
        "pack_heads",
        arrays,
        [pl.BlockSpec(memory_space=pl.ANY)] * 4,
        [jax.ShapeDtypeStruct(within_shape, jnp.bfloat16)]
        + [jax.ShapeDtypeStruct(across_shape, jnp.bfloat16)] * 2,
        [
            pltpu.VMEM((4, BLK, width), jnp.bfloat16),
            pltpu.VMEM(within_shape, jnp.bfloat16),
            pltpu.VMEM((2, *across_shape), jnp.bfloat16),
            pltpu.SemaphoreType.DMA((4, PIECES)),
            pltpu.SemaphoreType.DMA((4, 2)),
            pltpu.SemaphoreType.DMA((2,)),
        ],
        60,
        out_space=pl.ANY,
    )


def dot_rows(left, right):
    return lax.dot_general(
        left, right, (((1,), (1,)), ((), ())), preferred_element_type=jnp.float32
    )


def dot_plain(left, right):
    return lax.dot_general(
        left, right, (((1,), (0,)), ((), ())), preferred_element_type=jnp.float32
    )


def from_blocks(ref, place):
    def rows(start, stop):
        per_tile = TILE // BLK
        return jnp.concatenate(
            [
                ref[block, place * BLK : (place + 1) * BLK, :]
                for block in range(start * per_tile, stop * per_tile)
            ],
            axis=0,
        )

    return rows


def from_array(ref, place):
    return lambda start, stop: ref[place, start * TILE : stop * TILE, :]


class Region:
    def __init__(self, square, sources, tiles, scaling, bias_ref=None, corner_ref=None, first=0):
        self.square, self.sources, self.tiles, self.scaling = square, sources, tiles, scaling
        self.bias_ref, self.corner_ref, self.first = bias_ref, corner_ref, first

    def rows(self, which, start, stop):
        return self.sources[which](start, stop)

    def keys_of(self, tile):
        return range(self.tiles if self.square else tile + 1)

    def scores(self, tile_key, tile_query):
        per_tile = TILE // BLK
        scores = dot_rows(
            self.rows(KEY, tile_key, tile_key + 1), self.rows(QUERY, tile_query, tile_query + 1)
        ) * (self.scaling[:, :1] * math.log2(math.e))
        before = self.tiles * per_tile if self.square else 0
        rows = []
        for sub_key in range(per_tile):
            key_block = tile_key * per_tile + sub_key
            pieces = []
            for sub_query in range(per_tile):
                query_block = tile_query * per_tile + sub_query
                lanes = slice(sub_query * BLK, (sub_query + 1) * BLK)
                piece = scores[sub_key * BLK : (sub_key + 1) * BLK, lanes]
                apart = before + query_block - key_block
                if apart < 0:
                    piece = jnp.full_like(piece, blocked_score)
                elif apart == 0:
                    piece = jnp.where(key_minus_query() <= 0, piece, blocked_score)
                elif apart == 1:
                    piece = piece + self.corner_ref[self.first + (0 if self.square else key_block)]
                else:
                    at = slice(query_block * BLK, (query_block + 1) * BLK)
                    piece = piece + self.bias_ref[key_block : key_block + 1, at]
                pieces.append(piece)
            rows.append(jnp.concatenate(pieces, axis=1))
        return jnp.concatenate(rows, axis=0)


def diagonal(slot, arrived_ref, scales_ref, bias_ref=None, corner_ref=None):
    blocks = arrived_ref.shape[0]
    sources = [from_blocks(arrived_ref, slot * 4 + place) for place in range(4)]
    bias = None if bias_ref is None else bias_ref.at[slot]
    first = slot * (blocks - 1)
    scaling = scales_ref[slot : slot + 1, :]
    return Region(False, sources, blocks * BLK // TILE, scaling, bias, corner_ref, first)


def square(half, arrived_ref, foreign_ref, scales_ref, bias_ref=None, corner_ref=None):
    blocks = arrived_ref.shape[0]
    near = [from_blocks(arrived_ref, place) for place in range(4)]
    far = [from_array(foreign_ref, place) for place in range(2)]
    if half == 0:
        sources = [far[0], near[KEY], near[VALUE], far[1]]
    else:
        sources = [near[QUERY], far[0], far[1], near[GRAD]]
    bias = None if bias_ref is None else bias_ref.at[2]
    first = 2 * (blocks - 1)
    scaling = scales_ref[0:1, :]
    return Region(True, sources, blocks * BLK // TILE, scaling, bias, corner_ref, first)


def key_minus_query():
    shape = (BLK, BLK)
    return lax.broadcasted_iota(jnp.int32, shape, 0) - lax.broadcasted_iota(jnp.int32, shape, 1)


def statistics(region, weight_ref, towards_ref, out_ref, first_row):
    for tile in range(region.tiles):
        here = tile_rows(tile)
        top = jnp.full((1, TILE), blocked_score, jnp.float32)
        for other in region.keys_of(tile):
            raw = region.scores(other, tile)
            weight_ref[tile_rows(other), here] = raw
            top = jnp.maximum(top, jnp.max(raw, axis=0, keepdims=True))
        total = jnp.zeros((1, TILE), jnp.float32)
        mass = jnp.zeros((1, TILE), jnp.float32)
        for other in region.keys_of(tile):
            there = tile_rows(other)
            weight = jnp.exp2(weight_ref[there, here] - top)
            towards = dot_rows(
                region.rows(VALUE, other, other + 1), region.rows(GRAD, tile, tile + 1)
            )
            weight_ref[there, here] = weight
            towards_ref[there, here] = towards
            total += jnp.sum(weight, axis=0, keepdims=True)
            mass += jnp.sum(weight * towards, axis=0, keepdims=True)
        out_ref[first_row : first_row + 1, here] = top
        out_ref[first_row + 1 : first_row + 2, here] = total
        out_ref[first_row + 2 : first_row + 3, here] = mass


def gradients(
    region, weight_ref, towards_ref, top, log_total, delta, prob_low, grad_low, keys_flat
):
    keys_flat[...] = region.rows(KEY, 0, region.tiles).T
    share = jnp.exp2(top - log_total)
    temper = jnp.zeros((1, HD), jnp.float32)
    query_parts, key_parts, value_parts = [], [], []
    for tile in range(region.tiles):
        here = tile_rows(tile)
        for other in region.keys_of(tile):
            there = tile_rows(other)
            probability = weight_ref[there, here] * share[:, here]
            prob_low[there, here] = probability.astype(jnp.bfloat16)
            grad_low[there, here] = (
                probability * (towards_ref[there, here] - delta[:, here])
            ).astype(jnp.bfloat16)
        upto = slice(0, len(region.keys_of(tile)) * TILE)
        query_part = dot_plain(keys_flat[:, upto], grad_low[upto, here]).T
        temper += jnp.sum(
            query_part * region.rows(QUERY, tile, tile + 1).astype(jnp.float32),
            axis=0,
            keepdims=True,
        )
        query_parts.append(query_part)
    for tile in range(region.tiles):
        first = 0 if region.square else tile
        onward = slice(first * TILE, region.tiles * TILE)
        here = tile_rows(tile)
        key_parts.append(
            dot_plain(grad_low[here, onward], region.rows(QUERY, first, region.tiles))
        )
        value_parts.append(
            dot_plain(prob_low[here, onward], region.rows(GRAD, first, region.tiles))
        )
    return query_parts, key_parts, value_parts, temper


def merged(first, second):
    top = jnp.maximum(first[0], second[0])
    left, right = jnp.exp2(first[0] - top), jnp.exp2(second[0] - top)
    total = first[1] * left + second[1] * right
    mass = first[2] * left + second[2] * right
    return top + jnp.log2(total), mass / total


def alone(rows):
    return rows[0] + jnp.log2(rows[1]), rows[2] / rows[1]


def three_rows(ref, first):
    return [ref[first + row : first + row + 1, :] for row in range(3)]


def put(within_ref, array, tile, value):
    per_tile = TILE // BLK
    for sub in range(per_tile):
        within_ref[tile * per_tile + sub, array * BLK : (array + 1) * BLK, :] = value[
            sub * BLK : (sub + 1) * BLK, :
        ].astype(jnp.bfloat16)


def scaled(region, parts):
    return [
        [value * scale for value in part]
        for part, scale in zip(parts, (region.scaling, region.scaling, 1.0))
    ]


def masks_kernel(softness_ref, ids_ref, span_ref, scales_ref, bias_ref, corner_ref, *, half_count):
    me, half, _ = position(half_count)
    base = half * half_count
    regions = (
        (me, base, base),
        (me ^ half_count, base, base),
        (me, 0, half_count),
    )
    for slot, (head, key_base, query_base) in enumerate(regions):
        if slot < 2:
            scales_ref[slot : slot + 1, :] = jnp.full(
                (1, HD), softness_ref[head] * (1.0 / math.sqrt(HD)), jnp.float32
            )

        def same(key_block, query_block):
            return ids_ref[head, key_base + key_block] == ids_ref[head, query_base + query_block]

        def bias(key_block, query_block):
            return jnp.full(
                (1, BLK), jnp.where(same(key_block, query_block), 0.0, blocked_score), jnp.float32
            )

        for key_block in range(half_count):
            bias_ref[slot, key_block : key_block + 1, :] = jnp.concatenate(
                [bias(key_block, query_block) for query_block in range(half_count)], axis=1
            )
        pairs = [(block, block + 1) for block in range(half_count - 1)]
        if slot == 2:
            pairs = [(half_count - 1, 0)]
        for place, pair in enumerate(pairs):
            least = jnp.where(same(*pair), -BLK, BLK - span_ref[head])
            corner_ref[slot * (half_count - 1) + place] = jnp.where(
                key_minus_query() > least, 0.0, blocked_score
            )


def within_kernel(
    arrived_ref, scales_ref, bias_ref, corner_ref, stats_ref, parts_ref, temper_ref,
    own_weight, own_towards, other_weight, other_towards, *scratch, half_count
):
    _, half, _ = position(half_count)
    kept = ((own_weight, own_towards), (other_weight, other_towards))
    for slot in range(2):
        region = diagonal(slot, arrived_ref, scales_ref, bias_ref, corner_ref)
        statistics(region, *kept[slot], stats_ref, slot * 3)
    temper_ref[...] = jnp.zeros_like(temper_ref)

    @pl.when(half == 0)
    def _():
        region = diagonal(0, arrived_ref, scales_ref)
        single = alone(three_rows(stats_ref, 0))
        *parts, temper = gradients(region, *kept[0], stats_ref[0:1, :], *single, *scratch)
        for place, tiles in enumerate(scaled(region, parts)):
            for tile, value in enumerate(tiles):
                parts_ref[place, tile_rows(tile), :] = value
        temper_ref[0:1, :] = temper


def square_kernel(arrived_ref, scales_ref, bias_ref, corner_ref, stats_ref, *refs, half_count):
    across_refs = refs[: half_count // 2]
    foreign_ref, message_ref, square_stats, weight, towards = refs[half_count // 2 :]
    _, half, place = position(half_count)
    for step, across_ref in enumerate(across_refs):
        for core in range(2):
            rows = rows_of(place ^ core ^ (2 * step))
            foreign_ref[0, rows, :] = across_ref[core, :BLK, :]
            foreign_ref[1, rows, :] = across_ref[core, BLK:, :]

    for role in range(2):

        @pl.when(half == role)
        def _():
            region = square(role, arrived_ref, foreign_ref, scales_ref, bias_ref, corner_ref)
            statistics(region, weight, towards, square_stats, 0)
            source, first = ((square_stats, 0), (stats_ref, 3))[role]
            message_ref[0:3, :] = source[first : first + 3, :]


def other_diagonal(arrived_ref, scales_ref, kept, stats_ref, totals, scratch, within_ref):
    region = diagonal(1, arrived_ref, scales_ref)
    *parts, temper = gradients(region, *kept, stats_ref[3:4, :], *totals, *scratch)
    for array, tiles in enumerate(scaled(region, parts)):
        for tile, value in enumerate(tiles):
            put(within_ref, 3 + array, tile, value)
    return temper


def first_kernel(
    arrived_ref, scales_ref, foreign_ref, stats_ref, square_stats, temper_in,
    own_weight, own_towards, other_weight, other_towards, square_weight, square_towards,
    within_ref, across_ref, temper_ref, *scratch, half_count
):
    _, half, _ = position(half_count)
    temper_ref[...] = temper_in[...]

    @pl.when(half == 0)
    def _():
        totals = alone(three_rows(stats_ref, 3))
        kept = (other_weight, other_towards)
        temper_ref[1:2, :] = other_diagonal(
            arrived_ref, scales_ref, kept, stats_ref, totals, scratch, within_ref
        )

    @pl.when(half == 1)
    def _():
        totals = merged(three_rows(stats_ref, 0), three_rows(square_stats, 0))
        region = square(1, arrived_ref, foreign_ref, scales_ref)
        *parts, square_temper = gradients(
            region, square_weight, square_towards, square_stats[0:1, :], *totals, *scratch
        )
        across_query, *foreign = scaled(region, parts)
        for array, tiles in enumerate(foreign):
            for tile, value in enumerate(tiles):
                across_ref[array, tile_rows(tile), :] = value.astype(jnp.bfloat16)
        region = diagonal(0, arrived_ref, scales_ref)
        *parts, temper = gradients(
            region, own_weight, own_towards, stats_ref[0:1, :], *totals, *scratch
        )
        query_parts, key_parts, value_parts = scaled(region, parts)
        for tile in range(region.tiles):
            put(within_ref, 0, tile, query_parts[tile] + across_query[tile])
            put(within_ref, 1, tile, key_parts[tile])
            put(within_ref, 2, tile, value_parts[tile])
        temper_ref[0:1, :] = temper + square_temper


def temper_rows(own, other):
    row = lax.broadcasted_iota(jnp.int32, (EXTRA, HD), 0)
    rows = jnp.zeros((EXTRA, HD), jnp.float32)
    for place, terms in enumerate((own, other)):
        rest = jnp.broadcast_to(jnp.sum(terms, axis=1, keepdims=True), (EXTRA, HD)) * (
            1.0 / math.sqrt(HD)
        )
        for piece in range(3):
            high = rest.astype(jnp.bfloat16).astype(jnp.float32)
            rows = jnp.where(row == place * 3 + piece, high, rows)
            rest = rest - high
    return rows.astype(jnp.bfloat16)


def finish_kernel(
    arrived_ref, scales_ref, foreign_ref, message_ref, received_ref, stats_ref, square_stats,
    parts_ref, temper_ref, square_weight, square_towards, other_weight, other_towards,
    across_ref, begun_ref, within_ref, *refs, half_count
):
    chunk_refs = refs[:2]
    across, temper, done_sem, chunk_sem, *scratch = refs[2:]
    _, half, place = position(half_count)
    temper[...] = temper_ref[...]
    done = pl.ds(pl.multiple_of((1 - half) * 3 * BLK, BLK), 3 * BLK)
    finished = pltpu.make_async_copy(
        begun_ref.at[:, done, :], within_ref.at[:, done, :], done_sem
    )
    finished.start()
    totals = merged(three_rows(message_ref, 0), three_rows(received_ref, 0))

    def chunks():
        for core, chunk_ref in enumerate(chunk_refs):
            for step in range(half_count // 2):
                yield core, step, chunk_ref, rows_of(place ^ core ^ (2 * step))

    @pl.when(half == 0)
    def _():
        region = square(0, arrived_ref, foreign_ref, scales_ref)
        *parts, square_temper = gradients(
            region, square_weight, square_towards, square_stats[0:1, :], *totals, *scratch
        )
        query_parts, key_parts, value_parts = scaled(region, parts)
        for tile in range(region.tiles):
            here = tile_rows(tile)
            across[here, :] = query_parts[tile].astype(jnp.bfloat16)
            put(within_ref, 0, tile, parts_ref[0, here, :])
            put(within_ref, 1, tile, parts_ref[1, here, :] + key_parts[tile])
            put(within_ref, 2, tile, parts_ref[2, here, :] + value_parts[tile])
        for _, step, chunk_ref, rows in chunks():
            chunk_ref[step, :BLK, :] = across[rows, :]
            chunk_ref[step, BLK : 2 * BLK, :] = jnp.zeros((BLK, HD), jnp.bfloat16)
        temper[0:1, :] = temper_ref[0:1, :] + square_temper

    @pl.when(half == 1)
    def _():
        copies = [
            pltpu.make_async_copy(
                across_ref.at[array, rows, :],
                chunk_ref.at[step, array * BLK : (array + 1) * BLK, :],
                chunk_sem.at[core, step, array],
            )
            for core, step, chunk_ref, rows in chunks()
            for array in range(2)
        ]
        for copy in copies:
            copy.start()
        kept = (other_weight, other_towards)
        temper[1:2, :] = other_diagonal(
            arrived_ref, scales_ref, kept, stats_ref, totals, scratch, within_ref
        )
        for copy in copies:
            copy.wait()

    pieces = temper_rows(temper[0:1, :], temper[1:2, :])
    for block in range(half_count):
        within_ref[block, 6 * BLK : 6 * BLK + EXTRA, :] = pieces
    for _, step, chunk_ref, _ in chunks():
        chunk_ref[step, 2 * BLK :, :] = pieces
    finished.wait()


def temper_kernel(within_ref, *refs, half_count):
    across_refs, temper_ref = refs[: half_count // 2], refs[half_count // 2]
    _, half, place = position(half_count)

    def sums(rows):
        return [
            jnp.sum(rows[3 * slot : 3 * slot + 3, :].astype(jnp.float32), axis=0, keepdims=True)
            for slot in range(2)
        ]

    for step, across_ref in enumerate(across_refs):
        for core in range(2):
            peer = place ^ core ^ (2 * step)
            near, far = sums(within_ref[peer]), sums(across_ref[core])
            temper_ref[pl.ds(half * half_count + peer, 1), :] = near[0] + far[1]
            temper_ref[pl.ds((1 - half) * half_count + peer, 1), :] = near[1] + far[0]


def temper_sums(within, across, half_count):
    last = (6 * BLK // EXTRA, 2 * BLK // EXTRA)
    return pl.pallas_call(
        functools.partial(temper_kernel, half_count=half_count),
        grid=(1,),
        out_shape=jax.ShapeDtypeStruct((2 * half_count, HD), jnp.float32),
        in_specs=[pl.BlockSpec((half_count, EXTRA, HD), lambda step: (0, last[0], 0))]
        + [pl.BlockSpec((2, EXTRA, HD), lambda step: (0, last[1], 0))] * (half_count // 2),
        out_specs=pl.BlockSpec((2 * half_count, HD), lambda step: (0, 0)),
        compiler_params=pltpu.CompilerParams(vmem_limit_bytes=4 * MIB),
        name="temper_sums",
    )(within, *across)


def unpack_kernel(within_ref, *refs, half_count):
    across_refs = refs[: half_count // 2]
    out_refs = refs[half_count // 2 :]
    _, half, place = position(half_count)
    for step, across_ref in enumerate(across_refs):
        for core in range(2):
            peer = place ^ core ^ (2 * step)
            other = columns_of((1 - half) * half_count + peer)
            own = columns_of(half * half_count + peer)
            first = across_ref[core, :BLK, :].astype(jnp.float32)
            second = across_ref[core, BLK : 2 * BLK, :].astype(jnp.float32)
            added = (
                jnp.where(half == 0, 0.0, first),
                jnp.where(half == 0, first, 0.0),
                jnp.where(half == 0, second, 0.0),
            )
            for array, out_ref in enumerate(out_refs):
                out_ref[0, :, own] = within_ref[peer, array * BLK : (array + 1) * BLK, :]
                kept = within_ref[peer, (3 + array) * BLK : (4 + array) * BLK, :]
                out_ref[0, :, other] = (kept.astype(jnp.float32) + added[array]).astype(
                    jnp.bfloat16
                )


def join_kernel(kept_ref, taken_ref, *out_refs):
    for step, out_ref in enumerate(out_refs):
        out_ref[0] = kept_ref[step]
        out_ref[1] = taken_ref[step]


def crossed(kept, given, half_count):
    devices = range(2 * half_count)
    steps, *shape = kept.shape
    taken = lax.ppermute(given, "seq", [(source, source ^ 1) for source in devices])
    messages = kernel_call(
        join_kernel,
        "join_chunks",
        (kept, taken),
        [pl.BlockSpec(memory_space=pltpu.VMEM)] * 2,
        [jax.ShapeDtypeStruct((2, *shape), jnp.bfloat16)] * steps,
        [],
        4,
    )
    return [
        lax.ppermute(
            message, "seq", [(source, source ^ (half_count + 2 * step)) for source in devices]
        )
        for step, message in enumerate(messages)
    ]


def head_shards(
    probe_vectors,
    lookup_vectors,
    content_vectors,
    result_cotangent,
    logit_softness,
    block_grouping,
    neighborhood_span,
):
    seq_count, dp_count = lax.axis_size("seq"), lax.axis_size("dp")
    half_count = seq_count // 2
    tokens = half_count * BLK
    groups = [list(range(half_count)), list(range(half_count, seq_count))]
    settings = (logit_softness, block_grouping[0, :, :, 0], neighborhood_span)
    smem, vmem = pl.BlockSpec(memory_space=pltpu.SMEM), pl.BlockSpec(memory_space=pltpu.VMEM)
    lows = [pltpu.VMEM((tokens, tokens), jnp.bfloat16)] * 2 + [
        pltpu.VMEM((HD, tokens), jnp.bfloat16)
    ]
    rows_of_stats = jax.ShapeDtypeStruct((8, tokens), jnp.float32)
    pairs = jax.ShapeDtypeStruct((tokens, tokens), jnp.float32)
    pair_flops = 2 * tokens * tokens * HD

    def exchange_within(array_in):
        return lax.all_to_all(
            array_in, "seq", split_axis=0, concat_axis=0, axis_index_groups=groups, tiled=True
        )

    def call(kernel, name, operands, out_shape, scratch, flops, vmem_mib, scalars=()):
        return kernel_call(
            functools.partial(kernel, half_count=half_count),
            name,
            (*scalars, *operands),
            [smem] * len(scalars) + [vmem] * len(operands),
            out_shape,
            scratch,
            vmem_mib,
            flops,
        )

    sent, *foreign = packed(
        (probe_vectors, lookup_vectors, content_vectors, result_cotangent), half_count
    )
    arrived = exchange_within(sent)
    kept_parts = jax.ShapeDtypeStruct((3, tokens, HD), jnp.float32)
    tempers = jax.ShapeDtypeStruct((8, HD), jnp.float32)
    masks = call(
        masks_kernel,
        "scales_and_masks",
        (),
        [
            jax.ShapeDtypeStruct((8, HD), jnp.float32),
            jax.ShapeDtypeStruct((3, half_count, tokens), jnp.float32),
            jax.ShapeDtypeStruct((2 * half_count - 1, BLK, BLK), jnp.float32),
        ],
        [],
        0,
        6,
        settings,
    )
    foreign[0], *masks = lax.optimization_barrier((foreign[0], *masks))
    foreign = crossed(*foreign, half_count)
    scales = masks[0]
    stats, parts, temper, own_weight, own_towards, other_weight, other_towards = call(
        within_kernel,
        "diagonal_statistics",
        (arrived, *masks),
        [rows_of_stats, kept_parts, tempers] + [pairs] * 4,
        lows,
        2 * pair_flops,
        20,
    )
    far, message, square_stats, square_weight, square_towards = call(
        square_kernel,
        "square_statistics",
        (arrived, *masks, stats, *foreign),
        [jax.ShapeDtypeStruct((2, tokens, HD), jnp.bfloat16)] + [rows_of_stats] * 2 + [pairs] * 2,
        [],
        2 * pair_flops,
        12,
    )
    swap = [(source, source ^ half_count) for source in range(seq_count)]
    received = lax.ppermute(message, "seq", swap)
    begun, across, temper = call(
        first_kernel,
        "gradients_before_totals",
        (
            arrived, scales, far, stats, square_stats, temper, own_weight, own_towards,
            other_weight, other_towards, square_weight, square_towards,
        ),
        [
            jax.ShapeDtypeStruct((half_count, 6 * BLK, HD), jnp.bfloat16),
            jax.ShapeDtypeStruct((2, tokens, HD), jnp.bfloat16),
            tempers,
        ],
        lows,
        4 * pair_flops,
        14,
    )
    within, *foreign = call(
        finish_kernel,
        "gradients_after_totals",
        (
            arrived, scales, far, message, received, stats, square_stats, parts, temper,
            square_weight, square_towards, other_weight, other_towards, across, begun,
        ),
        [jax.ShapeDtypeStruct((half_count, 6 * BLK + EXTRA, HD), jnp.bfloat16)]
        + [jax.ShapeDtypeStruct((half_count // 2, 2 * BLK + EXTRA, HD), jnp.bfloat16)] * 2,
        [
            pltpu.VMEM((tokens, HD), jnp.bfloat16), pltpu.VMEM((8, HD), jnp.float32),
            pltpu.SemaphoreType.DMA, pltpu.SemaphoreType.DMA((2, half_count // 2, 2)), *lows,
        ],
        2 * pair_flops,
        20,
    )
    across = crossed(*foreign, half_count)
    within = exchange_within(within)
    tempers = temper_sums(within, across, half_count)
    temper_total = tempers
    for step in range(1, dp_count):
        swap = [(source, (source + step) % dp_count) for source in range(dp_count)]
        temper_total = temper_total + lax.ppermute(tempers, "dp", swap)
    outs = kernel_call(
        functools.partial(unpack_kernel, half_count=half_count),
        "unpack_heads",
        (within, *across),
        [vmem] * (1 + len(across)),
        [jax.ShapeDtypeStruct(probe_vectors.shape, jnp.bfloat16)] * 3,
        [],
        10,
    )
    return (*outs, temper_total[:, 0] / (dp_count * BLK * seq_count))


def shards(
    probe_vectors,
    lookup_vectors,
    content_vectors,
    result_cotangent,
    logit_softness,
    block_grouping,
    neighborhood_span,
):
    head_count = probe_vectors.shape[2] // HD
    seq_count = lax.axis_size("seq")
    one_block = probe_vectors.shape[1] == BLK
    whole_tiles = seq_count * BLK % (2 * TILE) == 0 and seq_count & (seq_count - 1) == 0
    if head_count == seq_count and one_block and whole_tiles:
        plan = head_shards
    else:
        plan = clustered_shards
    return plan(
        probe_vectors,
        lookup_vectors,
        content_vectors,
        result_cotangent,
        logit_softness,
        block_grouping,
        neighborhood_span,
    )


def solution(mesh):
    in_specs = (
        P("dp", "seq", None),
        P("dp", "seq", None),
        P("dp", "seq", None),
        P("dp", "seq", None),
        P(),
        P("dp", None, None, None),
        P(),
    )
    out_specs = (P("dp", "seq", None), P("dp", "seq", None), P("dp", "seq", None), P())
    return jax.shard_map(shards, mesh=mesh, in_specs=in_specs, out_specs=out_specs, check_vma=False)
```

```python
import functools
import math

import jax
import jax.numpy as jnp
from jax import lax
from jax.experimental import pallas as pl
from jax.experimental.pallas import tpu as pltpu
from jax.sharding import PartitionSpec as P

HD = 128
BLK = 128


blocked_score = -1e30


def shifted(value, axis, steps):
    count = lax.axis_size(axis)
    first, last = (max(0, -steps), min(count, count - steps))
    return lax.ppermute(value, axis, [(source, source + steps) for source in range(first, last)])


def lifted(array_in):
    return lax.optimization_barrier(array_in.astype(jnp.bfloat16)).astype(jnp.float32)


def head_major(tokens_in, block_len):
    token_count, feature_count = tokens_in.shape
    return tokens_in.reshape(
        token_count // block_len, block_len, feature_count // HD, HD
    ).transpose(2, 0, 1, 3)


def token_major(blocks_in):
    head_count, block_count, block_len, depth = blocks_in.shape
    return blocks_in.transpose(1, 2, 0, 3).reshape(1, block_count * block_len, head_count * depth)


def window_parts(query_block, prev_keys, prev_values, grad_block, usable, window_width, temper):
    block_len = query_block.shape[-2]
    inverse_root = 1.0 / math.sqrt(query_block.shape[-1])
    raw_scores = (
        jnp.einsum("...td,...sd->...ts", query_block, prev_keys, preferred_element_type=jnp.float32)
        * inverse_root
    )
    query_pos = lax.broadcasted_iota(jnp.int32, (block_len, block_len), 0)
    key_pos = lax.broadcasted_iota(jnp.int32, (block_len, block_len), 1)
    pair_mask = usable[..., None, None] & (
        key_pos > query_pos + block_len - window_width[..., None, None]
    )
    scores = temper[..., None, None] * raw_scores
    row_top = jnp.max(jnp.where(pair_mask, scores, blocked_score), axis=-1)
    weights = jnp.where(pair_mask, jnp.exp(scores - row_top[..., None]), 0.0)
    prob_grad = jnp.einsum(
        "...td,...sd->...ts", grad_block, prev_values, preferred_element_type=jnp.float32
    )
    return (
        raw_scores,
        pair_mask,
        prob_grad,
        row_top,
        jnp.sum(weights, axis=-1),
        jnp.sum(weights * prob_grad, axis=-1),
    )


def window_grads(
    raw_scores,
    pair_mask,
    prob_grad,
    query_block,
    prev_keys,
    grad_block,
    log_total,
    row_delta,
    temper,
):
    inverse_root = 1.0 / math.sqrt(query_block.shape[-1])
    scaling = (temper * inverse_root)[..., None, None]
    probability = jnp.where(
        pair_mask, jnp.exp(temper[..., None, None] * raw_scores - log_total[..., None]), 0.0
    )
    score_grad = probability * (prob_grad - row_delta[..., None])
    prob_low = probability.astype(jnp.bfloat16)
    grad_low = score_grad.astype(jnp.bfloat16)
    query_part = (
        jnp.einsum("...ts,...sd->...td", grad_low, prev_keys, preferred_element_type=jnp.float32)
        * scaling
    )
    key_part = (
        jnp.einsum("...ts,...td->...sd", grad_low, query_block, preferred_element_type=jnp.float32)
        * scaling
    )
    value_part = jnp.einsum(
        "...ts,...td->...sd", prob_low, grad_block, preferred_element_type=jnp.float32
    )
    temper_part = jnp.sum(score_grad * raw_scores, axis=(-2, -1))
    return (query_part, key_part, value_part, temper_part)


def cluster_pair(
    query_items,
    key_items,
    value_items,
    grad_items,
    live_items,
    temper,
    window_top,
    window_total,
    window_mass,
):
    item_count, block_len, depth = query_items.shape
    row_count = item_count * block_len
    group_rows = 4 * block_len
    inverse_root = 1.0 / math.sqrt(depth)
    scaling = temper * inverse_root
    query_rows = query_items.reshape(row_count, depth)
    key_rows = key_items.reshape(row_count, depth)
    value_rows = value_items.reshape(row_count, depth)
    grad_rows = grad_items.reshape(row_count, depth)
    key_item = jnp.arange(row_count) // block_len
    key_token = jnp.arange(row_count) % block_len
    live_rows = jnp.repeat(live_items, block_len)
    top_rows = window_top.reshape(row_count)
    total_rows = window_total.reshape(row_count)
    mass_rows = window_mass.reshape(row_count)

    def group_step(carry, start_row):
        key_acc, value_acc, temper_acc = carry
        query_group = lax.dynamic_slice_in_dim(query_rows, start_row, group_rows, 0)
        grad_group = lax.dynamic_slice_in_dim(grad_rows, start_row, group_rows, 0)
        group_live = lax.dynamic_slice_in_dim(live_rows, start_row, group_rows, 0)
        group_top = lax.dynamic_slice_in_dim(top_rows, start_row, group_rows, 0)
        group_total = lax.dynamic_slice_in_dim(total_rows, start_row, group_rows, 0)
        group_mass = lax.dynamic_slice_in_dim(mass_rows, start_row, group_rows, 0)
        query_item = (start_row + jnp.arange(group_rows)) // block_len
        query_token = jnp.arange(group_rows) % block_len
        earlier = (key_item[None, :] < query_item[:, None]) | (
            key_item[None, :] == query_item[:, None]
        ) & (key_token[None, :] <= query_token[:, None])
        pair_mask = group_live[:, None] & live_rows[None, :] & earlier
        raw_scores = (
            lax.dot_general(
                query_group, key_rows, (((1,), (1,)), ((), ())), preferred_element_type=jnp.float32
            )
            * inverse_root
        )
        scores = temper * raw_scores
        row_top = jnp.maximum(
            jnp.max(jnp.where(pair_mask, scores, blocked_score), axis=1), group_top
        )
        weights = jnp.where(pair_mask, jnp.exp(scores - row_top[:, None]), 0.0)
        row_total = jnp.sum(weights, axis=1) + group_total * jnp.exp(group_top - row_top)
        log_total = row_top + jnp.log(jnp.where(group_live, row_total, 1.0))
        probability = jnp.where(pair_mask, jnp.exp(scores - log_total[:, None]), 0.0)
        prob_grad = lax.dot_general(
            grad_group, value_rows, (((1,), (1,)), ((), ())), preferred_element_type=jnp.float32
        )
        row_delta = jnp.sum(probability * prob_grad, axis=1) + group_mass * jnp.exp(
            group_top - log_total
        )
        score_grad = probability * (prob_grad - row_delta[:, None])
        prob_low = probability.astype(jnp.bfloat16)
        grad_low = score_grad.astype(jnp.bfloat16)
        query_part = jnp.dot(grad_low, key_rows, preferred_element_type=jnp.float32) * scaling
        key_acc = (
            key_acc
            + lax.dot_general(
                grad_low, query_group, (((0,), (0,)), ((), ())), preferred_element_type=jnp.float32
            )
            * scaling
        )
        value_acc = value_acc + lax.dot_general(
            prob_low, grad_group, (((0,), (0,)), ((), ())), preferred_element_type=jnp.float32
        )
        temper_acc = temper_acc + jnp.sum(score_grad * raw_scores)
        return ((key_acc, value_acc, temper_acc), (query_part, log_total, row_delta))

    start_rows = jnp.arange(item_count // 4) * group_rows
    initial = (
        jnp.zeros((row_count, depth), jnp.float32),
        jnp.zeros((row_count, depth), jnp.float32),
        jnp.zeros((), jnp.float32),
    )
    (key_acc, value_acc, temper_acc), (query_part, log_total, row_delta) = lax.scan(
        group_step, initial, start_rows
    )
    return (
        query_part.reshape(item_count, block_len, depth),
        log_total.reshape(item_count, block_len),
        row_delta.reshape(item_count, block_len),
        key_acc.reshape(item_count, block_len, depth),
        value_acc.reshape(item_count, block_len, depth),
        temper_acc,
    )


def clustered_shards(
    probe_vectors,
    lookup_vectors,
    content_vectors,
    result_cotangent,
    logit_softness,
    block_grouping,
    neighborhood_span,
):
    seq_count = lax.axis_size("seq")
    position = lax.axis_index("seq")
    tokens = probe_vectors.shape[1]
    head_count = probe_vectors.shape[2] // HD
    local_blocks = tokens // BLK
    block_count = local_blocks * seq_count
    cluster_count = max(1, block_count // 8)
    capacity = min(12, block_count)
    owned_pairs = cluster_count * head_count // seq_count
    group_count = cluster_count // owned_pairs
    per_peer = max(1, local_blocks // group_count)
    cluster_ids = block_grouping[0, :, :, 0]
    query_home = head_major(probe_vectors[0], BLK)
    key_home = head_major(lookup_vectors[0], BLK)
    value_home = head_major(content_vectors[0], BLK)
    grad_home = head_major(result_cotangent[0], BLK)
    last_block = (lookup_vectors[0, tokens - BLK :], content_vectors[0, tokens - BLK :])
    prev_key_rows, prev_value_rows = shifted((last_block[0], last_block[1]), "seq", 1)
    prev_keys = jnp.concatenate([head_major(prev_key_rows, BLK), key_home[:, :-1]], axis=1)
    prev_values = jnp.concatenate([head_major(prev_value_rows, BLK), value_home[:, :-1]], axis=1)
    first_block = position * local_blocks
    before = jnp.concatenate(
        [jnp.full((head_count, 1), -1, jnp.int32), cluster_ids[:, :-1]], axis=1
    )
    my_ids = lax.dynamic_slice_in_dim(cluster_ids, first_block, local_blocks, 1)
    my_before = lax.dynamic_slice_in_dim(before, first_block, local_blocks, 1)
    global_block = first_block + jnp.arange(local_blocks)
    usable_home = (global_block[None, :] >= 1) & (my_before != my_ids)
    peer_index = jnp.arange(seq_count)
    peer_head = peer_index * owned_pairs // cluster_count
    slot_range = jnp.arange(per_peer)
    local_range = jnp.arange(local_blocks)
    owner_index = (jnp.arange(head_count)[:, None] * cluster_count + my_ids) // owned_pairs
    peer_ids = jnp.take(my_ids, peer_head, axis=0)
    goes = (peer_head[:, None] * cluster_count + peer_ids) // owned_pairs == peer_index[:, None]
    send_rank = jnp.cumsum(goes.astype(jnp.int32), axis=1) - 1
    send_pick = goes[:, None, :] & (send_rank[:, None, :] == slot_range[None, :, None])
    send_block = jnp.sum(jnp.where(send_pick, local_range[None, None, :], 0), axis=2)
    send_flat = peer_head[:, None] * local_blocks + send_block
    home_rank = jnp.take_along_axis(send_rank, owner_index, axis=0)
    home_pos = owner_index * per_peer + home_rank
    pair_index = position * owned_pairs + jnp.arange(owned_pairs)
    split_for_couple = pair_index // cluster_count
    pair_cluster = pair_index % cluster_count
    my_head = position * owned_pairs // cluster_count
    split_numbers = jnp.take(cluster_ids, my_head, axis=0)
    member = split_numbers[None, :] == pair_cluster[:, None]
    member_rank = jnp.cumsum(member.astype(jnp.int32), axis=1) - 1
    member_count = jnp.sum(member.astype(jnp.int32), axis=1)
    picked = member[:, None, :] & (member_rank[:, None, :] == jnp.arange(capacity)[None, :, None])
    member_block = jnp.sum(jnp.where(picked, jnp.arange(block_count)[None, None, :], 0), axis=2)
    live_members = jnp.arange(capacity)[None, :] < member_count[:, None]
    mine = (my_head * cluster_count + split_numbers) // owned_pairs == position
    mine_grid = mine.reshape(seq_count, local_blocks)
    recv_rank = jnp.cumsum(mine_grid.astype(jnp.int32), axis=1) - 1
    recv_pos = (peer_index[:, None] * per_peer + recv_rank).reshape(block_count)
    member_pos = jnp.take(recv_pos, member_block)
    couple_softness = jnp.take(logit_softness, split_for_couple)
    pair_onehot = (split_for_couple[:, None] == jnp.arange(head_count)[None, :]).astype(jnp.float32)
    slot_pair = my_head * cluster_count + split_numbers - position * owned_pairs
    same_cluster = split_numbers[:, None] == split_numbers[None, :]
    earlier_block = jnp.arange(block_count)[None, :] < jnp.arange(block_count)[:, None]
    slot_rank = jnp.sum((same_cluster & earlier_block).astype(jnp.int32), axis=1)
    back_pos = jnp.clip(slot_pair, 0, owned_pairs - 1) * capacity + jnp.clip(
        slot_rank, 0, capacity - 1
    )
    back_grid = back_pos.reshape(seq_count, local_blocks)
    back_pick = mine_grid[:, None, :] & (recv_rank[:, None, :] == slot_range[None, :, None])
    back_flat = jnp.sum(jnp.where(back_pick, back_grid[:, None, :], 0), axis=2)

    def to_peers(array_in):
        flat = array_in.reshape((head_count * local_blocks,) + array_in.shape[2:])
        return jnp.take(flat, send_flat, axis=0)

    def members(array_in):
        flat = array_in.reshape((seq_count * per_peer,) + array_in.shape[2:])
        return jnp.take(flat, member_pos, axis=0)

    def to_owner(array_in):
        flat = array_in.reshape((owned_pairs * capacity,) + array_in.shape[2:])
        return jnp.take(flat, back_flat, axis=0)

    def from_peers(array_in):
        flat = array_in.reshape((seq_count * per_peer,) + array_in.shape[2:])
        return jnp.take(flat, home_pos, axis=0)

    raw_w, mask_w, pgrad_w, top_w, total_w, mass_w = window_parts(
        query_home,
        prev_keys,
        prev_values,
        grad_home,
        usable_home,
        neighborhood_span[:, None],
        logit_softness[:, None],
    )
    arrived = (
        lax.all_to_all(to_peers(query_home), "seq", split_axis=0, concat_axis=0, tiled=True),
        lax.all_to_all(to_peers(key_home), "seq", split_axis=0, concat_axis=0, tiled=True),
        lax.all_to_all(to_peers(value_home), "seq", split_axis=0, concat_axis=0, tiled=True),
        lax.all_to_all(to_peers(grad_home), "seq", split_axis=0, concat_axis=0, tiled=True),
    )
    arrived_stats = (
        lax.all_to_all(to_peers(top_w), "seq", split_axis=0, concat_axis=0, tiled=True),
        lax.all_to_all(to_peers(total_w), "seq", split_axis=0, concat_axis=0, tiled=True),
        lax.all_to_all(to_peers(mass_w), "seq", split_axis=0, concat_axis=0, tiled=True),
    )
    query_m, key_m, value_m, grad_m = [members(item_in) for item_in in arrived]
    top_m, total_m, mass_m = [members(item_in) for item_in in arrived_stats]

    def split_pair(pair_inputs):
        query_i, key_i, value_i, grad_i, live_i, temper_i, top_i, total_i, mass_i = pair_inputs
        query_c, log_total, row_delta, key_c, value_c, temper_c = cluster_pair(
            query_i, key_i, value_i, grad_i, live_i, temper_i, top_i, total_i, mass_i
        )
        return (
            query_c.astype(jnp.bfloat16),
            key_c.astype(jnp.bfloat16),
            value_c.astype(jnp.bfloat16),
            log_total,
            row_delta,
            temper_c,
        )

    owner_results = lax.map(
        split_pair,
        (query_m, key_m, value_m, grad_m, live_members, couple_softness, top_m, total_m, mass_m),
    )
    returned = (
        lax.all_to_all(to_owner(owner_results[0]), "seq", split_axis=0, concat_axis=0, tiled=True),
        lax.all_to_all(to_owner(owner_results[1]), "seq", split_axis=0, concat_axis=0, tiled=True),
        lax.all_to_all(to_owner(owner_results[2]), "seq", split_axis=0, concat_axis=0, tiled=True),
    )
    returned_stats = (
        lax.all_to_all(to_owner(owner_results[3]), "seq", split_axis=0, concat_axis=0, tiled=True),
        lax.all_to_all(to_owner(owner_results[4]), "seq", split_axis=0, concat_axis=0, tiled=True),
    )
    query_cluster = from_peers(returned[0])
    key_cluster = from_peers(returned[1])
    value_cluster = from_peers(returned[2])
    log_home = from_peers(returned_stats[0])
    delta_home = from_peers(returned_stats[1])
    query_w, key_w, value_w, temper_w = window_grads(
        raw_w,
        mask_w,
        pgrad_w,
        query_home,
        prev_keys,
        grad_home,
        log_home,
        delta_home,
        logit_softness[:, None],
    )
    query_out = (query_cluster.astype(jnp.float32) + lifted(query_w)).astype(jnp.bfloat16)
    key_window = key_w.astype(jnp.bfloat16)
    value_window = value_w.astype(jnp.bfloat16)
    temper_local = jnp.sum(owner_results[5][:, None] * pair_onehot, axis=0) + jnp.sum(
        temper_w, axis=1
    )
    edge_keys, edge_values = shifted((key_window[:, 0], value_window[:, 0]), "seq", -1)
    key_next = jnp.concatenate([key_window[:, 1:], edge_keys[:, None]], axis=1)
    value_next = jnp.concatenate([value_window[:, 1:], edge_values[:, None]], axis=1)
    key_out = (key_cluster.astype(jnp.float32) + key_next.astype(jnp.float32)).astype(jnp.bfloat16)
    value_out = (value_cluster.astype(jnp.float32) + value_next.astype(jnp.float32)).astype(
        jnp.bfloat16
    )
    temper_total = lax.psum(temper_local, ("seq", "dp"))
    temper_grad = temper_total / (lax.axis_size("dp") * tokens * seq_count)
    return (token_major(query_out), token_major(key_out), token_major(value_out), temper_grad)


TILE = 256
EXTRA = 16
MIB = 1024 * 1024
PIECES = 4
QUERY, KEY, VALUE, GRAD = range(4)


def columns_of(index):
    return pl.ds(pl.multiple_of(index * HD, HD), HD)


def rows_of(index):
    return pl.ds(pl.multiple_of(index * BLK, BLK), BLK)


def tile_rows(tile):
    return slice(tile * TILE, (tile + 1) * TILE)


def position(half_count):
    me = lax.axis_index("seq")
    half = jnp.where(me >= half_count, 1, 0)
    return me, half, me - half * half_count


def kernel_call(
    kernel, name, operands, in_specs, out_shape, scratch, vmem_mib, flops=0, out_spaces=None
):
    bytes_accessed = sum(
        math.prod(item.shape) * item.dtype.itemsize for item in (*operands, *out_shape)
    )
    return pl.pallas_call(
        kernel,
        out_shape=out_shape,
        in_specs=in_specs,
        out_specs=[
            pl.BlockSpec(memory_space=space)
            for space in out_spaces or [pltpu.VMEM] * len(out_shape)
        ],
        scratch_shapes=scratch,
        cost_estimate=pl.CostEstimate(
            flops=flops, bytes_accessed=bytes_accessed, transcendentals=0
        ),
        compiler_params=pltpu.CompilerParams(vmem_limit_bytes=vmem_mib * MIB),
        name=name,
    )(*operands)


def pack_kernel(*refs, half_count):
    arrays, within_ref, foreign_refs = refs[:4], refs[4], refs[5:7]
    held, within, across, arrival, left_within, left_across = refs[7:]
    me, half, _ = position(half_count)
    piece = BLK // PIECES
    arrivals = [
        [
            pltpu.make_async_copy(
                array_ref.at[0, part * piece : (part + 1) * piece, :],
                held.at[place, part * piece : (part + 1) * piece, :],
                arrival.at[place, part],
            )
            for part in range(PIECES)
        ]
        for place, array_ref in enumerate(arrays)
    ]
    for copies in arrivals:
        for copy in copies:
            copy.start()
    leaving = []
    for place, copies in enumerate(arrivals):
        for copy in copies:
            copy.wait()
        for slot, base in enumerate((half * half_count, (1 - half) * half_count)):
            rows = slice((slot * 4 + place) * BLK, (slot * 4 + place + 1) * BLK)
            for peer in range(half_count):
                within[peer, rows, :] = held[place, :, columns_of(base + peer)]
            leaving.append(
                pltpu.make_async_copy(
                    within.at[:, rows, :], within_ref.at[:, rows, :], left_within.at[place, slot]
                )
            )
            leaving[-1].start()
    first = jnp.where(half == 0, KEY, QUERY)
    second = jnp.where(half == 0, VALUE, GRAD)
    for core, foreign_ref in enumerate(foreign_refs):
        for step in range(half_count // 2):
            columns = columns_of(me ^ core ^ (half_count + 2 * step))
            across[core, step, :BLK, :] = held[first, :, columns]
            across[core, step, BLK:, :] = held[second, :, columns]
        leaving.append(pltpu.make_async_copy(across.at[core], foreign_ref, left_across.at[core]))
        leaving[-1].start()
    for copy in leaving:
        copy.wait()


def packed(arrays, half_count):
    width = arrays[0].shape[2]
    within_shape, across_shape = (half_count, 8 * BLK, HD), (half_count // 2, 2 * BLK, HD)
    return kernel_call(
        functools.partial(pack_kernel, half_count=half_count),
        "pack_heads",
        arrays,
        [pl.BlockSpec(memory_space=pl.ANY)] * 4,
        [jax.ShapeDtypeStruct(within_shape, jnp.bfloat16)]
        + [jax.ShapeDtypeStruct(across_shape, jnp.bfloat16)] * 2,
        [
            pltpu.VMEM((4, BLK, width), jnp.bfloat16),
            pltpu.VMEM(within_shape, jnp.bfloat16),
            pltpu.VMEM((2, *across_shape), jnp.bfloat16),
            pltpu.SemaphoreType.DMA((4, PIECES)),
            pltpu.SemaphoreType.DMA((4, 2)),
            pltpu.SemaphoreType.DMA((2,)),
        ],
        60,
        out_spaces=[pl.ANY] * 3,
    )


def dot_rows(left, right):
    return lax.dot_general(
        left, right, (((1,), (1,)), ((), ())), preferred_element_type=jnp.float32
    )


def dot_plain(left, right):
    return lax.dot_general(
        left, right, (((1,), (0,)), ((), ())), preferred_element_type=jnp.float32
    )


def from_blocks(ref, place):
    def rows(start, stop):
        per_tile = TILE // BLK
        return jnp.concatenate(
            [
                ref[block, place * BLK : (place + 1) * BLK, :]
                for block in range(start * per_tile, stop * per_tile)
            ],
            axis=0,
        )

    return rows


def from_array(ref, place):
    return lambda start, stop: ref[place, start * TILE : stop * TILE, :]


class Region:
    def __init__(self, square, sources, tiles, scaling, bias_ref=None, corner_ref=None, first=0):
        self.square, self.sources, self.tiles, self.scaling = square, sources, tiles, scaling
        self.bias_ref, self.corner_ref, self.first = bias_ref, corner_ref, first

    def rows(self, which, start, stop):
        return self.sources[which](start, stop)

    def keys_of(self, tile):
        return range(self.tiles if self.square else tile + 1)

    def scores(self, tile_key, tile_query):
        per_tile = TILE // BLK
        scores = dot_rows(
            self.rows(KEY, tile_key, tile_key + 1), self.rows(QUERY, tile_query, tile_query + 1)
        ) * (self.scaling[:, :1] * math.log2(math.e))
        before = self.tiles * per_tile if self.square else 0
        rows = []
        for sub_key in range(per_tile):
            key_block = tile_key * per_tile + sub_key
            pieces = []
            for sub_query in range(per_tile):
                query_block = tile_query * per_tile + sub_query
                lanes = slice(sub_query * BLK, (sub_query + 1) * BLK)
                piece = scores[sub_key * BLK : (sub_key + 1) * BLK, lanes]
                apart = before + query_block - key_block
                if apart < 0:
                    piece = jnp.full_like(piece, blocked_score)
                elif apart == 0:
                    piece = jnp.where(key_minus_query() <= 0, piece, blocked_score)
                elif apart == 1:
                    piece = piece + self.corner_ref[self.first + (0 if self.square else key_block)]
                else:
                    at = slice(query_block * BLK, (query_block + 1) * BLK)
                    piece = piece + self.bias_ref[key_block : key_block + 1, at]
                pieces.append(piece)
            rows.append(jnp.concatenate(pieces, axis=1))
        return jnp.concatenate(rows, axis=0)


def diagonal(slot, arrived_ref, scales_ref, bias_ref=None, corner_ref=None):
    blocks = arrived_ref.shape[0]
    sources = [from_blocks(arrived_ref, slot * 4 + place) for place in range(4)]
    bias = None if bias_ref is None else bias_ref.at[slot]
    first = slot * (blocks - 1)
    scaling = scales_ref[slot : slot + 1, :]
    return Region(False, sources, blocks * BLK // TILE, scaling, bias, corner_ref, first)


def square(square_ref, scales_ref, bias_ref=None, corner_ref=None):
    tiles = square_ref.shape[1] // TILE
    sources = [from_array(square_ref, place) for place in range(4)]
    bias = None if bias_ref is None else bias_ref.at[2]
    first = 2 * (tiles * TILE // BLK - 1)
    return Region(True, sources, tiles, scales_ref[0:1, :], bias, corner_ref, first)


def key_minus_query():
    shape = (BLK, BLK)
    return lax.broadcasted_iota(jnp.int32, shape, 0) - lax.broadcasted_iota(jnp.int32, shape, 1)


def statistics(region, weight_ref, towards_ref, out_ref, first_row):
    for tile in range(region.tiles):
        here = tile_rows(tile)
        top = jnp.full((1, TILE), blocked_score, jnp.float32)
        for other in region.keys_of(tile):
            raw = region.scores(other, tile)
            weight_ref[tile_rows(other), here] = raw
            top = jnp.maximum(top, jnp.max(raw, axis=0, keepdims=True))
        total = jnp.zeros((1, TILE), jnp.float32)
        mass = jnp.zeros((1, TILE), jnp.float32)
        for other in region.keys_of(tile):
            there = tile_rows(other)
            weight = jnp.exp2(weight_ref[there, here] - top)
            towards = dot_rows(
                region.rows(VALUE, other, other + 1), region.rows(GRAD, tile, tile + 1)
            )
            weight_ref[there, here] = weight
            towards_ref[there, here] = towards
            total += jnp.sum(weight, axis=0, keepdims=True)
            mass += jnp.sum(weight * towards, axis=0, keepdims=True)
        out_ref[first_row : first_row + 1, here] = top
        out_ref[first_row + 1 : first_row + 2, here] = total
        out_ref[first_row + 2 : first_row + 3, here] = mass


def gradients(
    region, weight_ref, towards_ref, top, log_total, delta, prob_low, grad_low, keys_flat, emit=None
):
    keys_flat[...] = region.rows(KEY, 0, region.tiles).T
    share = jnp.exp2(top - log_total)
    temper = jnp.zeros((1, HD), jnp.float32)
    query_parts, key_parts, value_parts = [], [], []
    for tile in range(region.tiles):
        here = tile_rows(tile)
        for other in region.keys_of(tile):
            there = tile_rows(other)
            probability = weight_ref[there, here] * share[:, here]
            prob_low[there, here] = probability.astype(jnp.bfloat16)
            grad_low[there, here] = (
                probability * (towards_ref[there, here] - delta[:, here])
            ).astype(jnp.bfloat16)
        upto = slice(0, len(region.keys_of(tile)) * TILE)
        query_part = dot_plain(keys_flat[:, upto], grad_low[upto, here]).T
        temper += jnp.sum(
            query_part * region.rows(QUERY, tile, tile + 1).astype(jnp.float32),
            axis=0,
            keepdims=True,
        )
        query_parts.append(query_part)
    if emit is not None:
        emit(QUERY, query_parts)
    for low, which, parts in ((grad_low, QUERY, key_parts), (prob_low, GRAD, value_parts)):
        for tile in range(region.tiles):
            first = 0 if region.square else tile
            onward = slice(first * TILE, region.tiles * TILE)
            parts.append(
                dot_plain(low[tile_rows(tile), onward], region.rows(which, first, region.tiles))
            )
        if emit is not None:
            emit(KEY if which == QUERY else VALUE, parts)
    return query_parts, key_parts, value_parts, temper


def merged(first, second):
    top = jnp.maximum(first[0], second[0])
    left, right = jnp.exp2(first[0] - top), jnp.exp2(second[0] - top)
    total = first[1] * left + second[1] * right
    mass = first[2] * left + second[2] * right
    return top + jnp.log2(total), mass / total


def alone(rows):
    return rows[0] + jnp.log2(rows[1]), rows[2] / rows[1]


def three_rows(ref, first):
    return [ref[first + row : first + row + 1, :] for row in range(3)]


def put(within_ref, array, tile, value):
    per_tile = TILE // BLK
    for sub in range(per_tile):
        within_ref[tile * per_tile + sub, array * BLK : (array + 1) * BLK, :] = value[
            sub * BLK : (sub + 1) * BLK, :
        ].astype(jnp.bfloat16)


def scaled(region, parts):
    return [
        [value * scale for value in part]
        for part, scale in zip(parts, (region.scaling, region.scaling, 1.0))
    ]


def masks_kernel(softness_ref, ids_ref, span_ref, scales_ref, bias_ref, corner_ref, *, half_count):
    me, half, _ = position(half_count)
    base = half * half_count
    regions = (
        (me, base, base),
        (me ^ half_count, base, base),
        (me, 0, half_count),
    )
    for slot, (head, key_base, query_base) in enumerate(regions):
        if slot < 2:
            scales_ref[slot : slot + 1, :] = jnp.full(
                (1, HD), softness_ref[head] * (1.0 / math.sqrt(HD)), jnp.float32
            )

        def same(key_block, query_block):
            return ids_ref[head, key_base + key_block] == ids_ref[head, query_base + query_block]

        def bias(key_block, query_block):
            return jnp.full(
                (1, BLK), jnp.where(same(key_block, query_block), 0.0, blocked_score), jnp.float32
            )

        for key_block in range(half_count):
            bias_ref[slot, key_block : key_block + 1, :] = jnp.concatenate(
                [bias(key_block, query_block) for query_block in range(half_count)], axis=1
            )
        pairs = [(block, block + 1) for block in range(half_count - 1)]
        if slot == 2:
            pairs = [(half_count - 1, 0)]
        for place, pair in enumerate(pairs):
            least = jnp.where(same(*pair), -BLK, BLK - span_ref[head])
            corner_ref[slot * (half_count - 1) + place] = jnp.where(
                key_minus_query() > least, 0.0, blocked_score
            )


def within_kernel(
    arrived_ref, scales_ref, bias_ref, corner_ref, stats_ref, parts_ref, temper_ref,
    own_weight, own_towards, other_weight, other_towards, *scratch, half_count
):
    _, half, _ = position(half_count)
    kept = ((own_weight, own_towards), (other_weight, other_towards))
    for slot in range(2):
        region = diagonal(slot, arrived_ref, scales_ref, bias_ref, corner_ref)
        statistics(region, *kept[slot], stats_ref, slot * 3)
    temper_ref[...] = jnp.zeros_like(temper_ref)

    @pl.when(half == 0)
    def _():
        region = diagonal(0, arrived_ref, scales_ref)
        single = alone(three_rows(stats_ref, 0))
        *parts, temper = gradients(region, *kept[0], stats_ref[0:1, :], *single, *scratch)
        for place, tiles in enumerate(scaled(region, parts)):
            for tile, value in enumerate(tiles):
                parts_ref[place, tile_rows(tile), :] = value
        temper_ref[0:1, :] = temper


def square_kernel(arrived_ref, scales_ref, bias_ref, corner_ref, stats_ref, *refs, half_count):
    across_refs = refs[: half_count // 2]
    square_ref, message_ref, square_stats, weight, towards = refs[half_count // 2 :]
    _, half, place = position(half_count)
    first = jnp.where(half == 0, QUERY, KEY)
    second = jnp.where(half == 0, GRAD, VALUE)
    for step, across_ref in enumerate(across_refs):
        for core in range(2):
            rows = rows_of(place ^ core ^ (2 * step))
            square_ref[first, rows, :] = across_ref[core, :BLK, :]
            square_ref[second, rows, :] = across_ref[core, BLK:, :]
    for kept in (jnp.where(half == 0, KEY, QUERY), jnp.where(half == 0, VALUE, GRAD)):
        for block in range(half_count):
            square_ref[kept, block * BLK : (block + 1) * BLK, :] = arrived_ref[
                block, rows_of(kept), :
            ]
    region = square(square_ref, scales_ref, bias_ref, corner_ref)
    statistics(region, weight, towards, square_stats, 0)
    for row in range(3):
        message_ref[row : row + 1, :] = jnp.where(
            half == 0, square_stats[row : row + 1, :], stats_ref[3 + row : 4 + row, :]
        )


def first_kernel(
    arrived_ref, scales_ref, square_ref, stats_ref, square_stats, temper_in,
    own_weight, own_towards, other_weight, other_towards, square_weight, square_towards,
    within_ref, across_ref, temper_ref, *scratch, half_count
):
    _, half, _ = position(half_count)
    temper_ref[...] = temper_in[...]

    @pl.when(half == 0)
    def _():
        region = diagonal(1, arrived_ref, scales_ref)
        totals = alone(three_rows(stats_ref, 3))
        *parts, temper_ref[1:2, :] = gradients(
            region, other_weight, other_towards, stats_ref[3:4, :], *totals, *scratch
        )
        for array, tiles in enumerate(scaled(region, parts)):
            for tile, value in enumerate(tiles):
                put(within_ref, array, tile, value)

    @pl.when(half == 1)
    def _():
        totals = merged(three_rows(stats_ref, 0), three_rows(square_stats, 0))
        region = square(square_ref, scales_ref)
        *parts, square_temper = gradients(
            region, square_weight, square_towards, square_stats[0:1, :], *totals, *scratch
        )
        across_query, *foreign = scaled(region, parts)
        for array, tiles in enumerate(foreign):
            for tile, value in enumerate(tiles):
                across_ref[array, tile_rows(tile), :] = value.astype(jnp.bfloat16)
        region = diagonal(0, arrived_ref, scales_ref)
        *parts, temper = gradients(
            region, own_weight, own_towards, stats_ref[0:1, :], *totals, *scratch
        )
        query_parts, key_parts, value_parts = scaled(region, parts)
        for tile in range(region.tiles):
            put(within_ref, 0, tile, query_parts[tile] + across_query[tile])
            put(within_ref, 1, tile, key_parts[tile])
            put(within_ref, 2, tile, value_parts[tile])
        temper_ref[0:1, :] = temper + square_temper


def temper_rows(own, other):
    row = lax.broadcasted_iota(jnp.int32, (EXTRA, HD), 0)
    rows = jnp.zeros((EXTRA, HD), jnp.float32)
    for place, terms in enumerate((own, other)):
        rest = jnp.broadcast_to(jnp.sum(terms, axis=1, keepdims=True), (EXTRA, HD)) * (
            1.0 / math.sqrt(HD)
        )
        for piece in range(3):
            high = rest.astype(jnp.bfloat16).astype(jnp.float32)
            rows = jnp.where(row == place * 3 + piece, high, rows)
            rest = rest - high
    return rows.astype(jnp.bfloat16)


def finish_kernel(
    arrived_ref, scales_ref, square_ref, message_ref, received_ref, stats_ref, square_stats,
    parts_ref, temper_ref, square_weight, square_towards, other_weight, other_towards,
    across_ref, begun_ref, within_ref, *refs, half_count
):
    chunk_refs = refs[:2]
    across, temper, ready, tail, begun_sem, ready_sem, tail_sem, chunk_sem, *scratch = refs[2:]
    _, half, place = position(half_count)
    temper[...] = temper_ref[...]
    begun_at = pl.ds(pl.multiple_of((1 - half) * 3 * BLK, BLK), 3 * BLK)
    leaving = [pltpu.make_async_copy(begun_ref, within_ref.at[:, begun_at, :], begun_sem)]
    leaving[0].start()
    for array in range(3):
        rows = slice(array * BLK, (array + 1) * BLK)
        to = pl.ds(pl.multiple_of((half * 3 + array) * BLK, BLK), BLK)
        leaving.append(
            pltpu.make_async_copy(
                ready.at[:, rows, :], within_ref.at[:, to, :], ready_sem.at[array]
            )
        )
    totals = merged(three_rows(message_ref, 0), three_rows(received_ref, 0))

    def chunks():
        for core, chunk_ref in enumerate(chunk_refs):
            for step in range(half_count // 2):
                yield core, step, chunk_ref, rows_of(place ^ core ^ (2 * step))

    @pl.when(half == 0)
    def _():
        region = square(square_ref, scales_ref)

        def send(array, parts):
            for tile, part in enumerate(parts):
                here = tile_rows(tile)
                if array == QUERY:
                    across[here, :] = (part * region.scaling).astype(jnp.bfloat16)
                    put(ready, array, tile, parts_ref[array, here, :])
                else:
                    scale = region.scaling if array == KEY else 1.0
                    put(ready, array, tile, parts_ref[array, here, :] + part * scale)
            leaving[1 + array].start()

        *_, square_temper = gradients(
            region, square_weight, square_towards, square_stats[0:1, :], *totals, *scratch, emit=send
        )
        for _, step, chunk_ref, rows in chunks():
            chunk_ref[step, :BLK, :] = across[rows, :]
            chunk_ref[step, BLK : 2 * BLK, :] = jnp.zeros((BLK, HD), jnp.bfloat16)
        temper[0:1, :] = temper_ref[0:1, :] + square_temper

    @pl.when(half == 1)
    def _():
        copies = [
            pltpu.make_async_copy(
                across_ref.at[array, rows, :],
                chunk_ref.at[step, array * BLK : (array + 1) * BLK, :],
                chunk_sem.at[core, step, array],
            )
            for core, step, chunk_ref, rows in chunks()
            for array in range(2)
        ]
        for copy in copies:
            copy.start()
        region = diagonal(1, arrived_ref, scales_ref)

        def send(array, parts):
            scale = 1.0 if array == VALUE else region.scaling
            for tile, part in enumerate(parts):
                put(ready, array, tile, part * scale)
            leaving[1 + array].start()

        *_, temper[1:2, :] = gradients(
            region, other_weight, other_towards, stats_ref[3:4, :], *totals, *scratch, emit=send
        )
        for copy in copies:
            copy.wait()

    pieces = temper_rows(temper[0:1, :], temper[1:2, :])
    for block in range(half_count):
        tail[block] = pieces
    leaving.append(
        pltpu.make_async_copy(tail, within_ref.at[:, 6 * BLK : 6 * BLK + EXTRA, :], tail_sem)
    )
    leaving[-1].start()
    for _, step, chunk_ref, _ in chunks():
        chunk_ref[step, 2 * BLK :, :] = pieces
    for copy in leaving:
        copy.wait()


def temper_kernel(within_ref, *refs, half_count):
    across_refs, temper_ref = refs[: half_count // 2], refs[half_count // 2]
    _, half, place = position(half_count)

    def sums(rows):
        return [
            jnp.sum(rows[3 * slot : 3 * slot + 3, :].astype(jnp.float32), axis=0, keepdims=True)
            for slot in range(2)
        ]

    for step, across_ref in enumerate(across_refs):
        for core in range(2):
            peer = place ^ core ^ (2 * step)
            near, far = sums(within_ref[peer]), sums(across_ref[core])
            temper_ref[pl.ds(half * half_count + peer, 1), :] = near[0] + far[1]
            temper_ref[pl.ds((1 - half) * half_count + peer, 1), :] = near[1] + far[0]


def temper_sums(within, across, half_count):
    last = (6 * BLK // EXTRA, 2 * BLK // EXTRA)
    return pl.pallas_call(
        functools.partial(temper_kernel, half_count=half_count),
        grid=(1,),
        out_shape=jax.ShapeDtypeStruct((2 * half_count, HD), jnp.float32),
        in_specs=[pl.BlockSpec((half_count, EXTRA, HD), lambda step: (0, last[0], 0))]
        + [pl.BlockSpec((2, EXTRA, HD), lambda step: (0, last[1], 0))] * (half_count // 2),
        out_specs=pl.BlockSpec((2 * half_count, HD), lambda step: (0, 0)),
        compiler_params=pltpu.CompilerParams(vmem_limit_bytes=4 * MIB),
        name="temper_sums",
    )(within, *across)


def unpack_kernel(within_ref, *refs, half_count):
    across_refs = refs[: half_count // 2]
    out_refs = refs[half_count // 2 :]
    _, half, place = position(half_count)
    for step, across_ref in enumerate(across_refs):
        for core in range(2):
            peer = place ^ core ^ (2 * step)
            other = columns_of((1 - half) * half_count + peer)
            own = columns_of(half * half_count + peer)
            first = across_ref[core, :BLK, :].astype(jnp.float32)
            second = across_ref[core, BLK : 2 * BLK, :].astype(jnp.float32)
            added = (
                jnp.where(half == 0, 0.0, first),
                jnp.where(half == 0, first, 0.0),
                jnp.where(half == 0, second, 0.0),
            )
            for array, out_ref in enumerate(out_refs):
                out_ref[0, :, own] = within_ref[peer, array * BLK : (array + 1) * BLK, :]
                kept = within_ref[peer, (3 + array) * BLK : (4 + array) * BLK, :]
                out_ref[0, :, other] = (kept.astype(jnp.float32) + added[array]).astype(
                    jnp.bfloat16
                )


def join_kernel(kept_ref, taken_ref, *out_refs):
    for step, out_ref in enumerate(out_refs):
        out_ref[0] = kept_ref[step]
        out_ref[1] = taken_ref[step]


def crossed(kept, given, half_count):
    devices = range(2 * half_count)
    steps, *shape = kept.shape
    taken = lax.ppermute(given, "seq", [(source, source ^ 1) for source in devices])
    messages = kernel_call(
        join_kernel,
        "join_chunks",
        (kept, taken),
        [pl.BlockSpec(memory_space=pltpu.VMEM)] * 2,
        [jax.ShapeDtypeStruct((2, *shape), jnp.bfloat16)] * steps,
        [],
        4,
    )
    return [
        lax.ppermute(
            message, "seq", [(source, source ^ (half_count + 2 * step)) for source in devices]
        )
        for step, message in enumerate(messages)
    ]


def head_shards(
    probe_vectors,
    lookup_vectors,
    content_vectors,
    result_cotangent,
    logit_softness,
    block_grouping,
    neighborhood_span,
):
    seq_count, dp_count = lax.axis_size("seq"), lax.axis_size("dp")
    half_count = seq_count // 2
    tokens = half_count * BLK
    groups = [list(range(half_count)), list(range(half_count, seq_count))]
    settings = (logit_softness, block_grouping[0, :, :, 0], neighborhood_span)
    smem, vmem = pl.BlockSpec(memory_space=pltpu.SMEM), pl.BlockSpec(memory_space=pltpu.VMEM)
    lows = [pltpu.VMEM((tokens, tokens), jnp.bfloat16)] * 2 + [
        pltpu.VMEM((HD, tokens), jnp.bfloat16)
    ]
    rows_of_stats = jax.ShapeDtypeStruct((8, tokens), jnp.float32)
    pairs = jax.ShapeDtypeStruct((tokens, tokens), jnp.float32)
    pair_flops = 2 * tokens * tokens * HD

    def exchange_within(array_in):
        return lax.all_to_all(
            array_in, "seq", split_axis=0, concat_axis=0, axis_index_groups=groups, tiled=True
        )

    def call(
        kernel, name, operands, out_shape, scratch, flops, vmem_mib, scalars=(), out_spaces=None
    ):
        return kernel_call(
            functools.partial(kernel, half_count=half_count),
            name,
            (*scalars, *operands),
            [smem] * len(scalars) + [vmem] * len(operands),
            out_shape,
            scratch,
            vmem_mib,
            flops,
            out_spaces,
        )

    sent, *foreign = packed(
        (probe_vectors, lookup_vectors, content_vectors, result_cotangent), half_count
    )
    arrived = exchange_within(sent)
    kept_parts = jax.ShapeDtypeStruct((3, tokens, HD), jnp.float32)
    tempers = jax.ShapeDtypeStruct((8, HD), jnp.float32)
    masks = call(
        masks_kernel,
        "scales_and_masks",
        (),
        [
            jax.ShapeDtypeStruct((8, HD), jnp.float32),
            jax.ShapeDtypeStruct((3, half_count, tokens), jnp.float32),
            jax.ShapeDtypeStruct((2 * half_count - 1, BLK, BLK), jnp.float32),
        ],
        [],
        0,
        6,
        settings,
    )
    foreign[0], *masks = lax.optimization_barrier((foreign[0], *masks))
    foreign = crossed(*foreign, half_count)
    scales = masks[0]
    stats, parts, temper, own_weight, own_towards, other_weight, other_towards = call(
        within_kernel,
        "diagonal_statistics",
        (arrived, *masks),
        [rows_of_stats, kept_parts, tempers] + [pairs] * 4,
        lows,
        2 * pair_flops,
        20,
    )
    squared, message, square_stats, square_weight, square_towards = call(
        square_kernel,
        "square_statistics",
        (arrived, *masks, stats, *foreign),
        [jax.ShapeDtypeStruct((4, tokens, HD), jnp.bfloat16)] + [rows_of_stats] * 2 + [pairs] * 2,
        [],
        2 * pair_flops,
        12,
    )
    swap = [(source, source ^ half_count) for source in range(seq_count)]
    received = lax.ppermute(message, "seq", swap)
    begun, across, temper = call(
        first_kernel,
        "gradients_before_totals",
        (
            arrived, scales, squared, stats, square_stats, temper, own_weight, own_towards,
            other_weight, other_towards, square_weight, square_towards,
        ),
        [
            jax.ShapeDtypeStruct((half_count, 3 * BLK, HD), jnp.bfloat16),
            jax.ShapeDtypeStruct((2, tokens, HD), jnp.bfloat16),
            tempers,
        ],
        lows,
        4 * pair_flops,
        14,
    )
    within, *foreign = call(
        finish_kernel,
        "gradients_after_totals",
        (
            arrived, scales, squared, message, received, stats, square_stats, parts, temper,
            square_weight, square_towards, other_weight, other_towards, across, begun,
        ),
        [pltpu.HBM((half_count, 6 * BLK + EXTRA, HD), jnp.bfloat16)]
        + [jax.ShapeDtypeStruct((half_count // 2, 2 * BLK + EXTRA, HD), jnp.bfloat16)] * 2,
        [
            pltpu.VMEM((tokens, HD), jnp.bfloat16), pltpu.VMEM((8, HD), jnp.float32),
            pltpu.VMEM((half_count, 3 * BLK, HD), jnp.bfloat16),
            pltpu.VMEM((half_count, EXTRA, HD), jnp.bfloat16),
            pltpu.SemaphoreType.DMA, pltpu.SemaphoreType.DMA((3,)), pltpu.SemaphoreType.DMA,
            pltpu.SemaphoreType.DMA((2, half_count // 2, 2)), *lows,
        ],
        2 * pair_flops,
        20,
        out_spaces=(pl.ANY, pltpu.VMEM, pltpu.VMEM),
    )
    across = crossed(*foreign, half_count)
    within = exchange_within(within)
    tempers = temper_sums(within, across, half_count)
    temper_total = tempers
    for step in range(1, dp_count):
        swap = [(source, (source + step) % dp_count) for source in range(dp_count)]
        temper_total = temper_total + lax.ppermute(tempers, "dp", swap)
    outs = kernel_call(
        functools.partial(unpack_kernel, half_count=half_count),
        "unpack_heads",
        (within, *across),
        [vmem] * (1 + len(across)),
        [jax.ShapeDtypeStruct(probe_vectors.shape, jnp.bfloat16)] * 3,
        [],
        10,
    )
    return (*outs, temper_total[:, 0] / (dp_count * BLK * seq_count))


def shards(
    probe_vectors,
    lookup_vectors,
    content_vectors,
    result_cotangent,
    logit_softness,
    block_grouping,
    neighborhood_span,
):
    head_count = probe_vectors.shape[2] // HD
    seq_count = lax.axis_size("seq")
    one_block = probe_vectors.shape[1] == BLK
    whole_tiles = seq_count * BLK % (2 * TILE) == 0 and seq_count & (seq_count - 1) == 0
    if head_count == seq_count and one_block and whole_tiles:
        plan = head_shards
    else:
        plan = clustered_shards
    return plan(
        probe_vectors,
        lookup_vectors,
        content_vectors,
        result_cotangent,
        logit_softness,
        block_grouping,
        neighborhood_span,
    )


def solution(mesh):
    in_specs = (
        P("dp", "seq", None),
        P("dp", "seq", None),
        P("dp", "seq", None),
        P("dp", "seq", None),
        P(),
        P("dp", None, None, None),
        P(),
    )
    out_specs = (P("dp", "seq", None), P("dp", "seq", None), P("dp", "seq", None), P())
    return jax.shard_map(shards, mesh=mesh, in_specs=in_specs, out_specs=out_specs, check_vma=False)
```

```python
import functools
import math

import jax
import jax.numpy as jnp
from jax import lax
from jax.experimental import pallas as pl
from jax.experimental.pallas import tpu as pltpu
from jax.sharding import PartitionSpec as P

HD = 128
BLK = 128


blocked_score = -1e30


def shifted(value, axis, steps):
    count = lax.axis_size(axis)
    first, last = (max(0, -steps), min(count, count - steps))
    return lax.ppermute(value, axis, [(source, source + steps) for source in range(first, last)])


def lifted(array_in):
    return lax.optimization_barrier(array_in.astype(jnp.bfloat16)).astype(jnp.float32)


def head_major(tokens_in, block_len):
    token_count, feature_count = tokens_in.shape
    return tokens_in.reshape(
        token_count // block_len, block_len, feature_count // HD, HD
    ).transpose(2, 0, 1, 3)


def token_major(blocks_in):
    head_count, block_count, block_len, depth = blocks_in.shape
    return blocks_in.transpose(1, 2, 0, 3).reshape(1, block_count * block_len, head_count * depth)


def window_parts(query_block, prev_keys, prev_values, grad_block, usable, window_width, temper):
    block_len = query_block.shape[-2]
    inverse_root = 1.0 / math.sqrt(query_block.shape[-1])
    raw_scores = (
        jnp.einsum("...td,...sd->...ts", query_block, prev_keys, preferred_element_type=jnp.float32)
        * inverse_root
    )
    query_pos = lax.broadcasted_iota(jnp.int32, (block_len, block_len), 0)
    key_pos = lax.broadcasted_iota(jnp.int32, (block_len, block_len), 1)
    pair_mask = usable[..., None, None] & (
        key_pos > query_pos + block_len - window_width[..., None, None]
    )
    scores = temper[..., None, None] * raw_scores
    row_top = jnp.max(jnp.where(pair_mask, scores, blocked_score), axis=-1)
    weights = jnp.where(pair_mask, jnp.exp(scores - row_top[..., None]), 0.0)
    prob_grad = jnp.einsum(
        "...td,...sd->...ts", grad_block, prev_values, preferred_element_type=jnp.float32
    )
    return (
        raw_scores,
        pair_mask,
        prob_grad,
        row_top,
        jnp.sum(weights, axis=-1),
        jnp.sum(weights * prob_grad, axis=-1),
    )


def window_grads(
    raw_scores,
    pair_mask,
    prob_grad,
    query_block,
    prev_keys,
    grad_block,
    log_total,
    row_delta,
    temper,
):
    inverse_root = 1.0 / math.sqrt(query_block.shape[-1])
    scaling = (temper * inverse_root)[..., None, None]
    probability = jnp.where(
        pair_mask, jnp.exp(temper[..., None, None] * raw_scores - log_total[..., None]), 0.0
    )
    score_grad = probability * (prob_grad - row_delta[..., None])
    prob_low = probability.astype(jnp.bfloat16)
    grad_low = score_grad.astype(jnp.bfloat16)
    query_part = (
        jnp.einsum("...ts,...sd->...td", grad_low, prev_keys, preferred_element_type=jnp.float32)
        * scaling
    )
    key_part = (
        jnp.einsum("...ts,...td->...sd", grad_low, query_block, preferred_element_type=jnp.float32)
        * scaling
    )
    value_part = jnp.einsum(
        "...ts,...td->...sd", prob_low, grad_block, preferred_element_type=jnp.float32
    )
    temper_part = jnp.sum(score_grad * raw_scores, axis=(-2, -1))
    return (query_part, key_part, value_part, temper_part)


def cluster_pair(
    query_items,
    key_items,
    value_items,
    grad_items,
    live_items,
    temper,
    window_top,
    window_total,
    window_mass,
):
    item_count, block_len, depth = query_items.shape
    row_count = item_count * block_len
    group_rows = 4 * block_len
    inverse_root = 1.0 / math.sqrt(depth)
    scaling = temper * inverse_root
    query_rows = query_items.reshape(row_count, depth)
    key_rows = key_items.reshape(row_count, depth)
    value_rows = value_items.reshape(row_count, depth)
    grad_rows = grad_items.reshape(row_count, depth)
    key_item = jnp.arange(row_count) // block_len
    key_token = jnp.arange(row_count) % block_len
    live_rows = jnp.repeat(live_items, block_len)
    top_rows = window_top.reshape(row_count)
    total_rows = window_total.reshape(row_count)
    mass_rows = window_mass.reshape(row_count)

    def group_step(carry, start_row):
        key_acc, value_acc, temper_acc = carry
        query_group = lax.dynamic_slice_in_dim(query_rows, start_row, group_rows, 0)
        grad_group = lax.dynamic_slice_in_dim(grad_rows, start_row, group_rows, 0)
        group_live = lax.dynamic_slice_in_dim(live_rows, start_row, group_rows, 0)
        group_top = lax.dynamic_slice_in_dim(top_rows, start_row, group_rows, 0)
        group_total = lax.dynamic_slice_in_dim(total_rows, start_row, group_rows, 0)
        group_mass = lax.dynamic_slice_in_dim(mass_rows, start_row, group_rows, 0)
        query_item = (start_row + jnp.arange(group_rows)) // block_len
        query_token = jnp.arange(group_rows) % block_len
        earlier = (key_item[None, :] < query_item[:, None]) | (
            key_item[None, :] == query_item[:, None]
        ) & (key_token[None, :] <= query_token[:, None])
        pair_mask = group_live[:, None] & live_rows[None, :] & earlier
        raw_scores = (
            lax.dot_general(
                query_group, key_rows, (((1,), (1,)), ((), ())), preferred_element_type=jnp.float32
            )
            * inverse_root
        )
        scores = temper * raw_scores
        row_top = jnp.maximum(
            jnp.max(jnp.where(pair_mask, scores, blocked_score), axis=1), group_top
        )
        weights = jnp.where(pair_mask, jnp.exp(scores - row_top[:, None]), 0.0)
        row_total = jnp.sum(weights, axis=1) + group_total * jnp.exp(group_top - row_top)
        log_total = row_top + jnp.log(jnp.where(group_live, row_total, 1.0))
        probability = jnp.where(pair_mask, jnp.exp(scores - log_total[:, None]), 0.0)
        prob_grad = lax.dot_general(
            grad_group, value_rows, (((1,), (1,)), ((), ())), preferred_element_type=jnp.float32
        )
        row_delta = jnp.sum(probability * prob_grad, axis=1) + group_mass * jnp.exp(
            group_top - log_total
        )
        score_grad = probability * (prob_grad - row_delta[:, None])
        prob_low = probability.astype(jnp.bfloat16)
        grad_low = score_grad.astype(jnp.bfloat16)
        query_part = jnp.dot(grad_low, key_rows, preferred_element_type=jnp.float32) * scaling
        key_acc = (
            key_acc
            + lax.dot_general(
                grad_low, query_group, (((0,), (0,)), ((), ())), preferred_element_type=jnp.float32
            )
            * scaling
        )
        value_acc = value_acc + lax.dot_general(
            prob_low, grad_group, (((0,), (0,)), ((), ())), preferred_element_type=jnp.float32
        )
        temper_acc = temper_acc + jnp.sum(score_grad * raw_scores)
        return ((key_acc, value_acc, temper_acc), (query_part, log_total, row_delta))

    start_rows = jnp.arange(item_count // 4) * group_rows
    initial = (
        jnp.zeros((row_count, depth), jnp.float32),
        jnp.zeros((row_count, depth), jnp.float32),
        jnp.zeros((), jnp.float32),
    )
    (key_acc, value_acc, temper_acc), (query_part, log_total, row_delta) = lax.scan(
        group_step, initial, start_rows
    )
    return (
        query_part.reshape(item_count, block_len, depth),
        log_total.reshape(item_count, block_len),
        row_delta.reshape(item_count, block_len),
        key_acc.reshape(item_count, block_len, depth),
        value_acc.reshape(item_count, block_len, depth),
        temper_acc,
    )


def clustered_shards(
    probe_vectors,
    lookup_vectors,
    content_vectors,
    result_cotangent,
    logit_softness,
    block_grouping,
    neighborhood_span,
):
    seq_count = lax.axis_size("seq")
    position = lax.axis_index("seq")
    tokens = probe_vectors.shape[1]
    head_count = probe_vectors.shape[2] // HD
    local_blocks = tokens // BLK
    block_count = local_blocks * seq_count
    cluster_count = max(1, block_count // 8)
    capacity = min(12, block_count)
    owned_pairs = cluster_count * head_count // seq_count
    group_count = cluster_count // owned_pairs
    per_peer = max(1, local_blocks // group_count)
    cluster_ids = block_grouping[0, :, :, 0]
    query_home = head_major(probe_vectors[0], BLK)
    key_home = head_major(lookup_vectors[0], BLK)
    value_home = head_major(content_vectors[0], BLK)
    grad_home = head_major(result_cotangent[0], BLK)
    last_block = (lookup_vectors[0, tokens - BLK :], content_vectors[0, tokens - BLK :])
    prev_key_rows, prev_value_rows = shifted((last_block[0], last_block[1]), "seq", 1)
    prev_keys = jnp.concatenate([head_major(prev_key_rows, BLK), key_home[:, :-1]], axis=1)
    prev_values = jnp.concatenate([head_major(prev_value_rows, BLK), value_home[:, :-1]], axis=1)
    first_block = position * local_blocks
    before = jnp.concatenate(
        [jnp.full((head_count, 1), -1, jnp.int32), cluster_ids[:, :-1]], axis=1
    )
    my_ids = lax.dynamic_slice_in_dim(cluster_ids, first_block, local_blocks, 1)
    my_before = lax.dynamic_slice_in_dim(before, first_block, local_blocks, 1)
    global_block = first_block + jnp.arange(local_blocks)
    usable_home = (global_block[None, :] >= 1) & (my_before != my_ids)
    peer_index = jnp.arange(seq_count)
    peer_head = peer_index * owned_pairs // cluster_count
    slot_range = jnp.arange(per_peer)
    local_range = jnp.arange(local_blocks)
    owner_index = (jnp.arange(head_count)[:, None] * cluster_count + my_ids) // owned_pairs
    peer_ids = jnp.take(my_ids, peer_head, axis=0)
    goes = (peer_head[:, None] * cluster_count + peer_ids) // owned_pairs == peer_index[:, None]
    send_rank = jnp.cumsum(goes.astype(jnp.int32), axis=1) - 1
    send_pick = goes[:, None, :] & (send_rank[:, None, :] == slot_range[None, :, None])
    send_block = jnp.sum(jnp.where(send_pick, local_range[None, None, :], 0), axis=2)
    send_flat = peer_head[:, None] * local_blocks + send_block
    home_rank = jnp.take_along_axis(send_rank, owner_index, axis=0)
    home_pos = owner_index * per_peer + home_rank
    pair_index = position * owned_pairs + jnp.arange(owned_pairs)
    split_for_couple = pair_index // cluster_count
    pair_cluster = pair_index % cluster_count
    my_head = position * owned_pairs // cluster_count
    split_numbers = jnp.take(cluster_ids, my_head, axis=0)
    member = split_numbers[None, :] == pair_cluster[:, None]
    member_rank = jnp.cumsum(member.astype(jnp.int32), axis=1) - 1
    member_count = jnp.sum(member.astype(jnp.int32), axis=1)
    picked = member[:, None, :] & (member_rank[:, None, :] == jnp.arange(capacity)[None, :, None])
    member_block = jnp.sum(jnp.where(picked, jnp.arange(block_count)[None, None, :], 0), axis=2)
    live_members = jnp.arange(capacity)[None, :] < member_count[:, None]
    mine = (my_head * cluster_count + split_numbers) // owned_pairs == position
    mine_grid = mine.reshape(seq_count, local_blocks)
    recv_rank = jnp.cumsum(mine_grid.astype(jnp.int32), axis=1) - 1
    recv_pos = (peer_index[:, None] * per_peer + recv_rank).reshape(block_count)
    member_pos = jnp.take(recv_pos, member_block)
    couple_softness = jnp.take(logit_softness, split_for_couple)
    pair_onehot = (split_for_couple[:, None] == jnp.arange(head_count)[None, :]).astype(jnp.float32)
    slot_pair = my_head * cluster_count + split_numbers - position * owned_pairs
    same_cluster = split_numbers[:, None] == split_numbers[None, :]
    earlier_block = jnp.arange(block_count)[None, :] < jnp.arange(block_count)[:, None]
    slot_rank = jnp.sum((same_cluster & earlier_block).astype(jnp.int32), axis=1)
    back_pos = jnp.clip(slot_pair, 0, owned_pairs - 1) * capacity + jnp.clip(
        slot_rank, 0, capacity - 1
    )
    back_grid = back_pos.reshape(seq_count, local_blocks)
    back_pick = mine_grid[:, None, :] & (recv_rank[:, None, :] == slot_range[None, :, None])
    back_flat = jnp.sum(jnp.where(back_pick, back_grid[:, None, :], 0), axis=2)

    def to_peers(array_in):
        flat = array_in.reshape((head_count * local_blocks,) + array_in.shape[2:])
        return jnp.take(flat, send_flat, axis=0)

    def members(array_in):
        flat = array_in.reshape((seq_count * per_peer,) + array_in.shape[2:])
        return jnp.take(flat, member_pos, axis=0)

    def to_owner(array_in):
        flat = array_in.reshape((owned_pairs * capacity,) + array_in.shape[2:])
        return jnp.take(flat, back_flat, axis=0)

    def from_peers(array_in):
        flat = array_in.reshape((seq_count * per_peer,) + array_in.shape[2:])
        return jnp.take(flat, home_pos, axis=0)

    raw_w, mask_w, pgrad_w, top_w, total_w, mass_w = window_parts(
        query_home,
        prev_keys,
        prev_values,
        grad_home,
        usable_home,
        neighborhood_span[:, None],
        logit_softness[:, None],
    )
    arrived = (
        lax.all_to_all(to_peers(query_home), "seq", split_axis=0, concat_axis=0, tiled=True),
        lax.all_to_all(to_peers(key_home), "seq", split_axis=0, concat_axis=0, tiled=True),
        lax.all_to_all(to_peers(value_home), "seq", split_axis=0, concat_axis=0, tiled=True),
        lax.all_to_all(to_peers(grad_home), "seq", split_axis=0, concat_axis=0, tiled=True),
    )
    arrived_stats = (
        lax.all_to_all(to_peers(top_w), "seq", split_axis=0, concat_axis=0, tiled=True),
        lax.all_to_all(to_peers(total_w), "seq", split_axis=0, concat_axis=0, tiled=True),
        lax.all_to_all(to_peers(mass_w), "seq", split_axis=0, concat_axis=0, tiled=True),
    )
    query_m, key_m, value_m, grad_m = [members(item_in) for item_in in arrived]
    top_m, total_m, mass_m = [members(item_in) for item_in in arrived_stats]

    def split_pair(pair_inputs):
        query_i, key_i, value_i, grad_i, live_i, temper_i, top_i, total_i, mass_i = pair_inputs
        query_c, log_total, row_delta, key_c, value_c, temper_c = cluster_pair(
            query_i, key_i, value_i, grad_i, live_i, temper_i, top_i, total_i, mass_i
        )
        return (
            query_c.astype(jnp.bfloat16),
            key_c.astype(jnp.bfloat16),
            value_c.astype(jnp.bfloat16),
            log_total,
            row_delta,
            temper_c,
        )

    owner_results = lax.map(
        split_pair,
        (query_m, key_m, value_m, grad_m, live_members, couple_softness, top_m, total_m, mass_m),
    )
    returned = (
        lax.all_to_all(to_owner(owner_results[0]), "seq", split_axis=0, concat_axis=0, tiled=True),
        lax.all_to_all(to_owner(owner_results[1]), "seq", split_axis=0, concat_axis=0, tiled=True),
        lax.all_to_all(to_owner(owner_results[2]), "seq", split_axis=0, concat_axis=0, tiled=True),
    )
    returned_stats = (
        lax.all_to_all(to_owner(owner_results[3]), "seq", split_axis=0, concat_axis=0, tiled=True),
        lax.all_to_all(to_owner(owner_results[4]), "seq", split_axis=0, concat_axis=0, tiled=True),
    )
    query_cluster = from_peers(returned[0])
    key_cluster = from_peers(returned[1])
    value_cluster = from_peers(returned[2])
    log_home = from_peers(returned_stats[0])
    delta_home = from_peers(returned_stats[1])
    query_w, key_w, value_w, temper_w = window_grads(
        raw_w,
        mask_w,
        pgrad_w,
        query_home,
        prev_keys,
        grad_home,
        log_home,
        delta_home,
        logit_softness[:, None],
    )
    query_out = (query_cluster.astype(jnp.float32) + lifted(query_w)).astype(jnp.bfloat16)
    key_window = key_w.astype(jnp.bfloat16)
    value_window = value_w.astype(jnp.bfloat16)
    temper_local = jnp.sum(owner_results[5][:, None] * pair_onehot, axis=0) + jnp.sum(
        temper_w, axis=1
    )
    edge_keys, edge_values = shifted((key_window[:, 0], value_window[:, 0]), "seq", -1)
    key_next = jnp.concatenate([key_window[:, 1:], edge_keys[:, None]], axis=1)
    value_next = jnp.concatenate([value_window[:, 1:], edge_values[:, None]], axis=1)
    key_out = (key_cluster.astype(jnp.float32) + key_next.astype(jnp.float32)).astype(jnp.bfloat16)
    value_out = (value_cluster.astype(jnp.float32) + value_next.astype(jnp.float32)).astype(
        jnp.bfloat16
    )
    temper_total = lax.psum(temper_local, ("seq", "dp"))
    temper_grad = temper_total / (lax.axis_size("dp") * tokens * seq_count)
    return (token_major(query_out), token_major(key_out), token_major(value_out), temper_grad)


TILE = 256
EXTRA = 16
MIB = 1024 * 1024
PIECES = 4
QUERY, KEY, VALUE, GRAD = range(4)


def columns_of(index):
    return pl.ds(pl.multiple_of(index * HD, HD), HD)


def rows_of(index):
    return pl.ds(pl.multiple_of(index * BLK, BLK), BLK)


def tile_rows(tile):
    return slice(tile * TILE, (tile + 1) * TILE)


def position(half_count):
    me = lax.axis_index("seq")
    half = jnp.where(me >= half_count, 1, 0)
    return me, half, me - half * half_count


def kernel_call(
    kernel, name, operands, in_specs, out_shape, scratch, vmem_mib, flops=0, out_spaces=None,
    aliases=None,
):
    bytes_accessed = sum(
        math.prod(item.shape) * item.dtype.itemsize for item in (*operands, *out_shape)
    )
    return pl.pallas_call(
        kernel,
        out_shape=out_shape,
        in_specs=in_specs,
        out_specs=[
            pl.BlockSpec(memory_space=space)
            for space in out_spaces or [pltpu.VMEM] * len(out_shape)
        ],
        scratch_shapes=scratch,
        input_output_aliases=aliases or {},
        cost_estimate=pl.CostEstimate(
            flops=flops, bytes_accessed=bytes_accessed, transcendentals=0
        ),
        compiler_params=pltpu.CompilerParams(vmem_limit_bytes=vmem_mib * MIB),
        name=name,
    )(*operands)


def pack_kernel(*refs, half_count):
    arrays, within_ref, foreign_refs = refs[:4], refs[4], refs[5:7]
    held, within, across, arrival, left_within, left_across = refs[7:]
    me, half, _ = position(half_count)
    piece = BLK // PIECES
    arrivals = [
        [
            pltpu.make_async_copy(
                array_ref.at[0, part * piece : (part + 1) * piece, :],
                held.at[place, part * piece : (part + 1) * piece, :],
                arrival.at[place, part],
            )
            for part in range(PIECES)
        ]
        for place, array_ref in enumerate(arrays)
    ]
    for copies in arrivals:
        for copy in copies:
            copy.start()
    leaving = []
    for place, copies in enumerate(arrivals):
        for copy in copies:
            copy.wait()
        for slot, base in enumerate((half * half_count, (1 - half) * half_count)):
            rows = slice((slot * 4 + place) * BLK, (slot * 4 + place + 1) * BLK)
            for peer in range(half_count):
                within[peer, rows, :] = held[place, :, columns_of(base + peer)]
            leaving.append(
                pltpu.make_async_copy(
                    within.at[:, rows, :], within_ref.at[:, rows, :], left_within.at[place, slot]
                )
            )
            leaving[-1].start()
    first = jnp.where(half == 0, KEY, QUERY)
    second = jnp.where(half == 0, VALUE, GRAD)
    for core, foreign_ref in enumerate(foreign_refs):
        for step in range(half_count // 2):
            columns = columns_of(me ^ core ^ (half_count + 2 * step))
            across[core, step, :BLK, :] = held[first, :, columns]
            across[core, step, BLK:, :] = held[second, :, columns]
        leaving.append(pltpu.make_async_copy(across.at[core], foreign_ref, left_across.at[core]))
        leaving[-1].start()
    for copy in leaving:
        copy.wait()


def packed(arrays, half_count):
    width = arrays[0].shape[2]
    within_shape, across_shape = (half_count, 8 * BLK, HD), (half_count // 2, 2 * BLK, HD)
    return kernel_call(
        functools.partial(pack_kernel, half_count=half_count),
        "pack_heads",
        arrays,
        [pl.BlockSpec(memory_space=pl.ANY)] * 4,
        [jax.ShapeDtypeStruct(within_shape, jnp.bfloat16)]
        + [jax.ShapeDtypeStruct(across_shape, jnp.bfloat16)] * 2,
        [
            pltpu.VMEM((4, BLK, width), jnp.bfloat16),
            pltpu.VMEM(within_shape, jnp.bfloat16),
            pltpu.VMEM((2, *across_shape), jnp.bfloat16),
            pltpu.SemaphoreType.DMA((4, PIECES)),
            pltpu.SemaphoreType.DMA((4, 2)),
            pltpu.SemaphoreType.DMA((2,)),
        ],
        60,
        out_spaces=[pl.ANY] * 3,
    )


def dot_rows(left, right):
    return lax.dot_general(
        left, right, (((1,), (1,)), ((), ())), preferred_element_type=jnp.float32
    )


def dot_plain(left, right):
    return lax.dot_general(
        left, right, (((1,), (0,)), ((), ())), preferred_element_type=jnp.float32
    )


def from_blocks(ref, place):
    def rows(start, stop):
        per_tile = TILE // BLK
        return jnp.concatenate(
            [ref[block, place] for block in range(start * per_tile, stop * per_tile)],
            axis=0,
        )

    return rows


def from_array(ref, place):
    return lambda start, stop: ref[place, start * TILE : stop * TILE, :]


class Region:
    def __init__(self, square, sources, tiles, scaling, bias_ref=None, corner_ref=None, first=0):
        self.square, self.sources, self.tiles, self.scaling = square, sources, tiles, scaling
        self.bias_ref, self.corner_ref, self.first = bias_ref, corner_ref, first

    def rows(self, which, start, stop):
        return self.sources[which](start, stop)

    def scale_of(self, array):
        return 1.0 if array == VALUE else self.scaling[:, :HD]

    def keys_of(self, tile):
        return range(self.tiles if self.square else tile + 1)

    def scores(self, tile_key, tile_query):
        per_tile = TILE // BLK
        scores = dot_rows(
            self.rows(KEY, tile_key, tile_key + 1), self.rows(QUERY, tile_query, tile_query + 1)
        ) * (self.scaling * math.log2(math.e))
        before = self.tiles * per_tile if self.square else 0
        rows = []
        for sub_key in range(per_tile):
            key_block = tile_key * per_tile + sub_key
            pieces = []
            for sub_query in range(per_tile):
                query_block = tile_query * per_tile + sub_query
                lanes = slice(sub_query * BLK, (sub_query + 1) * BLK)
                piece = scores[sub_key * BLK : (sub_key + 1) * BLK, lanes]
                apart = before + query_block - key_block
                if apart < 0:
                    piece = jnp.full_like(piece, blocked_score)
                elif apart == 0:
                    piece = jnp.where(key_minus_query() <= 0, piece, blocked_score)
                elif apart == 1:
                    piece = piece + self.corner_ref[self.first + (0 if self.square else key_block)]
                else:
                    at = slice(query_block * BLK, (query_block + 1) * BLK)
                    piece = piece + self.bias_ref[key_block : key_block + 1, at]
                pieces.append(piece)
            rows.append(jnp.concatenate(pieces, axis=1))
        return jnp.concatenate(rows, axis=0)


def diagonal(slot, arrived_ref, scales_ref, bias_ref=None, corner_ref=None):
    blocks = arrived_ref.shape[0]
    sources = [from_blocks(arrived_ref, slot * 4 + place) for place in range(4)]
    bias = None if bias_ref is None else bias_ref.at[slot]
    first = slot * (blocks - 1)
    scaling = scales_ref[slot : slot + 1, :]
    return Region(False, sources, blocks * BLK // TILE, scaling, bias, corner_ref, first)


def square(square_ref, scales_ref, bias_ref=None, corner_ref=None):
    tiles = square_ref.shape[1] // TILE
    sources = [from_array(square_ref, place) for place in range(4)]
    bias = None if bias_ref is None else bias_ref.at[2]
    first = 2 * (tiles * TILE // BLK - 1)
    return Region(True, sources, tiles, scales_ref[0:1, :], bias, corner_ref, first)


def key_minus_query():
    shape = (BLK, BLK)
    return lax.broadcasted_iota(jnp.int32, shape, 0) - lax.broadcasted_iota(jnp.int32, shape, 1)


def statistics(region, weight_ref, towards_ref, out_ref, first_row):
    for tile in range(region.tiles):
        here = tile_rows(tile)
        top = jnp.full((1, TILE), blocked_score, jnp.float32)
        for other in region.keys_of(tile):
            raw = region.scores(other, tile)
            weight_ref[tile_rows(other), here] = raw
            top = jnp.maximum(top, jnp.max(raw, axis=0, keepdims=True))
        sums = [jnp.zeros((1, TILE), jnp.float32)] * 4
        for other in region.keys_of(tile):
            there = tile_rows(other)
            raw = weight_ref[there, here]
            weight = jnp.exp2(raw - top)
            towards = dot_rows(
                region.rows(VALUE, other, other + 1), region.rows(GRAD, tile, tile + 1)
            )
            weight_ref[there, here] = weight
            towards_ref[there, here] = towards
            pulled, weighted = weight * towards, weight * raw
            terms = (weight, pulled, pulled * raw, weighted)
            sums = [
                total + jnp.sum(term, axis=0, keepdims=True) for total, term in zip(sums, terms)
            ]
        for row, value in enumerate((top, *sums)):
            out_ref[first_row + row : first_row + row + 1, here] = value


def gradients(
    region, weight_ref, towards_ref, top, log_total, delta, prob_low, grad_low, keys_flat, emit=None
):
    keys_flat[...] = region.rows(KEY, 0, region.tiles).T
    share = jnp.exp2(top - log_total)
    query_parts, key_parts, value_parts = [], [], []
    for tile in range(region.tiles):
        here = tile_rows(tile)
        for other in region.keys_of(tile):
            there = tile_rows(other)
            probability = weight_ref[there, here] * share[:, here]
            prob_low[there, here] = probability.astype(jnp.bfloat16)
            grad_low[there, here] = (
                probability * (towards_ref[there, here] - delta[:, here])
            ).astype(jnp.bfloat16)
        upto = slice(0, len(region.keys_of(tile)) * TILE)
        query_parts.append(dot_plain(keys_flat[:, upto], grad_low[upto, here]).T)
    if emit is not None:
        emit(QUERY, query_parts)
    for low, which, parts in ((grad_low, QUERY, key_parts), (prob_low, GRAD, value_parts)):
        for tile in range(region.tiles):
            first = 0 if region.square else tile
            onward = slice(first * TILE, region.tiles * TILE)
            parts.append(
                dot_plain(low[tile_rows(tile), onward], region.rows(which, first, region.tiles))
            )
        if emit is not None:
            emit(KEY if which == QUERY else VALUE, parts)
    return query_parts, key_parts, value_parts


def merged(first, second):
    top = jnp.maximum(first[0], second[0])
    left, right = jnp.exp2(first[0] - top), jnp.exp2(second[0] - top)
    total = first[1] * left + second[1] * right
    mass = first[2] * left + second[2] * right
    return top + jnp.log2(total), mass / total


def alone(rows):
    return rows[0] + jnp.log2(rows[1]), rows[2] / rows[1]


def rows_at(ref, first, count=5):
    return [ref[first + row : first + row + 1, :] for row in range(count)]


def temper_terms(rows, totals, scale_row):
    log_total, delta = totals
    terms = (rows[3] - delta * rows[4]) * jnp.exp2(rows[0] - log_total)
    folded = sum(terms[:, start : start + HD] for start in range(0, terms.shape[1], HD))
    return folded / (scale_row[:, :HD] * (math.sqrt(HD) * math.log2(math.e)))


def put(within_ref, array, tile, value):
    per_tile = TILE // BLK
    for sub in range(per_tile):
        within_ref[tile * per_tile + sub, array * BLK : (array + 1) * BLK, :] = value[
            sub * BLK : (sub + 1) * BLK, :
        ].astype(jnp.bfloat16)


def scaled(region, parts):
    scale = region.scaling[:, :HD]
    return [[value * scale for value in part] for part in parts[:2]] + [parts[2]]


def masks_kernel(softness_ref, ids_ref, span_ref, scales_ref, bias_ref, corner_ref, *, half_count):
    me, half, _ = position(half_count)
    base = half * half_count
    regions = (
        (me, base, base),
        (me ^ half_count, base, base),
        (me, 0, half_count),
    )
    for slot, (head, key_base, query_base) in enumerate(regions):
        if slot < 2:
            scales_ref[slot : slot + 1, :] = jnp.full(
                (1, TILE), softness_ref[head] * (1.0 / math.sqrt(HD)), jnp.float32
            )

        def same(key_block, query_block):
            return ids_ref[head, key_base + key_block] == ids_ref[head, query_base + query_block]

        def bias(key_block, query_block):
            return jnp.full(
                (1, BLK), jnp.where(same(key_block, query_block), 0.0, blocked_score), jnp.float32
            )

        for key_block in range(half_count):
            bias_ref[slot, key_block : key_block + 1, :] = jnp.concatenate(
                [bias(key_block, query_block) for query_block in range(half_count)], axis=1
            )
        pairs = [(block, block + 1) for block in range(half_count - 1)]
        if slot == 2:
            pairs = [(half_count - 1, 0)]
        for place, pair in enumerate(pairs):
            least = jnp.where(same(*pair), -BLK, BLK - span_ref[head])
            corner_ref[slot * (half_count - 1) + place] = jnp.where(
                key_minus_query() > least, 0.0, blocked_score
            )


def within_kernel(
    arrived_ref, scales_ref, bias_ref, corner_ref, stats_ref, parts_ref, own_weight, own_towards, other_weight, other_towards, *scratch, half_count
):
    _, half, _ = position(half_count)
    kept = ((own_weight, own_towards), (other_weight, other_towards))
    for slot in range(2):
        region = diagonal(slot, arrived_ref, scales_ref, bias_ref, corner_ref)
        statistics(region, *kept[slot], stats_ref, slot * 5)

    @pl.when(half == 0)
    def _():
        region = diagonal(0, arrived_ref, scales_ref)
        single = alone(rows_at(stats_ref, 0))
        parts = gradients(region, *kept[0], stats_ref[0:1, :], *single, *scratch)
        for place, tiles in enumerate(scaled(region, parts)):
            for tile, value in enumerate(tiles):
                parts_ref[place, tile_rows(tile), :] = value


def square_kernel(arrived_ref, scales_ref, bias_ref, corner_ref, stats_ref, *refs, half_count):
    across_refs = refs[: half_count // 2]
    square_ref, message_ref, square_stats, weight, towards = refs[half_count // 2 :]
    _, half, place = position(half_count)
    first = jnp.where(half == 0, QUERY, KEY)
    second = jnp.where(half == 0, GRAD, VALUE)
    for step, across_ref in enumerate(across_refs):
        for core in range(2):
            rows = rows_of(place ^ core ^ (2 * step))
            square_ref[first, rows, :] = across_ref[core, :BLK, :]
            square_ref[second, rows, :] = across_ref[core, BLK:, :]
    for kept in (jnp.where(half == 0, KEY, QUERY), jnp.where(half == 0, VALUE, GRAD)):
        for block in range(half_count):
            square_ref[kept, block * BLK : (block + 1) * BLK, :] = arrived_ref[block, kept]
    region = square(square_ref, scales_ref, bias_ref, corner_ref)
    statistics(region, weight, towards, square_stats, 0)
    own, other, crossing = rows_at(stats_ref, 0), rows_at(stats_ref, 5), rows_at(square_stats, 0)
    for row in range(5):
        message_ref[row : row + 1, :] = jnp.where(half == 0, crossing[row], other[row])
    own_scale, other_scale = scales_ref[0:1, :], scales_ref[1:2, :]
    both = merged(own, crossing)
    whole = temper_terms(own, both, own_scale) + temper_terms(crossing, both, own_scale)
    single = temper_terms(own, alone(own), own_scale)
    message_ref[5:6, :HD] = jnp.where(half == 0, single, whole)
    message_ref[6:7, :HD] = temper_terms(other, alone(other), other_scale)


def first_kernel(
    arrived_ref, scales_ref, square_ref, stats_ref, square_stats,
    own_weight, own_towards, other_weight, other_towards, square_weight, square_towards,
    across_ref, within_ref, ready, ready_sem, *scratch, half_count
):
    _, half, _ = position(half_count)
    leaving = sends(ready, within_ref, ready_sem, (1 - half) * 3)

    @pl.when(half == 0)
    def _():
        region = diagonal(1, arrived_ref, scales_ref)

        def send(array, parts):
            for tile, part in enumerate(parts):
                put(ready, array, tile, part * region.scale_of(array))
            leaving[array].start()

        totals = alone(rows_at(stats_ref, 5))
        gradients(
            region, other_weight, other_towards, stats_ref[5:6, :], *totals, *scratch, emit=send
        )

    @pl.when(half == 1)
    def _():
        totals = merged(rows_at(stats_ref, 0), rows_at(square_stats, 0))
        region = square(square_ref, scales_ref)
        parts = gradients(
            region, square_weight, square_towards, square_stats[0:1, :], *totals, *scratch
        )
        across_query, *foreign = scaled(region, parts)
        for array, tiles in enumerate(foreign):
            for tile, value in enumerate(tiles):
                across_ref[array, tile_rows(tile), :] = value.astype(jnp.bfloat16)
        region = diagonal(0, arrived_ref, scales_ref)

        def send(array, parts):
            for tile, part in enumerate(parts):
                value = part * region.scale_of(array)
                put(ready, array, tile, value + across_query[tile] if array == QUERY else value)
            leaving[array].start()

        gradients(
            region, own_weight, own_towards, stats_ref[0:1, :], *totals, *scratch, emit=send
        )

    for copy in leaving:
        copy.wait()


def sends(ready, within_ref, sems, first):
    copies = []
    for array in range(3):
        rows = slice(array * BLK, (array + 1) * BLK)
        copies.append(
            pltpu.make_async_copy(
                ready.at[:, rows, :], within_ref.at[:, rows_of(first + array), :], sems.at[array]
            )
        )
    return copies


def temper_rows(own, other):
    row = lax.broadcasted_iota(jnp.int32, (EXTRA, HD), 0)
    rows = jnp.zeros((EXTRA, HD), jnp.float32)
    for place, terms in enumerate((own, other)):
        rest = jnp.broadcast_to(jnp.sum(terms, axis=1, keepdims=True), (EXTRA, HD))
        for piece in range(3):
            high = rest.astype(jnp.bfloat16).astype(jnp.float32)
            rows = jnp.where(row == place * 3 + piece, high, rows)
            rest = rest - high
    return rows.astype(jnp.bfloat16)


def finish_kernel(
    arrived_ref, scales_ref, square_ref, message_ref, received_ref, stats_ref, square_stats,
    parts_ref, square_weight, square_towards, other_weight, other_towards, across_ref, begun_ref,
    within_ref, *refs, half_count
):
    del begun_ref
    chunk_refs = refs[:2]
    across, ready, tail, ready_sem, tail_sem, *scratch = refs[2:]
    _, half, place = position(half_count)
    leaving = sends(ready, within_ref, ready_sem, half * 3)
    sent, came = rows_at(message_ref, 0), rows_at(received_ref, 0)
    totals = merged(sent, came)
    scale = jnp.where(half == 0, scales_ref[0:1, :], scales_ref[1:2, :])
    shared = temper_terms(sent, totals, scale) + temper_terms(came, totals, scale)
    mine, theirs = message_ref[5:6, :HD], received_ref[5:6, :HD]
    own = mine + jnp.where(half == 0, shared, received_ref[6:7, :HD])
    other = theirs + jnp.where(half == 0, message_ref[6:7, :HD], shared)
    pieces = temper_rows(own, other)
    for block in range(half_count):
        tail[block] = pieces
    leaving.append(
        pltpu.make_async_copy(tail, within_ref.at[:, 6 * BLK : 6 * BLK + EXTRA, :], tail_sem)
    )
    leaving[-1].start()

    def chunks():
        for core, chunk_ref in enumerate(chunk_refs):
            for step in range(half_count // 2):
                yield step, chunk_ref, rows_of(place ^ core ^ (2 * step))

    @pl.when(half == 0)
    def _():
        region = square(square_ref, scales_ref)

        def send(array, parts):
            for tile, part in enumerate(parts):
                here = tile_rows(tile)
                value = part * region.scale_of(array)
                if array == QUERY:
                    across[here, :] = value.astype(jnp.bfloat16)
                    put(ready, array, tile, parts_ref[array, here, :])
                else:
                    put(ready, array, tile, parts_ref[array, here, :] + value)
            leaving[array].start()

        gradients(
            region, square_weight, square_towards, square_stats[0:1, :], *totals, *scratch, emit=send
        )
        for step, chunk_ref, rows in chunks():
            chunk_ref[step, :BLK, :] = across[rows, :]
            chunk_ref[step, BLK:, :] = jnp.zeros((BLK, HD), jnp.bfloat16)

    @pl.when(half == 1)
    def _():
        region = diagonal(1, arrived_ref, scales_ref)

        def send(array, parts):
            for tile, part in enumerate(parts):
                put(ready, array, tile, part * region.scale_of(array))
            leaving[array].start()

        gradients(
            region, other_weight, other_towards, stats_ref[5:6, :], *totals, *scratch, emit=send
        )
        for step, chunk_ref, rows in chunks():
            chunk_ref[step, :BLK, :] = across_ref[0, rows, :]
            chunk_ref[step, BLK:, :] = across_ref[1, rows, :]

    for copy in leaving:
        copy.wait()


def temper_kernel(within_ref, temper_ref, *, half_count):
    _, half, _ = position(half_count)
    for peer in range(half_count):
        for slot, base in enumerate((half * half_count, (1 - half) * half_count)):
            rows = within_ref[peer, 3 * slot : 3 * slot + 3, :].astype(jnp.float32)
            temper_ref[pl.ds(base + peer, 1), :] = jnp.sum(rows, axis=0, keepdims=True)


def temper_sums(within, half_count):
    last = 6 * BLK // EXTRA
    return pl.pallas_call(
        functools.partial(temper_kernel, half_count=half_count),
        grid=(1,),
        out_shape=jax.ShapeDtypeStruct((2 * half_count, HD), jnp.float32),
        in_specs=[pl.BlockSpec((half_count, EXTRA, HD), lambda step: (0, last, 0))],
        out_specs=pl.BlockSpec((2 * half_count, HD), lambda step: (0, 0)),
        compiler_params=pltpu.CompilerParams(vmem_limit_bytes=4 * MIB),
        name="temper_sums",
    )(within)


def unpack_kernel(within_ref, *refs, half_count):
    across_refs = refs[: half_count // 2]
    out_refs = refs[half_count // 2 :]
    _, half, place = position(half_count)
    for step, across_ref in enumerate(across_refs):
        for core in range(2):
            peer = place ^ core ^ (2 * step)
            other = columns_of((1 - half) * half_count + peer)
            own = columns_of(half * half_count + peer)
            first = across_ref[core, :BLK, :].astype(jnp.float32)
            second = across_ref[core, BLK : 2 * BLK, :].astype(jnp.float32)
            added = (
                jnp.where(half == 0, 0.0, first),
                jnp.where(half == 0, first, 0.0),
                jnp.where(half == 0, second, 0.0),
            )
            for array, out_ref in enumerate(out_refs):
                out_ref[0, :, own] = within_ref[peer, array * BLK : (array + 1) * BLK, :]
                kept = within_ref[peer, (3 + array) * BLK : (4 + array) * BLK, :]
                out_ref[0, :, other] = (kept.astype(jnp.float32) + added[array]).astype(
                    jnp.bfloat16
                )


def join_kernel(kept_ref, taken_ref, *out_refs):
    for step, out_ref in enumerate(out_refs):
        out_ref[0] = kept_ref[step]
        out_ref[1] = taken_ref[step]


def crossed(kept, given, half_count):
    devices = range(2 * half_count)
    steps, *shape = kept.shape
    taken = lax.ppermute(given, "seq", [(source, source ^ 1) for source in devices])
    messages = kernel_call(
        join_kernel,
        "join_chunks",
        (kept, taken),
        [pl.BlockSpec(memory_space=pltpu.VMEM)] * 2,
        [jax.ShapeDtypeStruct((2, *shape), jnp.bfloat16)] * steps,
        [],
        4,
    )
    return [
        lax.ppermute(
            message, "seq", [(source, source ^ (half_count + 2 * step)) for source in devices]
        )
        for step, message in enumerate(messages)
    ]


def head_shards(
    probe_vectors,
    lookup_vectors,
    content_vectors,
    result_cotangent,
    logit_softness,
    block_grouping,
    neighborhood_span,
):
    seq_count, dp_count = lax.axis_size("seq"), lax.axis_size("dp")
    half_count = seq_count // 2
    tokens = half_count * BLK
    groups = [list(range(half_count)), list(range(half_count, seq_count))]
    settings = (logit_softness, block_grouping[0, :, :, 0], neighborhood_span)
    smem, vmem = pl.BlockSpec(memory_space=pltpu.SMEM), pl.BlockSpec(memory_space=pltpu.VMEM)
    lows = [pltpu.VMEM((tokens, tokens), jnp.bfloat16)] * 2 + [
        pltpu.VMEM((HD, tokens), jnp.bfloat16)
    ]
    rows_of_stats = jax.ShapeDtypeStruct((8, tokens), jnp.float32)
    pairs = jax.ShapeDtypeStruct((tokens, tokens), jnp.float32)
    pair_flops = 2 * tokens * tokens * HD

    def exchange_within(array_in):
        return lax.all_to_all(
            array_in, "seq", split_axis=0, concat_axis=0, axis_index_groups=groups, tiled=True
        )

    def call(
        kernel, name, operands, out_shape, scratch, flops, vmem_mib, scalars=(), out_spaces=None,
        last_in_place=False,
    ):
        in_specs = [smem] * len(scalars) + [vmem] * len(operands)
        if last_in_place:
            in_specs[-1] = pl.BlockSpec(memory_space=pl.ANY)
        return kernel_call(
            functools.partial(kernel, half_count=half_count),
            name,
            (*scalars, *operands),
            in_specs,
            out_shape,
            scratch,
            vmem_mib,
            flops,
            out_spaces,
            {len(operands) - 1: 0} if last_in_place else {},
        )

    sent, *foreign = packed(
        (probe_vectors, lookup_vectors, content_vectors, result_cotangent), half_count
    )
    arrived = exchange_within(sent).reshape(half_count, 8, BLK, HD)
    kept_parts = jax.ShapeDtypeStruct((3, tokens, HD), jnp.float32)
    masks = call(
        masks_kernel,
        "scales_and_masks",
        (),
        [
            jax.ShapeDtypeStruct((8, TILE), jnp.float32),
            jax.ShapeDtypeStruct((3, half_count, tokens), jnp.float32),
            jax.ShapeDtypeStruct((2 * half_count - 1, BLK, BLK), jnp.float32),
        ],
        [],
        0,
        6,
        settings,
    )
    foreign[0], *masks = lax.optimization_barrier((foreign[0], *masks))
    foreign = crossed(*foreign, half_count)
    scales = masks[0]
    stats, parts, own_weight, own_towards, other_weight, other_towards = call(
        within_kernel,
        "diagonal_statistics",
        (arrived, *masks),
        [jax.ShapeDtypeStruct((16, tokens), jnp.float32), kept_parts] + [pairs] * 4,
        lows,
        2 * pair_flops,
        20,
    )
    squared, message, square_stats, square_weight, square_towards = call(
        square_kernel,
        "square_statistics",
        (arrived, *masks, stats, *foreign),
        [jax.ShapeDtypeStruct((4, tokens, HD), jnp.bfloat16)] + [rows_of_stats] * 2 + [pairs] * 2,
        [],
        2 * pair_flops,
        12,
    )
    swap = [(source, source ^ half_count) for source in range(seq_count)]
    received = lax.ppermute(message, "seq", swap)
    result = pltpu.HBM((half_count, 6 * BLK + EXTRA, HD), jnp.bfloat16)
    ready = pltpu.VMEM((half_count, 3 * BLK, HD), jnp.bfloat16)
    across, begun = call(
        first_kernel,
        "gradients_before_totals",
        (
            arrived, scales, squared, stats, square_stats, own_weight, own_towards,
            other_weight, other_towards, square_weight, square_towards,
        ),
        [jax.ShapeDtypeStruct((2, tokens, HD), jnp.bfloat16), result],
        [ready, pltpu.SemaphoreType.DMA((3,)), *lows],
        4 * pair_flops,
        14,
        out_spaces=(pltpu.VMEM, pl.ANY),
    )
    operands = (
        arrived, scales, squared, message, received, stats, square_stats, parts,
        square_weight, square_towards, other_weight, other_towards, across, begun,
    )
    within, *foreign = call(
        finish_kernel,
        "gradients_after_totals",
        operands,
        [result]
        + [jax.ShapeDtypeStruct((half_count // 2, 2 * BLK, HD), jnp.bfloat16)] * 2,
        [
            pltpu.VMEM((tokens, HD), jnp.bfloat16), ready,
            pltpu.VMEM((half_count, EXTRA, HD), jnp.bfloat16),
            pltpu.SemaphoreType.DMA((3,)), pltpu.SemaphoreType.DMA, *lows,
        ],
        2 * pair_flops,
        20,
        out_spaces=(pl.ANY, pltpu.VMEM, pltpu.VMEM),
        last_in_place=True,
    )
    across = crossed(*foreign, half_count)
    within = exchange_within(within)
    tempers = temper_sums(within, half_count)
    temper_total = tempers
    for step in range(1, dp_count):
        swap = [(source, (source + step) % dp_count) for source in range(dp_count)]
        temper_total = temper_total + lax.ppermute(tempers, "dp", swap)
    outs = kernel_call(
        functools.partial(unpack_kernel, half_count=half_count),
        "unpack_heads",
        (within, *across),
        [vmem] * (1 + len(across)),
        [jax.ShapeDtypeStruct(probe_vectors.shape, jnp.bfloat16)] * 3,
        [],
        10,
    )
    return (*outs, temper_total[:, 0] / (dp_count * BLK * seq_count))


def shards(
    probe_vectors,
    lookup_vectors,
    content_vectors,
    result_cotangent,
    logit_softness,
    block_grouping,
    neighborhood_span,
):
    head_count = probe_vectors.shape[2] // HD
    seq_count = lax.axis_size("seq")
    one_block = probe_vectors.shape[1] == BLK
    whole_tiles = seq_count * BLK % (2 * TILE) == 0 and seq_count & (seq_count - 1) == 0
    if head_count == seq_count and one_block and whole_tiles:
        plan = head_shards
    else:
        plan = clustered_shards
    return plan(
        probe_vectors,
        lookup_vectors,
        content_vectors,
        result_cotangent,
        logit_softness,
        block_grouping,
        neighborhood_span,
    )


def solution(mesh):
    in_specs = (
        P("dp", "seq", None),
        P("dp", "seq", None),
        P("dp", "seq", None),
        P("dp", "seq", None),
        P(),
        P("dp", None, None, None),
        P(),
    )
    out_specs = (P("dp", "seq", None), P("dp", "seq", None), P("dp", "seq", None), P())
    return jax.shard_map(shards, mesh=mesh, in_specs=in_specs, out_specs=out_specs, check_vma=False)
```

```python
import functools
import math

import jax
import jax.numpy as jnp
from jax import lax
from jax.experimental import pallas as pl
from jax.experimental.pallas import tpu as pltpu
from jax.sharding import PartitionSpec as P

HD = 128
BLK = 128


blocked_score = -1e30


def shifted(value, axis, steps):
    count = lax.axis_size(axis)
    first, last = (max(0, -steps), min(count, count - steps))
    return lax.ppermute(value, axis, [(source, source + steps) for source in range(first, last)])


def lifted(array_in):
    return lax.optimization_barrier(array_in.astype(jnp.bfloat16)).astype(jnp.float32)


def head_major(tokens_in, block_len):
    token_count, feature_count = tokens_in.shape
    return tokens_in.reshape(
        token_count // block_len, block_len, feature_count // HD, HD
    ).transpose(2, 0, 1, 3)


def token_major(blocks_in):
    head_count, block_count, block_len, depth = blocks_in.shape
    return blocks_in.transpose(1, 2, 0, 3).reshape(1, block_count * block_len, head_count * depth)


def window_parts(query_block, prev_keys, prev_values, grad_block, usable, window_width, temper):
    block_len = query_block.shape[-2]
    inverse_root = 1.0 / math.sqrt(query_block.shape[-1])
    raw_scores = (
        jnp.einsum("...td,...sd->...ts", query_block, prev_keys, preferred_element_type=jnp.float32)
        * inverse_root
    )
    query_pos = lax.broadcasted_iota(jnp.int32, (block_len, block_len), 0)
    key_pos = lax.broadcasted_iota(jnp.int32, (block_len, block_len), 1)
    pair_mask = usable[..., None, None] & (
        key_pos > query_pos + block_len - window_width[..., None, None]
    )
    scores = temper[..., None, None] * raw_scores
    row_top = jnp.max(jnp.where(pair_mask, scores, blocked_score), axis=-1)
    weights = jnp.where(pair_mask, jnp.exp(scores - row_top[..., None]), 0.0)
    prob_grad = jnp.einsum(
        "...td,...sd->...ts", grad_block, prev_values, preferred_element_type=jnp.float32
    )
    return (
        raw_scores,
        pair_mask,
        prob_grad,
        row_top,
        jnp.sum(weights, axis=-1),
        jnp.sum(weights * prob_grad, axis=-1),
    )


def window_grads(
    raw_scores,
    pair_mask,
    prob_grad,
    query_block,
    prev_keys,
    grad_block,
    log_total,
    row_delta,
    temper,
):
    inverse_root = 1.0 / math.sqrt(query_block.shape[-1])
    scaling = (temper * inverse_root)[..., None, None]
    probability = jnp.where(
        pair_mask, jnp.exp(temper[..., None, None] * raw_scores - log_total[..., None]), 0.0
    )
    score_grad = probability * (prob_grad - row_delta[..., None])
    prob_low = probability.astype(jnp.bfloat16)
    grad_low = score_grad.astype(jnp.bfloat16)
    query_part = (
        jnp.einsum("...ts,...sd->...td", grad_low, prev_keys, preferred_element_type=jnp.float32)
        * scaling
    )
    key_part = (
        jnp.einsum("...ts,...td->...sd", grad_low, query_block, preferred_element_type=jnp.float32)
        * scaling
    )
    value_part = jnp.einsum(
        "...ts,...td->...sd", prob_low, grad_block, preferred_element_type=jnp.float32
    )
    temper_part = jnp.sum(score_grad * raw_scores, axis=(-2, -1))
    return (query_part, key_part, value_part, temper_part)


def cluster_pair(
    query_items,
    key_items,
    value_items,
    grad_items,
    live_items,
    temper,
    window_top,
    window_total,
    window_mass,
):
    item_count, block_len, depth = query_items.shape
    row_count = item_count * block_len
    group_rows = 4 * block_len
    inverse_root = 1.0 / math.sqrt(depth)
    scaling = temper * inverse_root
    query_rows = query_items.reshape(row_count, depth)
    key_rows = key_items.reshape(row_count, depth)
    value_rows = value_items.reshape(row_count, depth)
    grad_rows = grad_items.reshape(row_count, depth)
    key_item = jnp.arange(row_count) // block_len
    key_token = jnp.arange(row_count) % block_len
    live_rows = jnp.repeat(live_items, block_len)
    top_rows = window_top.reshape(row_count)
    total_rows = window_total.reshape(row_count)
    mass_rows = window_mass.reshape(row_count)

    def group_step(carry, start_row):
        key_acc, value_acc, temper_acc = carry
        query_group = lax.dynamic_slice_in_dim(query_rows, start_row, group_rows, 0)
        grad_group = lax.dynamic_slice_in_dim(grad_rows, start_row, group_rows, 0)
        group_live = lax.dynamic_slice_in_dim(live_rows, start_row, group_rows, 0)
        group_top = lax.dynamic_slice_in_dim(top_rows, start_row, group_rows, 0)
        group_total = lax.dynamic_slice_in_dim(total_rows, start_row, group_rows, 0)
        group_mass = lax.dynamic_slice_in_dim(mass_rows, start_row, group_rows, 0)
        query_item = (start_row + jnp.arange(group_rows)) // block_len
        query_token = jnp.arange(group_rows) % block_len
        earlier = (key_item[None, :] < query_item[:, None]) | (
            key_item[None, :] == query_item[:, None]
        ) & (key_token[None, :] <= query_token[:, None])
        pair_mask = group_live[:, None] & live_rows[None, :] & earlier
        raw_scores = (
            lax.dot_general(
                query_group, key_rows, (((1,), (1,)), ((), ())), preferred_element_type=jnp.float32
            )
            * inverse_root
        )
        scores = temper * raw_scores
        row_top = jnp.maximum(
            jnp.max(jnp.where(pair_mask, scores, blocked_score), axis=1), group_top
        )
        weights = jnp.where(pair_mask, jnp.exp(scores - row_top[:, None]), 0.0)
        row_total = jnp.sum(weights, axis=1) + group_total * jnp.exp(group_top - row_top)
        log_total = row_top + jnp.log(jnp.where(group_live, row_total, 1.0))
        probability = jnp.where(pair_mask, jnp.exp(scores - log_total[:, None]), 0.0)
        prob_grad = lax.dot_general(
            grad_group, value_rows, (((1,), (1,)), ((), ())), preferred_element_type=jnp.float32
        )
        row_delta = jnp.sum(probability * prob_grad, axis=1) + group_mass * jnp.exp(
            group_top - log_total
        )
        score_grad = probability * (prob_grad - row_delta[:, None])
        prob_low = probability.astype(jnp.bfloat16)
        grad_low = score_grad.astype(jnp.bfloat16)
        query_part = jnp.dot(grad_low, key_rows, preferred_element_type=jnp.float32) * scaling
        key_acc = (
            key_acc
            + lax.dot_general(
                grad_low, query_group, (((0,), (0,)), ((), ())), preferred_element_type=jnp.float32
            )
            * scaling
        )
        value_acc = value_acc + lax.dot_general(
            prob_low, grad_group, (((0,), (0,)), ((), ())), preferred_element_type=jnp.float32
        )
        temper_acc = temper_acc + jnp.sum(score_grad * raw_scores)
        return ((key_acc, value_acc, temper_acc), (query_part, log_total, row_delta))

    start_rows = jnp.arange(item_count // 4) * group_rows
    initial = (
        jnp.zeros((row_count, depth), jnp.float32),
        jnp.zeros((row_count, depth), jnp.float32),
        jnp.zeros((), jnp.float32),
    )
    (key_acc, value_acc, temper_acc), (query_part, log_total, row_delta) = lax.scan(
        group_step, initial, start_rows
    )
    return (
        query_part.reshape(item_count, block_len, depth),
        log_total.reshape(item_count, block_len),
        row_delta.reshape(item_count, block_len),
        key_acc.reshape(item_count, block_len, depth),
        value_acc.reshape(item_count, block_len, depth),
        temper_acc,
    )


def clustered_shards(
    probe_vectors,
    lookup_vectors,
    content_vectors,
    result_cotangent,
    logit_softness,
    block_grouping,
    neighborhood_span,
):
    seq_count = lax.axis_size("seq")
    position = lax.axis_index("seq")
    tokens = probe_vectors.shape[1]
    head_count = probe_vectors.shape[2] // HD
    local_blocks = tokens // BLK
    block_count = local_blocks * seq_count
    cluster_count = max(1, block_count // 8)
    capacity = min(12, block_count)
    owned_pairs = cluster_count * head_count // seq_count
    group_count = cluster_count // owned_pairs
    per_peer = max(1, local_blocks // group_count)
    cluster_ids = block_grouping[0, :, :, 0]
    query_home = head_major(probe_vectors[0], BLK)
    key_home = head_major(lookup_vectors[0], BLK)
    value_home = head_major(content_vectors[0], BLK)
    grad_home = head_major(result_cotangent[0], BLK)
    last_block = (lookup_vectors[0, tokens - BLK :], content_vectors[0, tokens - BLK :])
    prev_key_rows, prev_value_rows = shifted((last_block[0], last_block[1]), "seq", 1)
    prev_keys = jnp.concatenate([head_major(prev_key_rows, BLK), key_home[:, :-1]], axis=1)
    prev_values = jnp.concatenate([head_major(prev_value_rows, BLK), value_home[:, :-1]], axis=1)
    first_block = position * local_blocks
    before = jnp.concatenate(
        [jnp.full((head_count, 1), -1, jnp.int32), cluster_ids[:, :-1]], axis=1
    )
    my_ids = lax.dynamic_slice_in_dim(cluster_ids, first_block, local_blocks, 1)
    my_before = lax.dynamic_slice_in_dim(before, first_block, local_blocks, 1)
    global_block = first_block + jnp.arange(local_blocks)
    usable_home = (global_block[None, :] >= 1) & (my_before != my_ids)
    peer_index = jnp.arange(seq_count)
    peer_head = peer_index * owned_pairs // cluster_count
    slot_range = jnp.arange(per_peer)
    local_range = jnp.arange(local_blocks)
    owner_index = (jnp.arange(head_count)[:, None] * cluster_count + my_ids) // owned_pairs
    peer_ids = jnp.take(my_ids, peer_head, axis=0)
    goes = (peer_head[:, None] * cluster_count + peer_ids) // owned_pairs == peer_index[:, None]
    send_rank = jnp.cumsum(goes.astype(jnp.int32), axis=1) - 1
    send_pick = goes[:, None, :] & (send_rank[:, None, :] == slot_range[None, :, None])
    send_block = jnp.sum(jnp.where(send_pick, local_range[None, None, :], 0), axis=2)
    send_flat = peer_head[:, None] * local_blocks + send_block
    home_rank = jnp.take_along_axis(send_rank, owner_index, axis=0)
    home_pos = owner_index * per_peer + home_rank
    pair_index = position * owned_pairs + jnp.arange(owned_pairs)
    split_for_couple = pair_index // cluster_count
    pair_cluster = pair_index % cluster_count
    my_head = position * owned_pairs // cluster_count
    split_numbers = jnp.take(cluster_ids, my_head, axis=0)
    member = split_numbers[None, :] == pair_cluster[:, None]
    member_rank = jnp.cumsum(member.astype(jnp.int32), axis=1) - 1
    member_count = jnp.sum(member.astype(jnp.int32), axis=1)
    picked = member[:, None, :] & (member_rank[:, None, :] == jnp.arange(capacity)[None, :, None])
    member_block = jnp.sum(jnp.where(picked, jnp.arange(block_count)[None, None, :], 0), axis=2)
    live_members = jnp.arange(capacity)[None, :] < member_count[:, None]
    mine = (my_head * cluster_count + split_numbers) // owned_pairs == position
    mine_grid = mine.reshape(seq_count, local_blocks)
    recv_rank = jnp.cumsum(mine_grid.astype(jnp.int32), axis=1) - 1
    recv_pos = (peer_index[:, None] * per_peer + recv_rank).reshape(block_count)
    member_pos = jnp.take(recv_pos, member_block)
    couple_softness = jnp.take(logit_softness, split_for_couple)
    pair_onehot = (split_for_couple[:, None] == jnp.arange(head_count)[None, :]).astype(jnp.float32)
    slot_pair = my_head * cluster_count + split_numbers - position * owned_pairs
    same_cluster = split_numbers[:, None] == split_numbers[None, :]
    earlier_block = jnp.arange(block_count)[None, :] < jnp.arange(block_count)[:, None]
    slot_rank = jnp.sum((same_cluster & earlier_block).astype(jnp.int32), axis=1)
    back_pos = jnp.clip(slot_pair, 0, owned_pairs - 1) * capacity + jnp.clip(
        slot_rank, 0, capacity - 1
    )
    back_grid = back_pos.reshape(seq_count, local_blocks)
    back_pick = mine_grid[:, None, :] & (recv_rank[:, None, :] == slot_range[None, :, None])
    back_flat = jnp.sum(jnp.where(back_pick, back_grid[:, None, :], 0), axis=2)

    def to_peers(array_in):
        flat = array_in.reshape((head_count * local_blocks,) + array_in.shape[2:])
        return jnp.take(flat, send_flat, axis=0)

    def members(array_in):
        flat = array_in.reshape((seq_count * per_peer,) + array_in.shape[2:])
        return jnp.take(flat, member_pos, axis=0)

    def to_owner(array_in):
        flat = array_in.reshape((owned_pairs * capacity,) + array_in.shape[2:])
        return jnp.take(flat, back_flat, axis=0)

    def from_peers(array_in):
        flat = array_in.reshape((seq_count * per_peer,) + array_in.shape[2:])
        return jnp.take(flat, home_pos, axis=0)

    raw_w, mask_w, pgrad_w, top_w, total_w, mass_w = window_parts(
        query_home,
        prev_keys,
        prev_values,
        grad_home,
        usable_home,
        neighborhood_span[:, None],
        logit_softness[:, None],
    )
    arrived = (
        lax.all_to_all(to_peers(query_home), "seq", split_axis=0, concat_axis=0, tiled=True),
        lax.all_to_all(to_peers(key_home), "seq", split_axis=0, concat_axis=0, tiled=True),
        lax.all_to_all(to_peers(value_home), "seq", split_axis=0, concat_axis=0, tiled=True),
        lax.all_to_all(to_peers(grad_home), "seq", split_axis=0, concat_axis=0, tiled=True),
    )
    arrived_stats = (
        lax.all_to_all(to_peers(top_w), "seq", split_axis=0, concat_axis=0, tiled=True),
        lax.all_to_all(to_peers(total_w), "seq", split_axis=0, concat_axis=0, tiled=True),
        lax.all_to_all(to_peers(mass_w), "seq", split_axis=0, concat_axis=0, tiled=True),
    )
    query_m, key_m, value_m, grad_m = [members(item_in) for item_in in arrived]
    top_m, total_m, mass_m = [members(item_in) for item_in in arrived_stats]

    def split_pair(pair_inputs):
        query_i, key_i, value_i, grad_i, live_i, temper_i, top_i, total_i, mass_i = pair_inputs
        query_c, log_total, row_delta, key_c, value_c, temper_c = cluster_pair(
            query_i, key_i, value_i, grad_i, live_i, temper_i, top_i, total_i, mass_i
        )
        return (
            query_c.astype(jnp.bfloat16),
            key_c.astype(jnp.bfloat16),
            value_c.astype(jnp.bfloat16),
            log_total,
            row_delta,
            temper_c,
        )

    owner_results = lax.map(
        split_pair,
        (query_m, key_m, value_m, grad_m, live_members, couple_softness, top_m, total_m, mass_m),
    )
    returned = (
        lax.all_to_all(to_owner(owner_results[0]), "seq", split_axis=0, concat_axis=0, tiled=True),
        lax.all_to_all(to_owner(owner_results[1]), "seq", split_axis=0, concat_axis=0, tiled=True),
        lax.all_to_all(to_owner(owner_results[2]), "seq", split_axis=0, concat_axis=0, tiled=True),
    )
    returned_stats = (
        lax.all_to_all(to_owner(owner_results[3]), "seq", split_axis=0, concat_axis=0, tiled=True),
        lax.all_to_all(to_owner(owner_results[4]), "seq", split_axis=0, concat_axis=0, tiled=True),
    )
    query_cluster = from_peers(returned[0])
    key_cluster = from_peers(returned[1])
    value_cluster = from_peers(returned[2])
    log_home = from_peers(returned_stats[0])
    delta_home = from_peers(returned_stats[1])
    query_w, key_w, value_w, temper_w = window_grads(
        raw_w,
        mask_w,
        pgrad_w,
        query_home,
        prev_keys,
        grad_home,
        log_home,
        delta_home,
        logit_softness[:, None],
    )
    query_out = (query_cluster.astype(jnp.float32) + lifted(query_w)).astype(jnp.bfloat16)
    key_window = key_w.astype(jnp.bfloat16)
    value_window = value_w.astype(jnp.bfloat16)
    temper_local = jnp.sum(owner_results[5][:, None] * pair_onehot, axis=0) + jnp.sum(
        temper_w, axis=1
    )
    edge_keys, edge_values = shifted((key_window[:, 0], value_window[:, 0]), "seq", -1)
    key_next = jnp.concatenate([key_window[:, 1:], edge_keys[:, None]], axis=1)
    value_next = jnp.concatenate([value_window[:, 1:], edge_values[:, None]], axis=1)
    key_out = (key_cluster.astype(jnp.float32) + key_next.astype(jnp.float32)).astype(jnp.bfloat16)
    value_out = (value_cluster.astype(jnp.float32) + value_next.astype(jnp.float32)).astype(
        jnp.bfloat16
    )
    temper_total = lax.psum(temper_local, ("seq", "dp"))
    temper_grad = temper_total / (lax.axis_size("dp") * tokens * seq_count)
    return (token_major(query_out), token_major(key_out), token_major(value_out), temper_grad)


TILE = 256
EXTRA = 16
MIB = 1024 * 1024
PIECES = 4
QUERY, KEY, VALUE, GRAD = range(4)


def columns_of(index):
    return pl.ds(pl.multiple_of(index * HD, HD), HD)


def rows_of(index):
    return pl.ds(pl.multiple_of(index * BLK, BLK), BLK)


def tile_rows(tile):
    return slice(tile * TILE, (tile + 1) * TILE)


def position(half_count):
    me = lax.axis_index("seq")
    half = jnp.where(me >= half_count, 1, 0)
    return me, half, me - half * half_count


def kernel_call(
    kernel, name, operands, in_specs, out_shape, scratch, vmem_mib, flops=0, out_spaces=None,
    aliases=None,
):
    bytes_accessed = sum(
        math.prod(item.shape) * item.dtype.itemsize for item in (*operands, *out_shape)
    )
    return pl.pallas_call(
        kernel,
        out_shape=out_shape,
        in_specs=in_specs,
        out_specs=[
            pl.BlockSpec(memory_space=space)
            for space in out_spaces or [pltpu.VMEM] * len(out_shape)
        ],
        scratch_shapes=scratch,
        input_output_aliases=aliases or {},
        cost_estimate=pl.CostEstimate(
            flops=flops, bytes_accessed=bytes_accessed, transcendentals=0
        ),
        compiler_params=pltpu.CompilerParams(vmem_limit_bytes=vmem_mib * MIB),
        name=name,
    )(*operands)


def pack_kernel(*refs, half_count):
    arrays, within_ref, foreign_refs = refs[:4], refs[4], refs[5:7]
    held, within, across, arrival, left_within, left_across = refs[7:]
    me, half, _ = position(half_count)
    piece = BLK // PIECES
    arrivals = [
        [
            pltpu.make_async_copy(
                array_ref.at[0, part * piece : (part + 1) * piece, :],
                held.at[place, part * piece : (part + 1) * piece, :],
                arrival.at[place, part],
            )
            for part in range(PIECES)
        ]
        for place, array_ref in enumerate(arrays)
    ]
    for copies in arrivals:
        for copy in copies:
            copy.start()
    leaving = []
    for place, copies in enumerate(arrivals):
        for copy in copies:
            copy.wait()
        for slot, base in enumerate((half * half_count, (1 - half) * half_count)):
            rows = slice((slot * 4 + place) * BLK, (slot * 4 + place + 1) * BLK)
            for peer in range(half_count):
                within[peer, rows, :] = held[place, :, columns_of(base + peer)]
            leaving.append(
                pltpu.make_async_copy(
                    within.at[:, rows, :], within_ref.at[:, rows, :], left_within.at[place, slot]
                )
            )
            leaving[-1].start()
    first = jnp.where(half == 0, KEY, QUERY)
    second = jnp.where(half == 0, VALUE, GRAD)
    for core, foreign_ref in enumerate(foreign_refs):
        for step in range(half_count // 2):
            columns = columns_of(me ^ core ^ (half_count + 2 * step))
            across[core, step, :BLK, :] = held[first, :, columns]
            across[core, step, BLK:, :] = held[second, :, columns]
        leaving.append(pltpu.make_async_copy(across.at[core], foreign_ref, left_across.at[core]))
        leaving[-1].start()
    for copy in leaving:
        copy.wait()


def packed(arrays, half_count):
    width = arrays[0].shape[2]
    within_shape, across_shape = (half_count, 8 * BLK, HD), (half_count // 2, 2 * BLK, HD)
    return kernel_call(
        functools.partial(pack_kernel, half_count=half_count),
        "pack_heads",
        arrays,
        [pl.BlockSpec(memory_space=pl.ANY)] * 4,
        [jax.ShapeDtypeStruct(within_shape, jnp.bfloat16)]
        + [jax.ShapeDtypeStruct(across_shape, jnp.bfloat16)] * 2,
        [
            pltpu.VMEM((4, BLK, width), jnp.bfloat16),
            pltpu.VMEM(within_shape, jnp.bfloat16),
            pltpu.VMEM((2, *across_shape), jnp.bfloat16),
            pltpu.SemaphoreType.DMA((4, PIECES)),
            pltpu.SemaphoreType.DMA((4, 2)),
            pltpu.SemaphoreType.DMA((2,)),
        ],
        60,
        out_spaces=[pl.ANY] * 3,
    )


def dot_rows(left, right):
    return lax.dot_general(
        left, right, (((1,), (1,)), ((), ())), preferred_element_type=jnp.float32
    )


def dot_plain(left, right):
    return lax.dot_general(
        left, right, (((1,), (0,)), ((), ())), preferred_element_type=jnp.float32
    )


def from_blocks(ref, place):
    def rows(start, stop):
        per_tile = TILE // BLK
        return jnp.concatenate(
            [ref[block, place] for block in range(start * per_tile, stop * per_tile)],
            axis=0,
        )

    return rows


def from_array(ref, place):
    return lambda start, stop: ref[place, start * TILE : stop * TILE, :]


class Region:
    def __init__(self, square, sources, tiles, scaling, bias_ref=None, least_ref=None, first=0):
        self.square, self.sources, self.tiles, self.scaling = square, sources, tiles, scaling
        self.bias_ref, self.least_ref, self.first = bias_ref, least_ref, first

    def rows(self, which, start, stop):
        return self.sources[which](start, stop)

    def scale_of(self, array):
        return 1.0 if array == VALUE else self.scaling[:, :HD]

    def keys_of(self, tile):
        return range(self.tiles if self.square else tile + 1)

    def scores(self, tile_key, tile_query):
        per_tile = TILE // BLK
        scores = dot_rows(
            self.rows(KEY, tile_key, tile_key + 1), self.rows(QUERY, tile_query, tile_query + 1)
        ) * (self.scaling * math.log2(math.e))
        before = self.tiles * per_tile if self.square else 0
        rows = []
        for sub_key in range(per_tile):
            key_block = tile_key * per_tile + sub_key
            pieces = []
            for sub_query in range(per_tile):
                query_block = tile_query * per_tile + sub_query
                lanes = slice(sub_query * BLK, (sub_query + 1) * BLK)
                piece = scores[sub_key * BLK : (sub_key + 1) * BLK, lanes]
                apart = before + query_block - key_block
                if apart < 0:
                    piece = jnp.full_like(piece, blocked_score)
                elif apart == 0:
                    piece = jnp.where(key_minus_query() <= 0, piece, blocked_score)
                elif apart == 1:
                    row = self.first + (0 if self.square else key_block)
                    least = self.least_ref[row : row + 1, :]
                    piece = jnp.where(key_minus_query() > least, piece, blocked_score)
                else:
                    at = slice(query_block * BLK, (query_block + 1) * BLK)
                    piece = piece + self.bias_ref[key_block : key_block + 1, at]
                pieces.append(piece)
            rows.append(jnp.concatenate(pieces, axis=1))
        return jnp.concatenate(rows, axis=0)


def diagonal(slot, arrived_ref, scales_ref, bias_ref=None, least_ref=None):
    blocks = arrived_ref.shape[0]
    sources = [from_blocks(arrived_ref, slot * 4 + place) for place in range(4)]
    bias = None if bias_ref is None else bias_ref.at[slot]
    first = slot * (blocks - 1)
    scaling = scales_ref[slot : slot + 1, :]
    return Region(False, sources, blocks * BLK // TILE, scaling, bias, least_ref, first)


def square(square_ref, scales_ref, bias_ref=None, least_ref=None):
    tiles = square_ref.shape[1] // TILE
    sources = [from_array(square_ref, place) for place in range(4)]
    bias = None if bias_ref is None else bias_ref.at[2]
    first = 2 * (tiles * TILE // BLK - 1)
    return Region(True, sources, tiles, scales_ref[0:1, :], bias, least_ref, first)


def key_minus_query():
    shape = (BLK, BLK)
    return lax.broadcasted_iota(jnp.int32, shape, 0) - lax.broadcasted_iota(jnp.int32, shape, 1)


def statistics(region, weight_ref, towards_ref, out_ref, first_row):
    for tile in range(region.tiles):
        here = tile_rows(tile)
        top = jnp.full((1, TILE), blocked_score, jnp.float32)
        for other in region.keys_of(tile):
            raw = region.scores(other, tile)
            weight_ref[tile_rows(other), here] = raw
            top = jnp.maximum(top, jnp.max(raw, axis=0, keepdims=True))
        sums = [jnp.zeros((1, TILE), jnp.float32)] * 4
        for other in region.keys_of(tile):
            there = tile_rows(other)
            raw = weight_ref[there, here]
            weight = jnp.exp2(raw - top)
            towards = dot_rows(
                region.rows(VALUE, other, other + 1), region.rows(GRAD, tile, tile + 1)
            )
            weight_ref[there, here] = weight
            towards_ref[there, here] = towards
            pulled, weighted = weight * towards, weight * raw
            terms = (weight, pulled, pulled * raw, weighted)
            sums = [
                total + jnp.sum(term, axis=0, keepdims=True) for total, term in zip(sums, terms)
            ]
        for row, value in enumerate((top, *sums)):
            out_ref[first_row + row : first_row + row + 1, here] = value


def gradients(
    region, weight_ref, towards_ref, top, log_total, delta, prob_low, grad_low, keys_flat, emit=None
):
    keys_flat[...] = region.rows(KEY, 0, region.tiles).T
    share = jnp.exp2(top - log_total)
    query_parts, key_parts, value_parts = [], [], []
    for tile in range(region.tiles):
        here = tile_rows(tile)
        for other in region.keys_of(tile):
            there = tile_rows(other)
            probability = weight_ref[there, here] * share[:, here]
            prob_low[there, here] = probability.astype(jnp.bfloat16)
            grad_low[there, here] = (
                probability * (towards_ref[there, here] - delta[:, here])
            ).astype(jnp.bfloat16)
        upto = slice(0, len(region.keys_of(tile)) * TILE)
        query_parts.append(dot_plain(keys_flat[:, upto], grad_low[upto, here]).T)
    if emit is not None:
        emit(QUERY, query_parts)
    for low, which, parts in ((grad_low, QUERY, key_parts), (prob_low, GRAD, value_parts)):
        for tile in range(region.tiles):
            first = 0 if region.square else tile
            onward = slice(first * TILE, region.tiles * TILE)
            parts.append(
                dot_plain(low[tile_rows(tile), onward], region.rows(which, first, region.tiles))
            )
        if emit is not None:
            emit(KEY if which == QUERY else VALUE, parts)
    return query_parts, key_parts, value_parts


def merged(first, second):
    top = jnp.maximum(first[0], second[0])
    left, right = jnp.exp2(first[0] - top), jnp.exp2(second[0] - top)
    total = first[1] * left + second[1] * right
    mass = first[2] * left + second[2] * right
    return top + jnp.log2(total), mass / total


def alone(rows):
    return rows[0] + jnp.log2(rows[1]), rows[2] / rows[1]


def rows_at(ref, first, count=5):
    return [ref[first + row : first + row + 1, :] for row in range(count)]


def temper_terms(rows, totals, scale_row):
    log_total, delta = totals
    terms = (rows[3] - delta * rows[4]) * jnp.exp2(rows[0] - log_total)
    folded = sum(terms[:, start : start + HD] for start in range(0, terms.shape[1], HD))
    return folded / (scale_row[:, :HD] * (math.sqrt(HD) * math.log2(math.e)))


def put(within_ref, array, tile, value):
    per_tile = TILE // BLK
    for sub in range(per_tile):
        within_ref[tile * per_tile + sub, array * BLK : (array + 1) * BLK, :] = value[
            sub * BLK : (sub + 1) * BLK, :
        ].astype(jnp.bfloat16)


def scaled(region, parts):
    scale = region.scaling[:, :HD]
    return [[value * scale for value in part] for part in parts[:2]] + [parts[2]]


def masks_kernel(softness_ref, ids_ref, span_ref, scales_ref, bias_ref, least_ref, *, half_count):
    me, half, _ = position(half_count)
    base = half * half_count
    regions = (
        (me, base, base),
        (me ^ half_count, base, base),
        (me, 0, half_count),
    )
    for slot, (head, key_base, query_base) in enumerate(regions):
        if slot < 2:
            scales_ref[slot : slot + 1, :] = jnp.full(
                (1, TILE), softness_ref[head] * (1.0 / math.sqrt(HD)), jnp.float32
            )

        def same(key_block, query_block):
            return ids_ref[head, key_base + key_block] == ids_ref[head, query_base + query_block]

        def bias(key_block, query_block):
            return jnp.full(
                (1, BLK), jnp.where(same(key_block, query_block), 0.0, blocked_score), jnp.float32
            )

        for key_block in range(half_count):
            bias_ref[slot, key_block : key_block + 1, :] = jnp.concatenate(
                [bias(key_block, query_block) for query_block in range(half_count)], axis=1
            )
        pairs = [(block, block + 1) for block in range(half_count - 1)]
        if slot == 2:
            pairs = [(half_count - 1, 0)]
        for place, pair in enumerate(pairs):
            least = jnp.where(same(*pair), -BLK, BLK - span_ref[head])
            row = slot * (half_count - 1) + place
            least_ref[row : row + 1, :] = jnp.full((1, BLK), least, jnp.int32)


def within_kernel(
    arrived_ref, scales_ref, bias_ref, least_ref, stats_ref, parts_ref, own_weight, own_towards, other_weight, other_towards, *scratch, half_count
):
    _, half, _ = position(half_count)
    kept = ((own_weight, own_towards), (other_weight, other_towards))
    for slot in range(2):
        region = diagonal(slot, arrived_ref, scales_ref, bias_ref, least_ref)
        statistics(region, *kept[slot], stats_ref, slot * 5)

    @pl.when(half == 0)
    def _():
        region = diagonal(0, arrived_ref, scales_ref)
        single = alone(rows_at(stats_ref, 0))
        parts = gradients(region, *kept[0], stats_ref[0:1, :], *single, *scratch)
        for place, tiles in enumerate(scaled(region, parts)):
            for tile, value in enumerate(tiles):
                parts_ref[place, tile_rows(tile), :] = value


def square_kernel(arrived_ref, scales_ref, bias_ref, least_ref, stats_ref, *refs, half_count):
    across_refs = refs[: half_count // 2]
    square_ref, message_ref, square_stats, weight, towards = refs[half_count // 2 :]
    _, half, place = position(half_count)
    first = jnp.where(half == 0, QUERY, KEY)
    second = jnp.where(half == 0, GRAD, VALUE)
    for step, across_ref in enumerate(across_refs):
        for core in range(2):
            rows = rows_of(place ^ core ^ (2 * step))
            square_ref[first, rows, :] = across_ref[core, :BLK, :]
            square_ref[second, rows, :] = across_ref[core, BLK:, :]
    for kept in (jnp.where(half == 0, KEY, QUERY), jnp.where(half == 0, VALUE, GRAD)):
        for block in range(half_count):
            square_ref[kept, block * BLK : (block + 1) * BLK, :] = arrived_ref[block, kept]
    region = square(square_ref, scales_ref, bias_ref, least_ref)
    statistics(region, weight, towards, square_stats, 0)
    own, other, crossing = rows_at(stats_ref, 0), rows_at(stats_ref, 5), rows_at(square_stats, 0)
    for row in range(5):
        message_ref[row : row + 1, :] = jnp.where(half == 0, crossing[row], other[row])
    own_scale, other_scale = scales_ref[0:1, :], scales_ref[1:2, :]
    both = merged(own, crossing)
    whole = temper_terms(own, both, own_scale) + temper_terms(crossing, both, own_scale)
    single = temper_terms(own, alone(own), own_scale)
    message_ref[5:6, :HD] = jnp.where(half == 0, single, whole)
    message_ref[6:7, :HD] = temper_terms(other, alone(other), other_scale)


def first_kernel(
    arrived_ref, scales_ref, square_ref, stats_ref, square_stats,
    own_weight, own_towards, other_weight, other_towards, square_weight, square_towards,
    across_ref, within_ref, ready, ready_sem, *scratch, half_count
):
    _, half, _ = position(half_count)
    leaving = sends(ready, within_ref, ready_sem, (1 - half) * 3)

    @pl.when(half == 0)
    def _():
        region = diagonal(1, arrived_ref, scales_ref)

        def send(array, parts):
            for tile, part in enumerate(parts):
                put(ready, array, tile, part * region.scale_of(array))
            leaving[array].start()

        totals = alone(rows_at(stats_ref, 5))
        gradients(
            region, other_weight, other_towards, stats_ref[5:6, :], *totals, *scratch, emit=send
        )

    @pl.when(half == 1)
    def _():
        totals = merged(rows_at(stats_ref, 0), rows_at(square_stats, 0))
        region = square(square_ref, scales_ref)
        parts = gradients(
            region, square_weight, square_towards, square_stats[0:1, :], *totals, *scratch
        )
        across_query, *foreign = scaled(region, parts)
        for array, tiles in enumerate(foreign):
            for tile, value in enumerate(tiles):
                across_ref[array, tile_rows(tile), :] = value.astype(jnp.bfloat16)
        region = diagonal(0, arrived_ref, scales_ref)

        def send(array, parts):
            for tile, part in enumerate(parts):
                value = part * region.scale_of(array)
                put(ready, array, tile, value + across_query[tile] if array == QUERY else value)
            leaving[array].start()

        gradients(
            region, own_weight, own_towards, stats_ref[0:1, :], *totals, *scratch, emit=send
        )

    for copy in leaving:
        copy.wait()


def sends(ready, within_ref, sems, first):
    copies = []
    for array in range(3):
        rows = slice(array * BLK, (array + 1) * BLK)
        copies.append(
            pltpu.make_async_copy(
                ready.at[:, rows, :], within_ref.at[:, rows_of(first + array), :], sems.at[array]
            )
        )
    return copies


def temper_rows(own, other):
    row = lax.broadcasted_iota(jnp.int32, (EXTRA, HD), 0)
    rows = jnp.zeros((EXTRA, HD), jnp.float32)
    for place, terms in enumerate((own, other)):
        rest = jnp.broadcast_to(jnp.sum(terms, axis=1, keepdims=True), (EXTRA, HD))
        for piece in range(3):
            high = rest.astype(jnp.bfloat16).astype(jnp.float32)
            rows = jnp.where(row == place * 3 + piece, high, rows)
            rest = rest - high
    return rows.astype(jnp.bfloat16)


def finish_kernel(
    arrived_ref, scales_ref, square_ref, message_ref, received_ref, stats_ref, square_stats,
    parts_ref, square_weight, square_towards, other_weight, other_towards, across_ref, begun_ref,
    within_ref, *refs, half_count
):
    del begun_ref
    chunk_refs = refs[:2]
    across, ready, tail, ready_sem, tail_sem, *scratch = refs[2:]
    _, half, place = position(half_count)
    leaving = sends(ready, within_ref, ready_sem, half * 3)
    sent, came = rows_at(message_ref, 0), rows_at(received_ref, 0)
    totals = merged(sent, came)
    scale = jnp.where(half == 0, scales_ref[0:1, :], scales_ref[1:2, :])
    shared = temper_terms(sent, totals, scale) + temper_terms(came, totals, scale)
    mine, theirs = message_ref[5:6, :HD], received_ref[5:6, :HD]
    own = mine + jnp.where(half == 0, shared, received_ref[6:7, :HD])
    other = theirs + jnp.where(half == 0, message_ref[6:7, :HD], shared)
    pieces = temper_rows(own, other)
    for block in range(half_count):
        tail[block] = pieces
    leaving.append(
        pltpu.make_async_copy(tail, within_ref.at[:, 6 * BLK : 6 * BLK + EXTRA, :], tail_sem)
    )
    leaving[-1].start()

    def chunks():
        for core, chunk_ref in enumerate(chunk_refs):
            for step in range(half_count // 2):
                yield step, chunk_ref, rows_of(place ^ core ^ (2 * step))

    @pl.when(half == 0)
    def _():
        region = square(square_ref, scales_ref)

        def send(array, parts):
            for tile, part in enumerate(parts):
                here = tile_rows(tile)
                value = part * region.scale_of(array)
                if array == QUERY:
                    across[here, :] = value.astype(jnp.bfloat16)
                    put(ready, array, tile, parts_ref[array, here, :])
                else:
                    put(ready, array, tile, parts_ref[array, here, :] + value)
            leaving[array].start()

        gradients(
            region, square_weight, square_towards, square_stats[0:1, :], *totals, *scratch, emit=send
        )
        for step, chunk_ref, rows in chunks():
            chunk_ref[step, :BLK, :] = across[rows, :]
            chunk_ref[step, BLK:, :] = jnp.zeros((BLK, HD), jnp.bfloat16)

    @pl.when(half == 1)
    def _():
        region = diagonal(1, arrived_ref, scales_ref)

        def send(array, parts):
            for tile, part in enumerate(parts):
                put(ready, array, tile, part * region.scale_of(array))
            leaving[array].start()

        gradients(
            region, other_weight, other_towards, stats_ref[5:6, :], *totals, *scratch, emit=send
        )
        for step, chunk_ref, rows in chunks():
            chunk_ref[step, :BLK, :] = across_ref[0, rows, :]
            chunk_ref[step, BLK:, :] = across_ref[1, rows, :]

    for copy in leaving:
        copy.wait()


def temper_kernel(within_ref, temper_ref, *, half_count):
    _, half, _ = position(half_count)
    for peer in range(half_count):
        for slot, base in enumerate((half * half_count, (1 - half) * half_count)):
            rows = within_ref[peer, 3 * slot : 3 * slot + 3, :].astype(jnp.float32)
            temper_ref[pl.ds(base + peer, 1), :] = jnp.sum(rows, axis=0, keepdims=True)


def temper_sums(within, half_count):
    last = 6 * BLK // EXTRA
    return pl.pallas_call(
        functools.partial(temper_kernel, half_count=half_count),
        grid=(1,),
        out_shape=jax.ShapeDtypeStruct((2 * half_count, HD), jnp.float32),
        in_specs=[pl.BlockSpec((half_count, EXTRA, HD), lambda step: (0, last, 0))],
        out_specs=pl.BlockSpec((2 * half_count, HD), lambda step: (0, 0)),
        compiler_params=pltpu.CompilerParams(vmem_limit_bytes=4 * MIB),
        name="temper_sums",
    )(within)


def unpack_kernel(within_ref, *refs, half_count):
    across_refs = refs[: half_count // 2]
    out_refs = refs[half_count // 2 :]
    _, half, place = position(half_count)
    for step, across_ref in enumerate(across_refs):
        for core in range(2):
            peer = place ^ core ^ (2 * step)
            other = columns_of((1 - half) * half_count + peer)
            own = columns_of(half * half_count + peer)
            first = across_ref[core, :BLK, :].astype(jnp.float32)
            second = across_ref[core, BLK : 2 * BLK, :].astype(jnp.float32)
            added = (
                jnp.where(half == 0, 0.0, first),
                jnp.where(half == 0, first, 0.0),
                jnp.where(half == 0, second, 0.0),
            )
            for array, out_ref in enumerate(out_refs):
                out_ref[0, :, own] = within_ref[peer, array * BLK : (array + 1) * BLK, :]
                kept = within_ref[peer, (3 + array) * BLK : (4 + array) * BLK, :]
                out_ref[0, :, other] = (kept.astype(jnp.float32) + added[array]).astype(
                    jnp.bfloat16
                )


def join_kernel(kept_ref, taken_ref, *out_refs):
    for step, out_ref in enumerate(out_refs):
        out_ref[0] = kept_ref[step]
        out_ref[1] = taken_ref[step]


def crossed(kept, given, half_count):
    devices = range(2 * half_count)
    steps, *shape = kept.shape
    taken = lax.ppermute(given, "seq", [(source, source ^ 1) for source in devices])
    messages = kernel_call(
        join_kernel,
        "join_chunks",
        (kept, taken),
        [pl.BlockSpec(memory_space=pltpu.VMEM)] * 2,
        [jax.ShapeDtypeStruct((2, *shape), jnp.bfloat16)] * steps,
        [],
        4,
    )
    return [
        lax.ppermute(
            message, "seq", [(source, source ^ (half_count + 2 * step)) for source in devices]
        )
        for step, message in enumerate(messages)
    ]


def head_shards(
    probe_vectors,
    lookup_vectors,
    content_vectors,
    result_cotangent,
    logit_softness,
    block_grouping,
    neighborhood_span,
):
    seq_count, dp_count = lax.axis_size("seq"), lax.axis_size("dp")
    half_count = seq_count // 2
    tokens = half_count * BLK
    groups = [list(range(half_count)), list(range(half_count, seq_count))]
    settings = (logit_softness, block_grouping[0, :, :, 0], neighborhood_span)
    smem, vmem = pl.BlockSpec(memory_space=pltpu.SMEM), pl.BlockSpec(memory_space=pltpu.VMEM)
    lows = [pltpu.VMEM((tokens, tokens), jnp.bfloat16)] * 2 + [
        pltpu.VMEM((HD, tokens), jnp.bfloat16)
    ]
    rows_of_stats = jax.ShapeDtypeStruct((8, tokens), jnp.float32)
    pairs = jax.ShapeDtypeStruct((tokens, tokens), jnp.float32)
    pair_flops = 2 * tokens * tokens * HD

    def exchange_within(array_in):
        return lax.all_to_all(
            array_in, "seq", split_axis=0, concat_axis=0, axis_index_groups=groups, tiled=True
        )

    def call(
        kernel, name, operands, out_shape, scratch, flops, vmem_mib, scalars=(), out_spaces=None,
        last_in_place=False,
    ):
        in_specs = [smem] * len(scalars) + [vmem] * len(operands)
        if last_in_place:
            in_specs[-1] = pl.BlockSpec(memory_space=pl.ANY)
        return kernel_call(
            functools.partial(kernel, half_count=half_count),
            name,
            (*scalars, *operands),
            in_specs,
            out_shape,
            scratch,
            vmem_mib,
            flops,
            out_spaces,
            {len(operands) - 1: 0} if last_in_place else {},
        )

    sent, *foreign = packed(
        (probe_vectors, lookup_vectors, content_vectors, result_cotangent), half_count
    )
    arrived = exchange_within(sent).reshape(half_count, 8, BLK, HD)
    kept_parts = jax.ShapeDtypeStruct((3, tokens, HD), jnp.float32)
    masks = call(
        masks_kernel,
        "scales_and_masks",
        (),
        [
            jax.ShapeDtypeStruct((8, TILE), jnp.float32),
            jax.ShapeDtypeStruct((3, half_count, tokens), jnp.float32),
            jax.ShapeDtypeStruct((2 * half_count, BLK), jnp.int32),
        ],
        [],
        0,
        2,
        settings,
    )
    foreign[0], *masks = lax.optimization_barrier((foreign[0], *masks))
    foreign = crossed(*foreign, half_count)
    scales = masks[0]
    stats, parts, own_weight, own_towards, other_weight, other_towards = call(
        within_kernel,
        "diagonal_statistics",
        (arrived, *masks),
        [jax.ShapeDtypeStruct((16, tokens), jnp.float32), kept_parts] + [pairs] * 4,
        lows,
        2 * pair_flops,
        14,
    )
    squared, message, square_stats, square_weight, square_towards = call(
        square_kernel,
        "square_statistics",
        (arrived, *masks, stats, *foreign),
        [jax.ShapeDtypeStruct((4, tokens, HD), jnp.bfloat16)] + [rows_of_stats] * 2 + [pairs] * 2,
        [],
        2 * pair_flops,
        8,
    )
    swap = [(source, source ^ half_count) for source in range(seq_count)]
    received = lax.ppermute(message, "seq", swap)
    result = pltpu.HBM((half_count, 6 * BLK + EXTRA, HD), jnp.bfloat16)
    ready = pltpu.VMEM((half_count, 3 * BLK, HD), jnp.bfloat16)
    across, begun = call(
        first_kernel,
        "gradients_before_totals",
        (
            arrived, scales, squared, stats, square_stats, own_weight, own_towards,
            other_weight, other_towards, square_weight, square_towards,
        ),
        [jax.ShapeDtypeStruct((2, tokens, HD), jnp.bfloat16), result],
        [ready, pltpu.SemaphoreType.DMA((3,)), *lows],
        4 * pair_flops,
        14,
        out_spaces=(pltpu.VMEM, pl.ANY),
    )
    operands = (
        arrived, scales, squared, message, received, stats, square_stats, parts,
        square_weight, square_towards, other_weight, other_towards, across, begun,
    )
    within, *foreign = call(
        finish_kernel,
        "gradients_after_totals",
        operands,
        [result]
        + [jax.ShapeDtypeStruct((half_count // 2, 2 * BLK, HD), jnp.bfloat16)] * 2,
        [
            pltpu.VMEM((tokens, HD), jnp.bfloat16), ready,
            pltpu.VMEM((half_count, EXTRA, HD), jnp.bfloat16),
            pltpu.SemaphoreType.DMA((3,)), pltpu.SemaphoreType.DMA, *lows,
        ],
        2 * pair_flops,
        16,
        out_spaces=(pl.ANY, pltpu.VMEM, pltpu.VMEM),
        last_in_place=True,
    )
    across = crossed(*foreign, half_count)
    within = exchange_within(within)
    tempers = temper_sums(within, half_count)
    temper_total = tempers
    for step in range(1, dp_count):
        swap = [(source, (source + step) % dp_count) for source in range(dp_count)]
        temper_total = temper_total + lax.ppermute(tempers, "dp", swap)
    outs = kernel_call(
        functools.partial(unpack_kernel, half_count=half_count),
        "unpack_heads",
        (within, *across),
        [vmem] * (1 + len(across)),
        [jax.ShapeDtypeStruct(probe_vectors.shape, jnp.bfloat16)] * 3,
        [],
        10,
    )
    return (*outs, temper_total[:, 0] / (dp_count * BLK * seq_count))


def shards(
    probe_vectors,
    lookup_vectors,
    content_vectors,
    result_cotangent,
    logit_softness,
    block_grouping,
    neighborhood_span,
):
    head_count = probe_vectors.shape[2] // HD
    seq_count = lax.axis_size("seq")
    one_block = probe_vectors.shape[1] == BLK
    whole_tiles = seq_count * BLK % (2 * TILE) == 0 and seq_count & (seq_count - 1) == 0
    if head_count == seq_count and one_block and whole_tiles:
        plan = head_shards
    else:
        plan = clustered_shards
    return plan(
        probe_vectors,
        lookup_vectors,
        content_vectors,
        result_cotangent,
        logit_softness,
        block_grouping,
        neighborhood_span,
    )


def solution(mesh):
    in_specs = (
        P("dp", "seq", None),
        P("dp", "seq", None),
        P("dp", "seq", None),
        P("dp", "seq", None),
        P(),
        P("dp", None, None, None),
        P(),
    )
    out_specs = (P("dp", "seq", None), P("dp", "seq", None), P("dp", "seq", None), P())
    return jax.shard_map(shards, mesh=mesh, in_specs=in_specs, out_specs=out_specs, check_vma=False)
```

```python
import functools
import math

import jax
import jax.numpy as jnp
from jax import lax
from jax.experimental import pallas as pl
from jax.experimental.pallas import tpu as pltpu
from jax.sharding import PartitionSpec as P

HD = 128
BLK = 128


blocked_score = -1e30


def shifted(value, axis, steps):
    count = lax.axis_size(axis)
    first, last = (max(0, -steps), min(count, count - steps))
    return lax.ppermute(value, axis, [(source, source + steps) for source in range(first, last)])


def lifted(array_in):
    return lax.optimization_barrier(array_in.astype(jnp.bfloat16)).astype(jnp.float32)


def head_major(tokens_in, block_len):
    token_count, feature_count = tokens_in.shape
    return tokens_in.reshape(
        token_count // block_len, block_len, feature_count // HD, HD
    ).transpose(2, 0, 1, 3)


def token_major(blocks_in):
    head_count, block_count, block_len, depth = blocks_in.shape
    return blocks_in.transpose(1, 2, 0, 3).reshape(1, block_count * block_len, head_count * depth)


def window_parts(query_block, prev_keys, prev_values, grad_block, usable, window_width, temper):
    block_len = query_block.shape[-2]
    inverse_root = 1.0 / math.sqrt(query_block.shape[-1])
    raw_scores = (
        jnp.einsum("...td,...sd->...ts", query_block, prev_keys, preferred_element_type=jnp.float32)
        * inverse_root
    )
    query_pos = lax.broadcasted_iota(jnp.int32, (block_len, block_len), 0)
    key_pos = lax.broadcasted_iota(jnp.int32, (block_len, block_len), 1)
    pair_mask = usable[..., None, None] & (
        key_pos > query_pos + block_len - window_width[..., None, None]
    )
    scores = temper[..., None, None] * raw_scores
    row_top = jnp.max(jnp.where(pair_mask, scores, blocked_score), axis=-1)
    weights = jnp.where(pair_mask, jnp.exp(scores - row_top[..., None]), 0.0)
    prob_grad = jnp.einsum(
        "...td,...sd->...ts", grad_block, prev_values, preferred_element_type=jnp.float32
    )
    return (
        raw_scores,
        pair_mask,
        prob_grad,
        row_top,
        jnp.sum(weights, axis=-1),
        jnp.sum(weights * prob_grad, axis=-1),
    )


def window_grads(
    raw_scores,
    pair_mask,
    prob_grad,
    query_block,
    prev_keys,
    grad_block,
    log_total,
    row_delta,
    temper,
):
    inverse_root = 1.0 / math.sqrt(query_block.shape[-1])
    scaling = (temper * inverse_root)[..., None, None]
    probability = jnp.where(
        pair_mask, jnp.exp(temper[..., None, None] * raw_scores - log_total[..., None]), 0.0
    )
    score_grad = probability * (prob_grad - row_delta[..., None])
    prob_low = probability.astype(jnp.bfloat16)
    grad_low = score_grad.astype(jnp.bfloat16)
    query_part = (
        jnp.einsum("...ts,...sd->...td", grad_low, prev_keys, preferred_element_type=jnp.float32)
        * scaling
    )
    key_part = (
        jnp.einsum("...ts,...td->...sd", grad_low, query_block, preferred_element_type=jnp.float32)
        * scaling
    )
    value_part = jnp.einsum(
        "...ts,...td->...sd", prob_low, grad_block, preferred_element_type=jnp.float32
    )
    temper_part = jnp.sum(score_grad * raw_scores, axis=(-2, -1))
    return (query_part, key_part, value_part, temper_part)


def cluster_pair(
    query_items,
    key_items,
    value_items,
    grad_items,
    live_items,
    temper,
    window_top,
    window_total,
    window_mass,
):
    item_count, block_len, depth = query_items.shape
    row_count = item_count * block_len
    group_rows = 4 * block_len
    inverse_root = 1.0 / math.sqrt(depth)
    scaling = temper * inverse_root
    query_rows = query_items.reshape(row_count, depth)
    key_rows = key_items.reshape(row_count, depth)
    value_rows = value_items.reshape(row_count, depth)
    grad_rows = grad_items.reshape(row_count, depth)
    key_item = jnp.arange(row_count) // block_len
    key_token = jnp.arange(row_count) % block_len
    live_rows = jnp.repeat(live_items, block_len)
    top_rows = window_top.reshape(row_count)
    total_rows = window_total.reshape(row_count)
    mass_rows = window_mass.reshape(row_count)

    def group_step(carry, start_row):
        key_acc, value_acc, temper_acc = carry
        query_group = lax.dynamic_slice_in_dim(query_rows, start_row, group_rows, 0)
        grad_group = lax.dynamic_slice_in_dim(grad_rows, start_row, group_rows, 0)
        group_live = lax.dynamic_slice_in_dim(live_rows, start_row, group_rows, 0)
        group_top = lax.dynamic_slice_in_dim(top_rows, start_row, group_rows, 0)
        group_total = lax.dynamic_slice_in_dim(total_rows, start_row, group_rows, 0)
        group_mass = lax.dynamic_slice_in_dim(mass_rows, start_row, group_rows, 0)
        query_item = (start_row + jnp.arange(group_rows)) // block_len
        query_token = jnp.arange(group_rows) % block_len
        earlier = (key_item[None, :] < query_item[:, None]) | (
            key_item[None, :] == query_item[:, None]
        ) & (key_token[None, :] <= query_token[:, None])
        pair_mask = group_live[:, None] & live_rows[None, :] & earlier
        raw_scores = (
            lax.dot_general(
                query_group, key_rows, (((1,), (1,)), ((), ())), preferred_element_type=jnp.float32
            )
            * inverse_root
        )
        scores = temper * raw_scores
        row_top = jnp.maximum(
            jnp.max(jnp.where(pair_mask, scores, blocked_score), axis=1), group_top
        )
        weights = jnp.where(pair_mask, jnp.exp(scores - row_top[:, None]), 0.0)
        row_total = jnp.sum(weights, axis=1) + group_total * jnp.exp(group_top - row_top)
        log_total = row_top + jnp.log(jnp.where(group_live, row_total, 1.0))
        probability = jnp.where(pair_mask, jnp.exp(scores - log_total[:, None]), 0.0)
        prob_grad = lax.dot_general(
            grad_group, value_rows, (((1,), (1,)), ((), ())), preferred_element_type=jnp.float32
        )
        row_delta = jnp.sum(probability * prob_grad, axis=1) + group_mass * jnp.exp(
            group_top - log_total
        )
        score_grad = probability * (prob_grad - row_delta[:, None])
        prob_low = probability.astype(jnp.bfloat16)
        grad_low = score_grad.astype(jnp.bfloat16)
        query_part = jnp.dot(grad_low, key_rows, preferred_element_type=jnp.float32) * scaling
        key_acc = (
            key_acc
            + lax.dot_general(
                grad_low, query_group, (((0,), (0,)), ((), ())), preferred_element_type=jnp.float32
            )
            * scaling
        )
        value_acc = value_acc + lax.dot_general(
            prob_low, grad_group, (((0,), (0,)), ((), ())), preferred_element_type=jnp.float32
        )
        temper_acc = temper_acc + jnp.sum(score_grad * raw_scores)
        return ((key_acc, value_acc, temper_acc), (query_part, log_total, row_delta))

    start_rows = jnp.arange(item_count // 4) * group_rows
    initial = (
        jnp.zeros((row_count, depth), jnp.float32),
        jnp.zeros((row_count, depth), jnp.float32),
        jnp.zeros((), jnp.float32),
    )
    (key_acc, value_acc, temper_acc), (query_part, log_total, row_delta) = lax.scan(
        group_step, initial, start_rows
    )
    return (
        query_part.reshape(item_count, block_len, depth),
        log_total.reshape(item_count, block_len),
        row_delta.reshape(item_count, block_len),
        key_acc.reshape(item_count, block_len, depth),
        value_acc.reshape(item_count, block_len, depth),
        temper_acc,
    )


def clustered_shards(
    probe_vectors,
    lookup_vectors,
    content_vectors,
    result_cotangent,
    logit_softness,
    block_grouping,
    neighborhood_span,
):
    seq_count = lax.axis_size("seq")
    position = lax.axis_index("seq")
    tokens = probe_vectors.shape[1]
    head_count = probe_vectors.shape[2] // HD
    local_blocks = tokens // BLK
    block_count = local_blocks * seq_count
    cluster_count = max(1, block_count // 8)
    capacity = min(12, block_count)
    owned_pairs = cluster_count * head_count // seq_count
    group_count = cluster_count // owned_pairs
    per_peer = max(1, local_blocks // group_count)
    cluster_ids = block_grouping[0, :, :, 0]
    query_home = head_major(probe_vectors[0], BLK)
    key_home = head_major(lookup_vectors[0], BLK)
    value_home = head_major(content_vectors[0], BLK)
    grad_home = head_major(result_cotangent[0], BLK)
    last_block = (lookup_vectors[0, tokens - BLK :], content_vectors[0, tokens - BLK :])
    prev_key_rows, prev_value_rows = shifted((last_block[0], last_block[1]), "seq", 1)
    prev_keys = jnp.concatenate([head_major(prev_key_rows, BLK), key_home[:, :-1]], axis=1)
    prev_values = jnp.concatenate([head_major(prev_value_rows, BLK), value_home[:, :-1]], axis=1)
    first_block = position * local_blocks
    before = jnp.concatenate(
        [jnp.full((head_count, 1), -1, jnp.int32), cluster_ids[:, :-1]], axis=1
    )
    my_ids = lax.dynamic_slice_in_dim(cluster_ids, first_block, local_blocks, 1)
    my_before = lax.dynamic_slice_in_dim(before, first_block, local_blocks, 1)
    global_block = first_block + jnp.arange(local_blocks)
    usable_home = (global_block[None, :] >= 1) & (my_before != my_ids)
    peer_index = jnp.arange(seq_count)
    peer_head = peer_index * owned_pairs // cluster_count
    slot_range = jnp.arange(per_peer)
    local_range = jnp.arange(local_blocks)
    owner_index = (jnp.arange(head_count)[:, None] * cluster_count + my_ids) // owned_pairs
    peer_ids = jnp.take(my_ids, peer_head, axis=0)
    goes = (peer_head[:, None] * cluster_count + peer_ids) // owned_pairs == peer_index[:, None]
    send_rank = jnp.cumsum(goes.astype(jnp.int32), axis=1) - 1
    send_pick = goes[:, None, :] & (send_rank[:, None, :] == slot_range[None, :, None])
    send_block = jnp.sum(jnp.where(send_pick, local_range[None, None, :], 0), axis=2)
    send_flat = peer_head[:, None] * local_blocks + send_block
    home_rank = jnp.take_along_axis(send_rank, owner_index, axis=0)
    home_pos = owner_index * per_peer + home_rank
    pair_index = position * owned_pairs + jnp.arange(owned_pairs)
    split_for_couple = pair_index // cluster_count
    pair_cluster = pair_index % cluster_count
    my_head = position * owned_pairs // cluster_count
    split_numbers = jnp.take(cluster_ids, my_head, axis=0)
    member = split_numbers[None, :] == pair_cluster[:, None]
    member_rank = jnp.cumsum(member.astype(jnp.int32), axis=1) - 1
    member_count = jnp.sum(member.astype(jnp.int32), axis=1)
    picked = member[:, None, :] & (member_rank[:, None, :] == jnp.arange(capacity)[None, :, None])
    member_block = jnp.sum(jnp.where(picked, jnp.arange(block_count)[None, None, :], 0), axis=2)
    live_members = jnp.arange(capacity)[None, :] < member_count[:, None]
    mine = (my_head * cluster_count + split_numbers) // owned_pairs == position
    mine_grid = mine.reshape(seq_count, local_blocks)
    recv_rank = jnp.cumsum(mine_grid.astype(jnp.int32), axis=1) - 1
    recv_pos = (peer_index[:, None] * per_peer + recv_rank).reshape(block_count)
    member_pos = jnp.take(recv_pos, member_block)
    couple_softness = jnp.take(logit_softness, split_for_couple)
    pair_onehot = (split_for_couple[:, None] == jnp.arange(head_count)[None, :]).astype(jnp.float32)
    slot_pair = my_head * cluster_count + split_numbers - position * owned_pairs
    same_cluster = split_numbers[:, None] == split_numbers[None, :]
    earlier_block = jnp.arange(block_count)[None, :] < jnp.arange(block_count)[:, None]
    slot_rank = jnp.sum((same_cluster & earlier_block).astype(jnp.int32), axis=1)
    back_pos = jnp.clip(slot_pair, 0, owned_pairs - 1) * capacity + jnp.clip(
        slot_rank, 0, capacity - 1
    )
    back_grid = back_pos.reshape(seq_count, local_blocks)
    back_pick = mine_grid[:, None, :] & (recv_rank[:, None, :] == slot_range[None, :, None])
    back_flat = jnp.sum(jnp.where(back_pick, back_grid[:, None, :], 0), axis=2)

    def to_peers(array_in):
        flat = array_in.reshape((head_count * local_blocks,) + array_in.shape[2:])
        return jnp.take(flat, send_flat, axis=0)

    def members(array_in):
        flat = array_in.reshape((seq_count * per_peer,) + array_in.shape[2:])
        return jnp.take(flat, member_pos, axis=0)

    def to_owner(array_in):
        flat = array_in.reshape((owned_pairs * capacity,) + array_in.shape[2:])
        return jnp.take(flat, back_flat, axis=0)

    def from_peers(array_in):
        flat = array_in.reshape((seq_count * per_peer,) + array_in.shape[2:])
        return jnp.take(flat, home_pos, axis=0)

    raw_w, mask_w, pgrad_w, top_w, total_w, mass_w = window_parts(
        query_home,
        prev_keys,
        prev_values,
        grad_home,
        usable_home,
        neighborhood_span[:, None],
        logit_softness[:, None],
    )
    arrived = (
        lax.all_to_all(to_peers(query_home), "seq", split_axis=0, concat_axis=0, tiled=True),
        lax.all_to_all(to_peers(key_home), "seq", split_axis=0, concat_axis=0, tiled=True),
        lax.all_to_all(to_peers(value_home), "seq", split_axis=0, concat_axis=0, tiled=True),
        lax.all_to_all(to_peers(grad_home), "seq", split_axis=0, concat_axis=0, tiled=True),
    )
    arrived_stats = (
        lax.all_to_all(to_peers(top_w), "seq", split_axis=0, concat_axis=0, tiled=True),
        lax.all_to_all(to_peers(total_w), "seq", split_axis=0, concat_axis=0, tiled=True),
        lax.all_to_all(to_peers(mass_w), "seq", split_axis=0, concat_axis=0, tiled=True),
    )
    query_m, key_m, value_m, grad_m = [members(item_in) for item_in in arrived]
    top_m, total_m, mass_m = [members(item_in) for item_in in arrived_stats]

    def split_pair(pair_inputs):
        query_i, key_i, value_i, grad_i, live_i, temper_i, top_i, total_i, mass_i = pair_inputs
        query_c, log_total, row_delta, key_c, value_c, temper_c = cluster_pair(
            query_i, key_i, value_i, grad_i, live_i, temper_i, top_i, total_i, mass_i
        )
        return (
            query_c.astype(jnp.bfloat16),
            key_c.astype(jnp.bfloat16),
            value_c.astype(jnp.bfloat16),
            log_total,
            row_delta,
            temper_c,
        )

    owner_results = lax.map(
        split_pair,
        (query_m, key_m, value_m, grad_m, live_members, couple_softness, top_m, total_m, mass_m),
    )
    returned = (
        lax.all_to_all(to_owner(owner_results[0]), "seq", split_axis=0, concat_axis=0, tiled=True),
        lax.all_to_all(to_owner(owner_results[1]), "seq", split_axis=0, concat_axis=0, tiled=True),
        lax.all_to_all(to_owner(owner_results[2]), "seq", split_axis=0, concat_axis=0, tiled=True),
    )
    returned_stats = (
        lax.all_to_all(to_owner(owner_results[3]), "seq", split_axis=0, concat_axis=0, tiled=True),
        lax.all_to_all(to_owner(owner_results[4]), "seq", split_axis=0, concat_axis=0, tiled=True),
    )
    query_cluster = from_peers(returned[0])
    key_cluster = from_peers(returned[1])
    value_cluster = from_peers(returned[2])
    log_home = from_peers(returned_stats[0])
    delta_home = from_peers(returned_stats[1])
    query_w, key_w, value_w, temper_w = window_grads(
        raw_w,
        mask_w,
        pgrad_w,
        query_home,
        prev_keys,
        grad_home,
        log_home,
        delta_home,
        logit_softness[:, None],
    )
    query_out = (query_cluster.astype(jnp.float32) + lifted(query_w)).astype(jnp.bfloat16)
    key_window = key_w.astype(jnp.bfloat16)
    value_window = value_w.astype(jnp.bfloat16)
    temper_local = jnp.sum(owner_results[5][:, None] * pair_onehot, axis=0) + jnp.sum(
        temper_w, axis=1
    )
    edge_keys, edge_values = shifted((key_window[:, 0], value_window[:, 0]), "seq", -1)
    key_next = jnp.concatenate([key_window[:, 1:], edge_keys[:, None]], axis=1)
    value_next = jnp.concatenate([value_window[:, 1:], edge_values[:, None]], axis=1)
    key_out = (key_cluster.astype(jnp.float32) + key_next.astype(jnp.float32)).astype(jnp.bfloat16)
    value_out = (value_cluster.astype(jnp.float32) + value_next.astype(jnp.float32)).astype(
        jnp.bfloat16
    )
    temper_total = lax.psum(temper_local, ("seq", "dp"))
    temper_grad = temper_total / (lax.axis_size("dp") * tokens * seq_count)
    return (token_major(query_out), token_major(key_out), token_major(value_out), temper_grad)


TILE = 256
EXTRA = 16
MIB = 1024 * 1024
PIECES = 4
QUERY, KEY, VALUE, GRAD = range(4)


def columns_of(index):
    return pl.ds(pl.multiple_of(index * HD, HD), HD)


def rows_of(index):
    return pl.ds(pl.multiple_of(index * BLK, BLK), BLK)


def tile_rows(tile):
    return slice(tile * TILE, (tile + 1) * TILE)


def position(half_count):
    me = lax.axis_index("seq")
    half = jnp.where(me >= half_count, 1, 0)
    return me, half, me - half * half_count


def kernel_call(
    kernel, name, operands, in_specs, out_shape, scratch, vmem_mib, flops=0, out_spaces=None,
    aliases=None,
):
    bytes_accessed = sum(
        math.prod(item.shape) * item.dtype.itemsize for item in (*operands, *out_shape)
    )
    return pl.pallas_call(
        kernel,
        out_shape=out_shape,
        in_specs=in_specs,
        out_specs=[
            pl.BlockSpec(memory_space=space)
            for space in out_spaces or [pltpu.VMEM] * len(out_shape)
        ],
        scratch_shapes=scratch,
        input_output_aliases=aliases or {},
        cost_estimate=pl.CostEstimate(
            flops=flops, bytes_accessed=bytes_accessed, transcendentals=0
        ),
        compiler_params=pltpu.CompilerParams(vmem_limit_bytes=vmem_mib * MIB),
        name=name,
    )(*operands)


def pack_kernel(*refs, half_count):
    arrays, within_ref, foreign_refs = refs[:4], refs[4], refs[5:7]
    held, within, across, arrival, left_within, left_across = refs[7:]
    me, half, _ = position(half_count)
    piece = BLK // PIECES
    arrivals = [
        [
            pltpu.make_async_copy(
                array_ref.at[0, part * piece : (part + 1) * piece, :],
                held.at[place, part * piece : (part + 1) * piece, :],
                arrival.at[place, part],
            )
            for part in range(PIECES)
        ]
        for place, array_ref in enumerate(arrays)
    ]
    for copies in arrivals:
        for copy in copies:
            copy.start()
    leaving = []
    for place, copies in enumerate(arrivals):
        for copy in copies:
            copy.wait()
        for slot, base in enumerate((half * half_count, (1 - half) * half_count)):
            rows = slice((slot * 4 + place) * BLK, (slot * 4 + place + 1) * BLK)
            for peer in range(half_count):
                within[peer, rows, :] = held[place, :, columns_of(base + peer)]
            leaving.append(
                pltpu.make_async_copy(
                    within.at[:, rows, :], within_ref.at[:, rows, :], left_within.at[place, slot]
                )
            )
            leaving[-1].start()
    first = jnp.where(half == 0, KEY, QUERY)
    second = jnp.where(half == 0, VALUE, GRAD)
    for core, foreign_ref in enumerate(foreign_refs):
        for step in range(half_count // 2):
            columns = columns_of(me ^ core ^ (half_count + 2 * step))
            across[core, step, :BLK, :] = held[first, :, columns]
            across[core, step, BLK:, :] = held[second, :, columns]
        leaving.append(pltpu.make_async_copy(across.at[core], foreign_ref, left_across.at[core]))
        leaving[-1].start()
    for copy in leaving:
        copy.wait()


def packed(arrays, half_count):
    width = arrays[0].shape[2]
    within_shape, across_shape = (half_count, 8 * BLK, HD), (half_count // 2, 2 * BLK, HD)
    return kernel_call(
        functools.partial(pack_kernel, half_count=half_count),
        "pack_heads",
        arrays,
        [pl.BlockSpec(memory_space=pl.ANY)] * 4,
        [jax.ShapeDtypeStruct(within_shape, jnp.bfloat16)]
        + [jax.ShapeDtypeStruct(across_shape, jnp.bfloat16)] * 2,
        [
            pltpu.VMEM((4, BLK, width), jnp.bfloat16),
            pltpu.VMEM(within_shape, jnp.bfloat16),
            pltpu.VMEM((2, *across_shape), jnp.bfloat16),
            pltpu.SemaphoreType.DMA((4, PIECES)),
            pltpu.SemaphoreType.DMA((4, 2)),
            pltpu.SemaphoreType.DMA((2,)),
        ],
        60,
        out_spaces=[pl.ANY] * 3,
    )


def dot_rows(left, right):
    return lax.dot_general(
        left, right, (((1,), (1,)), ((), ())), preferred_element_type=jnp.float32
    )


def dot_plain(left, right):
    return lax.dot_general(
        left, right, (((1,), (0,)), ((), ())), preferred_element_type=jnp.float32
    )


def from_blocks(ref, place):
    def rows(start, stop):
        per_tile = TILE // BLK
        return jnp.concatenate(
            [ref[block, place] for block in range(start * per_tile, stop * per_tile)],
            axis=0,
        )

    return rows


def from_array(ref, place):
    return lambda start, stop: ref[place, start * TILE : stop * TILE, :]


class Region:
    def __init__(self, square, sources, tiles, scaling, bias_ref=None, least_ref=None, first=0):
        self.square, self.sources, self.tiles, self.scaling = square, sources, tiles, scaling
        self.bias_ref, self.least_ref, self.first = bias_ref, least_ref, first

    def rows(self, which, start, stop):
        return self.sources[which](start, stop)

    def scale_of(self, array):
        return 1.0 if array == VALUE else self.scaling[:, :HD]

    def keys_of(self, tile):
        return range(self.tiles if self.square else tile + 1)

    def scores(self, tile_key, tile_query):
        per_tile = TILE // BLK
        scores = dot_rows(
            self.rows(KEY, tile_key, tile_key + 1), self.rows(QUERY, tile_query, tile_query + 1)
        ) * (self.scaling * math.log2(math.e))
        before = self.tiles * per_tile if self.square else 0
        rows = []
        for sub_key in range(per_tile):
            key_block = tile_key * per_tile + sub_key
            pieces = []
            for sub_query in range(per_tile):
                query_block = tile_query * per_tile + sub_query
                lanes = slice(sub_query * BLK, (sub_query + 1) * BLK)
                piece = scores[sub_key * BLK : (sub_key + 1) * BLK, lanes]
                apart = before + query_block - key_block
                if apart < 0:
                    piece = jnp.full_like(piece, blocked_score)
                elif apart == 0:
                    piece = jnp.where(key_minus_query() <= 0, piece, blocked_score)
                elif apart == 1:
                    row = self.first + (0 if self.square else key_block)
                    least = self.least_ref[row : row + 1, :]
                    piece = jnp.where(key_minus_query() > least, piece, blocked_score)
                else:
                    at = slice(query_block * BLK, (query_block + 1) * BLK)
                    piece = piece + self.bias_ref[key_block : key_block + 1, at]
                pieces.append(piece)
            rows.append(jnp.concatenate(pieces, axis=1))
        return jnp.concatenate(rows, axis=0)


def diagonal(slot, arrived_ref, scales_ref, bias_ref=None, least_ref=None):
    blocks = arrived_ref.shape[0]
    sources = [from_blocks(arrived_ref, slot * 4 + place) for place in range(4)]
    bias = None if bias_ref is None else bias_ref.at[slot]
    first = slot * (blocks - 1)
    scaling = scales_ref[slot : slot + 1, :]
    return Region(False, sources, blocks * BLK // TILE, scaling, bias, least_ref, first)


def square(square_ref, scales_ref, bias_ref=None, least_ref=None):
    tiles = square_ref.shape[1] // TILE
    sources = [from_array(square_ref, place) for place in range(4)]
    bias = None if bias_ref is None else bias_ref.at[2]
    first = 2 * (tiles * TILE // BLK - 1)
    return Region(True, sources, tiles, scales_ref[0:1, :], bias, least_ref, first)


def key_minus_query():
    shape = (BLK, BLK)
    return lax.broadcasted_iota(jnp.int32, shape, 0) - lax.broadcasted_iota(jnp.int32, shape, 1)


def statistics(region, weight_ref, towards_ref, out_ref, first_row):
    for tile in range(region.tiles):
        here = tile_rows(tile)
        top = jnp.full((1, TILE), blocked_score, jnp.float32)
        for other in region.keys_of(tile):
            raw = region.scores(other, tile)
            weight_ref[tile_rows(other), here] = raw
            top = jnp.maximum(top, jnp.max(raw, axis=0, keepdims=True))
        sums = [jnp.zeros((1, TILE), jnp.float32)] * 4
        for other in region.keys_of(tile):
            there = tile_rows(other)
            raw = weight_ref[there, here]
            weight = jnp.exp2(raw - top)
            towards = dot_rows(
                region.rows(VALUE, other, other + 1), region.rows(GRAD, tile, tile + 1)
            )
            weight_ref[there, here] = weight
            towards_ref[there, here] = towards
            pulled, weighted = weight * towards, weight * raw
            terms = (weight, pulled, pulled * raw, weighted)
            sums = [
                total + jnp.sum(term, axis=0, keepdims=True) for total, term in zip(sums, terms)
            ]
        for row, value in enumerate((top, *sums)):
            out_ref[first_row + row : first_row + row + 1, here] = value


def gradients(
    region, weight_ref, towards_ref, top, log_total, delta, prob_low, grad_low, keys_flat, emit=None
):
    keys_flat[...] = region.rows(KEY, 0, region.tiles).T
    share = jnp.exp2(top - log_total)
    query_parts, key_parts, value_parts = [], [], []
    for tile in range(region.tiles):
        here = tile_rows(tile)
        for other in region.keys_of(tile):
            there = tile_rows(other)
            probability = weight_ref[there, here] * share[:, here]
            prob_low[there, here] = probability.astype(jnp.bfloat16)
            grad_low[there, here] = (
                probability * (towards_ref[there, here] - delta[:, here])
            ).astype(jnp.bfloat16)
        upto = slice(0, len(region.keys_of(tile)) * TILE)
        query_parts.append(dot_plain(keys_flat[:, upto], grad_low[upto, here]).T)
    if emit is not None:
        emit(QUERY, query_parts)
    for low, which, parts in ((grad_low, QUERY, key_parts), (prob_low, GRAD, value_parts)):
        for tile in range(region.tiles):
            first = 0 if region.square else tile
            onward = slice(first * TILE, region.tiles * TILE)
            parts.append(
                dot_plain(low[tile_rows(tile), onward], region.rows(which, first, region.tiles))
            )
        if emit is not None:
            emit(KEY if which == QUERY else VALUE, parts)
    return query_parts, key_parts, value_parts


def merged(first, second):
    top = jnp.maximum(first[0], second[0])
    left, right = jnp.exp2(first[0] - top), jnp.exp2(second[0] - top)
    total = first[1] * left + second[1] * right
    mass = first[2] * left + second[2] * right
    return top + jnp.log2(total), mass / total


def alone(rows):
    return rows[0] + jnp.log2(rows[1]), rows[2] / rows[1]


def rows_at(ref, first, count=5):
    return [ref[first + row : first + row + 1, :] for row in range(count)]


def temper_terms(rows, totals, scale_row):
    log_total, delta = totals
    terms = (rows[3] - delta * rows[4]) * jnp.exp2(rows[0] - log_total)
    folded = sum(terms[:, start : start + HD] for start in range(0, terms.shape[1], HD))
    return folded / (scale_row[:, :HD] * (math.sqrt(HD) * math.log2(math.e)))


def put(within_ref, array, tile, value):
    per_tile = TILE // BLK
    for sub in range(per_tile):
        within_ref[tile * per_tile + sub, array * BLK : (array + 1) * BLK, :] = value[
            sub * BLK : (sub + 1) * BLK, :
        ].astype(jnp.bfloat16)


def scaled(region, parts):
    scale = region.scaling[:, :HD]
    return [[value * scale for value in part] for part in parts[:2]] + [parts[2]]


def masks_kernel(softness_ref, ids_ref, span_ref, scales_ref, bias_ref, least_ref, *, half_count):
    me, half, _ = position(half_count)
    base = half * half_count
    regions = (
        (me, base, base),
        (me ^ half_count, base, base),
        (me, 0, half_count),
    )
    for slot, (head, key_base, query_base) in enumerate(regions):
        if slot < 2:
            scales_ref[slot : slot + 1, :] = jnp.full(
                (1, TILE), softness_ref[head] * (1.0 / math.sqrt(HD)), jnp.float32
            )

        def same(key_block, query_block):
            return ids_ref[head, key_base + key_block] == ids_ref[head, query_base + query_block]

        def bias(key_block, query_block):
            return jnp.full(
                (1, BLK), jnp.where(same(key_block, query_block), 0.0, blocked_score), jnp.float32
            )

        for key_block in range(half_count):
            bias_ref[slot, key_block : key_block + 1, :] = jnp.concatenate(
                [bias(key_block, query_block) for query_block in range(half_count)], axis=1
            )
        pairs = [(block, block + 1) for block in range(half_count - 1)]
        if slot == 2:
            pairs = [(half_count - 1, 0)]
        for place, pair in enumerate(pairs):
            least = jnp.where(same(*pair), -BLK, BLK - span_ref[head])
            row = slot * (half_count - 1) + place
            least_ref[row : row + 1, :] = jnp.full((1, BLK), least, jnp.int32)


def within_kernel(
    arrived_ref, scales_ref, bias_ref, least_ref, stats_ref, parts_ref, own_weight, own_towards, other_weight, other_towards, *scratch, half_count
):
    _, half, _ = position(half_count)
    kept = ((own_weight, own_towards), (other_weight, other_towards))
    for slot in range(2):
        region = diagonal(slot, arrived_ref, scales_ref, bias_ref, least_ref)
        statistics(region, *kept[slot], stats_ref, slot * 5)

    @pl.when(half == 0)
    def _():
        region = diagonal(0, arrived_ref, scales_ref)
        single = alone(rows_at(stats_ref, 0))
        parts = gradients(region, *kept[0], stats_ref[0:1, :], *single, *scratch)
        for place, tiles in enumerate(scaled(region, parts)):
            for tile, value in enumerate(tiles):
                parts_ref[place, tile_rows(tile), :] = value


def square_kernel(arrived_ref, scales_ref, bias_ref, least_ref, stats_ref, *refs, half_count):
    across_refs = refs[: half_count // 2]
    square_ref, message_ref, square_stats, weight, towards = refs[half_count // 2 :]
    _, half, place = position(half_count)
    first = jnp.where(half == 0, QUERY, KEY)
    second = jnp.where(half == 0, GRAD, VALUE)
    for step, across_ref in enumerate(across_refs):
        for core in range(2):
            rows = rows_of(place ^ core ^ (2 * step))
            square_ref[first, rows, :] = across_ref[core, :BLK, :]
            square_ref[second, rows, :] = across_ref[core, BLK:, :]
    for kept in (jnp.where(half == 0, KEY, QUERY), jnp.where(half == 0, VALUE, GRAD)):
        for block in range(half_count):
            square_ref[kept, block * BLK : (block + 1) * BLK, :] = arrived_ref[block, kept]
    region = square(square_ref, scales_ref, bias_ref, least_ref)
    statistics(region, weight, towards, square_stats, 0)
    own, other, crossing = rows_at(stats_ref, 0), rows_at(stats_ref, 5), rows_at(square_stats, 0)
    for row in range(5):
        message_ref[row : row + 1, :] = jnp.where(half == 0, crossing[row], other[row])
    own_scale, other_scale = scales_ref[0:1, :], scales_ref[1:2, :]
    both = merged(own, crossing)
    whole = temper_terms(own, both, own_scale) + temper_terms(crossing, both, own_scale)
    single = temper_terms(own, alone(own), own_scale)
    message_ref[5:6, :HD] = jnp.where(half == 0, single, whole)
    message_ref[6:7, :HD] = temper_terms(other, alone(other), other_scale)


def first_kernel(
    arrived_ref, scales_ref, square_ref, stats_ref, square_stats,
    own_weight, own_towards, other_weight, other_towards, square_weight, square_towards,
    across_ref, within_ref, ready, ready_sem, *scratch, half_count
):
    _, half, _ = position(half_count)
    leaving = sends(ready, within_ref, ready_sem, (1 - half) * 3)

    @pl.when(half == 0)
    def _():
        region = diagonal(1, arrived_ref, scales_ref)

        def send(array, parts):
            for tile, part in enumerate(parts):
                put(ready, array, tile, part * region.scale_of(array))
            leaving[array].start()

        totals = alone(rows_at(stats_ref, 5))
        gradients(
            region, other_weight, other_towards, stats_ref[5:6, :], *totals, *scratch, emit=send
        )

    @pl.when(half == 1)
    def _():
        totals = merged(rows_at(stats_ref, 0), rows_at(square_stats, 0))
        region = square(square_ref, scales_ref)
        parts = gradients(
            region, square_weight, square_towards, square_stats[0:1, :], *totals, *scratch
        )
        across_query, *foreign = scaled(region, parts)
        for array, tiles in enumerate(foreign):
            for tile, value in enumerate(tiles):
                across_ref[array, tile_rows(tile), :] = value.astype(jnp.bfloat16)
        region = diagonal(0, arrived_ref, scales_ref)

        def send(array, parts):
            for tile, part in enumerate(parts):
                value = part * region.scale_of(array)
                put(ready, array, tile, value + across_query[tile] if array == QUERY else value)
            leaving[array].start()

        gradients(
            region, own_weight, own_towards, stats_ref[0:1, :], *totals, *scratch, emit=send
        )

    for copy in leaving:
        copy.wait()


def sends(ready, within_ref, sems, first):
    copies = []
    for array in range(3):
        rows = slice(array * BLK, (array + 1) * BLK)
        copies.append(
            pltpu.make_async_copy(
                ready.at[:, rows, :], within_ref.at[:, rows_of(first + array), :], sems.at[array]
            )
        )
    return copies


def temper_rows(own, other):
    row = lax.broadcasted_iota(jnp.int32, (EXTRA, HD), 0)
    rows = jnp.zeros((EXTRA, HD), jnp.float32)
    for place, terms in enumerate((own, other)):
        rest = jnp.broadcast_to(jnp.sum(terms, axis=1, keepdims=True), (EXTRA, HD))
        for piece in range(3):
            high = rest.astype(jnp.bfloat16).astype(jnp.float32)
            rows = jnp.where(row == place * 3 + piece, high, rows)
            rest = rest - high
    return rows.astype(jnp.bfloat16)


def finish_kernel(
    arrived_ref, scales_ref, square_ref, message_ref, received_ref, stats_ref, square_stats,
    parts_ref, square_weight, square_towards, other_weight, other_towards, across_ref, begun_ref,
    within_ref, *refs, half_count
):
    del begun_ref
    chunk_refs = refs[:2]
    across, ready, tail, ready_sem, tail_sem, *scratch = refs[2:]
    _, half, place = position(half_count)
    leaving = sends(ready, within_ref, ready_sem, half * 3)
    sent, came = rows_at(message_ref, 0), rows_at(received_ref, 0)
    totals = merged(sent, came)
    scale = jnp.where(half == 0, scales_ref[0:1, :], scales_ref[1:2, :])
    shared = temper_terms(sent, totals, scale) + temper_terms(came, totals, scale)
    mine, theirs = message_ref[5:6, :HD], received_ref[5:6, :HD]
    own = mine + jnp.where(half == 0, shared, received_ref[6:7, :HD])
    other = theirs + jnp.where(half == 0, message_ref[6:7, :HD], shared)
    pieces = temper_rows(own, other)
    for block in range(half_count):
        tail[block] = pieces
    leaving.append(
        pltpu.make_async_copy(tail, within_ref.at[:, 6 * BLK : 6 * BLK + EXTRA, :], tail_sem)
    )
    leaving[-1].start()

    def chunks():
        for core, chunk_ref in enumerate(chunk_refs):
            for step in range(half_count // 2):
                yield step, chunk_ref, rows_of(place ^ core ^ (2 * step))

    @pl.when(half == 0)
    def _():
        region = square(square_ref, scales_ref)

        def send(array, parts):
            for tile, part in enumerate(parts):
                here = tile_rows(tile)
                value = part * region.scale_of(array)
                if array == QUERY:
                    across[here, :] = value.astype(jnp.bfloat16)
                    put(ready, array, tile, parts_ref[array, here, :])
                else:
                    put(ready, array, tile, parts_ref[array, here, :] + value)
            leaving[array].start()

        gradients(
            region, square_weight, square_towards, square_stats[0:1, :], *totals, *scratch, emit=send
        )
        for step, chunk_ref, rows in chunks():
            chunk_ref[step, :BLK, :] = across[rows, :]
            chunk_ref[step, BLK:, :] = jnp.zeros((BLK, HD), jnp.bfloat16)

    @pl.when(half == 1)
    def _():
        region = diagonal(1, arrived_ref, scales_ref)

        def send(array, parts):
            for tile, part in enumerate(parts):
                put(ready, array, tile, part * region.scale_of(array))
            leaving[array].start()

        gradients(
            region, other_weight, other_towards, stats_ref[5:6, :], *totals, *scratch, emit=send
        )
        for step, chunk_ref, rows in chunks():
            chunk_ref[step, :BLK, :] = across_ref[0, rows, :]
            chunk_ref[step, BLK:, :] = across_ref[1, rows, :]

    for copy in leaving:
        copy.wait()


def temper_kernel(within_ref, temper_ref, *, half_count):
    _, half, _ = position(half_count)
    for peer in range(half_count):
        for slot, base in enumerate((half * half_count, (1 - half) * half_count)):
            rows = within_ref[peer, 3 * slot : 3 * slot + 3, :].astype(jnp.float32)
            temper_ref[pl.ds(base + peer, 1), :] = jnp.sum(rows, axis=0, keepdims=True)


def temper_sums(within, half_count):
    last = 6 * BLK // EXTRA
    return pl.pallas_call(
        functools.partial(temper_kernel, half_count=half_count),
        grid=(1,),
        out_shape=jax.ShapeDtypeStruct((2 * half_count, HD), jnp.float32),
        in_specs=[pl.BlockSpec((half_count, EXTRA, HD), lambda step: (0, last, 0))],
        out_specs=pl.BlockSpec((2 * half_count, HD), lambda step: (0, 0)),
        compiler_params=pltpu.CompilerParams(vmem_limit_bytes=4 * MIB),
        name="temper_sums",
    )(within)


def own_columns_kernel(within_ref, *refs, half_count):
    out_refs, (staged, sems) = refs[:3], refs[3:]
    _, half, _ = position(half_count)
    width = half_count * HD
    for array in range(6):
        for peer in range(half_count):
            staged[array, :, peer * HD : (peer + 1) * HD] = within_ref[
                peer, array * BLK : (array + 1) * BLK, :
            ]

    def copies(arrays):
        return [
            pltpu.make_async_copy(
                staged.at[array],
                out_refs[array % 3].at[0, :, side(half if array < 3 else 1 - half, width)],
                sems.at[array],
            )
            for array in arrays
        ]

    for role, arrays in enumerate(((0, 1, 2, 3), (0, 1, 2, 4, 5))):

        @pl.when(half == role)
        def _():
            leaving = copies(arrays)
            for copy in leaving:
                copy.start()
            for copy in leaving:
                copy.wait()


def side(half, width):
    return pl.ds(pl.multiple_of(half * width, width), width)


def other_columns_kernel(within_ref, *refs, half_count):
    messages = half_count // 2
    across_refs = refs[:messages]
    out_refs, (staged, sems) = refs[messages + 3 : messages + 6], refs[messages + 6 :]
    _, half, place = position(half_count)

    for role, arrays in enumerate(((1, 2), (0,))):

        @pl.when(half == role)
        def _():
            leaving = []
            for step, across_ref in enumerate(across_refs):
                pair = (place ^ (2 * step)) >> 1
                for part, array in enumerate(arrays):
                    rows = slice(part * BLK, (part + 1) * BLK)
                    for core in range(2):
                        peer = place ^ core ^ (2 * step)
                        kept = within_ref[peer, (3 + array) * BLK : (4 + array) * BLK, :]
                        total = kept.astype(jnp.float32) + across_ref[core, rows, :].astype(
                            jnp.float32
                        )
                        staged[part, :, columns_of(peer)] = total.astype(jnp.bfloat16)
                    start = (1 - role) * messages + pair
                    leaving.append(
                        pltpu.make_async_copy(
                            staged.at[part, :, side(pair, 2 * HD)],
                            out_refs[array].at[0, :, side(start, 2 * HD)],
                            sems.at[step, part],
                        )
                    )
                    leaving[-1].start()
            for copy in leaving:
                copy.wait()


def join_kernel(kept_ref, taken_ref, *out_refs):
    for step, out_ref in enumerate(out_refs):
        out_ref[0] = kept_ref[step]
        out_ref[1] = taken_ref[step]


def crossed(kept, given, half_count):
    devices = range(2 * half_count)
    steps, *shape = kept.shape
    taken = lax.ppermute(given, "seq", [(source, source ^ 1) for source in devices])
    messages = kernel_call(
        join_kernel,
        "join_chunks",
        (kept, taken),
        [pl.BlockSpec(memory_space=pltpu.VMEM)] * 2,
        [jax.ShapeDtypeStruct((2, *shape), jnp.bfloat16)] * steps,
        [],
        4,
    )
    return [
        lax.ppermute(
            message, "seq", [(source, source ^ (half_count + 2 * step)) for source in devices]
        )
        for step, message in enumerate(messages)
    ]


def head_shards(
    probe_vectors,
    lookup_vectors,
    content_vectors,
    result_cotangent,
    logit_softness,
    block_grouping,
    neighborhood_span,
):
    seq_count, dp_count = lax.axis_size("seq"), lax.axis_size("dp")
    half_count = seq_count // 2
    tokens = half_count * BLK
    groups = [list(range(half_count)), list(range(half_count, seq_count))]
    settings = (logit_softness, block_grouping[0, :, :, 0], neighborhood_span)
    smem, vmem = pl.BlockSpec(memory_space=pltpu.SMEM), pl.BlockSpec(memory_space=pltpu.VMEM)
    lows = [pltpu.VMEM((tokens, tokens), jnp.bfloat16)] * 2 + [
        pltpu.VMEM((HD, tokens), jnp.bfloat16)
    ]
    rows_of_stats = jax.ShapeDtypeStruct((8, tokens), jnp.float32)
    pairs = jax.ShapeDtypeStruct((tokens, tokens), jnp.float32)
    pair_flops = 2 * tokens * tokens * HD

    def exchange_within(array_in):
        return lax.all_to_all(
            array_in, "seq", split_axis=0, concat_axis=0, axis_index_groups=groups, tiled=True
        )

    def call(
        kernel, name, operands, out_shape, scratch, flops, vmem_mib, scalars=(), out_spaces=None,
        last_in_place=False,
    ):
        in_specs = [smem] * len(scalars) + [vmem] * len(operands)
        if last_in_place:
            in_specs[-1] = pl.BlockSpec(memory_space=pl.ANY)
        return kernel_call(
            functools.partial(kernel, half_count=half_count),
            name,
            (*scalars, *operands),
            in_specs,
            out_shape,
            scratch,
            vmem_mib,
            flops,
            out_spaces,
            {len(operands) - 1: 0} if last_in_place else {},
        )

    sent, *foreign = packed(
        (probe_vectors, lookup_vectors, content_vectors, result_cotangent), half_count
    )
    arrived = exchange_within(sent).reshape(half_count, 8, BLK, HD)
    kept_parts = jax.ShapeDtypeStruct((3, tokens, HD), jnp.float32)
    masks = call(
        masks_kernel,
        "scales_and_masks",
        (),
        [
            jax.ShapeDtypeStruct((8, TILE), jnp.float32),
            jax.ShapeDtypeStruct((3, half_count, tokens), jnp.float32),
            jax.ShapeDtypeStruct((2 * half_count, BLK), jnp.int32),
        ],
        [],
        0,
        2,
        settings,
    )
    foreign[0], *masks = lax.optimization_barrier((foreign[0], *masks))
    foreign = crossed(*foreign, half_count)
    scales = masks[0]
    stats, parts, own_weight, own_towards, other_weight, other_towards = call(
        within_kernel,
        "diagonal_statistics",
        (arrived, *masks),
        [jax.ShapeDtypeStruct((16, tokens), jnp.float32), kept_parts] + [pairs] * 4,
        lows,
        2 * pair_flops,
        14,
    )
    squared, message, square_stats, square_weight, square_towards = call(
        square_kernel,
        "square_statistics",
        (arrived, *masks, stats, *foreign),
        [jax.ShapeDtypeStruct((4, tokens, HD), jnp.bfloat16)] + [rows_of_stats] * 2 + [pairs] * 2,
        [],
        2 * pair_flops,
        8,
    )
    swap = [(source, source ^ half_count) for source in range(seq_count)]
    received = lax.ppermute(message, "seq", swap)
    result = pltpu.HBM((half_count, 6 * BLK + EXTRA, HD), jnp.bfloat16)
    ready = pltpu.VMEM((half_count, 3 * BLK, HD), jnp.bfloat16)
    across, begun = call(
        first_kernel,
        "gradients_before_totals",
        (
            arrived, scales, squared, stats, square_stats, own_weight, own_towards,
            other_weight, other_towards, square_weight, square_towards,
        ),
        [jax.ShapeDtypeStruct((2, tokens, HD), jnp.bfloat16), result],
        [ready, pltpu.SemaphoreType.DMA((3,)), *lows],
        4 * pair_flops,
        14,
        out_spaces=(pltpu.VMEM, pl.ANY),
    )
    operands = (
        arrived, scales, squared, message, received, stats, square_stats, parts,
        square_weight, square_towards, other_weight, other_towards, across, begun,
    )
    within, *foreign = call(
        finish_kernel,
        "gradients_after_totals",
        operands,
        [result]
        + [jax.ShapeDtypeStruct((half_count // 2, 2 * BLK, HD), jnp.bfloat16)] * 2,
        [
            pltpu.VMEM((tokens, HD), jnp.bfloat16), ready,
            pltpu.VMEM((half_count, EXTRA, HD), jnp.bfloat16),
            pltpu.SemaphoreType.DMA((3,)), pltpu.SemaphoreType.DMA, *lows,
        ],
        2 * pair_flops,
        16,
        out_spaces=(pl.ANY, pltpu.VMEM, pltpu.VMEM),
        last_in_place=True,
    )
    across = crossed(*foreign, half_count)
    within = exchange_within(within)
    tempers = temper_sums(within, half_count)
    temper_total = tempers
    for step in range(1, dp_count):
        swap = [(source, (source + step) % dp_count) for source in range(dp_count)]
        temper_total = temper_total + lax.ppermute(tempers, "dp", swap)
    temper = temper_total[:, 0] / (dp_count * BLK * seq_count)
    result = [pltpu.HBM(probe_vectors.shape, jnp.bfloat16)] * 3
    width = half_count * HD
    outs = kernel_call(
        functools.partial(own_columns_kernel, half_count=half_count),
        "unpack_own",
        (within,),
        [vmem],
        result,
        [pltpu.VMEM((6, BLK, width), jnp.bfloat16), pltpu.SemaphoreType.DMA((6,))],
        6,
        out_spaces=[pl.ANY] * 3,
    )
    across[0], temper = lax.optimization_barrier((across[0], temper))
    outs = kernel_call(
        functools.partial(other_columns_kernel, half_count=half_count),
        "unpack_other",
        (within, *across, *outs),
        [vmem] * (1 + len(across)) + [pl.BlockSpec(memory_space=pl.ANY)] * 3,
        result,
        [pltpu.VMEM((2, BLK, width), jnp.bfloat16), pltpu.SemaphoreType.DMA((len(across), 2))],
        6,
        out_spaces=[pl.ANY] * 3,
        aliases={1 + len(across) + array: array for array in range(3)},
    )
    return (*outs, temper)


def shards(
    probe_vectors,
    lookup_vectors,
    content_vectors,
    result_cotangent,
    logit_softness,
    block_grouping,
    neighborhood_span,
):
    head_count = probe_vectors.shape[2] // HD
    seq_count = lax.axis_size("seq")
    one_block = probe_vectors.shape[1] == BLK
    whole_tiles = seq_count * BLK % (2 * TILE) == 0 and seq_count & (seq_count - 1) == 0
    if head_count == seq_count and one_block and whole_tiles:
        plan = head_shards
    else:
        plan = clustered_shards
    return plan(
        probe_vectors,
        lookup_vectors,
        content_vectors,
        result_cotangent,
        logit_softness,
        block_grouping,
        neighborhood_span,
    )


def solution(mesh):
    in_specs = (
        P("dp", "seq", None),
        P("dp", "seq", None),
        P("dp", "seq", None),
        P("dp", "seq", None),
        P(),
        P("dp", None, None, None),
        P(),
    )
    out_specs = (P("dp", "seq", None), P("dp", "seq", None), P("dp", "seq", None), P())
    return jax.shard_map(shards, mesh=mesh, in_specs=in_specs, out_specs=out_specs, check_vma=False)
```

```python
import functools
import math

import jax
import jax.numpy as jnp
from jax import lax
from jax.experimental import pallas as pl
from jax.experimental.pallas import tpu as pltpu
from jax.sharding import PartitionSpec as P

HD = 128
BLK = 128


blocked_score = -1e30


def shifted(value, axis, steps):
    count = lax.axis_size(axis)
    first, last = (max(0, -steps), min(count, count - steps))
    return lax.ppermute(value, axis, [(source, source + steps) for source in range(first, last)])


def lifted(array_in):
    return lax.optimization_barrier(array_in.astype(jnp.bfloat16)).astype(jnp.float32)


def head_major(tokens_in, block_len):
    token_count, feature_count = tokens_in.shape
    return tokens_in.reshape(
        token_count // block_len, block_len, feature_count // HD, HD
    ).transpose(2, 0, 1, 3)


def token_major(blocks_in):
    head_count, block_count, block_len, depth = blocks_in.shape
    return blocks_in.transpose(1, 2, 0, 3).reshape(1, block_count * block_len, head_count * depth)


def window_parts(query_block, prev_keys, prev_values, grad_block, usable, window_width, temper):
    block_len = query_block.shape[-2]
    inverse_root = 1.0 / math.sqrt(query_block.shape[-1])
    raw_scores = (
        jnp.einsum("...td,...sd->...ts", query_block, prev_keys, preferred_element_type=jnp.float32)
        * inverse_root
    )
    query_pos = lax.broadcasted_iota(jnp.int32, (block_len, block_len), 0)
    key_pos = lax.broadcasted_iota(jnp.int32, (block_len, block_len), 1)
    pair_mask = usable[..., None, None] & (
        key_pos > query_pos + block_len - window_width[..., None, None]
    )
    scores = temper[..., None, None] * raw_scores
    row_top = jnp.max(jnp.where(pair_mask, scores, blocked_score), axis=-1)
    weights = jnp.where(pair_mask, jnp.exp(scores - row_top[..., None]), 0.0)
    prob_grad = jnp.einsum(
        "...td,...sd->...ts", grad_block, prev_values, preferred_element_type=jnp.float32
    )
    return (
        raw_scores,
        pair_mask,
        prob_grad,
        row_top,
        jnp.sum(weights, axis=-1),
        jnp.sum(weights * prob_grad, axis=-1),
    )


def window_grads(
    raw_scores,
    pair_mask,
    prob_grad,
    query_block,
    prev_keys,
    grad_block,
    log_total,
    row_delta,
    temper,
):
    inverse_root = 1.0 / math.sqrt(query_block.shape[-1])
    scaling = (temper * inverse_root)[..., None, None]
    probability = jnp.where(
        pair_mask, jnp.exp(temper[..., None, None] * raw_scores - log_total[..., None]), 0.0
    )
    score_grad = probability * (prob_grad - row_delta[..., None])
    prob_low = probability.astype(jnp.bfloat16)
    grad_low = score_grad.astype(jnp.bfloat16)
    query_part = (
        jnp.einsum("...ts,...sd->...td", grad_low, prev_keys, preferred_element_type=jnp.float32)
        * scaling
    )
    key_part = (
        jnp.einsum("...ts,...td->...sd", grad_low, query_block, preferred_element_type=jnp.float32)
        * scaling
    )
    value_part = jnp.einsum(
        "...ts,...td->...sd", prob_low, grad_block, preferred_element_type=jnp.float32
    )
    temper_part = jnp.sum(score_grad * raw_scores, axis=(-2, -1))
    return (query_part, key_part, value_part, temper_part)


def cluster_pair(
    query_items,
    key_items,
    value_items,
    grad_items,
    live_items,
    temper,
    window_top,
    window_total,
    window_mass,
):
    item_count, block_len, depth = query_items.shape
    row_count = item_count * block_len
    group_rows = 4 * block_len
    inverse_root = 1.0 / math.sqrt(depth)
    scaling = temper * inverse_root
    query_rows = query_items.reshape(row_count, depth)
    key_rows = key_items.reshape(row_count, depth)
    value_rows = value_items.reshape(row_count, depth)
    grad_rows = grad_items.reshape(row_count, depth)
    key_item = jnp.arange(row_count) // block_len
    key_token = jnp.arange(row_count) % block_len
    live_rows = jnp.repeat(live_items, block_len)
    top_rows = window_top.reshape(row_count)
    total_rows = window_total.reshape(row_count)
    mass_rows = window_mass.reshape(row_count)

    def group_step(carry, start_row):
        key_acc, value_acc, temper_acc = carry
        query_group = lax.dynamic_slice_in_dim(query_rows, start_row, group_rows, 0)
        grad_group = lax.dynamic_slice_in_dim(grad_rows, start_row, group_rows, 0)
        group_live = lax.dynamic_slice_in_dim(live_rows, start_row, group_rows, 0)
        group_top = lax.dynamic_slice_in_dim(top_rows, start_row, group_rows, 0)
        group_total = lax.dynamic_slice_in_dim(total_rows, start_row, group_rows, 0)
        group_mass = lax.dynamic_slice_in_dim(mass_rows, start_row, group_rows, 0)
        query_item = (start_row + jnp.arange(group_rows)) // block_len
        query_token = jnp.arange(group_rows) % block_len
        earlier = (key_item[None, :] < query_item[:, None]) | (
            key_item[None, :] == query_item[:, None]
        ) & (key_token[None, :] <= query_token[:, None])
        pair_mask = group_live[:, None] & live_rows[None, :] & earlier
        raw_scores = (
            lax.dot_general(
                query_group, key_rows, (((1,), (1,)), ((), ())), preferred_element_type=jnp.float32
            )
            * inverse_root
        )
        scores = temper * raw_scores
        row_top = jnp.maximum(
            jnp.max(jnp.where(pair_mask, scores, blocked_score), axis=1), group_top
        )
        weights = jnp.where(pair_mask, jnp.exp(scores - row_top[:, None]), 0.0)
        row_total = jnp.sum(weights, axis=1) + group_total * jnp.exp(group_top - row_top)
        log_total = row_top + jnp.log(jnp.where(group_live, row_total, 1.0))
        probability = jnp.where(pair_mask, jnp.exp(scores - log_total[:, None]), 0.0)
        prob_grad = lax.dot_general(
            grad_group, value_rows, (((1,), (1,)), ((), ())), preferred_element_type=jnp.float32
        )
        row_delta = jnp.sum(probability * prob_grad, axis=1) + group_mass * jnp.exp(
            group_top - log_total
        )
        score_grad = probability * (prob_grad - row_delta[:, None])
        prob_low = probability.astype(jnp.bfloat16)
        grad_low = score_grad.astype(jnp.bfloat16)
        query_part = jnp.dot(grad_low, key_rows, preferred_element_type=jnp.float32) * scaling
        key_acc = (
            key_acc
            + lax.dot_general(
                grad_low, query_group, (((0,), (0,)), ((), ())), preferred_element_type=jnp.float32
            )
            * scaling
        )
        value_acc = value_acc + lax.dot_general(
            prob_low, grad_group, (((0,), (0,)), ((), ())), preferred_element_type=jnp.float32
        )
        temper_acc = temper_acc + jnp.sum(score_grad * raw_scores)
        return ((key_acc, value_acc, temper_acc), (query_part, log_total, row_delta))

    start_rows = jnp.arange(item_count // 4) * group_rows
    initial = (
        jnp.zeros((row_count, depth), jnp.float32),
        jnp.zeros((row_count, depth), jnp.float32),
        jnp.zeros((), jnp.float32),
    )
    (key_acc, value_acc, temper_acc), (query_part, log_total, row_delta) = lax.scan(
        group_step, initial, start_rows
    )
    return (
        query_part.reshape(item_count, block_len, depth),
        log_total.reshape(item_count, block_len),
        row_delta.reshape(item_count, block_len),
        key_acc.reshape(item_count, block_len, depth),
        value_acc.reshape(item_count, block_len, depth),
        temper_acc,
    )


def clustered_shards(
    probe_vectors,
    lookup_vectors,
    content_vectors,
    result_cotangent,
    logit_softness,
    block_grouping,
    neighborhood_span,
):
    seq_count = lax.axis_size("seq")
    position = lax.axis_index("seq")
    tokens = probe_vectors.shape[1]
    head_count = probe_vectors.shape[2] // HD
    local_blocks = tokens // BLK
    block_count = local_blocks * seq_count
    cluster_count = max(1, block_count // 8)
    capacity = min(12, block_count)
    owned_pairs = cluster_count * head_count // seq_count
    group_count = cluster_count // owned_pairs
    per_peer = max(1, local_blocks // group_count)
    cluster_ids = block_grouping[0, :, :, 0]
    query_home = head_major(probe_vectors[0], BLK)
    key_home = head_major(lookup_vectors[0], BLK)
    value_home = head_major(content_vectors[0], BLK)
    grad_home = head_major(result_cotangent[0], BLK)
    last_block = (lookup_vectors[0, tokens - BLK :], content_vectors[0, tokens - BLK :])
    prev_key_rows, prev_value_rows = shifted((last_block[0], last_block[1]), "seq", 1)
    prev_keys = jnp.concatenate([head_major(prev_key_rows, BLK), key_home[:, :-1]], axis=1)
    prev_values = jnp.concatenate([head_major(prev_value_rows, BLK), value_home[:, :-1]], axis=1)
    first_block = position * local_blocks
    before = jnp.concatenate(
        [jnp.full((head_count, 1), -1, jnp.int32), cluster_ids[:, :-1]], axis=1
    )
    my_ids = lax.dynamic_slice_in_dim(cluster_ids, first_block, local_blocks, 1)
    my_before = lax.dynamic_slice_in_dim(before, first_block, local_blocks, 1)
    global_block = first_block + jnp.arange(local_blocks)
    usable_home = (global_block[None, :] >= 1) & (my_before != my_ids)
    peer_index = jnp.arange(seq_count)
    peer_head = peer_index * owned_pairs // cluster_count
    slot_range = jnp.arange(per_peer)
    local_range = jnp.arange(local_blocks)
    owner_index = (jnp.arange(head_count)[:, None] * cluster_count + my_ids) // owned_pairs
    peer_ids = jnp.take(my_ids, peer_head, axis=0)
    goes = (peer_head[:, None] * cluster_count + peer_ids) // owned_pairs == peer_index[:, None]
    send_rank = jnp.cumsum(goes.astype(jnp.int32), axis=1) - 1
    send_pick = goes[:, None, :] & (send_rank[:, None, :] == slot_range[None, :, None])
    send_block = jnp.sum(jnp.where(send_pick, local_range[None, None, :], 0), axis=2)
    send_flat = peer_head[:, None] * local_blocks + send_block
    home_rank = jnp.take_along_axis(send_rank, owner_index, axis=0)
    home_pos = owner_index * per_peer + home_rank
    pair_index = position * owned_pairs + jnp.arange(owned_pairs)
    split_for_couple = pair_index // cluster_count
    pair_cluster = pair_index % cluster_count
    my_head = position * owned_pairs // cluster_count
    split_numbers = jnp.take(cluster_ids, my_head, axis=0)
    member = split_numbers[None, :] == pair_cluster[:, None]
    member_rank = jnp.cumsum(member.astype(jnp.int32), axis=1) - 1
    member_count = jnp.sum(member.astype(jnp.int32), axis=1)
    picked = member[:, None, :] & (member_rank[:, None, :] == jnp.arange(capacity)[None, :, None])
    member_block = jnp.sum(jnp.where(picked, jnp.arange(block_count)[None, None, :], 0), axis=2)
    live_members = jnp.arange(capacity)[None, :] < member_count[:, None]
    mine = (my_head * cluster_count + split_numbers) // owned_pairs == position
    mine_grid = mine.reshape(seq_count, local_blocks)
    recv_rank = jnp.cumsum(mine_grid.astype(jnp.int32), axis=1) - 1
    recv_pos = (peer_index[:, None] * per_peer + recv_rank).reshape(block_count)
    member_pos = jnp.take(recv_pos, member_block)
    couple_softness = jnp.take(logit_softness, split_for_couple)
    pair_onehot = (split_for_couple[:, None] == jnp.arange(head_count)[None, :]).astype(jnp.float32)
    slot_pair = my_head * cluster_count + split_numbers - position * owned_pairs
    same_cluster = split_numbers[:, None] == split_numbers[None, :]
    earlier_block = jnp.arange(block_count)[None, :] < jnp.arange(block_count)[:, None]
    slot_rank = jnp.sum((same_cluster & earlier_block).astype(jnp.int32), axis=1)
    back_pos = jnp.clip(slot_pair, 0, owned_pairs - 1) * capacity + jnp.clip(
        slot_rank, 0, capacity - 1
    )
    back_grid = back_pos.reshape(seq_count, local_blocks)
    back_pick = mine_grid[:, None, :] & (recv_rank[:, None, :] == slot_range[None, :, None])
    back_flat = jnp.sum(jnp.where(back_pick, back_grid[:, None, :], 0), axis=2)

    def to_peers(array_in):
        flat = array_in.reshape((head_count * local_blocks,) + array_in.shape[2:])
        return jnp.take(flat, send_flat, axis=0)

    def members(array_in):
        flat = array_in.reshape((seq_count * per_peer,) + array_in.shape[2:])
        return jnp.take(flat, member_pos, axis=0)

    def to_owner(array_in):
        flat = array_in.reshape((owned_pairs * capacity,) + array_in.shape[2:])
        return jnp.take(flat, back_flat, axis=0)

    def from_peers(array_in):
        flat = array_in.reshape((seq_count * per_peer,) + array_in.shape[2:])
        return jnp.take(flat, home_pos, axis=0)

    raw_w, mask_w, pgrad_w, top_w, total_w, mass_w = window_parts(
        query_home,
        prev_keys,
        prev_values,
        grad_home,
        usable_home,
        neighborhood_span[:, None],
        logit_softness[:, None],
    )
    arrived = (
        lax.all_to_all(to_peers(query_home), "seq", split_axis=0, concat_axis=0, tiled=True),
        lax.all_to_all(to_peers(key_home), "seq", split_axis=0, concat_axis=0, tiled=True),
        lax.all_to_all(to_peers(value_home), "seq", split_axis=0, concat_axis=0, tiled=True),
        lax.all_to_all(to_peers(grad_home), "seq", split_axis=0, concat_axis=0, tiled=True),
    )
    arrived_stats = (
        lax.all_to_all(to_peers(top_w), "seq", split_axis=0, concat_axis=0, tiled=True),
        lax.all_to_all(to_peers(total_w), "seq", split_axis=0, concat_axis=0, tiled=True),
        lax.all_to_all(to_peers(mass_w), "seq", split_axis=0, concat_axis=0, tiled=True),
    )
    query_m, key_m, value_m, grad_m = [members(item_in) for item_in in arrived]
    top_m, total_m, mass_m = [members(item_in) for item_in in arrived_stats]

    def split_pair(pair_inputs):
        query_i, key_i, value_i, grad_i, live_i, temper_i, top_i, total_i, mass_i = pair_inputs
        query_c, log_total, row_delta, key_c, value_c, temper_c = cluster_pair(
            query_i, key_i, value_i, grad_i, live_i, temper_i, top_i, total_i, mass_i
        )
        return (
            query_c.astype(jnp.bfloat16),
            key_c.astype(jnp.bfloat16),
            value_c.astype(jnp.bfloat16),
            log_total,
            row_delta,
            temper_c,
        )

    owner_results = lax.map(
        split_pair,
        (query_m, key_m, value_m, grad_m, live_members, couple_softness, top_m, total_m, mass_m),
    )
    returned = (
        lax.all_to_all(to_owner(owner_results[0]), "seq", split_axis=0, concat_axis=0, tiled=True),
        lax.all_to_all(to_owner(owner_results[1]), "seq", split_axis=0, concat_axis=0, tiled=True),
        lax.all_to_all(to_owner(owner_results[2]), "seq", split_axis=0, concat_axis=0, tiled=True),
    )
    returned_stats = (
        lax.all_to_all(to_owner(owner_results[3]), "seq", split_axis=0, concat_axis=0, tiled=True),
        lax.all_to_all(to_owner(owner_results[4]), "seq", split_axis=0, concat_axis=0, tiled=True),
    )
    query_cluster = from_peers(returned[0])
    key_cluster = from_peers(returned[1])
    value_cluster = from_peers(returned[2])
    log_home = from_peers(returned_stats[0])
    delta_home = from_peers(returned_stats[1])
    query_w, key_w, value_w, temper_w = window_grads(
        raw_w,
        mask_w,
        pgrad_w,
        query_home,
        prev_keys,
        grad_home,
        log_home,
        delta_home,
        logit_softness[:, None],
    )
    query_out = (query_cluster.astype(jnp.float32) + lifted(query_w)).astype(jnp.bfloat16)
    key_window = key_w.astype(jnp.bfloat16)
    value_window = value_w.astype(jnp.bfloat16)
    temper_local = jnp.sum(owner_results[5][:, None] * pair_onehot, axis=0) + jnp.sum(
        temper_w, axis=1
    )
    edge_keys, edge_values = shifted((key_window[:, 0], value_window[:, 0]), "seq", -1)
    key_next = jnp.concatenate([key_window[:, 1:], edge_keys[:, None]], axis=1)
    value_next = jnp.concatenate([value_window[:, 1:], edge_values[:, None]], axis=1)
    key_out = (key_cluster.astype(jnp.float32) + key_next.astype(jnp.float32)).astype(jnp.bfloat16)
    value_out = (value_cluster.astype(jnp.float32) + value_next.astype(jnp.float32)).astype(
        jnp.bfloat16
    )
    temper_total = lax.psum(temper_local, ("seq", "dp"))
    temper_grad = temper_total / (lax.axis_size("dp") * tokens * seq_count)
    return (token_major(query_out), token_major(key_out), token_major(value_out), temper_grad)


TILE = 256
EXTRA = 16
MIB = 1024 * 1024
PIECES = 4
QUERY, KEY, VALUE, GRAD = range(4)


def columns_of(index):
    return pl.ds(pl.multiple_of(index * HD, HD), HD)


def rows_of(index):
    return pl.ds(pl.multiple_of(index * BLK, BLK), BLK)


def tile_rows(tile):
    return slice(tile * TILE, (tile + 1) * TILE)


def position(half_count):
    me = lax.axis_index("seq")
    half = jnp.where(me >= half_count, 1, 0)
    return me, half, me - half * half_count


def kernel_call(
    kernel, name, operands, in_specs, out_shape, scratch, vmem_mib, flops=0, out_spaces=None,
    aliases=None,
):
    bytes_accessed = sum(
        math.prod(item.shape) * item.dtype.itemsize for item in (*operands, *out_shape)
    )
    return pl.pallas_call(
        kernel,
        out_shape=out_shape,
        in_specs=in_specs,
        out_specs=[
            pl.BlockSpec(memory_space=space)
            for space in out_spaces or [pltpu.VMEM] * len(out_shape)
        ],
        scratch_shapes=scratch,
        input_output_aliases=aliases or {},
        cost_estimate=pl.CostEstimate(
            flops=flops, bytes_accessed=bytes_accessed, transcendentals=0
        ),
        compiler_params=pltpu.CompilerParams(vmem_limit_bytes=vmem_mib * MIB),
        name=name,
    )(*operands)


def pack_kernel(*refs, half_count):
    arrays, within_ref, foreign_refs = refs[:4], refs[4], refs[5:7]
    held, within, across, arrival, left_within, left_across = refs[7:]
    me, half, _ = position(half_count)
    piece = BLK // PIECES
    arrivals = [
        [
            pltpu.make_async_copy(
                array_ref.at[0, part * piece : (part + 1) * piece, :],
                held.at[place, part * piece : (part + 1) * piece, :],
                arrival.at[place, part],
            )
            for part in range(PIECES)
        ]
        for place, array_ref in enumerate(arrays)
    ]
    for copies in arrivals:
        for copy in copies:
            copy.start()
    leaving = []
    for place, copies in enumerate(arrivals):
        for copy in copies:
            copy.wait()
        for slot, base in enumerate((half * half_count, (1 - half) * half_count)):
            rows = slice((slot * 4 + place) * BLK, (slot * 4 + place + 1) * BLK)
            for peer in range(half_count):
                within[peer, rows, :] = held[place, :, columns_of(base + peer)]
            leaving.append(
                pltpu.make_async_copy(
                    within.at[:, rows, :], within_ref.at[:, rows, :], left_within.at[place, slot]
                )
            )
            leaving[-1].start()
    first = jnp.where(half == 0, KEY, QUERY)
    second = jnp.where(half == 0, VALUE, GRAD)
    for core, foreign_ref in enumerate(foreign_refs):
        for step in range(half_count // 2):
            columns = columns_of(me ^ core ^ (half_count + 2 * step))
            across[core, step, :BLK, :] = held[first, :, columns]
            across[core, step, BLK:, :] = held[second, :, columns]
        leaving.append(pltpu.make_async_copy(across.at[core], foreign_ref, left_across.at[core]))
        leaving[-1].start()
    for copy in leaving:
        copy.wait()


def packed(arrays, half_count):
    width = arrays[0].shape[2]
    within_shape, across_shape = (half_count, 8 * BLK, HD), (half_count // 2, 2 * BLK, HD)
    return kernel_call(
        functools.partial(pack_kernel, half_count=half_count),
        "pack_heads",
        arrays,
        [pl.BlockSpec(memory_space=pl.ANY)] * 4,
        [jax.ShapeDtypeStruct(within_shape, jnp.bfloat16)]
        + [jax.ShapeDtypeStruct(across_shape, jnp.bfloat16)] * 2,
        [
            pltpu.VMEM((4, BLK, width), jnp.bfloat16),
            pltpu.VMEM(within_shape, jnp.bfloat16),
            pltpu.VMEM((2, *across_shape), jnp.bfloat16),
            pltpu.SemaphoreType.DMA((4, PIECES)),
            pltpu.SemaphoreType.DMA((4, 2)),
            pltpu.SemaphoreType.DMA((2,)),
        ],
        60,
        out_spaces=[pl.ANY] * 3,
    )


def dot_rows(left, right):
    return lax.dot_general(
        left, right, (((1,), (1,)), ((), ())), preferred_element_type=jnp.float32
    )


def dot_plain(left, right):
    return lax.dot_general(
        left, right, (((1,), (0,)), ((), ())), preferred_element_type=jnp.float32
    )


def from_blocks(ref, place):
    def rows(start, stop):
        per_tile = TILE // BLK
        return jnp.concatenate(
            [ref[block, place] for block in range(start * per_tile, stop * per_tile)],
            axis=0,
        )

    return rows


def from_array(ref, place):
    return lambda start, stop: ref[place, start * TILE : stop * TILE, :]


class Region:
    def __init__(self, square, sources, tiles, scaling, bias_ref=None, least_ref=None, first=0):
        self.square, self.sources, self.tiles, self.scaling = square, sources, tiles, scaling
        self.bias_ref, self.least_ref, self.first = bias_ref, least_ref, first

    def rows(self, which, start, stop):
        return self.sources[which](start, stop)

    def scale_of(self, array):
        return 1.0 if array == VALUE else self.scaling[:, :HD]

    def keys_of(self, tile):
        return range(self.tiles if self.square else tile + 1)

    def scores(self, tile_key, tile_query):
        per_tile = TILE // BLK
        scores = dot_rows(
            self.rows(KEY, tile_key, tile_key + 1), self.rows(QUERY, tile_query, tile_query + 1)
        ) * (self.scaling * math.log2(math.e))
        before = self.tiles * per_tile if self.square else 0
        rows = []
        for sub_key in range(per_tile):
            key_block = tile_key * per_tile + sub_key
            pieces = []
            for sub_query in range(per_tile):
                query_block = tile_query * per_tile + sub_query
                lanes = slice(sub_query * BLK, (sub_query + 1) * BLK)
                piece = scores[sub_key * BLK : (sub_key + 1) * BLK, lanes]
                apart = before + query_block - key_block
                if apart < 0:
                    piece = jnp.full_like(piece, blocked_score)
                elif apart == 0:
                    piece = jnp.where(key_minus_query() <= 0, piece, blocked_score)
                elif apart == 1:
                    row = self.first + (0 if self.square else key_block)
                    least = self.least_ref[row : row + 1, :]
                    piece = jnp.where(key_minus_query() > least, piece, blocked_score)
                else:
                    at = slice(query_block * BLK, (query_block + 1) * BLK)
                    piece = piece + self.bias_ref[key_block : key_block + 1, at]
                pieces.append(piece)
            rows.append(jnp.concatenate(pieces, axis=1))
        return jnp.concatenate(rows, axis=0)


def diagonal(slot, arrived_ref, scales_ref, bias_ref=None, least_ref=None):
    blocks = arrived_ref.shape[0]
    sources = [from_blocks(arrived_ref, slot * 4 + place) for place in range(4)]
    bias = None if bias_ref is None else bias_ref.at[slot]
    first = slot * (blocks - 1)
    scaling = scales_ref[slot : slot + 1, :]
    return Region(False, sources, blocks * BLK // TILE, scaling, bias, least_ref, first)


def square(square_ref, scales_ref, bias_ref=None, least_ref=None):
    tiles = square_ref.shape[1] // TILE
    sources = [from_array(square_ref, place) for place in range(4)]
    bias = None if bias_ref is None else bias_ref.at[2]
    first = 2 * (tiles * TILE // BLK - 1)
    return Region(True, sources, tiles, scales_ref[0:1, :], bias, least_ref, first)


def key_minus_query():
    shape = (BLK, BLK)
    return lax.broadcasted_iota(jnp.int32, shape, 0) - lax.broadcasted_iota(jnp.int32, shape, 1)


def statistics(region, weight_ref, towards_ref, out_ref, first_row):
    for tile in range(region.tiles):
        here = tile_rows(tile)
        top = jnp.full((1, TILE), blocked_score, jnp.float32)
        for other in region.keys_of(tile):
            raw = region.scores(other, tile)
            weight_ref[tile_rows(other), here] = raw
            top = jnp.maximum(top, jnp.max(raw, axis=0, keepdims=True))
        sums = [jnp.zeros((1, TILE), jnp.float32)] * 4
        for other in region.keys_of(tile):
            there = tile_rows(other)
            raw = weight_ref[there, here]
            weight = jnp.exp2(raw - top)
            towards = dot_rows(
                region.rows(VALUE, other, other + 1), region.rows(GRAD, tile, tile + 1)
            )
            weight_ref[there, here] = weight
            towards_ref[there, here] = towards
            pulled, weighted = weight * towards, weight * raw
            terms = (weight, pulled, pulled * raw, weighted)
            sums = [
                total + jnp.sum(term, axis=0, keepdims=True) for total, term in zip(sums, terms)
            ]
        for row, value in enumerate((top, *sums)):
            out_ref[first_row + row : first_row + row + 1, here] = value


def gradients(
    region, weight_ref, towards_ref, top, log_total, delta, prob_low, grad_low, keys_flat, emit=None
):
    keys_flat[...] = region.rows(KEY, 0, region.tiles).T
    share = jnp.exp2(top - log_total)
    query_parts, key_parts, value_parts = [], [], []
    for tile in range(region.tiles):
        here = tile_rows(tile)
        for other in region.keys_of(tile):
            there = tile_rows(other)
            probability = weight_ref[there, here] * share[:, here]
            prob_low[there, here] = probability.astype(jnp.bfloat16)
            grad_low[there, here] = (
                probability * (towards_ref[there, here] - delta[:, here])
            ).astype(jnp.bfloat16)
        upto = slice(0, len(region.keys_of(tile)) * TILE)
        query_parts.append(dot_plain(keys_flat[:, upto], grad_low[upto, here]).T)
    if emit is not None:
        emit(QUERY, query_parts)
    for low, which, parts in ((grad_low, QUERY, key_parts), (prob_low, GRAD, value_parts)):
        for tile in range(region.tiles):
            first = 0 if region.square else tile
            onward = slice(first * TILE, region.tiles * TILE)
            parts.append(
                dot_plain(low[tile_rows(tile), onward], region.rows(which, first, region.tiles))
            )
        if emit is not None:
            emit(KEY if which == QUERY else VALUE, parts)
    return query_parts, key_parts, value_parts


def merged(first, second):
    top = jnp.maximum(first[0], second[0])
    left, right = jnp.exp2(first[0] - top), jnp.exp2(second[0] - top)
    total = first[1] * left + second[1] * right
    mass = first[2] * left + second[2] * right
    return top + jnp.log2(total), mass / total


def alone(rows):
    return rows[0] + jnp.log2(rows[1]), rows[2] / rows[1]


def rows_at(ref, first, count=5):
    return [ref[first + row : first + row + 1, :] for row in range(count)]


def temper_terms(rows, totals, scale_row):
    log_total, delta = totals
    terms = (rows[3] - delta * rows[4]) * jnp.exp2(rows[0] - log_total)
    folded = sum(terms[:, start : start + HD] for start in range(0, terms.shape[1], HD))
    return folded / (scale_row[:, :HD] * (math.sqrt(HD) * math.log2(math.e)))


def put(within_ref, array, tile, value):
    per_tile = TILE // BLK
    for sub in range(per_tile):
        within_ref[tile * per_tile + sub, array * BLK : (array + 1) * BLK, :] = value[
            sub * BLK : (sub + 1) * BLK, :
        ].astype(jnp.bfloat16)


def scaled(region, parts):
    scale = region.scaling[:, :HD]
    return [[value * scale for value in part] for part in parts[:2]] + [parts[2]]


def masks_kernel(softness_ref, ids_ref, span_ref, scales_ref, bias_ref, least_ref, *, half_count):
    me, half, _ = position(half_count)
    base = half * half_count
    regions = (
        (me, base, base),
        (me ^ half_count, base, base),
        (me, 0, half_count),
    )
    for slot, (head, key_base, query_base) in enumerate(regions):
        if slot < 2:
            scales_ref[slot : slot + 1, :] = jnp.full(
                (1, TILE), softness_ref[head] * (1.0 / math.sqrt(HD)), jnp.float32
            )

        def same(key_block, query_block):
            return ids_ref[head, key_base + key_block] == ids_ref[head, query_base + query_block]

        def bias(key_block, query_block):
            return jnp.full(
                (1, BLK), jnp.where(same(key_block, query_block), 0.0, blocked_score), jnp.float32
            )

        for key_block in range(half_count):
            bias_ref[slot, key_block : key_block + 1, :] = jnp.concatenate(
                [bias(key_block, query_block) for query_block in range(half_count)], axis=1
            )
        pairs = [(block, block + 1) for block in range(half_count - 1)]
        if slot == 2:
            pairs = [(half_count - 1, 0)]
        for place, pair in enumerate(pairs):
            least = jnp.where(same(*pair), -BLK, BLK - span_ref[head])
            row = slot * (half_count - 1) + place
            least_ref[row : row + 1, :] = jnp.full((1, BLK), least, jnp.int32)


def within_kernel(
    arrived_ref, scales_ref, bias_ref, least_ref, stats_ref, parts_ref, own_weight, own_towards, other_weight, other_towards, *scratch, half_count
):
    _, half, _ = position(half_count)
    kept = ((own_weight, own_towards), (other_weight, other_towards))
    for slot in range(2):
        region = diagonal(slot, arrived_ref, scales_ref, bias_ref, least_ref)
        statistics(region, *kept[slot], stats_ref, slot * 5)

    @pl.when(half == 0)
    def _():
        region = diagonal(0, arrived_ref, scales_ref)
        single = alone(rows_at(stats_ref, 0))
        parts = gradients(region, *kept[0], stats_ref[0:1, :], *single, *scratch)
        for place, tiles in enumerate(scaled(region, parts)):
            for tile, value in enumerate(tiles):
                parts_ref[place, tile_rows(tile), :] = value


def square_kernel(arrived_ref, scales_ref, bias_ref, least_ref, stats_ref, *refs, half_count):
    across_refs = refs[: half_count // 2]
    square_ref, message_ref, square_stats, weight, towards = refs[half_count // 2 :]
    _, half, place = position(half_count)
    first = jnp.where(half == 0, QUERY, KEY)
    second = jnp.where(half == 0, GRAD, VALUE)
    for step, across_ref in enumerate(across_refs):
        for core in range(2):
            rows = rows_of(place ^ core ^ (2 * step))
            square_ref[first, rows, :] = across_ref[core, :BLK, :]
            square_ref[second, rows, :] = across_ref[core, BLK:, :]
    for kept in (jnp.where(half == 0, KEY, QUERY), jnp.where(half == 0, VALUE, GRAD)):
        for block in range(half_count):
            square_ref[kept, block * BLK : (block + 1) * BLK, :] = arrived_ref[block, kept]
    region = square(square_ref, scales_ref, bias_ref, least_ref)
    statistics(region, weight, towards, square_stats, 0)
    own, other, crossing = rows_at(stats_ref, 0), rows_at(stats_ref, 5), rows_at(square_stats, 0)
    for row in range(5):
        message_ref[row : row + 1, :] = jnp.where(half == 0, crossing[row], other[row])
    own_scale, other_scale = scales_ref[0:1, :], scales_ref[1:2, :]
    both = merged(own, crossing)
    whole = temper_terms(own, both, own_scale) + temper_terms(crossing, both, own_scale)
    single = temper_terms(own, alone(own), own_scale)
    message_ref[5:6, :HD] = jnp.where(half == 0, single, whole)
    message_ref[6:7, :HD] = temper_terms(other, alone(other), other_scale)


def first_kernel(
    arrived_ref, scales_ref, square_ref, stats_ref, square_stats,
    own_weight, own_towards, other_weight, other_towards, square_weight, square_towards,
    across_ref, within_ref, ready, ready_sem, *scratch, half_count
):
    _, half, _ = position(half_count)
    leaving = sends(ready, within_ref, ready_sem, (1 - half) * 3)

    @pl.when(half == 0)
    def _():
        region = diagonal(1, arrived_ref, scales_ref)

        def send(array, parts):
            for tile, part in enumerate(parts):
                put(ready, array, tile, part * region.scale_of(array))
            leaving[array].start()

        totals = alone(rows_at(stats_ref, 5))
        gradients(
            region, other_weight, other_towards, stats_ref[5:6, :], *totals, *scratch, emit=send
        )

    @pl.when(half == 1)
    def _():
        totals = merged(rows_at(stats_ref, 0), rows_at(square_stats, 0))
        region = square(square_ref, scales_ref)
        parts = gradients(
            region, square_weight, square_towards, square_stats[0:1, :], *totals, *scratch
        )
        across_query, *foreign = scaled(region, parts)
        for array, tiles in enumerate(foreign):
            for tile, value in enumerate(tiles):
                across_ref[array, tile_rows(tile), :] = value.astype(jnp.bfloat16)
        region = diagonal(0, arrived_ref, scales_ref)

        def send(array, parts):
            for tile, part in enumerate(parts):
                value = part * region.scale_of(array)
                put(ready, array, tile, value + across_query[tile] if array == QUERY else value)
            leaving[array].start()

        gradients(
            region, own_weight, own_towards, stats_ref[0:1, :], *totals, *scratch, emit=send
        )

    for copy in leaving:
        copy.wait()


def sends(ready, within_ref, sems, first):
    copies = []
    for array in range(3):
        rows = slice(array * BLK, (array + 1) * BLK)
        copies.append(
            pltpu.make_async_copy(
                ready.at[:, rows, :], within_ref.at[:, rows_of(first + array), :], sems.at[array]
            )
        )
    return copies


def temper_rows(own, other):
    row = lax.broadcasted_iota(jnp.int32, (EXTRA, HD), 0)
    rows = jnp.zeros((EXTRA, HD), jnp.float32)
    for place, terms in enumerate((own, other)):
        rest = jnp.broadcast_to(jnp.sum(terms, axis=1, keepdims=True), (EXTRA, HD))
        for piece in range(3):
            high = rest.astype(jnp.bfloat16).astype(jnp.float32)
            rows = jnp.where(row == place * 3 + piece, high, rows)
            rest = rest - high
    return rows.astype(jnp.bfloat16)


def finish_kernel(
    arrived_ref, scales_ref, square_ref, message_ref, received_ref, stats_ref, square_stats,
    parts_ref, square_weight, square_towards, other_weight, other_towards, across_ref, begun_ref,
    within_ref, *refs, half_count
):
    del begun_ref
    chunk_refs = refs[:2]
    across, ready, ready_sem, *scratch = refs[2:]
    _, half, place = position(half_count)
    leaving = sends(ready, within_ref, ready_sem, half * 3)
    sent, came = rows_at(message_ref, 0), rows_at(received_ref, 0)
    totals = merged(sent, came)
    scale = jnp.where(half == 0, scales_ref[0:1, :], scales_ref[1:2, :])
    shared = temper_terms(sent, totals, scale) + temper_terms(came, totals, scale)
    mine, theirs = message_ref[5:6, :HD], received_ref[5:6, :HD]
    own = mine + jnp.where(half == 0, shared, received_ref[6:7, :HD])
    other = theirs + jnp.where(half == 0, message_ref[6:7, :HD], shared)
    pieces = temper_rows(own, other)

    def chunks():
        for core, chunk_ref in enumerate(chunk_refs):
            for step in range(half_count // 2):
                yield step, chunk_ref, rows_of(place ^ core ^ (2 * step))

    @pl.when(half == 0)
    def _():
        region = square(square_ref, scales_ref)

        def send(array, parts):
            for tile, part in enumerate(parts):
                here = tile_rows(tile)
                value = part * region.scale_of(array)
                if array == QUERY:
                    across[here, :] = value.astype(jnp.bfloat16)
                    put(ready, array, tile, parts_ref[array, here, :])
                else:
                    put(ready, array, tile, parts_ref[array, here, :] + value)
            leaving[array].start()

        gradients(
            region, square_weight, square_towards, square_stats[0:1, :], *totals, *scratch, emit=send
        )
        for step, chunk_ref, rows in chunks():
            chunk_ref[step, :BLK, :] = across[rows, :]
            chunk_ref[step, BLK : 2 * BLK, :] = jnp.zeros((BLK, HD), jnp.bfloat16)

    @pl.when(half == 1)
    def _():
        region = diagonal(1, arrived_ref, scales_ref)

        def send(array, parts):
            for tile, part in enumerate(parts):
                put(ready, array, tile, part * region.scale_of(array))
            leaving[array].start()

        gradients(
            region, other_weight, other_towards, stats_ref[5:6, :], *totals, *scratch, emit=send
        )
        for step, chunk_ref, rows in chunks():
            chunk_ref[step, :BLK, :] = across_ref[0, rows, :]
            chunk_ref[step, BLK : 2 * BLK, :] = across_ref[1, rows, :]

    for step, chunk_ref, _ in chunks():
        chunk_ref[step, 2 * BLK :, :] = pieces
    for copy in leaving:
        copy.wait()


def temper_kernel(*refs, half_count):
    across_refs, temper_ref = refs[:-1], refs[-1]
    _, half, place = position(half_count)
    for step, across_ref in enumerate(across_refs):
        for core in range(2):
            peer = place ^ core ^ (2 * step)
            for slot, base in enumerate(((1 - half) * half_count, half * half_count)):
                rows = across_ref[core, 3 * slot : 3 * slot + 3, :].astype(jnp.float32)
                temper_ref[pl.ds(base + peer, 1), :] = jnp.sum(rows, axis=0, keepdims=True)


def temper_sums(across, half_count):
    last = 2 * BLK // EXTRA
    return pl.pallas_call(
        functools.partial(temper_kernel, half_count=half_count),
        grid=(1,),
        out_shape=jax.ShapeDtypeStruct((2 * half_count, HD), jnp.float32),
        in_specs=[pl.BlockSpec((2, EXTRA, HD), lambda step: (0, last, 0))] * len(across),
        out_specs=pl.BlockSpec((2 * half_count, HD), lambda step: (0, 0)),
        compiler_params=pltpu.CompilerParams(vmem_limit_bytes=4 * MIB),
        name="temper_sums",
    )(*across)


def unpack_kernel(within_ref, *refs, half_count):
    across_refs = refs[: half_count // 2]
    out_refs = refs[half_count // 2 :]
    _, half, place = position(half_count)
    for step, across_ref in enumerate(across_refs):
        for core in range(2):
            peer = place ^ core ^ (2 * step)
            other = columns_of((1 - half) * half_count + peer)
            own = columns_of(half * half_count + peer)
            first = across_ref[core, :BLK, :].astype(jnp.float32)
            second = across_ref[core, BLK : 2 * BLK, :].astype(jnp.float32)
            added = (
                jnp.where(half == 0, 0.0, first),
                jnp.where(half == 0, first, 0.0),
                jnp.where(half == 0, second, 0.0),
            )
            for array, out_ref in enumerate(out_refs):
                out_ref[0, :, own] = within_ref[peer, array * BLK : (array + 1) * BLK, :]
                kept = within_ref[peer, (3 + array) * BLK : (4 + array) * BLK, :]
                out_ref[0, :, other] = (kept.astype(jnp.float32) + added[array]).astype(
                    jnp.bfloat16
                )


def join_kernel(kept_ref, taken_ref, *out_refs):
    for step, out_ref in enumerate(out_refs):
        out_ref[0] = kept_ref[step]
        out_ref[1] = taken_ref[step]


def crossed(kept, given, half_count):
    devices = range(2 * half_count)
    steps, *shape = kept.shape
    taken = lax.ppermute(given, "seq", [(source, source ^ 1) for source in devices])
    messages = kernel_call(
        join_kernel,
        "join_chunks",
        (kept, taken),
        [pl.BlockSpec(memory_space=pltpu.VMEM)] * 2,
        [jax.ShapeDtypeStruct((2, *shape), jnp.bfloat16)] * steps,
        [],
        4,
    )
    return [
        lax.ppermute(
            message, "seq", [(source, source ^ (half_count + 2 * step)) for source in devices]
        )
        for step, message in enumerate(messages)
    ]


def head_shards(
    probe_vectors,
    lookup_vectors,
    content_vectors,
    result_cotangent,
    logit_softness,
    block_grouping,
    neighborhood_span,
):
    seq_count, dp_count = lax.axis_size("seq"), lax.axis_size("dp")
    half_count = seq_count // 2
    tokens = half_count * BLK
    groups = [list(range(half_count)), list(range(half_count, seq_count))]
    settings = (logit_softness, block_grouping[0, :, :, 0], neighborhood_span)
    smem, vmem = pl.BlockSpec(memory_space=pltpu.SMEM), pl.BlockSpec(memory_space=pltpu.VMEM)
    lows = [pltpu.VMEM((tokens, tokens), jnp.bfloat16)] * 2 + [
        pltpu.VMEM((HD, tokens), jnp.bfloat16)
    ]
    rows_of_stats = jax.ShapeDtypeStruct((8, tokens), jnp.float32)
    pairs = jax.ShapeDtypeStruct((tokens, tokens), jnp.float32)
    pair_flops = 2 * tokens * tokens * HD

    def exchange_within(array_in):
        return lax.all_to_all(
            array_in, "seq", split_axis=0, concat_axis=0, axis_index_groups=groups, tiled=True
        )

    def call(
        kernel, name, operands, out_shape, scratch, flops, vmem_mib, scalars=(), out_spaces=None,
        last_in_place=False,
    ):
        in_specs = [smem] * len(scalars) + [vmem] * len(operands)
        if last_in_place:
            in_specs[-1] = pl.BlockSpec(memory_space=pl.ANY)
        return kernel_call(
            functools.partial(kernel, half_count=half_count),
            name,
            (*scalars, *operands),
            in_specs,
            out_shape,
            scratch,
            vmem_mib,
            flops,
            out_spaces,
            {len(operands) - 1: 0} if last_in_place else {},
        )

    sent, *foreign = packed(
        (probe_vectors, lookup_vectors, content_vectors, result_cotangent), half_count
    )
    arrived = exchange_within(sent).reshape(half_count, 8, BLK, HD)
    kept_parts = jax.ShapeDtypeStruct((3, tokens, HD), jnp.float32)
    masks = call(
        masks_kernel,
        "scales_and_masks",
        (),
        [
            jax.ShapeDtypeStruct((8, TILE), jnp.float32),
            jax.ShapeDtypeStruct((3, half_count, tokens), jnp.float32),
            jax.ShapeDtypeStruct((2 * half_count, BLK), jnp.int32),
        ],
        [],
        0,
        2,
        settings,
    )
    foreign[0], *masks = lax.optimization_barrier((foreign[0], *masks))
    foreign = crossed(*foreign, half_count)
    scales = masks[0]
    stats, parts, own_weight, own_towards, other_weight, other_towards = call(
        within_kernel,
        "diagonal_statistics",
        (arrived, *masks),
        [jax.ShapeDtypeStruct((16, tokens), jnp.float32), kept_parts] + [pairs] * 4,
        lows,
        2 * pair_flops,
        14,
    )
    squared, message, square_stats, square_weight, square_towards = call(
        square_kernel,
        "square_statistics",
        (arrived, *masks, stats, *foreign),
        [jax.ShapeDtypeStruct((4, tokens, HD), jnp.bfloat16)] + [rows_of_stats] * 2 + [pairs] * 2,
        [],
        2 * pair_flops,
        8,
    )
    swap = [(source, source ^ half_count) for source in range(seq_count)]
    received = lax.ppermute(message, "seq", swap)
    result = pltpu.HBM((half_count, 6 * BLK, HD), jnp.bfloat16)
    ready = pltpu.VMEM((half_count, 3 * BLK, HD), jnp.bfloat16)
    across, begun = call(
        first_kernel,
        "gradients_before_totals",
        (
            arrived, scales, squared, stats, square_stats, own_weight, own_towards,
            other_weight, other_towards, square_weight, square_towards,
        ),
        [jax.ShapeDtypeStruct((2, tokens, HD), jnp.bfloat16), result],
        [ready, pltpu.SemaphoreType.DMA((3,)), *lows],
        4 * pair_flops,
        14,
        out_spaces=(pltpu.VMEM, pl.ANY),
    )
    operands = (
        arrived, scales, squared, message, received, stats, square_stats, parts,
        square_weight, square_towards, other_weight, other_towards, across, begun,
    )
    within, *foreign = call(
        finish_kernel,
        "gradients_after_totals",
        operands,
        [result]
        + [jax.ShapeDtypeStruct((half_count // 2, 2 * BLK + EXTRA, HD), jnp.bfloat16)] * 2,
        [
            pltpu.VMEM((tokens, HD), jnp.bfloat16), ready,
            pltpu.SemaphoreType.DMA((3,)), *lows,
        ],
        2 * pair_flops,
        16,
        out_spaces=(pl.ANY, pltpu.VMEM, pltpu.VMEM),
        last_in_place=True,
    )
    across = crossed(*foreign, half_count)
    across[0], within = lax.optimization_barrier((across[0], within))
    within = exchange_within(within)
    tempers = temper_sums(across, half_count)
    temper_total = tempers
    for step in range(1, dp_count):
        swap = [(source, (source + step) % dp_count) for source in range(dp_count)]
        temper_total = temper_total + lax.ppermute(tempers, "dp", swap)
    temper = temper_total[:, 0] / (dp_count * BLK * seq_count)
    within, temper = lax.optimization_barrier((within, temper))
    outs = kernel_call(
        functools.partial(unpack_kernel, half_count=half_count),
        "unpack_heads",
        (within, *across),
        [vmem] * (1 + len(across)),
        [jax.ShapeDtypeStruct(probe_vectors.shape, jnp.bfloat16)] * 3,
        [],
        10,
    )
    return (*outs, temper)


def shards(
    probe_vectors,
    lookup_vectors,
    content_vectors,
    result_cotangent,
    logit_softness,
    block_grouping,
    neighborhood_span,
):
    head_count = probe_vectors.shape[2] // HD
    seq_count = lax.axis_size("seq")
    one_block = probe_vectors.shape[1] == BLK
    whole_tiles = seq_count * BLK % (2 * TILE) == 0 and seq_count & (seq_count - 1) == 0
    if head_count == seq_count and one_block and whole_tiles:
        plan = head_shards
    else:
        plan = clustered_shards
    return plan(
        probe_vectors,
        lookup_vectors,
        content_vectors,
        result_cotangent,
        logit_softness,
        block_grouping,
        neighborhood_span,
    )


def solution(mesh):
    in_specs = (
        P("dp", "seq", None),
        P("dp", "seq", None),
        P("dp", "seq", None),
        P("dp", "seq", None),
        P(),
        P("dp", None, None, None),
        P(),
    )
    out_specs = (P("dp", "seq", None), P("dp", "seq", None), P("dp", "seq", None), P())
    return jax.shard_map(shards, mesh=mesh, in_specs=in_specs, out_specs=out_specs, check_vma=False)
```

```python
import functools
import math

import jax
import jax.numpy as jnp
from jax import lax
from jax.experimental import pallas as pl
from jax.experimental.pallas import tpu as pltpu
from jax.sharding import PartitionSpec as P

HD = 128
BLK = 128


blocked_score = -1e30


def shifted(value, axis, steps):
    count = lax.axis_size(axis)
    first, last = (max(0, -steps), min(count, count - steps))
    return lax.ppermute(value, axis, [(source, source + steps) for source in range(first, last)])


def lifted(array_in):
    return lax.optimization_barrier(array_in.astype(jnp.bfloat16)).astype(jnp.float32)


def head_major(tokens_in, block_len):
    token_count, feature_count = tokens_in.shape
    return tokens_in.reshape(
        token_count // block_len, block_len, feature_count // HD, HD
    ).transpose(2, 0, 1, 3)


def token_major(blocks_in):
    head_count, block_count, block_len, depth = blocks_in.shape
    return blocks_in.transpose(1, 2, 0, 3).reshape(1, block_count * block_len, head_count * depth)


def window_parts(query_block, prev_keys, prev_values, grad_block, usable, window_width, temper):
    block_len = query_block.shape[-2]
    inverse_root = 1.0 / math.sqrt(query_block.shape[-1])
    raw_scores = (
        jnp.einsum("...td,...sd->...ts", query_block, prev_keys, preferred_element_type=jnp.float32)
        * inverse_root
    )
    query_pos = lax.broadcasted_iota(jnp.int32, (block_len, block_len), 0)
    key_pos = lax.broadcasted_iota(jnp.int32, (block_len, block_len), 1)
    pair_mask = usable[..., None, None] & (
        key_pos > query_pos + block_len - window_width[..., None, None]
    )
    scores = temper[..., None, None] * raw_scores
    row_top = jnp.max(jnp.where(pair_mask, scores, blocked_score), axis=-1)
    weights = jnp.where(pair_mask, jnp.exp(scores - row_top[..., None]), 0.0)
    prob_grad = jnp.einsum(
        "...td,...sd->...ts", grad_block, prev_values, preferred_element_type=jnp.float32
    )
    return (
        raw_scores,
        pair_mask,
        prob_grad,
        row_top,
        jnp.sum(weights, axis=-1),
        jnp.sum(weights * prob_grad, axis=-1),
    )


def window_grads(
    raw_scores,
    pair_mask,
    prob_grad,
    query_block,
    prev_keys,
    grad_block,
    log_total,
    row_delta,
    temper,
):
    inverse_root = 1.0 / math.sqrt(query_block.shape[-1])
    scaling = (temper * inverse_root)[..., None, None]
    probability = jnp.where(
        pair_mask, jnp.exp(temper[..., None, None] * raw_scores - log_total[..., None]), 0.0
    )
    score_grad = probability * (prob_grad - row_delta[..., None])
    prob_low = probability.astype(jnp.bfloat16)
    grad_low = score_grad.astype(jnp.bfloat16)
    query_part = (
        jnp.einsum("...ts,...sd->...td", grad_low, prev_keys, preferred_element_type=jnp.float32)
        * scaling
    )
    key_part = (
        jnp.einsum("...ts,...td->...sd", grad_low, query_block, preferred_element_type=jnp.float32)
        * scaling
    )
    value_part = jnp.einsum(
        "...ts,...td->...sd", prob_low, grad_block, preferred_element_type=jnp.float32
    )
    temper_part = jnp.sum(score_grad * raw_scores, axis=(-2, -1))
    return (query_part, key_part, value_part, temper_part)


def cluster_pair(
    query_items,
    key_items,
    value_items,
    grad_items,
    live_items,
    temper,
    window_top,
    window_total,
    window_mass,
):
    item_count, block_len, depth = query_items.shape
    row_count = item_count * block_len
    group_rows = 4 * block_len
    inverse_root = 1.0 / math.sqrt(depth)
    scaling = temper * inverse_root
    query_rows = query_items.reshape(row_count, depth)
    key_rows = key_items.reshape(row_count, depth)
    value_rows = value_items.reshape(row_count, depth)
    grad_rows = grad_items.reshape(row_count, depth)
    key_item = jnp.arange(row_count) // block_len
    key_token = jnp.arange(row_count) % block_len
    live_rows = jnp.repeat(live_items, block_len)
    top_rows = window_top.reshape(row_count)
    total_rows = window_total.reshape(row_count)
    mass_rows = window_mass.reshape(row_count)

    def group_step(carry, start_row):
        key_acc, value_acc, temper_acc = carry
        query_group = lax.dynamic_slice_in_dim(query_rows, start_row, group_rows, 0)
        grad_group = lax.dynamic_slice_in_dim(grad_rows, start_row, group_rows, 0)
        group_live = lax.dynamic_slice_in_dim(live_rows, start_row, group_rows, 0)
        group_top = lax.dynamic_slice_in_dim(top_rows, start_row, group_rows, 0)
        group_total = lax.dynamic_slice_in_dim(total_rows, start_row, group_rows, 0)
        group_mass = lax.dynamic_slice_in_dim(mass_rows, start_row, group_rows, 0)
        query_item = (start_row + jnp.arange(group_rows)) // block_len
        query_token = jnp.arange(group_rows) % block_len
        earlier = (key_item[None, :] < query_item[:, None]) | (
            key_item[None, :] == query_item[:, None]
        ) & (key_token[None, :] <= query_token[:, None])
        pair_mask = group_live[:, None] & live_rows[None, :] & earlier
        raw_scores = (
            lax.dot_general(
                query_group, key_rows, (((1,), (1,)), ((), ())), preferred_element_type=jnp.float32
            )
            * inverse_root
        )
        scores = temper * raw_scores
        row_top = jnp.maximum(
            jnp.max(jnp.where(pair_mask, scores, blocked_score), axis=1), group_top
        )
        weights = jnp.where(pair_mask, jnp.exp(scores - row_top[:, None]), 0.0)
        row_total = jnp.sum(weights, axis=1) + group_total * jnp.exp(group_top - row_top)
        log_total = row_top + jnp.log(jnp.where(group_live, row_total, 1.0))
        probability = jnp.where(pair_mask, jnp.exp(scores - log_total[:, None]), 0.0)
        prob_grad = lax.dot_general(
            grad_group, value_rows, (((1,), (1,)), ((), ())), preferred_element_type=jnp.float32
        )
        row_delta = jnp.sum(probability * prob_grad, axis=1) + group_mass * jnp.exp(
            group_top - log_total
        )
        score_grad = probability * (prob_grad - row_delta[:, None])
        prob_low = probability.astype(jnp.bfloat16)
        grad_low = score_grad.astype(jnp.bfloat16)
        query_part = jnp.dot(grad_low, key_rows, preferred_element_type=jnp.float32) * scaling
        key_acc = (
            key_acc
            + lax.dot_general(
                grad_low, query_group, (((0,), (0,)), ((), ())), preferred_element_type=jnp.float32
            )
            * scaling
        )
        value_acc = value_acc + lax.dot_general(
            prob_low, grad_group, (((0,), (0,)), ((), ())), preferred_element_type=jnp.float32
        )
        temper_acc = temper_acc + jnp.sum(score_grad * raw_scores)
        return ((key_acc, value_acc, temper_acc), (query_part, log_total, row_delta))

    start_rows = jnp.arange(item_count // 4) * group_rows
    initial = (
        jnp.zeros((row_count, depth), jnp.float32),
        jnp.zeros((row_count, depth), jnp.float32),
        jnp.zeros((), jnp.float32),
    )
    (key_acc, value_acc, temper_acc), (query_part, log_total, row_delta) = lax.scan(
        group_step, initial, start_rows
    )
    return (
        query_part.reshape(item_count, block_len, depth),
        log_total.reshape(item_count, block_len),
        row_delta.reshape(item_count, block_len),
        key_acc.reshape(item_count, block_len, depth),
        value_acc.reshape(item_count, block_len, depth),
        temper_acc,
    )


def clustered_shards(
    probe_vectors,
    lookup_vectors,
    content_vectors,
    result_cotangent,
    logit_softness,
    block_grouping,
    neighborhood_span,
):
    seq_count = lax.axis_size("seq")
    position = lax.axis_index("seq")
    tokens = probe_vectors.shape[1]
    head_count = probe_vectors.shape[2] // HD
    local_blocks = tokens // BLK
    block_count = local_blocks * seq_count
    cluster_count = max(1, block_count // 8)
    capacity = min(12, block_count)
    owned_pairs = cluster_count * head_count // seq_count
    group_count = cluster_count // owned_pairs
    per_peer = max(1, local_blocks // group_count)
    cluster_ids = block_grouping[0, :, :, 0]
    query_home = head_major(probe_vectors[0], BLK)
    key_home = head_major(lookup_vectors[0], BLK)
    value_home = head_major(content_vectors[0], BLK)
    grad_home = head_major(result_cotangent[0], BLK)
    last_block = (lookup_vectors[0, tokens - BLK :], content_vectors[0, tokens - BLK :])
    prev_key_rows, prev_value_rows = shifted((last_block[0], last_block[1]), "seq", 1)
    prev_keys = jnp.concatenate([head_major(prev_key_rows, BLK), key_home[:, :-1]], axis=1)
    prev_values = jnp.concatenate([head_major(prev_value_rows, BLK), value_home[:, :-1]], axis=1)
    first_block = position * local_blocks
    before = jnp.concatenate(
        [jnp.full((head_count, 1), -1, jnp.int32), cluster_ids[:, :-1]], axis=1
    )
    my_ids = lax.dynamic_slice_in_dim(cluster_ids, first_block, local_blocks, 1)
    my_before = lax.dynamic_slice_in_dim(before, first_block, local_blocks, 1)
    global_block = first_block + jnp.arange(local_blocks)
    usable_home = (global_block[None, :] >= 1) & (my_before != my_ids)
    peer_index = jnp.arange(seq_count)
    peer_head = peer_index * owned_pairs // cluster_count
    slot_range = jnp.arange(per_peer)
    local_range = jnp.arange(local_blocks)
    owner_index = (jnp.arange(head_count)[:, None] * cluster_count + my_ids) // owned_pairs
    peer_ids = jnp.take(my_ids, peer_head, axis=0)
    goes = (peer_head[:, None] * cluster_count + peer_ids) // owned_pairs == peer_index[:, None]
    send_rank = jnp.cumsum(goes.astype(jnp.int32), axis=1) - 1
    send_pick = goes[:, None, :] & (send_rank[:, None, :] == slot_range[None, :, None])
    send_block = jnp.sum(jnp.where(send_pick, local_range[None, None, :], 0), axis=2)
    send_flat = peer_head[:, None] * local_blocks + send_block
    home_rank = jnp.take_along_axis(send_rank, owner_index, axis=0)
    home_pos = owner_index * per_peer + home_rank
    pair_index = position * owned_pairs + jnp.arange(owned_pairs)
    split_for_couple = pair_index // cluster_count
    pair_cluster = pair_index % cluster_count
    my_head = position * owned_pairs // cluster_count
    split_numbers = jnp.take(cluster_ids, my_head, axis=0)
    member = split_numbers[None, :] == pair_cluster[:, None]
    member_rank = jnp.cumsum(member.astype(jnp.int32), axis=1) - 1
    member_count = jnp.sum(member.astype(jnp.int32), axis=1)
    picked = member[:, None, :] & (member_rank[:, None, :] == jnp.arange(capacity)[None, :, None])
    member_block = jnp.sum(jnp.where(picked, jnp.arange(block_count)[None, None, :], 0), axis=2)
    live_members = jnp.arange(capacity)[None, :] < member_count[:, None]
    mine = (my_head * cluster_count + split_numbers) // owned_pairs == position
    mine_grid = mine.reshape(seq_count, local_blocks)
    recv_rank = jnp.cumsum(mine_grid.astype(jnp.int32), axis=1) - 1
    recv_pos = (peer_index[:, None] * per_peer + recv_rank).reshape(block_count)
    member_pos = jnp.take(recv_pos, member_block)
    couple_softness = jnp.take(logit_softness, split_for_couple)
    pair_onehot = (split_for_couple[:, None] == jnp.arange(head_count)[None, :]).astype(jnp.float32)
    slot_pair = my_head * cluster_count + split_numbers - position * owned_pairs
    same_cluster = split_numbers[:, None] == split_numbers[None, :]
    earlier_block = jnp.arange(block_count)[None, :] < jnp.arange(block_count)[:, None]
    slot_rank = jnp.sum((same_cluster & earlier_block).astype(jnp.int32), axis=1)
    back_pos = jnp.clip(slot_pair, 0, owned_pairs - 1) * capacity + jnp.clip(
        slot_rank, 0, capacity - 1
    )
    back_grid = back_pos.reshape(seq_count, local_blocks)
    back_pick = mine_grid[:, None, :] & (recv_rank[:, None, :] == slot_range[None, :, None])
    back_flat = jnp.sum(jnp.where(back_pick, back_grid[:, None, :], 0), axis=2)

    def to_peers(array_in):
        flat = array_in.reshape((head_count * local_blocks,) + array_in.shape[2:])
        return jnp.take(flat, send_flat, axis=0)

    def members(array_in):
        flat = array_in.reshape((seq_count * per_peer,) + array_in.shape[2:])
        return jnp.take(flat, member_pos, axis=0)

    def to_owner(array_in):
        flat = array_in.reshape((owned_pairs * capacity,) + array_in.shape[2:])
        return jnp.take(flat, back_flat, axis=0)

    def from_peers(array_in):
        flat = array_in.reshape((seq_count * per_peer,) + array_in.shape[2:])
        return jnp.take(flat, home_pos, axis=0)

    raw_w, mask_w, pgrad_w, top_w, total_w, mass_w = window_parts(
        query_home,
        prev_keys,
        prev_values,
        grad_home,
        usable_home,
        neighborhood_span[:, None],
        logit_softness[:, None],
    )
    arrived = (
        lax.all_to_all(to_peers(query_home), "seq", split_axis=0, concat_axis=0, tiled=True),
        lax.all_to_all(to_peers(key_home), "seq", split_axis=0, concat_axis=0, tiled=True),
        lax.all_to_all(to_peers(value_home), "seq", split_axis=0, concat_axis=0, tiled=True),
        lax.all_to_all(to_peers(grad_home), "seq", split_axis=0, concat_axis=0, tiled=True),
    )
    arrived_stats = (
        lax.all_to_all(to_peers(top_w), "seq", split_axis=0, concat_axis=0, tiled=True),
        lax.all_to_all(to_peers(total_w), "seq", split_axis=0, concat_axis=0, tiled=True),
        lax.all_to_all(to_peers(mass_w), "seq", split_axis=0, concat_axis=0, tiled=True),
    )
    query_m, key_m, value_m, grad_m = [members(item_in) for item_in in arrived]
    top_m, total_m, mass_m = [members(item_in) for item_in in arrived_stats]

    def split_pair(pair_inputs):
        query_i, key_i, value_i, grad_i, live_i, temper_i, top_i, total_i, mass_i = pair_inputs
        query_c, log_total, row_delta, key_c, value_c, temper_c = cluster_pair(
            query_i, key_i, value_i, grad_i, live_i, temper_i, top_i, total_i, mass_i
        )
        return (
            query_c.astype(jnp.bfloat16),
            key_c.astype(jnp.bfloat16),
            value_c.astype(jnp.bfloat16),
            log_total,
            row_delta,
            temper_c,
        )

    owner_results = lax.map(
        split_pair,
        (query_m, key_m, value_m, grad_m, live_members, couple_softness, top_m, total_m, mass_m),
    )
    returned = (
        lax.all_to_all(to_owner(owner_results[0]), "seq", split_axis=0, concat_axis=0, tiled=True),
        lax.all_to_all(to_owner(owner_results[1]), "seq", split_axis=0, concat_axis=0, tiled=True),
        lax.all_to_all(to_owner(owner_results[2]), "seq", split_axis=0, concat_axis=0, tiled=True),
    )
    returned_stats = (
        lax.all_to_all(to_owner(owner_results[3]), "seq", split_axis=0, concat_axis=0, tiled=True),
        lax.all_to_all(to_owner(owner_results[4]), "seq", split_axis=0, concat_axis=0, tiled=True),
    )
    query_cluster = from_peers(returned[0])
    key_cluster = from_peers(returned[1])
    value_cluster = from_peers(returned[2])
    log_home = from_peers(returned_stats[0])
    delta_home = from_peers(returned_stats[1])
    query_w, key_w, value_w, temper_w = window_grads(
        raw_w,
        mask_w,
        pgrad_w,
        query_home,
        prev_keys,
        grad_home,
        log_home,
        delta_home,
        logit_softness[:, None],
    )
    query_out = (query_cluster.astype(jnp.float32) + lifted(query_w)).astype(jnp.bfloat16)
    key_window = key_w.astype(jnp.bfloat16)
    value_window = value_w.astype(jnp.bfloat16)
    temper_local = jnp.sum(owner_results[5][:, None] * pair_onehot, axis=0) + jnp.sum(
        temper_w, axis=1
    )
    edge_keys, edge_values = shifted((key_window[:, 0], value_window[:, 0]), "seq", -1)
    key_next = jnp.concatenate([key_window[:, 1:], edge_keys[:, None]], axis=1)
    value_next = jnp.concatenate([value_window[:, 1:], edge_values[:, None]], axis=1)
    key_out = (key_cluster.astype(jnp.float32) + key_next.astype(jnp.float32)).astype(jnp.bfloat16)
    value_out = (value_cluster.astype(jnp.float32) + value_next.astype(jnp.float32)).astype(
        jnp.bfloat16
    )
    temper_total = lax.psum(temper_local, ("seq", "dp"))
    temper_grad = temper_total / (lax.axis_size("dp") * tokens * seq_count)
    return (token_major(query_out), token_major(key_out), token_major(value_out), temper_grad)


TILE = 256
EXTRA = 16
MIB = 1024 * 1024
PIECES = 4
QUERY, KEY, VALUE, GRAD = range(4)


def columns_of(index):
    return pl.ds(pl.multiple_of(index * HD, HD), HD)


def rows_of(index):
    return pl.ds(pl.multiple_of(index * BLK, BLK), BLK)


def tile_rows(tile):
    return slice(tile * TILE, (tile + 1) * TILE)


def position(half_count):
    me = lax.axis_index("seq")
    half = jnp.where(me >= half_count, 1, 0)
    return me, half, me - half * half_count


def kernel_call(
    kernel, name, operands, in_specs, out_shape, scratch, vmem_mib, flops=0, out_spaces=None,
    aliases=None,
):
    bytes_accessed = sum(
        math.prod(item.shape) * item.dtype.itemsize for item in (*operands, *out_shape)
    )
    return pl.pallas_call(
        kernel,
        out_shape=out_shape,
        in_specs=in_specs,
        out_specs=[
            pl.BlockSpec(memory_space=space)
            for space in out_spaces or [pltpu.VMEM] * len(out_shape)
        ],
        scratch_shapes=scratch,
        input_output_aliases=aliases or {},
        cost_estimate=pl.CostEstimate(
            flops=flops, bytes_accessed=bytes_accessed, transcendentals=0
        ),
        compiler_params=pltpu.CompilerParams(vmem_limit_bytes=vmem_mib * MIB),
        name=name,
    )(*operands)


def pack_kernel(*refs, half_count):
    arrays, within_ref, foreign_refs = refs[:4], refs[4], refs[5:7]
    held, within, across, arrival, left_within, left_across = refs[7:]
    me, half, _ = position(half_count)
    piece = BLK // PIECES
    arrivals = [
        [
            pltpu.make_async_copy(
                array_ref.at[0, part * piece : (part + 1) * piece, :],
                held.at[place, part * piece : (part + 1) * piece, :],
                arrival.at[place, part],
            )
            for part in range(PIECES)
        ]
        for place, array_ref in enumerate(arrays)
    ]
    for copies in arrivals:
        for copy in copies:
            copy.start()
    leaving = []
    for place, copies in enumerate(arrivals):
        for copy in copies:
            copy.wait()
        for slot, base in enumerate((half * half_count, (1 - half) * half_count)):
            rows = slice((slot * 4 + place) * BLK, (slot * 4 + place + 1) * BLK)
            for peer in range(half_count):
                within[peer, rows, :] = held[place, :, columns_of(base + peer)]
            leaving.append(
                pltpu.make_async_copy(
                    within.at[:, rows, :], within_ref.at[:, rows, :], left_within.at[place, slot]
                )
            )
            leaving[-1].start()
    first = jnp.where(half == 0, KEY, QUERY)
    second = jnp.where(half == 0, VALUE, GRAD)
    for core, foreign_ref in enumerate(foreign_refs):
        for step in range(half_count // 2):
            columns = columns_of(me ^ core ^ (half_count + 2 * step))
            across[core, step, :BLK, :] = held[first, :, columns]
            across[core, step, BLK:, :] = held[second, :, columns]
        leaving.append(pltpu.make_async_copy(across.at[core], foreign_ref, left_across.at[core]))
        leaving[-1].start()
    for copy in leaving:
        copy.wait()


def packed(arrays, half_count):
    width = arrays[0].shape[2]
    within_shape, across_shape = (half_count, 8 * BLK, HD), (half_count // 2, 2 * BLK, HD)
    return kernel_call(
        functools.partial(pack_kernel, half_count=half_count),
        "pack_heads",
        arrays,
        [pl.BlockSpec(memory_space=pl.ANY)] * 4,
        [jax.ShapeDtypeStruct(within_shape, jnp.bfloat16)]
        + [jax.ShapeDtypeStruct(across_shape, jnp.bfloat16)] * 2,
        [
            pltpu.VMEM((4, BLK, width), jnp.bfloat16),
            pltpu.VMEM(within_shape, jnp.bfloat16),
            pltpu.VMEM((2, *across_shape), jnp.bfloat16),
            pltpu.SemaphoreType.DMA((4, PIECES)),
            pltpu.SemaphoreType.DMA((4, 2)),
            pltpu.SemaphoreType.DMA((2,)),
        ],
        60,
        out_spaces=[pl.ANY] * 3,
    )


def dot_rows(left, right):
    return lax.dot_general(
        left, right, (((1,), (1,)), ((), ())), preferred_element_type=jnp.float32
    )


def dot_plain(left, right):
    return lax.dot_general(
        left, right, (((1,), (0,)), ((), ())), preferred_element_type=jnp.float32
    )


def from_blocks(ref, place):
    def rows(start, stop):
        per_tile = TILE // BLK
        return jnp.concatenate(
            [ref[block, place] for block in range(start * per_tile, stop * per_tile)],
            axis=0,
        )

    return rows


def from_array(ref, place):
    return lambda start, stop: ref[place, start * TILE : stop * TILE, :]


class Region:
    def __init__(self, square, sources, tiles, scaling, bias_ref=None, least_ref=None, first=0):
        self.square, self.sources, self.tiles, self.scaling = square, sources, tiles, scaling
        self.bias_ref, self.least_ref, self.first = bias_ref, least_ref, first

    def rows(self, which, start, stop):
        return self.sources[which](start, stop)

    def scale_of(self, array):
        return 1.0 if array == VALUE else self.scaling[:, :HD]

    def keys_of(self, tile):
        return range(self.tiles if self.square else tile + 1)

    def scores(self, tile_key, tile_query):
        per_tile = TILE // BLK
        scores = dot_rows(
            self.rows(KEY, tile_key, tile_key + 1), self.rows(QUERY, tile_query, tile_query + 1)
        ) * (self.scaling * math.log2(math.e))
        before = self.tiles * per_tile if self.square else 0
        rows = []
        for sub_key in range(per_tile):
            key_block = tile_key * per_tile + sub_key
            pieces = []
            for sub_query in range(per_tile):
                query_block = tile_query * per_tile + sub_query
                lanes = slice(sub_query * BLK, (sub_query + 1) * BLK)
                piece = scores[sub_key * BLK : (sub_key + 1) * BLK, lanes]
                apart = before + query_block - key_block
                if apart < 0:
                    piece = jnp.full_like(piece, blocked_score)
                elif apart == 0:
                    piece = jnp.where(key_minus_query() <= 0, piece, blocked_score)
                elif apart == 1:
                    row = self.first + (0 if self.square else key_block)
                    least = self.least_ref[row : row + 1, :]
                    piece = jnp.where(key_minus_query() > least, piece, blocked_score)
                else:
                    at = slice(query_block * BLK, (query_block + 1) * BLK)
                    piece = piece + self.bias_ref[key_block : key_block + 1, at]
                pieces.append(piece)
            rows.append(jnp.concatenate(pieces, axis=1))
        return jnp.concatenate(rows, axis=0)


def diagonal(slot, arrived_ref, scales_ref, bias_ref=None, least_ref=None):
    blocks = arrived_ref.shape[0]
    sources = [from_blocks(arrived_ref, slot * 4 + place) for place in range(4)]
    bias = None if bias_ref is None else bias_ref.at[slot]
    first = slot * (blocks - 1)
    scaling = scales_ref[slot : slot + 1, :]
    return Region(False, sources, blocks * BLK // TILE, scaling, bias, least_ref, first)


def square(square_ref, scales_ref, bias_ref=None, least_ref=None):
    tiles = square_ref.shape[1] // TILE
    sources = [from_array(square_ref, place) for place in range(4)]
    bias = None if bias_ref is None else bias_ref.at[2]
    first = 2 * (tiles * TILE // BLK - 1)
    return Region(True, sources, tiles, scales_ref[0:1, :], bias, least_ref, first)


def key_minus_query():
    shape = (BLK, BLK)
    return lax.broadcasted_iota(jnp.int32, shape, 0) - lax.broadcasted_iota(jnp.int32, shape, 1)


def statistics(region, weight_ref, towards_ref, out_ref, first_row):
    for tile in range(region.tiles):
        here = tile_rows(tile)
        top = jnp.full((1, TILE), blocked_score, jnp.float32)
        for other in region.keys_of(tile):
            raw = region.scores(other, tile)
            weight_ref[tile_rows(other), here] = raw
            top = jnp.maximum(top, jnp.max(raw, axis=0, keepdims=True))
        sums = [jnp.zeros((1, TILE), jnp.float32)] * 4
        for other in region.keys_of(tile):
            there = tile_rows(other)
            raw = weight_ref[there, here]
            weight = jnp.exp2(raw - top)
            towards = dot_rows(
                region.rows(VALUE, other, other + 1), region.rows(GRAD, tile, tile + 1)
            )
            weight_ref[there, here] = weight
            towards_ref[there, here] = towards
            pulled, weighted = weight * towards, weight * raw
            terms = (weight, pulled, pulled * raw, weighted)
            sums = [
                total + jnp.sum(term, axis=0, keepdims=True) for total, term in zip(sums, terms)
            ]
        for row, value in enumerate((top, *sums)):
            out_ref[first_row + row : first_row + row + 1, here] = value


def gradients(
    region, weight_ref, towards_ref, top, log_total, delta, prob_low, grad_low, keys_flat, emit=None
):
    keys_flat[...] = region.rows(KEY, 0, region.tiles).T
    share = jnp.exp2(top - log_total)
    query_parts, key_parts, value_parts = [], [], []
    for tile in range(region.tiles):
        here = tile_rows(tile)
        for other in region.keys_of(tile):
            there = tile_rows(other)
            probability = weight_ref[there, here] * share[:, here]
            prob_low[there, here] = probability.astype(jnp.bfloat16)
            grad_low[there, here] = (
                probability * (towards_ref[there, here] - delta[:, here])
            ).astype(jnp.bfloat16)
        upto = slice(0, len(region.keys_of(tile)) * TILE)
        query_parts.append(dot_plain(keys_flat[:, upto], grad_low[upto, here]).T)
    if emit is not None:
        emit(QUERY, query_parts)
    for low, which, parts in ((grad_low, QUERY, key_parts), (prob_low, GRAD, value_parts)):
        for tile in range(region.tiles):
            first = 0 if region.square else tile
            onward = slice(first * TILE, region.tiles * TILE)
            parts.append(
                dot_plain(low[tile_rows(tile), onward], region.rows(which, first, region.tiles))
            )
        if emit is not None:
            emit(KEY if which == QUERY else VALUE, parts)
    return query_parts, key_parts, value_parts


def merged(first, second):
    top = jnp.maximum(first[0], second[0])
    left, right = jnp.exp2(first[0] - top), jnp.exp2(second[0] - top)
    total = first[1] * left + second[1] * right
    mass = first[2] * left + second[2] * right
    return top + jnp.log2(total), mass / total


def alone(rows):
    return rows[0] + jnp.log2(rows[1]), rows[2] / rows[1]


def rows_at(ref, first, count=5):
    return [ref[first + row : first + row + 1, :] for row in range(count)]


def temper_terms(rows, totals, scale_row):
    log_total, delta = totals
    terms = (rows[3] - delta * rows[4]) * jnp.exp2(rows[0] - log_total)
    folded = sum(terms[:, start : start + HD] for start in range(0, terms.shape[1], HD))
    return folded / (scale_row[:, :HD] * (math.sqrt(HD) * math.log2(math.e)))


def put(within_ref, array, tile, value):
    per_tile = TILE // BLK
    for sub in range(per_tile):
        within_ref[tile * per_tile + sub, array * BLK : (array + 1) * BLK, :] = value[
            sub * BLK : (sub + 1) * BLK, :
        ].astype(jnp.bfloat16)


def scaled(region, parts):
    scale = region.scaling[:, :HD]
    return [[value * scale for value in part] for part in parts[:2]] + [parts[2]]


def masks_kernel(softness_ref, ids_ref, span_ref, scales_ref, bias_ref, least_ref, *, half_count):
    me, half, _ = position(half_count)
    base = half * half_count
    regions = (
        (me, base, base),
        (me ^ half_count, base, base),
        (me, 0, half_count),
    )
    for slot, (head, key_base, query_base) in enumerate(regions):
        if slot < 2:
            scales_ref[slot : slot + 1, :] = jnp.full(
                (1, TILE), softness_ref[head] * (1.0 / math.sqrt(HD)), jnp.float32
            )

        def same(key_block, query_block):
            return ids_ref[head, key_base + key_block] == ids_ref[head, query_base + query_block]

        def bias(key_block, query_block):
            return jnp.full(
                (1, BLK), jnp.where(same(key_block, query_block), 0.0, blocked_score), jnp.float32
            )

        for key_block in range(half_count):
            bias_ref[slot, key_block : key_block + 1, :] = jnp.concatenate(
                [bias(key_block, query_block) for query_block in range(half_count)], axis=1
            )
        pairs = [(block, block + 1) for block in range(half_count - 1)]
        if slot == 2:
            pairs = [(half_count - 1, 0)]
        for place, pair in enumerate(pairs):
            least = jnp.where(same(*pair), -BLK, BLK - span_ref[head])
            row = slot * (half_count - 1) + place
            least_ref[row : row + 1, :] = jnp.full((1, BLK), least, jnp.int32)


def within_kernel(
    arrived_ref, scales_ref, bias_ref, least_ref, stats_ref, parts_ref, own_weight, own_towards, other_weight, other_towards, *scratch, half_count
):
    _, half, _ = position(half_count)
    kept = ((own_weight, own_towards), (other_weight, other_towards))
    for slot in range(2):
        region = diagonal(slot, arrived_ref, scales_ref, bias_ref, least_ref)
        statistics(region, *kept[slot], stats_ref, slot * 5)

    @pl.when(half == 0)
    def _():
        region = diagonal(0, arrived_ref, scales_ref)
        single = alone(rows_at(stats_ref, 0))
        parts = gradients(region, *kept[0], stats_ref[0:1, :], *single, *scratch)
        for place, tiles in enumerate(scaled(region, parts)):
            for tile, value in enumerate(tiles):
                parts_ref[place, tile_rows(tile), :] = value


def square_kernel(arrived_ref, scales_ref, bias_ref, least_ref, stats_ref, *refs, half_count):
    across_refs = refs[: half_count // 2]
    square_ref, message_ref, square_stats, weight, towards = refs[half_count // 2 :]
    _, half, place = position(half_count)
    first = jnp.where(half == 0, QUERY, KEY)
    second = jnp.where(half == 0, GRAD, VALUE)
    for step, across_ref in enumerate(across_refs):
        for core in range(2):
            rows = rows_of(place ^ core ^ (2 * step))
            square_ref[first, rows, :] = across_ref[core, :BLK, :]
            square_ref[second, rows, :] = across_ref[core, BLK:, :]
    for kept in (jnp.where(half == 0, KEY, QUERY), jnp.where(half == 0, VALUE, GRAD)):
        for block in range(half_count):
            square_ref[kept, block * BLK : (block + 1) * BLK, :] = arrived_ref[block, kept]
    region = square(square_ref, scales_ref, bias_ref, least_ref)
    statistics(region, weight, towards, square_stats, 0)
    own, other, crossing = rows_at(stats_ref, 0), rows_at(stats_ref, 5), rows_at(square_stats, 0)
    for row in range(5):
        message_ref[row : row + 1, :] = jnp.where(half == 0, crossing[row], other[row])
    own_scale, other_scale = scales_ref[0:1, :], scales_ref[1:2, :]
    both = merged(own, crossing)
    whole = temper_terms(own, both, own_scale) + temper_terms(crossing, both, own_scale)
    single = temper_terms(own, alone(own), own_scale)
    message_ref[5:6, :HD] = jnp.where(half == 0, single, whole)
    message_ref[6:7, :HD] = temper_terms(other, alone(other), other_scale)


def first_kernel(
    arrived_ref, scales_ref, square_ref, stats_ref, square_stats,
    own_weight, own_towards, other_weight, other_towards, square_weight, square_towards,
    across_ref, within_ref, ready, ready_sem, *scratch, half_count
):
    _, half, _ = position(half_count)
    leaving = sends(ready, within_ref, ready_sem, (1 - half) * 3)

    @pl.when(half == 0)
    def _():
        region = diagonal(1, arrived_ref, scales_ref)

        def send(array, parts):
            for tile, part in enumerate(parts):
                put(ready, array, tile, part * region.scale_of(array))
            leaving[array].start()

        totals = alone(rows_at(stats_ref, 5))
        gradients(
            region, other_weight, other_towards, stats_ref[5:6, :], *totals, *scratch, emit=send
        )

    @pl.when(half == 1)
    def _():
        totals = merged(rows_at(stats_ref, 0), rows_at(square_stats, 0))
        region = square(square_ref, scales_ref)
        parts = gradients(
            region, square_weight, square_towards, square_stats[0:1, :], *totals, *scratch
        )
        across_query, *foreign = scaled(region, parts)
        for array, tiles in enumerate(foreign):
            for tile, value in enumerate(tiles):
                across_ref[array, tile_rows(tile), :] = value.astype(jnp.bfloat16)
        region = diagonal(0, arrived_ref, scales_ref)

        def send(array, parts):
            for tile, part in enumerate(parts):
                value = part * region.scale_of(array)
                put(ready, array, tile, value + across_query[tile] if array == QUERY else value)
            leaving[array].start()

        gradients(
            region, own_weight, own_towards, stats_ref[0:1, :], *totals, *scratch, emit=send
        )

    for copy in leaving:
        copy.wait()


def sends(ready, within_ref, sems, first):
    copies = []
    for array in range(3):
        rows = slice(array * BLK, (array + 1) * BLK)
        copies.append(
            pltpu.make_async_copy(
                ready.at[:, rows, :], within_ref.at[:, rows_of(first + array), :], sems.at[array]
            )
        )
    return copies


def temper_rows(own, other):
    row = lax.broadcasted_iota(jnp.int32, (EXTRA, HD), 0)
    rows = jnp.zeros((EXTRA, HD), jnp.float32)
    for place, terms in enumerate((own, other)):
        rest = jnp.broadcast_to(jnp.sum(terms, axis=1, keepdims=True), (EXTRA, HD))
        for piece in range(3):
            high = rest.astype(jnp.bfloat16).astype(jnp.float32)
            rows = jnp.where(row == place * 3 + piece, high, rows)
            rest = rest - high
    return rows.astype(jnp.bfloat16)


def finish_kernel(
    arrived_ref, scales_ref, square_ref, message_ref, received_ref, stats_ref, square_stats,
    parts_ref, square_weight, square_towards, other_weight, other_towards, across_ref, begun_ref,
    within_ref, *refs, half_count
):
    del begun_ref
    chunk_refs = refs[:2]
    across, ready, tail, ready_sem, tail_sem, *scratch = refs[2:]
    _, half, place = position(half_count)
    leaving = sends(ready, within_ref, ready_sem, half * 3)
    sent, came = rows_at(message_ref, 0), rows_at(received_ref, 0)
    totals = merged(sent, came)
    scale = jnp.where(half == 0, scales_ref[0:1, :], scales_ref[1:2, :])
    shared = temper_terms(sent, totals, scale) + temper_terms(came, totals, scale)
    mine, theirs = message_ref[5:6, :HD], received_ref[5:6, :HD]
    own = mine + jnp.where(half == 0, shared, received_ref[6:7, :HD])
    other = theirs + jnp.where(half == 0, message_ref[6:7, :HD], shared)
    pieces = temper_rows(own, other)
    for block in range(half_count):
        tail[block] = pieces
    leaving.append(
        pltpu.make_async_copy(tail, within_ref.at[:, 6 * BLK : 6 * BLK + EXTRA, :], tail_sem)
    )
    leaving[-1].start()

    def chunks():
        for core, chunk_ref in enumerate(chunk_refs):
            for step in range(half_count // 2):
                yield step, chunk_ref, rows_of(place ^ core ^ (2 * step))

    @pl.when(half == 0)
    def _():
        region = square(square_ref, scales_ref)

        def send(array, parts):
            for tile, part in enumerate(parts):
                here = tile_rows(tile)
                value = part * region.scale_of(array)
                if array == QUERY:
                    across[here, :] = value.astype(jnp.bfloat16)
                    put(ready, array, tile, parts_ref[array, here, :])
                else:
                    put(ready, array, tile, parts_ref[array, here, :] + value)
            leaving[array].start()

        gradients(
            region, square_weight, square_towards, square_stats[0:1, :], *totals, *scratch, emit=send
        )
        for step, chunk_ref, rows in chunks():
            chunk_ref[step, :BLK, :] = across[rows, :]
            chunk_ref[step, BLK:, :] = jnp.zeros((BLK, HD), jnp.bfloat16)

    @pl.when(half == 1)
    def _():
        region = diagonal(1, arrived_ref, scales_ref)

        def send(array, parts):
            for tile, part in enumerate(parts):
                put(ready, array, tile, part * region.scale_of(array))
            leaving[array].start()

        gradients(
            region, other_weight, other_towards, stats_ref[5:6, :], *totals, *scratch, emit=send
        )
        for step, chunk_ref, rows in chunks():
            chunk_ref[step, :BLK, :] = across_ref[0, rows, :]
            chunk_ref[step, BLK:, :] = across_ref[1, rows, :]

    for copy in leaving:
        copy.wait()


def temper_kernel(within_ref, temper_ref, *, half_count):
    _, half, _ = position(half_count)
    for peer in range(half_count):
        for slot, base in enumerate((half * half_count, (1 - half) * half_count)):
            rows = within_ref[peer, 3 * slot : 3 * slot + 3, :].astype(jnp.float32)
            temper_ref[pl.ds(base + peer, 1), :] = jnp.sum(rows, axis=0, keepdims=True)


def temper_sums(within, half_count):
    last = 6 * BLK // EXTRA
    return pl.pallas_call(
        functools.partial(temper_kernel, half_count=half_count),
        grid=(1,),
        out_shape=jax.ShapeDtypeStruct((2 * half_count, HD), jnp.float32),
        in_specs=[pl.BlockSpec((half_count, EXTRA, HD), lambda step: (0, last, 0))],
        out_specs=pl.BlockSpec((2 * half_count, HD), lambda step: (0, 0)),
        compiler_params=pltpu.CompilerParams(vmem_limit_bytes=4 * MIB),
        name="temper_sums",
    )(within)


def own_columns_kernel(within_ref, *refs, half_count):
    out_refs, (staged, sems) = refs[:3], refs[3:]
    _, half, _ = position(half_count)
    width = half_count * HD
    for array in range(6):
        for peer in range(half_count):
            staged[array, :, peer * HD : (peer + 1) * HD] = within_ref[
                peer, array * BLK : (array + 1) * BLK, :
            ]

    def copies(arrays):
        return [
            pltpu.make_async_copy(
                staged.at[array],
                out_refs[array % 3].at[0, :, side(half if array < 3 else 1 - half, width)],
                sems.at[array],
            )
            for array in arrays
        ]

    for role, arrays in enumerate(((0, 1, 2, 3), (0, 1, 2, 4, 5))):

        @pl.when(half == role)
        def _():
            leaving = copies(arrays)
            for copy in leaving:
                copy.start()
            for copy in leaving:
                copy.wait()


def side(half, width):
    return pl.ds(pl.multiple_of(half * width, width), width)


def other_columns_kernel(within_ref, *refs, half_count):
    messages = half_count // 2
    across_refs = refs[:messages]
    out_refs, (staged, sems) = refs[messages + 3 : messages + 6], refs[messages + 6 :]
    _, half, place = position(half_count)

    for role, arrays in enumerate(((1, 2), (0,))):

        @pl.when(half == role)
        def _():
            leaving = []
            for step, across_ref in enumerate(across_refs):
                pair = (place ^ (2 * step)) >> 1
                for part, array in enumerate(arrays):
                    rows = slice(part * BLK, (part + 1) * BLK)
                    for core in range(2):
                        peer = place ^ core ^ (2 * step)
                        kept = within_ref[peer, (3 + array) * BLK : (4 + array) * BLK, :]
                        total = kept.astype(jnp.float32) + across_ref[core, rows, :].astype(
                            jnp.float32
                        )
                        staged[part, :, columns_of(peer)] = total.astype(jnp.bfloat16)
                    start = (1 - role) * messages + pair
                    leaving.append(
                        pltpu.make_async_copy(
                            staged.at[part, :, side(pair, 2 * HD)],
                            out_refs[array].at[0, :, side(start, 2 * HD)],
                            sems.at[step, part],
                        )
                    )
                    leaving[-1].start()
            for copy in leaving:
                copy.wait()


def join_kernel(kept_ref, taken_ref, *out_refs):
    for step, out_ref in enumerate(out_refs):
        out_ref[0] = kept_ref[step]
        out_ref[1] = taken_ref[step]


def crossed(kept, given, half_count):
    devices = range(2 * half_count)
    steps, *shape = kept.shape
    taken = lax.ppermute(given, "seq", [(source, source ^ 1) for source in devices])
    messages = kernel_call(
        join_kernel,
        "join_chunks",
        (kept, taken),
        [pl.BlockSpec(memory_space=pltpu.VMEM)] * 2,
        [jax.ShapeDtypeStruct((2, *shape), jnp.bfloat16)] * steps,
        [],
        4,
    )
    received = {}
    for step in reversed(range(steps)):
        pairs = [(source, source ^ (half_count + 2 * step)) for source in devices]
        received[step] = lax.ppermute(messages[step], "seq", pairs)
    return [received[step] for step in range(steps)]


def head_shards(
    probe_vectors,
    lookup_vectors,
    content_vectors,
    result_cotangent,
    logit_softness,
    block_grouping,
    neighborhood_span,
):
    seq_count, dp_count = lax.axis_size("seq"), lax.axis_size("dp")
    half_count = seq_count // 2
    tokens = half_count * BLK
    groups = [list(range(half_count)), list(range(half_count, seq_count))]
    settings = (logit_softness, block_grouping[0, :, :, 0], neighborhood_span)
    smem, vmem = pl.BlockSpec(memory_space=pltpu.SMEM), pl.BlockSpec(memory_space=pltpu.VMEM)
    lows = [pltpu.VMEM((tokens, tokens), jnp.bfloat16)] * 2 + [
        pltpu.VMEM((HD, tokens), jnp.bfloat16)
    ]
    rows_of_stats = jax.ShapeDtypeStruct((8, tokens), jnp.float32)
    pairs = jax.ShapeDtypeStruct((tokens, tokens), jnp.float32)
    pair_flops = 2 * tokens * tokens * HD

    def exchange_within(array_in):
        return lax.all_to_all(
            array_in, "seq", split_axis=0, concat_axis=0, axis_index_groups=groups, tiled=True
        )

    def call(
        kernel, name, operands, out_shape, scratch, flops, vmem_mib, scalars=(), out_spaces=None,
        last_in_place=False,
    ):
        in_specs = [smem] * len(scalars) + [vmem] * len(operands)
        if last_in_place:
            in_specs[-1] = pl.BlockSpec(memory_space=pl.ANY)
        return kernel_call(
            functools.partial(kernel, half_count=half_count),
            name,
            (*scalars, *operands),
            in_specs,
            out_shape,
            scratch,
            vmem_mib,
            flops,
            out_spaces,
            {len(operands) - 1: 0} if last_in_place else {},
        )

    sent, *foreign = packed(
        (probe_vectors, lookup_vectors, content_vectors, result_cotangent), half_count
    )
    arrived = exchange_within(sent).reshape(half_count, 8, BLK, HD)
    kept_parts = jax.ShapeDtypeStruct((3, tokens, HD), jnp.float32)
    masks = call(
        masks_kernel,
        "scales_and_masks",
        (),
        [
            jax.ShapeDtypeStruct((8, TILE), jnp.float32),
            jax.ShapeDtypeStruct((3, half_count, tokens), jnp.float32),
            jax.ShapeDtypeStruct((2 * half_count, BLK), jnp.int32),
        ],
        [],
        0,
        2,
        settings,
    )
    foreign[0], *masks = lax.optimization_barrier((foreign[0], *masks))
    foreign = crossed(*foreign, half_count)
    scales = masks[0]
    stats, parts, own_weight, own_towards, other_weight, other_towards = call(
        within_kernel,
        "diagonal_statistics",
        (arrived, *masks),
        [jax.ShapeDtypeStruct((16, tokens), jnp.float32), kept_parts] + [pairs] * 4,
        lows,
        2 * pair_flops,
        14,
    )
    squared, message, square_stats, square_weight, square_towards = call(
        square_kernel,
        "square_statistics",
        (arrived, *masks, stats, *foreign),
        [jax.ShapeDtypeStruct((4, tokens, HD), jnp.bfloat16)] + [rows_of_stats] * 2 + [pairs] * 2,
        [],
        2 * pair_flops,
        8,
    )
    swap = [(source, source ^ half_count) for source in range(seq_count)]
    received = lax.ppermute(message, "seq", swap)
    result = pltpu.HBM((half_count, 6 * BLK + EXTRA, HD), jnp.bfloat16)
    ready = pltpu.VMEM((half_count, 3 * BLK, HD), jnp.bfloat16)
    across, begun = call(
        first_kernel,
        "gradients_before_totals",
        (
            arrived, scales, squared, stats, square_stats, own_weight, own_towards,
            other_weight, other_towards, square_weight, square_towards,
        ),
        [jax.ShapeDtypeStruct((2, tokens, HD), jnp.bfloat16), result],
        [ready, pltpu.SemaphoreType.DMA((3,)), *lows],
        4 * pair_flops,
        14,
        out_spaces=(pltpu.VMEM, pl.ANY),
    )
    operands = (
        arrived, scales, squared, message, received, stats, square_stats, parts,
        square_weight, square_towards, other_weight, other_towards, across, begun,
    )
    within, *foreign = call(
        finish_kernel,
        "gradients_after_totals",
        operands,
        [result]
        + [jax.ShapeDtypeStruct((half_count // 2, 2 * BLK, HD), jnp.bfloat16)] * 2,
        [
            pltpu.VMEM((tokens, HD), jnp.bfloat16), ready,
            pltpu.VMEM((half_count, EXTRA, HD), jnp.bfloat16),
            pltpu.SemaphoreType.DMA((3,)), pltpu.SemaphoreType.DMA, *lows,
        ],
        2 * pair_flops,
        16,
        out_spaces=(pl.ANY, pltpu.VMEM, pltpu.VMEM),
        last_in_place=True,
    )
    across = crossed(*foreign, half_count)
    within = exchange_within(within)
    tempers = temper_sums(within, half_count)
    temper_total = tempers
    for step in range(1, dp_count):
        swap = [(source, (source + step) % dp_count) for source in range(dp_count)]
        temper_total = temper_total + lax.ppermute(tempers, "dp", swap)
    temper = temper_total[:, 0] / (dp_count * BLK * seq_count)
    result = [pltpu.HBM(probe_vectors.shape, jnp.bfloat16)] * 3
    width = half_count * HD
    outs = kernel_call(
        functools.partial(own_columns_kernel, half_count=half_count),
        "unpack_own",
        (within,),
        [vmem],
        result,
        [pltpu.VMEM((6, BLK, width), jnp.bfloat16), pltpu.SemaphoreType.DMA((6,))],
        6,
        out_spaces=[pl.ANY] * 3,
    )
    across[0], temper = lax.optimization_barrier((across[0], temper))
    outs = kernel_call(
        functools.partial(other_columns_kernel, half_count=half_count),
        "unpack_other",
        (within, *across, *outs),
        [vmem] * (1 + len(across)) + [pl.BlockSpec(memory_space=pl.ANY)] * 3,
        result,
        [pltpu.VMEM((2, BLK, width), jnp.bfloat16), pltpu.SemaphoreType.DMA((len(across), 2))],
        6,
        out_spaces=[pl.ANY] * 3,
        aliases={1 + len(across) + array: array for array in range(3)},
    )
    return (*outs, temper)


def shards(
    probe_vectors,
    lookup_vectors,
    content_vectors,
    result_cotangent,
    logit_softness,
    block_grouping,
    neighborhood_span,
):
    head_count = probe_vectors.shape[2] // HD
    seq_count = lax.axis_size("seq")
    one_block = probe_vectors.shape[1] == BLK
    whole_tiles = seq_count * BLK % (2 * TILE) == 0 and seq_count & (seq_count - 1) == 0
    if head_count == seq_count and one_block and whole_tiles:
        plan = head_shards
    else:
        plan = clustered_shards
    return plan(
        probe_vectors,
        lookup_vectors,
        content_vectors,
        result_cotangent,
        logit_softness,
        block_grouping,
        neighborhood_span,
    )


def solution(mesh):
    in_specs = (
        P("dp", "seq", None),
        P("dp", "seq", None),
        P("dp", "seq", None),
        P("dp", "seq", None),
        P(),
        P("dp", None, None, None),
        P(),
    )
    out_specs = (P("dp", "seq", None), P("dp", "seq", None), P("dp", "seq", None), P())
    return jax.shard_map(shards, mesh=mesh, in_specs=in_specs, out_specs=out_specs, check_vma=False)
```

```python
import functools
import math

import jax
import jax.numpy as jnp
from jax import lax
from jax.experimental import pallas as pl
from jax.experimental.pallas import tpu as pltpu
from jax.sharding import PartitionSpec as P

HD = 128
BLK = 128


blocked_score = -1e30


def shifted(value, axis, steps):
    count = lax.axis_size(axis)
    first, last = (max(0, -steps), min(count, count - steps))
    return lax.ppermute(value, axis, [(source, source + steps) for source in range(first, last)])


def lifted(array_in):
    return lax.optimization_barrier(array_in.astype(jnp.bfloat16)).astype(jnp.float32)


def head_major(tokens_in, block_len):
    token_count, feature_count = tokens_in.shape
    return tokens_in.reshape(
        token_count // block_len, block_len, feature_count // HD, HD
    ).transpose(2, 0, 1, 3)


def token_major(blocks_in):
    head_count, block_count, block_len, depth = blocks_in.shape
    return blocks_in.transpose(1, 2, 0, 3).reshape(1, block_count * block_len, head_count * depth)


def window_parts(query_block, prev_keys, prev_values, grad_block, usable, window_width, temper):
    block_len = query_block.shape[-2]
    inverse_root = 1.0 / math.sqrt(query_block.shape[-1])
    raw_scores = (
        jnp.einsum("...td,...sd->...ts", query_block, prev_keys, preferred_element_type=jnp.float32)
        * inverse_root
    )
    query_pos = lax.broadcasted_iota(jnp.int32, (block_len, block_len), 0)
    key_pos = lax.broadcasted_iota(jnp.int32, (block_len, block_len), 1)
    pair_mask = usable[..., None, None] & (
        key_pos > query_pos + block_len - window_width[..., None, None]
    )
    scores = temper[..., None, None] * raw_scores
    row_top = jnp.max(jnp.where(pair_mask, scores, blocked_score), axis=-1)
    weights = jnp.where(pair_mask, jnp.exp(scores - row_top[..., None]), 0.0)
    prob_grad = jnp.einsum(
        "...td,...sd->...ts", grad_block, prev_values, preferred_element_type=jnp.float32
    )
    return (
        raw_scores,
        pair_mask,
        prob_grad,
        row_top,
        jnp.sum(weights, axis=-1),
        jnp.sum(weights * prob_grad, axis=-1),
    )


def window_grads(
    raw_scores,
    pair_mask,
    prob_grad,
    query_block,
    prev_keys,
    grad_block,
    log_total,
    row_delta,
    temper,
):
    inverse_root = 1.0 / math.sqrt(query_block.shape[-1])
    scaling = (temper * inverse_root)[..., None, None]
    probability = jnp.where(
        pair_mask, jnp.exp(temper[..., None, None] * raw_scores - log_total[..., None]), 0.0
    )
    score_grad = probability * (prob_grad - row_delta[..., None])
    prob_low = probability.astype(jnp.bfloat16)
    grad_low = score_grad.astype(jnp.bfloat16)
    query_part = (
        jnp.einsum("...ts,...sd->...td", grad_low, prev_keys, preferred_element_type=jnp.float32)
        * scaling
    )
    key_part = (
        jnp.einsum("...ts,...td->...sd", grad_low, query_block, preferred_element_type=jnp.float32)
        * scaling
    )
    value_part = jnp.einsum(
        "...ts,...td->...sd", prob_low, grad_block, preferred_element_type=jnp.float32
    )
    temper_part = jnp.sum(score_grad * raw_scores, axis=(-2, -1))
    return (query_part, key_part, value_part, temper_part)


def cluster_pair(
    query_items,
    key_items,
    value_items,
    grad_items,
    live_items,
    temper,
    window_top,
    window_total,
    window_mass,
):
    item_count, block_len, depth = query_items.shape
    row_count = item_count * block_len
    group_rows = 4 * block_len
    inverse_root = 1.0 / math.sqrt(depth)
    scaling = temper * inverse_root
    query_rows = query_items.reshape(row_count, depth)
    key_rows = key_items.reshape(row_count, depth)
    value_rows = value_items.reshape(row_count, depth)
    grad_rows = grad_items.reshape(row_count, depth)
    key_item = jnp.arange(row_count) // block_len
    key_token = jnp.arange(row_count) % block_len
    live_rows = jnp.repeat(live_items, block_len)
    top_rows = window_top.reshape(row_count)
    total_rows = window_total.reshape(row_count)
    mass_rows = window_mass.reshape(row_count)

    def group_step(carry, start_row):
        key_acc, value_acc, temper_acc = carry
        query_group = lax.dynamic_slice_in_dim(query_rows, start_row, group_rows, 0)
        grad_group = lax.dynamic_slice_in_dim(grad_rows, start_row, group_rows, 0)
        group_live = lax.dynamic_slice_in_dim(live_rows, start_row, group_rows, 0)
        group_top = lax.dynamic_slice_in_dim(top_rows, start_row, group_rows, 0)
        group_total = lax.dynamic_slice_in_dim(total_rows, start_row, group_rows, 0)
        group_mass = lax.dynamic_slice_in_dim(mass_rows, start_row, group_rows, 0)
        query_item = (start_row + jnp.arange(group_rows)) // block_len
        query_token = jnp.arange(group_rows) % block_len
        earlier = (key_item[None, :] < query_item[:, None]) | (
            key_item[None, :] == query_item[:, None]
        ) & (key_token[None, :] <= query_token[:, None])
        pair_mask = group_live[:, None] & live_rows[None, :] & earlier
        raw_scores = (
            lax.dot_general(
                query_group, key_rows, (((1,), (1,)), ((), ())), preferred_element_type=jnp.float32
            )
            * inverse_root
        )
        scores = temper * raw_scores
        row_top = jnp.maximum(
            jnp.max(jnp.where(pair_mask, scores, blocked_score), axis=1), group_top
        )
        weights = jnp.where(pair_mask, jnp.exp(scores - row_top[:, None]), 0.0)
        row_total = jnp.sum(weights, axis=1) + group_total * jnp.exp(group_top - row_top)
        log_total = row_top + jnp.log(jnp.where(group_live, row_total, 1.0))
        probability = jnp.where(pair_mask, jnp.exp(scores - log_total[:, None]), 0.0)
        prob_grad = lax.dot_general(
            grad_group, value_rows, (((1,), (1,)), ((), ())), preferred_element_type=jnp.float32
        )
        row_delta = jnp.sum(probability * prob_grad, axis=1) + group_mass * jnp.exp(
            group_top - log_total
        )
        score_grad = probability * (prob_grad - row_delta[:, None])
        prob_low = probability.astype(jnp.bfloat16)
        grad_low = score_grad.astype(jnp.bfloat16)
        query_part = jnp.dot(grad_low, key_rows, preferred_element_type=jnp.float32) * scaling
        key_acc = (
            key_acc
            + lax.dot_general(
                grad_low, query_group, (((0,), (0,)), ((), ())), preferred_element_type=jnp.float32
            )
            * scaling
        )
        value_acc = value_acc + lax.dot_general(
            prob_low, grad_group, (((0,), (0,)), ((), ())), preferred_element_type=jnp.float32
        )
        temper_acc = temper_acc + jnp.sum(score_grad * raw_scores)
        return ((key_acc, value_acc, temper_acc), (query_part, log_total, row_delta))

    start_rows = jnp.arange(item_count // 4) * group_rows
    initial = (
        jnp.zeros((row_count, depth), jnp.float32),
        jnp.zeros((row_count, depth), jnp.float32),
        jnp.zeros((), jnp.float32),
    )
    (key_acc, value_acc, temper_acc), (query_part, log_total, row_delta) = lax.scan(
        group_step, initial, start_rows
    )
    return (
        query_part.reshape(item_count, block_len, depth),
        log_total.reshape(item_count, block_len),
        row_delta.reshape(item_count, block_len),
        key_acc.reshape(item_count, block_len, depth),
        value_acc.reshape(item_count, block_len, depth),
        temper_acc,
    )


def clustered_shards(
    probe_vectors,
    lookup_vectors,
    content_vectors,
    result_cotangent,
    logit_softness,
    block_grouping,
    neighborhood_span,
):
    seq_count = lax.axis_size("seq")
    position = lax.axis_index("seq")
    tokens = probe_vectors.shape[1]
    head_count = probe_vectors.shape[2] // HD
    local_blocks = tokens // BLK
    block_count = local_blocks * seq_count
    cluster_count = max(1, block_count // 8)
    capacity = min(12, block_count)
    owned_pairs = cluster_count * head_count // seq_count
    group_count = cluster_count // owned_pairs
    per_peer = max(1, local_blocks // group_count)
    cluster_ids = block_grouping[0, :, :, 0]
    query_home = head_major(probe_vectors[0], BLK)
    key_home = head_major(lookup_vectors[0], BLK)
    value_home = head_major(content_vectors[0], BLK)
    grad_home = head_major(result_cotangent[0], BLK)
    last_block = (lookup_vectors[0, tokens - BLK :], content_vectors[0, tokens - BLK :])
    prev_key_rows, prev_value_rows = shifted((last_block[0], last_block[1]), "seq", 1)
    prev_keys = jnp.concatenate([head_major(prev_key_rows, BLK), key_home[:, :-1]], axis=1)
    prev_values = jnp.concatenate([head_major(prev_value_rows, BLK), value_home[:, :-1]], axis=1)
    first_block = position * local_blocks
    before = jnp.concatenate(
        [jnp.full((head_count, 1), -1, jnp.int32), cluster_ids[:, :-1]], axis=1
    )
    my_ids = lax.dynamic_slice_in_dim(cluster_ids, first_block, local_blocks, 1)
    my_before = lax.dynamic_slice_in_dim(before, first_block, local_blocks, 1)
    global_block = first_block + jnp.arange(local_blocks)
    usable_home = (global_block[None, :] >= 1) & (my_before != my_ids)
    peer_index = jnp.arange(seq_count)
    peer_head = peer_index * owned_pairs // cluster_count
    slot_range = jnp.arange(per_peer)
    local_range = jnp.arange(local_blocks)
    owner_index = (jnp.arange(head_count)[:, None] * cluster_count + my_ids) // owned_pairs
    peer_ids = jnp.take(my_ids, peer_head, axis=0)
    goes = (peer_head[:, None] * cluster_count + peer_ids) // owned_pairs == peer_index[:, None]
    send_rank = jnp.cumsum(goes.astype(jnp.int32), axis=1) - 1
    send_pick = goes[:, None, :] & (send_rank[:, None, :] == slot_range[None, :, None])
    send_block = jnp.sum(jnp.where(send_pick, local_range[None, None, :], 0), axis=2)
    send_flat = peer_head[:, None] * local_blocks + send_block
    home_rank = jnp.take_along_axis(send_rank, owner_index, axis=0)
    home_pos = owner_index * per_peer + home_rank
    pair_index = position * owned_pairs + jnp.arange(owned_pairs)
    split_for_couple = pair_index // cluster_count
    pair_cluster = pair_index % cluster_count
    my_head = position * owned_pairs // cluster_count
    split_numbers = jnp.take(cluster_ids, my_head, axis=0)
    member = split_numbers[None, :] == pair_cluster[:, None]
    member_rank = jnp.cumsum(member.astype(jnp.int32), axis=1) - 1
    member_count = jnp.sum(member.astype(jnp.int32), axis=1)
    picked = member[:, None, :] & (member_rank[:, None, :] == jnp.arange(capacity)[None, :, None])
    member_block = jnp.sum(jnp.where(picked, jnp.arange(block_count)[None, None, :], 0), axis=2)
    live_members = jnp.arange(capacity)[None, :] < member_count[:, None]
    mine = (my_head * cluster_count + split_numbers) // owned_pairs == position
    mine_grid = mine.reshape(seq_count, local_blocks)
    recv_rank = jnp.cumsum(mine_grid.astype(jnp.int32), axis=1) - 1
    recv_pos = (peer_index[:, None] * per_peer + recv_rank).reshape(block_count)
    member_pos = jnp.take(recv_pos, member_block)
    couple_softness = jnp.take(logit_softness, split_for_couple)
    pair_onehot = (split_for_couple[:, None] == jnp.arange(head_count)[None, :]).astype(jnp.float32)
    slot_pair = my_head * cluster_count + split_numbers - position * owned_pairs
    same_cluster = split_numbers[:, None] == split_numbers[None, :]
    earlier_block = jnp.arange(block_count)[None, :] < jnp.arange(block_count)[:, None]
    slot_rank = jnp.sum((same_cluster & earlier_block).astype(jnp.int32), axis=1)
    back_pos = jnp.clip(slot_pair, 0, owned_pairs - 1) * capacity + jnp.clip(
        slot_rank, 0, capacity - 1
    )
    back_grid = back_pos.reshape(seq_count, local_blocks)
    back_pick = mine_grid[:, None, :] & (recv_rank[:, None, :] == slot_range[None, :, None])
    back_flat = jnp.sum(jnp.where(back_pick, back_grid[:, None, :], 0), axis=2)

    def to_peers(array_in):
        flat = array_in.reshape((head_count * local_blocks,) + array_in.shape[2:])
        return jnp.take(flat, send_flat, axis=0)

    def members(array_in):
        flat = array_in.reshape((seq_count * per_peer,) + array_in.shape[2:])
        return jnp.take(flat, member_pos, axis=0)

    def to_owner(array_in):
        flat = array_in.reshape((owned_pairs * capacity,) + array_in.shape[2:])
        return jnp.take(flat, back_flat, axis=0)

    def from_peers(array_in):
        flat = array_in.reshape((seq_count * per_peer,) + array_in.shape[2:])
        return jnp.take(flat, home_pos, axis=0)

    raw_w, mask_w, pgrad_w, top_w, total_w, mass_w = window_parts(
        query_home,
        prev_keys,
        prev_values,
        grad_home,
        usable_home,
        neighborhood_span[:, None],
        logit_softness[:, None],
    )
    arrived = (
        lax.all_to_all(to_peers(query_home), "seq", split_axis=0, concat_axis=0, tiled=True),
        lax.all_to_all(to_peers(key_home), "seq", split_axis=0, concat_axis=0, tiled=True),
        lax.all_to_all(to_peers(value_home), "seq", split_axis=0, concat_axis=0, tiled=True),
        lax.all_to_all(to_peers(grad_home), "seq", split_axis=0, concat_axis=0, tiled=True),
    )
    arrived_stats = (
        lax.all_to_all(to_peers(top_w), "seq", split_axis=0, concat_axis=0, tiled=True),
        lax.all_to_all(to_peers(total_w), "seq", split_axis=0, concat_axis=0, tiled=True),
        lax.all_to_all(to_peers(mass_w), "seq", split_axis=0, concat_axis=0, tiled=True),
    )
    query_m, key_m, value_m, grad_m = [members(item_in) for item_in in arrived]
    top_m, total_m, mass_m = [members(item_in) for item_in in arrived_stats]

    def split_pair(pair_inputs):
        query_i, key_i, value_i, grad_i, live_i, temper_i, top_i, total_i, mass_i = pair_inputs
        query_c, log_total, row_delta, key_c, value_c, temper_c = cluster_pair(
            query_i, key_i, value_i, grad_i, live_i, temper_i, top_i, total_i, mass_i
        )
        return (
            query_c.astype(jnp.bfloat16),
            key_c.astype(jnp.bfloat16),
            value_c.astype(jnp.bfloat16),
            log_total,
            row_delta,
            temper_c,
        )

    owner_results = lax.map(
        split_pair,
        (query_m, key_m, value_m, grad_m, live_members, couple_softness, top_m, total_m, mass_m),
    )
    returned = (
        lax.all_to_all(to_owner(owner_results[0]), "seq", split_axis=0, concat_axis=0, tiled=True),
        lax.all_to_all(to_owner(owner_results[1]), "seq", split_axis=0, concat_axis=0, tiled=True),
        lax.all_to_all(to_owner(owner_results[2]), "seq", split_axis=0, concat_axis=0, tiled=True),
    )
    returned_stats = (
        lax.all_to_all(to_owner(owner_results[3]), "seq", split_axis=0, concat_axis=0, tiled=True),
        lax.all_to_all(to_owner(owner_results[4]), "seq", split_axis=0, concat_axis=0, tiled=True),
    )
    query_cluster = from_peers(returned[0])
    key_cluster = from_peers(returned[1])
    value_cluster = from_peers(returned[2])
    log_home = from_peers(returned_stats[0])
    delta_home = from_peers(returned_stats[1])
    query_w, key_w, value_w, temper_w = window_grads(
        raw_w,
        mask_w,
        pgrad_w,
        query_home,
        prev_keys,
        grad_home,
        log_home,
        delta_home,
        logit_softness[:, None],
    )
    query_out = (query_cluster.astype(jnp.float32) + lifted(query_w)).astype(jnp.bfloat16)
    key_window = key_w.astype(jnp.bfloat16)
    value_window = value_w.astype(jnp.bfloat16)
    temper_local = jnp.sum(owner_results[5][:, None] * pair_onehot, axis=0) + jnp.sum(
        temper_w, axis=1
    )
    edge_keys, edge_values = shifted((key_window[:, 0], value_window[:, 0]), "seq", -1)
    key_next = jnp.concatenate([key_window[:, 1:], edge_keys[:, None]], axis=1)
    value_next = jnp.concatenate([value_window[:, 1:], edge_values[:, None]], axis=1)
    key_out = (key_cluster.astype(jnp.float32) + key_next.astype(jnp.float32)).astype(jnp.bfloat16)
    value_out = (value_cluster.astype(jnp.float32) + value_next.astype(jnp.float32)).astype(
        jnp.bfloat16
    )
    temper_total = lax.psum(temper_local, ("seq", "dp"))
    temper_grad = temper_total / (lax.axis_size("dp") * tokens * seq_count)
    return (token_major(query_out), token_major(key_out), token_major(value_out), temper_grad)


TILE = 256
EXTRA = 16
MIB = 1024 * 1024
PIECES = 4
QUERY, KEY, VALUE, GRAD = range(4)


def columns_of(index):
    return pl.ds(pl.multiple_of(index * HD, HD), HD)


def rows_of(index):
    return pl.ds(pl.multiple_of(index * BLK, BLK), BLK)


def tile_rows(tile):
    return slice(tile * TILE, (tile + 1) * TILE)


def position(half_count):
    me = lax.axis_index("seq")
    half = jnp.where(me >= half_count, 1, 0)
    return me, half, me - half * half_count


def hop(step, half_count):
    return half_count - 2 - 2 * step


def kernel_call(
    kernel, name, operands, in_specs, out_shape, scratch, vmem_mib, flops=0, out_spaces=None,
    aliases=None,
):
    bytes_accessed = sum(
        math.prod(item.shape) * item.dtype.itemsize for item in (*operands, *out_shape)
    )
    return pl.pallas_call(
        kernel,
        out_shape=out_shape,
        in_specs=in_specs,
        out_specs=[
            pl.BlockSpec(memory_space=space)
            for space in out_spaces or [pltpu.VMEM] * len(out_shape)
        ],
        scratch_shapes=scratch,
        input_output_aliases=aliases or {},
        cost_estimate=pl.CostEstimate(
            flops=flops, bytes_accessed=bytes_accessed, transcendentals=0
        ),
        compiler_params=pltpu.CompilerParams(vmem_limit_bytes=vmem_mib * MIB),
        name=name,
    )(*operands)


def pack_kernel(*refs, half_count):
    arrays, within_ref, foreign_refs = refs[:4], refs[4], refs[5:7]
    held, within, across, arrival, left_within, left_across = refs[7:]
    me, half, _ = position(half_count)
    piece = BLK // PIECES
    arrivals = [
        [
            pltpu.make_async_copy(
                array_ref.at[0, part * piece : (part + 1) * piece, :],
                held.at[place, part * piece : (part + 1) * piece, :],
                arrival.at[place, part],
            )
            for part in range(PIECES)
        ]
        for place, array_ref in enumerate(arrays)
    ]
    for copies in arrivals:
        for copy in copies:
            copy.start()
    leaving = []
    for place, copies in enumerate(arrivals):
        for copy in copies:
            copy.wait()
        for slot, base in enumerate((half * half_count, (1 - half) * half_count)):
            rows = slice((slot * 4 + place) * BLK, (slot * 4 + place + 1) * BLK)
            for peer in range(half_count):
                within[peer, rows, :] = held[place, :, columns_of(base + peer)]
            leaving.append(
                pltpu.make_async_copy(
                    within.at[:, rows, :], within_ref.at[:, rows, :], left_within.at[place, slot]
                )
            )
            leaving[-1].start()
    first = jnp.where(half == 0, KEY, QUERY)
    second = jnp.where(half == 0, VALUE, GRAD)
    for core, foreign_ref in enumerate(foreign_refs):
        for step in range(half_count // 2):
            columns = columns_of(me ^ core ^ (half_count + hop(step, half_count)))
            across[core, step, :BLK, :] = held[first, :, columns]
            across[core, step, BLK:, :] = held[second, :, columns]
        leaving.append(pltpu.make_async_copy(across.at[core], foreign_ref, left_across.at[core]))
        leaving[-1].start()
    for copy in leaving:
        copy.wait()


def packed(arrays, half_count):
    width = arrays[0].shape[2]
    within_shape, across_shape = (half_count, 8 * BLK, HD), (half_count // 2, 2 * BLK, HD)
    return kernel_call(
        functools.partial(pack_kernel, half_count=half_count),
        "pack_heads",
        arrays,
        [pl.BlockSpec(memory_space=pl.ANY)] * 4,
        [jax.ShapeDtypeStruct(within_shape, jnp.bfloat16)]
        + [jax.ShapeDtypeStruct(across_shape, jnp.bfloat16)] * 2,
        [
            pltpu.VMEM((4, BLK, width), jnp.bfloat16),
            pltpu.VMEM(within_shape, jnp.bfloat16),
            pltpu.VMEM((2, *across_shape), jnp.bfloat16),
            pltpu.SemaphoreType.DMA((4, PIECES)),
            pltpu.SemaphoreType.DMA((4, 2)),
            pltpu.SemaphoreType.DMA((2,)),
        ],
        60,
        out_spaces=[pl.ANY] * 3,
    )


def dot_rows(left, right):
    return lax.dot_general(
        left, right, (((1,), (1,)), ((), ())), preferred_element_type=jnp.float32
    )


def dot_plain(left, right):
    return lax.dot_general(
        left, right, (((1,), (0,)), ((), ())), preferred_element_type=jnp.float32
    )


def from_blocks(ref, place):
    def rows(start, stop):
        per_tile = TILE // BLK
        return jnp.concatenate(
            [ref[block, place] for block in range(start * per_tile, stop * per_tile)],
            axis=0,
        )

    return rows


def from_array(ref, place):
    return lambda start, stop: ref[place, start * TILE : stop * TILE, :]


class Region:
    def __init__(self, square, sources, tiles, scaling, bias_ref=None, least_ref=None, first=0):
        self.square, self.sources, self.tiles, self.scaling = square, sources, tiles, scaling
        self.bias_ref, self.least_ref, self.first = bias_ref, least_ref, first

    def rows(self, which, start, stop):
        return self.sources[which](start, stop)

    def scale_of(self, array):
        return 1.0 if array == VALUE else self.scaling[:, :HD]

    def keys_of(self, tile):
        return range(self.tiles if self.square else tile + 1)

    def scores(self, tile_key, tile_query):
        per_tile = TILE // BLK
        scores = dot_rows(
            self.rows(KEY, tile_key, tile_key + 1), self.rows(QUERY, tile_query, tile_query + 1)
        ) * (self.scaling * math.log2(math.e))
        before = self.tiles * per_tile if self.square else 0
        rows = []
        for sub_key in range(per_tile):
            key_block = tile_key * per_tile + sub_key
            pieces = []
            for sub_query in range(per_tile):
                query_block = tile_query * per_tile + sub_query
                lanes = slice(sub_query * BLK, (sub_query + 1) * BLK)
                piece = scores[sub_key * BLK : (sub_key + 1) * BLK, lanes]
                apart = before + query_block - key_block
                if apart < 0:
                    piece = jnp.full_like(piece, blocked_score)
                elif apart == 0:
                    piece = jnp.where(key_minus_query() <= 0, piece, blocked_score)
                elif apart == 1:
                    row = self.first + (0 if self.square else key_block)
                    least = self.least_ref[row : row + 1, :]
                    piece = jnp.where(key_minus_query() > least, piece, blocked_score)
                else:
                    at = slice(query_block * BLK, (query_block + 1) * BLK)
                    piece = piece + self.bias_ref[key_block : key_block + 1, at]
                pieces.append(piece)
            rows.append(jnp.concatenate(pieces, axis=1))
        return jnp.concatenate(rows, axis=0)


def diagonal(slot, arrived_ref, scales_ref, bias_ref=None, least_ref=None):
    blocks = arrived_ref.shape[0]
    sources = [from_blocks(arrived_ref, slot * 4 + place) for place in range(4)]
    bias = None if bias_ref is None else bias_ref.at[slot]
    first = slot * (blocks - 1)
    scaling = scales_ref[slot : slot + 1, :]
    return Region(False, sources, blocks * BLK // TILE, scaling, bias, least_ref, first)


def square(square_ref, scales_ref, bias_ref=None, least_ref=None):
    tiles = square_ref.shape[1] // TILE
    sources = [from_array(square_ref, place) for place in range(4)]
    bias = None if bias_ref is None else bias_ref.at[2]
    first = 2 * (tiles * TILE // BLK - 1)
    return Region(True, sources, tiles, scales_ref[0:1, :], bias, least_ref, first)


def key_minus_query():
    shape = (BLK, BLK)
    return lax.broadcasted_iota(jnp.int32, shape, 0) - lax.broadcasted_iota(jnp.int32, shape, 1)


def statistics(region, weight_ref, towards_ref, out_ref, first_row):
    for tile in range(region.tiles):
        here = tile_rows(tile)
        top = jnp.full((1, TILE), blocked_score, jnp.float32)
        for other in region.keys_of(tile):
            raw = region.scores(other, tile)
            weight_ref[tile_rows(other), here] = raw
            top = jnp.maximum(top, jnp.max(raw, axis=0, keepdims=True))
        sums = [jnp.zeros((1, TILE), jnp.float32)] * 4
        for other in region.keys_of(tile):
            there = tile_rows(other)
            raw = weight_ref[there, here]
            weight = jnp.exp2(raw - top)
            towards = dot_rows(
                region.rows(VALUE, other, other + 1), region.rows(GRAD, tile, tile + 1)
            )
            weight_ref[there, here] = weight
            towards_ref[there, here] = towards
            pulled, weighted = weight * towards, weight * raw
            terms = (weight, pulled, pulled * raw, weighted)
            sums = [
                total + jnp.sum(term, axis=0, keepdims=True) for total, term in zip(sums, terms)
            ]
        for row, value in enumerate((top, *sums)):
            out_ref[first_row + row : first_row + row + 1, here] = value


def gradients(
    region, weight_ref, towards_ref, top, log_total, delta, prob_low, grad_low, keys_flat, emit=None
):
    keys_flat[...] = region.rows(KEY, 0, region.tiles).T
    share = jnp.exp2(top - log_total)
    query_parts, key_parts, value_parts = [], [], []
    for tile in range(region.tiles):
        here = tile_rows(tile)
        for other in region.keys_of(tile):
            there = tile_rows(other)
            probability = weight_ref[there, here] * share[:, here]
            prob_low[there, here] = probability.astype(jnp.bfloat16)
            grad_low[there, here] = (
                probability * (towards_ref[there, here] - delta[:, here])
            ).astype(jnp.bfloat16)
        upto = slice(0, len(region.keys_of(tile)) * TILE)
        query_parts.append(dot_plain(keys_flat[:, upto], grad_low[upto, here]).T)
    if emit is not None:
        emit(QUERY, query_parts)
    for low, which, parts in ((grad_low, QUERY, key_parts), (prob_low, GRAD, value_parts)):
        for tile in range(region.tiles):
            first = 0 if region.square else tile
            onward = slice(first * TILE, region.tiles * TILE)
            parts.append(
                dot_plain(low[tile_rows(tile), onward], region.rows(which, first, region.tiles))
            )
        if emit is not None:
            emit(KEY if which == QUERY else VALUE, parts)
    return query_parts, key_parts, value_parts


def merged(first, second):
    top = jnp.maximum(first[0], second[0])
    left, right = jnp.exp2(first[0] - top), jnp.exp2(second[0] - top)
    total = first[1] * left + second[1] * right
    mass = first[2] * left + second[2] * right
    return top + jnp.log2(total), mass / total


def alone(rows):
    return rows[0] + jnp.log2(rows[1]), rows[2] / rows[1]


def rows_at(ref, first, count=5):
    return [ref[first + row : first + row + 1, :] for row in range(count)]


def temper_terms(rows, totals, scale_row):
    log_total, delta = totals
    terms = (rows[3] - delta * rows[4]) * jnp.exp2(rows[0] - log_total)
    folded = sum(terms[:, start : start + HD] for start in range(0, terms.shape[1], HD))
    return folded / (scale_row[:, :HD] * (math.sqrt(HD) * math.log2(math.e)))


def put(within_ref, array, tile, value):
    per_tile = TILE // BLK
    for sub in range(per_tile):
        within_ref[tile * per_tile + sub, array * BLK : (array + 1) * BLK, :] = value[
            sub * BLK : (sub + 1) * BLK, :
        ].astype(jnp.bfloat16)


def scaled(region, parts):
    scale = region.scaling[:, :HD]
    return [[value * scale for value in part] for part in parts[:2]] + [parts[2]]


def masks_kernel(softness_ref, ids_ref, span_ref, scales_ref, bias_ref, least_ref, *, half_count):
    me, half, _ = position(half_count)
    base = half * half_count
    regions = (
        (me, base, base),
        (me ^ half_count, base, base),
        (me, 0, half_count),
    )
    for slot, (head, key_base, query_base) in enumerate(regions):
        if slot < 2:
            scales_ref[slot : slot + 1, :] = jnp.full(
                (1, TILE), softness_ref[head] * (1.0 / math.sqrt(HD)), jnp.float32
            )

        def same(key_block, query_block):
            return ids_ref[head, key_base + key_block] == ids_ref[head, query_base + query_block]

        def bias(key_block, query_block):
            return jnp.full(
                (1, BLK), jnp.where(same(key_block, query_block), 0.0, blocked_score), jnp.float32
            )

        for key_block in range(half_count):
            bias_ref[slot, key_block : key_block + 1, :] = jnp.concatenate(
                [bias(key_block, query_block) for query_block in range(half_count)], axis=1
            )
        pairs = [(block, block + 1) for block in range(half_count - 1)]
        if slot == 2:
            pairs = [(half_count - 1, 0)]
        for place, pair in enumerate(pairs):
            least = jnp.where(same(*pair), -BLK, BLK - span_ref[head])
            row = slot * (half_count - 1) + place
            least_ref[row : row + 1, :] = jnp.full((1, BLK), least, jnp.int32)


def within_kernel(
    arrived_ref, scales_ref, bias_ref, least_ref, stats_ref, parts_ref, own_weight, own_towards, other_weight, other_towards, *scratch, half_count
):
    _, half, _ = position(half_count)
    kept = ((own_weight, own_towards), (other_weight, other_towards))
    for slot in range(2):
        region = diagonal(slot, arrived_ref, scales_ref, bias_ref, least_ref)
        statistics(region, *kept[slot], stats_ref, slot * 5)

    @pl.when(half == 0)
    def _():
        region = diagonal(0, arrived_ref, scales_ref)
        single = alone(rows_at(stats_ref, 0))
        parts = gradients(region, *kept[0], stats_ref[0:1, :], *single, *scratch)
        for place, tiles in enumerate(scaled(region, parts)):
            for tile, value in enumerate(tiles):
                parts_ref[place, tile_rows(tile), :] = value


def square_kernel(arrived_ref, scales_ref, bias_ref, least_ref, stats_ref, *refs, half_count):
    across_refs = refs[: half_count // 2]
    square_ref, message_ref, square_stats, weight, towards = refs[half_count // 2 :]
    _, half, place = position(half_count)
    first = jnp.where(half == 0, QUERY, KEY)
    second = jnp.where(half == 0, GRAD, VALUE)
    for step, across_ref in enumerate(across_refs):
        for core in range(2):
            rows = rows_of(place ^ core ^ hop(step, half_count))
            square_ref[first, rows, :] = across_ref[core, :BLK, :]
            square_ref[second, rows, :] = across_ref[core, BLK:, :]
    for kept in (jnp.where(half == 0, KEY, QUERY), jnp.where(half == 0, VALUE, GRAD)):
        for block in range(half_count):
            square_ref[kept, block * BLK : (block + 1) * BLK, :] = arrived_ref[block, kept]
    region = square(square_ref, scales_ref, bias_ref, least_ref)
    statistics(region, weight, towards, square_stats, 0)
    own, other, crossing = rows_at(stats_ref, 0), rows_at(stats_ref, 5), rows_at(square_stats, 0)
    for row in range(5):
        message_ref[row : row + 1, :] = jnp.where(half == 0, crossing[row], other[row])
    own_scale, other_scale = scales_ref[0:1, :], scales_ref[1:2, :]
    both = merged(own, crossing)
    whole = temper_terms(own, both, own_scale) + temper_terms(crossing, both, own_scale)
    single = temper_terms(own, alone(own), own_scale)
    message_ref[5:6, :HD] = jnp.where(half == 0, single, whole)
    message_ref[6:7, :HD] = temper_terms(other, alone(other), other_scale)


def first_kernel(
    arrived_ref, scales_ref, square_ref, stats_ref, square_stats,
    own_weight, own_towards, other_weight, other_towards, square_weight, square_towards,
    across_ref, within_ref, ready, ready_sem, *scratch, half_count
):
    _, half, _ = position(half_count)
    leaving = sends(ready, within_ref, ready_sem, (1 - half) * 3)

    @pl.when(half == 0)
    def _():
        region = diagonal(1, arrived_ref, scales_ref)

        def send(array, parts):
            for tile, part in enumerate(parts):
                put(ready, array, tile, part * region.scale_of(array))
            leaving[array].start()

        totals = alone(rows_at(stats_ref, 5))
        gradients(
            region, other_weight, other_towards, stats_ref[5:6, :], *totals, *scratch, emit=send
        )

    @pl.when(half == 1)
    def _():
        totals = merged(rows_at(stats_ref, 0), rows_at(square_stats, 0))
        region = square(square_ref, scales_ref)
        parts = gradients(
            region, square_weight, square_towards, square_stats[0:1, :], *totals, *scratch
        )
        across_query, *foreign = scaled(region, parts)
        for array, tiles in enumerate(foreign):
            for tile, value in enumerate(tiles):
                across_ref[array, tile_rows(tile), :] = value.astype(jnp.bfloat16)
        region = diagonal(0, arrived_ref, scales_ref)

        def send(array, parts):
            for tile, part in enumerate(parts):
                value = part * region.scale_of(array)
                put(ready, array, tile, value + across_query[tile] if array == QUERY else value)
            leaving[array].start()

        gradients(
            region, own_weight, own_towards, stats_ref[0:1, :], *totals, *scratch, emit=send
        )

    for copy in leaving:
        copy.wait()


def sends(ready, within_ref, sems, first):
    copies = []
    for array in range(3):
        rows = slice(array * BLK, (array + 1) * BLK)
        copies.append(
            pltpu.make_async_copy(
                ready.at[:, rows, :], within_ref.at[:, rows_of(first + array), :], sems.at[array]
            )
        )
    return copies


def temper_rows(own, other):
    row = lax.broadcasted_iota(jnp.int32, (EXTRA, HD), 0)
    rows = jnp.zeros((EXTRA, HD), jnp.float32)
    for place, terms in enumerate((own, other)):
        rest = jnp.broadcast_to(jnp.sum(terms, axis=1, keepdims=True), (EXTRA, HD))
        for piece in range(3):
            high = rest.astype(jnp.bfloat16).astype(jnp.float32)
            rows = jnp.where(row == place * 3 + piece, high, rows)
            rest = rest - high
    return rows.astype(jnp.bfloat16)


def finish_kernel(
    arrived_ref, scales_ref, square_ref, message_ref, received_ref, stats_ref, square_stats,
    parts_ref, square_weight, square_towards, other_weight, other_towards, across_ref, begun_ref,
    within_ref, *refs, half_count
):
    del begun_ref
    chunk_refs = refs[:2]
    across, ready, tail, ready_sem, tail_sem, *scratch = refs[2:]
    _, half, place = position(half_count)
    leaving = sends(ready, within_ref, ready_sem, half * 3)
    sent, came = rows_at(message_ref, 0), rows_at(received_ref, 0)
    totals = merged(sent, came)
    scale = jnp.where(half == 0, scales_ref[0:1, :], scales_ref[1:2, :])
    shared = temper_terms(sent, totals, scale) + temper_terms(came, totals, scale)
    mine, theirs = message_ref[5:6, :HD], received_ref[5:6, :HD]
    own = mine + jnp.where(half == 0, shared, received_ref[6:7, :HD])
    other = theirs + jnp.where(half == 0, message_ref[6:7, :HD], shared)
    pieces = temper_rows(own, other)
    for block in range(half_count):
        tail[block] = pieces
    leaving.append(
        pltpu.make_async_copy(tail, within_ref.at[:, 6 * BLK : 6 * BLK + EXTRA, :], tail_sem)
    )
    leaving[-1].start()

    def chunks():
        for core, chunk_ref in enumerate(chunk_refs):
            for step in range(half_count // 2):
                yield step, chunk_ref, rows_of(place ^ core ^ hop(step, half_count))

    @pl.when(half == 0)
    def _():
        region = square(square_ref, scales_ref)

        def send(array, parts):
            for tile, part in enumerate(parts):
                here = tile_rows(tile)
                value = part * region.scale_of(array)
                if array == QUERY:
                    across[here, :] = value.astype(jnp.bfloat16)
                    put(ready, array, tile, parts_ref[array, here, :])
                else:
                    put(ready, array, tile, parts_ref[array, here, :] + value)
            leaving[array].start()

        gradients(
            region, square_weight, square_towards, square_stats[0:1, :], *totals, *scratch, emit=send
        )
        for step, chunk_ref, rows in chunks():
            chunk_ref[step, :BLK, :] = across[rows, :]
            chunk_ref[step, BLK:, :] = jnp.zeros((BLK, HD), jnp.bfloat16)

    @pl.when(half == 1)
    def _():
        region = diagonal(1, arrived_ref, scales_ref)

        def send(array, parts):
            for tile, part in enumerate(parts):
                put(ready, array, tile, part * region.scale_of(array))
            leaving[array].start()

        gradients(
            region, other_weight, other_towards, stats_ref[5:6, :], *totals, *scratch, emit=send
        )
        for step, chunk_ref, rows in chunks():
            chunk_ref[step, :BLK, :] = across_ref[0, rows, :]
            chunk_ref[step, BLK:, :] = across_ref[1, rows, :]

    for copy in leaving:
        copy.wait()


def temper_kernel(within_ref, temper_ref, *, half_count):
    _, half, _ = position(half_count)
    for peer in range(half_count):
        for slot, base in enumerate((half * half_count, (1 - half) * half_count)):
            rows = within_ref[peer, 3 * slot : 3 * slot + 3, :].astype(jnp.float32)
            temper_ref[pl.ds(base + peer, 1), :] = jnp.sum(rows, axis=0, keepdims=True)


def temper_sums(within, half_count):
    last = 6 * BLK // EXTRA
    return pl.pallas_call(
        functools.partial(temper_kernel, half_count=half_count),
        grid=(1,),
        out_shape=jax.ShapeDtypeStruct((2 * half_count, HD), jnp.float32),
        in_specs=[pl.BlockSpec((half_count, EXTRA, HD), lambda step: (0, last, 0))],
        out_specs=pl.BlockSpec((2 * half_count, HD), lambda step: (0, 0)),
        compiler_params=pltpu.CompilerParams(vmem_limit_bytes=4 * MIB),
        name="temper_sums",
    )(within)


def own_columns_kernel(within_ref, *refs, half_count):
    out_refs, (staged, sems) = refs[:3], refs[3:]
    _, half, _ = position(half_count)
    width = half_count * HD
    for array in range(6):
        for peer in range(half_count):
            staged[array, :, peer * HD : (peer + 1) * HD] = within_ref[
                peer, array * BLK : (array + 1) * BLK, :
            ]

    def copies(arrays):
        return [
            pltpu.make_async_copy(
                staged.at[array],
                out_refs[array % 3].at[0, :, side(half if array < 3 else 1 - half, width)],
                sems.at[array],
            )
            for array in arrays
        ]

    for role, arrays in enumerate(((0, 1, 2, 3), (0, 1, 2, 4, 5))):

        @pl.when(half == role)
        def _():
            leaving = copies(arrays)
            for copy in leaving:
                copy.start()
            for copy in leaving:
                copy.wait()


def side(half, width):
    return pl.ds(pl.multiple_of(half * width, width), width)


def other_columns_kernel(within_ref, *refs, half_count):
    messages = half_count // 2
    across_refs = refs[:messages]
    out_refs, (staged, sems) = refs[messages + 3 : messages + 6], refs[messages + 6 :]
    _, half, place = position(half_count)

    for role, arrays in enumerate(((1, 2), (0,))):

        @pl.when(half == role)
        def _():
            leaving = []
            for step, across_ref in enumerate(across_refs):
                pair = (place ^ hop(step, half_count)) >> 1
                for part, array in enumerate(arrays):
                    rows = slice(part * BLK, (part + 1) * BLK)
                    for core in range(2):
                        peer = place ^ core ^ hop(step, half_count)
                        kept = within_ref[peer, (3 + array) * BLK : (4 + array) * BLK, :]
                        total = kept.astype(jnp.float32) + across_ref[core, rows, :].astype(
                            jnp.float32
                        )
                        staged[part, :, columns_of(peer)] = total.astype(jnp.bfloat16)
                    start = (1 - role) * messages + pair
                    leaving.append(
                        pltpu.make_async_copy(
                            staged.at[part, :, side(pair, 2 * HD)],
                            out_refs[array].at[0, :, side(start, 2 * HD)],
                            sems.at[step, part],
                        )
                    )
                    leaving[-1].start()
            for copy in leaving:
                copy.wait()


def join_kernel(kept_ref, taken_ref, *out_refs):
    for step, out_ref in enumerate(out_refs):
        out_ref[0] = kept_ref[step]
        out_ref[1] = taken_ref[step]


def crossed(kept, given, half_count):
    devices = range(2 * half_count)
    steps, *shape = kept.shape
    taken = lax.ppermute(given, "seq", [(source, source ^ 1) for source in devices])
    messages = kernel_call(
        join_kernel,
        "join_chunks",
        (kept, taken),
        [pl.BlockSpec(memory_space=pltpu.VMEM)] * 2,
        [jax.ShapeDtypeStruct((2, *shape), jnp.bfloat16)] * steps,
        [],
        4,
    )
    return [
        lax.ppermute(
            message, "seq", [(source, source ^ (half_count + hop(step, half_count))) for source in devices]
        )
        for step, message in enumerate(messages)
    ]


def head_shards(
    probe_vectors,
    lookup_vectors,
    content_vectors,
    result_cotangent,
    logit_softness,
    block_grouping,
    neighborhood_span,
):
    seq_count, dp_count = lax.axis_size("seq"), lax.axis_size("dp")
    half_count = seq_count // 2
    tokens = half_count * BLK
    groups = [list(range(half_count)), list(range(half_count, seq_count))]
    settings = (logit_softness, block_grouping[0, :, :, 0], neighborhood_span)
    smem, vmem = pl.BlockSpec(memory_space=pltpu.SMEM), pl.BlockSpec(memory_space=pltpu.VMEM)
    lows = [pltpu.VMEM((tokens, tokens), jnp.bfloat16)] * 2 + [
        pltpu.VMEM((HD, tokens), jnp.bfloat16)
    ]
    rows_of_stats = jax.ShapeDtypeStruct((8, tokens), jnp.float32)
    pairs = jax.ShapeDtypeStruct((tokens, tokens), jnp.float32)
    pair_flops = 2 * tokens * tokens * HD

    def exchange_within(array_in):
        return lax.all_to_all(
            array_in, "seq", split_axis=0, concat_axis=0, axis_index_groups=groups, tiled=True
        )

    def call(
        kernel, name, operands, out_shape, scratch, flops, vmem_mib, scalars=(), out_spaces=None,
        last_in_place=False,
    ):
        in_specs = [smem] * len(scalars) + [vmem] * len(operands)
        if last_in_place:
            in_specs[-1] = pl.BlockSpec(memory_space=pl.ANY)
        return kernel_call(
            functools.partial(kernel, half_count=half_count),
            name,
            (*scalars, *operands),
            in_specs,
            out_shape,
            scratch,
            vmem_mib,
            flops,
            out_spaces,
            {len(operands) - 1: 0} if last_in_place else {},
        )

    sent, *foreign = packed(
        (probe_vectors, lookup_vectors, content_vectors, result_cotangent), half_count
    )
    arrived = exchange_within(sent).reshape(half_count, 8, BLK, HD)
    kept_parts = jax.ShapeDtypeStruct((3, tokens, HD), jnp.float32)
    masks = call(
        masks_kernel,
        "scales_and_masks",
        (),
        [
            jax.ShapeDtypeStruct((8, TILE), jnp.float32),
            jax.ShapeDtypeStruct((3, half_count, tokens), jnp.float32),
            jax.ShapeDtypeStruct((2 * half_count, BLK), jnp.int32),
        ],
        [],
        0,
        2,
        settings,
    )
    foreign[0], *masks = lax.optimization_barrier((foreign[0], *masks))
    foreign = crossed(*foreign, half_count)
    scales = masks[0]
    stats, parts, own_weight, own_towards, other_weight, other_towards = call(
        within_kernel,
        "diagonal_statistics",
        (arrived, *masks),
        [jax.ShapeDtypeStruct((16, tokens), jnp.float32), kept_parts] + [pairs] * 4,
        lows,
        2 * pair_flops,
        14,
    )
    squared, message, square_stats, square_weight, square_towards = call(
        square_kernel,
        "square_statistics",
        (arrived, *masks, stats, *foreign),
        [jax.ShapeDtypeStruct((4, tokens, HD), jnp.bfloat16)] + [rows_of_stats] * 2 + [pairs] * 2,
        [],
        2 * pair_flops,
        8,
    )
    swap = [(source, source ^ half_count) for source in range(seq_count)]
    received = lax.ppermute(message, "seq", swap)
    result = pltpu.HBM((half_count, 6 * BLK + EXTRA, HD), jnp.bfloat16)
    ready = pltpu.VMEM((half_count, 3 * BLK, HD), jnp.bfloat16)
    across, begun = call(
        first_kernel,
        "gradients_before_totals",
        (
            arrived, scales, squared, stats, square_stats, own_weight, own_towards,
            other_weight, other_towards, square_weight, square_towards,
        ),
        [jax.ShapeDtypeStruct((2, tokens, HD), jnp.bfloat16), result],
        [ready, pltpu.SemaphoreType.DMA((3,)), *lows],
        4 * pair_flops,
        14,
        out_spaces=(pltpu.VMEM, pl.ANY),
    )
    operands = (
        arrived, scales, squared, message, received, stats, square_stats, parts,
        square_weight, square_towards, other_weight, other_towards, across, begun,
    )
    within, *foreign = call(
        finish_kernel,
        "gradients_after_totals",
        operands,
        [result]
        + [jax.ShapeDtypeStruct((half_count // 2, 2 * BLK, HD), jnp.bfloat16)] * 2,
        [
            pltpu.VMEM((tokens, HD), jnp.bfloat16), ready,
            pltpu.VMEM((half_count, EXTRA, HD), jnp.bfloat16),
            pltpu.SemaphoreType.DMA((3,)), pltpu.SemaphoreType.DMA, *lows,
        ],
        2 * pair_flops,
        16,
        out_spaces=(pl.ANY, pltpu.VMEM, pltpu.VMEM),
        last_in_place=True,
    )
    across = crossed(*foreign, half_count)
    within = exchange_within(within)
    tempers = temper_sums(within, half_count)
    temper_total = tempers
    for step in range(1, dp_count):
        swap = [(source, (source + step) % dp_count) for source in range(dp_count)]
        temper_total = temper_total + lax.ppermute(tempers, "dp", swap)
    temper = temper_total[:, 0] / (dp_count * BLK * seq_count)
    result = [pltpu.HBM(probe_vectors.shape, jnp.bfloat16)] * 3
    width = half_count * HD
    outs = kernel_call(
        functools.partial(own_columns_kernel, half_count=half_count),
        "unpack_own",
        (within,),
        [vmem],
        result,
        [pltpu.VMEM((6, BLK, width), jnp.bfloat16), pltpu.SemaphoreType.DMA((6,))],
        6,
        out_spaces=[pl.ANY] * 3,
    )
    across[0], temper = lax.optimization_barrier((across[0], temper))
    outs = kernel_call(
        functools.partial(other_columns_kernel, half_count=half_count),
        "unpack_other",
        (within, *across, *outs),
        [vmem] * (1 + len(across)) + [pl.BlockSpec(memory_space=pl.ANY)] * 3,
        result,
        [pltpu.VMEM((2, BLK, width), jnp.bfloat16), pltpu.SemaphoreType.DMA((len(across), 2))],
        6,
        out_spaces=[pl.ANY] * 3,
        aliases={1 + len(across) + array: array for array in range(3)},
    )
    return (*outs, temper)


def shards(
    probe_vectors,
    lookup_vectors,
    content_vectors,
    result_cotangent,
    logit_softness,
    block_grouping,
    neighborhood_span,
):
    head_count = probe_vectors.shape[2] // HD
    seq_count = lax.axis_size("seq")
    one_block = probe_vectors.shape[1] == BLK
    whole_tiles = seq_count * BLK % (2 * TILE) == 0 and seq_count & (seq_count - 1) == 0
    if head_count == seq_count and one_block and whole_tiles:
        plan = head_shards
    else:
        plan = clustered_shards
    return plan(
        probe_vectors,
        lookup_vectors,
        content_vectors,
        result_cotangent,
        logit_softness,
        block_grouping,
        neighborhood_span,
    )


def solution(mesh):
    in_specs = (
        P("dp", "seq", None),
        P("dp", "seq", None),
        P("dp", "seq", None),
        P("dp", "seq", None),
        P(),
        P("dp", None, None, None),
        P(),
    )
    out_specs = (P("dp", "seq", None), P("dp", "seq", None), P("dp", "seq", None), P())
    return jax.shard_map(shards, mesh=mesh, in_specs=in_specs, out_specs=out_specs, check_vma=False)
```

```python
import functools
import math

import jax
import jax.numpy as jnp
from jax import lax
from jax.experimental import pallas as pl
from jax.experimental.pallas import tpu as pltpu
from jax.sharding import PartitionSpec as P

HD = 128
BLK = 128


blocked_score = -1e30


def shifted(value, axis, steps):
    count = lax.axis_size(axis)
    first, last = (max(0, -steps), min(count, count - steps))
    return lax.ppermute(value, axis, [(source, source + steps) for source in range(first, last)])


def lifted(array_in):
    return lax.optimization_barrier(array_in.astype(jnp.bfloat16)).astype(jnp.float32)


def head_major(tokens_in, block_len):
    token_count, feature_count = tokens_in.shape
    return tokens_in.reshape(
        token_count // block_len, block_len, feature_count // HD, HD
    ).transpose(2, 0, 1, 3)


def token_major(blocks_in):
    head_count, block_count, block_len, depth = blocks_in.shape
    return blocks_in.transpose(1, 2, 0, 3).reshape(1, block_count * block_len, head_count * depth)


def window_parts(query_block, prev_keys, prev_values, grad_block, usable, window_width, temper):
    block_len = query_block.shape[-2]
    inverse_root = 1.0 / math.sqrt(query_block.shape[-1])
    raw_scores = (
        jnp.einsum("...td,...sd->...ts", query_block, prev_keys, preferred_element_type=jnp.float32)
        * inverse_root
    )
    query_pos = lax.broadcasted_iota(jnp.int32, (block_len, block_len), 0)
    key_pos = lax.broadcasted_iota(jnp.int32, (block_len, block_len), 1)
    pair_mask = usable[..., None, None] & (
        key_pos > query_pos + block_len - window_width[..., None, None]
    )
    scores = temper[..., None, None] * raw_scores
    row_top = jnp.max(jnp.where(pair_mask, scores, blocked_score), axis=-1)
    weights = jnp.where(pair_mask, jnp.exp(scores - row_top[..., None]), 0.0)
    prob_grad = jnp.einsum(
        "...td,...sd->...ts", grad_block, prev_values, preferred_element_type=jnp.float32
    )
    return (
        raw_scores,
        pair_mask,
        prob_grad,
        row_top,
        jnp.sum(weights, axis=-1),
        jnp.sum(weights * prob_grad, axis=-1),
    )


def window_grads(
    raw_scores,
    pair_mask,
    prob_grad,
    query_block,
    prev_keys,
    grad_block,
    log_total,
    row_delta,
    temper,
):
    inverse_root = 1.0 / math.sqrt(query_block.shape[-1])
    scaling = (temper * inverse_root)[..., None, None]
    probability = jnp.where(
        pair_mask, jnp.exp(temper[..., None, None] * raw_scores - log_total[..., None]), 0.0
    )
    score_grad = probability * (prob_grad - row_delta[..., None])
    prob_low = probability.astype(jnp.bfloat16)
    grad_low = score_grad.astype(jnp.bfloat16)
    query_part = (
        jnp.einsum("...ts,...sd->...td", grad_low, prev_keys, preferred_element_type=jnp.float32)
        * scaling
    )
    key_part = (
        jnp.einsum("...ts,...td->...sd", grad_low, query_block, preferred_element_type=jnp.float32)
        * scaling
    )
    value_part = jnp.einsum(
        "...ts,...td->...sd", prob_low, grad_block, preferred_element_type=jnp.float32
    )
    temper_part = jnp.sum(score_grad * raw_scores, axis=(-2, -1))
    return (query_part, key_part, value_part, temper_part)


def cluster_pair(
    query_items,
    key_items,
    value_items,
    grad_items,
    live_items,
    temper,
    window_top,
    window_total,
    window_mass,
):
    item_count, block_len, depth = query_items.shape
    row_count = item_count * block_len
    group_rows = 4 * block_len
    inverse_root = 1.0 / math.sqrt(depth)
    scaling = temper * inverse_root
    query_rows = query_items.reshape(row_count, depth)
    key_rows = key_items.reshape(row_count, depth)
    value_rows = value_items.reshape(row_count, depth)
    grad_rows = grad_items.reshape(row_count, depth)
    key_item = jnp.arange(row_count) // block_len
    key_token = jnp.arange(row_count) % block_len
    live_rows = jnp.repeat(live_items, block_len)
    top_rows = window_top.reshape(row_count)
    total_rows = window_total.reshape(row_count)
    mass_rows = window_mass.reshape(row_count)

    def group_step(carry, start_row):
        key_acc, value_acc, temper_acc = carry
        query_group = lax.dynamic_slice_in_dim(query_rows, start_row, group_rows, 0)
        grad_group = lax.dynamic_slice_in_dim(grad_rows, start_row, group_rows, 0)
        group_live = lax.dynamic_slice_in_dim(live_rows, start_row, group_rows, 0)
        group_top = lax.dynamic_slice_in_dim(top_rows, start_row, group_rows, 0)
        group_total = lax.dynamic_slice_in_dim(total_rows, start_row, group_rows, 0)
        group_mass = lax.dynamic_slice_in_dim(mass_rows, start_row, group_rows, 0)
        query_item = (start_row + jnp.arange(group_rows)) // block_len
        query_token = jnp.arange(group_rows) % block_len
        earlier = (key_item[None, :] < query_item[:, None]) | (
            key_item[None, :] == query_item[:, None]
        ) & (key_token[None, :] <= query_token[:, None])
        pair_mask = group_live[:, None] & live_rows[None, :] & earlier
        raw_scores = (
            lax.dot_general(
                query_group, key_rows, (((1,), (1,)), ((), ())), preferred_element_type=jnp.float32
            )
            * inverse_root
        )
        scores = temper * raw_scores
        row_top = jnp.maximum(
            jnp.max(jnp.where(pair_mask, scores, blocked_score), axis=1), group_top
        )
        weights = jnp.where(pair_mask, jnp.exp(scores - row_top[:, None]), 0.0)
        row_total = jnp.sum(weights, axis=1) + group_total * jnp.exp(group_top - row_top)
        log_total = row_top + jnp.log(jnp.where(group_live, row_total, 1.0))
        probability = jnp.where(pair_mask, jnp.exp(scores - log_total[:, None]), 0.0)
        prob_grad = lax.dot_general(
            grad_group, value_rows, (((1,), (1,)), ((), ())), preferred_element_type=jnp.float32
        )
        row_delta = jnp.sum(probability * prob_grad, axis=1) + group_mass * jnp.exp(
            group_top - log_total
        )
        score_grad = probability * (prob_grad - row_delta[:, None])
        prob_low = probability.astype(jnp.bfloat16)
        grad_low = score_grad.astype(jnp.bfloat16)
        query_part = jnp.dot(grad_low, key_rows, preferred_element_type=jnp.float32) * scaling
        key_acc = (
            key_acc
            + lax.dot_general(
                grad_low, query_group, (((0,), (0,)), ((), ())), preferred_element_type=jnp.float32
            )
            * scaling
        )
        value_acc = value_acc + lax.dot_general(
            prob_low, grad_group, (((0,), (0,)), ((), ())), preferred_element_type=jnp.float32
        )
        temper_acc = temper_acc + jnp.sum(score_grad * raw_scores)
        return ((key_acc, value_acc, temper_acc), (query_part, log_total, row_delta))

    start_rows = jnp.arange(item_count // 4) * group_rows
    initial = (
        jnp.zeros((row_count, depth), jnp.float32),
        jnp.zeros((row_count, depth), jnp.float32),
        jnp.zeros((), jnp.float32),
    )
    (key_acc, value_acc, temper_acc), (query_part, log_total, row_delta) = lax.scan(
        group_step, initial, start_rows
    )
    return (
        query_part.reshape(item_count, block_len, depth),
        log_total.reshape(item_count, block_len),
        row_delta.reshape(item_count, block_len),
        key_acc.reshape(item_count, block_len, depth),
        value_acc.reshape(item_count, block_len, depth),
        temper_acc,
    )


def clustered_shards(
    probe_vectors,
    lookup_vectors,
    content_vectors,
    result_cotangent,
    logit_softness,
    block_grouping,
    neighborhood_span,
):
    seq_count = lax.axis_size("seq")
    position = lax.axis_index("seq")
    tokens = probe_vectors.shape[1]
    head_count = probe_vectors.shape[2] // HD
    local_blocks = tokens // BLK
    block_count = local_blocks * seq_count
    cluster_count = max(1, block_count // 8)
    capacity = min(12, block_count)
    owned_pairs = cluster_count * head_count // seq_count
    group_count = cluster_count // owned_pairs
    per_peer = max(1, local_blocks // group_count)
    cluster_ids = block_grouping[0, :, :, 0]
    query_home = head_major(probe_vectors[0], BLK)
    key_home = head_major(lookup_vectors[0], BLK)
    value_home = head_major(content_vectors[0], BLK)
    grad_home = head_major(result_cotangent[0], BLK)
    last_block = (lookup_vectors[0, tokens - BLK :], content_vectors[0, tokens - BLK :])
    prev_key_rows, prev_value_rows = shifted((last_block[0], last_block[1]), "seq", 1)
    prev_keys = jnp.concatenate([head_major(prev_key_rows, BLK), key_home[:, :-1]], axis=1)
    prev_values = jnp.concatenate([head_major(prev_value_rows, BLK), value_home[:, :-1]], axis=1)
    first_block = position * local_blocks
    before = jnp.concatenate(
        [jnp.full((head_count, 1), -1, jnp.int32), cluster_ids[:, :-1]], axis=1
    )
    my_ids = lax.dynamic_slice_in_dim(cluster_ids, first_block, local_blocks, 1)
    my_before = lax.dynamic_slice_in_dim(before, first_block, local_blocks, 1)
    global_block = first_block + jnp.arange(local_blocks)
    usable_home = (global_block[None, :] >= 1) & (my_before != my_ids)
    peer_index = jnp.arange(seq_count)
    peer_head = peer_index * owned_pairs // cluster_count
    slot_range = jnp.arange(per_peer)
    local_range = jnp.arange(local_blocks)
    owner_index = (jnp.arange(head_count)[:, None] * cluster_count + my_ids) // owned_pairs
    peer_ids = jnp.take(my_ids, peer_head, axis=0)
    goes = (peer_head[:, None] * cluster_count + peer_ids) // owned_pairs == peer_index[:, None]
    send_rank = jnp.cumsum(goes.astype(jnp.int32), axis=1) - 1
    send_pick = goes[:, None, :] & (send_rank[:, None, :] == slot_range[None, :, None])
    send_block = jnp.sum(jnp.where(send_pick, local_range[None, None, :], 0), axis=2)
    send_flat = peer_head[:, None] * local_blocks + send_block
    home_rank = jnp.take_along_axis(send_rank, owner_index, axis=0)
    home_pos = owner_index * per_peer + home_rank
    pair_index = position * owned_pairs + jnp.arange(owned_pairs)
    split_for_couple = pair_index // cluster_count
    pair_cluster = pair_index % cluster_count
    my_head = position * owned_pairs // cluster_count
    split_numbers = jnp.take(cluster_ids, my_head, axis=0)
    member = split_numbers[None, :] == pair_cluster[:, None]
    member_rank = jnp.cumsum(member.astype(jnp.int32), axis=1) - 1
    member_count = jnp.sum(member.astype(jnp.int32), axis=1)
    picked = member[:, None, :] & (member_rank[:, None, :] == jnp.arange(capacity)[None, :, None])
    member_block = jnp.sum(jnp.where(picked, jnp.arange(block_count)[None, None, :], 0), axis=2)
    live_members = jnp.arange(capacity)[None, :] < member_count[:, None]
    mine = (my_head * cluster_count + split_numbers) // owned_pairs == position
    mine_grid = mine.reshape(seq_count, local_blocks)
    recv_rank = jnp.cumsum(mine_grid.astype(jnp.int32), axis=1) - 1
    recv_pos = (peer_index[:, None] * per_peer + recv_rank).reshape(block_count)
    member_pos = jnp.take(recv_pos, member_block)
    couple_softness = jnp.take(logit_softness, split_for_couple)
    pair_onehot = (split_for_couple[:, None] == jnp.arange(head_count)[None, :]).astype(jnp.float32)
    slot_pair = my_head * cluster_count + split_numbers - position * owned_pairs
    same_cluster = split_numbers[:, None] == split_numbers[None, :]
    earlier_block = jnp.arange(block_count)[None, :] < jnp.arange(block_count)[:, None]
    slot_rank = jnp.sum((same_cluster & earlier_block).astype(jnp.int32), axis=1)
    back_pos = jnp.clip(slot_pair, 0, owned_pairs - 1) * capacity + jnp.clip(
        slot_rank, 0, capacity - 1
    )
    back_grid = back_pos.reshape(seq_count, local_blocks)
    back_pick = mine_grid[:, None, :] & (recv_rank[:, None, :] == slot_range[None, :, None])
    back_flat = jnp.sum(jnp.where(back_pick, back_grid[:, None, :], 0), axis=2)

    def to_peers(array_in):
        flat = array_in.reshape((head_count * local_blocks,) + array_in.shape[2:])
        return jnp.take(flat, send_flat, axis=0)

    def members(array_in):
        flat = array_in.reshape((seq_count * per_peer,) + array_in.shape[2:])
        return jnp.take(flat, member_pos, axis=0)

    def to_owner(array_in):
        flat = array_in.reshape((owned_pairs * capacity,) + array_in.shape[2:])
        return jnp.take(flat, back_flat, axis=0)

    def from_peers(array_in):
        flat = array_in.reshape((seq_count * per_peer,) + array_in.shape[2:])
        return jnp.take(flat, home_pos, axis=0)

    raw_w, mask_w, pgrad_w, top_w, total_w, mass_w = window_parts(
        query_home,
        prev_keys,
        prev_values,
        grad_home,
        usable_home,
        neighborhood_span[:, None],
        logit_softness[:, None],
    )
    arrived = (
        lax.all_to_all(to_peers(query_home), "seq", split_axis=0, concat_axis=0, tiled=True),
        lax.all_to_all(to_peers(key_home), "seq", split_axis=0, concat_axis=0, tiled=True),
        lax.all_to_all(to_peers(value_home), "seq", split_axis=0, concat_axis=0, tiled=True),
        lax.all_to_all(to_peers(grad_home), "seq", split_axis=0, concat_axis=0, tiled=True),
    )
    arrived_stats = (
        lax.all_to_all(to_peers(top_w), "seq", split_axis=0, concat_axis=0, tiled=True),
        lax.all_to_all(to_peers(total_w), "seq", split_axis=0, concat_axis=0, tiled=True),
        lax.all_to_all(to_peers(mass_w), "seq", split_axis=0, concat_axis=0, tiled=True),
    )
    query_m, key_m, value_m, grad_m = [members(item_in) for item_in in arrived]
    top_m, total_m, mass_m = [members(item_in) for item_in in arrived_stats]

    def split_pair(pair_inputs):
        query_i, key_i, value_i, grad_i, live_i, temper_i, top_i, total_i, mass_i = pair_inputs
        query_c, log_total, row_delta, key_c, value_c, temper_c = cluster_pair(
            query_i, key_i, value_i, grad_i, live_i, temper_i, top_i, total_i, mass_i
        )
        return (
            query_c.astype(jnp.bfloat16),
            key_c.astype(jnp.bfloat16),
            value_c.astype(jnp.bfloat16),
            log_total,
            row_delta,
            temper_c,
        )

    owner_results = lax.map(
        split_pair,
        (query_m, key_m, value_m, grad_m, live_members, couple_softness, top_m, total_m, mass_m),
    )
    returned = (
        lax.all_to_all(to_owner(owner_results[0]), "seq", split_axis=0, concat_axis=0, tiled=True),
        lax.all_to_all(to_owner(owner_results[1]), "seq", split_axis=0, concat_axis=0, tiled=True),
        lax.all_to_all(to_owner(owner_results[2]), "seq", split_axis=0, concat_axis=0, tiled=True),
    )
    returned_stats = (
        lax.all_to_all(to_owner(owner_results[3]), "seq", split_axis=0, concat_axis=0, tiled=True),
        lax.all_to_all(to_owner(owner_results[4]), "seq", split_axis=0, concat_axis=0, tiled=True),
    )
    query_cluster = from_peers(returned[0])
    key_cluster = from_peers(returned[1])
    value_cluster = from_peers(returned[2])
    log_home = from_peers(returned_stats[0])
    delta_home = from_peers(returned_stats[1])
    query_w, key_w, value_w, temper_w = window_grads(
        raw_w,
        mask_w,
        pgrad_w,
        query_home,
        prev_keys,
        grad_home,
        log_home,
        delta_home,
        logit_softness[:, None],
    )
    query_out = (query_cluster.astype(jnp.float32) + lifted(query_w)).astype(jnp.bfloat16)
    key_window = key_w.astype(jnp.bfloat16)
    value_window = value_w.astype(jnp.bfloat16)
    temper_local = jnp.sum(owner_results[5][:, None] * pair_onehot, axis=0) + jnp.sum(
        temper_w, axis=1
    )
    edge_keys, edge_values = shifted((key_window[:, 0], value_window[:, 0]), "seq", -1)
    key_next = jnp.concatenate([key_window[:, 1:], edge_keys[:, None]], axis=1)
    value_next = jnp.concatenate([value_window[:, 1:], edge_values[:, None]], axis=1)
    key_out = (key_cluster.astype(jnp.float32) + key_next.astype(jnp.float32)).astype(jnp.bfloat16)
    value_out = (value_cluster.astype(jnp.float32) + value_next.astype(jnp.float32)).astype(
        jnp.bfloat16
    )
    temper_total = lax.psum(temper_local, ("seq", "dp"))
    temper_grad = temper_total / (lax.axis_size("dp") * tokens * seq_count)
    return (token_major(query_out), token_major(key_out), token_major(value_out), temper_grad)


TILE = 256
EXTRA = 16
MIB = 1024 * 1024
PIECES = 4
QUERY, KEY, VALUE, GRAD = range(4)


def columns_of(index):
    return pl.ds(pl.multiple_of(index * HD, HD), HD)


def rows_of(index):
    return pl.ds(pl.multiple_of(index * BLK, BLK), BLK)


def tile_rows(tile):
    return slice(tile * TILE, (tile + 1) * TILE)


def position(half_count):
    me = lax.axis_index("seq")
    half = jnp.where(me >= half_count, 1, 0)
    return me, half, me - half * half_count


def hop(step, half_count):
    return half_count - 1 - step if step % 2 else step


def kernel_call(
    kernel, name, operands, in_specs, out_shape, scratch, vmem_mib, flops=0, out_spaces=None,
    aliases=None,
):
    bytes_accessed = sum(
        math.prod(item.shape) * item.dtype.itemsize for item in (*operands, *out_shape)
    )
    return pl.pallas_call(
        kernel,
        out_shape=out_shape,
        in_specs=in_specs,
        out_specs=[
            pl.BlockSpec(memory_space=space)
            for space in out_spaces or [pltpu.VMEM] * len(out_shape)
        ],
        scratch_shapes=scratch,
        input_output_aliases=aliases or {},
        cost_estimate=pl.CostEstimate(
            flops=flops, bytes_accessed=bytes_accessed, transcendentals=0
        ),
        compiler_params=pltpu.CompilerParams(vmem_limit_bytes=vmem_mib * MIB),
        name=name,
    )(*operands)


def pack_kernel(*refs, half_count):
    arrays, within_ref, foreign_refs = refs[:4], refs[4], refs[5:7]
    held, within, across, arrival, left_within, left_across = refs[7:]
    me, half, _ = position(half_count)
    piece = BLK // PIECES
    arrivals = [
        [
            pltpu.make_async_copy(
                array_ref.at[0, part * piece : (part + 1) * piece, :],
                held.at[place, part * piece : (part + 1) * piece, :],
                arrival.at[place, part],
            )
            for part in range(PIECES)
        ]
        for place, array_ref in enumerate(arrays)
    ]
    for copies in arrivals:
        for copy in copies:
            copy.start()
    leaving = []
    for place, copies in enumerate(arrivals):
        for copy in copies:
            copy.wait()
        for slot, base in enumerate((half * half_count, (1 - half) * half_count)):
            rows = slice((slot * 4 + place) * BLK, (slot * 4 + place + 1) * BLK)
            for peer in range(half_count):
                within[peer, rows, :] = held[place, :, columns_of(base + peer)]
            leaving.append(
                pltpu.make_async_copy(
                    within.at[:, rows, :], within_ref.at[:, rows, :], left_within.at[place, slot]
                )
            )
            leaving[-1].start()
    first = jnp.where(half == 0, KEY, QUERY)
    second = jnp.where(half == 0, VALUE, GRAD)
    for core, foreign_ref in enumerate(foreign_refs):
        for step in range(half_count // 2):
            columns = columns_of(me ^ core ^ (half_count + hop(step, half_count)))
            across[core, step, :BLK, :] = held[first, :, columns]
            across[core, step, BLK:, :] = held[second, :, columns]
        leaving.append(pltpu.make_async_copy(across.at[core], foreign_ref, left_across.at[core]))
        leaving[-1].start()
    for copy in leaving:
        copy.wait()


def packed(arrays, half_count):
    width = arrays[0].shape[2]
    within_shape, across_shape = (half_count, 8 * BLK, HD), (half_count // 2, 2 * BLK, HD)
    return kernel_call(
        functools.partial(pack_kernel, half_count=half_count),
        "pack_heads",
        arrays,
        [pl.BlockSpec(memory_space=pl.ANY)] * 4,
        [jax.ShapeDtypeStruct(within_shape, jnp.bfloat16)]
        + [jax.ShapeDtypeStruct(across_shape, jnp.bfloat16)] * 2,
        [
            pltpu.VMEM((4, BLK, width), jnp.bfloat16),
            pltpu.VMEM(within_shape, jnp.bfloat16),
            pltpu.VMEM((2, *across_shape), jnp.bfloat16),
            pltpu.SemaphoreType.DMA((4, PIECES)),
            pltpu.SemaphoreType.DMA((4, 2)),
            pltpu.SemaphoreType.DMA((2,)),
        ],
        60,
        out_spaces=[pl.ANY] * 3,
    )


def dot_rows(left, right):
    return lax.dot_general(
        left, right, (((1,), (1,)), ((), ())), preferred_element_type=jnp.float32
    )


def dot_plain(left, right):
    return lax.dot_general(
        left, right, (((1,), (0,)), ((), ())), preferred_element_type=jnp.float32
    )


def from_blocks(ref, place):
    def rows(start, stop):
        per_tile = TILE // BLK
        return jnp.concatenate(
            [ref[block, place] for block in range(start * per_tile, stop * per_tile)],
            axis=0,
        )

    return rows


def from_array(ref, place):
    return lambda start, stop: ref[place, start * TILE : stop * TILE, :]


class Region:
    def __init__(self, square, sources, tiles, scaling, bias_ref=None, least_ref=None, first=0):
        self.square, self.sources, self.tiles, self.scaling = square, sources, tiles, scaling
        self.bias_ref, self.least_ref, self.first = bias_ref, least_ref, first

    def rows(self, which, start, stop):
        return self.sources[which](start, stop)

    def scale_of(self, array):
        return 1.0 if array == VALUE else self.scaling[:, :HD]

    def keys_of(self, tile):
        return range(self.tiles if self.square else tile + 1)

    def scores(self, tile_key, tile_query):
        per_tile = TILE // BLK
        scores = dot_rows(
            self.rows(KEY, tile_key, tile_key + 1), self.rows(QUERY, tile_query, tile_query + 1)
        ) * (self.scaling * math.log2(math.e))
        before = self.tiles * per_tile if self.square else 0
        rows = []
        for sub_key in range(per_tile):
            key_block = tile_key * per_tile + sub_key
            pieces = []
            for sub_query in range(per_tile):
                query_block = tile_query * per_tile + sub_query
                lanes = slice(sub_query * BLK, (sub_query + 1) * BLK)
                piece = scores[sub_key * BLK : (sub_key + 1) * BLK, lanes]
                apart = before + query_block - key_block
                if apart < 0:
                    piece = jnp.full_like(piece, blocked_score)
                elif apart == 0:
                    piece = jnp.where(key_minus_query() <= 0, piece, blocked_score)
                elif apart == 1:
                    row = self.first + (0 if self.square else key_block)
                    least = self.least_ref[row : row + 1, :]
                    piece = jnp.where(key_minus_query() > least, piece, blocked_score)
                else:
                    at = slice(query_block * BLK, (query_block + 1) * BLK)
                    piece = piece + self.bias_ref[key_block : key_block + 1, at]
                pieces.append(piece)
            rows.append(jnp.concatenate(pieces, axis=1))
        return jnp.concatenate(rows, axis=0)


def diagonal(slot, arrived_ref, scales_ref, bias_ref=None, least_ref=None):
    blocks = arrived_ref.shape[0]
    sources = [from_blocks(arrived_ref, slot * 4 + place) for place in range(4)]
    bias = None if bias_ref is None else bias_ref.at[slot]
    first = slot * (blocks - 1)
    scaling = scales_ref[slot : slot + 1, :]
    return Region(False, sources, blocks * BLK // TILE, scaling, bias, least_ref, first)


def square(square_ref, scales_ref, bias_ref=None, least_ref=None):
    tiles = square_ref.shape[1] // TILE
    sources = [from_array(square_ref, place) for place in range(4)]
    bias = None if bias_ref is None else bias_ref.at[2]
    first = 2 * (tiles * TILE // BLK - 1)
    return Region(True, sources, tiles, scales_ref[0:1, :], bias, least_ref, first)


def key_minus_query():
    shape = (BLK, BLK)
    return lax.broadcasted_iota(jnp.int32, shape, 0) - lax.broadcasted_iota(jnp.int32, shape, 1)


def statistics(region, weight_ref, towards_ref, out_ref, first_row):
    for tile in range(region.tiles):
        here = tile_rows(tile)
        top = jnp.full((1, TILE), blocked_score, jnp.float32)
        for other in region.keys_of(tile):
            raw = region.scores(other, tile)
            weight_ref[tile_rows(other), here] = raw
            top = jnp.maximum(top, jnp.max(raw, axis=0, keepdims=True))
        sums = [jnp.zeros((1, TILE), jnp.float32)] * 4
        for other in region.keys_of(tile):
            there = tile_rows(other)
            raw = weight_ref[there, here]
            weight = jnp.exp2(raw - top)
            towards = dot_rows(
                region.rows(VALUE, other, other + 1), region.rows(GRAD, tile, tile + 1)
            )
            weight_ref[there, here] = weight
            towards_ref[there, here] = towards
            pulled, weighted = weight * towards, weight * raw
            terms = (weight, pulled, pulled * raw, weighted)
            sums = [
                total + jnp.sum(term, axis=0, keepdims=True) for total, term in zip(sums, terms)
            ]
        for row, value in enumerate((top, *sums)):
            out_ref[first_row + row : first_row + row + 1, here] = value


def gradients(
    region, weight_ref, towards_ref, top, log_total, delta, prob_low, grad_low, keys_flat, emit=None
):
    keys_flat[...] = region.rows(KEY, 0, region.tiles).T
    share = jnp.exp2(top - log_total)
    query_parts, key_parts, value_parts = [], [], []
    for tile in range(region.tiles):
        here = tile_rows(tile)
        for other in region.keys_of(tile):
            there = tile_rows(other)
            probability = weight_ref[there, here] * share[:, here]
            prob_low[there, here] = probability.astype(jnp.bfloat16)
            grad_low[there, here] = (
                probability * (towards_ref[there, here] - delta[:, here])
            ).astype(jnp.bfloat16)
        upto = slice(0, len(region.keys_of(tile)) * TILE)
        query_parts.append(dot_plain(keys_flat[:, upto], grad_low[upto, here]).T)
    if emit is not None:
        emit(QUERY, query_parts)
    for low, which, parts in ((grad_low, QUERY, key_parts), (prob_low, GRAD, value_parts)):
        for tile in range(region.tiles):
            first = 0 if region.square else tile
            onward = slice(first * TILE, region.tiles * TILE)
            parts.append(
                dot_plain(low[tile_rows(tile), onward], region.rows(which, first, region.tiles))
            )
        if emit is not None:
            emit(KEY if which == QUERY else VALUE, parts)
    return query_parts, key_parts, value_parts


def merged(first, second):
    top = jnp.maximum(first[0], second[0])
    left, right = jnp.exp2(first[0] - top), jnp.exp2(second[0] - top)
    total = first[1] * left + second[1] * right
    mass = first[2] * left + second[2] * right
    return top + jnp.log2(total), mass / total


def alone(rows):
    return rows[0] + jnp.log2(rows[1]), rows[2] / rows[1]


def rows_at(ref, first, count=5):
    return [ref[first + row : first + row + 1, :] for row in range(count)]


def temper_terms(rows, totals, scale_row):
    log_total, delta = totals
    terms = (rows[3] - delta * rows[4]) * jnp.exp2(rows[0] - log_total)
    folded = sum(terms[:, start : start + HD] for start in range(0, terms.shape[1], HD))
    return folded / (scale_row[:, :HD] * (math.sqrt(HD) * math.log2(math.e)))


def put(within_ref, array, tile, value):
    per_tile = TILE // BLK
    for sub in range(per_tile):
        within_ref[tile * per_tile + sub, array * BLK : (array + 1) * BLK, :] = value[
            sub * BLK : (sub + 1) * BLK, :
        ].astype(jnp.bfloat16)


def scaled(region, parts):
    scale = region.scaling[:, :HD]
    return [[value * scale for value in part] for part in parts[:2]] + [parts[2]]


def masks_kernel(softness_ref, ids_ref, span_ref, scales_ref, bias_ref, least_ref, *, half_count):
    me, half, _ = position(half_count)
    base = half * half_count
    regions = (
        (me, base, base),
        (me ^ half_count, base, base),
        (me, 0, half_count),
    )
    for slot, (head, key_base, query_base) in enumerate(regions):
        if slot < 2:
            scales_ref[slot : slot + 1, :] = jnp.full(
                (1, TILE), softness_ref[head] * (1.0 / math.sqrt(HD)), jnp.float32
            )

        def same(key_block, query_block):
            return ids_ref[head, key_base + key_block] == ids_ref[head, query_base + query_block]

        def bias(key_block, query_block):
            return jnp.full(
                (1, BLK), jnp.where(same(key_block, query_block), 0.0, blocked_score), jnp.float32
            )

        for key_block in range(half_count):
            bias_ref[slot, key_block : key_block + 1, :] = jnp.concatenate(
                [bias(key_block, query_block) for query_block in range(half_count)], axis=1
            )
        pairs = [(block, block + 1) for block in range(half_count - 1)]
        if slot == 2:
            pairs = [(half_count - 1, 0)]
        for place, pair in enumerate(pairs):
            least = jnp.where(same(*pair), -BLK, BLK - span_ref[head])
            row = slot * (half_count - 1) + place
            least_ref[row : row + 1, :] = jnp.full((1, BLK), least, jnp.int32)


def within_kernel(
    arrived_ref, scales_ref, bias_ref, least_ref, stats_ref, parts_ref, own_weight, own_towards, other_weight, other_towards, *scratch, half_count
):
    _, half, _ = position(half_count)
    kept = ((own_weight, own_towards), (other_weight, other_towards))
    for slot in range(2):
        region = diagonal(slot, arrived_ref, scales_ref, bias_ref, least_ref)
        statistics(region, *kept[slot], stats_ref, slot * 5)

    @pl.when(half == 0)
    def _():
        region = diagonal(0, arrived_ref, scales_ref)
        single = alone(rows_at(stats_ref, 0))
        parts = gradients(region, *kept[0], stats_ref[0:1, :], *single, *scratch)
        for place, tiles in enumerate(scaled(region, parts)):
            for tile, value in enumerate(tiles):
                parts_ref[place, tile_rows(tile), :] = value


def square_kernel(arrived_ref, scales_ref, bias_ref, least_ref, stats_ref, *refs, half_count):
    across_refs = refs[: half_count // 2]
    square_ref, message_ref, square_stats, weight, towards = refs[half_count // 2 :]
    _, half, place = position(half_count)
    first = jnp.where(half == 0, QUERY, KEY)
    second = jnp.where(half == 0, GRAD, VALUE)
    for step, across_ref in enumerate(across_refs):
        for core in range(2):
            rows = rows_of(place ^ core ^ hop(step, half_count))
            square_ref[first, rows, :] = across_ref[core, :BLK, :]
            square_ref[second, rows, :] = across_ref[core, BLK:, :]
    for kept in (jnp.where(half == 0, KEY, QUERY), jnp.where(half == 0, VALUE, GRAD)):
        for block in range(half_count):
            square_ref[kept, block * BLK : (block + 1) * BLK, :] = arrived_ref[block, kept]
    region = square(square_ref, scales_ref, bias_ref, least_ref)
    statistics(region, weight, towards, square_stats, 0)
    own, other, crossing = rows_at(stats_ref, 0), rows_at(stats_ref, 5), rows_at(square_stats, 0)
    for row in range(5):
        message_ref[row : row + 1, :] = jnp.where(half == 0, crossing[row], other[row])
    own_scale, other_scale = scales_ref[0:1, :], scales_ref[1:2, :]
    both = merged(own, crossing)
    whole = temper_terms(own, both, own_scale) + temper_terms(crossing, both, own_scale)
    single = temper_terms(own, alone(own), own_scale)
    message_ref[5:6, :HD] = jnp.where(half == 0, single, whole)
    message_ref[6:7, :HD] = temper_terms(other, alone(other), other_scale)


def first_kernel(
    arrived_ref, scales_ref, square_ref, stats_ref, square_stats,
    own_weight, own_towards, other_weight, other_towards, square_weight, square_towards,
    across_ref, within_ref, ready, ready_sem, *scratch, half_count
):
    _, half, _ = position(half_count)
    leaving = sends(ready, within_ref, ready_sem, (1 - half) * 3)

    @pl.when(half == 0)
    def _():
        region = diagonal(1, arrived_ref, scales_ref)

        def send(array, parts):
            for tile, part in enumerate(parts):
                put(ready, array, tile, part * region.scale_of(array))
            leaving[array].start()

        totals = alone(rows_at(stats_ref, 5))
        gradients(
            region, other_weight, other_towards, stats_ref[5:6, :], *totals, *scratch, emit=send
        )

    @pl.when(half == 1)
    def _():
        totals = merged(rows_at(stats_ref, 0), rows_at(square_stats, 0))
        region = square(square_ref, scales_ref)
        parts = gradients(
            region, square_weight, square_towards, square_stats[0:1, :], *totals, *scratch
        )
        across_query, *foreign = scaled(region, parts)
        for array, tiles in enumerate(foreign):
            for tile, value in enumerate(tiles):
                across_ref[array, tile_rows(tile), :] = value.astype(jnp.bfloat16)
        region = diagonal(0, arrived_ref, scales_ref)

        def send(array, parts):
            for tile, part in enumerate(parts):
                value = part * region.scale_of(array)
                put(ready, array, tile, value + across_query[tile] if array == QUERY else value)
            leaving[array].start()

        gradients(
            region, own_weight, own_towards, stats_ref[0:1, :], *totals, *scratch, emit=send
        )

    for copy in leaving:
        copy.wait()


def sends(ready, within_ref, sems, first):
    copies = []
    for array in range(3):
        rows = slice(array * BLK, (array + 1) * BLK)
        copies.append(
            pltpu.make_async_copy(
                ready.at[:, rows, :], within_ref.at[:, rows_of(first + array), :], sems.at[array]
            )
        )
    return copies


def temper_rows(own, other):
    row = lax.broadcasted_iota(jnp.int32, (EXTRA, HD), 0)
    rows = jnp.zeros((EXTRA, HD), jnp.float32)
    for place, terms in enumerate((own, other)):
        rest = jnp.broadcast_to(jnp.sum(terms, axis=1, keepdims=True), (EXTRA, HD))
        for piece in range(3):
            high = rest.astype(jnp.bfloat16).astype(jnp.float32)
            rows = jnp.where(row == place * 3 + piece, high, rows)
            rest = rest - high
    return rows.astype(jnp.bfloat16)


def finish_kernel(
    arrived_ref, scales_ref, square_ref, message_ref, received_ref, stats_ref, square_stats,
    parts_ref, square_weight, square_towards, other_weight, other_towards, across_ref, begun_ref,
    within_ref, *refs, half_count
):
    del begun_ref
    chunk_refs = refs[:2]
    across, ready, tail, ready_sem, tail_sem, *scratch = refs[2:]
    _, half, place = position(half_count)
    leaving = sends(ready, within_ref, ready_sem, half * 3)
    sent, came = rows_at(message_ref, 0), rows_at(received_ref, 0)
    totals = merged(sent, came)
    scale = jnp.where(half == 0, scales_ref[0:1, :], scales_ref[1:2, :])
    shared = temper_terms(sent, totals, scale) + temper_terms(came, totals, scale)
    mine, theirs = message_ref[5:6, :HD], received_ref[5:6, :HD]
    own = mine + jnp.where(half == 0, shared, received_ref[6:7, :HD])
    other = theirs + jnp.where(half == 0, message_ref[6:7, :HD], shared)
    pieces = temper_rows(own, other)
    for block in range(half_count):
        tail[block] = pieces
    leaving.append(
        pltpu.make_async_copy(tail, within_ref.at[:, 6 * BLK : 6 * BLK + EXTRA, :], tail_sem)
    )
    leaving[-1].start()

    def chunks():
        for core, chunk_ref in enumerate(chunk_refs):
            for step in range(half_count // 2):
                yield step, chunk_ref, rows_of(place ^ core ^ hop(step, half_count))

    @pl.when(half == 0)
    def _():
        region = square(square_ref, scales_ref)

        def send(array, parts):
            for tile, part in enumerate(parts):
                here = tile_rows(tile)
                value = part * region.scale_of(array)
                if array == QUERY:
                    across[here, :] = value.astype(jnp.bfloat16)
                    put(ready, array, tile, parts_ref[array, here, :])
                else:
                    put(ready, array, tile, parts_ref[array, here, :] + value)
            leaving[array].start()

        gradients(
            region, square_weight, square_towards, square_stats[0:1, :], *totals, *scratch, emit=send
        )
        for step, chunk_ref, rows in chunks():
            chunk_ref[step, :BLK, :] = across[rows, :]
            chunk_ref[step, BLK:, :] = jnp.zeros((BLK, HD), jnp.bfloat16)

    @pl.when(half == 1)
    def _():
        region = diagonal(1, arrived_ref, scales_ref)

        def send(array, parts):
            for tile, part in enumerate(parts):
                put(ready, array, tile, part * region.scale_of(array))
            leaving[array].start()

        gradients(
            region, other_weight, other_towards, stats_ref[5:6, :], *totals, *scratch, emit=send
        )
        for step, chunk_ref, rows in chunks():
            chunk_ref[step, :BLK, :] = across_ref[0, rows, :]
            chunk_ref[step, BLK:, :] = across_ref[1, rows, :]

    for copy in leaving:
        copy.wait()


def temper_kernel(within_ref, temper_ref, *, half_count):
    _, half, _ = position(half_count)
    for peer in range(half_count):
        for slot, base in enumerate((half * half_count, (1 - half) * half_count)):
            rows = within_ref[peer, 3 * slot : 3 * slot + 3, :].astype(jnp.float32)
            temper_ref[pl.ds(base + peer, 1), :] = jnp.sum(rows, axis=0, keepdims=True)


def temper_sums(within, half_count):
    last = 6 * BLK // EXTRA
    return pl.pallas_call(
        functools.partial(temper_kernel, half_count=half_count),
        grid=(1,),
        out_shape=jax.ShapeDtypeStruct((2 * half_count, HD), jnp.float32),
        in_specs=[pl.BlockSpec((half_count, EXTRA, HD), lambda step: (0, last, 0))],
        out_specs=pl.BlockSpec((2 * half_count, HD), lambda step: (0, 0)),
        compiler_params=pltpu.CompilerParams(vmem_limit_bytes=4 * MIB),
        name="temper_sums",
    )(within)


def own_columns_kernel(within_ref, *refs, half_count):
    out_refs, (staged, sems) = refs[:3], refs[3:]
    _, half, _ = position(half_count)
    width = half_count * HD
    for array in range(6):
        for peer in range(half_count):
            staged[array, :, peer * HD : (peer + 1) * HD] = within_ref[
                peer, array * BLK : (array + 1) * BLK, :
            ]

    def copies(arrays):
        return [
            pltpu.make_async_copy(
                staged.at[array],
                out_refs[array % 3].at[0, :, side(half if array < 3 else 1 - half, width)],
                sems.at[array],
            )
            for array in arrays
        ]

    for role, arrays in enumerate(((0, 1, 2, 3), (0, 1, 2, 4, 5))):

        @pl.when(half == role)
        def _():
            leaving = copies(arrays)
            for copy in leaving:
                copy.start()
            for copy in leaving:
                copy.wait()


def side(half, width):
    return pl.ds(pl.multiple_of(half * width, width), width)


def other_columns_kernel(within_ref, *refs, half_count):
    messages = half_count // 2
    across_refs = refs[:messages]
    out_refs, (staged, sems) = refs[messages + 3 : messages + 6], refs[messages + 6 :]
    _, half, place = position(half_count)

    for role, arrays in enumerate(((1, 2), (0,))):

        @pl.when(half == role)
        def _():
            leaving = []
            for step, across_ref in enumerate(across_refs):
                pair = (place ^ hop(step, half_count)) >> 1
                for part, array in enumerate(arrays):
                    rows = slice(part * BLK, (part + 1) * BLK)
                    for core in range(2):
                        peer = place ^ core ^ hop(step, half_count)
                        kept = within_ref[peer, (3 + array) * BLK : (4 + array) * BLK, :]
                        total = kept.astype(jnp.float32) + across_ref[core, rows, :].astype(
                            jnp.float32
                        )
                        staged[part, :, columns_of(peer)] = total.astype(jnp.bfloat16)
                    start = (1 - role) * messages + pair
                    leaving.append(
                        pltpu.make_async_copy(
                            staged.at[part, :, side(pair, 2 * HD)],
                            out_refs[array].at[0, :, side(start, 2 * HD)],
                            sems.at[step, part],
                        )
                    )
                    leaving[-1].start()
            for copy in leaving:
                copy.wait()


def join_kernel(kept_ref, taken_ref, *out_refs):
    for step, out_ref in enumerate(out_refs):
        out_ref[0] = kept_ref[step]
        out_ref[1] = taken_ref[step]


def crossed(kept, given, half_count):
    devices = range(2 * half_count)
    steps, *shape = kept.shape
    taken = lax.ppermute(given, "seq", [(source, source ^ 1) for source in devices])
    messages = kernel_call(
        join_kernel,
        "join_chunks",
        (kept, taken),
        [pl.BlockSpec(memory_space=pltpu.VMEM)] * 2,
        [jax.ShapeDtypeStruct((2, *shape), jnp.bfloat16)] * steps,
        [],
        4,
    )
    return [
        lax.ppermute(
            message, "seq", [(source, source ^ (half_count + hop(step, half_count))) for source in devices]
        )
        for step, message in enumerate(messages)
    ]


def head_shards(
    probe_vectors,
    lookup_vectors,
    content_vectors,
    result_cotangent,
    logit_softness,
    block_grouping,
    neighborhood_span,
):
    seq_count, dp_count = lax.axis_size("seq"), lax.axis_size("dp")
    half_count = seq_count // 2
    tokens = half_count * BLK
    groups = [list(range(half_count)), list(range(half_count, seq_count))]
    settings = (logit_softness, block_grouping[0, :, :, 0], neighborhood_span)
    smem, vmem = pl.BlockSpec(memory_space=pltpu.SMEM), pl.BlockSpec(memory_space=pltpu.VMEM)
    lows = [pltpu.VMEM((tokens, tokens), jnp.bfloat16)] * 2 + [
        pltpu.VMEM((HD, tokens), jnp.bfloat16)
    ]
    rows_of_stats = jax.ShapeDtypeStruct((8, tokens), jnp.float32)
    pairs = jax.ShapeDtypeStruct((tokens, tokens), jnp.float32)
    pair_flops = 2 * tokens * tokens * HD

    def exchange_within(array_in):
        return lax.all_to_all(
            array_in, "seq", split_axis=0, concat_axis=0, axis_index_groups=groups, tiled=True
        )

    def call(
        kernel, name, operands, out_shape, scratch, flops, vmem_mib, scalars=(), out_spaces=None,
        last_in_place=False,
    ):
        in_specs = [smem] * len(scalars) + [vmem] * len(operands)
        if last_in_place:
            in_specs[-1] = pl.BlockSpec(memory_space=pl.ANY)
        return kernel_call(
            functools.partial(kernel, half_count=half_count),
            name,
            (*scalars, *operands),
            in_specs,
            out_shape,
            scratch,
            vmem_mib,
            flops,
            out_spaces,
            {len(operands) - 1: 0} if last_in_place else {},
        )

    sent, *foreign = packed(
        (probe_vectors, lookup_vectors, content_vectors, result_cotangent), half_count
    )
    arrived = exchange_within(sent).reshape(half_count, 8, BLK, HD)
    kept_parts = jax.ShapeDtypeStruct((3, tokens, HD), jnp.float32)
    masks = call(
        masks_kernel,
        "scales_and_masks",
        (),
        [
            jax.ShapeDtypeStruct((8, TILE), jnp.float32),
            jax.ShapeDtypeStruct((3, half_count, tokens), jnp.float32),
            jax.ShapeDtypeStruct((2 * half_count, BLK), jnp.int32),
        ],
        [],
        0,
        2,
        settings,
    )
    foreign[0], *masks = lax.optimization_barrier((foreign[0], *masks))
    foreign = crossed(*foreign, half_count)
    scales = masks[0]
    stats, parts, own_weight, own_towards, other_weight, other_towards = call(
        within_kernel,
        "diagonal_statistics",
        (arrived, *masks),
        [jax.ShapeDtypeStruct((16, tokens), jnp.float32), kept_parts] + [pairs] * 4,
        lows,
        2 * pair_flops,
        14,
    )
    squared, message, square_stats, square_weight, square_towards = call(
        square_kernel,
        "square_statistics",
        (arrived, *masks, stats, *foreign),
        [jax.ShapeDtypeStruct((4, tokens, HD), jnp.bfloat16)] + [rows_of_stats] * 2 + [pairs] * 2,
        [],
        2 * pair_flops,
        8,
    )
    swap = [(source, source ^ half_count) for source in range(seq_count)]
    received = lax.ppermute(message, "seq", swap)
    result = pltpu.HBM((half_count, 6 * BLK + EXTRA, HD), jnp.bfloat16)
    ready = pltpu.VMEM((half_count, 3 * BLK, HD), jnp.bfloat16)
    across, begun = call(
        first_kernel,
        "gradients_before_totals",
        (
            arrived, scales, squared, stats, square_stats, own_weight, own_towards,
            other_weight, other_towards, square_weight, square_towards,
        ),
        [jax.ShapeDtypeStruct((2, tokens, HD), jnp.bfloat16), result],
        [ready, pltpu.SemaphoreType.DMA((3,)), *lows],
        4 * pair_flops,
        14,
        out_spaces=(pltpu.VMEM, pl.ANY),
    )
    operands = (
        arrived, scales, squared, message, received, stats, square_stats, parts,
        square_weight, square_towards, other_weight, other_towards, across, begun,
    )
    within, *foreign = call(
        finish_kernel,
        "gradients_after_totals",
        operands,
        [result]
        + [jax.ShapeDtypeStruct((half_count // 2, 2 * BLK, HD), jnp.bfloat16)] * 2,
        [
            pltpu.VMEM((tokens, HD), jnp.bfloat16), ready,
            pltpu.VMEM((half_count, EXTRA, HD), jnp.bfloat16),
            pltpu.SemaphoreType.DMA((3,)), pltpu.SemaphoreType.DMA, *lows,
        ],
        2 * pair_flops,
        16,
        out_spaces=(pl.ANY, pltpu.VMEM, pltpu.VMEM),
        last_in_place=True,
    )
    across = crossed(*foreign, half_count)
    within = exchange_within(within)
    tempers = temper_sums(within, half_count)
    temper_total = tempers
    for step in range(1, dp_count):
        swap = [(source, (source + step) % dp_count) for source in range(dp_count)]
        temper_total = temper_total + lax.ppermute(tempers, "dp", swap)
    temper = temper_total[:, 0] / (dp_count * BLK * seq_count)
    result = [pltpu.HBM(probe_vectors.shape, jnp.bfloat16)] * 3
    width = half_count * HD
    outs = kernel_call(
        functools.partial(own_columns_kernel, half_count=half_count),
        "unpack_own",
        (within,),
        [vmem],
        result,
        [pltpu.VMEM((6, BLK, width), jnp.bfloat16), pltpu.SemaphoreType.DMA((6,))],
        6,
        out_spaces=[pl.ANY] * 3,
    )
    across[0], temper = lax.optimization_barrier((across[0], temper))
    outs = kernel_call(
        functools.partial(other_columns_kernel, half_count=half_count),
        "unpack_other",
        (within, *across, *outs),
        [vmem] * (1 + len(across)) + [pl.BlockSpec(memory_space=pl.ANY)] * 3,
        result,
        [pltpu.VMEM((2, BLK, width), jnp.bfloat16), pltpu.SemaphoreType.DMA((len(across), 2))],
        6,
        out_spaces=[pl.ANY] * 3,
        aliases={1 + len(across) + array: array for array in range(3)},
    )
    return (*outs, temper)


def shards(
    probe_vectors,
    lookup_vectors,
    content_vectors,
    result_cotangent,
    logit_softness,
    block_grouping,
    neighborhood_span,
):
    head_count = probe_vectors.shape[2] // HD
    seq_count = lax.axis_size("seq")
    one_block = probe_vectors.shape[1] == BLK
    whole_tiles = seq_count * BLK % (2 * TILE) == 0 and seq_count & (seq_count - 1) == 0
    if head_count == seq_count and one_block and whole_tiles:
        plan = head_shards
    else:
        plan = clustered_shards
    return plan(
        probe_vectors,
        lookup_vectors,
        content_vectors,
        result_cotangent,
        logit_softness,
        block_grouping,
        neighborhood_span,
    )


def solution(mesh):
    in_specs = (
        P("dp", "seq", None),
        P("dp", "seq", None),
        P("dp", "seq", None),
        P("dp", "seq", None),
        P(),
        P("dp", None, None, None),
        P(),
    )
    out_specs = (P("dp", "seq", None), P("dp", "seq", None), P("dp", "seq", None), P())
    return jax.shard_map(shards, mesh=mesh, in_specs=in_specs, out_specs=out_specs, check_vma=False)
```

```python
import functools
import math

import jax
import jax.numpy as jnp
from jax import lax
from jax.experimental import pallas as pl
from jax.experimental.pallas import tpu as pltpu
from jax.sharding import PartitionSpec as P

HD = 128
BLK = 128


blocked_score = -1e30


def shifted(value, axis, steps):
    count = lax.axis_size(axis)
    first, last = (max(0, -steps), min(count, count - steps))
    return lax.ppermute(value, axis, [(source, source + steps) for source in range(first, last)])


def lifted(array_in):
    return lax.optimization_barrier(array_in.astype(jnp.bfloat16)).astype(jnp.float32)


def head_major(tokens_in, block_len):
    token_count, feature_count = tokens_in.shape
    return tokens_in.reshape(
        token_count // block_len, block_len, feature_count // HD, HD
    ).transpose(2, 0, 1, 3)


def token_major(blocks_in):
    head_count, block_count, block_len, depth = blocks_in.shape
    return blocks_in.transpose(1, 2, 0, 3).reshape(1, block_count * block_len, head_count * depth)


def window_parts(query_block, prev_keys, prev_values, grad_block, usable, window_width, temper):
    block_len = query_block.shape[-2]
    inverse_root = 1.0 / math.sqrt(query_block.shape[-1])
    raw_scores = (
        jnp.einsum("...td,...sd->...ts", query_block, prev_keys, preferred_element_type=jnp.float32)
        * inverse_root
    )
    query_pos = lax.broadcasted_iota(jnp.int32, (block_len, block_len), 0)
    key_pos = lax.broadcasted_iota(jnp.int32, (block_len, block_len), 1)
    pair_mask = usable[..., None, None] & (
        key_pos > query_pos + block_len - window_width[..., None, None]
    )
    scores = temper[..., None, None] * raw_scores
    row_top = jnp.max(jnp.where(pair_mask, scores, blocked_score), axis=-1)
    weights = jnp.where(pair_mask, jnp.exp(scores - row_top[..., None]), 0.0)
    prob_grad = jnp.einsum(
        "...td,...sd->...ts", grad_block, prev_values, preferred_element_type=jnp.float32
    )
    return (
        raw_scores,
        pair_mask,
        prob_grad,
        row_top,
        jnp.sum(weights, axis=-1),
        jnp.sum(weights * prob_grad, axis=-1),
    )


def window_grads(
    raw_scores,
    pair_mask,
    prob_grad,
    query_block,
    prev_keys,
    grad_block,
    log_total,
    row_delta,
    temper,
):
    inverse_root = 1.0 / math.sqrt(query_block.shape[-1])
    scaling = (temper * inverse_root)[..., None, None]
    probability = jnp.where(
        pair_mask, jnp.exp(temper[..., None, None] * raw_scores - log_total[..., None]), 0.0
    )
    score_grad = probability * (prob_grad - row_delta[..., None])
    prob_low = probability.astype(jnp.bfloat16)
    grad_low = score_grad.astype(jnp.bfloat16)
    query_part = (
        jnp.einsum("...ts,...sd->...td", grad_low, prev_keys, preferred_element_type=jnp.float32)
        * scaling
    )
    key_part = (
        jnp.einsum("...ts,...td->...sd", grad_low, query_block, preferred_element_type=jnp.float32)
        * scaling
    )
    value_part = jnp.einsum(
        "...ts,...td->...sd", prob_low, grad_block, preferred_element_type=jnp.float32
    )
    temper_part = jnp.sum(score_grad * raw_scores, axis=(-2, -1))
    return (query_part, key_part, value_part, temper_part)


def cluster_pair(
    query_items,
    key_items,
    value_items,
    grad_items,
    live_items,
    temper,
    window_top,
    window_total,
    window_mass,
):
    item_count, block_len, depth = query_items.shape
    row_count = item_count * block_len
    group_rows = 4 * block_len
    inverse_root = 1.0 / math.sqrt(depth)
    scaling = temper * inverse_root
    query_rows = query_items.reshape(row_count, depth)
    key_rows = key_items.reshape(row_count, depth)
    value_rows = value_items.reshape(row_count, depth)
    grad_rows = grad_items.reshape(row_count, depth)
    key_item = jnp.arange(row_count) // block_len
    key_token = jnp.arange(row_count) % block_len
    live_rows = jnp.repeat(live_items, block_len)
    top_rows = window_top.reshape(row_count)
    total_rows = window_total.reshape(row_count)
    mass_rows = window_mass.reshape(row_count)

    def group_step(carry, start_row):
        key_acc, value_acc, temper_acc = carry
        query_group = lax.dynamic_slice_in_dim(query_rows, start_row, group_rows, 0)
        grad_group = lax.dynamic_slice_in_dim(grad_rows, start_row, group_rows, 0)
        group_live = lax.dynamic_slice_in_dim(live_rows, start_row, group_rows, 0)
        group_top = lax.dynamic_slice_in_dim(top_rows, start_row, group_rows, 0)
        group_total = lax.dynamic_slice_in_dim(total_rows, start_row, group_rows, 0)
        group_mass = lax.dynamic_slice_in_dim(mass_rows, start_row, group_rows, 0)
        query_item = (start_row + jnp.arange(group_rows)) // block_len
        query_token = jnp.arange(group_rows) % block_len
        earlier = (key_item[None, :] < query_item[:, None]) | (
            key_item[None, :] == query_item[:, None]
        ) & (key_token[None, :] <= query_token[:, None])
        pair_mask = group_live[:, None] & live_rows[None, :] & earlier
        raw_scores = (
            lax.dot_general(
                query_group, key_rows, (((1,), (1,)), ((), ())), preferred_element_type=jnp.float32
            )
            * inverse_root
        )
        scores = temper * raw_scores
        row_top = jnp.maximum(
            jnp.max(jnp.where(pair_mask, scores, blocked_score), axis=1), group_top
        )
        weights = jnp.where(pair_mask, jnp.exp(scores - row_top[:, None]), 0.0)
        row_total = jnp.sum(weights, axis=1) + group_total * jnp.exp(group_top - row_top)
        log_total = row_top + jnp.log(jnp.where(group_live, row_total, 1.0))
        probability = jnp.where(pair_mask, jnp.exp(scores - log_total[:, None]), 0.0)
        prob_grad = lax.dot_general(
            grad_group, value_rows, (((1,), (1,)), ((), ())), preferred_element_type=jnp.float32
        )
        row_delta = jnp.sum(probability * prob_grad, axis=1) + group_mass * jnp.exp(
            group_top - log_total
        )
        score_grad = probability * (prob_grad - row_delta[:, None])
        prob_low = probability.astype(jnp.bfloat16)
        grad_low = score_grad.astype(jnp.bfloat16)
        query_part = jnp.dot(grad_low, key_rows, preferred_element_type=jnp.float32) * scaling
        key_acc = (
            key_acc
            + lax.dot_general(
                grad_low, query_group, (((0,), (0,)), ((), ())), preferred_element_type=jnp.float32
            )
            * scaling
        )
        value_acc = value_acc + lax.dot_general(
            prob_low, grad_group, (((0,), (0,)), ((), ())), preferred_element_type=jnp.float32
        )
        temper_acc = temper_acc + jnp.sum(score_grad * raw_scores)
        return ((key_acc, value_acc, temper_acc), (query_part, log_total, row_delta))

    start_rows = jnp.arange(item_count // 4) * group_rows
    initial = (
        jnp.zeros((row_count, depth), jnp.float32),
        jnp.zeros((row_count, depth), jnp.float32),
        jnp.zeros((), jnp.float32),
    )
    (key_acc, value_acc, temper_acc), (query_part, log_total, row_delta) = lax.scan(
        group_step, initial, start_rows
    )
    return (
        query_part.reshape(item_count, block_len, depth),
        log_total.reshape(item_count, block_len),
        row_delta.reshape(item_count, block_len),
        key_acc.reshape(item_count, block_len, depth),
        value_acc.reshape(item_count, block_len, depth),
        temper_acc,
    )


def clustered_shards(
    probe_vectors,
    lookup_vectors,
    content_vectors,
    result_cotangent,
    logit_softness,
    block_grouping,
    neighborhood_span,
):
    seq_count = lax.axis_size("seq")
    position = lax.axis_index("seq")
    tokens = probe_vectors.shape[1]
    head_count = probe_vectors.shape[2] // HD
    local_blocks = tokens // BLK
    block_count = local_blocks * seq_count
    cluster_count = max(1, block_count // 8)
    capacity = min(12, block_count)
    owned_pairs = cluster_count * head_count // seq_count
    group_count = cluster_count // owned_pairs
    per_peer = max(1, local_blocks // group_count)
    cluster_ids = block_grouping[0, :, :, 0]
    query_home = head_major(probe_vectors[0], BLK)
    key_home = head_major(lookup_vectors[0], BLK)
    value_home = head_major(content_vectors[0], BLK)
    grad_home = head_major(result_cotangent[0], BLK)
    last_block = (lookup_vectors[0, tokens - BLK :], content_vectors[0, tokens - BLK :])
    prev_key_rows, prev_value_rows = shifted((last_block[0], last_block[1]), "seq", 1)
    prev_keys = jnp.concatenate([head_major(prev_key_rows, BLK), key_home[:, :-1]], axis=1)
    prev_values = jnp.concatenate([head_major(prev_value_rows, BLK), value_home[:, :-1]], axis=1)
    first_block = position * local_blocks
    before = jnp.concatenate(
        [jnp.full((head_count, 1), -1, jnp.int32), cluster_ids[:, :-1]], axis=1
    )
    my_ids = lax.dynamic_slice_in_dim(cluster_ids, first_block, local_blocks, 1)
    my_before = lax.dynamic_slice_in_dim(before, first_block, local_blocks, 1)
    global_block = first_block + jnp.arange(local_blocks)
    usable_home = (global_block[None, :] >= 1) & (my_before != my_ids)
    peer_index = jnp.arange(seq_count)
    peer_head = peer_index * owned_pairs // cluster_count
    slot_range = jnp.arange(per_peer)
    local_range = jnp.arange(local_blocks)
    owner_index = (jnp.arange(head_count)[:, None] * cluster_count + my_ids) // owned_pairs
    peer_ids = jnp.take(my_ids, peer_head, axis=0)
    goes = (peer_head[:, None] * cluster_count + peer_ids) // owned_pairs == peer_index[:, None]
    send_rank = jnp.cumsum(goes.astype(jnp.int32), axis=1) - 1
    send_pick = goes[:, None, :] & (send_rank[:, None, :] == slot_range[None, :, None])
    send_block = jnp.sum(jnp.where(send_pick, local_range[None, None, :], 0), axis=2)
    send_flat = peer_head[:, None] * local_blocks + send_block
    home_rank = jnp.take_along_axis(send_rank, owner_index, axis=0)
    home_pos = owner_index * per_peer + home_rank
    pair_index = position * owned_pairs + jnp.arange(owned_pairs)
    split_for_couple = pair_index // cluster_count
    pair_cluster = pair_index % cluster_count
    my_head = position * owned_pairs // cluster_count
    split_numbers = jnp.take(cluster_ids, my_head, axis=0)
    member = split_numbers[None, :] == pair_cluster[:, None]
    member_rank = jnp.cumsum(member.astype(jnp.int32), axis=1) - 1
    member_count = jnp.sum(member.astype(jnp.int32), axis=1)
    picked = member[:, None, :] & (member_rank[:, None, :] == jnp.arange(capacity)[None, :, None])
    member_block = jnp.sum(jnp.where(picked, jnp.arange(block_count)[None, None, :], 0), axis=2)
    live_members = jnp.arange(capacity)[None, :] < member_count[:, None]
    mine = (my_head * cluster_count + split_numbers) // owned_pairs == position
    mine_grid = mine.reshape(seq_count, local_blocks)
    recv_rank = jnp.cumsum(mine_grid.astype(jnp.int32), axis=1) - 1
    recv_pos = (peer_index[:, None] * per_peer + recv_rank).reshape(block_count)
    member_pos = jnp.take(recv_pos, member_block)
    couple_softness = jnp.take(logit_softness, split_for_couple)
    pair_onehot = (split_for_couple[:, None] == jnp.arange(head_count)[None, :]).astype(jnp.float32)
    slot_pair = my_head * cluster_count + split_numbers - position * owned_pairs
    same_cluster = split_numbers[:, None] == split_numbers[None, :]
    earlier_block = jnp.arange(block_count)[None, :] < jnp.arange(block_count)[:, None]
    slot_rank = jnp.sum((same_cluster & earlier_block).astype(jnp.int32), axis=1)
    back_pos = jnp.clip(slot_pair, 0, owned_pairs - 1) * capacity + jnp.clip(
        slot_rank, 0, capacity - 1
    )
    back_grid = back_pos.reshape(seq_count, local_blocks)
    back_pick = mine_grid[:, None, :] & (recv_rank[:, None, :] == slot_range[None, :, None])
    back_flat = jnp.sum(jnp.where(back_pick, back_grid[:, None, :], 0), axis=2)

    def to_peers(array_in):
        flat = array_in.reshape((head_count * local_blocks,) + array_in.shape[2:])
        return jnp.take(flat, send_flat, axis=0)

    def members(array_in):
        flat = array_in.reshape((seq_count * per_peer,) + array_in.shape[2:])
        return jnp.take(flat, member_pos, axis=0)

    def to_owner(array_in):
        flat = array_in.reshape((owned_pairs * capacity,) + array_in.shape[2:])
        return jnp.take(flat, back_flat, axis=0)

    def from_peers(array_in):
        flat = array_in.reshape((seq_count * per_peer,) + array_in.shape[2:])
        return jnp.take(flat, home_pos, axis=0)

    raw_w, mask_w, pgrad_w, top_w, total_w, mass_w = window_parts(
        query_home,
        prev_keys,
        prev_values,
        grad_home,
        usable_home,
        neighborhood_span[:, None],
        logit_softness[:, None],
    )
    arrived = (
        lax.all_to_all(to_peers(query_home), "seq", split_axis=0, concat_axis=0, tiled=True),
        lax.all_to_all(to_peers(key_home), "seq", split_axis=0, concat_axis=0, tiled=True),
        lax.all_to_all(to_peers(value_home), "seq", split_axis=0, concat_axis=0, tiled=True),
        lax.all_to_all(to_peers(grad_home), "seq", split_axis=0, concat_axis=0, tiled=True),
    )
    arrived_stats = (
        lax.all_to_all(to_peers(top_w), "seq", split_axis=0, concat_axis=0, tiled=True),
        lax.all_to_all(to_peers(total_w), "seq", split_axis=0, concat_axis=0, tiled=True),
        lax.all_to_all(to_peers(mass_w), "seq", split_axis=0, concat_axis=0, tiled=True),
    )
    query_m, key_m, value_m, grad_m = [members(item_in) for item_in in arrived]
    top_m, total_m, mass_m = [members(item_in) for item_in in arrived_stats]

    def split_pair(pair_inputs):
        query_i, key_i, value_i, grad_i, live_i, temper_i, top_i, total_i, mass_i = pair_inputs
        query_c, log_total, row_delta, key_c, value_c, temper_c = cluster_pair(
            query_i, key_i, value_i, grad_i, live_i, temper_i, top_i, total_i, mass_i
        )
        return (
            query_c.astype(jnp.bfloat16),
            key_c.astype(jnp.bfloat16),
            value_c.astype(jnp.bfloat16),
            log_total,
            row_delta,
            temper_c,
        )

    owner_results = lax.map(
        split_pair,
        (query_m, key_m, value_m, grad_m, live_members, couple_softness, top_m, total_m, mass_m),
    )
    returned = (
        lax.all_to_all(to_owner(owner_results[0]), "seq", split_axis=0, concat_axis=0, tiled=True),
        lax.all_to_all(to_owner(owner_results[1]), "seq", split_axis=0, concat_axis=0, tiled=True),
        lax.all_to_all(to_owner(owner_results[2]), "seq", split_axis=0, concat_axis=0, tiled=True),
    )
    returned_stats = (
        lax.all_to_all(to_owner(owner_results[3]), "seq", split_axis=0, concat_axis=0, tiled=True),
        lax.all_to_all(to_owner(owner_results[4]), "seq", split_axis=0, concat_axis=0, tiled=True),
    )
    query_cluster = from_peers(returned[0])
    key_cluster = from_peers(returned[1])
    value_cluster = from_peers(returned[2])
    log_home = from_peers(returned_stats[0])
    delta_home = from_peers(returned_stats[1])
    query_w, key_w, value_w, temper_w = window_grads(
        raw_w,
        mask_w,
        pgrad_w,
        query_home,
        prev_keys,
        grad_home,
        log_home,
        delta_home,
        logit_softness[:, None],
    )
    query_out = (query_cluster.astype(jnp.float32) + lifted(query_w)).astype(jnp.bfloat16)
    key_window = key_w.astype(jnp.bfloat16)
    value_window = value_w.astype(jnp.bfloat16)
    temper_local = jnp.sum(owner_results[5][:, None] * pair_onehot, axis=0) + jnp.sum(
        temper_w, axis=1
    )
    edge_keys, edge_values = shifted((key_window[:, 0], value_window[:, 0]), "seq", -1)
    key_next = jnp.concatenate([key_window[:, 1:], edge_keys[:, None]], axis=1)
    value_next = jnp.concatenate([value_window[:, 1:], edge_values[:, None]], axis=1)
    key_out = (key_cluster.astype(jnp.float32) + key_next.astype(jnp.float32)).astype(jnp.bfloat16)
    value_out = (value_cluster.astype(jnp.float32) + value_next.astype(jnp.float32)).astype(
        jnp.bfloat16
    )
    temper_total = lax.psum(temper_local, ("seq", "dp"))
    temper_grad = temper_total / (lax.axis_size("dp") * tokens * seq_count)
    return (token_major(query_out), token_major(key_out), token_major(value_out), temper_grad)


TILE = 256
EXTRA = 16
MIB = 1024 * 1024
PIECES = 4
QUERY, KEY, VALUE, GRAD = range(4)


def columns_of(index):
    return pl.ds(pl.multiple_of(index * HD, HD), HD)


def rows_of(index):
    return pl.ds(pl.multiple_of(index * BLK, BLK), BLK)


def tile_rows(tile):
    return slice(tile * TILE, (tile + 1) * TILE)


def position(half_count):
    me = lax.axis_index("seq")
    half = jnp.where(me >= half_count, 1, 0)
    return me, half, me - half * half_count


def hop(step, half_count):
    near = half_count // 4
    return 2 * step if step < near else 2 * (half_count // 2 - 1 - (step - near))


def kernel_call(
    kernel, name, operands, in_specs, out_shape, scratch, vmem_mib, flops=0, out_spaces=None,
    aliases=None,
):
    bytes_accessed = sum(
        math.prod(item.shape) * item.dtype.itemsize for item in (*operands, *out_shape)
    )
    return pl.pallas_call(
        kernel,
        out_shape=out_shape,
        in_specs=in_specs,
        out_specs=[
            pl.BlockSpec(memory_space=space)
            for space in out_spaces or [pltpu.VMEM] * len(out_shape)
        ],
        scratch_shapes=scratch,
        input_output_aliases=aliases or {},
        cost_estimate=pl.CostEstimate(
            flops=flops, bytes_accessed=bytes_accessed, transcendentals=0
        ),
        compiler_params=pltpu.CompilerParams(vmem_limit_bytes=vmem_mib * MIB),
        name=name,
    )(*operands)


def pack_kernel(*refs, half_count):
    arrays, within_ref, foreign_refs = refs[:4], refs[4], refs[5:7]
    held, within, across, arrival, left_within, left_across = refs[7:]
    me, half, _ = position(half_count)
    piece = BLK // PIECES
    arrivals = [
        [
            pltpu.make_async_copy(
                array_ref.at[0, part * piece : (part + 1) * piece, :],
                held.at[place, part * piece : (part + 1) * piece, :],
                arrival.at[place, part],
            )
            for part in range(PIECES)
        ]
        for place, array_ref in enumerate(arrays)
    ]
    for copies in arrivals:
        for copy in copies:
            copy.start()
    leaving = []
    for place, copies in enumerate(arrivals):
        for copy in copies:
            copy.wait()
        for slot, base in enumerate((half * half_count, (1 - half) * half_count)):
            rows = slice((slot * 4 + place) * BLK, (slot * 4 + place + 1) * BLK)
            for peer in range(half_count):
                within[peer, rows, :] = held[place, :, columns_of(base + peer)]
            leaving.append(
                pltpu.make_async_copy(
                    within.at[:, rows, :], within_ref.at[:, rows, :], left_within.at[place, slot]
                )
            )
            leaving[-1].start()
    first = jnp.where(half == 0, KEY, QUERY)
    second = jnp.where(half == 0, VALUE, GRAD)
    for core, foreign_ref in enumerate(foreign_refs):
        for step in range(half_count // 2):
            columns = columns_of(me ^ core ^ (half_count + hop(step, half_count)))
            across[core, step, :BLK, :] = held[first, :, columns]
            across[core, step, BLK:, :] = held[second, :, columns]
        leaving.append(pltpu.make_async_copy(across.at[core], foreign_ref, left_across.at[core]))
        leaving[-1].start()
    for copy in leaving:
        copy.wait()


def packed(arrays, half_count):
    width = arrays[0].shape[2]
    within_shape, across_shape = (half_count, 8 * BLK, HD), (half_count // 2, 2 * BLK, HD)
    return kernel_call(
        functools.partial(pack_kernel, half_count=half_count),
        "pack_heads",
        arrays,
        [pl.BlockSpec(memory_space=pl.ANY)] * 4,
        [jax.ShapeDtypeStruct(within_shape, jnp.bfloat16)]
        + [jax.ShapeDtypeStruct(across_shape, jnp.bfloat16)] * 2,
        [
            pltpu.VMEM((4, BLK, width), jnp.bfloat16),
            pltpu.VMEM(within_shape, jnp.bfloat16),
            pltpu.VMEM((2, *across_shape), jnp.bfloat16),
            pltpu.SemaphoreType.DMA((4, PIECES)),
            pltpu.SemaphoreType.DMA((4, 2)),
            pltpu.SemaphoreType.DMA((2,)),
        ],
        60,
        out_spaces=[pl.ANY] * 3,
    )


def dot_rows(left, right):
    return lax.dot_general(
        left, right, (((1,), (1,)), ((), ())), preferred_element_type=jnp.float32
    )


def dot_plain(left, right):
    return lax.dot_general(
        left, right, (((1,), (0,)), ((), ())), preferred_element_type=jnp.float32
    )


def from_blocks(ref, place):
    def rows(start, stop):
        per_tile = TILE // BLK
        return jnp.concatenate(
            [ref[block, place] for block in range(start * per_tile, stop * per_tile)],
            axis=0,
        )

    return rows


def from_array(ref, place):
    return lambda start, stop: ref[place, start * TILE : stop * TILE, :]


class Region:
    def __init__(self, square, sources, tiles, scaling, bias_ref=None, least_ref=None, first=0):
        self.square, self.sources, self.tiles, self.scaling = square, sources, tiles, scaling
        self.bias_ref, self.least_ref, self.first = bias_ref, least_ref, first

    def rows(self, which, start, stop):
        return self.sources[which](start, stop)

    def scale_of(self, array):
        return 1.0 if array == VALUE else self.scaling[:, :HD]

    def keys_of(self, tile):
        return range(self.tiles if self.square else tile + 1)

    def scores(self, tile_key, tile_query):
        per_tile = TILE // BLK
        scores = dot_rows(
            self.rows(KEY, tile_key, tile_key + 1), self.rows(QUERY, tile_query, tile_query + 1)
        ) * (self.scaling * math.log2(math.e))
        before = self.tiles * per_tile if self.square else 0
        rows = []
        for sub_key in range(per_tile):
            key_block = tile_key * per_tile + sub_key
            pieces = []
            for sub_query in range(per_tile):
                query_block = tile_query * per_tile + sub_query
                lanes = slice(sub_query * BLK, (sub_query + 1) * BLK)
                piece = scores[sub_key * BLK : (sub_key + 1) * BLK, lanes]
                apart = before + query_block - key_block
                if apart < 0:
                    piece = jnp.full_like(piece, blocked_score)
                elif apart == 0:
                    piece = jnp.where(key_minus_query() <= 0, piece, blocked_score)
                elif apart == 1:
                    row = self.first + (0 if self.square else key_block)
                    least = self.least_ref[row : row + 1, :]
                    piece = jnp.where(key_minus_query() > least, piece, blocked_score)
                else:
                    at = slice(query_block * BLK, (query_block + 1) * BLK)
                    piece = piece + self.bias_ref[key_block : key_block + 1, at]
                pieces.append(piece)
            rows.append(jnp.concatenate(pieces, axis=1))
        return jnp.concatenate(rows, axis=0)


def diagonal(slot, arrived_ref, scales_ref, bias_ref=None, least_ref=None):
    blocks = arrived_ref.shape[0]
    sources = [from_blocks(arrived_ref, slot * 4 + place) for place in range(4)]
    bias = None if bias_ref is None else bias_ref.at[slot]
    first = slot * (blocks - 1)
    scaling = scales_ref[slot : slot + 1, :]
    return Region(False, sources, blocks * BLK // TILE, scaling, bias, least_ref, first)


def square(square_ref, scales_ref, bias_ref=None, least_ref=None):
    tiles = square_ref.shape[1] // TILE
    sources = [from_array(square_ref, place) for place in range(4)]
    bias = None if bias_ref is None else bias_ref.at[2]
    first = 2 * (tiles * TILE // BLK - 1)
    return Region(True, sources, tiles, scales_ref[0:1, :], bias, least_ref, first)


def key_minus_query():
    shape = (BLK, BLK)
    return lax.broadcasted_iota(jnp.int32, shape, 0) - lax.broadcasted_iota(jnp.int32, shape, 1)


def statistics(region, weight_ref, towards_ref, out_ref, first_row):
    for tile in range(region.tiles):
        here = tile_rows(tile)
        top = jnp.full((1, TILE), blocked_score, jnp.float32)
        for other in region.keys_of(tile):
            raw = region.scores(other, tile)
            weight_ref[tile_rows(other), here] = raw
            top = jnp.maximum(top, jnp.max(raw, axis=0, keepdims=True))
        sums = [jnp.zeros((1, TILE), jnp.float32)] * 4
        for other in region.keys_of(tile):
            there = tile_rows(other)
            raw = weight_ref[there, here]
            weight = jnp.exp2(raw - top)
            towards = dot_rows(
                region.rows(VALUE, other, other + 1), region.rows(GRAD, tile, tile + 1)
            )
            weight_ref[there, here] = weight
            towards_ref[there, here] = towards
            pulled, weighted = weight * towards, weight * raw
            terms = (weight, pulled, pulled * raw, weighted)
            sums = [
                total + jnp.sum(term, axis=0, keepdims=True) for total, term in zip(sums, terms)
            ]
        for row, value in enumerate((top, *sums)):
            out_ref[first_row + row : first_row + row + 1, here] = value


def gradients(
    region, weight_ref, towards_ref, top, log_total, delta, prob_low, grad_low, keys_flat, emit=None
):
    keys_flat[...] = region.rows(KEY, 0, region.tiles).T
    share = jnp.exp2(top - log_total)
    query_parts, key_parts, value_parts = [], [], []
    for tile in range(region.tiles):
        here = tile_rows(tile)
        for other in region.keys_of(tile):
            there = tile_rows(other)
            probability = weight_ref[there, here] * share[:, here]
            prob_low[there, here] = probability.astype(jnp.bfloat16)
            grad_low[there, here] = (
                probability * (towards_ref[there, here] - delta[:, here])
            ).astype(jnp.bfloat16)
        upto = slice(0, len(region.keys_of(tile)) * TILE)
        query_parts.append(dot_plain(keys_flat[:, upto], grad_low[upto, here]).T)
    if emit is not None:
        emit(QUERY, query_parts)
    for low, which, parts in ((grad_low, QUERY, key_parts), (prob_low, GRAD, value_parts)):
        for tile in range(region.tiles):
            first = 0 if region.square else tile
            onward = slice(first * TILE, region.tiles * TILE)
            parts.append(
                dot_plain(low[tile_rows(tile), onward], region.rows(which, first, region.tiles))
            )
        if emit is not None:
            emit(KEY if which == QUERY else VALUE, parts)
    return query_parts, key_parts, value_parts


def merged(first, second):
    top = jnp.maximum(first[0], second[0])
    left, right = jnp.exp2(first[0] - top), jnp.exp2(second[0] - top)
    total = first[1] * left + second[1] * right
    mass = first[2] * left + second[2] * right
    return top + jnp.log2(total), mass / total


def alone(rows):
    return rows[0] + jnp.log2(rows[1]), rows[2] / rows[1]


def rows_at(ref, first, count=5):
    return [ref[first + row : first + row + 1, :] for row in range(count)]


def temper_terms(rows, totals, scale_row):
    log_total, delta = totals
    terms = (rows[3] - delta * rows[4]) * jnp.exp2(rows[0] - log_total)
    folded = sum(terms[:, start : start + HD] for start in range(0, terms.shape[1], HD))
    return folded / (scale_row[:, :HD] * (math.sqrt(HD) * math.log2(math.e)))


def put(within_ref, array, tile, value):
    per_tile = TILE // BLK
    for sub in range(per_tile):
        within_ref[tile * per_tile + sub, array * BLK : (array + 1) * BLK, :] = value[
            sub * BLK : (sub + 1) * BLK, :
        ].astype(jnp.bfloat16)


def scaled(region, parts):
    scale = region.scaling[:, :HD]
    return [[value * scale for value in part] for part in parts[:2]] + [parts[2]]


def masks_kernel(softness_ref, ids_ref, span_ref, scales_ref, bias_ref, least_ref, *, half_count):
    me, half, _ = position(half_count)
    base = half * half_count
    regions = (
        (me, base, base),
        (me ^ half_count, base, base),
        (me, 0, half_count),
    )
    for slot, (head, key_base, query_base) in enumerate(regions):
        if slot < 2:
            scales_ref[slot : slot + 1, :] = jnp.full(
                (1, TILE), softness_ref[head] * (1.0 / math.sqrt(HD)), jnp.float32
            )

        def same(key_block, query_block):
            return ids_ref[head, key_base + key_block] == ids_ref[head, query_base + query_block]

        def bias(key_block, query_block):
            return jnp.full(
                (1, BLK), jnp.where(same(key_block, query_block), 0.0, blocked_score), jnp.float32
            )

        for key_block in range(half_count):
            bias_ref[slot, key_block : key_block + 1, :] = jnp.concatenate(
                [bias(key_block, query_block) for query_block in range(half_count)], axis=1
            )
        pairs = [(block, block + 1) for block in range(half_count - 1)]
        if slot == 2:
            pairs = [(half_count - 1, 0)]
        for place, pair in enumerate(pairs):
            least = jnp.where(same(*pair), -BLK, BLK - span_ref[head])
            row = slot * (half_count - 1) + place
            least_ref[row : row + 1, :] = jnp.full((1, BLK), least, jnp.int32)


def within_kernel(
    arrived_ref, scales_ref, bias_ref, least_ref, stats_ref, parts_ref, own_weight, own_towards, other_weight, other_towards, *scratch, half_count
):
    _, half, _ = position(half_count)
    kept = ((own_weight, own_towards), (other_weight, other_towards))
    for slot in range(2):
        region = diagonal(slot, arrived_ref, scales_ref, bias_ref, least_ref)
        statistics(region, *kept[slot], stats_ref, slot * 5)

    @pl.when(half == 0)
    def _():
        region = diagonal(0, arrived_ref, scales_ref)
        single = alone(rows_at(stats_ref, 0))
        parts = gradients(region, *kept[0], stats_ref[0:1, :], *single, *scratch)
        for place, tiles in enumerate(scaled(region, parts)):
            for tile, value in enumerate(tiles):
                parts_ref[place, tile_rows(tile), :] = value


def square_kernel(arrived_ref, scales_ref, bias_ref, least_ref, stats_ref, *refs, half_count):
    across_refs = refs[: half_count // 2]
    square_ref, message_ref, square_stats, weight, towards = refs[half_count // 2 :]
    _, half, place = position(half_count)
    first = jnp.where(half == 0, QUERY, KEY)
    second = jnp.where(half == 0, GRAD, VALUE)
    for step, across_ref in enumerate(across_refs):
        for core in range(2):
            rows = rows_of(place ^ core ^ hop(step, half_count))
            square_ref[first, rows, :] = across_ref[core, :BLK, :]
            square_ref[second, rows, :] = across_ref[core, BLK:, :]
    for kept in (jnp.where(half == 0, KEY, QUERY), jnp.where(half == 0, VALUE, GRAD)):
        for block in range(half_count):
            square_ref[kept, block * BLK : (block + 1) * BLK, :] = arrived_ref[block, kept]
    region = square(square_ref, scales_ref, bias_ref, least_ref)
    statistics(region, weight, towards, square_stats, 0)
    own, other, crossing = rows_at(stats_ref, 0), rows_at(stats_ref, 5), rows_at(square_stats, 0)
    for row in range(5):
        message_ref[row : row + 1, :] = jnp.where(half == 0, crossing[row], other[row])
    own_scale, other_scale = scales_ref[0:1, :], scales_ref[1:2, :]
    both = merged(own, crossing)
    whole = temper_terms(own, both, own_scale) + temper_terms(crossing, both, own_scale)
    single = temper_terms(own, alone(own), own_scale)
    message_ref[5:6, :HD] = jnp.where(half == 0, single, whole)
    message_ref[6:7, :HD] = temper_terms(other, alone(other), other_scale)


def first_kernel(
    arrived_ref, scales_ref, square_ref, stats_ref, square_stats,
    own_weight, own_towards, other_weight, other_towards, square_weight, square_towards,
    across_ref, within_ref, ready, ready_sem, *scratch, half_count
):
    _, half, _ = position(half_count)
    leaving = sends(ready, within_ref, ready_sem, (1 - half) * 3)

    @pl.when(half == 0)
    def _():
        region = diagonal(1, arrived_ref, scales_ref)

        def send(array, parts):
            for tile, part in enumerate(parts):
                put(ready, array, tile, part * region.scale_of(array))
            leaving[array].start()

        totals = alone(rows_at(stats_ref, 5))
        gradients(
            region, other_weight, other_towards, stats_ref[5:6, :], *totals, *scratch, emit=send
        )

    @pl.when(half == 1)
    def _():
        totals = merged(rows_at(stats_ref, 0), rows_at(square_stats, 0))
        region = square(square_ref, scales_ref)
        parts = gradients(
            region, square_weight, square_towards, square_stats[0:1, :], *totals, *scratch
        )
        across_query, *foreign = scaled(region, parts)
        for array, tiles in enumerate(foreign):
            for tile, value in enumerate(tiles):
                across_ref[array, tile_rows(tile), :] = value.astype(jnp.bfloat16)
        region = diagonal(0, arrived_ref, scales_ref)

        def send(array, parts):
            for tile, part in enumerate(parts):
                value = part * region.scale_of(array)
                put(ready, array, tile, value + across_query[tile] if array == QUERY else value)
            leaving[array].start()

        gradients(
            region, own_weight, own_towards, stats_ref[0:1, :], *totals, *scratch, emit=send
        )

    for copy in leaving:
        copy.wait()


def sends(ready, within_ref, sems, first):
    copies = []
    for array in range(3):
        rows = slice(array * BLK, (array + 1) * BLK)
        copies.append(
            pltpu.make_async_copy(
                ready.at[:, rows, :], within_ref.at[:, rows_of(first + array), :], sems.at[array]
            )
        )
    return copies


def temper_rows(own, other):
    row = lax.broadcasted_iota(jnp.int32, (EXTRA, HD), 0)
    rows = jnp.zeros((EXTRA, HD), jnp.float32)
    for place, terms in enumerate((own, other)):
        rest = jnp.broadcast_to(jnp.sum(terms, axis=1, keepdims=True), (EXTRA, HD))
        for piece in range(3):
            high = rest.astype(jnp.bfloat16).astype(jnp.float32)
            rows = jnp.where(row == place * 3 + piece, high, rows)
            rest = rest - high
    return rows.astype(jnp.bfloat16)


def finish_kernel(
    arrived_ref, scales_ref, square_ref, message_ref, received_ref, stats_ref, square_stats,
    parts_ref, square_weight, square_towards, other_weight, other_towards, across_ref, begun_ref,
    within_ref, *refs, half_count
):
    del begun_ref
    chunk_refs = refs[:2]
    across, ready, tail, ready_sem, tail_sem, *scratch = refs[2:]
    _, half, place = position(half_count)
    leaving = sends(ready, within_ref, ready_sem, half * 3)
    sent, came = rows_at(message_ref, 0), rows_at(received_ref, 0)
    totals = merged(sent, came)
    scale = jnp.where(half == 0, scales_ref[0:1, :], scales_ref[1:2, :])
    shared = temper_terms(sent, totals, scale) + temper_terms(came, totals, scale)
    mine, theirs = message_ref[5:6, :HD], received_ref[5:6, :HD]
    own = mine + jnp.where(half == 0, shared, received_ref[6:7, :HD])
    other = theirs + jnp.where(half == 0, message_ref[6:7, :HD], shared)
    pieces = temper_rows(own, other)
    for block in range(half_count):
        tail[block] = pieces
    leaving.append(
        pltpu.make_async_copy(tail, within_ref.at[:, 6 * BLK : 6 * BLK + EXTRA, :], tail_sem)
    )
    leaving[-1].start()

    def chunks():
        for core, chunk_ref in enumerate(chunk_refs):
            for step in range(half_count // 2):
                yield step, chunk_ref, rows_of(place ^ core ^ hop(step, half_count))

    @pl.when(half == 0)
    def _():
        region = square(square_ref, scales_ref)

        def send(array, parts):
            for tile, part in enumerate(parts):
                here = tile_rows(tile)
                value = part * region.scale_of(array)
                if array == QUERY:
                    across[here, :] = value.astype(jnp.bfloat16)
                    put(ready, array, tile, parts_ref[array, here, :])
                else:
                    put(ready, array, tile, parts_ref[array, here, :] + value)
            leaving[array].start()

        gradients(
            region, square_weight, square_towards, square_stats[0:1, :], *totals, *scratch, emit=send
        )
        for step, chunk_ref, rows in chunks():
            chunk_ref[step, :BLK, :] = across[rows, :]
            chunk_ref[step, BLK:, :] = jnp.zeros((BLK, HD), jnp.bfloat16)

    @pl.when(half == 1)
    def _():
        region = diagonal(1, arrived_ref, scales_ref)

        def send(array, parts):
            for tile, part in enumerate(parts):
                put(ready, array, tile, part * region.scale_of(array))
            leaving[array].start()

        gradients(
            region, other_weight, other_towards, stats_ref[5:6, :], *totals, *scratch, emit=send
        )
        for step, chunk_ref, rows in chunks():
            chunk_ref[step, :BLK, :] = across_ref[0, rows, :]
            chunk_ref[step, BLK:, :] = across_ref[1, rows, :]

    for copy in leaving:
        copy.wait()


def temper_kernel(within_ref, temper_ref, *, half_count):
    _, half, _ = position(half_count)
    for peer in range(half_count):
        for slot, base in enumerate((half * half_count, (1 - half) * half_count)):
            rows = within_ref[peer, 3 * slot : 3 * slot + 3, :].astype(jnp.float32)
            temper_ref[pl.ds(base + peer, 1), :] = jnp.sum(rows, axis=0, keepdims=True)


def temper_sums(within, half_count):
    last = 6 * BLK // EXTRA
    return pl.pallas_call(
        functools.partial(temper_kernel, half_count=half_count),
        grid=(1,),
        out_shape=jax.ShapeDtypeStruct((2 * half_count, HD), jnp.float32),
        in_specs=[pl.BlockSpec((half_count, EXTRA, HD), lambda step: (0, last, 0))],
        out_specs=pl.BlockSpec((2 * half_count, HD), lambda step: (0, 0)),
        compiler_params=pltpu.CompilerParams(vmem_limit_bytes=4 * MIB),
        name="temper_sums",
    )(within)


def own_columns_kernel(within_ref, *refs, half_count):
    out_refs, (staged, sems) = refs[:3], refs[3:]
    _, half, _ = position(half_count)
    width = half_count * HD
    for array in range(6):
        for peer in range(half_count):
            staged[array, :, peer * HD : (peer + 1) * HD] = within_ref[
                peer, array * BLK : (array + 1) * BLK, :
            ]

    def copies(arrays):
        return [
            pltpu.make_async_copy(
                staged.at[array],
                out_refs[array % 3].at[0, :, side(half if array < 3 else 1 - half, width)],
                sems.at[array],
            )
            for array in arrays
        ]

    for role, arrays in enumerate(((0, 1, 2, 3), (0, 1, 2, 4, 5))):

        @pl.when(half == role)
        def _():
            leaving = copies(arrays)
            for copy in leaving:
                copy.start()
            for copy in leaving:
                copy.wait()


def side(half, width):
    return pl.ds(pl.multiple_of(half * width, width), width)


def other_columns_kernel(within_ref, *refs, half_count):
    messages = half_count // 2
    across_refs = refs[:messages]
    out_refs, (staged, sems) = refs[messages + 3 : messages + 6], refs[messages + 6 :]
    _, half, place = position(half_count)

    for role, arrays in enumerate(((1, 2), (0,))):

        @pl.when(half == role)
        def _():
            leaving = []
            for step, across_ref in enumerate(across_refs):
                pair = (place ^ hop(step, half_count)) >> 1
                for part, array in enumerate(arrays):
                    rows = slice(part * BLK, (part + 1) * BLK)
                    for core in range(2):
                        peer = place ^ core ^ hop(step, half_count)
                        kept = within_ref[peer, (3 + array) * BLK : (4 + array) * BLK, :]
                        total = kept.astype(jnp.float32) + across_ref[core, rows, :].astype(
                            jnp.float32
                        )
                        staged[part, :, columns_of(peer)] = total.astype(jnp.bfloat16)
                    start = (1 - role) * messages + pair
                    leaving.append(
                        pltpu.make_async_copy(
                            staged.at[part, :, side(pair, 2 * HD)],
                            out_refs[array].at[0, :, side(start, 2 * HD)],
                            sems.at[step, part],
                        )
                    )
                    leaving[-1].start()
            for copy in leaving:
                copy.wait()


def join_kernel(kept_ref, taken_ref, *out_refs):
    for step, out_ref in enumerate(out_refs):
        out_ref[0] = kept_ref[step]
        out_ref[1] = taken_ref[step]


def crossed(kept, given, half_count):
    devices = range(2 * half_count)
    steps, *shape = kept.shape
    taken = lax.ppermute(given, "seq", [(source, source ^ 1) for source in devices])
    messages = kernel_call(
        join_kernel,
        "join_chunks",
        (kept, taken),
        [pl.BlockSpec(memory_space=pltpu.VMEM)] * 2,
        [jax.ShapeDtypeStruct((2, *shape), jnp.bfloat16)] * steps,
        [],
        4,
    )
    return [
        lax.ppermute(
            message, "seq", [(source, source ^ (half_count + hop(step, half_count))) for source in devices]
        )
        for step, message in enumerate(messages)
    ]


def head_shards(
    probe_vectors,
    lookup_vectors,
    content_vectors,
    result_cotangent,
    logit_softness,
    block_grouping,
    neighborhood_span,
):
    seq_count, dp_count = lax.axis_size("seq"), lax.axis_size("dp")
    half_count = seq_count // 2
    tokens = half_count * BLK
    groups = [list(range(half_count)), list(range(half_count, seq_count))]
    settings = (logit_softness, block_grouping[0, :, :, 0], neighborhood_span)
    smem, vmem = pl.BlockSpec(memory_space=pltpu.SMEM), pl.BlockSpec(memory_space=pltpu.VMEM)
    lows = [pltpu.VMEM((tokens, tokens), jnp.bfloat16)] * 2 + [
        pltpu.VMEM((HD, tokens), jnp.bfloat16)
    ]
    rows_of_stats = jax.ShapeDtypeStruct((8, tokens), jnp.float32)
    pairs = jax.ShapeDtypeStruct((tokens, tokens), jnp.float32)
    pair_flops = 2 * tokens * tokens * HD

    def exchange_within(array_in):
        return lax.all_to_all(
            array_in, "seq", split_axis=0, concat_axis=0, axis_index_groups=groups, tiled=True
        )

    def call(
        kernel, name, operands, out_shape, scratch, flops, vmem_mib, scalars=(), out_spaces=None,
        last_in_place=False,
    ):
        in_specs = [smem] * len(scalars) + [vmem] * len(operands)
        if last_in_place:
            in_specs[-1] = pl.BlockSpec(memory_space=pl.ANY)
        return kernel_call(
            functools.partial(kernel, half_count=half_count),
            name,
            (*scalars, *operands),
            in_specs,
            out_shape,
            scratch,
            vmem_mib,
            flops,
            out_spaces,
            {len(operands) - 1: 0} if last_in_place else {},
        )

    sent, *foreign = packed(
        (probe_vectors, lookup_vectors, content_vectors, result_cotangent), half_count
    )
    arrived = exchange_within(sent).reshape(half_count, 8, BLK, HD)
    kept_parts = jax.ShapeDtypeStruct((3, tokens, HD), jnp.float32)
    masks = call(
        masks_kernel,
        "scales_and_masks",
        (),
        [
            jax.ShapeDtypeStruct((8, TILE), jnp.float32),
            jax.ShapeDtypeStruct((3, half_count, tokens), jnp.float32),
            jax.ShapeDtypeStruct((2 * half_count, BLK), jnp.int32),
        ],
        [],
        0,
        2,
        settings,
    )
    foreign[0], *masks = lax.optimization_barrier((foreign[0], *masks))
    foreign = crossed(*foreign, half_count)
    scales = masks[0]
    stats, parts, own_weight, own_towards, other_weight, other_towards = call(
        within_kernel,
        "diagonal_statistics",
        (arrived, *masks),
        [jax.ShapeDtypeStruct((16, tokens), jnp.float32), kept_parts] + [pairs] * 4,
        lows,
        2 * pair_flops,
        14,
    )
    squared, message, square_stats, square_weight, square_towards = call(
        square_kernel,
        "square_statistics",
        (arrived, *masks, stats, *foreign),
        [jax.ShapeDtypeStruct((4, tokens, HD), jnp.bfloat16)] + [rows_of_stats] * 2 + [pairs] * 2,
        [],
        2 * pair_flops,
        8,
    )
    swap = [(source, source ^ half_count) for source in range(seq_count)]
    received = lax.ppermute(message, "seq", swap)
    result = pltpu.HBM((half_count, 6 * BLK + EXTRA, HD), jnp.bfloat16)
    ready = pltpu.VMEM((half_count, 3 * BLK, HD), jnp.bfloat16)
    across, begun = call(
        first_kernel,
        "gradients_before_totals",
        (
            arrived, scales, squared, stats, square_stats, own_weight, own_towards,
            other_weight, other_towards, square_weight, square_towards,
        ),
        [jax.ShapeDtypeStruct((2, tokens, HD), jnp.bfloat16), result],
        [ready, pltpu.SemaphoreType.DMA((3,)), *lows],
        4 * pair_flops,
        14,
        out_spaces=(pltpu.VMEM, pl.ANY),
    )
    operands = (
        arrived, scales, squared, message, received, stats, square_stats, parts,
        square_weight, square_towards, other_weight, other_towards, across, begun,
    )
    within, *foreign = call(
        finish_kernel,
        "gradients_after_totals",
        operands,
        [result]
        + [jax.ShapeDtypeStruct((half_count // 2, 2 * BLK, HD), jnp.bfloat16)] * 2,
        [
            pltpu.VMEM((tokens, HD), jnp.bfloat16), ready,
            pltpu.VMEM((half_count, EXTRA, HD), jnp.bfloat16),
            pltpu.SemaphoreType.DMA((3,)), pltpu.SemaphoreType.DMA, *lows,
        ],
        2 * pair_flops,
        16,
        out_spaces=(pl.ANY, pltpu.VMEM, pltpu.VMEM),
        last_in_place=True,
    )
    across = crossed(*foreign, half_count)
    within = exchange_within(within)
    tempers = temper_sums(within, half_count)
    temper_total = tempers
    for step in range(1, dp_count):
        swap = [(source, (source + step) % dp_count) for source in range(dp_count)]
        temper_total = temper_total + lax.ppermute(tempers, "dp", swap)
    temper = temper_total[:, 0] / (dp_count * BLK * seq_count)
    result = [pltpu.HBM(probe_vectors.shape, jnp.bfloat16)] * 3
    width = half_count * HD
    outs = kernel_call(
        functools.partial(own_columns_kernel, half_count=half_count),
        "unpack_own",
        (within,),
        [vmem],
        result,
        [pltpu.VMEM((6, BLK, width), jnp.bfloat16), pltpu.SemaphoreType.DMA((6,))],
        6,
        out_spaces=[pl.ANY] * 3,
    )
    across[0], temper = lax.optimization_barrier((across[0], temper))
    outs = kernel_call(
        functools.partial(other_columns_kernel, half_count=half_count),
        "unpack_other",
        (within, *across, *outs),
        [vmem] * (1 + len(across)) + [pl.BlockSpec(memory_space=pl.ANY)] * 3,
        result,
        [pltpu.VMEM((2, BLK, width), jnp.bfloat16), pltpu.SemaphoreType.DMA((len(across), 2))],
        6,
        out_spaces=[pl.ANY] * 3,
        aliases={1 + len(across) + array: array for array in range(3)},
    )
    return (*outs, temper)


def shards(
    probe_vectors,
    lookup_vectors,
    content_vectors,
    result_cotangent,
    logit_softness,
    block_grouping,
    neighborhood_span,
):
    head_count = probe_vectors.shape[2] // HD
    seq_count = lax.axis_size("seq")
    one_block = probe_vectors.shape[1] == BLK
    whole_tiles = seq_count * BLK % (2 * TILE) == 0 and seq_count & (seq_count - 1) == 0
    if head_count == seq_count and one_block and whole_tiles:
        plan = head_shards
    else:
        plan = clustered_shards
    return plan(
        probe_vectors,
        lookup_vectors,
        content_vectors,
        result_cotangent,
        logit_softness,
        block_grouping,
        neighborhood_span,
    )


def solution(mesh):
    in_specs = (
        P("dp", "seq", None),
        P("dp", "seq", None),
        P("dp", "seq", None),
        P("dp", "seq", None),
        P(),
        P("dp", None, None, None),
        P(),
    )
    out_specs = (P("dp", "seq", None), P("dp", "seq", None), P("dp", "seq", None), P())
    return jax.shard_map(shards, mesh=mesh, in_specs=in_specs, out_specs=out_specs, check_vma=False)
```
